32 devices in a mesh: groups: 2 (over y), leaf: 4 (over z), tensor: 2 (over x), sub: 2 (over core).
Axes of the slice: x: 2, y: 2, z: 4, core: 2. Of those that a mesh axis runs over, the one named last changes fastest.
Arguments:
- queries: bfloat16 [6144, 8192], P(('groups', 'leaf', 'sub'), 'tensor'), parts along dimension 0, may hold values from -6 to 6
- grad_out: bfloat16 [6144, 8192], P(('groups', 'leaf', 'sub'), 'tensor'), parts along dimension 0, may hold values from -12 to 12
- keys: bfloat16 [6144, 1024], P(('groups', 'leaf', 'sub'), 'tensor'), parts along dimension 0, may hold values from -6 to 6
- values: bfloat16 [6144, 1024], P(('groups', 'leaf', 'sub'), 'tensor'), parts along dimension 0, may hold values from -6 to 6
- log_norms: float32 [64, 6144], P('tensor', ('groups', 'leaf', 'sub')), parts along dimension 1, may hold values from 4 to 6
- row_deltas: float32 [64, 6144], P('tensor', ('groups', 'leaf', 'sub')), parts along dimension 1, may hold values from -12 to 12
- ancestors: int32 [16, 5], P(('groups', 'leaf', 'sub')), parts along dimension 0, may hold values from 0 to 23, as said below
- counts: int32 [16, 3], P(('groups', 'leaf', 'sub')), parts along dimension 0, may hold values from 16 to 128
- w_value: bfloat16 [5120, 1024], P('tensor'), may hold values from -0.078125 to 0.078125
Outputs:
- grad_queries: bfloat16 [6144, 8192], P(('groups', 'leaf', 'sub'), 'tensor'), parts along dimension 0
- grad_keys: bfloat16 [6144, 1024], P(('groups', 'leaf', 'sub'), 'tensor'), parts along dimension 0
- grad_values: bfloat16 [6144, 1024], P(('groups', 'leaf', 'sub'), 'tensor'), parts along dimension 0
- grad_input: bfloat16 [6144, 5120], P(('groups', 'leaf', 'sub'), 'tensor'), parts along dimension 0
The draws below stay inside these ranges and needn't reach their ends.
There are 2 independent parts, one for each index of `groups`. The reference program is written for one: setup_inputs(seed, part) draws one part's arguments, and reference() takes and returns one part's arrays. A program takes and returns all parts, laid end to end along the dimension named above; an argument that names none is the same for every part. Nothing has to cross between parts.
Inputs may be any that keep to these rules, and one draw needn't show every extreme that they name: ancestors[d, j] is the page id (leaf times 3 plus slot) of leaf d's level-j page. For j < 3 the leaves whose level-j pages are the same page form exactly an aligned block of 8 >> j consecutive leaves, and that page is slot 0 of one leaf of the block; no slot 0 serves two blocks or levels. ancestors[d, 3] = d * 3 + 1 and ancestors[d, 4] = d * 3 + 2.
All inputs are finite; a program needn't handle non-finite values.
Results may differ from the reference program's by a relative error of at most 0.0061.
Values may be sent and summed in bfloat16 or wider, within the bound.
No kernel may reach another device: no remote copies, remote signals or barrier semaphores. Data moves between devices by JAX's collectives and lax.ppermute only.
A program may use at most 128 MiB of HBM per device.

```python
import math
import jax
import jax.numpy as jnp
from jax import lax

D = 5120
QH = 64
KVH = 8
HD = 128
PAGE = 128
SLOTS = 3
INNER = 3
LEVELS = 5
LEAVES = 8
PAGES = 24
ROWS = 3072


def draw_ancestors(key, part):
    key = jax.random.fold_in(key, 11)
    key_perm, key_half, key_root = jax.random.split(key, 3)
    quarter = LEAVES // 4
    quarter_keys = jax.random.split(key_perm, 4)
    orders = jnp.stack([jax.random.permutation(quarter_keys[index], quarter) for index in range(4)])
    quarter_leaves = (orders + jnp.arange(4, dtype=jnp.int32)[:, None] * quarter).astype(jnp.int32)
    level_two = quarter_leaves[:, 0]
    halves = jax.random.randint(key_half, (2,), 0, 2).astype(jnp.int32)
    level_one = jnp.stack([quarter_leaves[halves[0], 1], quarter_leaves[2 + halves[1], 1]])
    root_half = jax.random.randint(key_root, (), 0, 2).astype(jnp.int32)
    level_zero = quarter_leaves[2 * root_half + 1 - halves[root_half], 1]
    leaf_ids = jnp.arange(LEAVES, dtype=jnp.int32)
    columns = [jnp.zeros((LEAVES,), jnp.int32) + level_zero * SLOTS, level_one[leaf_ids // (LEAVES // 2)] * SLOTS, level_two[leaf_ids // quarter] * SLOTS, leaf_ids * SLOTS + 1, leaf_ids * SLOTS + 2]
    return jnp.stack(columns, axis=1).astype(jnp.int32)


def draw_counts(key, part):
    key = jax.random.fold_in(key, 23)
    raw_counts = jax.random.randint(key, (LEAVES, SLOTS), 0, PAGE * 25 // 16)
    return jnp.clip(raw_counts, PAGE // 8, PAGE).astype(jnp.int32)


def steps_of(stream_key, dims, pieces, least, top_value):
    factor_of = 1.0
    for position, shards_of in pieces:
        steps = jax.random.uniform(jax.random.fold_in(jax.random.fold_in(stream_key, 6), position), (shards_of,), jnp.float32, least / len(pieces), top_value / len(pieces))
        factor_of = factor_of * jnp.repeat(jnp.exp(steps), dims[position] // shards_of).reshape((-1,) + (1,) * (len(dims) - 1 - position))
    return factor_of


def centred(rng, shape, width, bound, cuts=(), held_as=jnp.bfloat16):
    level = steps_of(rng, shape, cuts, -0.22, 0.18) if cuts else 1.0
    entries = jax.random.normal(rng, shape, jnp.float32) * width * level
    return jnp.minimum(jnp.maximum(entries, -bound), bound).astype(held_as)


def setup_inputs(seed: int = 0, part: int = 0) -> dict:
    seeds = jax.random.split(jax.random.key(seed), 10)
    part_keys = jax.random.split(jax.random.fold_in(seeds[9], part), 10)
    return {
        "queries": centred(part_keys[0], (ROWS, QH * HD), 1.0, 6.0, ((0, 8), (1, 2))),
        "grad_out": centred(part_keys[1], (ROWS, QH * HD), 2.0, 12.0, ((0, 8), (1, 2))),
        "keys": centred(part_keys[2], (ROWS, KVH * HD), 1.0, 6.0, ((0, 8), (1, 2))),
        "values": centred(part_keys[3], (ROWS, KVH * HD), 1.0, 6.0, ((0, 8), (1, 2))),
        "log_norms": jnp.clip(4.0 + 2.0 * jax.random.uniform(part_keys[4], (QH, ROWS), jnp.float32) ** steps_of(part_keys[4], (QH, ROWS), ((0, 2), (1, 8)), -0.2, 0.2), 4.0, 6.0),
        "row_deltas": centred(part_keys[5], (QH, ROWS), 2.0, 12.0, ((0, 2), (1, 8)), jnp.float32),
        "ancestors": draw_ancestors(jax.random.fold_in(jax.random.fold_in(seeds[9], part), 71), part),
        "counts": draw_counts(jax.random.fold_in(jax.random.fold_in(seeds[9], part), 71), part),
        "w_value": centred(seeds[8], (D, KVH * HD), D ** -0.5, 0.078125, ((0, 2),)),
    }


def rounded(values_in):
    return lax.optimization_barrier(values_in.astype(jnp.bfloat16)).astype(jnp.float32)

def attend(query_rows, grad_rows, norm_rows, delta_rows, key_rows, value_rows, allowed):
    score_scale = 1.0 / math.sqrt(HD)
    scores = jnp.einsum('rkgd,nkd->kgrn', query_rows, key_rows) * score_scale
    weights = jnp.where(allowed[None, None], jnp.exp(scores - norm_rows[..., None]), 0.0)
    grad_weights = jnp.einsum('rkgd,nkd->kgrn', grad_rows, value_rows)
    grad_scores = rounded(weights * (grad_weights - delta_rows[..., None]))
    weights_low = rounded(weights)
    grad_value_part = jnp.einsum('kgrn,rkgd->nkd', weights_low, grad_rows)
    grad_key_part = jnp.einsum('kgrn,rkgd->nkd', grad_scores, query_rows) * score_scale
    grad_query_part = jnp.einsum('kgrn,nkd->rkgd', grad_scores, key_rows) * score_scale
    return (grad_query_part, grad_key_part, grad_value_part)

def reference(queries, grad_out, keys, values, log_norms, row_deltas, ancestors, counts, w_value):
    group_size = QH // KVH
    query_pages = queries.astype(jnp.float32).reshape(PAGES, PAGE, KVH, group_size, HD)
    grad_pages = grad_out.astype(jnp.float32).reshape(PAGES, PAGE, KVH, group_size, HD)
    key_pages = keys.astype(jnp.float32).reshape(PAGES, PAGE, KVH, HD)
    value_pages = values.astype(jnp.float32).reshape(PAGES, PAGE, KVH, HD)
    norm_pages = log_norms.reshape(KVH, group_size, PAGES, PAGE)
    delta_pages = row_deltas.reshape(KVH, group_size, PAGES, PAGE)
    page_counts = counts.reshape(PAGES)
    positions = jnp.arange(PAGE, dtype=jnp.int32)
    level_ids = jnp.arange(LEVELS, dtype=jnp.int32)
    key_level = jnp.repeat(level_ids, PAGE)
    key_pos = jnp.tile(positions, LEVELS)
    inner_rows = INNER * PAGE

    def one_leaf(leaf_index):
        path_ids = ancestors[leaf_index]
        own_page = (leaf_index * SLOTS).astype(jnp.int32)
        path_keys = key_pages[path_ids].reshape(LEVELS * PAGE, KVH, HD)
        path_values = value_pages[path_ids].reshape(LEVELS * PAGE, KVH, HD)
        key_ok = key_pos < jnp.repeat(page_counts[path_ids], PAGE)
        leaf_counts = counts[leaf_index]
        own_queries = lax.dynamic_slice_in_dim(query_pages, own_page, SLOTS, 0)
        own_grads = lax.dynamic_slice_in_dim(grad_pages, own_page, SLOTS, 0)
        own_norms = lax.dynamic_slice_in_dim(norm_pages, own_page, SLOTS, 2)
        own_deltas = lax.dynamic_slice_in_dim(delta_pages, own_page, SLOTS, 2)
        row_slot = jnp.repeat(jnp.arange(1, 3, dtype=jnp.int32), PAGE)
        row_pos = jnp.tile(positions, 2)
        row_level = INNER - 1 + row_slot
        row_ok = row_pos < jnp.repeat(leaf_counts[1:], PAGE)
        earlier = key_level[None, :] < row_level[:, None]
        same_page = (key_level[None, :] == row_level[:, None]) & (key_pos[None, :] <= row_pos[:, None])
        allowed_leaf = row_ok[:, None] & key_ok[None, :] & (earlier | same_page)
        grad_q_leaf, grad_k_leaf, grad_v_leaf = attend(own_queries[1:].reshape(2 * PAGE, KVH, group_size, HD), own_grads[1:].reshape(2 * PAGE, KVH, group_size, HD), own_norms[:, :, 1:].reshape(KVH, group_size, 2 * PAGE), own_deltas[:, :, 1:].reshape(KVH, group_size, 2 * PAGE), path_keys, path_values, allowed_leaf)
        owned_levels = path_ids[:INNER] == own_page
        inner_level = jnp.sum(jnp.where(owned_levels, level_ids[:INNER], 0))
        has_inner = jnp.any(owned_levels)
        inner_key_level = key_level[:inner_rows]
        inner_key_pos = key_pos[:inner_rows]
        inner_earlier = inner_key_level[None, :] < inner_level
        inner_same = (inner_key_level[None, :] == inner_level) & (inner_key_pos[None, :] <= positions[:, None])
        allowed_inner = has_inner & (positions < leaf_counts[0])[:, None] & key_ok[None, :inner_rows] & (inner_earlier | inner_same)
        grad_q_inner, grad_k_inner, grad_v_inner = attend(own_queries[0], own_grads[0], own_norms[:, :, 0], own_deltas[:, :, 0], path_keys[:inner_rows], path_values[:inner_rows], allowed_inner)
        grad_k_path = jnp.concatenate([grad_k_leaf[:inner_rows] + grad_k_inner, grad_k_leaf[inner_rows:]])
        grad_v_path = jnp.concatenate([grad_v_leaf[:inner_rows] + grad_v_inner, grad_v_leaf[inner_rows:]])
        grad_q_own = jnp.concatenate([grad_q_inner, grad_q_leaf])
        return (grad_q_own, grad_k_path, grad_v_path)
    leaf_ids = jnp.arange(LEAVES, dtype=jnp.int32)
    grad_q_all, grad_k_paths, grad_v_paths = lax.map(one_leaf, leaf_ids)
    flat_ids = ancestors.reshape(LEAVES * LEVELS)
    key_total = jnp.zeros((PAGES, PAGE, KVH, HD), jnp.float32).at[flat_ids].add(grad_k_paths.reshape(LEAVES * LEVELS, PAGE, KVH, HD))
    value_total = jnp.zeros((PAGES, PAGE, KVH, HD), jnp.float32).at[flat_ids].add(grad_v_paths.reshape(LEAVES * LEVELS, PAGE, KVH, HD))
    grad_queries = grad_q_all.reshape(ROWS, QH * HD).astype(jnp.bfloat16)
    grad_keys = key_total.reshape(ROWS, KVH * HD).astype(jnp.bfloat16)
    grad_values = value_total.reshape(ROWS, KVH * HD).astype(jnp.bfloat16)
    grad_input = jnp.dot(grad_values, w_value.T, preferred_element_type=jnp.float32).astype(jnp.bfloat16)
    return (grad_queries, grad_keys, grad_values, grad_input)
```

```python
import functools
import math

import jax
import jax.numpy as jnp
from jax import lax
from jax.experimental import pallas as pl
from jax.experimental.pallas import tpu as pltpu
from jax.sharding import PartitionSpec as P

HD = 128
PAGE = 128
SLOTS = 3
INNER = 3
LOG2E = math.log2(math.e)
SCALE = 1.0 / math.sqrt(HD)
BF16 = jnp.bfloat16
F32 = jnp.float32
I32 = jnp.int32
VMEM_LIMIT = 40 << 20
SMALL_LIMIT = 16 << 20


def params(limit=VMEM_LIMIT):
    return pltpu.CompilerParams(vmem_limit_bytes=limit)


def dot_t(left, right):
    return lax.dot_general(left, right, (((1,), (1,)), ((), ())), preferred_element_type=F32)


def dot_n(left, right):
    return lax.dot_general(left, right, (((1,), (0,)), ((), ())), preferred_element_type=F32)


def dot_rows(left, right):
    return lax.dot_general(left, right, (((0,), (0,)), ((), ())), preferred_element_type=F32)


class Path:
    def __init__(self, ids_ref):
        self.pages = [ids_ref[j] for j in range(INNER)]
        self.own = ids_ref[INNER] - 1
        self.leaf = self.own // SLOTS
        self.core = lax.rem(self.leaf, 2)
        self.owns = [self.pages[j] == self.own for j in range(INNER)]
        self.has_inner = self.owns[0] | self.owns[1] | self.owns[2]

    def owner(self, level):
        return self.pages[level] // SLOTS

    def same(self, level, shift):
        return (self.owner(level) >> shift) == (self.leaf >> shift)


def row_ok(count, rows, width):
    return lax.broadcasted_iota(I32, (rows, width), 0) < count


def whole(shape):
    return pl.BlockSpec(shape, lambda *_: (0,) * len(shape))


def small(body, ids, counts, arrays, outs, aliases=None):
    return pl.pallas_call(
        body,
        out_shape=tuple(jax.ShapeDtypeStruct(s, d) for s, d in outs),
        grid_spec=pltpu.PrefetchScalarGridSpec(
            num_scalar_prefetch=2,
            grid=(1,),
            in_specs=[whole(a.shape) for a in arrays],
            out_specs=tuple(whole(s) for s, _ in outs),
        ),
        compiler_params=params(SMALL_LIMIT),
    )(ids, counts, *arrays)


def probabilities(q, g, k, v, norm, delta, keep):
    p = jnp.exp2(dot_t(q, k) * (SCALE * LOG2E) - norm)
    if keep is not None:
        p = jnp.where(keep, p, 0.0)
    ds = p * (dot_t(g, v) - delta)
    return p.astype(BF16), ds.astype(BF16)


def own_pages_kernel(group, ids, counts, q, g, k, v, norms, deltas, l2_own, l2_far, *refs):
    dq, dk, dv, dv12, own0, send2 = refs[-7:-1]
    acc = refs[-1]
    path = Path(ids)
    n0 = jnp.where(path.has_inner, counts[0], 0)
    ok = [row_ok(n, PAGE, HD) for n in (n0, counts[1], counts[2])]
    ok3 = jnp.concatenate(ok, axis=0)
    zero = jnp.zeros((), BF16)
    kk = jnp.where(ok3, k[...], zero)
    vv = jnp.where(ok3, v[...], zero)
    mine = path.owns[2]
    k2 = jnp.where(mine, l2_own[0], l2_far[0])
    v2 = jnp.where(mine, l2_own[1], l2_far[1])
    k0, v0 = kk[:PAGE], vv[:PAGE]
    k3 = jnp.concatenate([kk[PAGE:], k2], axis=0)
    v3 = jnp.concatenate([vv[PAGE:], v2], axis=0)
    keep0 = lax.broadcasted_iota(I32, (PAGE, PAGE), 1) <= lax.broadcasted_iota(
        I32, (PAGE, PAGE), 0
    )
    col = lax.broadcasted_iota(I32, (2 * PAGE, 3 * PAGE), 1)
    row = lax.broadcasted_iota(I32, (2 * PAGE, 3 * PAGE), 0)
    keep3 = (col <= row) | (col >= 2 * PAGE)
    norm_t = (norms[...] * LOG2E).T
    delta_t = deltas[...].T
    acc[...] = jnp.zeros_like(acc)
    for h in range(group):
        lanes = slice(h * HD, (h + 1) * HD)
        qh = jnp.where(ok3, q[:, lanes], zero)
        gh = jnp.where(ok3, g[:, lanes], zero)
        norm, delta = norm_t[:, h : h + 1], delta_t[:, h : h + 1]
        p, ds = probabilities(
            qh[:PAGE], gh[:PAGE], k0, v0, norm[:PAGE], delta[:PAGE], keep0
        )
        dq[:PAGE, lanes] = dot_n(ds, k0)
        acc[0, :, :PAGE] += dot_rows(qh[:PAGE], ds)
        acc[1, :, :PAGE] += dot_rows(gh[:PAGE], p)
        p, ds = probabilities(
            qh[PAGE:], gh[PAGE:], k3, v3, norm[PAGE:], delta[PAGE:], keep3
        )
        dq[PAGE:, lanes] = dot_n(ds, k3)
        acc[0, :, PAGE:] += dot_rows(qh[PAGE:], ds)
        acc[1, :, PAGE:] += dot_rows(gh[PAGE:], p)
    grad_k = acc[0].T * SCALE
    grad_v = acc[1].T
    ok12 = ok3[PAGE:]
    dk[:PAGE] = jnp.zeros((PAGE, HD), BF16)
    dv[:PAGE] = jnp.zeros((PAGE, HD), BF16)
    dk[PAGE:] = jnp.where(ok12, grad_k[PAGE : 3 * PAGE], 0.0).astype(BF16)
    low = jnp.where(ok12, grad_v[PAGE : 3 * PAGE], 0.0).astype(BF16)
    dv[PAGE:] = low
    dv12[...] = low
    own0[0] = grad_k[:PAGE] + jnp.where(mine, grad_k[3 * PAGE :], 0.0)
    own0[1] = grad_v[:PAGE] + jnp.where(mine, grad_v[3 * PAGE :], 0.0)
    send2[0] = grad_k[3 * PAGE :].astype(BF16)
    send2[1] = grad_v[3 * PAGE :].astype(BF16)


def shared_pages_kernel(group, ids, counts, q, g, norms, deltas, mine, far, prev, *refs):
    dq, keep_out, send_out = refs[-4:-1]
    acc = refs[-1]
    path = Path(ids)
    n0 = jnp.where(path.has_inner, counts[0], 0)
    ok3 = jnp.concatenate([row_ok(n, PAGE, HD) for n in (n0, counts[1], counts[2])], axis=0)
    zero = jnp.zeros((), BF16)
    first = path.core == 0
    near = jnp.concatenate([mine[0], mine[1]], axis=0)
    away = jnp.concatenate([far[0], far[1]], axis=0)
    kk = jnp.where(first, near, away)
    vv = jnp.where(first, away, near)
    col = lax.broadcasted_iota(I32, (PAGE, 2 * PAGE), 1)
    limit = jnp.where(path.owns[2], 2 * PAGE, jnp.where(path.owns[1], PAGE, 0))
    keep0 = col < limit
    norm_t = (norms[...] * LOG2E).T
    delta_t = deltas[...].T
    acc[...] = jnp.zeros_like(acc)
    for h in range(group):
        lanes = slice(h * HD, (h + 1) * HD)
        qh = jnp.where(ok3, q[:, lanes], zero)
        gh = jnp.where(ok3, g[:, lanes], zero)
        norm, delta = norm_t[:, h : h + 1], delta_t[:, h : h + 1]
        for rows, keep in ((slice(0, PAGE), keep0), (slice(PAGE, 3 * PAGE), None)):
            p, ds = probabilities(qh[rows], gh[rows], kk, vv, norm[rows], delta[rows], keep)
            total = (prev[rows, lanes] + dot_n(ds, kk)) * SCALE
            dq[rows, lanes] = jnp.where(ok3[rows], total, 0.0).astype(BF16)
            acc[0] += dot_rows(qh[rows], ds)
            acc[1] += dot_rows(gh[rows], p)
    grad_k = acc[0].T * SCALE
    grad_v = acc[1].T
    kept = jnp.where(first, grad_k, grad_v)
    sent = jnp.where(first, grad_v, grad_k).astype(BF16)
    for j in range(2):
        keep_out[j] = kept[j * PAGE : (j + 1) * PAGE]
        send_out[j] = sent[j * PAGE : (j + 1) * PAGE]


def cost(rows, keys, kv, group):
    return pl.CostEstimate(
        flops=10 * rows * keys * HD * kv * group,
        bytes_accessed=kv * group * HD * SLOTS * PAGE * 8,
        transcendentals=rows * keys * kv * group,
    )


def own_pages(start, count, group, ids, counts, q, g, k, v, norms, deltas, l2_own, l2_far, carry):
    rows = SLOTS * PAGE
    width = k.shape[1]
    wide = group * HD
    part = count * HD
    at = lambda i, *_: (0, start + i)
    col = lambda i, *_: (0, i)
    page = pl.BlockSpec((2, PAGE, HD), lambda i, *_: (0, 0, start + i))
    here = pl.BlockSpec((2, PAGE, HD), lambda i, *_: (0, 0, i))
    vec = pl.BlockSpec((group, rows), lambda i, *_: (start + i, 0))
    args = [q, g, k, v, norms, deltas, l2_own, l2_far]
    in_specs = [
        pl.BlockSpec((rows, wide), at),
        pl.BlockSpec((rows, wide), at),
        pl.BlockSpec((rows, HD), at),
        pl.BlockSpec((rows, HD), at),
        vec,
        vec,
        page,
        page,
    ]
    aliases = {}
    if carry is not None:
        aliases = {2 + len(args): 1, 3 + len(args): 2}
        args += list(carry)
        in_specs += [pl.BlockSpec(memory_space=pl.ANY)] * 2
    return pl.pallas_call(
        functools.partial(own_pages_kernel, group),
        out_shape=(
            jax.ShapeDtypeStruct((rows, count * wide), F32),
            jax.ShapeDtypeStruct((rows, width), BF16),
            jax.ShapeDtypeStruct((rows, width), BF16),
            jax.ShapeDtypeStruct((2 * PAGE, part), BF16),
            jax.ShapeDtypeStruct((2, PAGE, part), F32),
            jax.ShapeDtypeStruct((2, PAGE, part), BF16),
        ),
        grid_spec=pltpu.PrefetchScalarGridSpec(
            num_scalar_prefetch=2,
            grid=(count,),
            in_specs=in_specs,
            out_specs=(
                pl.BlockSpec((rows, wide), col),
                pl.BlockSpec((rows, HD), at),
                pl.BlockSpec((rows, HD), at),
                pl.BlockSpec((2 * PAGE, HD), col),
                here,
                here,
            ),
            scratch_shapes=[pltpu.VMEM((2, HD, 4 * PAGE), F32)],
        ),
        input_output_aliases=aliases,
        compiler_params=params(),
        cost_estimate=cost(2 * PAGE, 4 * PAGE, count, group),
    )(ids, counts, *args)


def shared_pages(start, count, group, ids, counts, q, g, norms, deltas, mine, far, prev, carry):
    rows = SLOTS * PAGE
    wide = group * HD
    part = count * HD
    at = lambda i, *_: (0, start + i)
    page = pl.BlockSpec((2, PAGE, HD), lambda i, *_: (0, 0, start + i))
    here = pl.BlockSpec((2, PAGE, HD), lambda i, *_: (0, 0, i))
    vec = pl.BlockSpec((group, rows), lambda i, *_: (start + i, 0))
    args = [q, g, norms, deltas, mine, far, prev]
    in_specs = [
        pl.BlockSpec((rows, wide), at),
        pl.BlockSpec((rows, wide), at),
        vec,
        vec,
        page,
        page,
        pl.BlockSpec((rows, wide), lambda i, *_: (0, i)),
    ]
    aliases = {}
    if carry is not None:
        aliases = {2 + len(args): 0}
        args.append(carry)
        in_specs.append(pl.BlockSpec(memory_space=pl.ANY))
    return pl.pallas_call(
        functools.partial(shared_pages_kernel, group),
        out_shape=(
            jax.ShapeDtypeStruct(q.shape, BF16),
            jax.ShapeDtypeStruct((2, PAGE, part), F32),
            jax.ShapeDtypeStruct((2, PAGE, part), BF16),
        ),
        grid_spec=pltpu.PrefetchScalarGridSpec(
            num_scalar_prefetch=2,
            grid=(count,),
            in_specs=in_specs,
            out_specs=(pl.BlockSpec((rows, wide), at), here, here),
            scratch_shapes=[pltpu.VMEM((2, HD, 2 * PAGE), F32)],
        ),
        input_output_aliases=aliases,
        compiler_params=params(),
        cost_estimate=cost(3 * PAGE, 2 * PAGE, count, group),
    )(ids, counts, *args)


def input_grad(parts, first, w, rows, carry):
    total = SLOTS * PAGE
    out_cols, depth = w.shape
    tile = next(t for t in (640, 512, 320, 128, out_cols) if out_cols % t == 0)
    lead = total - rows if carry is None else 0

    def body(flag, *refs):
        w_ref, out = refs[len(parts)], refs[-1]
        if len(parts) == 1:
            product = dot_t(refs[0][...], w_ref[...])
        else:
            mine, other = refs[0][...], refs[1][...]
            lead_half = flag[0] == 0
            half = depth // 2
            product = dot_t(jnp.where(lead_half, mine, other), w_ref[:, :half])
            product += dot_t(jnp.where(lead_half, other, mine), w_ref[:, half:])
        if lead:
            out[:lead] = jnp.zeros((lead, tile), BF16)
        out[lead:] = product.astype(BF16)

    args = [*parts, w]
    in_specs = [whole(a.shape) for a in parts] + [
        pl.BlockSpec((tile, depth), lambda i, *_: (i, 0))
    ]
    aliases = {}
    if carry is not None:
        aliases = {1 + len(args): 0}
        args.append(carry)
        in_specs.append(pl.BlockSpec(memory_space=pl.ANY))
    return pl.pallas_call(
        body,
        out_shape=jax.ShapeDtypeStruct((total, out_cols), BF16),
        grid_spec=pltpu.PrefetchScalarGridSpec(
            num_scalar_prefetch=1,
            grid=(out_cols // tile,),
            in_specs=in_specs,
            out_specs=pl.BlockSpec((rows + lead, tile), lambda i, *_: (0, i)),
        ),
        input_output_aliases=aliases,
        compiler_params=params(),
        cost_estimate=pl.CostEstimate(
            flops=2 * rows * depth * out_cols,
            bytes_accessed=2 * (depth * out_cols + rows * out_cols),
            transcendentals=0,
        ),
    )(first, *args)


def flipped(block, axis, bit):
    count = lax.axis_size(axis)
    return lax.ppermute(block, axis, [(i, i ^ bit) for i in range(count) if i ^ bit < count])


def spanning(leaves, bit_index):
    return len([j for j in range(INNER) if 2 << bit_index <= leaves >> j])


def gather_small_tree(ids, counts, own, width):
    page = ((PAGE, width), BF16)
    from_core = flipped(own, "sub", 1)

    def choose_chip(ids_ref, _, own_ref, far_ref, out):
        path = Path(ids_ref)
        for kind in range(2):
            for mine in (False, True):

                @pl.when((path.core == kind) & (path.owns[2] != mine))
                def _copy(kind=kind, mine=mine):
                    out[...] = (own_ref if mine else far_ref)[kind]

    (chip,) = small(choose_chip, ids, counts, [own, from_core], [page])
    from_pair = flipped(chip, "leaf", 1)

    def choose_pair(ids_ref, _, near_ref, far_ref, out):
        path = Path(ids_ref)
        out[...] = jnp.where(path.same(0, 1), near_ref[...], far_ref[...])

    (pair,) = small(choose_pair, ids, counts, [chip, from_pair], [page])
    from_half = flipped(pair, "leaf", 2)

    def choose_all(ids_ref, _, chip_ref, pair_far, pair_ref, half_far, out):
        path = Path(ids_ref)
        out[0] = jnp.where(path.same(0, 2), pair_ref[...], half_far[...])
        out[1] = jnp.where(path.same(1, 1), chip_ref[...], pair_far[...])

    (mine,) = small(
        choose_all,
        ids,
        counts,
        [chip, from_pair, pair, from_half],
        [((2, PAGE, width), BF16)],
    )
    return from_core, mine, flipped(mine, "sub", 1)


def reduce_small_tree(ids, counts, kept, sent):
    width = kept.shape[-1]
    two = (2, PAGE, width)
    far = flipped(sent, "sub", 1)

    def add_low(_, __, near, away, total, low):
        value = near[...] + away[...].astype(F32)
        total[...] = value
        low[...] = value.astype(BF16)

    total, low = small(add_low, ids, counts, [kept, far], [(two, F32), (two, BF16)])
    far = flipped(low, "leaf", 1)

    def add_pair(_, __, near, away, total, low):
        value = near[...] + away[...].astype(F32)
        total[...] = value
        low[...] = value[0].astype(BF16)

    total, low = small(
        add_pair, ids, counts, [total, far], [(two, F32), ((PAGE, width), BF16)]
    )
    far = flipped(low, "leaf", 2)

    def pick(ids_ref, _, near, away, out):
        path = Path(ids_ref)
        root = near[0] + away[...].astype(F32)
        out[...] = jnp.where(path.same(0, 1), root, near[1]).astype(BF16)

    (mine,) = small(pick, ids, counts, [total, far], [((PAGE, width), BF16)])
    return mine, flipped(mine, "sub", 1)


def finish_small_tree(ids, counts, own0, far2, mine, far, dk, dv):
    width = dk.shape[1]
    pieces = len(own0)

    def body(ids_ref, counts_ref, *refs):
        dk_out, dv_out, dv0_out = refs[-3:]
        path = Path(ids_ref)
        n0 = jnp.where(path.has_inner, counts_ref[0], 0)
        leads = path.core == 0
        for i in range(pieces):
            own_r, far2_r, mine_r, far_r = refs[4 * i : 4 * i + 4]
            part = own_r.shape[-1]
            cols = slice(i * part, (i + 1) * part)
            ok = row_ok(n0, PAGE, part)
            near, away = mine_r[...], far_r[...]
            k_in = jnp.where(path.owns[2], far2_r[0], jnp.where(leads, near, away))
            v_in = jnp.where(path.owns[2], far2_r[1], jnp.where(leads, away, near))
            dk_out[:, cols] = jnp.where(ok, own_r[0] + k_in.astype(F32), 0.0).astype(BF16)
            low = jnp.where(ok, own_r[1] + v_in.astype(F32), 0.0).astype(BF16)
            dv_out[:, cols] = low
            dv0_out[:, cols] = low

    args = [a for group in zip(own0, far2, mine, far) for a in group]
    return pl.pallas_call(
        body,
        out_shape=(
            jax.ShapeDtypeStruct(dk.shape, BF16),
            jax.ShapeDtypeStruct(dv.shape, BF16),
            jax.ShapeDtypeStruct((PAGE, width), BF16),
        ),
        grid_spec=pltpu.PrefetchScalarGridSpec(
            num_scalar_prefetch=2,
            grid=(1,),
            in_specs=[whole(a.shape) for a in args] + [pl.BlockSpec(memory_space=pl.ANY)] * 2,
            out_specs=(whole((PAGE, width)),) * 3,
        ),
        input_output_aliases={2 + len(args): 0, 3 + len(args): 1},
        compiler_params=params(SMALL_LIMIT),
    )(ids, counts, *args, dk, dv)


def gather_tree(ids, counts, own, width):
    leaves = lax.axis_size(("leaf", "sub"))
    owned = ids[:INNER] == ids[INNER] - 1
    pages = jnp.where(owned[:, None, None, None], own[None], jnp.zeros((), BF16))
    for bit in range(leaves.bit_length() - 1):
        active = spanning(leaves, bit)
        far = flipped(pages[:active], ("leaf", "sub"), 1 << bit)
        pages = jnp.concatenate([pages[:active] + far, pages[active:]])
    return pages


def reduce_tree(ids, parts):
    leaves = lax.axis_size(("leaf", "sub"))
    for bit in range(leaves.bit_length() - 1):
        active = spanning(leaves, bit)
        far = flipped(parts[:active], ("leaf", "sub"), 1 << bit)
        parts = jnp.concatenate([parts[:active] + far, parts[active:]])
    owned = ids[:INNER] == ids[INNER] - 1
    return jnp.sum(jnp.where(owned[:, None, None, None], parts, 0.0), axis=0)


def on_device(queries, grad_out, keys, values, log_norms, row_deltas, ancestors, counts, w_value):
    width = keys.shape[1]
    kv = width // HD
    group = queries.shape[1] // width
    leaves = lax.axis_size(("leaf", "sub"))
    ids = ancestors[0]
    rows_of = counts[0]
    pieces = 2 if kv % 2 == 0 else 1
    per = kv // pieces
    fast = leaves == 8 and lax.axis_size("sub") == 2

    def own_page(_, counts_ref, k_ref, v_ref, out):
        ok = row_ok(counts_ref[0], PAGE, width)
        out[0] = jnp.where(ok, k_ref[...], jnp.zeros((), BF16))
        out[1] = jnp.where(ok, v_ref[...], jnp.zeros((), BF16))

    own = pl.pallas_call(
        own_page,
        out_shape=jax.ShapeDtypeStruct((2, PAGE, width), BF16),
        grid_spec=pltpu.PrefetchScalarGridSpec(
            num_scalar_prefetch=2,
            grid=(1,),
            in_specs=[whole((PAGE, width))] * 2,
            out_specs=whole((2, PAGE, width)),
        ),
        compiler_params=params(SMALL_LIMIT),
    )(ids, rows_of, keys, values)
    if fast:
        l2_far, mine, theirs = gather_small_tree(ids, rows_of, own, width)
        l2_own = own
    else:
        pages = gather_tree(ids, rows_of, own, width)
        l2_own = l2_far = pages[2]
        first = lax.axis_index("sub") == 0
        mine = jnp.where(first, pages[:2, 0], pages[:2, 1])
        theirs = jnp.where(first, pages[:2, 1], pages[:2, 0])

    own_out, dk, dv = [], None, None
    for i in range(pieces):
        carry = None if dk is None else (dk, dv)
        dq, dk, dv, dv12, own0, send2 = own_pages(
            i * per, per, group, ids, rows_of, queries, grad_out, keys, values,
            log_norms, row_deltas, l2_own, l2_far, carry,
        )
        own_out.append((dq, dv12, own0, send2))

    grad_queries, shared_out = None, []
    for i in range(pieces):
        grad_queries, kept, sent = shared_pages(
            i * per, per, group, ids, rows_of, queries, grad_out, log_norms, row_deltas,
            mine, theirs, own_out[i][0], grad_queries,
        )
        shared_out.append((kept, sent))

    if fast:
        far2 = [flipped(o[3], "sub", 1) for o in own_out]
        reduced = [reduce_small_tree(ids, rows_of, *s) for s in shared_out]
        grad_keys, grad_values, dv0 = finish_small_tree(
            ids, rows_of, [o[2] for o in own_out], far2,
            [r[0] for r in reduced], [r[1] for r in reduced], dk, dv,
        )
    else:
        first = lax.axis_index("sub") == 0
        zero = jnp.zeros((), BF16)
        own0, gained = [], []
        for o, (kept, sent) in zip(own_out, shared_out):
            sent = sent.astype(F32)
            upper = jnp.stack([jnp.where(first, kept, sent), jnp.where(first, sent, kept)], axis=1)
            low = o[3].astype(F32)
            gained.append(reduce_tree(ids, jnp.concatenate([upper, low[None]])))
            owns2 = ids[2] == ids[INNER] - 1
            own0.append(o[2] - jnp.where(owns2, low, 0.0))
        total = jnp.concatenate(gained, axis=-1) + jnp.concatenate(own0, axis=-1)
        has = jnp.any(ids[:INNER] == ids[INNER] - 1)
        ok = (jnp.arange(PAGE) < jnp.where(has, rows_of[0], 0))[:, None]
        total = jnp.where(ok, total, 0.0).astype(BF16)
        grad_keys = lax.dynamic_update_slice(dk, total[0], (0, 0))
        grad_values = lax.dynamic_update_slice(dv, total[1], (0, 0))
        dv0 = total[1]

    dv12 = jnp.concatenate([o[1] for o in own_out], axis=1)
    tensor = lax.axis_size("tensor")
    side = lax.axis_index("tensor").astype(I32).reshape(1)
    if tensor == 2:
        spread = lambda part: [part, flipped(part, "tensor", 1)]
    else:
        spread = lambda part: [lax.all_gather(part, "tensor", axis=1, tiled=True)]
    grad_input = input_grad(spread(dv12), side, w_value, 2 * PAGE, None)
    grad_input = input_grad(spread(dv0), side, w_value, PAGE, grad_input)
    return (grad_queries, grad_keys, grad_values, grad_input)


def solution(mesh):
    placed = (
        P(("groups", "leaf", "sub"), "tensor"),
        P(("groups", "leaf", "sub"), "tensor"),
        P(("groups", "leaf", "sub"), "tensor"),
        P(("groups", "leaf", "sub"), "tensor"),
        P("tensor", ("groups", "leaf", "sub")),
        P("tensor", ("groups", "leaf", "sub")),
        P(("groups", "leaf", "sub"), None),
        P(("groups", "leaf", "sub"), None),
        P("tensor", None),
    )
    return jax.shard_map(
        on_device,
        mesh=mesh,
        in_specs=placed,
        out_specs=(
            P(("groups", "leaf", "sub"), "tensor"),
            P(("groups", "leaf", "sub"), "tensor"),
            P(("groups", "leaf", "sub"), "tensor"),
            P(("groups", "leaf", "sub"), "tensor"),
        ),
        check_vma=False,
    )
```

```python
import functools
import math

import jax
import jax.numpy as jnp
from jax import lax
from jax.experimental import pallas as pl
from jax.experimental.pallas import tpu as pltpu
from jax.sharding import PartitionSpec as P

HD = 128
PAGE = 128
SLOTS = 3
INNER = 3
LOG2E = math.log2(math.e)
SCALE = 1.0 / math.sqrt(HD)
BF16 = jnp.bfloat16
F32 = jnp.float32
I32 = jnp.int32
VMEM_LIMIT = 40 << 20
SMALL_LIMIT = 16 << 20


def params(limit=VMEM_LIMIT):
    return pltpu.CompilerParams(vmem_limit_bytes=limit)


def dot_t(left, right):
    return lax.dot_general(left, right, (((1,), (1,)), ((), ())), preferred_element_type=F32)


def dot_n(left, right):
    return lax.dot_general(left, right, (((1,), (0,)), ((), ())), preferred_element_type=F32)


def dot_rows(left, right):
    return lax.dot_general(left, right, (((0,), (0,)), ((), ())), preferred_element_type=F32)


class Path:
    def __init__(self, ids_ref):
        self.pages = [ids_ref[j] for j in range(INNER)]
        self.own = ids_ref[INNER] - 1
        self.leaf = self.own // SLOTS
        self.core = lax.rem(self.leaf, 2)
        self.owns = [self.pages[j] == self.own for j in range(INNER)]
        self.has_inner = self.owns[0] | self.owns[1] | self.owns[2]

    def owner(self, level):
        return self.pages[level] // SLOTS

    def same(self, level, shift):
        return (self.owner(level) >> shift) == (self.leaf >> shift)


def row_ok(count, rows, width):
    return lax.broadcasted_iota(I32, (rows, width), 0) < count


def whole(shape):
    return pl.BlockSpec(shape, lambda *_: (0,) * len(shape))


def small(body, ids, counts, arrays, outs, after=()):
    taken = 2 + len(arrays)

    def kernel(*refs):
        body(*refs[:taken], *refs[taken + len(after) :])

    return pl.pallas_call(
        kernel,
        out_shape=tuple(jax.ShapeDtypeStruct(s, d) for s, d in outs),
        grid_spec=pltpu.PrefetchScalarGridSpec(
            num_scalar_prefetch=2,
            grid=(1,),
            in_specs=[whole(a.shape) for a in arrays]
            + [pl.BlockSpec(memory_space=pl.ANY)] * len(after),
            out_specs=tuple(whole(s) for s, _ in outs),
        ),
        compiler_params=params(SMALL_LIMIT),
    )(ids, counts, *arrays, *after)


def turned(keys, queries, values, grads, norm, delta, keep):
    p = jnp.exp2(dot_t(keys, queries) * (SCALE * LOG2E) - norm)
    if keep is not None:
        p = jnp.where(keep, p, 0.0)
    ds = p * (dot_t(values, grads) - delta)
    return p.astype(BF16), ds.astype(BF16)


def stacked(ref, rows, pair):
    return jnp.concatenate([ref[rows, h * HD : (h + 1) * HD] for h in pair], axis=0)


def prepare_rows(path, counts, norms, deltas, norm_s, delta_s):
    steps, heads, _ = norm_s.shape
    lane = lax.broadcasted_iota(I32, norms.shape, 1)
    n0 = jnp.where(path.has_inner, counts[0], 0)
    slot, pos = lane // PAGE, lane % PAGE
    limit = jnp.where(slot == 0, n0, jnp.where(slot == 1, counts[1], counts[2]))
    norm = jnp.where(pos < limit, norms[...] * LOG2E, 1e30)
    for s in range(steps):
        norm_s[s] = norm[s * heads : (s + 1) * heads]
        delta_s[s] = deltas[s * heads : (s + 1) * heads]


def finish_queries(dq, prev, rows, heads, parts):
    size = rows.stop - rows.start
    for n, h in enumerate(heads):
        part = parts[:, n * size : (n + 1) * size]
        down = slice(h * HD, (h + 1) * HD)
        if prev is not None:
            part = part + prev[down, rows]
        if dq.dtype == F32:
            dq[down, rows] = part
        else:
            dq[rows, down] = (part.T * SCALE).astype(BF16)


def own_pages_kernel(heads, second, ids, counts, q, g, k, v, norms, deltas, l2_own, l2_far, *refs):
    prev = refs[0] if second else None
    dq, dk, dv, dv12, own0, send2 = refs[-14:-8]
    k0_s, v0_s, k3_s, v3_s, turn_s, acc, norm_s, delta_s = refs[-8:]
    path = Path(ids)
    mine = path.owns[2]
    step = pl.program_id(1)

    @pl.when(step == 0)
    def _start():
        n0 = jnp.where(path.has_inner, counts[0], 0)
        zero = jnp.zeros((), BF16)
        for slot, n in enumerate((n0, counts[1], counts[2])):
            rows = slice(slot * PAGE, (slot + 1) * PAGE)
            ok = row_ok(n, PAGE, HD)
            kk = jnp.where(ok, k[rows], zero)
            vv = jnp.where(ok, v[rows], zero)
            if slot == 0:
                k0_s[...] = kk
                v0_s[...] = vv
                turn_s[:, 3 * PAGE :] = kk.T
            else:
                at = slice((slot - 1) * PAGE, slot * PAGE)
                k3_s[at] = kk
                v3_s[at] = vv
                turn_s[:, at] = kk.T
        k2 = jnp.where(mine, l2_own[0], l2_far[0])
        k3_s[2 * PAGE :] = k2
        v3_s[2 * PAGE :] = jnp.where(mine, l2_own[1], l2_far[1])
        turn_s[:, 2 * PAGE : 3 * PAGE] = k2.T
        acc[...] = jnp.zeros_like(acc)
        prepare_rows(path, counts, norms, deltas, norm_s, delta_s)

    key = lax.broadcasted_iota(I32, (PAGE, 2 * PAGE), 0)
    row = lax.broadcasted_iota(I32, (PAGE, 2 * PAGE), 1)
    keep0 = key <= row % PAGE
    key = lax.broadcasted_iota(I32, (3 * PAGE, 4 * PAGE), 0)
    row = lax.broadcasted_iota(I32, (3 * PAGE, 4 * PAGE), 1) % (2 * PAGE)
    keep3 = (key <= row) | (key >= 2 * PAGE)
    top, rest = slice(0, PAGE), slice(PAGE, 3 * PAGE)
    for first in range(0, heads, 2):
        pair = (first, first + 1)

        def vectors(ref, rows):
            return jnp.concatenate(
                [ref[step, h : h + 1, rows] for h in pair], axis=1
            )

        for rows, keep, ks, vs, kt, at in (
            (top, keep0, k0_s, v0_s, slice(3 * PAGE, 4 * PAGE), slice(0, PAGE)),
            (rest, keep3, k3_s, v3_s, slice(0, 3 * PAGE), slice(PAGE, 4 * PAGE)),
        ):
            qq, gg = stacked(q, rows, pair), stacked(g, rows, pair)
            p, ds = turned(
                ks[...], qq, vs[...], gg, vectors(norm_s, rows), vectors(delta_s, rows), keep
            )
            acc[0, at] += dot_n(ds, qq)
            acc[1, at] += dot_n(p, gg)
            finish_queries(dq, prev, rows, pair, dot_n(turn_s[:, kt], ds))

    @pl.when(step == pl.num_programs(1) - 1)
    def _end():
        dk[:PAGE] = jnp.zeros((PAGE, HD), BF16)
        dv[:PAGE] = jnp.zeros((PAGE, HD), BF16)
        for slot in (1, 2):
            ok = row_ok(counts[slot], PAGE, HD)
            rows = slice(slot * PAGE, (slot + 1) * PAGE)
            dk[rows] = jnp.where(ok, acc[0, rows] * SCALE, 0.0).astype(BF16)
            low = jnp.where(ok, acc[1, rows], 0.0).astype(BF16)
            dv[rows] = low
            dv12[(slot - 1) * PAGE : slot * PAGE] = low
        k2, v2 = acc[0, 3 * PAGE :] * SCALE, acc[1, 3 * PAGE :]
        own0[0] = acc[0, :PAGE] * SCALE + jnp.where(mine, k2, 0.0)
        own0[1] = acc[1, :PAGE] + jnp.where(mine, v2, 0.0)
        send2[0] = k2.astype(BF16)
        send2[1] = v2.astype(BF16)


def shared_pages_kernel(heads, second, ids, counts, q, g, norms, deltas, mine, far, *refs):
    prev = refs[0] if second else None
    dq, keep_out, send_out = refs[-9:-6]
    k_s, v_s, turn_s, acc, norm_s, delta_s = refs[-6:]
    path = Path(ids)
    leads = path.core == 0
    step = pl.program_id(1)

    @pl.when(step == 0)
    def _start():
        for j in range(2):
            at = slice(j * PAGE, (j + 1) * PAGE)
            near, away = mine[j], far[j]
            kk = jnp.where(leads, near, away)
            k_s[at] = kk
            turn_s[:, at] = kk.T
            v_s[at] = jnp.where(leads, away, near)
        acc[...] = jnp.zeros_like(acc)
        prepare_rows(path, counts, norms, deltas, norm_s, delta_s)

    limit = jnp.where(path.owns[2], 2 * PAGE, jnp.where(path.owns[1], PAGE, 0))
    key = lax.broadcasted_iota(I32, (2 * PAGE, 3 * PAGE), 0)
    row = lax.broadcasted_iota(I32, (2 * PAGE, 3 * PAGE), 1)
    keep = (key < limit) | (row >= PAGE)
    keep = jnp.concatenate([keep, keep], axis=1)
    rows = slice(0, 3 * PAGE)
    for first in range(0, heads, 2):
        pair = (first, first + 1)

        def vectors(ref):
            return jnp.concatenate([ref[step, h : h + 1, :] for h in pair], axis=1)

        qq, gg = stacked(q, rows, pair), stacked(g, rows, pair)
        p, ds = turned(k_s[...], qq, v_s[...], gg, vectors(norm_s), vectors(delta_s), keep)
        acc[0] += dot_n(ds, qq)
        acc[1] += dot_n(p, gg)
        finish_queries(dq, prev, rows, pair, dot_n(turn_s[...], ds))

    @pl.when(step == pl.num_programs(1) - 1)
    def _end():
        for j in range(2):
            at = slice(j * PAGE, (j + 1) * PAGE)
            grad_k, grad_v = acc[0, at] * SCALE, acc[1, at]
            keep_out[j] = jnp.where(leads, grad_k, grad_v)
            send_out[j] = jnp.where(leads, grad_v, grad_k).astype(BF16)


def cost(rows, keys, group):
    return pl.CostEstimate(
        flops=40 * rows * keys * HD * group,
        bytes_accessed=group * HD * SLOTS * PAGE * 8,
        transcendentals=rows * keys * group,
    )


def steps_of(group):
    return 2 if group % 4 == 0 else 1


def query_out(queries, group, kv, second, steps):
    rows = SLOTS * PAGE
    heads = group // steps
    if second:
        shape = jax.ShapeDtypeStruct(queries.shape, BF16)
        return shape, pl.BlockSpec((rows, heads * HD), lambda i, s, *_: (0, kv * steps + s))
    shape = jax.ShapeDtypeStruct((group * HD, rows), F32)
    return shape, pl.BlockSpec((heads * HD, rows), lambda i, s, *_: (s, 0))


def head_kernel(body, kv, group, ids, counts, q, g, rest, rest_specs, prev, queries, carries,
                outs, out_specs, scratch, estimate, after):
    rows = SLOTS * PAGE
    steps = steps_of(group)
    heads = group // steps
    second = prev is not None
    block = pl.BlockSpec((rows, heads * HD), lambda i, s, *_: (0, kv * steps + s))
    args = [q, g, *rest]
    in_specs = [block, block, *rest_specs]
    if second:
        args.append(prev)
        in_specs.append(pl.BlockSpec((heads * HD, rows), lambda i, s, *_: (s, 0)))
    aliases = {}
    for out, array in carries.items():
        if array is not None:
            aliases[2 + len(args)] = out
            args.append(array)
            in_specs.append(pl.BlockSpec(memory_space=pl.ANY))
    for array in after:
        args.append(array)
        in_specs.append(pl.BlockSpec(memory_space=pl.ANY))
    dq_shape, dq_spec = query_out(q, group, kv, second, steps)
    return pl.pallas_call(
        functools.partial(body, heads, second),
        out_shape=(dq_shape, *outs),
        grid_spec=pltpu.PrefetchScalarGridSpec(
            num_scalar_prefetch=2,
            grid=(1, steps),
            in_specs=in_specs,
            out_specs=(dq_spec, *out_specs),
            scratch_shapes=[
                *scratch,
                pltpu.VMEM((steps, heads, rows), F32),
                pltpu.VMEM((steps, heads, rows), F32),
            ],
        ),
        input_output_aliases=aliases,
        compiler_params=params(),
        cost_estimate=estimate,
    )(ids, counts, *args)


def own_pages(kv, group, ids, counts, q, g, k, v, norms, deltas, l2_own, l2_far, prev, grad_q,
              grad_kv, after):
    rows = SLOTS * PAGE
    col = lambda *_: (0, kv)
    page = pl.BlockSpec((2, PAGE, HD), lambda *_: (0, 0, kv))
    vec = pl.BlockSpec((group, rows), lambda *_: (kv, 0))
    one = pl.BlockSpec((rows, HD), col)
    full = jax.ShapeDtypeStruct(k.shape, BF16)
    return head_kernel(
        own_pages_kernel, kv, group, ids, counts, q, g,
        [k, v, norms, deltas, l2_own, l2_far], [one, one, vec, vec, page, page],
        prev, q, {0: grad_q, 1: grad_kv[0], 2: grad_kv[1]},
        (
            full,
            full,
            jax.ShapeDtypeStruct((2 * PAGE, HD), BF16),
            jax.ShapeDtypeStruct((2, PAGE, HD), F32),
            jax.ShapeDtypeStruct((2, PAGE, HD), BF16),
        ),
        (one, one, whole((2 * PAGE, HD)), whole((2, PAGE, HD)), whole((2, PAGE, HD))),
        [
            pltpu.VMEM((PAGE, HD), BF16),
            pltpu.VMEM((PAGE, HD), BF16),
            pltpu.VMEM((3 * PAGE, HD), BF16),
            pltpu.VMEM((3 * PAGE, HD), BF16),
            pltpu.VMEM((HD, 4 * PAGE), BF16),
            pltpu.VMEM((2, 4 * PAGE, HD), F32),
        ],
        cost(2 * PAGE, 4 * PAGE, group), after,
    )


def shared_pages(kv, group, ids, counts, q, g, norms, deltas, mine, far, prev, grad_q, after):
    rows = SLOTS * PAGE
    page = pl.BlockSpec((2, PAGE, HD), lambda *_: (0, 0, kv))
    vec = pl.BlockSpec((group, rows), lambda *_: (kv, 0))
    return head_kernel(
        shared_pages_kernel, kv, group, ids, counts, q, g,
        [norms, deltas, mine, far], [vec, vec, page, page],
        prev, q, {0: grad_q},
        (
            jax.ShapeDtypeStruct((2, PAGE, HD), F32),
            jax.ShapeDtypeStruct((2, PAGE, HD), BF16),
        ),
        (whole((2, PAGE, HD)), whole((2, PAGE, HD))),
        [
            pltpu.VMEM((2 * PAGE, HD), BF16),
            pltpu.VMEM((2 * PAGE, HD), BF16),
            pltpu.VMEM((HD, 2 * PAGE), BF16),
            pltpu.VMEM((2, 2 * PAGE, HD), F32),
        ],
        cost(3 * PAGE, 2 * PAGE, group), after,
    )


def input_grad(near, far, side, w, rows, carry):
    total = SLOTS * PAGE
    out_cols, depth = w.shape
    tile = next(t for t in (640, 512, 320, 128, out_cols) if out_cols % t == 0)
    lead = total - rows if carry is None else 0
    count = len(near)

    def body(flag, *refs):
        w_ref, out = refs[2 * count if far else count], refs[-1]
        mine = jnp.concatenate([r[...] for r in refs[:count]], axis=1)
        if far:
            other = jnp.concatenate([r[...] for r in refs[count : 2 * count]], axis=1)
            leads = flag[0] == 0
            half = depth // 2
            product = dot_t(jnp.where(leads, mine, other), w_ref[:, :half])
            product += dot_t(jnp.where(leads, other, mine), w_ref[:, half:])
        else:
            product = dot_t(mine, w_ref[...])
        if lead:
            out[:lead] = jnp.zeros((lead, tile), BF16)
        out[lead:] = product.astype(BF16)

    args = [*near, *(far or []), w]
    in_specs = [whole(a.shape) for a in args[:-1]]
    in_specs.append(pl.BlockSpec((tile, depth), lambda i, *_: (i, 0)))
    aliases = {}
    if carry is not None:
        aliases = {1 + len(args): 0}
        args.append(carry)
        in_specs.append(pl.BlockSpec(memory_space=pl.ANY))
    return pl.pallas_call(
        body,
        out_shape=jax.ShapeDtypeStruct((total, out_cols), BF16),
        grid_spec=pltpu.PrefetchScalarGridSpec(
            num_scalar_prefetch=1,
            grid=(out_cols // tile,),
            in_specs=in_specs,
            out_specs=pl.BlockSpec((rows + lead, tile), lambda i, *_: (0, i)),
        ),
        input_output_aliases=aliases,
        compiler_params=params(),
        cost_estimate=pl.CostEstimate(
            flops=4 * rows * depth * out_cols,
            bytes_accessed=2 * (depth * out_cols + rows * out_cols),
            transcendentals=0,
        ),
    )(side, *args)


def flipped(block, axis, bit):
    count = lax.axis_size(axis)
    return lax.ppermute(block, axis, [(i, i ^ bit) for i in range(count) if i ^ bit < count])


def spanning(leaves, bit_index):
    return len([j for j in range(INNER) if 2 << bit_index <= leaves >> j])


def gather_small_tree(ids, counts, own, width, meanwhile):
    page = ((PAGE, width), BF16)
    from_core = flipped(own, "sub", 1)

    def choose_chip(ids_ref, _, own_ref, far_ref, out):
        path = Path(ids_ref)
        for kind in range(2):
            for mine in (False, True):

                @pl.when((path.core == kind) & (path.owns[2] != mine))
                def _copy(kind=kind, mine=mine):
                    out[...] = (own_ref if mine else far_ref)[kind]

    (chip,) = small(choose_chip, ids, counts, [own, from_core], [page])
    from_pair = flipped(chip, "leaf", 1)

    def choose_pair(ids_ref, _, near_ref, far_ref, out):
        path = Path(ids_ref)
        out[...] = jnp.where(path.same(0, 1), near_ref[...], far_ref[...])

    after = meanwhile(from_core, chip)
    (pair,) = small(choose_pair, ids, counts, [chip, from_pair], [page], after)
    from_half = flipped(pair, "leaf", 2)

    def choose_all(ids_ref, _, chip_ref, pair_far, pair_ref, half_far, out):
        path = Path(ids_ref)
        out[0] = jnp.where(path.same(0, 2), pair_ref[...], half_far[...])
        out[1] = jnp.where(path.same(1, 1), chip_ref[...], pair_far[...])

    after = meanwhile(from_core, pair)
    (mine,) = small(
        choose_all,
        ids,
        counts,
        [chip, from_pair, pair, from_half],
        [((2, PAGE, width), BF16)],
        after,
    )
    theirs = flipped(mine, "sub", 1)
    return from_core, mine, theirs


def reduce_small_tree(ids, counts, kept, sent):
    count = len(kept)
    part = kept[0].shape[-1]
    width = part * count
    two = (2, PAGE, width)
    far = [flipped(s, "sub", 1) for s in sent]

    def add_low(_, __, *refs):
        total, low = refs[-2:]
        for i in range(count):
            cols = slice(i * part, (i + 1) * part)
            value = refs[i][...] + refs[count + i][...].astype(F32)
            total[:, :, cols] = value
            low[:, :, cols] = value.astype(BF16)

    total, low = small(add_low, ids, counts, [*kept, *far], [(two, F32), (two, BF16)])
    far = flipped(low, "leaf", 1)

    def add_pair(_, __, near, away, total, low):
        value = near[...] + away[...].astype(F32)
        total[...] = value
        low[...] = value[0].astype(BF16)

    total, low = small(
        add_pair, ids, counts, [total, far], [(two, F32), ((PAGE, width), BF16)]
    )
    far = flipped(low, "leaf", 2)

    def pick(ids_ref, _, near, away, out):
        path = Path(ids_ref)
        root = near[0] + away[...].astype(F32)
        out[...] = jnp.where(path.same(0, 1), root, near[1]).astype(BF16)

    (mine,) = small(pick, ids, counts, [total, far], [((PAGE, width), BF16)])
    return mine, flipped(mine, "sub", 1)


def finish_small_tree(ids, counts, own0, far2, mine, far, dk, dv):
    width = dk.shape[1]
    heads, groups = len(own0), len(mine)
    part = width // groups

    def body(ids_ref, counts_ref, *refs):
        own_r, far2_r = refs[:heads], refs[heads : 2 * heads]
        mine_r = refs[2 * heads : 2 * heads + groups]
        far_r = refs[2 * heads + groups : 2 * (heads + groups)]
        dk_out, dv_out, dv0_out = refs[-3:]
        path = Path(ids_ref)
        n0 = jnp.where(path.has_inner, counts_ref[0], 0)
        leads = path.core == 0
        ok = row_ok(n0, PAGE, HD)
        for i in range(heads):
            cols = slice(i * HD, (i + 1) * HD)
            n, at = divmod(i * HD, part)
            near, away = mine_r[n][:, at : at + HD], far_r[n][:, at : at + HD]
            k_in = jnp.where(path.owns[2], far2_r[i][0], jnp.where(leads, near, away))
            v_in = jnp.where(path.owns[2], far2_r[i][1], jnp.where(leads, away, near))
            dk_out[:, cols] = jnp.where(ok, own_r[i][0] + k_in.astype(F32), 0.0).astype(BF16)
            low = jnp.where(ok, own_r[i][1] + v_in.astype(F32), 0.0).astype(BF16)
            dv_out[:, cols] = low
            dv0_out[:, cols] = low

    args = [*own0, *far2, *mine, *far]
    return pl.pallas_call(
        body,
        out_shape=(
            jax.ShapeDtypeStruct(dk.shape, BF16),
            jax.ShapeDtypeStruct(dv.shape, BF16),
            jax.ShapeDtypeStruct((PAGE, width), BF16),
        ),
        grid_spec=pltpu.PrefetchScalarGridSpec(
            num_scalar_prefetch=2,
            grid=(1,),
            in_specs=[whole(a.shape) for a in args] + [pl.BlockSpec(memory_space=pl.ANY)] * 2,
            out_specs=(whole((PAGE, width)),) * 3,
        ),
        input_output_aliases={2 + len(args): 0, 3 + len(args): 1},
        compiler_params=params(SMALL_LIMIT),
    )(ids, counts, *args, dk, dv)


def gather_tree(ids, counts, own, width):
    leaves = lax.axis_size(("leaf", "sub"))
    owned = ids[:INNER] == ids[INNER] - 1
    pages = jnp.where(owned[:, None, None, None], own[None], jnp.zeros((), BF16))
    for bit in range(leaves.bit_length() - 1):
        active = spanning(leaves, bit)
        far = flipped(pages[:active], ("leaf", "sub"), 1 << bit)
        pages = jnp.concatenate([pages[:active] + far, pages[active:]])
    return pages


def reduce_tree(ids, parts):
    leaves = lax.axis_size(("leaf", "sub"))
    for bit in range(leaves.bit_length() - 1):
        active = spanning(leaves, bit)
        far = flipped(parts[:active], ("leaf", "sub"), 1 << bit)
        parts = jnp.concatenate([parts[:active] + far, parts[active:]])
    owned = ids[:INNER] == ids[INNER] - 1
    return jnp.sum(jnp.where(owned[:, None, None, None], parts, 0.0), axis=0)


def on_device(queries, grad_out, keys, values, log_norms, row_deltas, ancestors, counts, w_value):
    width = keys.shape[1]
    kv = width // HD
    group = queries.shape[1] // width
    leaves = lax.axis_size(("leaf", "sub"))
    ids = ancestors[0]
    rows_of = counts[0]
    fast = leaves == 8 and lax.axis_size("sub") == 2
    queries, grad_out, keys, values, log_norms, row_deltas, w_value = (
        pltpu.with_memory_space_constraint(a, pltpu.HBM)
        for a in (queries, grad_out, keys, values, log_norms, row_deltas, w_value)
    )

    def own_page(_, counts_ref, k_ref, v_ref, out):
        ok = row_ok(counts_ref[0], PAGE, width)
        out[0] = jnp.where(ok, k_ref[...], jnp.zeros((), BF16))
        out[1] = jnp.where(ok, v_ref[...], jnp.zeros((), BF16))

    own = pl.pallas_call(
        own_page,
        out_shape=jax.ShapeDtypeStruct((2, PAGE, width), BF16),
        grid_spec=pltpu.PrefetchScalarGridSpec(
            num_scalar_prefetch=2,
            grid=(1,),
            in_specs=[whole((PAGE, width))] * 2,
            out_specs=whole((2, PAGE, width)),
        ),
        compiler_params=params(SMALL_LIMIT),
    )(ids, rows_of, keys, values)

    state = {"gq": None, "kv": (None, None), "l2": (own, own)}
    own_out, shared_out, turned_q = {}, {}, {}

    def run_own(i, after=()):
        prev = turned_q.get(i)
        dq, dk, dv, *rest = own_pages(
            i, group, ids, rows_of, queries, grad_out, keys, values, log_norms, row_deltas,
            *state["l2"], prev, None if prev is None else state["gq"], state["kv"], after,
        )
        state["kv"] = (dk, dv)
        if prev is None:
            turned_q[i] = dq
        else:
            state["gq"] = dq
        own_out[i] = rest

    def run_shared(i, after=()):
        prev = turned_q.get(i)
        dq, *rest = shared_pages(
            i, group, ids, rows_of, queries, grad_out, log_norms, row_deltas, *state["shared"],
            prev, None if prev is None else state["gq"], after,
        )
        if prev is None:
            turned_q[i] = dq
        else:
            state["gq"] = dq
        shared_out[i] = rest

    last = kv - 1 if fast and kv > 1 else kv
    if fast:
        todo = list(range(last))
        quota = [1, len(todo) - 1]

        def meanwhile(from_core, token):
            state["l2"] = (own, from_core)
            done = ()
            for _ in range(quota.pop(0)):
                run_own(todo[0], (token,))
                done = (own_out[todo.pop(0)][1],)
            return done

        _, mine, theirs = gather_small_tree(ids, rows_of, own, width, meanwhile)
    else:
        pages = gather_tree(ids, rows_of, own, width)
        state["l2"] = (pages[2], pages[2])
        first = lax.axis_index("sub") == 0
        mine = jnp.where(first, pages[:2, 0], pages[:2, 1])
        theirs = jnp.where(first, pages[:2, 1], pages[:2, 0])
        for i in range(last):
            run_own(i)
    state["shared"] = (mine, theirs)
    for i in range(kv):
        run_shared(i)
    for i in range(last, kv):
        run_own(i, (shared_out[kv - 1][0],))

    if fast:
        far2 = [flipped(own_out[i][2], "sub", 1) for i in range(kv)]
        cuts = [range(0, kv // 2), range(kv // 2, kv)] if kv > 1 else [range(kv)]
        reduced = [
            reduce_small_tree(
                ids, rows_of, [shared_out[i][0] for i in cut], [shared_out[i][1] for i in cut]
            )
            for cut in cuts
        ]
        grad_keys, grad_values, dv0 = finish_small_tree(
            ids, rows_of, [own_out[i][1] for i in range(kv)], far2,
            [r[0] for r in reduced], [r[1] for r in reduced], *state["kv"],
        )
    else:
        first = lax.axis_index("sub") == 0
        own0, gained = [], []
        for i in range(kv):
            kept, sent = shared_out[i]
            sent = sent.astype(F32)
            upper = jnp.stack([jnp.where(first, kept, sent), jnp.where(first, sent, kept)], axis=1)
            low = own_out[i][2].astype(F32)
            gained.append(reduce_tree(ids, jnp.concatenate([upper, low[None]])))
            owns2 = ids[2] == ids[INNER] - 1
            own0.append(own_out[i][1] - jnp.where(owns2, low, 0.0))
        total = jnp.concatenate(gained, axis=-1) + jnp.concatenate(own0, axis=-1)
        has = jnp.any(ids[:INNER] == ids[INNER] - 1)
        ok = (jnp.arange(PAGE) < jnp.where(has, rows_of[0], 0))[:, None]
        total = jnp.where(ok, total, 0.0).astype(BF16)
        grad_keys = lax.dynamic_update_slice(state["kv"][0], total[0], (0, 0))
        grad_values = lax.dynamic_update_slice(state["kv"][1], total[1], (0, 0))
        dv0 = total[1]

    dv12 = [own_out[i][0] for i in range(kv)]
    side = lax.axis_index("tensor").astype(I32).reshape(1)
    if lax.axis_size("tensor") == 2:
        spread = lambda parts: (parts, [flipped(p, "tensor", 1) for p in parts])
    else:
        spread = lambda parts: (
            [lax.all_gather(jnp.concatenate(parts, axis=1), "tensor", axis=1, tiled=True)],
            None,
        )
    grad_input = input_grad(*spread(dv12), side, w_value, 2 * PAGE, None)
    grad_input = input_grad(*spread([dv0]), side, w_value, PAGE, grad_input)
    return (state["gq"], grad_keys, grad_values, grad_input)


def solution(mesh):
    placed = (
        P(("groups", "leaf", "sub"), "tensor"),
        P(("groups", "leaf", "sub"), "tensor"),
        P(("groups", "leaf", "sub"), "tensor"),
        P(("groups", "leaf", "sub"), "tensor"),
        P("tensor", ("groups", "leaf", "sub")),
        P("tensor", ("groups", "leaf", "sub")),
        P(("groups", "leaf", "sub"), None),
        P(("groups", "leaf", "sub"), None),
        P("tensor", None),
    )
    return jax.shard_map(
        on_device,
        mesh=mesh,
        in_specs=placed,
        out_specs=(
            P(("groups", "leaf", "sub"), "tensor"),
            P(("groups", "leaf", "sub"), "tensor"),
            P(("groups", "leaf", "sub"), "tensor"),
            P(("groups", "leaf", "sub"), "tensor"),
        ),
        check_vma=False,
    )
```

```python
import functools
import math

import jax
import jax.numpy as jnp
from jax import lax
from jax.experimental import pallas as pl
from jax.experimental.pallas import tpu as pltpu
from jax.sharding import PartitionSpec as P

HD = 128
PAGE = 128
SLOTS = 3
INNER = 3
ROWS = SLOTS * PAGE
LOG2E = math.log2(math.e)
SCALE = 1.0 / math.sqrt(HD)
BF16 = jnp.bfloat16
F32 = jnp.float32
I32 = jnp.int32
VMEM_LIMIT = 24 << 20
BLOCKED = 1e30


def dot_t(left, right):
    return lax.dot_general(left, right, (((1,), (1,)), ((), ())), preferred_element_type=F32)


def dot_n(left, right):
    return lax.dot_general(left, right, (((1,), (0,)), ((), ())), preferred_element_type=F32)


class Path:
    def __init__(self, ids_ref):
        self.pages = [ids_ref[j] for j in range(INNER)]
        self.own = ids_ref[INNER] - 1
        self.leaf = self.own // SLOTS
        self.core = lax.rem(self.leaf, 2)
        self.owns = [self.pages[j] == self.own for j in range(INNER)]
        self.has_inner = self.owns[0] | self.owns[1] | self.owns[2]

    def owner(self, level):
        return self.pages[level] // SLOTS

    def same(self, level, shift):
        return (self.owner(level) >> shift) == (self.leaf >> shift)

    def counts(self, counts_ref):
        return jnp.where(self.has_inner, counts_ref[0], 0), counts_ref[1], counts_ref[2]


def row_ok(count, rows, width):
    return lax.broadcasted_iota(I32, (rows, width), 0) < count


def kernel_call(body, ids, counts, near, far, outs, scratch=(), aliases=None, after=(), cost=None):
    smem = pl.BlockSpec(memory_space=pltpu.SMEM)
    vmem = pl.BlockSpec(memory_space=pltpu.VMEM)
    hbm = pl.BlockSpec(memory_space=pl.ANY)
    near = [pltpu.with_memory_space_constraint(a, pltpu.VMEM) for a in near]
    first = 2
    place = {("near", i): first + i for i in range(len(near))}
    place |= {("far", i): first + len(near) + i for i in range(len(far))}
    used = first + len(near) + len(far)

    def kernel(*refs):
        body(*refs[:used], *refs[used + len(after) :])

    return pl.pallas_call(
        kernel,
        out_shape=tuple(
            pltpu.VMEM(s, d) if inside else jax.ShapeDtypeStruct(s, d) for s, d, inside in outs
        ),
        in_specs=[smem] * 2 + [vmem] * len(near) + [hbm] * (len(far) + len(after)),
        out_specs=tuple(vmem if inside else hbm for _, _, inside in outs),
        scratch_shapes=list(scratch),
        input_output_aliases={place[k]: v for k, v in (aliases or {}).items()},
        compiler_params=pltpu.CompilerParams(vmem_limit_bytes=VMEM_LIMIT),
        cost_estimate=cost,
    )(ids, counts, *near, *far, *after)


def load_all(ids, counts, queries, grads, keys, values, norms, deltas, after=()):
    arrays = [queries, grads, keys, values, norms, deltas]
    cuts = []
    for n, a in enumerate(arrays):
        pieces = 4 if a.shape[1] >= 4096 else 1
        step = a.shape[1] // pieces
        cuts += [(n, i * step, step) for i in range(pieces)]

    def body(ids_ref, counts_ref, *refs):
        src, dst, sem = refs[: len(arrays)], refs[len(arrays) : 2 * len(arrays)], refs[-1]
        copies = [
            pltpu.make_async_copy(
                src[n].at[:, start : start + size], dst[n].at[:, start : start + size], sem.at[i]
            )
            for i, (n, start, size) in enumerate(cuts)
        ]
        for c in copies:
            c.start()
        for c in copies:
            c.wait()
        norm = dst[4]
        lane = lax.broadcasted_iota(I32, norm.shape, 1)
        n0, n1, n2 = Path(ids_ref).counts(counts_ref)
        limit = jnp.where(lane < PAGE, n0, jnp.where(lane < 2 * PAGE, n1, n2))
        norm[...] = jnp.where(lane % PAGE < limit, norm[...] * (1.0 / SCALE), BLOCKED)

    return kernel_call(
        body, ids, counts, [], arrays, [(a.shape, a.dtype, True) for a in arrays],
        [pltpu.SemaphoreType.DMA((len(cuts),))], after=after,
    )


def row_terms(rows):
    high = rows.astype(BF16).astype(F32)
    rest = rows - high
    middle = rest.astype(BF16).astype(F32)
    parts = [high, middle, rest - middle]
    spare = HD - 3 * rows.shape[0]
    parts.append(jnp.zeros((spare, rows.shape[1]), F32))
    return jnp.concatenate(parts, axis=0).T.astype(BF16)


class Head:
    def __init__(self, kv, group, q, g, norms, deltas, en, ed):
        self.kv, self.group, self.q, self.g, self.en, self.ed = kv, group, q, g, en, ed
        self.heads = min(4, group)
        heads = slice(kv * group, (kv + 1) * group)
        en[...] = row_terms(norms[heads, :])
        ed[...] = row_terms(deltas[heads, :])

    def lanes(self, part, j):
        at = self.kv * self.group * HD + part * (self.heads * HD) + j * HD
        return pl.ds(pl.multiple_of(at, HD), HD)

    def stacked(self, ref, part, slot):
        rows = slice(slot * PAGE, (slot + 1) * PAGE)
        return jnp.concatenate(
            [ref[rows, self.lanes(part, j)] for j in range(self.heads)], axis=0
        )

    def deep(self, stacked, terms, part, slot):
        rows = slice(slot * PAGE, (slot + 1) * PAGE)
        column = lax.broadcasted_iota(I32, (1, HD), 1) % self.group
        extra = [
            terms[rows] * (column == part * self.heads + j).astype(F32).astype(BF16)
            for j in range(self.heads)
        ]
        return jnp.concatenate([stacked, jnp.concatenate(extra, axis=0)], axis=1)

    def scores(self, part, slot, qs, gs, k_deep, v_deep, keep):
        p = keep(jnp.exp2(dot_n(self.deep(qs, self.en, part, slot), k_deep) * (SCALE * LOG2E)))
        ds = p * dot_n(self.deep(gs, self.ed, part, slot), v_deep)
        return p.astype(BF16), ds.astype(BF16)

    def turned_at(self, part, slot):
        wide = self.heads * PAGE
        parts = self.group // self.heads
        at = ((self.kv * parts + part) * SLOTS + slot) * wide
        return pl.ds(pl.multiple_of(at, wide), wide)

    def put_queries(self, part, slot, rows_by_head, dq, prev, stage):
        rows = slice(slot * PAGE, (slot + 1) * PAGE)
        for j in range(self.heads):
            value = rows_by_head[j * PAGE : (j + 1) * PAGE]
            if stage is None:
                dq[rows, self.lanes(part, j)] = value
            else:
                if prev is not None:
                    value = value + prev[rows, self.lanes(part, j)]
                stage[rows, j * HD : (j + 1) * HD] = (value * SCALE).astype(BF16)


def set_keys(deep, upright, at, page):
    where = slice(at * PAGE, (at + 1) * PAGE)
    deep[:HD, where] = page.T
    if upright is not None:
        upright[where] = page


def run_heads(kvs, group, finish, one_part, stage, sem, gq):
    parts = group // min(4, group)
    wide = min(4, group) * HD
    copies = []
    for n, kv in enumerate(kvs):
        setup, part_body, end = one_part(n, kv)
        setup()

        def step(part, _, n=n, kv=kv, part_body=part_body):
            slot = n * parts + part
            done = finish[n]
            part_body(part, stage.at[slot] if done else None)
            if done:
                at = pl.multiple_of((kv * parts + part) * wide, wide)
                pltpu.make_async_copy(
                    stage.at[slot], gq.at[:, pl.ds(at, wide)], sem.at[slot]
                ).start()
            return 0

        lax.fori_loop(0, parts, step, 0)
        end()
        if finish[n]:
            copies += [(n * parts + p, (kv * parts + p) * wide) for p in range(parts)]
    for slot, at in copies:
        pltpu.make_async_copy(
            stage.at[slot], gq.at[:, at : at + wide], sem.at[slot]
        ).wait()


def cost(blocks, heads):
    return pl.CostEstimate(
        flops=40 * blocks * PAGE * PAGE * HD * heads,
        bytes_accessed=4 * heads * HD * ROWS,
        transcendentals=blocks * PAGE * PAGE * heads,
    )


def attend(own, kvs, group, ids, counts, loaded, pages, state, w=None, after=()):
    q, g, k, v, norms, deltas = loaded
    count = len(kvs)
    parts = group // min(4, group)
    width = count * HD
    finish = [kv in state["done"] for kv in kvs]
    fresh = [kv not in state["done"] for kv in kvs]
    kv_total = k.shape[1] // HD
    names = ["dq", "qt", "gt", "gq"]
    full = {
        "dq": (q.shape, F32, True),
        "qt": ((HD, kv_total * group * ROWS), BF16, True),
        "gt": ((HD, kv_total * group * ROWS), BF16, True),
        "gq": (q.shape, BF16, False),
    }
    if not any(finish):
        names.remove("gq")
    near = [q, g, norms, deltas, *pages]
    if own:
        near += [k, v]
    far, aliases, outs = [], {}, []
    for name in names:
        outs.append(full[name])
        array = state.get(name)
        if array is None:
            continue
        if full[name][2]:
            aliases["near", len(near)] = len(outs) - 1
            near.append(array)
        else:
            aliases["far", len(far)] = len(outs) - 1
            far.append(array)
    if own:
        outs += [
            ((2 * PAGE, width), BF16, True),
            ((2 * PAGE, width), BF16, True),
            ((2, PAGE, width), F32, True),
            ((2, PAGE, width), BF16, True),
        ]
        keys_in = 4
    else:
        outs += [((2, PAGE, width), F32, True), ((2, PAGE, width), BF16, True)]
        keys_in = 2
    if w is not None:
        far.append(w)
        outs.append((w.shape, w.dtype, True))
    scratch = [
        pltpu.VMEM((2 * HD, keys_in * PAGE), BF16),
        pltpu.VMEM((2 * HD, keys_in * PAGE), BF16),
        pltpu.VMEM((keys_in * PAGE, HD), BF16),
        pltpu.VMEM((2, HD, keys_in * PAGE), F32),
        pltpu.VMEM((ROWS, HD), BF16),
        pltpu.VMEM((ROWS, HD), BF16),
        pltpu.VMEM((count * parts, ROWS, min(4, group) * HD), BF16),
        pltpu.SemaphoreType.DMA((count * parts + 1,)),
    ]

    def body(ids_ref, counts_ref, q, g, norms, deltas, *refs):
        k_deep, v_deep, k_up, acc, en, ed, stage, sem = refs[-8:]
        out_refs = refs[-8 - len(outs) : -8]
        held = dict(zip(names, out_refs))
        results = out_refs[len(names) :]
        path = Path(ids_ref)
        if w is not None:
            w_copy = pltpu.make_async_copy(
                refs[-8 - len(outs) - 1], results[-1], sem.at[count * parts]
            )
            w_copy.start()
        k_deep[HD:] = jnp.full((HD, keys_in * PAGE), -1.0, BF16)
        v_deep[HD:] = jnp.full((HD, keys_in * PAGE), -1.0, BF16)
        tall = min(4, group) * PAGE
        tri = lax.broadcasted_iota(I32, (tall, PAGE), 1) <= (
            lax.broadcasted_iota(I32, (tall, PAGE), 0) % PAGE
        )
        cols = lambda a, b: slice(a * PAGE, b * PAGE)

        def one_part(n, kv):
            head = Head(kv, group, q, g, norms, deltas, en, ed)
            lane = slice(kv * HD, (kv + 1) * HD)
            here = slice(n * HD, (n + 1) * HD)

            def setup_own():
                l2_own, l2_far, k, v = refs[:4]
                zero = jnp.zeros((), BF16)
                for slot, (at, c) in enumerate(zip((3, 0, 2), path.counts(counts_ref))):
                    ok = row_ok(c, PAGE, HD)
                    set_keys(k_deep, k_up, at, jnp.where(ok, k[cols(slot, slot + 1), lane], zero))
                    set_keys(v_deep, None, at, jnp.where(ok, v[cols(slot, slot + 1), lane], zero))
                mine = path.owns[2]
                set_keys(k_deep, k_up, 1, jnp.where(mine, l2_own[0, :, lane], l2_far[0, :, lane]))
                set_keys(v_deep, None, 1, jnp.where(mine, l2_own[1, :, lane], l2_far[1, :, lane]))
                acc[...] = jnp.zeros_like(acc)

            def setup_shared():
                mine, theirs = refs[:2]
                leads = path.core == 0
                for j in range(2):
                    near_page, far_page = mine[j, :, lane], theirs[j, :, lane]
                    set_keys(k_deep, k_up, j, jnp.where(leads, near_page, far_page))
                    set_keys(v_deep, None, j, jnp.where(leads, far_page, near_page))
                acc[...] = jnp.zeros_like(acc)

            def keep_own(slot):
                def keep(p):
                    masked = jnp.where(tri, p[:, :PAGE] if slot != 2 else p[:, 2 * PAGE :], 0.0)
                    if slot == 0:
                        return masked
                    if slot == 1:
                        return jnp.concatenate([masked, p[:, PAGE:]], axis=1)
                    return jnp.concatenate([p[:, : 2 * PAGE], masked], axis=1)

                return keep

            limit = jnp.where(path.owns[2], 2 * PAGE, jnp.where(path.owns[1], PAGE, 0))

            def keep_shared(slot):
                if slot:
                    return lambda p: p
                column = lax.broadcasted_iota(I32, (tall, 2 * PAGE), 1)
                return lambda p: jnp.where(column < limit, p, 0.0)

            spans = {0: cols(3, 4), 1: cols(0, 2), 2: cols(0, 3)} if own else dict.fromkeys(
                range(SLOTS), cols(0, 2)
            )

            def part_body(part, stage_ref):
                for slot in range(SLOTS):
                    span = spans[slot]
                    qs, gs = head.stacked(q, part, slot), head.stacked(g, part, slot)
                    keep = (keep_own if own else keep_shared)(slot)
                    p, ds = head.scores(
                        part, slot, qs, gs, k_deep[:, span], v_deep[:, span], keep
                    )
                    turn = head.turned_at(part, slot)
                    if fresh[n]:
                        qt, gt = qs.T, gs.T
                        held["qt"][:, turn] = qt
                        held["gt"][:, turn] = gt
                    else:
                        qt, gt = held["qt"][:, turn], held["gt"][:, turn]
                    acc[0, :, span] += dot_n(qt, ds)
                    acc[1, :, span] += dot_n(gt, p)
                    head.put_queries(
                        part, slot, dot_n(ds, k_up[span]), held["dq"],
                        None if fresh[n] else held["dq"], stage_ref,
                    )

            def end_own():
                dk12, dv12, own0, send2 = results[:4]
                grad = [acc[0].T * SCALE, acc[1].T]
                for at, c, to in ((0, counts_ref[1], 0), (2, counts_ref[2], 1)):
                    ok = row_ok(c, PAGE, HD)
                    for kind, out in ((0, dk12), (1, dv12)):
                        out[cols(to, to + 1), here] = jnp.where(
                            ok, grad[kind][cols(at, at + 1)], 0.0
                        ).astype(BF16)
                for kind in range(2):
                    level2 = grad[kind][cols(1, 2)]
                    own0[kind, :, here] = grad[kind][cols(3, 4)] + jnp.where(
                        path.owns[2], level2, 0.0
                    )
                    send2[kind, :, here] = level2.astype(BF16)

            def end_shared():
                kept, sent = results[:2]
                leads = path.core == 0
                grad_k, grad_v = acc[0].T * SCALE, acc[1].T
                for j in range(2):
                    a, b = grad_k[cols(j, j + 1)], grad_v[cols(j, j + 1)]
                    kept[j, :, here] = jnp.where(leads, a, b)
                    sent[j, :, here] = jnp.where(leads, b, a).astype(BF16)

            if own:
                return setup_own, part_body, end_own
            return setup_shared, part_body, end_shared

        run_heads(kvs, group, finish, one_part, stage, sem, held.get("gq"))
        if w is not None:
            w_copy.wait()

    made = kernel_call(
        body, ids, counts, near, far, outs, scratch, aliases, after,
        cost(6, group * count),
    )
    for name, array in zip(names, made):
        state[name] = array
    state["done"] = state["done"] | set(kvs)
    return made[len(names) :]


def input_grad(ids, counts, near, far, side, w, rows, carry):
    out_cols, depth = w.shape
    tile = next(t for t in (640, 512, 320, 128, out_cols) if out_cols % t == 0)
    top = 0 if rows == PAGE else PAGE
    count = len(near)
    steps = out_cols // tile
    pieces = [*near, *(far or [])]

    def body(_, counts_ref, w_ref, *refs):
        flag, out, stage, sem = refs[-4:]
        mine = jnp.concatenate([r[...] for r in refs[:count]], axis=1)
        if far:
            other = jnp.concatenate([r[...] for r in refs[count : 2 * count]], axis=1)
            leads = flag[0] == 0
            left = jnp.where(leads, mine, other)
            right = jnp.where(leads, other, mine)
            mine = jnp.concatenate([left, right], axis=1)
        copies = []
        for i in range(steps):
            at = slice(i * tile, (i + 1) * tile)
            stage[i] = dot_t(mine, w_ref[at]).astype(BF16)
            copies.append(
                pltpu.make_async_copy(stage.at[i], out.at[top : top + rows, at], sem.at[i])
            )
            copies[-1].start()
        for c in copies:
            c.wait()

    used = 1 + len(pieces)
    vmem = pl.BlockSpec(memory_space=pltpu.VMEM)
    smem = pl.BlockSpec(memory_space=pltpu.SMEM)
    hbm = pl.BlockSpec(memory_space=pl.ANY)
    more = [] if carry is None else [carry]

    def kernel(ids_ref, counts_ref, *refs):
        body(ids_ref, counts_ref, *refs[:used], refs[used], *refs[used + 1 + len(more) :])

    return pl.pallas_call(
        kernel,
        out_shape=jax.ShapeDtypeStruct((ROWS, out_cols), BF16),
        in_specs=[smem] * 2 + [vmem] * used + [smem] + [hbm] * len(more),
        out_specs=hbm,
        scratch_shapes=[
            pltpu.VMEM((steps, rows, tile), BF16),
            pltpu.SemaphoreType.DMA((steps,)),
        ],
        input_output_aliases={} if carry is None else {2 + used + 1: 0},
        compiler_params=pltpu.CompilerParams(vmem_limit_bytes=VMEM_LIMIT),
        cost_estimate=pl.CostEstimate(
            flops=4 * rows * depth * out_cols,
            bytes_accessed=2 * (depth * out_cols + rows * out_cols),
            transcendentals=0,
        ),
    )(
        ids, counts, pltpu.with_memory_space_constraint(w, pltpu.VMEM), *pieces, side, *more
    )


def flipped(block, axis, bit):
    count = lax.axis_size(axis)
    return lax.ppermute(block, axis, [(i, i ^ bit) for i in range(count) if i ^ bit < count])


def spanning(leaves, bit_index):
    return len([j for j in range(INNER) if 2 << bit_index <= leaves >> j])


def own_shared_page(ids, counts, keys, values):
    width = keys.shape[1]

    def body(_, counts_ref, k_ref, v_ref, out, held, sem):
        copies = [
            pltpu.make_async_copy(ref.at[:PAGE], held.at[i], sem.at[i])
            for i, ref in enumerate((k_ref, v_ref))
        ]
        for c in copies:
            c.start()
        for c in copies:
            c.wait()
        ok = row_ok(counts_ref[0], PAGE, width)
        for i in range(2):
            out[i] = jnp.where(ok, held[i], jnp.zeros((), BF16))

    (own,) = kernel_call(
        body, ids, counts, [], [keys, values], [((2, PAGE, width), BF16, True)],
        [pltpu.VMEM((2, PAGE, width), BF16), pltpu.SemaphoreType.DMA((2,))],
    )
    return own


def gather_small_tree(ids, counts, own, width, beside_pair, beside_half):
    page = ((PAGE, width), BF16, True)
    from_core = flipped(own, "sub", 1)

    def choose_chip(ids_ref, _, own_ref, far_ref, out):
        path = Path(ids_ref)
        for kind in range(2):
            for mine in (False, True):

                @pl.when((path.core == kind) & (path.owns[2] != mine))
                def _copy(kind=kind, mine=mine):
                    out[...] = (own_ref if mine else far_ref)[kind]

    (chip,) = kernel_call(choose_chip, ids, counts, [own, from_core], [], [page])
    from_pair = flipped(chip, "leaf", 1)

    def choose_pair(ids_ref, _, near_ref, far_ref, out):
        path = Path(ids_ref)
        out[...] = jnp.where(path.same(0, 1), near_ref[...], far_ref[...])

    after = beside_pair(from_core, chip)
    (pair,) = kernel_call(choose_pair, ids, counts, [chip, from_pair], [], [page], after=after)
    from_half = flipped(pair, "leaf", 2)

    def choose_all(ids_ref, _, chip_ref, pair_far, pair_ref, half_far, out):
        path = Path(ids_ref)
        out[0] = jnp.where(path.same(0, 2), pair_ref[...], half_far[...])
        out[1] = jnp.where(path.same(1, 1), chip_ref[...], pair_far[...])

    after = beside_half(pair)
    (mine,) = kernel_call(
        choose_all, ids, counts, [chip, from_pair, pair, from_half], [],
        [((2, PAGE, width), BF16, True)], after=after,
    )
    return mine, flipped(mine, "sub", 1)


class Reduction:
    def __init__(self, ids, counts, kept, sent):
        self.ids, self.counts, self.kept = ids, counts, kept
        self.width = kept.shape[-1]
        self.far = flipped(sent, "sub", 1)

    def call(self, body, near, outs, after):
        return kernel_call(body, self.ids, self.counts, near, [], outs, after=after)

    def over_cores(self, after=()):
        def body(_, __, near, away, total, low):
            value = near[...] + away[...].astype(F32)
            total[...] = value
            low[...] = value.astype(BF16)

        two = (2, PAGE, self.width)
        self.total, low = self.call(
            body, [self.kept, self.far], [(two, F32, True), (two, BF16, True)], after
        )
        self.far = flipped(low, "leaf", 1)
        return low

    def over_pair(self, after=()):
        def body(_, __, near, away, total, low):
            value = near[...] + away[...].astype(F32)
            total[...] = value
            low[...] = value[0].astype(BF16)

        two = (2, PAGE, self.width)
        self.total, low = self.call(
            body, [self.total, self.far], [(two, F32, True), ((PAGE, self.width), BF16, True)],
            after,
        )
        self.far = flipped(low, "leaf", 2)
        return low

    def over_half(self, after=()):
        def body(ids_ref, _, near, away, out):
            path = Path(ids_ref)
            root = near[0] + away[...].astype(F32)
            out[...] = jnp.where(path.same(0, 1), root, near[1]).astype(BF16)

        (self.mine,) = self.call(
            body, [self.total, self.far], [((PAGE, self.width), BF16, True)], after
        )
        self.far = flipped(self.mine, "sub", 1)
        return self.mine


def place_own_pages(ids, counts, parts):
    width = sum(k.shape[1] for k, _ in parts)
    near = [k for k, _ in parts] + [v for _, v in parts]

    def body(_, __, *refs):
        outs, held, sem = refs[-4:-2], refs[-2], refs[-1]
        copies = []
        for kind in range(2):
            at = 0
            for r in refs[kind * len(parts) : (kind + 1) * len(parts)]:
                held[kind, :, at : at + r.shape[1]] = r[...]
                at += r.shape[1]
            copies.append(
                pltpu.make_async_copy(held.at[kind], outs[kind].at[PAGE:], sem.at[kind])
            )
            copies[-1].start()
        for c in copies:
            c.wait()

    full = ((ROWS, width), BF16, False)
    return kernel_call(
        body, ids, counts, near, [], [full, full],
        [pltpu.VMEM((2, 2 * PAGE, width), BF16), pltpu.SemaphoreType.DMA((2,))],
    )


def finish_small_tree(ids, counts, own0, far2, mine, far, dk, dv):
    width = dk.shape[1]

    def columns(refs, at):
        for r in refs:
            if at < r.shape[-1]:
                return r, slice(at, at + HD)
            at -= r.shape[-1]

    def body(ids_ref, counts_ref, *refs):
        groups, start = [], 0
        for arrays in (own0, far2, mine, far):
            groups.append(refs[start : start + len(arrays)])
            start += len(arrays)
        dk_out, dv_out, dv0_out, held, sem = refs[-5:]
        path = Path(ids_ref)
        leads = path.core == 0
        ok = row_ok(path.counts(counts_ref)[0], PAGE, HD)
        for at in range(0, width, HD):
            own_r, c = columns(groups[0], at)
            base = [own_r[0, :, c], own_r[1, :, c]]
            low_r, c = columns(groups[1], at)
            low = [low_r[0, :, c], low_r[1, :, c]]
            near_r, c = columns(groups[2], at)
            far_r, _ = columns(groups[3], at)
            near, away = near_r[:, c], far_r[:, c]
            gained = [jnp.where(leads, near, away), jnp.where(leads, away, near)]
            for kind in range(2):
                more = jnp.where(path.owns[2], low[kind], gained[kind]).astype(F32)
                total = jnp.where(ok, base[kind] + more, 0.0).astype(BF16)
                held[kind, :, at : at + HD] = total
                if kind:
                    dv0_out[:, at : at + HD] = total
        copies = [
            pltpu.make_async_copy(held.at[i], out.at[:PAGE], sem.at[i])
            for i, out in enumerate((dk_out, dv_out))
        ]
        for c in copies:
            c.start()
        for c in copies:
            c.wait()

    full = ((ROWS, width), BF16, False)
    return kernel_call(
        body, ids, counts, [*own0, *far2, *mine, *far], [dk, dv],
        [full, full, ((PAGE, width), BF16, True)],
        [pltpu.VMEM((2, PAGE, width), BF16), pltpu.SemaphoreType.DMA((2,))],
        aliases={("far", 0): 0, ("far", 1): 1},
    )


def gather_tree(ids, own):
    leaves = lax.axis_size(("leaf", "sub"))
    owned = ids[:INNER] == ids[INNER] - 1
    pages = jnp.where(owned[:, None, None, None], own[None], jnp.zeros((), BF16))
    for bit in range(leaves.bit_length() - 1):
        active = spanning(leaves, bit)
        far = flipped(pages[:active], ("leaf", "sub"), 1 << bit)
        pages = jnp.concatenate([pages[:active] + far, pages[active:]])
    return pages


def reduce_tree(ids, parts):
    leaves = lax.axis_size(("leaf", "sub"))
    for bit in range(leaves.bit_length() - 1):
        active = spanning(leaves, bit)
        far = flipped(parts[:active], ("leaf", "sub"), 1 << bit)
        parts = jnp.concatenate([parts[:active] + far, parts[active:]])
    owned = ids[:INNER] == ids[INNER] - 1
    return jnp.sum(jnp.where(owned[:, None, None, None], parts, 0.0), axis=0)


def on_device(queries, grad_out, keys, values, log_norms, row_deltas, ancestors, counts, w_value):
    width = keys.shape[1]
    kv = width // HD
    group = queries.shape[1] // width
    leaves = lax.axis_size(("leaf", "sub"))
    hbm = lambda a: pltpu.with_memory_space_constraint(a, pltpu.HBM)
    ids = hbm(ancestors[0])
    rows_of = hbm(counts[0])
    side = lax.axis_index("tensor").astype(I32).reshape(1)
    two_sides = lax.axis_size("tensor") == 2
    queries, grad_out, keys, values, log_norms, row_deltas, w_value = map(
        hbm, (queries, grad_out, keys, values, log_norms, row_deltas, w_value)
    )
    state = {"done": frozenset()}
    loaded = []
    outcome = {}

    def load(after=()):
        loaded.extend(
            load_all(
                ids, rows_of, queries, grad_out, keys, values, log_norms, row_deltas, after
            )
        )

    def own_pages(kvs, pages, after=()):
        outcome["own", kvs] = attend(
            True, kvs, group, ids, rows_of, loaded, pages, state, after=after
        )
        return outcome["own", kvs]

    def shared_pages(kvs, pages, after=(), w=None):
        outcome["shared", kvs] = attend(
            False, kvs, group, ids, rows_of, loaded, pages, state, w, after
        )
        return outcome["shared", kvs]

    def spread(part):
        if two_sides:
            return flipped(part, "tensor", 1)
        return lax.all_gather(part, "tensor", axis=1, tiled=True)

    own = own_shared_page(ids, rows_of, keys, values)
    if leaves == 8 and lax.axis_size("sub") == 2 and kv == 4 and two_sides:
        level2 = []

        def beside_pair(from_core, chip):
            load((chip,))
            level2.extend((own, from_core))
            return (own_pages((0,), level2)[3],)

        def beside_half(pair):
            return (own_pages((1, 2), level2, (pair,))[3],)

        mine, theirs = gather_small_tree(ids, rows_of, own, width, beside_pair, beside_half)
        shared = (mine, theirs)
        first = [(0,), (1, 2)]
        far_v = [spread(outcome["own", c][1]) for c in first]
        far2 = [flipped(outcome["own", c][3], "sub", 1) for c in first]
        kept, sent, w_near = shared_pages((0, 1), shared, w=w_value)
        lead = Reduction(ids, rows_of, kept, sent)
        kept, sent = shared_pages((2, 3), shared, (*far_v, *far2))
        tail = Reduction(ids, rows_of, kept, sent)
        lead.over_cores((kept,))
        low = tail.over_cores()
        last = own_pages((3,), level2, (low,))
        far_v.append(spread(last[1]))
        far2.append(flipped(last[3], "sub", 1))
        lead.over_pair((last[3],))
        low = tail.over_pair((last[3],))
        cuts = [*first, (3,)]
        dk, dv = place_own_pages(
            ids, rows_of, [outcome["own", c][:2] for c in cuts]
        )
        lead.over_half()
        tail.over_half()
        grad_keys, grad_values, dv0 = finish_small_tree(
            ids, rows_of, [outcome["own", c][2] for c in cuts], far2,
            [lead.mine, tail.mine], [lead.far, tail.far], dk, dv,
        )
        near_v = [outcome["own", c][1] for c in cuts]
        far0 = spread(dv0)
        grad_input = input_grad(ids, rows_of, near_v, far_v, side, w_near, 2 * PAGE, None)
        grad_input = input_grad(ids, rows_of, [dv0], [far0], side, w_near, PAGE, grad_input)
        return (state["gq"], grad_keys, grad_values, grad_input)

    kvs = tuple(range(kv))
    first = lax.axis_index("sub") == 0
    path_ids = ancestors[0]
    pages = gather_tree(path_ids, own)
    load()
    dk12, dv12, own0, send2 = own_pages(kvs, (pages[2], pages[2]))
    kept, sent, w_near = shared_pages(
        kvs,
        (
            jnp.where(first, pages[:2, 0], pages[:2, 1]),
            jnp.where(first, pages[:2, 1], pages[:2, 0]),
        ),
        w=w_value,
    )
    sent = sent.astype(F32)
    upper = jnp.stack([jnp.where(first, kept, sent), jnp.where(first, sent, kept)], axis=1)
    low = send2.astype(F32)
    total = reduce_tree(path_ids, jnp.concatenate([upper, low[None]]))
    total += own0 - jnp.where(path_ids[2] == path_ids[INNER] - 1, low, 0.0)
    has = jnp.any(path_ids[:INNER] == path_ids[INNER] - 1)
    ok = (jnp.arange(PAGE) < jnp.where(has, counts[0, 0], 0))[:, None]
    total = jnp.where(ok, total, 0.0).astype(BF16)
    dk, dv = place_own_pages(ids, rows_of, [(dk12, dv12)])
    grad_keys = lax.dynamic_update_slice(dk, total[0], (0, 0))
    grad_values = lax.dynamic_update_slice(dv, total[1], (0, 0))
    if two_sides:
        pair = lambda part: ([part], [spread(part)])
    else:
        pair = lambda part: ([spread(part)], None)
    grad_input = input_grad(ids, rows_of, *pair(dv12), side, w_near, 2 * PAGE, None)
    grad_input = input_grad(ids, rows_of, *pair(total[1]), side, w_near, PAGE, grad_input)
    return (state["gq"], grad_keys, grad_values, grad_input)


def solution(mesh):
    placed = (
        P(("groups", "leaf", "sub"), "tensor"),
        P(("groups", "leaf", "sub"), "tensor"),
        P(("groups", "leaf", "sub"), "tensor"),
        P(("groups", "leaf", "sub"), "tensor"),
        P("tensor", ("groups", "leaf", "sub")),
        P("tensor", ("groups", "leaf", "sub")),
        P(("groups", "leaf", "sub"), None),
        P(("groups", "leaf", "sub"), None),
        P("tensor", None),
    )
    return jax.shard_map(
        on_device,
        mesh=mesh,
        in_specs=placed,
        out_specs=(
            P(("groups", "leaf", "sub"), "tensor"),
            P(("groups", "leaf", "sub"), "tensor"),
            P(("groups", "leaf", "sub"), "tensor"),
            P(("groups", "leaf", "sub"), "tensor"),
        ),
        check_vma=False,
    )
```

```python
import math

import jax
import jax.numpy as jnp
from jax import lax
from jax.experimental import pallas as pl
from jax.experimental.pallas import tpu as pltpu
from jax.sharding import PartitionSpec as P

HD = 128
PAGE = 128
SLOTS = 3
INNER = 3
ROWS = SLOTS * PAGE
LOG2E = math.log2(math.e)
SCALE = 1.0 / math.sqrt(HD)
BF16 = jnp.bfloat16
F32 = jnp.float32
I32 = jnp.int32
LARGE = 16 << 20
SMALL = 6 << 20
BLOCKED = 1e30


def dot_t(left, right):
    return lax.dot_general(left, right, (((1,), (1,)), ((), ())), preferred_element_type=F32)


def dot_n(left, right):
    return lax.dot_general(left, right, (((1,), (0,)), ((), ())), preferred_element_type=F32)


FACTS = 16
N0, N1, N2, OWNS2, LIMIT, LEADS, ROOT_IN_PAIR, ROOT_IN_HALF, NEXT_IN_CHIP = range(9)


def write_facts(facts, ids, counts):
    own = ids[INNER] - 1
    leaf = own // SLOTS
    owns = [ids[j] == own for j in range(INNER)]
    same = lambda level, shift: ((ids[level] // SLOTS) >> shift) == (leaf >> shift)
    number = lambda flag: jnp.where(flag, 1, 0)
    facts[N0] = jnp.where(owns[0] | owns[1] | owns[2], counts[0], 0)
    facts[N1] = counts[1]
    facts[N2] = counts[2]
    facts[OWNS2] = number(owns[2])
    facts[LIMIT] = jnp.where(owns[2], 2 * PAGE, jnp.where(owns[1], PAGE, 0))
    facts[LEADS] = number(lax.rem(leaf, 2) == 0)
    facts[ROOT_IN_PAIR] = number(same(0, 1))
    facts[ROOT_IN_HALF] = number(same(0, 2))
    facts[NEXT_IN_CHIP] = number(same(1, 1))
    for i in range(NEXT_IN_CHIP + 1, FACTS):
        facts[i] = 0


def row_ok(count, rows, width):
    return lax.broadcasted_iota(I32, (rows, width), 0) < count


def kernel_call(body, facts, near, far, outs, scratch=(), aliases=None, after=(), cost=None,
                limit=SMALL):
    smem = pl.BlockSpec(memory_space=pltpu.SMEM)
    vmem = pl.BlockSpec(memory_space=pltpu.VMEM)
    hbm = pl.BlockSpec(memory_space=pl.ANY)
    near = [pltpu.with_memory_space_constraint(a, pltpu.VMEM) for a in near]
    place = {("near", i): 1 + i for i in range(len(near))}
    place |= {("far", i): 1 + len(near) + i for i in range(len(far))}
    used = 1 + len(near) + len(far)

    def kernel(*refs):
        body(*refs[:used], *refs[used + len(after) :])

    return pl.pallas_call(
        kernel,
        out_shape=tuple(
            pltpu.VMEM(s, d) if inside else jax.ShapeDtypeStruct(s, d) for s, d, inside in outs
        ),
        in_specs=[smem] + [vmem] * len(near) + [hbm] * (len(far) + len(after)),
        out_specs=tuple(vmem if inside else hbm for _, _, inside in outs),
        scratch_shapes=list(scratch),
        input_output_aliases={place[k]: v for k, v in (aliases or {}).items()},
        compiler_params=pltpu.CompilerParams(vmem_limit_bytes=limit),
        cost_estimate=cost,
    )(pltpu.with_memory_space_constraint(facts, pltpu.SMEM), *near, *far, *after)


def start(ids, counts, keys, values):
    width = keys.shape[1]

    def body(ids_ref, counts_ref, k_ref, v_ref, facts, out, held, sem):
        copies = [
            pltpu.make_async_copy(ref.at[:PAGE], held.at[i], sem.at[i])
            for i, ref in enumerate((k_ref, v_ref))
        ]
        for c in copies:
            c.start()
        write_facts(facts, ids_ref, counts_ref)
        for c in copies:
            c.wait()
        ok = row_ok(counts_ref[0], PAGE, width)
        for i in range(2):
            out[i] = jnp.where(ok, held[i], jnp.zeros((), BF16))

    smem = pl.BlockSpec(memory_space=pltpu.SMEM)
    hbm = pl.BlockSpec(memory_space=pl.ANY)
    return pl.pallas_call(
        body,
        out_shape=(pltpu.SMEM((FACTS,), I32), pltpu.VMEM((2, PAGE, width), BF16)),
        in_specs=[smem, smem, hbm, hbm],
        out_specs=(smem, pl.BlockSpec(memory_space=pltpu.VMEM)),
        scratch_shapes=[pltpu.VMEM((2, PAGE, width), BF16), pltpu.SemaphoreType.DMA((2,))],
        compiler_params=pltpu.CompilerParams(vmem_limit_bytes=SMALL),
    )(ids, counts, keys, values)


def row_terms(rows):
    high = rows.astype(BF16).astype(F32)
    rest = rows - high
    middle = rest.astype(BF16).astype(F32)
    parts = [high, middle, rest - middle]
    spare = HD - 3 * rows.shape[0]
    parts.append(jnp.zeros((spare, rows.shape[1]), F32))
    return jnp.concatenate(parts, axis=0).T.astype(BF16)


class Head:
    def __init__(self, kv, group, q, g, norms, deltas, en, ed):
        self.kv, self.group, self.q, self.g, self.en, self.ed = kv, group, q, g, en, ed
        self.heads = min(4, group)
        self.parts = group // self.heads
        self.tall = self.heads * PAGE
        heads = slice(kv * group, (kv + 1) * group)
        en[...] = row_terms(norms[heads, :])
        ed[...] = row_terms(deltas[heads, :])

    def lanes(self, part, j):
        at = self.kv * self.group * HD + part * (self.heads * HD) + j * HD
        return pl.ds(pl.multiple_of(at, HD), HD)

    def stacked(self, ref, part, slots):
        return jnp.concatenate(
            [
                ref[slot * PAGE : (slot + 1) * PAGE, self.lanes(part, j)]
                for slot in slots
                for j in range(self.heads)
            ],
            axis=0,
        )

    def deep(self, stacked, terms, part, slots):
        column = lax.broadcasted_iota(I32, (1, HD), 1) % self.group
        picks = [
            (column == part * self.heads + j).astype(F32).astype(BF16)
            for j in range(self.heads)
        ]
        extra = [
            terms[slot * PAGE : (slot + 1) * PAGE] * pick for slot in slots for pick in picks
        ]
        return jnp.concatenate([stacked, jnp.concatenate(extra, axis=0)], axis=1)

    def turned_at(self, part, slot, count):
        at = ((self.kv * self.parts + part) * SLOTS + slot) * self.tall
        return pl.ds(pl.multiple_of(at, self.tall), self.tall * count)

    def put_queries(self, part, slot, rows_by_head, dq, add, stage):
        rows = slice(slot * PAGE, (slot + 1) * PAGE)
        for j in range(self.heads):
            value = rows_by_head[j * PAGE : (j + 1) * PAGE]
            if stage is None:
                dq[rows, self.lanes(part, j)] = value
            else:
                if add:
                    value = value + dq[rows, self.lanes(part, j)]
                stage[rows, j * HD : (j + 1) * HD] = (value * SCALE).astype(BF16)


def set_keys(deep, upright, at, page):
    where = slice(at * PAGE, (at + 1) * PAGE)
    deep[:HD, where] = page.T
    if upright is not None:
        upright[where] = page


def weigh(scores, grads, keep):
    p = keep(jnp.exp2(scores * (SCALE * LOG2E)))
    return p.astype(BF16), (p * grads).astype(BF16)


def attend(own, kvs, group, facts, inputs, pages, state, w=None, prior=(), ride=None, after=()):
    loading = "loaded" not in state
    q, g, k, v, norms, deltas = inputs if loading else state["loaded"]
    count = len(kvs)
    parts = group // min(4, group)
    tall = min(4, group) * PAGE
    wide = min(4, group) * HD
    width = count * HD
    base = prior[0].shape[1] if prior else 0
    kv_total = k.shape[1] // HD
    fresh = [kv not in state["done"] for kv in kvs]
    names = ["dq", "qt", "gt"] + ([] if all(fresh) else ["gq"])
    turned = ((HD, kv_total * group * ROWS), BF16, True)
    full = {"dq": (q.shape, F32, True), "qt": turned, "gt": turned, "gq": (q.shape, BF16, False)}

    near, far, aliases, outs = [], [], {}, []
    at_near, at_far = {}, {}

    def add_near(name, array):
        at_near[name] = len(near)
        near.append(array)

    def add_far(name, array):
        at_far[name] = len(far)
        far.append(array)

    for name in names:
        outs.append(full[name])
        if name in state:
            if full[name][2]:
                add_near(name, state[name])
                aliases["near", at_near[name]] = len(outs) - 1
            else:
                add_far(name, state[name])
                aliases["far", at_far[name]] = len(outs) - 1
    at_results = len(outs)
    if own:
        outs += [
            ((2 * PAGE, base + width), BF16, True),
            ((2 * PAGE, base + width), BF16, True),
            ((2, PAGE, base + width), F32, True),
            ((2, PAGE, base + width), BF16, True),
        ]
    else:
        outs += [
            ((2, PAGE, width), F32, True),
            ((2 if ride is None else 4, PAGE, width), BF16, True),
        ]
    at_loaded = len(outs)
    in_names = ["q", "g", "k", "v", "norms", "deltas"]
    in_arrays = [q, g, k, v, norms, deltas]
    for name, array in zip(in_names, in_arrays):
        if loading:
            add_far(name, array)
            outs.append((array.shape, array.dtype, True))
        else:
            add_near(name, array)
    at_w = len(outs)
    if w is not None:
        add_far("w", w)
        outs.append((w.shape, w.dtype, True))
    for i, page in enumerate(pages):
        add_near(("page", i), page)
    for i, array in enumerate(prior):
        add_near(("prior", i), array)
    if ride is not None:
        add_near("ride", ride[0])
    key_pages = 4 if own else 2
    scratch = [
        pltpu.VMEM((2 * HD, key_pages * PAGE), BF16),
        pltpu.VMEM((2 * HD, key_pages * PAGE), BF16),
        pltpu.VMEM((key_pages * PAGE, HD), BF16),
        pltpu.VMEM((2, HD, key_pages * PAGE), F32),
        pltpu.VMEM((ROWS, HD), BF16),
        pltpu.VMEM((ROWS, HD), BF16),
        pltpu.VMEM((count * parts, ROWS, wide), BF16),
        pltpu.SemaphoreType.DMA((count * parts,)),
        pltpu.SemaphoreType.DMA((2 * kv_total + 5,)),
    ]
    cols = lambda a, b: slice(a * PAGE, b * PAGE)

    def body(facts, *refs):
        ins, out_refs = refs[: len(near) + len(far)], refs[len(near) + len(far) : -len(scratch)]
        k_deep, v_deep, k_up, acc, en, ed, stage, sem, load_sem = refs[-len(scratch) :]
        near_ref = lambda name: ins[at_near[name]]
        far_ref = lambda name: ins[len(near) + at_far[name]]
        held = dict(zip(names, out_refs))
        results = out_refs[at_results:at_loaded]
        copies = {}
        if loading:
            into = dict(zip(in_names, out_refs[at_loaded:at_w]))

            def load(key, name, columns=None):
                src, dst = far_ref(name), into[name]
                if columns is not None:
                    src, dst = src.at[:, columns], dst.at[:, columns]
                copies[key] = pltpu.make_async_copy(src, dst, load_sem.at[len(copies)])
                copies[key].start()

            for name in in_names[2:]:
                load(name, name)
            for kv in range(kv_total):
                at = slice(kv * group * HD, (kv + 1) * group * HD)
                load(("q", kv), "q", at)
                load(("g", kv), "g", at)
        else:
            into = {name: near_ref(name) for name in in_names}
        if w is not None:
            w_copy = pltpu.make_async_copy(
                far_ref("w"), out_refs[at_w], load_sem.at[2 * kv_total + 4]
            )
            w_copy.start()
        q, g, k, v, norms, deltas = (into[name] for name in in_names)

        def arrived(*keys):
            for key in keys:
                if key in copies:
                    copies.pop(key).wait()

        k_deep[HD:] = jnp.full((HD, key_pages * PAGE), -1.0, BF16)
        v_deep[HD:] = jnp.full((HD, key_pages * PAGE), -1.0, BF16)
        for out, i in zip(results, range(len(prior))):
            out[..., :base] = near_ref(("prior", i))[...]
        if ride is not None:
            results[1][2:] = near_ref("ride")[:, :, ride[1] : ride[1] + width]
        owns2, leads = facts[OWNS2] == 1, facts[LEADS] == 1
        if loading:
            arrived("norms", "deltas", "k", "v")
            lane = lax.broadcasted_iota(I32, norms.shape, 1)
            limit = jnp.where(
                lane < PAGE, facts[N0], jnp.where(lane < 2 * PAGE, facts[N1], facts[N2])
            )
            norms[...] = jnp.where(lane % PAGE < limit, norms[...] * (1.0 / SCALE), BLOCKED)
        lower = lambda rows: lax.broadcasted_iota(I32, (rows, PAGE), 1) <= (
            lax.broadcasted_iota(I32, (rows, PAGE), 0) % PAGE
        )

        def set_pages(n, kv):
            lane = slice(kv * HD, (kv + 1) * HD)
            first, second = (near_ref(("page", i)) for i in range(2))
            if own:
                zero = jnp.zeros((), BF16)
                for slot, (at, c) in enumerate(((3, N0), (0, N1), (2, N2))):
                    ok = row_ok(facts[c], PAGE, HD)
                    rows = cols(slot, slot + 1)
                    set_keys(k_deep, k_up, at, jnp.where(ok, k[rows, lane], zero))
                    set_keys(v_deep, None, at, jnp.where(ok, v[rows, lane], zero))
                level2 = [jnp.where(owns2, first[i, :, lane], second[i, :, lane]) for i in (0, 1)]
                set_keys(k_deep, k_up, 1, level2[0])
                set_keys(v_deep, None, 1, level2[1])
            else:
                for j in range(2):
                    mine, theirs = first[j, :, lane], second[j, :, lane]
                    set_keys(k_deep, k_up, j, jnp.where(leads, mine, theirs))
                    set_keys(v_deep, None, j, jnp.where(leads, theirs, mine))
            acc[...] = jnp.zeros_like(acc)

        def turned_rows(head, part, is_fresh, qs, gs, order):
            if is_fresh:
                for name, rows in (("qt", qs), ("gt", gs)):
                    for i, slot in enumerate(order):
                        held[name][:, head.turned_at(part, slot, 1)] = rows[
                            i * tall : (i + 1) * tall
                        ].T
            return lambda name, slot, slots: held[name][:, head.turned_at(part, slot, slots)]

        def own_part(head, part, n, stage_ref):
            order = (1, 2, 0)
            qs, gs = head.stacked(q, part, order), head.stacked(g, part, order)
            qd, gd = head.deep(qs, en, part, order), head.deep(gs, ed, part, order)
            turn = turned_rows(head, part, fresh[n], qs, gs, order)
            low = lower(tall)

            def keep_first(p):
                masked = jnp.where(low, p[:tall, :PAGE], 0.0)
                return jnp.concatenate(
                    [jnp.concatenate([masked, p[:tall, PAGE:]], axis=1), p[tall:]], axis=0
                )

            pa, da = weigh(
                dot_n(qd[: 2 * tall], k_deep[:, : 2 * PAGE]),
                dot_n(gd[: 2 * tall], v_deep[:, : 2 * PAGE]),
                keep_first,
            )
            both = lambda x: jnp.concatenate([x[:tall, :PAGE], x[tall:, PAGE:]], axis=0)
            low2 = lower(2 * tall)
            pb, db = weigh(
                both(dot_n(qd[tall:], k_deep[:, 2 * PAGE :])),
                both(dot_n(gd[tall:], v_deep[:, 2 * PAGE :])),
                lambda p: jnp.where(low2, p, 0.0),
            )
            for i, (name, a, b) in enumerate((("qt", da, db), ("gt", pa, pb))):
                acc[i, :, : 2 * PAGE] += dot_n(turn(name, 1, 2), a)
                acc[i, :, cols(2, 3)] += dot_n(turn(name, 2, 1), b[:tall])
                acc[i, :, cols(3, 4)] += dot_n(turn(name, 0, 1), b[tall:])
            first = dot_n(da, k_up[: 2 * PAGE])
            put = lambda slot, rows: head.put_queries(
                part, slot, rows, held["dq"], not fresh[n], stage_ref
            )
            put(1, first[:tall])
            put(2, first[tall:] + dot_n(db[:tall], k_up[cols(2, 3)]))
            put(0, dot_n(db[tall:], k_up[cols(3, 4)]))

        def shared_part(head, part, n, stage_ref):
            order = (0, 1, 2)
            qs, gs = head.stacked(q, part, order), head.stacked(g, part, order)
            qd, gd = head.deep(qs, en, part, order), head.deep(gs, ed, part, order)
            turn = turned_rows(head, part, fresh[n], qs, gs, order)
            column = lax.broadcasted_iota(I32, (tall, 2 * PAGE), 1)
            seen = column < facts[LIMIT]

            def keep(p):
                return jnp.concatenate([jnp.where(seen, p[:tall], 0.0), p[tall:]], axis=0)

            p, ds = weigh(dot_n(qd, k_deep[...]), dot_n(gd, v_deep[...]), keep)
            acc[0] += dot_n(turn("qt", 0, SLOTS), ds)
            acc[1] += dot_n(turn("gt", 0, SLOTS), p)
            dq = dot_n(ds, k_up[...])
            for slot in range(SLOTS):
                head.put_queries(
                    part, slot, dq[slot * tall : (slot + 1) * tall], held["dq"], not fresh[n],
                    stage_ref,
                )

        def put_own(n):
            dk12, dv12, own0, send2 = results
            here = slice(base + n * HD, base + (n + 1) * HD)
            grad = [acc[0].T * SCALE, acc[1].T]
            for at, c, to in ((0, N1, 0), (2, N2, 1)):
                ok = row_ok(facts[c], PAGE, HD)
                for kind, out in ((0, dk12), (1, dv12)):
                    out[cols(to, to + 1), here] = jnp.where(
                        ok, grad[kind][cols(at, at + 1)], 0.0
                    ).astype(BF16)
            for kind in range(2):
                level2 = grad[kind][cols(1, 2)]
                own0[kind, :, here] = grad[kind][cols(3, 4)] + jnp.where(owns2, level2, 0.0)
                send2[kind, :, here] = level2.astype(BF16)

        def put_shared(n):
            kept, sent = results
            here = slice(n * HD, (n + 1) * HD)
            grad_k, grad_v = acc[0].T * SCALE, acc[1].T
            for j in range(2):
                a, b = grad_k[cols(j, j + 1)], grad_v[cols(j, j + 1)]
                kept[j, :, here] = jnp.where(leads, a, b)
                sent[j, :, here] = jnp.where(leads, b, a).astype(BF16)

        sends = []
        for n, kv in enumerate(kvs):
            arrived(("q", kv), ("g", kv))
            head = Head(kv, group, q, g, norms, deltas, en, ed)
            set_pages(n, kv)

            def step(part, _, n=n, kv=kv, head=head):
                slot = n * parts + part
                (own_part if own else shared_part)(
                    head, part, n, None if fresh[n] else stage.at[slot]
                )
                if not fresh[n]:
                    at = pl.multiple_of((kv * parts + part) * wide, wide)
                    pltpu.make_async_copy(
                        stage.at[slot], held["gq"].at[:, pl.ds(at, wide)], sem.at[slot]
                    ).start()
                return 0

            lax.fori_loop(0, parts, step, 0)
            (put_own if own else put_shared)(n)
            if not fresh[n]:
                sends += [(n * parts + p, (kv * parts + p) * wide) for p in range(parts)]
        for slot, at in sends:
            pltpu.make_async_copy(
                stage.at[slot], held["gq"].at[:, at : at + wide], sem.at[slot]
            ).wait()
        arrived(*list(copies))
        if w is not None:
            w_copy.wait()

    made = kernel_call(
        body, facts, near, far, outs, scratch, aliases, after,
        pl.CostEstimate(
            flops=240 * PAGE * PAGE * HD * group * count,
            bytes_accessed=4 * group * count * HD * ROWS,
            transcendentals=6 * PAGE * PAGE * group * count,
        ),
        LARGE,
    )
    for name, array in zip(names, made):
        state[name] = array
    state["done"] = state["done"] | set(kvs)
    if loading:
        state["loaded"] = made[at_loaded:at_w]
    results = list(made[at_results:at_loaded])
    return results + ([made[at_w]] if w is not None else [])


def input_grad(facts, near, far, side, w, rows, grads, carry):
    out_cols, depth = w.shape
    tile = next(t for t in (640, 512, 320, 128, out_cols) if out_cols % t == 0)
    top = 0 if rows == PAGE else PAGE
    steps = out_cols // tile
    width = sum(a.shape[1] for a in grads[0])
    arrays = [w, *near, *(far or []), *grads[0], *grads[1]]
    count = len(grads[0])

    def body(facts, flag, w_ref, *refs):
        near_r, refs = refs[: len(near)], refs[len(near) :]
        far_r, refs = refs[: len(far or [])], refs[len(far or []) :]
        grad_r = refs[: 2 * count]
        out, dk, dv, made, stage, sem = refs[-6:]
        made[...] = jnp.zeros_like(made)
        copies = []
        for dst, pieces in ((dk, grad_r[:count]), (dv, grad_r[count:])):
            at = 0
            for src in pieces:
                here = dst.at[top : top + rows, at : at + src.shape[1]]
                copies.append(pltpu.make_async_copy(src, here, sem.at[steps + len(copies)]))
                copies[-1].start()
                at += src.shape[1]
        full = jnp.concatenate([r[...] for r in near_r], axis=1)
        if far:
            other = jnp.concatenate([r[...] for r in far_r], axis=1)
            leads = flag[0] == 0
            full = jnp.concatenate(
                [jnp.where(leads, full, other), jnp.where(leads, other, full)], axis=1
            )
        for i in range(steps):
            at = slice(i * tile, (i + 1) * tile)
            stage[i] = dot_t(w_ref[at], full).T.astype(BF16)
            copies.append(
                pltpu.make_async_copy(stage.at[i], out.at[top : top + rows, at], sem.at[i])
            )
            copies[-1].start()
        for c in copies:
            c.wait()

    smem = pl.BlockSpec(memory_space=pltpu.SMEM)
    hbm = pl.BlockSpec(memory_space=pl.ANY)
    arrays = [pltpu.with_memory_space_constraint(a, pltpu.VMEM) for a in arrays]
    carry = list(carry or [])
    kept = jax.ShapeDtypeStruct((ROWS, width), BF16)
    return pl.pallas_call(
        body,
        out_shape=(
            jax.ShapeDtypeStruct((ROWS, out_cols), BF16), kept, kept, pltpu.VMEM((8, HD), F32)
        ),
        in_specs=[smem] * 2
        + [pl.BlockSpec(memory_space=pltpu.VMEM)] * len(arrays)
        + [hbm] * len(carry),
        out_specs=(hbm, hbm, hbm, pl.BlockSpec(memory_space=pltpu.VMEM)),
        scratch_shapes=[
            pltpu.VMEM((steps, rows, tile), BF16),
            pltpu.SemaphoreType.DMA((steps + 2 * count,)),
        ],
        input_output_aliases={2 + len(arrays) + i: i for i in range(len(carry))},
        compiler_params=pltpu.CompilerParams(vmem_limit_bytes=LARGE),
        cost_estimate=pl.CostEstimate(
            flops=4 * rows * depth * out_cols,
            bytes_accessed=2 * rows * out_cols,
            transcendentals=0,
        ),
    )(pltpu.with_memory_space_constraint(facts, pltpu.SMEM), side, *arrays, *carry)


def flipped(block, axis, bit):
    count = lax.axis_size(axis)
    return lax.ppermute(block, axis, [(i, i ^ bit) for i in range(count) if i ^ bit < count])


def spanning(leaves, bit_index):
    return len([j for j in range(INNER) if 2 << bit_index <= leaves >> j])


def gather_small_tree(facts, own, beside_pair, beside_half):
    two = (own.shape, BF16, True)
    page = (own.shape[1:], BF16, True)
    from_core = flipped(own, "sub", 1)

    def choose_chip(facts, own_ref, far_ref, out):
        for kind in range(2):
            for mine in range(2):

                @pl.when((facts[LEADS] != kind) & (facts[OWNS2] != mine))
                def _copy(kind=kind, mine=mine):
                    out[...] = (own_ref if mine else far_ref)[kind]

    (chip,) = kernel_call(choose_chip, facts, [own, from_core], [], [page])
    from_pair = flipped(chip, "leaf", 1)

    def choose_pair(facts, near_ref, far_ref, out):
        out[...] = jnp.where(facts[ROOT_IN_PAIR] == 1, near_ref[...], far_ref[...])

    after = beside_pair(from_core, chip)
    (pair,) = kernel_call(choose_pair, facts, [chip, from_pair], [], [page], after=after)
    from_half = flipped(pair, "leaf", 2)

    def choose_all(facts, chip_ref, pair_far, pair_ref, half_far, out):
        out[0] = jnp.where(facts[ROOT_IN_HALF] == 1, pair_ref[...], half_far[...])
        out[1] = jnp.where(facts[NEXT_IN_CHIP] == 1, chip_ref[...], pair_far[...])

    after = beside_half(pair)
    (mine,) = kernel_call(
        choose_all, facts, [chip, from_pair, pair, from_half], [], [two], after=after
    )
    return mine, flipped(mine, "sub", 1)


class Reduction:
    def __init__(self, facts, kept, sent):
        self.facts, self.kept = facts, kept
        self.width = sum(k.shape[-1] for k in kept)
        self.first_far = [flipped(s, "sub", 1) for s in sent]

    def call(self, body, near, outs, after):
        return kernel_call(body, self.facts, near, [], outs, after=after)

    def over_cores(self, after=()):
        count = len(self.kept)

        def body(_, *refs):
            total, low = refs[-2:]
            at = 0
            for near, away in zip(refs[:count], refs[count : 2 * count]):
                here = slice(at, at + near.shape[-1])
                at += near.shape[-1]
                value = near[...] + away[:2].astype(F32)
                total[:, :, here] = value
                low[:, :, here] = value.astype(BF16)

        two = (2, PAGE, self.width)
        self.total, low = self.call(
            body, [*self.kept, *self.first_far], [(two, F32, True), (two, BF16, True)], after
        )
        self.far = flipped(low, "leaf", 1)
        return low

    def over_pair(self, after=()):
        def body(_, near, away, total, low):
            value = near[...] + away[...].astype(F32)
            total[...] = value
            low[...] = value[0].astype(BF16)

        two = (2, PAGE, self.width)
        self.total, low = self.call(
            body, [self.total, self.far], [(two, F32, True), ((PAGE, self.width), BF16, True)],
            after,
        )
        self.far = flipped(low, "leaf", 2)
        return low

    def over_half(self, passenger=None, after=()):
        more = [] if passenger is None else [passenger]

        def body(facts, near, away, *refs):
            out = refs[-1]
            root = near[0] + away[...].astype(F32)
            out[0] = jnp.where(facts[ROOT_IN_PAIR] == 1, root, near[1]).astype(BF16)
            if more:
                half = refs[0].shape[-1]
                out[1, :, :half] = refs[0][0]
                out[1, :, half:] = refs[0][1]

        shape = (1 + len(more), PAGE, self.width)
        (self.mine,) = self.call(
            body, [self.total, self.far, *more], [(shape, BF16, True)], after
        )
        self.last_far = flipped(self.mine, "sub", 1)


def finish_small_tree(facts, own0, lead, tail):
    width = sum(a.shape[-1] for a in own0)
    half = width // 2
    near = [*own0, lead.mine, lead.last_far, tail.mine, tail.last_far, lead.first_far[0],
            tail.first_far[0]]

    def body(facts, own_r, own_last, lead_near, lead_far, tail_near, tail_far, lead2, tail2, dk, dv):
        owns2, leads = facts[OWNS2] == 1, facts[LEADS] == 1
        ok = row_ok(facts[N0], PAGE, HD)
        for at in range(0, width, HD):
            c = slice(at % half, at % half + HD)
            first = at < half
            near = (lead_near if first else tail_near)[0, :, c]
            away = (lead_far if first else tail_far)[0, :, c]
            gained = [jnp.where(leads, near, away), jnp.where(leads, away, near)]
            for kind, out in enumerate((dk, dv)):
                if first:
                    level2 = lead2[2 + kind, :, c]
                elif at + HD < width:
                    level2 = tail2[2 + kind, :, c]
                else:
                    level2 = tail_far[1, :, kind * HD : (kind + 1) * HD]
                more = jnp.where(owns2, level2, gained[kind]).astype(F32)
                if at + HD < width:
                    mine = own_r[kind, :, at : at + HD]
                else:
                    mine = own_last[kind]
                out[:, at : at + HD] = jnp.where(ok, mine + more, 0.0).astype(BF16)

    page = ((PAGE, width), BF16, True)
    return kernel_call(body, facts, near, [], [page, page])


def gather_tree(ids, own):
    leaves = lax.axis_size(("leaf", "sub"))
    owned = ids[:INNER] == ids[INNER] - 1
    pages = jnp.where(owned[:, None, None, None], own[None], jnp.zeros((), BF16))
    for bit in range(leaves.bit_length() - 1):
        active = spanning(leaves, bit)
        far = flipped(pages[:active], ("leaf", "sub"), 1 << bit)
        pages = jnp.concatenate([pages[:active] + far, pages[active:]])
    return pages


def reduce_tree(ids, parts):
    leaves = lax.axis_size(("leaf", "sub"))
    for bit in range(leaves.bit_length() - 1):
        active = spanning(leaves, bit)
        far = flipped(parts[:active], ("leaf", "sub"), 1 << bit)
        parts = jnp.concatenate([parts[:active] + far, parts[active:]])
    owned = ids[:INNER] == ids[INNER] - 1
    return jnp.sum(jnp.where(owned[:, None, None, None], parts, 0.0), axis=0)


def on_device(queries, grad_out, keys, values, log_norms, row_deltas, ancestors, counts, w_value):
    kv = keys.shape[1] // HD
    group = queries.shape[1] // keys.shape[1]
    leaves = lax.axis_size(("leaf", "sub"))
    hbm = lambda a: pltpu.with_memory_space_constraint(a, pltpu.HBM)
    side = lax.axis_index("tensor").astype(I32).reshape(1)
    two_sides = lax.axis_size("tensor") == 2
    inputs = [hbm(a) for a in (queries, grad_out, keys, values, log_norms, row_deltas)]
    facts, own = start(hbm(ancestors[0]), hbm(counts[0]), *inputs[2:4])
    state = {"done": frozenset()}

    def own_pages(kvs, pages, prior=(), after=()):
        return attend(
            True, kvs, group, facts, inputs, pages, state, prior=prior, after=after
        )

    def shared_pages(kvs, pages, w=None, ride=None, after=()):
        return attend(False, kvs, group, facts, inputs, pages, state, w, ride=ride, after=after)

    def spread(part):
        if two_sides:
            return flipped(part, "tensor", 1)
        return lax.all_gather(part, "tensor", axis=1, tiled=True)

    if leaves == 8 and lax.axis_size("sub") == 2 and kv == 4 and two_sides:
        level2, results = [], []

        def beside_pair(from_core, chip):
            level2.extend((own, from_core))
            results.append(own_pages((0,), level2, after=(chip,)))
            return (results[-1][3],)

        def beside_half(pair):
            results.append(own_pages((1, 2), level2, results[-1], (pair,)))
            return (results[-1][3],)

        shared = gather_small_tree(facts, own, beside_pair, beside_half)
        _, dv12, _, send2 = results[-1]
        far_v = [spread(dv12)]
        kept, sent, w_near = shared_pages((0, 1), shared, hbm(w_value), (send2, 0))
        lead = Reduction(facts, [kept], [sent])
        kept, sent = shared_pages((2,), shared, ride=(send2, 2 * HD), after=far_v)
        low = lead.over_cores((kept,))
        last_kept, last_sent = shared_pages((3,), shared, after=(low,))
        tail = Reduction(facts, [kept, last_kept], [sent, last_sent])
        low = lead.over_pair((last_kept,))
        last = own_pages((3,), level2, after=(low, tail.over_cores()))
        far_v.append(spread(last[1]))
        low = tail.over_pair((last[3],))
        lead.over_half(after=(low,))
        near_v = [dv12, last[1]]
        both = list(zip(results[-1], last))
        *grads, made = input_grad(facts, near_v, far_v, side, w_near, 2 * PAGE, both[:2], None)
        tail.over_half(last[3], (made,))
        dk0, dv0 = finish_small_tree(facts, both[2], lead, tail)
        grad_input, grad_keys, grad_values, _ = input_grad(
            facts, [dv0], [spread(dv0)], side, w_near, PAGE, ([dk0], [dv0]), grads
        )
        return (state["gq"], grad_keys, grad_values, grad_input)

    kvs = tuple(range(kv))
    first = lax.axis_index("sub") == 0
    path_ids = ancestors[0]
    pages = gather_tree(path_ids, own)
    dk12, dv12, own0, send2 = own_pages(kvs, (pages[2], pages[2]))
    kept, sent, w_near = shared_pages(
        kvs,
        (
            jnp.where(first, pages[:2, 0], pages[:2, 1]),
            jnp.where(first, pages[:2, 1], pages[:2, 0]),
        ),
        hbm(w_value),
    )
    sent = sent.astype(F32)
    upper = jnp.stack([jnp.where(first, kept, sent), jnp.where(first, sent, kept)], axis=1)
    low = send2.astype(F32)
    total = reduce_tree(path_ids, jnp.concatenate([upper, low[None]]))
    total += own0 - jnp.where(path_ids[2] == path_ids[INNER] - 1, low, 0.0)
    has = jnp.any(path_ids[:INNER] == path_ids[INNER] - 1)
    ok = (jnp.arange(PAGE) < jnp.where(has, counts[0, 0], 0))[:, None]
    dk0, dv0 = jnp.where(ok, total, 0.0).astype(BF16)
    if two_sides:
        pair = lambda part: ([part], [spread(part)])
    else:
        pair = lambda part: ([spread(part)], None)
    *grads, _ = input_grad(facts, *pair(dv12), side, w_near, 2 * PAGE, ([dk12], [dv12]), None)
    grad_input, grad_keys, grad_values, _ = input_grad(
        facts, *pair(dv0), side, w_near, PAGE, ([dk0], [dv0]), grads
    )
    return (state["gq"], grad_keys, grad_values, grad_input)


def solution(mesh):
    placed = (
        P(("groups", "leaf", "sub"), "tensor"),
        P(("groups", "leaf", "sub"), "tensor"),
        P(("groups", "leaf", "sub"), "tensor"),
        P(("groups", "leaf", "sub"), "tensor"),
        P("tensor", ("groups", "leaf", "sub")),
        P("tensor", ("groups", "leaf", "sub")),
        P(("groups", "leaf", "sub"), None),
        P(("groups", "leaf", "sub"), None),
        P("tensor", None),
    )
    return jax.shard_map(
        on_device,
        mesh=mesh,
        in_specs=placed,
        out_specs=(
            P(("groups", "leaf", "sub"), "tensor"),
            P(("groups", "leaf", "sub"), "tensor"),
            P(("groups", "leaf", "sub"), "tensor"),
            P(("groups", "leaf", "sub"), "tensor"),
        ),
        check_vma=False,
    )
```

```python
import math

import jax
import jax.numpy as jnp
from jax import lax
from jax.experimental import pallas as pl
from jax.experimental.pallas import tpu as pltpu
from jax.sharding import PartitionSpec as P

HD = 128
PAGE = 128
SLOTS = 3
INNER = 3
ROWS = SLOTS * PAGE
LOG2E = math.log2(math.e)
SCALE = 1.0 / math.sqrt(HD)
BF16 = jnp.bfloat16
F32 = jnp.float32
I32 = jnp.int32
LARGE = 10 << 20
SMALL = 4 << 20
SLIGHT = pl.CostEstimate(flops=1000, bytes_accessed=1000, transcendentals=0)
BLOCKED = 1e30


def dot_t(left, right):
    return lax.dot_general(left, right, (((1,), (1,)), ((), ())), preferred_element_type=F32)


def dot_n(left, right):
    return lax.dot_general(left, right, (((1,), (0,)), ((), ())), preferred_element_type=F32)


FACTS = 16
N0, N1, N2, OWNS2, LIMIT, LEADS, ROOT_IN_PAIR, ROOT_IN_HALF, NEXT_IN_CHIP = range(9)


def write_facts(facts, ids, counts):
    own = ids[INNER] - 1
    leaf = own // SLOTS
    owns = [ids[j] == own for j in range(INNER)]
    same = lambda level, shift: ((ids[level] // SLOTS) >> shift) == (leaf >> shift)
    number = lambda flag: jnp.where(flag, 1, 0)
    facts[N0] = jnp.where(owns[0] | owns[1] | owns[2], counts[0], 0)
    facts[N1] = counts[1]
    facts[N2] = counts[2]
    facts[OWNS2] = number(owns[2])
    facts[LIMIT] = jnp.where(owns[2], 2 * PAGE, jnp.where(owns[1], PAGE, 0))
    facts[LEADS] = number(lax.rem(leaf, 2) == 0)
    facts[ROOT_IN_PAIR] = number(same(0, 1))
    facts[ROOT_IN_HALF] = number(same(0, 2))
    facts[NEXT_IN_CHIP] = number(same(1, 1))
    for i in range(NEXT_IN_CHIP + 1, FACTS):
        facts[i] = 0


def row_ok(count, rows, width):
    return lax.broadcasted_iota(I32, (rows, width), 0) < count


def kernel_call(body, facts, near, far, outs, scratch=(), aliases=None, after=(), cost=None,
                limit=SMALL):
    smem = pl.BlockSpec(memory_space=pltpu.SMEM)
    vmem = pl.BlockSpec(memory_space=pltpu.VMEM)
    hbm = pl.BlockSpec(memory_space=pl.ANY)
    near = [pltpu.with_memory_space_constraint(a, pltpu.VMEM) for a in near]
    place = {("near", i): 1 + i for i in range(len(near))}
    place |= {("far", i): 1 + len(near) + i for i in range(len(far))}
    used = 1 + len(near) + len(far)

    def kernel(*refs):
        body(*refs[:used], *refs[used + len(after) :])

    return pl.pallas_call(
        kernel,
        out_shape=tuple(
            pltpu.VMEM(s, d) if inside else jax.ShapeDtypeStruct(s, d) for s, d, inside in outs
        ),
        in_specs=[smem] + [vmem] * len(near) + [hbm] * (len(far) + len(after)),
        out_specs=tuple(vmem if inside else hbm for _, _, inside in outs),
        scratch_shapes=list(scratch),
        input_output_aliases={place[k]: v for k, v in (aliases or {}).items()},
        compiler_params=pltpu.CompilerParams(vmem_limit_bytes=limit),
        cost_estimate=cost or SLIGHT,
    )(pltpu.with_memory_space_constraint(facts, pltpu.SMEM), *near, *far, *after)


def start(ids, counts, keys, values):
    width = keys.shape[1]

    def body(ids_ref, counts_ref, k_ref, v_ref, facts, out, held, sem):
        copies = [
            pltpu.make_async_copy(ref.at[:PAGE], held.at[i], sem.at[i])
            for i, ref in enumerate((k_ref, v_ref))
        ]
        for c in copies:
            c.start()
        write_facts(facts, ids_ref, counts_ref)
        for c in copies:
            c.wait()
        ok = row_ok(counts_ref[0], PAGE, width)
        for i in range(2):
            out[i] = jnp.where(ok, held[i], jnp.zeros((), BF16))

    smem = pl.BlockSpec(memory_space=pltpu.SMEM)
    hbm = pl.BlockSpec(memory_space=pl.ANY)
    return pl.pallas_call(
        body,
        out_shape=(pltpu.SMEM((FACTS,), I32), pltpu.VMEM((2, PAGE, width), BF16)),
        in_specs=[smem, smem, hbm, hbm],
        out_specs=(smem, pl.BlockSpec(memory_space=pltpu.VMEM)),
        scratch_shapes=[pltpu.VMEM((2, PAGE, width), BF16), pltpu.SemaphoreType.DMA((2,))],
        compiler_params=pltpu.CompilerParams(vmem_limit_bytes=SMALL),
    )(ids, counts, keys, values)


def row_terms(rows):
    high = rows.astype(BF16).astype(F32)
    rest = rows - high
    middle = rest.astype(BF16).astype(F32)
    parts = [high, middle, rest - middle]
    spare = HD - 3 * rows.shape[0]
    parts.append(jnp.zeros((spare, rows.shape[1]), F32))
    return jnp.concatenate(parts, axis=0).T.astype(BF16)


class Head:
    def __init__(self, kv, group, q, g, norms, deltas, en, ed):
        self.kv, self.group, self.q, self.g, self.en, self.ed = kv, group, q, g, en, ed
        self.heads = min(4, group)
        self.parts = group // self.heads
        self.tall = self.heads * PAGE
        heads = slice(kv * group, (kv + 1) * group)
        en[...] = row_terms(norms[heads, :])
        ed[...] = row_terms(deltas[heads, :])

    def lanes(self, part, j):
        at = self.kv * self.group * HD + part * (self.heads * HD) + j * HD
        return pl.ds(pl.multiple_of(at, HD), HD)

    def stacked(self, ref, part, slots):
        return jnp.concatenate(
            [
                ref[slot * PAGE : (slot + 1) * PAGE, self.lanes(part, j)]
                for slot in slots
                for j in range(self.heads)
            ],
            axis=0,
        )

    def deep(self, stacked, terms, part, slots):
        column = lax.broadcasted_iota(I32, (1, HD), 1) % self.group
        picks = [
            (column == part * self.heads + j).astype(F32).astype(BF16)
            for j in range(self.heads)
        ]
        extra = [
            terms[slot * PAGE : (slot + 1) * PAGE] * pick for slot in slots for pick in picks
        ]
        return jnp.concatenate([stacked, jnp.concatenate(extra, axis=0)], axis=1)

    def turned_at(self, part, slot, count):
        at = ((self.kv * self.parts + part) * SLOTS + slot) * self.tall
        return pl.ds(pl.multiple_of(at, self.tall), self.tall * count)

    def put_queries(self, part, slot, rows_by_head, dq, add, stage):
        rows = slice(slot * PAGE, (slot + 1) * PAGE)
        for j in range(self.heads):
            value = rows_by_head[j * PAGE : (j + 1) * PAGE]
            if stage is None:
                dq[rows, self.lanes(part, j)] = value
            else:
                if add:
                    value = value + dq[rows, self.lanes(part, j)]
                stage[rows, j * HD : (j + 1) * HD] = (value * SCALE).astype(BF16)


def set_keys(deep, upright, at, page):
    where = slice(at * PAGE, (at + 1) * PAGE)
    deep[:HD, where] = page.T
    if upright is not None:
        upright[where] = page


def weigh(scores, grads, keep):
    p = keep(jnp.exp2(scores * (SCALE * LOG2E)))
    return p.astype(BF16), (p * grads).astype(BF16)


def attend(own, kvs, group, facts, inputs, pages, state, w=None, prior=(), ride=None, after=(),
           load=240):
    loading = "loaded" not in state
    q, g, k, v, norms, deltas = inputs if loading else state["loaded"]
    count = len(kvs)
    parts = group // min(4, group)
    tall = min(4, group) * PAGE
    wide = min(4, group) * HD
    width = count * HD
    base = prior[0].shape[1] if prior else 0
    kv_total = k.shape[1] // HD
    fresh = [kv not in state["done"] for kv in kvs]
    names = ["dq", "qt", "gt"] + ([] if all(fresh) else ["gq"])
    turned = ((HD, kv_total * group * ROWS), BF16, True)
    full = {"dq": (q.shape, F32, True), "qt": turned, "gt": turned, "gq": (q.shape, BF16, False)}

    near, far, aliases, outs = [], [], {}, []
    at_near, at_far = {}, {}

    def add_near(name, array):
        at_near[name] = len(near)
        near.append(array)

    def add_far(name, array):
        at_far[name] = len(far)
        far.append(array)

    for name in names:
        outs.append(full[name])
        if name in state:
            if full[name][2]:
                add_near(name, state[name])
                aliases["near", at_near[name]] = len(outs) - 1
            else:
                add_far(name, state[name])
                aliases["far", at_far[name]] = len(outs) - 1
    at_results = len(outs)
    if own:
        outs += [
            ((2 * PAGE, base + width), BF16, True),
            ((2 * PAGE, base + width), BF16, True),
            ((2, PAGE, base + width), F32, True),
            ((2, PAGE, base + width), BF16, True),
        ]
    else:
        outs += [
            ((2, PAGE, width), F32, True),
            ((2 if ride is None else 4, PAGE, width), BF16, True),
        ]
    at_loaded = len(outs)
    in_names = ["q", "g", "k", "v", "norms", "deltas"]
    in_arrays = [q, g, k, v, norms, deltas]
    for name, array in zip(in_names, in_arrays):
        if loading:
            add_far(name, array)
            outs.append((array.shape, array.dtype, True))
        else:
            add_near(name, array)
    at_w = len(outs)
    if w is not None:
        add_far("w", w)
        outs.append((w.shape, w.dtype, True))
    for i, page in enumerate(pages):
        add_near(("page", i), page)
    for i, array in enumerate(prior):
        add_near(("prior", i), array)
    if ride is not None:
        add_near("ride", ride[0])
    key_pages = 4 if own else 2
    scratch = [
        pltpu.VMEM((2 * HD, key_pages * PAGE), BF16),
        pltpu.VMEM((2 * HD, key_pages * PAGE), BF16),
        pltpu.VMEM((key_pages * PAGE, HD), BF16),
        pltpu.VMEM((2, HD, key_pages * PAGE), F32),
        pltpu.VMEM((ROWS, HD), BF16),
        pltpu.VMEM((ROWS, HD), BF16),
        pltpu.VMEM((count * parts, ROWS, wide), BF16),
        pltpu.SemaphoreType.DMA((count * parts,)),
        pltpu.SemaphoreType.DMA((2 * kv_total + 5,)),
    ]
    cols = lambda a, b: slice(a * PAGE, b * PAGE)

    def body(facts, *refs):
        ins, out_refs = refs[: len(near) + len(far)], refs[len(near) + len(far) : -len(scratch)]
        k_deep, v_deep, k_up, acc, en, ed, stage, sem, load_sem = refs[-len(scratch) :]
        near_ref = lambda name: ins[at_near[name]]
        far_ref = lambda name: ins[len(near) + at_far[name]]
        held = dict(zip(names, out_refs))
        results = out_refs[at_results:at_loaded]
        copies = {}
        if loading:
            into = dict(zip(in_names, out_refs[at_loaded:at_w]))

            def load(key, name, columns=None):
                src, dst = far_ref(name), into[name]
                if columns is not None:
                    src, dst = src.at[:, columns], dst.at[:, columns]
                copies[key] = pltpu.make_async_copy(src, dst, load_sem.at[len(copies)])
                copies[key].start()

            for name in in_names[2:]:
                load(name, name)
            for kv in range(kv_total):
                at = slice(kv * group * HD, (kv + 1) * group * HD)
                load(("q", kv), "q", at)
                load(("g", kv), "g", at)
        else:
            into = {name: near_ref(name) for name in in_names}
        if w is not None:
            w_copy = pltpu.make_async_copy(
                far_ref("w"), out_refs[at_w], load_sem.at[2 * kv_total + 4]
            )
            w_copy.start()
        q, g, k, v, norms, deltas = (into[name] for name in in_names)

        def arrived(*keys):
            for key in keys:
                if key in copies:
                    copies.pop(key).wait()

        k_deep[HD:] = jnp.full((HD, key_pages * PAGE), -1.0, BF16)
        v_deep[HD:] = jnp.full((HD, key_pages * PAGE), -1.0, BF16)
        for out, i in zip(results, range(len(prior))):
            out[..., :base] = near_ref(("prior", i))[...]
        if ride is not None:
            results[1][2:] = near_ref("ride")[:, :, ride[1] : ride[1] + width]
        owns2, leads = facts[OWNS2] == 1, facts[LEADS] == 1
        if loading:
            arrived("norms", "deltas", "k", "v")
            lane = lax.broadcasted_iota(I32, norms.shape, 1)
            limit = jnp.where(
                lane < PAGE, facts[N0], jnp.where(lane < 2 * PAGE, facts[N1], facts[N2])
            )
            norms[...] = jnp.where(lane % PAGE < limit, norms[...] * (1.0 / SCALE), BLOCKED)
        lower = lambda rows: lax.broadcasted_iota(I32, (rows, PAGE), 1) <= (
            lax.broadcasted_iota(I32, (rows, PAGE), 0) % PAGE
        )

        def set_pages(n, kv):
            lane = slice(kv * HD, (kv + 1) * HD)
            first, second = (near_ref(("page", i)) for i in range(2))
            if own:
                zero = jnp.zeros((), BF16)
                for slot, (at, c) in enumerate(((3, N0), (0, N1), (2, N2))):
                    ok = row_ok(facts[c], PAGE, HD)
                    rows = cols(slot, slot + 1)
                    set_keys(k_deep, k_up, at, jnp.where(ok, k[rows, lane], zero))
                    set_keys(v_deep, None, at, jnp.where(ok, v[rows, lane], zero))
                level2 = [jnp.where(owns2, first[i, :, lane], second[i, :, lane]) for i in (0, 1)]
                set_keys(k_deep, k_up, 1, level2[0])
                set_keys(v_deep, None, 1, level2[1])
            else:
                for j in range(2):
                    mine, theirs = first[j, :, lane], second[j, :, lane]
                    set_keys(k_deep, k_up, j, jnp.where(leads, mine, theirs))
                    set_keys(v_deep, None, j, jnp.where(leads, theirs, mine))
            acc[...] = jnp.zeros_like(acc)

        def turned_rows(head, part, is_fresh, qs, gs, order):
            if is_fresh:
                for name, rows in (("qt", qs), ("gt", gs)):
                    for i, slot in enumerate(order):
                        held[name][:, head.turned_at(part, slot, 1)] = rows[
                            i * tall : (i + 1) * tall
                        ].T
            return lambda name, slot, slots: held[name][:, head.turned_at(part, slot, slots)]

        def own_part(head, part, n, stage_ref):
            order = (1, 2, 0)
            qs, gs = head.stacked(q, part, order), head.stacked(g, part, order)
            qd, gd = head.deep(qs, en, part, order), head.deep(gs, ed, part, order)
            turn = turned_rows(head, part, fresh[n], qs, gs, order)
            low = lower(tall)

            def keep_first(p):
                masked = jnp.where(low, p[:tall, :PAGE], 0.0)
                return jnp.concatenate(
                    [jnp.concatenate([masked, p[:tall, PAGE:]], axis=1), p[tall:]], axis=0
                )

            pa, da = weigh(
                dot_n(qd[: 2 * tall], k_deep[:, : 2 * PAGE]),
                dot_n(gd[: 2 * tall], v_deep[:, : 2 * PAGE]),
                keep_first,
            )
            both = lambda x: jnp.concatenate([x[:tall, :PAGE], x[tall:, PAGE:]], axis=0)
            low2 = lower(2 * tall)
            pb, db = weigh(
                both(dot_n(qd[tall:], k_deep[:, 2 * PAGE :])),
                both(dot_n(gd[tall:], v_deep[:, 2 * PAGE :])),
                lambda p: jnp.where(low2, p, 0.0),
            )
            for i, (name, a, b) in enumerate((("qt", da, db), ("gt", pa, pb))):
                acc[i, :, : 2 * PAGE] += dot_n(turn(name, 1, 2), a)
                acc[i, :, cols(2, 3)] += dot_n(turn(name, 2, 1), b[:tall])
                acc[i, :, cols(3, 4)] += dot_n(turn(name, 0, 1), b[tall:])
            first = dot_n(da, k_up[: 2 * PAGE])
            put = lambda slot, rows: head.put_queries(
                part, slot, rows, held["dq"], not fresh[n], stage_ref
            )
            put(1, first[:tall])
            put(2, first[tall:] + dot_n(db[:tall], k_up[cols(2, 3)]))
            put(0, dot_n(db[tall:], k_up[cols(3, 4)]))

        def shared_part(head, part, n, stage_ref):
            order = (0, 1, 2)
            qs, gs = head.stacked(q, part, order), head.stacked(g, part, order)
            qd, gd = head.deep(qs, en, part, order), head.deep(gs, ed, part, order)
            turn = turned_rows(head, part, fresh[n], qs, gs, order)
            column = lax.broadcasted_iota(I32, (tall, 2 * PAGE), 1)
            seen = column < facts[LIMIT]

            def keep(p):
                return jnp.concatenate([jnp.where(seen, p[:tall], 0.0), p[tall:]], axis=0)

            p, ds = weigh(dot_n(qd, k_deep[...]), dot_n(gd, v_deep[...]), keep)
            acc[0] += dot_n(turn("qt", 0, SLOTS), ds)
            acc[1] += dot_n(turn("gt", 0, SLOTS), p)
            dq = dot_n(ds, k_up[...])
            for slot in range(SLOTS):
                head.put_queries(
                    part, slot, dq[slot * tall : (slot + 1) * tall], held["dq"], not fresh[n],
                    stage_ref,
                )

        def put_own(n):
            dk12, dv12, own0, send2 = results
            here = slice(base + n * HD, base + (n + 1) * HD)
            grad = [acc[0].T * SCALE, acc[1].T]
            for at, c, to in ((0, N1, 0), (2, N2, 1)):
                ok = row_ok(facts[c], PAGE, HD)
                for kind, out in ((0, dk12), (1, dv12)):
                    out[cols(to, to + 1), here] = jnp.where(
                        ok, grad[kind][cols(at, at + 1)], 0.0
                    ).astype(BF16)
            for kind in range(2):
                level2 = grad[kind][cols(1, 2)]
                own0[kind, :, here] = grad[kind][cols(3, 4)] + jnp.where(owns2, level2, 0.0)
                send2[kind, :, here] = level2.astype(BF16)

        def put_shared(n):
            kept, sent = results
            here = slice(n * HD, (n + 1) * HD)
            grad_k, grad_v = acc[0].T * SCALE, acc[1].T
            for j in range(2):
                a, b = grad_k[cols(j, j + 1)], grad_v[cols(j, j + 1)]
                kept[j, :, here] = jnp.where(leads, a, b)
                sent[j, :, here] = jnp.where(leads, b, a).astype(BF16)

        sends = []
        for n, kv in enumerate(kvs):
            arrived(("q", kv), ("g", kv))
            head = Head(kv, group, q, g, norms, deltas, en, ed)
            set_pages(n, kv)

            def step(part, _, n=n, kv=kv, head=head):
                slot = n * parts + part
                (own_part if own else shared_part)(
                    head, part, n, None if fresh[n] else stage.at[slot]
                )
                if not fresh[n]:
                    at = pl.multiple_of((kv * parts + part) * wide, wide)
                    pltpu.make_async_copy(
                        stage.at[slot], held["gq"].at[:, pl.ds(at, wide)], sem.at[slot]
                    ).start()
                return 0

            for part in range(parts):
                step(part, 0)
            (put_own if own else put_shared)(n)
            if not fresh[n]:
                sends += [(n * parts + p, (kv * parts + p) * wide) for p in range(parts)]
        for slot, at in sends:
            pltpu.make_async_copy(
                stage.at[slot], held["gq"].at[:, at : at + wide], sem.at[slot]
            ).wait()
        arrived(*list(copies))
        if w is not None:
            w_copy.wait()

    made = kernel_call(
        body, facts, near, far, outs, scratch, aliases, after,
        pl.CostEstimate(
            flops=load * PAGE * PAGE * HD * group * count, bytes_accessed=1000, transcendentals=0
        ),
        LARGE,
    )
    for name, array in zip(names, made):
        state[name] = array
    state["done"] = state["done"] | set(kvs)
    if loading:
        state["loaded"] = made[at_loaded:at_w]
    results = list(made[at_results:at_loaded])
    return results + ([made[at_w]] if w is not None else [])


def input_grad(facts, side, w, rows, own=None, far=None, begun=None, grads=None, carry=None):
    out_cols, depth = w.shape
    tile = next(t for t in (640, 512, 320, 128, out_cols) if out_cols % t == 0)
    top = 0 if rows == PAGE else PAGE
    steps = out_cols // tile
    width = sum(a.shape[1] for a in grads[0])
    own, far = list(own or []), list(far or [])
    extra = [] if begun is None else [begun]
    arrays = [w, *own, *far, *extra, *grads[0], *grads[1]]
    count = len(grads[0])

    def body(facts, flag, w_ref, *refs):
        own_r, refs = refs[: len(own)], refs[len(own) :]
        far_r, refs = refs[: len(far)], refs[len(far) :]
        begun_r, refs = refs[: len(extra)], refs[len(extra) :]
        grad_r = refs[: 2 * count]
        out, dk, dv, made, stage, sem = refs[-6:]
        made[...] = jnp.zeros_like(made)
        copies = []
        for dst, pieces in ((dk, grad_r[:count]), (dv, grad_r[count:])):
            at = 0
            for src in pieces:
                here = dst.at[top : top + rows, at : at + src.shape[1]]
                copies.append(pltpu.make_async_copy(src, here, sem.at[steps + len(copies)]))
                copies[-1].start()
                at += src.shape[1]
        columns = lambda rs: jnp.concatenate([r[...] for r in rs], axis=1) if rs else None
        mine, other = columns(own_r), columns(far_r)
        half = depth // 2
        where = slice(None)
        if far and own:
            lead = flag[0] == 0
            mine = jnp.concatenate(
                [jnp.where(lead, mine, other), jnp.where(lead, other, mine)], axis=1
            )
        elif far:
            mine = other
            where = pl.ds(pl.multiple_of((1 - flag[0]) * half, half), half)
        for i in range(steps):
            at = slice(i * tile, (i + 1) * tile)
            product = dot_t(w_ref[at, where], mine)
            if extra:
                product += begun_r[0][at]
            stage[i] = product.T.astype(BF16)
            copies.append(
                pltpu.make_async_copy(stage.at[i], out.at[top : top + rows, at], sem.at[i])
            )
            copies[-1].start()
        for c in copies:
            c.wait()

    smem = pl.BlockSpec(memory_space=pltpu.SMEM)
    vmem = pl.BlockSpec(memory_space=pltpu.VMEM)
    hbm = pl.BlockSpec(memory_space=pl.ANY)
    arrays = [pltpu.with_memory_space_constraint(a, pltpu.VMEM) for a in arrays]
    carry = list(carry or [])
    kept = jax.ShapeDtypeStruct((ROWS, width), BF16)
    return pl.pallas_call(
        body,
        out_shape=(
            jax.ShapeDtypeStruct((ROWS, out_cols), BF16), kept, kept, pltpu.VMEM((8, HD), F32)
        ),
        in_specs=[smem] * 2 + [vmem] * len(arrays) + [hbm] * len(carry),
        out_specs=(hbm, hbm, hbm, vmem),
        scratch_shapes=[
            pltpu.VMEM((steps, rows, tile), BF16),
            pltpu.SemaphoreType.DMA((steps + 2 * count,)),
        ],
        input_output_aliases={2 + len(arrays) + i: i for i in range(len(carry))},
        compiler_params=pltpu.CompilerParams(vmem_limit_bytes=LARGE),
        cost_estimate=SLIGHT,
    )(pltpu.with_memory_space_constraint(facts, pltpu.SMEM), side, *arrays, *carry)


def begin_input_grad(facts, side, w, own):
    out_cols, depth = w.shape
    tile = next(t for t in (640, 512, 320, 128, out_cols) if out_cols % t == 0)
    half = depth // 2

    def body(facts, side_r, w_ref, own_r, out):
        where = pl.ds(pl.multiple_of(side_r[0] * half, half), half)
        for i in range(out_cols // tile):
            at = slice(i * tile, (i + 1) * tile)
            out[at] = dot_t(w_ref[at, where], own_r[...])

    smem = pl.BlockSpec(memory_space=pltpu.SMEM)
    vmem = pl.BlockSpec(memory_space=pltpu.VMEM)
    arrays = [pltpu.with_memory_space_constraint(a, pltpu.VMEM) for a in (w, own)]
    return pl.pallas_call(
        body,
        out_shape=pltpu.VMEM((out_cols, own.shape[0]), F32),
        in_specs=[smem, smem, vmem, vmem],
        out_specs=vmem,
        compiler_params=pltpu.CompilerParams(vmem_limit_bytes=LARGE),
        cost_estimate=pl.CostEstimate(
            flops=own.shape[0] * depth * out_cols, bytes_accessed=1000, transcendentals=0
        ),
    )(pltpu.with_memory_space_constraint(facts, pltpu.SMEM), side, *arrays)


def flipped(block, axis, bit):
    count = lax.axis_size(axis)
    return lax.ppermute(block, axis, [(i, i ^ bit) for i in range(count) if i ^ bit < count])


def spanning(leaves, bit_index):
    return len([j for j in range(INNER) if 2 << bit_index <= leaves >> j])


def gather_small_tree(facts, own, beside_pair, beside_half):
    two = (own.shape, BF16, True)
    page = (own.shape[1:], BF16, True)
    from_core = flipped(own, "sub", 1)

    def choose_chip(facts, own_ref, far_ref, out):
        for kind in range(2):
            for mine in range(2):

                @pl.when((facts[LEADS] != kind) & (facts[OWNS2] != mine))
                def _copy(kind=kind, mine=mine):
                    out[...] = (own_ref if mine else far_ref)[kind]

    (chip,) = kernel_call(choose_chip, facts, [own, from_core], [], [page])
    from_pair = flipped(chip, "leaf", 1)

    def choose_pair(facts, near_ref, far_ref, out):
        out[...] = jnp.where(facts[ROOT_IN_PAIR] == 1, near_ref[...], far_ref[...])

    after = beside_pair(from_core, chip)
    (pair,) = kernel_call(choose_pair, facts, [chip, from_pair], [], [page], after=after)
    from_half = flipped(pair, "leaf", 2)

    def choose_all(facts, chip_ref, pair_far, pair_ref, half_far, out):
        out[0] = jnp.where(facts[ROOT_IN_HALF] == 1, pair_ref[...], half_far[...])
        out[1] = jnp.where(facts[NEXT_IN_CHIP] == 1, chip_ref[...], pair_far[...])

    after = beside_half(pair)
    (mine,) = kernel_call(
        choose_all, facts, [chip, from_pair, pair, from_half], [], [two], after=after
    )
    return mine, flipped(mine, "sub", 1)


class Reduction:
    def __init__(self, facts, kept, sent):
        self.facts, self.kept = facts, kept
        self.width = sum(k.shape[-1] for k in kept)
        self.first_far = [flipped(s, "sub", 1) for s in sent]

    def call(self, body, near, outs, after):
        return kernel_call(body, self.facts, near, [], outs, after=after)

    def over_cores(self, after=()):
        count = len(self.kept)

        def body(_, *refs):
            total, low = refs[-2:]
            at = 0
            for near, away in zip(refs[:count], refs[count : 2 * count]):
                here = slice(at, at + near.shape[-1])
                at += near.shape[-1]
                value = near[...] + away[:2].astype(F32)
                total[:, :, here] = value
                low[:, :, here] = value.astype(BF16)

        two = (2, PAGE, self.width)
        self.total, low = self.call(
            body, [*self.kept, *self.first_far], [(two, F32, True), (two, BF16, True)], after
        )
        self.far = flipped(low, "leaf", 1)
        return low


def over_pair(facts, pieces, handed=()):
    count = len(pieces)
    width = sum(r.width for r in pieces)

    def body(_, *refs):
        ins, handed_in = refs[: 2 * count], refs[2 * count : 2 * count + len(handed)]
        total, low = refs[2 * count + len(handed) :][:2]
        at = 0
        for near, away in zip(ins[:count], ins[count:]):
            here = slice(at, at + near.shape[-1])
            at += near.shape[-1]
            value = near[...] + away[...].astype(F32)
            total[:, :, here] = value
            low[:, here] = value[0].astype(BF16)
        for src, dst in zip(handed_in, refs[2 * count + len(handed) + 2 :]):
            dst[...] = src[...]

    outs = [((2, PAGE, width), F32, True), ((PAGE, width), BF16, True)]
    outs += [(a.shape, a.dtype, True) for a in handed]
    near = [r.total for r in pieces] + [r.far for r in pieces] + list(handed)
    total, low, *passed = kernel_call(body, facts, near, [], outs)
    return total, flipped(low, "leaf", 2), passed


def over_half(facts, total, far, passenger, after=()):
    width = total.shape[-1]
    more = passenger.shape[-1]

    def body(facts, near, away, extra, out):
        root = near[0] + away[...].astype(F32)
        out[:, :width] = jnp.where(facts[ROOT_IN_PAIR] == 1, root, near[1]).astype(BF16)
        for kind in range(2):
            out[:, width + kind * more : width + (kind + 1) * more] = extra[kind]

    outs = [((PAGE, width + 2 * more), BF16, True)]
    (mine,) = kernel_call(body, facts, [total, far, passenger], [], outs, after=after)
    return mine, flipped(mine, "sub", 1)


def finish_small_tree(facts, own0, mine, far, lead2, tail2):
    width = sum(a.shape[-1] for a in own0)
    half = width // 2

    def body(facts, own_r, own_last, mine_r, far_r, lead_r, tail_r, dk, dv):
        owns2, leads = facts[OWNS2] == 1, facts[LEADS] == 1
        ok = row_ok(facts[N0], PAGE, HD)
        for at in range(0, width, HD):
            c = slice(at, at + HD)
            last = at + HD == width
            near, away = mine_r[:, c], far_r[:, c]
            gained = [jnp.where(leads, near, away), jnp.where(leads, away, near)]
            for kind, out in enumerate((dk, dv)):
                if last:
                    level2 = far_r[:, width + kind * HD : width + (kind + 1) * HD]
                elif at < half:
                    level2 = lead_r[2 + kind, :, c]
                else:
                    level2 = tail_r[2 + kind, :, at - half : at - half + HD]
                more = jnp.where(owns2, level2, gained[kind]).astype(F32)
                base = own_last[kind] if last else own_r[kind, :, c]
                out[:, c] = jnp.where(ok, base + more, 0.0).astype(BF16)

    page = ((PAGE, width), BF16, True)
    return kernel_call(body, facts, [*own0, mine, far, lead2, tail2], [], [page, page])


def gather_tree(ids, own):
    leaves = lax.axis_size(("leaf", "sub"))
    owned = ids[:INNER] == ids[INNER] - 1
    pages = jnp.where(owned[:, None, None, None], own[None], jnp.zeros((), BF16))
    for bit in range(leaves.bit_length() - 1):
        active = spanning(leaves, bit)
        far = flipped(pages[:active], ("leaf", "sub"), 1 << bit)
        pages = jnp.concatenate([pages[:active] + far, pages[active:]])
    return pages


def reduce_tree(ids, parts):
    leaves = lax.axis_size(("leaf", "sub"))
    for bit in range(leaves.bit_length() - 1):
        active = spanning(leaves, bit)
        far = flipped(parts[:active], ("leaf", "sub"), 1 << bit)
        parts = jnp.concatenate([parts[:active] + far, parts[active:]])
    owned = ids[:INNER] == ids[INNER] - 1
    return jnp.sum(jnp.where(owned[:, None, None, None], parts, 0.0), axis=0)


def on_device(queries, grad_out, keys, values, log_norms, row_deltas, ancestors, counts, w_value):
    kv = keys.shape[1] // HD
    group = queries.shape[1] // keys.shape[1]
    leaves = lax.axis_size(("leaf", "sub"))
    hbm = lambda a: pltpu.with_memory_space_constraint(a, pltpu.HBM)
    side = lax.axis_index("tensor").astype(I32).reshape(1)
    two_sides = lax.axis_size("tensor") == 2
    inputs = [hbm(a) for a in (queries, grad_out, keys, values, log_norms, row_deltas)]
    facts, own = start(hbm(ancestors[0]), hbm(counts[0]), *inputs[2:4])
    state = {"done": frozenset()}

    def own_pages(kvs, pages, prior=(), after=(), w=None, load=240):
        return attend(
            True, kvs, group, facts, inputs, pages, state, w, prior, after=after, load=load
        )

    def shared_pages(kvs, pages, ride=None, after=()):
        return attend(False, kvs, group, facts, inputs, pages, state, ride=ride, after=after)

    def spread(part):
        if two_sides:
            return flipped(part, "tensor", 1)
        return lax.all_gather(part, "tensor", axis=1, tiled=True)

    if leaves == 8 and lax.axis_size("sub") == 2 and kv == 4 and two_sides:
        level2, results = [], []

        def beside_pair(from_core, chip):
            level2.extend((own, from_core))
            results.append(own_pages((0,), level2, after=(chip,)))
            return (results[-1][3],)

        def beside_half(pair):
            results.append(own_pages((1, 2), level2, results[-1], (pair,)))
            return (results[-1][3],)

        shared = gather_small_tree(facts, own, beside_pair, beside_half)
        _, dv12, _, send2 = results[-1]
        far_v = [spread(dv12)]
        kept, sent = shared_pages((0, 1), shared, (send2, 0))
        lead = Reduction(facts, [kept], [sent])
        kept, sent = shared_pages((2,), shared, ride=(send2, 2 * HD), after=far_v)
        low = lead.over_cores((kept,))
        last_kept, last_sent = shared_pages((3,), shared, after=(low,))
        tail = Reduction(facts, [kept, last_kept], [sent, last_sent])
        *last, w_near = own_pages(
            (3,), level2, after=(tail.over_cores((lead.far,)),), w=hbm(w_value)
        )
        total, from_half, (last[1],) = over_pair(facts, [lead, tail], [last[1]])
        far_v.append(spread(last[1]))
        near_v = [dv12, last[1]]
        both = list(zip(results[-1], last))
        *grads, made = input_grad(
            facts, side, w_near, 2 * PAGE, near_v, far_v, grads=both[:2]
        )
        dk0, dv0 = finish_small_tree(
            facts, both[2], *over_half(facts, total, from_half, last[3], (made,)),
            lead.first_far[0], tail.first_far[0],
        )
        far_v = [spread(dv0)]
        begun = begin_input_grad(facts, side, w_near, dv0)
        grad_input, grad_keys, grad_values, _ = input_grad(
            facts, side, w_near, PAGE, far=far_v, begun=begun, grads=([dk0], [dv0]), carry=grads
        )
        return (state["gq"], grad_keys, grad_values, grad_input)

    kvs = tuple(range(kv))
    first = lax.axis_index("sub") == 0
    path_ids = ancestors[0]
    pages = gather_tree(path_ids, own)
    dk12, dv12, own0, send2, w_near = own_pages(kvs, (pages[2], pages[2]), w=hbm(w_value))
    kept, sent = shared_pages(
        kvs,
        (
            jnp.where(first, pages[:2, 0], pages[:2, 1]),
            jnp.where(first, pages[:2, 1], pages[:2, 0]),
        ),
    )
    sent = sent.astype(F32)
    upper = jnp.stack([jnp.where(first, kept, sent), jnp.where(first, sent, kept)], axis=1)
    low = send2.astype(F32)
    total = reduce_tree(path_ids, jnp.concatenate([upper, low[None]]))
    total += own0 - jnp.where(path_ids[2] == path_ids[INNER] - 1, low, 0.0)
    has = jnp.any(path_ids[:INNER] == path_ids[INNER] - 1)
    ok = (jnp.arange(PAGE) < jnp.where(has, counts[0, 0], 0))[:, None]
    dk0, dv0 = jnp.where(ok, total, 0.0).astype(BF16)
    if two_sides:
        pair = lambda part: ([part], [spread(part)])
    else:
        pair = lambda part: ([spread(part)], None)
    *grads, _ = input_grad(
        facts, side, w_near, 2 * PAGE, *pair(dv12), grads=([dk12], [dv12])
    )
    grad_input, grad_keys, grad_values, _ = input_grad(
        facts, side, w_near, PAGE, *pair(dv0), grads=([dk0], [dv0]), carry=grads
    )
    return (state["gq"], grad_keys, grad_values, grad_input)


def solution(mesh):
    placed = (
        P(("groups", "leaf", "sub"), "tensor"),
        P(("groups", "leaf", "sub"), "tensor"),
        P(("groups", "leaf", "sub"), "tensor"),
        P(("groups", "leaf", "sub"), "tensor"),
        P("tensor", ("groups", "leaf", "sub")),
        P("tensor", ("groups", "leaf", "sub")),
        P(("groups", "leaf", "sub"), None),
        P(("groups", "leaf", "sub"), None),
        P("tensor", None),
    )
    return jax.shard_map(
        on_device,
        mesh=mesh,
        in_specs=placed,
        out_specs=(
            P(("groups", "leaf", "sub"), "tensor"),
            P(("groups", "leaf", "sub"), "tensor"),
            P(("groups", "leaf", "sub"), "tensor"),
            P(("groups", "leaf", "sub"), "tensor"),
        ),
        check_vma=False,
    )
```

```python
import math

import jax
import jax.numpy as jnp
from jax import lax
from jax.experimental import pallas as pl
from jax.experimental.pallas import tpu as pltpu
from jax.sharding import PartitionSpec as P

HD = 128
PAGE = 128
SLOTS = 3
INNER = 3
ROWS = SLOTS * PAGE
LOG2E = math.log2(math.e)
SCALE = 1.0 / math.sqrt(HD)
BF16 = jnp.bfloat16
F32 = jnp.float32
I32 = jnp.int32
LARGE = 10 << 20
SMALL = 4 << 20
SLIGHT = pl.CostEstimate(flops=1000, bytes_accessed=1000, transcendentals=0)
BLOCKED = 1e30


def dot_t(left, right):
    return lax.dot_general(left, right, (((1,), (1,)), ((), ())), preferred_element_type=F32)


def dot_n(left, right):
    return lax.dot_general(left, right, (((1,), (0,)), ((), ())), preferred_element_type=F32)


FACTS = 16
N0, N1, N2, OWNS2, LIMIT, LEADS, ROOT_IN_CHIP, ROOT_IN_PAIR, NEXT_IN_CHIP = range(9)


def write_facts(facts, ids, counts):
    page = [ids[0, j] for j in range(INNER + 1)]
    own = page[INNER] - 1
    leaf = own // SLOTS
    owns = [page[j] == own for j in range(INNER)]
    same = lambda level, shift: ((page[level] // SLOTS) >> shift) == (leaf >> shift)
    number = lambda flag: jnp.where(flag, 1, 0)
    facts[N0] = jnp.where(owns[0] | owns[1] | owns[2], counts[0, 0], 0)
    facts[N1] = counts[0, 1]
    facts[N2] = counts[0, 2]
    facts[OWNS2] = number(owns[2])
    facts[LIMIT] = jnp.where(owns[2], 2 * PAGE, jnp.where(owns[1], PAGE, 0))
    facts[LEADS] = number(lax.rem(leaf, 2) == 0)
    facts[ROOT_IN_CHIP] = number(same(0, 1))
    facts[ROOT_IN_PAIR] = number(same(0, 2))
    facts[NEXT_IN_CHIP] = number(same(1, 1))
    for i in range(NEXT_IN_CHIP + 1, FACTS):
        facts[i] = 0


def row_ok(count, rows, width):
    return lax.broadcasted_iota(I32, (rows, width), 0) < count


def kernel_call(body, facts, near, far, outs, scratch=(), aliases=None, after=(), cost=None,
                limit=SMALL):
    smem = pl.BlockSpec(memory_space=pltpu.SMEM)
    vmem = pl.BlockSpec(memory_space=pltpu.VMEM)
    hbm = pl.BlockSpec(memory_space=pl.ANY)
    near = [pltpu.with_memory_space_constraint(a, pltpu.VMEM) for a in near]
    place = {("near", i): 1 + i for i in range(len(near))}
    place |= {("far", i): 1 + len(near) + i for i in range(len(far))}
    used = 1 + len(near) + len(far)

    def kernel(*refs):
        body(*refs[:used], *refs[used + len(after) :])

    return pl.pallas_call(
        kernel,
        out_shape=tuple(
            pltpu.VMEM(s, d) if inside else jax.ShapeDtypeStruct(s, d) for s, d, inside in outs
        ),
        in_specs=[smem] + [vmem] * len(near) + [hbm] * (len(far) + len(after)),
        out_specs=tuple(vmem if inside else hbm for _, _, inside in outs),
        scratch_shapes=list(scratch),
        input_output_aliases={place[k]: v for k, v in (aliases or {}).items()},
        compiler_params=pltpu.CompilerParams(vmem_limit_bytes=limit),
        cost_estimate=cost or SLIGHT,
    )(pltpu.with_memory_space_constraint(facts, pltpu.SMEM), *near, *far, *after)


def start(ids, counts, keys, values):
    width = keys.shape[1]

    def body(ids_ref, counts_ref, k_ref, v_ref, facts, out, held, ids_s, counts_s, sem):
        copies = [
            pltpu.make_async_copy(src, dst, sem.at[i])
            for i, (src, dst) in enumerate(
                (
                    (ids_ref, ids_s),
                    (counts_ref, counts_s),
                    (k_ref.at[:PAGE], held.at[0]),
                    (v_ref.at[:PAGE], held.at[1]),
                )
            )
        ]
        for c in copies:
            c.start()
        copies[0].wait()
        copies[1].wait()
        write_facts(facts, ids_s, counts_s)
        ok = row_ok(counts_s[0, 0], PAGE, width)
        for i in range(2):
            copies[2 + i].wait()
            out[i] = jnp.where(ok, held[i], jnp.zeros((), BF16))

    smem = pl.BlockSpec(memory_space=pltpu.SMEM)
    hbm = pl.BlockSpec(memory_space=pl.ANY)
    return pl.pallas_call(
        body,
        out_shape=(pltpu.SMEM((FACTS,), I32), pltpu.VMEM((2, PAGE, width), BF16)),
        in_specs=[hbm] * 4,
        out_specs=(smem, pl.BlockSpec(memory_space=pltpu.VMEM)),
        scratch_shapes=[
            pltpu.VMEM((2, PAGE, width), BF16),
            pltpu.SMEM(ids.shape, I32),
            pltpu.SMEM(counts.shape, I32),
            pltpu.SemaphoreType.DMA((4,)),
        ],
        compiler_params=pltpu.CompilerParams(vmem_limit_bytes=SMALL),
    )(ids, counts, keys, values)


def row_terms(rows):
    high = rows.astype(BF16).astype(F32)
    rest = rows - high
    middle = rest.astype(BF16).astype(F32)
    parts = [high, middle, rest - middle]
    spare = HD - 3 * rows.shape[0]
    parts.append(jnp.zeros((spare, rows.shape[1]), F32))
    return jnp.concatenate(parts, axis=0).T.astype(BF16)


class Head:
    def __init__(self, kv, group, q, g, norms, deltas, en, ed):
        self.kv, self.group, self.q, self.g, self.en, self.ed = kv, group, q, g, en, ed
        self.heads = min(4, group)
        self.parts = group // self.heads
        self.tall = self.heads * PAGE
        heads = slice(kv * group, (kv + 1) * group)
        en[...] = row_terms(norms[heads, :])
        ed[...] = row_terms(deltas[heads, :])

    def lanes(self, part, j):
        at = self.kv * self.group * HD + part * (self.heads * HD) + j * HD
        return pl.ds(pl.multiple_of(at, HD), HD)

    def stacked(self, ref, part, slots):
        return jnp.concatenate(
            [
                ref[slot * PAGE : (slot + 1) * PAGE, self.lanes(part, j)]
                for slot in slots
                for j in range(self.heads)
            ],
            axis=0,
        )

    def deep(self, stacked, terms, part, slots):
        column = lax.broadcasted_iota(I32, (1, HD), 1) % self.group
        picks = [
            (column == part * self.heads + j).astype(F32).astype(BF16)
            for j in range(self.heads)
        ]
        extra = [
            terms[slot * PAGE : (slot + 1) * PAGE] * pick for slot in slots for pick in picks
        ]
        return jnp.concatenate([stacked, jnp.concatenate(extra, axis=0)], axis=1)

    def turned_at(self, part, slot, count):
        at = ((self.kv * self.parts + part) * SLOTS + slot) * self.tall
        return pl.ds(pl.multiple_of(at, self.tall), self.tall * count)

    def put_queries(self, part, slot, rows_by_head, dq, add, stage):
        rows = slice(slot * PAGE, (slot + 1) * PAGE)
        for j in range(self.heads):
            value = rows_by_head[j * PAGE : (j + 1) * PAGE]
            if stage is None:
                dq[rows, self.lanes(part, j)] = value
            else:
                if add:
                    value = value + dq[rows, self.lanes(part, j)]
                stage[rows, j * HD : (j + 1) * HD] = (value * SCALE).astype(BF16)


def set_keys(deep, upright, at, page):
    where = slice(at * PAGE, (at + 1) * PAGE)
    deep[:HD, where] = page.T
    if upright is not None:
        upright[where] = page


def weigh(scores, grads, keep):
    p = keep(jnp.exp2(scores * (SCALE * LOG2E)))
    return p.astype(BF16), (p * grads).astype(BF16)


def attend(own, kvs, group, facts, inputs, pages, state, prior=(), after=()):
    loading = "loaded" not in state
    q, g, k, v, norms, deltas = inputs if loading else state["loaded"]
    count = len(kvs)
    parts = group // min(4, group)
    tall = min(4, group) * PAGE
    wide = min(4, group) * HD
    width = count * HD
    base = prior[0].shape[1] if prior else 0
    kv_total = k.shape[1] // HD
    fresh = [kv not in state["done"] for kv in kvs]
    names = ["dq", "qt", "gt"] + ([] if all(fresh) else ["gq"])
    turned = ((HD, kv_total * group * ROWS), BF16, True)
    full = {"dq": (q.shape, F32, True), "qt": turned, "gt": turned, "gq": (q.shape, BF16, False)}

    near, far, aliases, outs = [], [], {}, []
    at_near, at_far = {}, {}

    def add_near(name, array):
        at_near[name] = len(near)
        near.append(array)

    def add_far(name, array):
        at_far[name] = len(far)
        far.append(array)

    for name in names:
        outs.append(full[name])
        if name in state:
            if full[name][2]:
                add_near(name, state[name])
                aliases["near", at_near[name]] = len(outs) - 1
            else:
                add_far(name, state[name])
                aliases["far", at_far[name]] = len(outs) - 1
    at_results = len(outs)
    if own:
        outs += [
            ((2 * PAGE, base + width), BF16, True),
            ((2 * PAGE, base + width), BF16, True),
            ((2, PAGE, base + width), F32, True),
            ((2, PAGE, base + width), BF16, True),
        ]
    else:
        outs += [
            ((2, PAGE, width), F32, True),
            ((2, PAGE, width), BF16, True),
        ]
    at_loaded = len(outs)
    in_names = ["q", "g", "k", "v", "norms", "deltas"]
    in_arrays = [q, g, k, v, norms, deltas]
    for name, array in zip(in_names, in_arrays):
        if loading:
            add_far(name, array)
            outs.append((array.shape, array.dtype, True))
        else:
            add_near(name, array)
    at_end = len(outs)
    for i, page in enumerate(pages):
        add_near(("page", i), page)
    for i, array in enumerate(prior):
        add_near(("prior", i), array)
    key_pages = 4 if own else 2
    scratch = [
        pltpu.VMEM((2 * HD, key_pages * PAGE), BF16),
        pltpu.VMEM((2 * HD, key_pages * PAGE), BF16),
        pltpu.VMEM((key_pages * PAGE, HD), BF16),
        pltpu.VMEM((2, HD, key_pages * PAGE), F32),
        pltpu.VMEM((ROWS, HD), BF16),
        pltpu.VMEM((ROWS, HD), BF16),
        pltpu.VMEM((count * parts, ROWS, wide), BF16),
        pltpu.SemaphoreType.DMA((count * parts,)),
        pltpu.SemaphoreType.DMA((2 * kv_total + 4,)),
    ]
    cols = lambda a, b: slice(a * PAGE, b * PAGE)

    def body(facts, *refs):
        ins, out_refs = refs[: len(near) + len(far)], refs[len(near) + len(far) : -len(scratch)]
        k_deep, v_deep, k_up, acc, en, ed, stage, sem, load_sem = refs[-len(scratch) :]
        near_ref = lambda name: ins[at_near[name]]
        far_ref = lambda name: ins[len(near) + at_far[name]]
        held = dict(zip(names, out_refs))
        results = out_refs[at_results:at_loaded]
        copies = {}
        if loading:
            into = dict(zip(in_names, out_refs[at_loaded:at_end]))

            def load(key, name, columns=None):
                src, dst = far_ref(name), into[name]
                if columns is not None:
                    src, dst = src.at[:, columns], dst.at[:, columns]
                copies[key] = pltpu.make_async_copy(src, dst, load_sem.at[len(copies)])
                copies[key].start()

            for name in in_names[2:]:
                load(name, name)
            for kv in range(kv_total):
                at = slice(kv * group * HD, (kv + 1) * group * HD)
                load(("q", kv), "q", at)
                load(("g", kv), "g", at)
        else:
            into = {name: near_ref(name) for name in in_names}
        q, g, k, v, norms, deltas = (into[name] for name in in_names)

        def arrived(*keys):
            for key in keys:
                if key in copies:
                    copies.pop(key).wait()

        k_deep[HD:] = jnp.full((HD, key_pages * PAGE), -1.0, BF16)
        v_deep[HD:] = jnp.full((HD, key_pages * PAGE), -1.0, BF16)
        for out, i in zip(results, range(len(prior))):
            out[..., :base] = near_ref(("prior", i))[...]
        owns2, leads = facts[OWNS2] == 1, facts[LEADS] == 1
        if loading:
            arrived("norms", "deltas", "k", "v")
            lane = lax.broadcasted_iota(I32, norms.shape, 1)
            limit = jnp.where(
                lane < PAGE, facts[N0], jnp.where(lane < 2 * PAGE, facts[N1], facts[N2])
            )
            norms[...] = jnp.where(lane % PAGE < limit, norms[...] * (1.0 / SCALE), BLOCKED)
        lower = lambda rows: lax.broadcasted_iota(I32, (rows, PAGE), 1) <= (
            lax.broadcasted_iota(I32, (rows, PAGE), 0) % PAGE
        )

        def set_pages(n, kv):
            lane = slice(kv * HD, (kv + 1) * HD)
            first, second = (near_ref(("page", i)) for i in range(2))
            if own:
                zero = jnp.zeros((), BF16)
                for slot, (at, c) in enumerate(((3, N0), (0, N1), (2, N2))):
                    ok = row_ok(facts[c], PAGE, HD)
                    rows = cols(slot, slot + 1)
                    set_keys(k_deep, k_up, at, jnp.where(ok, k[rows, lane], zero))
                    set_keys(v_deep, None, at, jnp.where(ok, v[rows, lane], zero))
                level2 = [jnp.where(owns2, first[i, :, lane], second[i, :, lane]) for i in (0, 1)]
                set_keys(k_deep, k_up, 1, level2[0])
                set_keys(v_deep, None, 1, level2[1])
            else:
                for j in range(2):
                    mine, theirs = first[j, :, lane], second[j, :, lane]
                    set_keys(k_deep, k_up, j, jnp.where(leads, mine, theirs))
                    set_keys(v_deep, None, j, jnp.where(leads, theirs, mine))
            acc[...] = jnp.zeros_like(acc)

        def turned_rows(head, part, is_fresh, qs, gs, order):
            if is_fresh:
                for name, rows in (("qt", qs), ("gt", gs)):
                    for i, slot in enumerate(order):
                        held[name][:, head.turned_at(part, slot, 1)] = rows[
                            i * tall : (i + 1) * tall
                        ].T
            return lambda name, slot, slots: held[name][:, head.turned_at(part, slot, slots)]

        def own_part(head, part, n, stage_ref):
            order = (1, 2, 0)
            qs, gs = head.stacked(q, part, order), head.stacked(g, part, order)
            qd, gd = head.deep(qs, en, part, order), head.deep(gs, ed, part, order)
            turn = turned_rows(head, part, fresh[n], qs, gs, order)
            low = lower(tall)

            def keep_first(p):
                masked = jnp.where(low, p[:tall, :PAGE], 0.0)
                return jnp.concatenate(
                    [jnp.concatenate([masked, p[:tall, PAGE:]], axis=1), p[tall:]], axis=0
                )

            pa, da = weigh(
                dot_n(qd[: 2 * tall], k_deep[:, : 2 * PAGE]),
                dot_n(gd[: 2 * tall], v_deep[:, : 2 * PAGE]),
                keep_first,
            )
            both = lambda x: jnp.concatenate([x[:tall, :PAGE], x[tall:, PAGE:]], axis=0)
            low2 = lower(2 * tall)
            pb, db = weigh(
                both(dot_n(qd[tall:], k_deep[:, 2 * PAGE :])),
                both(dot_n(gd[tall:], v_deep[:, 2 * PAGE :])),
                lambda p: jnp.where(low2, p, 0.0),
            )
            for i, (name, a, b) in enumerate((("qt", da, db), ("gt", pa, pb))):
                acc[i, :, : 2 * PAGE] += dot_n(turn(name, 1, 2), a)
                acc[i, :, cols(2, 3)] += dot_n(turn(name, 2, 1), b[:tall])
                acc[i, :, cols(3, 4)] += dot_n(turn(name, 0, 1), b[tall:])
            first = dot_n(da, k_up[: 2 * PAGE])
            put = lambda slot, rows: head.put_queries(
                part, slot, rows, held["dq"], not fresh[n], stage_ref
            )
            put(1, first[:tall])
            put(2, first[tall:] + dot_n(db[:tall], k_up[cols(2, 3)]))
            put(0, dot_n(db[tall:], k_up[cols(3, 4)]))

        def shared_part(head, part, n, stage_ref):
            order = (0, 1, 2)
            qs, gs = head.stacked(q, part, order), head.stacked(g, part, order)
            qd, gd = head.deep(qs, en, part, order), head.deep(gs, ed, part, order)
            turn = turned_rows(head, part, fresh[n], qs, gs, order)
            column = lax.broadcasted_iota(I32, (tall, 2 * PAGE), 1)
            seen = column < facts[LIMIT]

            def keep(p):
                return jnp.concatenate([jnp.where(seen, p[:tall], 0.0), p[tall:]], axis=0)

            p, ds = weigh(dot_n(qd, k_deep[...]), dot_n(gd, v_deep[...]), keep)
            acc[0] += dot_n(turn("qt", 0, SLOTS), ds)
            acc[1] += dot_n(turn("gt", 0, SLOTS), p)
            dq = dot_n(ds, k_up[...])
            for slot in range(SLOTS):
                head.put_queries(
                    part, slot, dq[slot * tall : (slot + 1) * tall], held["dq"], not fresh[n],
                    stage_ref,
                )

        def put_own(n):
            dk12, dv12, own0, send2 = results
            here = slice(base + n * HD, base + (n + 1) * HD)
            grad = [acc[0].T * SCALE, acc[1].T]
            for at, c, to in ((0, N1, 0), (2, N2, 1)):
                ok = row_ok(facts[c], PAGE, HD)
                for kind, out in ((0, dk12), (1, dv12)):
                    out[cols(to, to + 1), here] = jnp.where(
                        ok, grad[kind][cols(at, at + 1)], 0.0
                    ).astype(BF16)
            for kind in range(2):
                level2 = grad[kind][cols(1, 2)]
                own0[kind, :, here] = grad[kind][cols(3, 4)] + jnp.where(owns2, level2, 0.0)
                send2[kind, :, here] = level2.astype(BF16)

        def put_shared(n):
            kept, sent = results
            here = slice(n * HD, (n + 1) * HD)
            grad_k, grad_v = acc[0].T * SCALE, acc[1].T
            for j in range(2):
                a, b = grad_k[cols(j, j + 1)], grad_v[cols(j, j + 1)]
                kept[j, :, here] = jnp.where(leads, a, b)
                sent[j, :, here] = jnp.where(leads, b, a).astype(BF16)

        sends = []
        for n, kv in enumerate(kvs):
            arrived(("q", kv), ("g", kv))
            head = Head(kv, group, q, g, norms, deltas, en, ed)
            set_pages(n, kv)

            def step(part, _, n=n, kv=kv, head=head):
                slot = n * parts + part
                (own_part if own else shared_part)(
                    head, part, n, None if fresh[n] else stage.at[slot]
                )
                if not fresh[n]:
                    at = pl.multiple_of((kv * parts + part) * wide, wide)
                    pltpu.make_async_copy(
                        stage.at[slot], held["gq"].at[:, pl.ds(at, wide)], sem.at[slot]
                    ).start()
                return 0

            for part in range(parts):
                step(part, 0)
            (put_own if own else put_shared)(n)
            if not fresh[n]:
                sends += [(n * parts + p, (kv * parts + p) * wide) for p in range(parts)]
        for slot, at in sends:
            pltpu.make_async_copy(
                stage.at[slot], held["gq"].at[:, at : at + wide], sem.at[slot]
            ).wait()
        arrived(*list(copies))

    made = kernel_call(
        body, facts, near, far, outs, scratch, aliases, after,
        pl.CostEstimate(
            flops=240 * PAGE * PAGE * HD * group * count, bytes_accessed=1000, transcendentals=0
        ),
        LARGE,
    )
    for name, array in zip(names, made):
        state[name] = array
    state["done"] = state["done"] | set(kvs)
    if loading:
        state["loaded"] = made[at_loaded:at_end]
    return list(made[at_results:at_loaded])


def width_tiles(w):
    tile = next(t for t in (512, 640, 320, 128, w.shape[0]) if w.shape[0] % t == 0)
    return [slice(i, i + tile) for i in range(0, w.shape[0], tile)]


def input_grad(facts, side, w, rows, own, far, grads, carry=None):
    out_cols, depth = w.shape
    tiles = width_tiles(w)
    top = 0 if rows == PAGE else PAGE
    steps = len(tiles)
    width = sum(a.shape[1] for a in grads[0])
    arrays = [*own, *far, *grads[0], *grads[1]]
    count = len(grads[0])
    carry = list(carry or [])

    def body(facts, flag, *refs):
        own_r, refs = refs[: len(own)], refs[len(own) :]
        far_r, refs = refs[: len(far)], refs[len(far) :]
        grad_r, w_ref = refs[: 2 * count], refs[2 * count]
        out, dk, dv, made, w_near, stage, w_sem, sem = refs[-8:]
        loads = [
            pltpu.make_async_copy(w_ref.at[at], w_near.at[at], w_sem.at[i])
            for i, at in enumerate(tiles)
        ]
        for c in loads:
            c.start()
        made[...] = jnp.zeros_like(made)
        columns = lambda rs: jnp.concatenate([r[...] for r in rs], axis=1)
        full = columns(own_r)
        if far:
            other, leads = columns(far_r), flag[0] == 0
            full = jnp.concatenate(
                [jnp.where(leads, full, other), jnp.where(leads, other, full)], axis=1
            )
        copies = put_rows(grad_r, dk, dv, top, rows, sem, steps)
        for i, at in enumerate(tiles):
            loads[i].wait()
            stage[i] = dot_t(w_near[at], full).astype(BF16).T
            copies.append(
                pltpu.make_async_copy(stage.at[i], out.at[top : top + rows, at], sem.at[i])
            )
            copies[-1].start()
        for c in copies:
            c.wait()

    smem = pl.BlockSpec(memory_space=pltpu.SMEM)
    vmem = pl.BlockSpec(memory_space=pltpu.VMEM)
    hbm = pl.BlockSpec(memory_space=pl.ANY)
    arrays = [pltpu.with_memory_space_constraint(a, pltpu.VMEM) for a in arrays]
    kept = jax.ShapeDtypeStruct((ROWS, width), BF16)
    return pl.pallas_call(
        body,
        out_shape=(
            jax.ShapeDtypeStruct((ROWS, out_cols), BF16), kept, kept, pltpu.VMEM((8, HD), F32)
        ),
        in_specs=[smem] * 2 + [vmem] * len(arrays) + [hbm] * (1 + len(carry)),
        out_specs=(hbm, hbm, hbm, vmem),
        scratch_shapes=[
            pltpu.VMEM(w.shape, BF16),
            pltpu.VMEM((steps, rows, out_cols // steps), BF16),
            pltpu.SemaphoreType.DMA((steps,)),
            pltpu.SemaphoreType.DMA((steps + 2 * count,)),
        ],
        input_output_aliases={3 + len(arrays) + i: i for i in range(len(carry))},
        compiler_params=pltpu.CompilerParams(vmem_limit_bytes=LARGE),
        cost_estimate=SLIGHT,
    )(pltpu.with_memory_space_constraint(facts, pltpu.SMEM), side, *arrays, w, *carry)


def put_rows(pieces, dk, dv, top, rows, sem, first):
    copies = []
    count = len(pieces) // 2
    for dst, mine in ((dk, pieces[:count]), (dv, pieces[count:])):
        at = 0
        for src in mine:
            here = dst.at[top : top + rows, at : at + src.shape[1]]
            copies.append(pltpu.make_async_copy(src, here, sem.at[first + len(copies)]))
            copies[-1].start()
            at += src.shape[1]
    return copies


def begin_input_grad(facts, side, w, own):
    out_cols, depth = w.shape
    tiles = width_tiles(w)
    half = depth // 2

    def body(facts, flag, own_r, w_ref, out, w_far, w_near, sem):
        place = lambda which: pl.ds(pl.multiple_of(which * half, half), half)
        loads = [
            pltpu.make_async_copy(w_ref.at[at, place(flag[0])], w_near.at[at], sem.at[i])
            for i, at in enumerate(tiles)
        ]
        rest = pltpu.make_async_copy(w_ref.at[:, place(1 - flag[0])], w_far, sem.at[len(tiles)])
        for c in [*loads, rest]:
            c.start()
        for i, at in enumerate(tiles):
            loads[i].wait()
            out[at] = dot_t(w_near[at], own_r[...])
        rest.wait()

    smem = pl.BlockSpec(memory_space=pltpu.SMEM)
    vmem = pl.BlockSpec(memory_space=pltpu.VMEM)
    return pl.pallas_call(
        body,
        out_shape=(pltpu.VMEM((out_cols, own.shape[0]), F32), pltpu.VMEM((out_cols, half), BF16)),
        in_specs=[smem, smem, vmem, pl.BlockSpec(memory_space=pl.ANY)],
        out_specs=(vmem, vmem),
        scratch_shapes=[
            pltpu.VMEM((out_cols, half), BF16), pltpu.SemaphoreType.DMA((len(tiles) + 1,))
        ],
        compiler_params=pltpu.CompilerParams(vmem_limit_bytes=LARGE),
        cost_estimate=pl.CostEstimate(
            flops=own.shape[0] * depth * out_cols, bytes_accessed=1000, transcendentals=0
        ),
    )(
        pltpu.with_memory_space_constraint(facts, pltpu.SMEM), side,
        pltpu.with_memory_space_constraint(own, pltpu.VMEM), w,
    )


def end_input_grad(facts, far, begun, w_far, grads, carry):
    tiles = width_tiles(w_far)
    steps = len(tiles)
    rows = far.shape[0]

    def body(facts, far_r, begun_r, w_r, *refs):
        out, dk, dv, stage, sem = refs[-5:]
        copies = put_rows(refs[:2], dk, dv, 0, rows, sem, steps)
        for i, at in enumerate(tiles):
            stage[i] = (dot_t(w_r[at], far_r[...]) + begun_r[at]).astype(BF16).T
            copies.append(pltpu.make_async_copy(stage.at[i], out.at[:rows, at], sem.at[i]))
            copies[-1].start()
        for c in copies:
            c.wait()

    return kernel_call(
        body, facts, [far, begun, w_far, *grads], carry,
        [(a.shape, a.dtype, False) for a in carry],
        [
            pltpu.VMEM((steps, rows, w_far.shape[0] // steps), BF16),
            pltpu.SemaphoreType.DMA((steps + 2,)),
        ],
        {("far", i): i for i in range(len(carry))},
    )


def flipped(block, axis, bit):
    count = lax.axis_size(axis)
    return lax.ppermute(block, axis, [(i, i ^ bit) for i in range(count) if i ^ bit < count])


def spanning(leaves, bit_index):
    return len([j for j in range(INNER) if 2 << bit_index <= leaves >> j])


def gather_small_tree(facts, own, beside_pair, beside_half):
    two = (own.shape, BF16, True)
    page = (own.shape[1:], BF16, True)
    from_core = flipped(own, "sub", 1)

    def choose_chip(facts, own_ref, far_ref, out):
        for kind in range(2):
            for mine in range(2):

                @pl.when((facts[LEADS] != kind) & (facts[OWNS2] != mine))
                def _copy(kind=kind, mine=mine):
                    out[...] = (own_ref if mine else far_ref)[kind]

    (chip,) = kernel_call(choose_chip, facts, [own, from_core], [], [page])
    from_pair = flipped(chip, "leaf", 1)

    def choose_pair(facts, near_ref, far_ref, out):
        out[...] = jnp.where(facts[ROOT_IN_CHIP] == 1, near_ref[...], far_ref[...])

    after = beside_pair(from_core, chip)
    (pair,) = kernel_call(choose_pair, facts, [chip, from_pair], [], [page], after=after)
    from_half = flipped(pair, "leaf", 2)

    def choose_all(facts, chip_ref, pair_far, pair_ref, half_far, out):
        out[0] = jnp.where(facts[ROOT_IN_PAIR] == 1, pair_ref[...], half_far[...])
        out[1] = jnp.where(facts[NEXT_IN_CHIP] == 1, chip_ref[...], pair_far[...])

    after = beside_half(pair)
    (mine,) = kernel_call(
        choose_all, facts, [chip, from_pair, pair, from_half], [], [two], after=after
    )
    return mine, flipped(mine, "sub", 1)


def over_cores(facts, kept, sent):
    width = kept.shape[-1]

    def body(_, near, away, total, root, next_one):
        for j, low in enumerate((root, next_one)):
            value = near[j] + away[j].astype(F32)
            total[j] = value
            low[...] = value.astype(BF16)

    page = ((PAGE, width), BF16, True)
    total, root, next_one = kernel_call(
        body, facts, [kept, flipped(sent, "sub", 1)], [],
        [((2, PAGE, width), F32, True), page, page],
    )
    return total, root, flipped(root, "leaf", 2), flipped(next_one, "leaf", 1)


def over_halves(facts, total, root_far, next_far, after):
    width = total.shape[-1]

    def body(_, near, root_r, next_r, out, low):
        root = near[0] + root_r[...].astype(F32)
        out[0] = root
        low[...] = root.astype(BF16)
        out[1] = near[1] + next_r[...].astype(F32)

    total, low = kernel_call(
        body, facts, [total, root_far, next_far], [],
        [((2, PAGE, width), F32, True), ((PAGE, width), BF16, True)], after=after,
    )
    return total, flipped(low, "leaf", 1)


def over_chips(facts, total, far, passenger, after=()):
    width = total.shape[-1]
    more = passenger.shape[-1]

    def body(facts, near, away, extra, out):
        root = near[0] + away[...].astype(F32)
        out[:, :width] = jnp.where(facts[ROOT_IN_CHIP] == 1, root, near[1]).astype(BF16)
        for kind in range(2):
            out[:, width + kind * more : width + (kind + 1) * more] = extra[kind]

    outs = [((PAGE, width + 2 * more), BF16, True)]
    (mine,) = kernel_call(body, facts, [total, far, passenger], [], outs, after=after)
    return mine, flipped(mine, "sub", 1)


def finish_small_tree(facts, own0, mine, far, level2_far):
    width = sum(a.shape[-1] for a in own0)

    def body(facts, own_r, own_last, mine_r, far_r, low_r, dk, dv):
        owns2, leads = facts[OWNS2] == 1, facts[LEADS] == 1
        ok = row_ok(facts[N0], PAGE, HD)
        for at in range(0, width, HD):
            c = slice(at, at + HD)
            last = at + HD == width
            near, away = mine_r[:, c], far_r[:, c]
            gained = [jnp.where(leads, near, away), jnp.where(leads, away, near)]
            for kind, out in enumerate((dk, dv)):
                if last:
                    level2 = far_r[:, width + kind * HD : width + (kind + 1) * HD]
                else:
                    level2 = low_r[kind, :, c]
                more = jnp.where(owns2, level2, gained[kind]).astype(F32)
                base = own_last[kind] if last else own_r[kind, :, c]
                out[:, c] = jnp.where(ok, base + more, 0.0).astype(BF16)

    page = ((PAGE, width), BF16, True)
    return kernel_call(body, facts, [*own0, mine, far, level2_far], [], [page, page])


def gather_tree(ids, own):
    leaves = lax.axis_size(("leaf", "sub"))
    owned = ids[:INNER] == ids[INNER] - 1
    pages = jnp.where(owned[:, None, None, None], own[None], jnp.zeros((), BF16))
    for bit in range(leaves.bit_length() - 1):
        active = spanning(leaves, bit)
        far = flipped(pages[:active], ("leaf", "sub"), 1 << bit)
        pages = jnp.concatenate([pages[:active] + far, pages[active:]])
    return pages


def reduce_tree(ids, parts):
    leaves = lax.axis_size(("leaf", "sub"))
    for bit in range(leaves.bit_length() - 1):
        active = spanning(leaves, bit)
        far = flipped(parts[:active], ("leaf", "sub"), 1 << bit)
        parts = jnp.concatenate([parts[:active] + far, parts[active:]])
    owned = ids[:INNER] == ids[INNER] - 1
    return jnp.sum(jnp.where(owned[:, None, None, None], parts, 0.0), axis=0)


def on_device(queries, grad_out, keys, values, log_norms, row_deltas, ancestors, counts, w_value):
    kv = keys.shape[1] // HD
    group = queries.shape[1] // keys.shape[1]
    leaves = lax.axis_size(("leaf", "sub"))
    hbm = lambda a: pltpu.with_memory_space_constraint(a, pltpu.HBM)
    side = lax.axis_index("tensor").astype(I32).reshape(1)
    two_sides = lax.axis_size("tensor") == 2
    inputs = [hbm(a) for a in (queries, grad_out, keys, values, log_norms, row_deltas)]
    facts, own = start(hbm(ancestors), hbm(counts), *inputs[2:4])
    state = {"done": frozenset()}

    def own_pages(kvs, pages, prior=(), after=()):
        return attend(True, kvs, group, facts, inputs, pages, state, prior, after)

    def shared_pages(kvs, pages, after=()):
        return attend(False, kvs, group, facts, inputs, pages, state, after=after)

    def spread(part):
        if two_sides:
            return flipped(part, "tensor", 1)
        return lax.all_gather(part, "tensor", axis=1, tiled=True)

    kvs = tuple(range(kv))
    w = hbm(w_value)
    if leaves == 8 and lax.axis_size("sub") == 2 and kv >= 3 and two_sides:
        level2, results = [], []

        def beside_pair(from_core, chip):
            level2.extend((own, from_core))
            results.append(own_pages(kvs[:1], level2, after=(chip,)))
            return (results[-1][3],)

        def beside_half(pair):
            results.append(own_pages(kvs[1:-1], level2, results[-1], (pair,)))
            return (results[-1][3],)

        shared = gather_small_tree(facts, own, beside_pair, beside_half)
        most = results[-1]
        far_v = [spread(most[1])]
        level2_far = flipped(most[3], "sub", 1)
        kept, sent = shared_pages(kvs, shared)
        total, root, root_far, next_far = over_cores(facts, kept, sent)
        last = own_pages(kvs[-1:], level2, after=(root, far_v[0], level2_far))
        far_v.append(spread(last[1]))
        total, far = over_halves(facts, total, root_far, next_far, (last[3],))
        both = list(zip(most, last))
        *grads, made = input_grad(facts, side, w, 2 * PAGE, both[1], far_v, both[:2])
        mine, far = over_chips(facts, total, far, last[3], (made,))
        dk0, dv0 = finish_small_tree(facts, both[2], mine, far, level2_far)
        far_v = spread(dv0)
        begun, w_far = begin_input_grad(facts, side, w, dv0)
        grads = end_input_grad(facts, far_v, begun, w_far, [dk0, dv0], grads)
        return (state["gq"], grads[1], grads[2], grads[0])

    first = lax.axis_index("sub") == 0
    path_ids = ancestors[0]
    pages = gather_tree(path_ids, own)
    dk12, dv12, own0, send2 = own_pages(kvs, (pages[2], pages[2]))
    kept, sent = shared_pages(
        kvs,
        (
            jnp.where(first, pages[:2, 0], pages[:2, 1]),
            jnp.where(first, pages[:2, 1], pages[:2, 0]),
        ),
    )
    sent = sent.astype(F32)
    upper = jnp.stack([jnp.where(first, kept, sent), jnp.where(first, sent, kept)], axis=1)
    low = send2.astype(F32)
    total = reduce_tree(path_ids, jnp.concatenate([upper, low[None]]))
    total += own0 - jnp.where(path_ids[2] == path_ids[INNER] - 1, low, 0.0)
    has = jnp.any(path_ids[:INNER] == path_ids[INNER] - 1)
    ok = (jnp.arange(PAGE) < jnp.where(has, counts[0, 0], 0))[:, None]
    dk0, dv0 = jnp.where(ok, total, 0.0).astype(BF16)
    if two_sides:
        pair = lambda part: ([part], [spread(part)])
    else:
        pair = lambda part: ([spread(part)], [])
    *grads, _ = input_grad(facts, side, w, 2 * PAGE, *pair(dv12), ([dk12], [dv12]))
    grads = input_grad(facts, side, w, PAGE, *pair(dv0), ([dk0], [dv0]), grads)
    return (state["gq"], grads[1], grads[2], grads[0])


def solution(mesh):
    placed = (
        P(("groups", "leaf", "sub"), "tensor"),
        P(("groups", "leaf", "sub"), "tensor"),
        P(("groups", "leaf", "sub"), "tensor"),
        P(("groups", "leaf", "sub"), "tensor"),
        P("tensor", ("groups", "leaf", "sub")),
        P("tensor", ("groups", "leaf", "sub")),
        P(("groups", "leaf", "sub"), None),
        P(("groups", "leaf", "sub"), None),
        P("tensor", None),
    )
    return jax.shard_map(
        on_device,
        mesh=mesh,
        in_specs=placed,
        out_specs=(
            P(("groups", "leaf", "sub"), "tensor"),
            P(("groups", "leaf", "sub"), "tensor"),
            P(("groups", "leaf", "sub"), "tensor"),
            P(("groups", "leaf", "sub"), "tensor"),
        ),
        check_vma=False,
    )
```

```python
import math

import jax
import jax.numpy as jnp
from jax import lax
from jax.experimental import pallas as pl
from jax.experimental.pallas import tpu as pltpu
from jax.sharding import PartitionSpec as P

HD = 128
PAGE = 128
SLOTS = 3
INNER = 3
ROWS = SLOTS * PAGE
LOG2E = math.log2(math.e)
SCALE = 1.0 / math.sqrt(HD)
BF16 = jnp.bfloat16
F32 = jnp.float32
I32 = jnp.int32
LARGE = 10 << 20
SMALL = 4 << 20
SLIGHT = pl.CostEstimate(flops=1000, bytes_accessed=1000, transcendentals=0)
BLOCKED = 1e30


def dot_t(left, right):
    return lax.dot_general(left, right, (((1,), (1,)), ((), ())), preferred_element_type=F32)


def dot_n(left, right):
    return lax.dot_general(left, right, (((1,), (0,)), ((), ())), preferred_element_type=F32)


FACTS = 16
N0, N1, N2, OWNS2, LIMIT, LEADS, ROOT_IN_CHIP, ROOT_IN_PAIR, NEXT_IN_CHIP = range(9)


def write_facts(facts, ids, counts):
    page = [ids[0, j] for j in range(INNER + 1)]
    own = page[INNER] - 1
    leaf = own // SLOTS
    owns = [page[j] == own for j in range(INNER)]
    same = lambda level, shift: ((page[level] // SLOTS) >> shift) == (leaf >> shift)
    number = lambda flag: jnp.where(flag, 1, 0)
    facts[N0] = jnp.where(owns[0] | owns[1] | owns[2], counts[0, 0], 0)
    facts[N1] = counts[0, 1]
    facts[N2] = counts[0, 2]
    facts[OWNS2] = number(owns[2])
    facts[LIMIT] = jnp.where(owns[2], 2 * PAGE, jnp.where(owns[1], PAGE, 0))
    facts[LEADS] = number(lax.rem(leaf, 2) == 0)
    facts[ROOT_IN_CHIP] = number(same(0, 1))
    facts[ROOT_IN_PAIR] = number(same(0, 2))
    facts[NEXT_IN_CHIP] = number(same(1, 1))
    for i in range(NEXT_IN_CHIP + 1, FACTS):
        facts[i] = 0


def row_ok(count, rows, width):
    return lax.broadcasted_iota(I32, (rows, width), 0) < count


def kernel_call(body, facts, near, far, outs, scratch=(), aliases=None, after=(), cost=None,
                limit=SMALL, hold=()):
    smem = pl.BlockSpec(memory_space=pltpu.SMEM)
    vmem = pl.BlockSpec(memory_space=pltpu.VMEM)
    hbm = pl.BlockSpec(memory_space=pl.ANY)
    near = [pltpu.with_memory_space_constraint(a, pltpu.VMEM) for a in near]
    hold = [pltpu.with_memory_space_constraint(a, pltpu.VMEM) for a in hold]
    place = {("near", i): 1 + i for i in range(len(near))}
    place |= {("far", i): 1 + len(near) + i for i in range(len(far))}
    used = 1 + len(near) + len(far)

    def kernel(*refs):
        body(*refs[:used], *refs[used + len(hold) + len(after) :])

    return pl.pallas_call(
        kernel,
        out_shape=tuple(
            pltpu.VMEM(s, d) if inside else jax.ShapeDtypeStruct(s, d) for s, d, inside in outs
        ),
        in_specs=[smem] + [vmem] * len(near) + [hbm] * len(far) + [vmem] * len(hold)
        + [hbm] * len(after),
        out_specs=tuple(vmem if inside else hbm for _, _, inside in outs),
        scratch_shapes=list(scratch),
        input_output_aliases={place[k]: v for k, v in (aliases or {}).items()},
        compiler_params=pltpu.CompilerParams(vmem_limit_bytes=limit),
        cost_estimate=cost or SLIGHT,
    )(pltpu.with_memory_space_constraint(facts, pltpu.SMEM), *near, *far, *hold, *after)


def start(ids, counts, keys, values):
    width = keys.shape[1]

    def body(ids_ref, counts_ref, k_ref, v_ref, facts, out, held, ids_s, counts_s, sem):
        copies = [
            pltpu.make_async_copy(src, dst, sem.at[i])
            for i, (src, dst) in enumerate(
                (
                    (ids_ref, ids_s),
                    (counts_ref, counts_s),
                    (k_ref.at[:PAGE], held.at[0]),
                    (v_ref.at[:PAGE], held.at[1]),
                )
            )
        ]
        for c in copies:
            c.start()
        copies[0].wait()
        copies[1].wait()
        write_facts(facts, ids_s, counts_s)
        ok = row_ok(counts_s[0, 0], PAGE, width)
        for i in range(2):
            copies[2 + i].wait()
            out[i] = jnp.where(ok, held[i], jnp.zeros((), BF16))

    smem = pl.BlockSpec(memory_space=pltpu.SMEM)
    hbm = pl.BlockSpec(memory_space=pl.ANY)
    return pl.pallas_call(
        body,
        out_shape=(pltpu.SMEM((FACTS,), I32), pltpu.VMEM((2, PAGE, width), BF16)),
        in_specs=[hbm] * 4,
        out_specs=(smem, pl.BlockSpec(memory_space=pltpu.VMEM)),
        scratch_shapes=[
            pltpu.VMEM((2, PAGE, width), BF16),
            pltpu.SMEM(ids.shape, I32),
            pltpu.SMEM(counts.shape, I32),
            pltpu.SemaphoreType.DMA((4,)),
        ],
        compiler_params=pltpu.CompilerParams(vmem_limit_bytes=SMALL),
    )(ids, counts, keys, values)


def row_terms(rows):
    high = rows.astype(BF16).astype(F32)
    rest = rows - high
    middle = rest.astype(BF16).astype(F32)
    parts = [high, middle, rest - middle]
    spare = HD - 3 * rows.shape[0]
    parts.append(jnp.zeros((spare, rows.shape[1]), F32))
    return jnp.concatenate(parts, axis=0).T.astype(BF16)


class Head:
    def __init__(self, kv, group, q, g, norms, deltas, en, ed):
        self.kv, self.group, self.q, self.g, self.en, self.ed = kv, group, q, g, en, ed
        self.heads = min(4, group)
        self.parts = group // self.heads
        self.tall = self.heads * PAGE
        heads = slice(kv * group, (kv + 1) * group)
        en[...] = row_terms(norms[heads, :])
        ed[...] = row_terms(deltas[heads, :])

    def lanes(self, part, j):
        at = self.kv * self.group * HD + part * (self.heads * HD) + j * HD
        return pl.ds(pl.multiple_of(at, HD), HD)

    def stacked(self, ref, part, slots):
        return jnp.concatenate(
            [
                ref[slot * PAGE : (slot + 1) * PAGE, self.lanes(part, j)]
                for slot in slots
                for j in range(self.heads)
            ],
            axis=0,
        )

    def deep(self, stacked, terms, part, slots):
        column = lax.broadcasted_iota(I32, (1, HD), 1) % self.group
        picks = [
            (column == part * self.heads + j).astype(F32).astype(BF16)
            for j in range(self.heads)
        ]
        extra = [
            terms[slot * PAGE : (slot + 1) * PAGE] * pick for slot in slots for pick in picks
        ]
        return jnp.concatenate([stacked, jnp.concatenate(extra, axis=0)], axis=1)

    def turned_at(self, part, slot, count):
        at = ((self.kv * self.parts + part) * SLOTS + slot) * self.tall
        return pl.ds(pl.multiple_of(at, self.tall), self.tall * count)

    def put_queries(self, part, slot, rows_by_head, dq, add, stage):
        rows = slice(slot * PAGE, (slot + 1) * PAGE)
        for j in range(self.heads):
            value = rows_by_head[j * PAGE : (j + 1) * PAGE]
            if stage is None:
                dq[rows, self.lanes(part, j)] = value
            else:
                if add:
                    value = value + dq[rows, self.lanes(part, j)]
                stage[rows, j * HD : (j + 1) * HD] = (value * SCALE).astype(BF16)


def set_keys(deep, upright, at, page):
    where = slice(at * PAGE, (at + 1) * PAGE)
    deep[:HD, where] = page.T
    if upright is not None:
        upright[where] = page


def weigh(scores, grads, keep):
    p = keep(jnp.exp2(scores * (SCALE * LOG2E)))
    return p.astype(BF16), (p * grads).astype(BF16)


def attend(own, kvs, group, facts, inputs, pages, state, prior=(), after=(), w=None,
           hold=()):
    loading = "loaded" not in state
    q, g, k, v, norms, deltas = inputs if loading else state["loaded"]
    count = len(kvs)
    parts = group // min(4, group)
    tall = min(4, group) * PAGE
    wide = min(4, group) * HD
    width = count * HD
    base = prior[0].shape[1] if prior else 0
    kv_total = k.shape[1] // HD
    fresh = [kv not in state["done"] for kv in kvs]
    names = ["dq", "qt", "gt"] + ([] if all(fresh) else ["gq"])
    turned = ((HD, kv_total * group * ROWS), BF16, True)
    full = {"dq": (q.shape, F32, True), "qt": turned, "gt": turned, "gq": (q.shape, BF16, False)}

    near, far, aliases, outs = [], [], {}, []
    at_near, at_far = {}, {}

    def add_near(name, array):
        at_near[name] = len(near)
        near.append(array)

    def add_far(name, array):
        at_far[name] = len(far)
        far.append(array)

    for name in names:
        outs.append(full[name])
        if name in state:
            if full[name][2]:
                add_near(name, state[name])
                aliases["near", at_near[name]] = len(outs) - 1
            else:
                add_far(name, state[name])
                aliases["far", at_far[name]] = len(outs) - 1
    at_results = len(outs)
    if own:
        outs += [
            ((2 * PAGE, base + width), BF16, True),
            ((2 * PAGE, base + width), BF16, True),
            ((2, PAGE, base + width), F32, True),
            ((2, PAGE, base + width), BF16, True),
        ]
    else:
        outs += [
            ((2, PAGE, width), F32, True),
            ((2, PAGE, width), BF16, True),
        ]
    at_loaded = len(outs)
    in_names = ["q", "g", "k", "v", "norms", "deltas"]
    in_arrays = [q, g, k, v, norms, deltas]
    for name, array in zip(in_names, in_arrays):
        if loading:
            add_far(name, array)
            outs.append((array.shape, array.dtype, True))
        else:
            add_near(name, array)
    at_end = len(outs)
    if w is not None:
        add_far("w", w)
        outs.append((w.shape, w.dtype, True))
    for i, page in enumerate(pages):
        add_near(("page", i), page)
    for i, array in enumerate(prior):
        add_near(("prior", i), array)
    key_pages = 4 if own else 2
    scratch = [
        pltpu.VMEM((2 * HD, key_pages * PAGE), BF16),
        pltpu.VMEM((2 * HD, key_pages * PAGE), BF16),
        pltpu.VMEM((key_pages * PAGE, HD), BF16),
        pltpu.VMEM((2, HD, key_pages * PAGE), F32),
        pltpu.VMEM((ROWS, HD), BF16),
        pltpu.VMEM((ROWS, HD), BF16),
        pltpu.VMEM((count * parts, ROWS, wide), BF16),
        pltpu.SemaphoreType.DMA((count * parts,)),
        pltpu.SemaphoreType.DMA((2 * kv_total + 5,)),
    ]
    cols = lambda a, b: slice(a * PAGE, b * PAGE)

    def body(facts, *refs):
        ins, out_refs = refs[: len(near) + len(far)], refs[len(near) + len(far) : -len(scratch)]
        k_deep, v_deep, k_up, acc, en, ed, stage, sem, load_sem = refs[-len(scratch) :]
        near_ref = lambda name: ins[at_near[name]]
        far_ref = lambda name: ins[len(near) + at_far[name]]
        held = dict(zip(names, out_refs))
        results = out_refs[at_results:at_loaded]
        copies = {}
        if loading:
            into = dict(zip(in_names, out_refs[at_loaded:at_end]))

            def load(key, name, columns=None):
                src, dst = far_ref(name), into[name]
                if columns is not None:
                    src, dst = src.at[:, columns], dst.at[:, columns]
                copies[key] = pltpu.make_async_copy(src, dst, load_sem.at[len(copies)])
                copies[key].start()

            for name in in_names[2:]:
                load(name, name)
            for kv in range(kv_total):
                at = slice(kv * group * HD, (kv + 1) * group * HD)
                load(("q", kv), "q", at)
                load(("g", kv), "g", at)
        else:
            into = {name: near_ref(name) for name in in_names}
        if w is not None:
            w_copy = pltpu.make_async_copy(
                far_ref("w"), out_refs[at_end], load_sem.at[2 * kv_total + 4]
            )
            w_copy.start()
        q, g, k, v, norms, deltas = (into[name] for name in in_names)

        def arrived(*keys):
            for key in keys:
                if key in copies:
                    copies.pop(key).wait()

        k_deep[HD:] = jnp.full((HD, key_pages * PAGE), -1.0, BF16)
        v_deep[HD:] = jnp.full((HD, key_pages * PAGE), -1.0, BF16)
        for out, i in zip(results, range(len(prior))):
            out[..., :base] = near_ref(("prior", i))[...]
        owns2, leads = facts[OWNS2] == 1, facts[LEADS] == 1
        if loading:
            arrived("norms", "deltas", "k", "v")
            lane = lax.broadcasted_iota(I32, norms.shape, 1)
            limit = jnp.where(
                lane < PAGE, facts[N0], jnp.where(lane < 2 * PAGE, facts[N1], facts[N2])
            )
            norms[...] = jnp.where(lane % PAGE < limit, norms[...] * (1.0 / SCALE), BLOCKED)
        lower = lambda rows: lax.broadcasted_iota(I32, (rows, PAGE), 1) <= (
            lax.broadcasted_iota(I32, (rows, PAGE), 0) % PAGE
        )

        def set_pages(n, kv):
            lane = slice(kv * HD, (kv + 1) * HD)
            first, second = (near_ref(("page", i)) for i in range(2))
            if own:
                zero = jnp.zeros((), BF16)
                for slot, (at, c) in enumerate(((3, N0), (0, N1), (2, N2))):
                    ok = row_ok(facts[c], PAGE, HD)
                    rows = cols(slot, slot + 1)
                    set_keys(k_deep, k_up, at, jnp.where(ok, k[rows, lane], zero))
                    set_keys(v_deep, None, at, jnp.where(ok, v[rows, lane], zero))
                level2 = [jnp.where(owns2, first[i, :, lane], second[i, :, lane]) for i in (0, 1)]
                set_keys(k_deep, k_up, 1, level2[0])
                set_keys(v_deep, None, 1, level2[1])
            else:
                for j in range(2):
                    mine, theirs = first[j, :, lane], second[j, :, lane]
                    set_keys(k_deep, k_up, j, jnp.where(leads, mine, theirs))
                    set_keys(v_deep, None, j, jnp.where(leads, theirs, mine))
            acc[...] = jnp.zeros_like(acc)

        def turned_rows(head, part, is_fresh, qs, gs, order):
            if is_fresh:
                for name, rows in (("qt", qs), ("gt", gs)):
                    for i, slot in enumerate(order):
                        held[name][:, head.turned_at(part, slot, 1)] = rows[
                            i * tall : (i + 1) * tall
                        ].T
            return lambda name, slot, slots: held[name][:, head.turned_at(part, slot, slots)]

        def own_part(head, part, n, stage_ref):
            order = (1, 2, 0)
            qs, gs = head.stacked(q, part, order), head.stacked(g, part, order)
            qd, gd = head.deep(qs, en, part, order), head.deep(gs, ed, part, order)
            turn = turned_rows(head, part, fresh[n], qs, gs, order)
            low = lower(tall)

            def keep_first(p):
                masked = jnp.where(low, p[:tall, :PAGE], 0.0)
                return jnp.concatenate(
                    [jnp.concatenate([masked, p[:tall, PAGE:]], axis=1), p[tall:]], axis=0
                )

            pa, da = weigh(
                dot_n(qd[: 2 * tall], k_deep[:, : 2 * PAGE]),
                dot_n(gd[: 2 * tall], v_deep[:, : 2 * PAGE]),
                keep_first,
            )
            both = lambda x: jnp.concatenate([x[:tall, :PAGE], x[tall:, PAGE:]], axis=0)
            low2 = lower(2 * tall)
            pb, db = weigh(
                both(dot_n(qd[tall:], k_deep[:, 2 * PAGE :])),
                both(dot_n(gd[tall:], v_deep[:, 2 * PAGE :])),
                lambda p: jnp.where(low2, p, 0.0),
            )
            for i, (name, a, b) in enumerate((("qt", da, db), ("gt", pa, pb))):
                acc[i, :, : 2 * PAGE] += dot_n(turn(name, 1, 2), a)
                acc[i, :, cols(2, 3)] += dot_n(turn(name, 2, 1), b[:tall])
                acc[i, :, cols(3, 4)] += dot_n(turn(name, 0, 1), b[tall:])
            first = dot_n(da, k_up[: 2 * PAGE])
            put = lambda slot, rows: head.put_queries(
                part, slot, rows, held["dq"], not fresh[n], stage_ref
            )
            put(1, first[:tall])
            put(2, first[tall:] + dot_n(db[:tall], k_up[cols(2, 3)]))
            put(0, dot_n(db[tall:], k_up[cols(3, 4)]))

        def shared_part(head, part, n, stage_ref):
            order = (0, 1, 2)
            qs, gs = head.stacked(q, part, order), head.stacked(g, part, order)
            qd, gd = head.deep(qs, en, part, order), head.deep(gs, ed, part, order)
            turn = turned_rows(head, part, fresh[n], qs, gs, order)
            column = lax.broadcasted_iota(I32, (tall, 2 * PAGE), 1)
            seen = column < facts[LIMIT]

            def keep(p):
                return jnp.concatenate([jnp.where(seen, p[:tall], 0.0), p[tall:]], axis=0)

            p, ds = weigh(dot_n(qd, k_deep[...]), dot_n(gd, v_deep[...]), keep)
            acc[0] += dot_n(turn("qt", 0, SLOTS), ds)
            acc[1] += dot_n(turn("gt", 0, SLOTS), p)
            dq = dot_n(ds, k_up[...])
            for slot in range(SLOTS):
                head.put_queries(
                    part, slot, dq[slot * tall : (slot + 1) * tall], held["dq"], not fresh[n],
                    stage_ref,
                )

        def put_own(n):
            dk12, dv12, own0, send2 = results
            here = slice(base + n * HD, base + (n + 1) * HD)
            grad = [acc[0].T * SCALE, acc[1].T]
            for at, c, to in ((0, N1, 0), (2, N2, 1)):
                ok = row_ok(facts[c], PAGE, HD)
                for kind, out in ((0, dk12), (1, dv12)):
                    out[cols(to, to + 1), here] = jnp.where(
                        ok, grad[kind][cols(at, at + 1)], 0.0
                    ).astype(BF16)
            for kind in range(2):
                level2 = grad[kind][cols(1, 2)]
                own0[kind, :, here] = grad[kind][cols(3, 4)] + jnp.where(owns2, level2, 0.0)
                send2[kind, :, here] = level2.astype(BF16)

        def put_shared(n):
            kept, sent = results
            here = slice(n * HD, (n + 1) * HD)
            grad_k, grad_v = acc[0].T * SCALE, acc[1].T
            for j in range(2):
                a, b = grad_k[cols(j, j + 1)], grad_v[cols(j, j + 1)]
                kept[j, :, here] = jnp.where(leads, a, b)
                sent[j, :, here] = jnp.where(leads, b, a).astype(BF16)

        sends = []
        for n, kv in enumerate(kvs):
            arrived(("q", kv), ("g", kv))
            head = Head(kv, group, q, g, norms, deltas, en, ed)
            set_pages(n, kv)

            def step(part, _, n=n, kv=kv, head=head):
                slot = n * parts + part
                (own_part if own else shared_part)(
                    head, part, n, None if fresh[n] else stage.at[slot]
                )
                if not fresh[n]:
                    at = pl.multiple_of((kv * parts + part) * wide, wide)
                    pltpu.make_async_copy(
                        stage.at[slot], held["gq"].at[:, pl.ds(at, wide)], sem.at[slot]
                    ).start()
                return 0

            for part in range(parts):
                step(part, 0)
            (put_own if own else put_shared)(n)
            if not fresh[n]:
                sends += [(n * parts + p, (kv * parts + p) * wide) for p in range(parts)]
        for slot, at in sends:
            pltpu.make_async_copy(
                stage.at[slot], held["gq"].at[:, at : at + wide], sem.at[slot]
            ).wait()
        arrived(*list(copies))
        if w is not None:
            w_copy.wait()

    made = kernel_call(
        body, facts, near, far, outs, scratch, aliases, after,
        pl.CostEstimate(
            flops=240 * PAGE * PAGE * HD * group * count, bytes_accessed=1000, transcendentals=0
        ),
        LARGE,
        hold,
    )
    for name, array in zip(names, made):
        state[name] = array
    state["done"] = state["done"] | set(kvs)
    if loading:
        state["loaded"] = made[at_loaded:at_end]
    return list(made[at_results:at_loaded]) + list(made[at_end:])


def width_tiles(w):
    tile = next(t for t in (512, 640, 320, 128, w.shape[0]) if w.shape[0] % t == 0)
    return [slice(i, i + tile) for i in range(0, w.shape[0], tile)]


def input_grad(facts, side, w, rows, own, far, grads, carry=None):
    out_cols, depth = w.shape
    tiles = width_tiles(w)
    top = 0 if rows == PAGE else PAGE
    steps = len(tiles)
    width = sum(a.shape[1] for a in grads[0])
    arrays = [*own, *far, *grads[0], *grads[1]]
    count = len(grads[0])
    carry = list(carry or [])

    def body(facts, flag, *refs):
        own_r, refs = refs[: len(own)], refs[len(own) :]
        far_r, refs = refs[: len(far)], refs[len(far) :]
        grad_r, w_ref = refs[: 2 * count], refs[2 * count]
        out, dk, dv, made, w_near, stage, w_sem, sem = refs[-8:]
        loads = [
            pltpu.make_async_copy(w_ref.at[at], w_near.at[at], w_sem.at[i])
            for i, at in enumerate(tiles)
        ]
        for c in loads:
            c.start()
        made[...] = jnp.zeros_like(made)
        columns = lambda rs: jnp.concatenate([r[...] for r in rs], axis=1)
        full = columns(own_r)
        if far:
            other, leads = columns(far_r), flag[0] == 0
            full = jnp.concatenate(
                [jnp.where(leads, full, other), jnp.where(leads, other, full)], axis=1
            )
        copies = put_rows(grad_r, dk, dv, top, rows, sem, steps)
        for i, at in enumerate(tiles):
            loads[i].wait()
            stage[i] = dot_t(w_near[at], full).astype(BF16).T
            copies.append(
                pltpu.make_async_copy(stage.at[i], out.at[top : top + rows, at], sem.at[i])
            )
            copies[-1].start()
        for c in copies:
            c.wait()

    smem = pl.BlockSpec(memory_space=pltpu.SMEM)
    vmem = pl.BlockSpec(memory_space=pltpu.VMEM)
    hbm = pl.BlockSpec(memory_space=pl.ANY)
    arrays = [pltpu.with_memory_space_constraint(a, pltpu.VMEM) for a in arrays]
    kept = jax.ShapeDtypeStruct((ROWS, width), BF16)
    return pl.pallas_call(
        body,
        out_shape=(
            jax.ShapeDtypeStruct((ROWS, out_cols), BF16), kept, kept, pltpu.VMEM((8, HD), F32)
        ),
        in_specs=[smem] * 2 + [vmem] * len(arrays) + [hbm] * (1 + len(carry)),
        out_specs=(hbm, hbm, hbm, vmem),
        scratch_shapes=[
            pltpu.VMEM(w.shape, BF16),
            pltpu.VMEM((steps, rows, out_cols // steps), BF16),
            pltpu.SemaphoreType.DMA((steps,)),
            pltpu.SemaphoreType.DMA((steps + 2 * count,)),
        ],
        input_output_aliases={3 + len(arrays) + i: i for i in range(len(carry))},
        compiler_params=pltpu.CompilerParams(vmem_limit_bytes=LARGE),
        cost_estimate=SLIGHT,
    )(pltpu.with_memory_space_constraint(facts, pltpu.SMEM), side, *arrays, w, *carry)


def put_rows(pieces, dk, dv, top, rows, sem, first):
    copies = []
    count = len(pieces) // 2
    for dst, mine in ((dk, pieces[:count]), (dv, pieces[count:])):
        at = 0
        for src in mine:
            here = dst.at[top : top + rows, at : at + src.shape[1]]
            copies.append(pltpu.make_async_copy(src, here, sem.at[first + len(copies)]))
            copies[-1].start()
            at += src.shape[1]
    return copies


def begin_input_grad(facts, side, w, own, after=()):
    out_cols, depth = w.shape
    half = depth // 2
    rows = own[0].shape[0]
    count = len(own)

    def body(facts, flag, w_ref, *refs):
        mine, out = jnp.concatenate([r[...] for r in refs[:count]], axis=1), refs[-1]
        where = pl.ds(pl.multiple_of(flag[0] * half, half), half)
        for at in width_tiles(w):
            out[at] = dot_t(w_ref[at, where], mine)

    smem = pl.BlockSpec(memory_space=pltpu.SMEM)
    vmem = pl.BlockSpec(memory_space=pltpu.VMEM)
    near = [pltpu.with_memory_space_constraint(a, pltpu.VMEM) for a in (w, *own)]

    def kernel(*refs):
        body(*refs[: 3 + count], refs[-1])

    return pl.pallas_call(
        kernel,
        out_shape=pltpu.VMEM((out_cols, rows), F32),
        in_specs=[smem, smem] + [vmem] * len(near) + [pl.BlockSpec(memory_space=pl.ANY)] * len(after),
        out_specs=vmem,
        compiler_params=pltpu.CompilerParams(vmem_limit_bytes=LARGE),
        cost_estimate=SLIGHT,
    )(pltpu.with_memory_space_constraint(facts, pltpu.SMEM), side, *near, *after)


def end_input_grad(facts, side, w, far, begun, grads, carry=None, after=()):
    tiles = width_tiles(w)
    out_cols, depth = w.shape
    half = depth // 2
    steps = len(tiles)
    rows = far[0].shape[0]
    top = 0 if rows == PAGE else PAGE
    width = sum(a.shape[1] for a in grads[0])
    near = [w, begun, *far, *grads[0], *grads[1]]
    carry = list(carry or [])

    def body(facts, flag, w_r, begun_r, *refs):
        far_r, grad_r = refs[: len(far)], refs[len(far) : len(near) - 2]
        out, dk, dv, made, stage, sem = refs[-6:]
        made[...] = jnp.zeros_like(made)
        copies = put_rows(grad_r, dk, dv, top, rows, sem, steps)
        other = jnp.concatenate([r[...] for r in far_r], axis=1)
        where = pl.ds(pl.multiple_of((1 - flag[0]) * half, half), half)
        for i, at in enumerate(tiles):
            stage[i] = (dot_t(w_r[at, where], other) + begun_r[at]).astype(BF16).T
            copies.append(
                pltpu.make_async_copy(stage.at[i], out.at[top : top + rows, at], sem.at[i])
            )
            copies[-1].start()
        for c in copies:
            c.wait()

    smem = pl.BlockSpec(memory_space=pltpu.SMEM)
    vmem = pl.BlockSpec(memory_space=pltpu.VMEM)
    hbm = pl.BlockSpec(memory_space=pl.ANY)
    near = [pltpu.with_memory_space_constraint(a, pltpu.VMEM) for a in near]
    kept = jax.ShapeDtypeStruct((ROWS, width), BF16)

    def kernel(*refs):
        body(*refs[: 2 + len(near)], *refs[2 + len(near) + len(carry) + len(after) :])

    return pl.pallas_call(
        kernel,
        out_shape=(
            jax.ShapeDtypeStruct((ROWS, out_cols), BF16), kept, kept, pltpu.VMEM((8, HD), F32)
        ),
        in_specs=[smem, smem] + [vmem] * len(near) + [hbm] * (len(carry) + len(after)),
        out_specs=(hbm, hbm, hbm, vmem),
        scratch_shapes=[
            pltpu.VMEM((steps, rows, out_cols // steps), BF16),
            pltpu.SemaphoreType.DMA((steps + 2 * len(grads[0]),)),
        ],
        input_output_aliases={2 + len(near) + i: i for i in range(len(carry))},
        compiler_params=pltpu.CompilerParams(vmem_limit_bytes=LARGE),
        cost_estimate=SLIGHT,
    )(pltpu.with_memory_space_constraint(facts, pltpu.SMEM), side, *near, *carry, *after)


def flipped(block, axis, bit):
    count = lax.axis_size(axis)
    return lax.ppermute(block, axis, [(i, i ^ bit) for i in range(count) if i ^ bit < count])


def spanning(leaves, bit_index):
    return len([j for j in range(INNER) if 2 << bit_index <= leaves >> j])


def gather_small_tree(facts, own, beside_pair, beside_half):
    two = (own.shape, BF16, True)
    page = (own.shape[1:], BF16, True)
    from_core = flipped(own, "sub", 1)

    def choose_chip(facts, own_ref, far_ref, out):
        for kind in range(2):
            for mine in range(2):

                @pl.when((facts[LEADS] != kind) & (facts[OWNS2] != mine))
                def _copy(kind=kind, mine=mine):
                    out[...] = (own_ref if mine else far_ref)[kind]

    (chip,) = kernel_call(choose_chip, facts, [own, from_core], [], [page])
    from_pair = flipped(chip, "leaf", 1)

    def choose_pair(facts, near_ref, far_ref, out):
        out[...] = jnp.where(facts[ROOT_IN_CHIP] == 1, near_ref[...], far_ref[...])

    after = beside_pair(from_core, chip)
    (pair,) = kernel_call(choose_pair, facts, [chip, from_pair], [], [page], after=after)
    from_half = flipped(pair, "leaf", 2)

    def choose_all(facts, chip_ref, pair_far, pair_ref, half_far, out):
        out[0] = jnp.where(facts[ROOT_IN_PAIR] == 1, pair_ref[...], half_far[...])
        out[1] = jnp.where(facts[NEXT_IN_CHIP] == 1, chip_ref[...], pair_far[...])

    after = beside_half(pair)
    (mine,) = kernel_call(
        choose_all, facts, [chip, from_pair, pair, from_half], [], [two], after=after
    )
    return mine, flipped(mine, "sub", 1)


def over_cores(facts, kept, sent, hold):
    width = kept.shape[-1]

    def body(_, near, away, total, root, next_one):
        for j, low in enumerate((root, next_one)):
            value = near[j] + away[j].astype(F32)
            total[j] = value
            low[...] = value.astype(BF16)

    page = ((PAGE, width), BF16, True)
    total, root, next_one = kernel_call(
        body, facts, [kept, flipped(sent, "sub", 1)], [],
        [((2, PAGE, width), F32, True), page, page], hold=hold,
    )
    return total, root, flipped(root, "leaf", 2), flipped(next_one, "leaf", 1)


def over_halves(facts, total, root_far, next_far, after, hold):
    width = total.shape[-1]

    def body(_, near, root_r, next_r, out, low):
        root = near[0] + root_r[...].astype(F32)
        out[0] = root
        low[...] = root.astype(BF16)
        out[1] = near[1] + next_r[...].astype(F32)

    total, low = kernel_call(
        body, facts, [total, root_far, next_far], [],
        [((2, PAGE, width), F32, True), ((PAGE, width), BF16, True)], after=after,
        hold=hold,
    )
    return total, low, flipped(low, "leaf", 1)


def over_chips(facts, total, far, passenger, after, hold):
    width = total.shape[-1]
    more = passenger.shape[-1]

    def body(facts, near, away, extra, out):
        root = near[0] + away[...].astype(F32)
        out[:, :width] = jnp.where(facts[ROOT_IN_CHIP] == 1, root, near[1]).astype(BF16)
        for kind in range(2):
            out[:, width + kind * more : width + (kind + 1) * more] = extra[kind]

    outs = [((PAGE, width + 2 * more), BF16, True)]
    (mine,) = kernel_call(
        body, facts, [total, far, passenger], [], outs, after=after, hold=hold
    )
    return mine, flipped(mine, "sub", 1)


def finish_small_tree(facts, own0, mine, far, level2_far, hold):
    width = sum(a.shape[-1] for a in own0)

    def body(facts, own_r, own_last, mine_r, far_r, low_r, dk, dv):
        owns2, leads = facts[OWNS2] == 1, facts[LEADS] == 1
        ok = row_ok(facts[N0], PAGE, HD)
        for at in range(0, width, HD):
            c = slice(at, at + HD)
            last = at + HD == width
            near, away = mine_r[:, c], far_r[:, c]
            gained = [jnp.where(leads, near, away), jnp.where(leads, away, near)]
            for kind, out in enumerate((dk, dv)):
                if last:
                    level2 = far_r[:, width + kind * HD : width + (kind + 1) * HD]
                else:
                    level2 = low_r[kind, :, c]
                more = jnp.where(owns2, level2, gained[kind]).astype(F32)
                base = own_last[kind] if last else own_r[kind, :, c]
                out[:, c] = jnp.where(ok, base + more, 0.0).astype(BF16)

    page = ((PAGE, width), BF16, True)
    return kernel_call(
        body, facts, [*own0, mine, far, level2_far], [], [page, page], hold=hold
    )


def gather_tree(ids, own):
    leaves = lax.axis_size(("leaf", "sub"))
    owned = ids[:INNER] == ids[INNER] - 1
    pages = jnp.where(owned[:, None, None, None], own[None], jnp.zeros((), BF16))
    for bit in range(leaves.bit_length() - 1):
        active = spanning(leaves, bit)
        far = flipped(pages[:active], ("leaf", "sub"), 1 << bit)
        pages = jnp.concatenate([pages[:active] + far, pages[active:]])
    return pages


def reduce_tree(ids, parts):
    leaves = lax.axis_size(("leaf", "sub"))
    for bit in range(leaves.bit_length() - 1):
        active = spanning(leaves, bit)
        far = flipped(parts[:active], ("leaf", "sub"), 1 << bit)
        parts = jnp.concatenate([parts[:active] + far, parts[active:]])
    owned = ids[:INNER] == ids[INNER] - 1
    return jnp.sum(jnp.where(owned[:, None, None, None], parts, 0.0), axis=0)


def on_device(queries, grad_out, keys, values, log_norms, row_deltas, ancestors, counts, w_value):
    kv = keys.shape[1] // HD
    group = queries.shape[1] // keys.shape[1]
    leaves = lax.axis_size(("leaf", "sub"))
    hbm = lambda a: pltpu.with_memory_space_constraint(a, pltpu.HBM)
    side = lax.axis_index("tensor").astype(I32).reshape(1)
    two_sides = lax.axis_size("tensor") == 2
    inputs = [hbm(a) for a in (queries, grad_out, keys, values, log_norms, row_deltas)]
    facts, own = start(hbm(ancestors), hbm(counts), *inputs[2:4])
    state = {"done": frozenset()}

    def own_pages(kvs, pages, prior=(), after=(), hold=()):
        return attend(True, kvs, group, facts, inputs, pages, state, prior, after, hold=hold)

    def shared_pages(kvs, pages, after=(), w=None):
        return attend(False, kvs, group, facts, inputs, pages, state, after=after, w=w)

    def spread(part):
        if two_sides:
            return flipped(part, "tensor", 1)
        return lax.all_gather(part, "tensor", axis=1, tiled=True)

    kvs = tuple(range(kv))
    w = hbm(w_value)
    if leaves == 8 and lax.axis_size("sub") == 2 and kv >= 3 and two_sides:
        level2, results = [], []

        def beside_pair(from_core, chip):
            level2.extend((own, from_core))
            results.append(own_pages(kvs[:1], level2, after=(chip,)))
            return (results[-1][3],)

        def beside_half(pair):
            results.append(own_pages(kvs[1:-1], level2, results[-1], (pair,)))
            return (results[-1][3],)

        shared = gather_small_tree(facts, own, beside_pair, beside_half)
        most = results[-1]
        far_v = [spread(most[1])]
        level2_far = flipped(most[3], "sub", 1)
        kept, sent, w_near = shared_pages(kvs, shared, w=w)
        hold = (w_near,)
        total, root, root_far, next_far = over_cores(facts, kept, sent, hold)
        last = own_pages(kvs[-1:], level2, after=(root,), hold=hold)
        both = list(zip(most, last))
        begun = begin_input_grad(facts, side, w_near, both[1], (far_v[0], level2_far))
        far_v.append(spread(last[1]))
        total, low, far = over_halves(facts, total, root_far, next_far, (begun,), hold)
        *grads, made = end_input_grad(facts, side, w_near, far_v, begun, both[:2], after=(low,))
        mine, far = over_chips(facts, total, far, last[3], (made,), hold)
        dk0, dv0 = finish_small_tree(facts, both[2], mine, far, level2_far, hold)
        far_v = spread(dv0)
        begun = begin_input_grad(facts, side, w_near, [dv0])
        grads = end_input_grad(facts, side, w_near, [far_v], begun, ([dk0], [dv0]), grads)
        return (state["gq"], grads[1], grads[2], grads[0])

    first = lax.axis_index("sub") == 0
    path_ids = ancestors[0]
    pages = gather_tree(path_ids, own)
    dk12, dv12, own0, send2 = own_pages(kvs, (pages[2], pages[2]))
    kept, sent = shared_pages(
        kvs,
        (
            jnp.where(first, pages[:2, 0], pages[:2, 1]),
            jnp.where(first, pages[:2, 1], pages[:2, 0]),
        ),
    )
    sent = sent.astype(F32)
    upper = jnp.stack([jnp.where(first, kept, sent), jnp.where(first, sent, kept)], axis=1)
    low = send2.astype(F32)
    total = reduce_tree(path_ids, jnp.concatenate([upper, low[None]]))
    total += own0 - jnp.where(path_ids[2] == path_ids[INNER] - 1, low, 0.0)
    has = jnp.any(path_ids[:INNER] == path_ids[INNER] - 1)
    ok = (jnp.arange(PAGE) < jnp.where(has, counts[0, 0], 0))[:, None]
    dk0, dv0 = jnp.where(ok, total, 0.0).astype(BF16)
    if two_sides:
        pair = lambda part: ([part], [spread(part)])
    else:
        pair = lambda part: ([spread(part)], [])
    *grads, _ = input_grad(facts, side, w, 2 * PAGE, *pair(dv12), ([dk12], [dv12]))
    grads = input_grad(facts, side, w, PAGE, *pair(dv0), ([dk0], [dv0]), grads)
    return (state["gq"], grads[1], grads[2], grads[0])


def solution(mesh):
    placed = (
        P(("groups", "leaf", "sub"), "tensor"),
        P(("groups", "leaf", "sub"), "tensor"),
        P(("groups", "leaf", "sub"), "tensor"),
        P(("groups", "leaf", "sub"), "tensor"),
        P("tensor", ("groups", "leaf", "sub")),
        P("tensor", ("groups", "leaf", "sub")),
        P(("groups", "leaf", "sub"), None),
        P(("groups", "leaf", "sub"), None),
        P("tensor", None),
    )
    return jax.shard_map(
        on_device,
        mesh=mesh,
        in_specs=placed,
        out_specs=(
            P(("groups", "leaf", "sub"), "tensor"),
            P(("groups", "leaf", "sub"), "tensor"),
            P(("groups", "leaf", "sub"), "tensor"),
            P(("groups", "leaf", "sub"), "tensor"),
        ),
        check_vma=False,
    )
```

```python
import math

import jax
import jax.numpy as jnp
from jax import lax
from jax.experimental import pallas as pl
from jax.experimental.pallas import tpu as pltpu
from jax.sharding import PartitionSpec as P

HD = 128
PAGE = 128
SLOTS = 3
INNER = 3
ROWS = SLOTS * PAGE
LOG2E = math.log2(math.e)
SCALE = 1.0 / math.sqrt(HD)
BF16 = jnp.bfloat16
F32 = jnp.float32
I32 = jnp.int32
LARGE = 10 << 20
SMALL = 4 << 20
SLIGHT = pl.CostEstimate(flops=1000, bytes_accessed=1000, transcendentals=0)
BLOCKED = 1e30


def dot_t(left, right):
    return lax.dot_general(left, right, (((1,), (1,)), ((), ())), preferred_element_type=F32)


def dot_n(left, right):
    return lax.dot_general(left, right, (((1,), (0,)), ((), ())), preferred_element_type=F32)


FACTS = 16
N0, N1, N2, OWNS2, LIMIT, LEADS, ROOT_IN_CHIP, ROOT_IN_PAIR, NEXT_IN_CHIP = range(9)


def write_facts(facts, ids, counts):
    page = [ids[0, j] for j in range(INNER + 1)]
    own = page[INNER] - 1
    leaf = own // SLOTS
    owns = [page[j] == own for j in range(INNER)]
    same = lambda level, shift: ((page[level] // SLOTS) >> shift) == (leaf >> shift)
    number = lambda flag: jnp.where(flag, 1, 0)
    facts[N0] = jnp.where(owns[0] | owns[1] | owns[2], counts[0, 0], 0)
    facts[N1] = counts[0, 1]
    facts[N2] = counts[0, 2]
    facts[OWNS2] = number(owns[2])
    facts[LIMIT] = jnp.where(owns[2], 2 * PAGE, jnp.where(owns[1], PAGE, 0))
    facts[LEADS] = number(lax.rem(leaf, 2) == 0)
    facts[ROOT_IN_CHIP] = number(same(0, 1))
    facts[ROOT_IN_PAIR] = number(same(0, 2))
    facts[NEXT_IN_CHIP] = number(same(1, 1))
    for i in range(NEXT_IN_CHIP + 1, FACTS):
        facts[i] = 0


def row_ok(count, rows, width):
    return lax.broadcasted_iota(I32, (rows, width), 0) < count


def kernel_call(body, facts, near, far, outs, scratch=(), aliases=None, after=(), cost=None,
                limit=SMALL):
    smem = pl.BlockSpec(memory_space=pltpu.SMEM)
    vmem = pl.BlockSpec(memory_space=pltpu.VMEM)
    hbm = pl.BlockSpec(memory_space=pl.ANY)
    near = [pltpu.with_memory_space_constraint(a, pltpu.VMEM) for a in near]
    place = {("near", i): 1 + i for i in range(len(near))}
    place |= {("far", i): 1 + len(near) + i for i in range(len(far))}
    used = 1 + len(near) + len(far)

    def kernel(*refs):
        body(*refs[:used], *refs[used + len(after) :])

    return pl.pallas_call(
        kernel,
        out_shape=tuple(
            pltpu.VMEM(s, d) if inside else jax.ShapeDtypeStruct(s, d) for s, d, inside in outs
        ),
        in_specs=[smem] + [vmem] * len(near) + [hbm] * (len(far) + len(after)),
        out_specs=tuple(vmem if inside else hbm for _, _, inside in outs),
        scratch_shapes=list(scratch),
        input_output_aliases={place[k]: v for k, v in (aliases or {}).items()},
        compiler_params=pltpu.CompilerParams(vmem_limit_bytes=limit),
        cost_estimate=cost or SLIGHT,
    )(pltpu.with_memory_space_constraint(facts, pltpu.SMEM), *near, *far, *after)


def start(ids, counts, keys, values):
    width = keys.shape[1]

    def body(ids_ref, counts_ref, k_ref, v_ref, facts, out, held, ids_s, counts_s, sem):
        copies = [
            pltpu.make_async_copy(src, dst, sem.at[i])
            for i, (src, dst) in enumerate(
                (
                    (ids_ref, ids_s),
                    (counts_ref, counts_s),
                    (k_ref.at[:PAGE], held.at[0]),
                    (v_ref.at[:PAGE], held.at[1]),
                )
            )
        ]
        for c in copies:
            c.start()
        copies[0].wait()
        copies[1].wait()
        write_facts(facts, ids_s, counts_s)
        ok = row_ok(counts_s[0, 0], PAGE, width)
        for i in range(2):
            copies[2 + i].wait()
            out[i] = jnp.where(ok, held[i], jnp.zeros((), BF16))

    smem = pl.BlockSpec(memory_space=pltpu.SMEM)
    hbm = pl.BlockSpec(memory_space=pl.ANY)
    return pl.pallas_call(
        body,
        out_shape=(pltpu.SMEM((FACTS,), I32), pltpu.VMEM((2, PAGE, width), BF16)),
        in_specs=[hbm] * 4,
        out_specs=(smem, pl.BlockSpec(memory_space=pltpu.VMEM)),
        scratch_shapes=[
            pltpu.VMEM((2, PAGE, width), BF16),
            pltpu.SMEM(ids.shape, I32),
            pltpu.SMEM(counts.shape, I32),
            pltpu.SemaphoreType.DMA((4,)),
        ],
        compiler_params=pltpu.CompilerParams(vmem_limit_bytes=SMALL),
    )(ids, counts, keys, values)


def row_terms(rows):
    high = rows.astype(BF16).astype(F32)
    rest = rows - high
    middle = rest.astype(BF16).astype(F32)
    parts = [high, middle, rest - middle]
    spare = HD - 3 * rows.shape[0]
    parts.append(jnp.zeros((spare, rows.shape[1]), F32))
    return jnp.concatenate(parts, axis=0).T.astype(BF16)


class Head:
    def __init__(self, kv, group, norms, deltas, en, ed):
        self.group = group
        self.heads = min(4, group)
        self.parts = group // self.heads
        self.tall = self.heads * PAGE
        heads = slice(kv * group, (kv + 1) * group)
        en[...] = row_terms(norms[heads, :])
        ed[...] = row_terms(deltas[heads, :])

    def lanes(self, part, j):
        at = (part * self.heads + j) * HD
        return slice(at, at + HD)

    def stacked(self, ref, part, slots):
        return jnp.concatenate(
            [
                ref[slot * PAGE : (slot + 1) * PAGE, self.lanes(part, j)]
                for slot in slots
                for j in range(self.heads)
            ],
            axis=0,
        )

    def deep(self, stacked, terms, part, slots):
        column = lax.broadcasted_iota(I32, (1, HD), 1) % self.group
        picks = [
            (column == part * self.heads + j).astype(F32).astype(BF16)
            for j in range(self.heads)
        ]
        extra = [
            terms[slot * PAGE : (slot + 1) * PAGE] * pick for slot in slots for pick in picks
        ]
        return jnp.concatenate([stacked, jnp.concatenate(extra, axis=0)], axis=1)

    def turned_at(self, part, slot, count):
        at = (part * SLOTS + slot) * self.tall
        return slice(at, at + self.tall * count)

    def put_queries(self, part, slot, rows_by_head, dq, add, stage):
        rows = slice(slot * PAGE, (slot + 1) * PAGE)
        for j in range(self.heads):
            value = rows_by_head[j * PAGE : (j + 1) * PAGE]
            if stage is None:
                dq[rows, self.lanes(part, j)] = value
            else:
                if add:
                    value = value + dq[rows, self.lanes(part, j)]
                stage[rows, j * HD : (j + 1) * HD] = (value * SCALE).astype(BF16)


def set_keys(deep, upright, at, page):
    where = slice(at * PAGE, (at + 1) * PAGE)
    deep[:HD, where] = page.T
    if upright is not None:
        upright[where] = page


def weigh(scores, grads, keep):
    p = keep(jnp.exp2(scores * (SCALE * LOG2E)))
    return p.astype(BF16), (p * grads).astype(BF16)


def attend(own, kvs, group, facts, inputs, pages, state, prior=(), after=(), w=None):
    loading = "k" not in state
    q_all, k_all = inputs[0], inputs[2]
    count = len(kvs)
    parts = group // min(4, group)
    tall = min(4, group) * PAGE
    wide = min(4, group) * HD
    width = count * HD
    base = prior[0].shape[1] if prior else 0
    kv_total = k_all.shape[1] // HD
    fresh = [("dq", kv) not in state for kv in kvs]
    one_head = (ROWS, group * HD)
    turned = ((HD, group * ROWS), BF16, True)
    shapes = {"dq": (one_head, F32, True), "qt": turned, "gt": turned}

    near, far, aliases, outs = [], [], {}, []
    at_near, at_far, at_out = {}, {}, {}

    def add_near(name, array):
        at_near[name] = len(near)
        near.append(array)

    def add_far(name, array):
        at_far[name] = len(far)
        far.append(array)

    def add_out(name, out):
        at_out[name] = len(outs)
        outs.append(out)

    for kv, is_fresh in zip(kvs, fresh):
        for name, shape in shapes.items():
            if is_fresh:
                add_out((name, kv), shape)
            else:
                add_near((name, kv), state[name, kv])
    if not all(fresh):
        add_out("gq", (q_all.shape, BF16, False))
        if "gq" in state:
            add_far("gq", state["gq"])
            aliases["far", at_far["gq"]] = at_out["gq"]
    at_results = len(outs)
    if own:
        outs += [
            ((2 * PAGE, base + width), BF16, True),
            ((2 * PAGE, base + width), BF16, True),
            ((2, PAGE, base + width), F32, True),
            ((2, PAGE, base + width), BF16, True),
        ]
    else:
        outs += [
            ((2, PAGE, width), F32, True),
            ((2, PAGE, width), BF16, True),
        ]
    at_loaded = len(outs)
    if loading:
        for name, array in zip(("q", "g", "k", "v", "norms", "deltas"), inputs):
            add_far(name, array)
            if name in ("q", "g"):
                for kv in range(kv_total):
                    add_out((name, kv), (one_head, BF16, True))
            else:
                add_out(name, (array.shape, array.dtype, True))
    else:
        for name in ("k", "v", "norms", "deltas"):
            add_near(name, state[name])
        for kv in kvs:
            for name in ("q", "g"):
                add_near((name, kv), state[name, kv])
    at_end = len(outs)
    if w is not None:
        add_far("w", w)
        outs.append((w.shape, w.dtype, True))
    for i, page in enumerate(pages):
        add_near(("page", i), page)
    for i, array in enumerate(prior):
        add_near(("prior", i), array)
    key_pages = 4 if own else 2
    scratch = [
        pltpu.VMEM((2 * HD, key_pages * PAGE), BF16),
        pltpu.VMEM((2 * HD, key_pages * PAGE), BF16),
        pltpu.VMEM((key_pages * PAGE, HD), BF16),
        pltpu.VMEM((2, HD, key_pages * PAGE), F32),
        pltpu.VMEM((ROWS, HD), BF16),
        pltpu.VMEM((ROWS, HD), BF16),
        pltpu.VMEM((count * parts, ROWS, wide), BF16),
        pltpu.SemaphoreType.DMA((count * parts,)),
        pltpu.SemaphoreType.DMA((2 * kv_total + 5,)),
    ]
    cols = lambda a, b: slice(a * PAGE, b * PAGE)

    def body(facts, *refs):
        ins, out_refs = refs[: len(near) + len(far)], refs[len(near) + len(far) : -len(scratch)]
        k_deep, v_deep, k_up, acc, en, ed, stage, sem, load_sem = refs[-len(scratch) :]
        near_ref = lambda name: ins[at_near[name]]
        far_ref = lambda name: ins[len(near) + at_far[name]]
        held = lambda name: out_refs[at_out[name]] if name in at_out else near_ref(name)
        results = out_refs[at_results:at_loaded]
        copies = {}
        if loading:

            def load(key, src):
                copies[key] = pltpu.make_async_copy(src, held(key), load_sem.at[len(copies)])
                copies[key].start()

            for name in ("k", "v", "norms", "deltas"):
                load(name, far_ref(name))
            for kv in range(kv_total):
                at = slice(kv * group * HD, (kv + 1) * group * HD)
                for name in ("q", "g"):
                    load((name, kv), far_ref(name).at[:, at])
        if w is not None:
            w_copy = pltpu.make_async_copy(
                far_ref("w"), out_refs[at_end], load_sem.at[2 * kv_total + 4]
            )
            w_copy.start()
        k, v, norms, deltas = (held(name) for name in ("k", "v", "norms", "deltas"))

        def arrived(*keys):
            for key in keys:
                if key in copies:
                    copies.pop(key).wait()

        k_deep[HD:] = jnp.full((HD, key_pages * PAGE), -1.0, BF16)
        v_deep[HD:] = jnp.full((HD, key_pages * PAGE), -1.0, BF16)
        for out, i in zip(results, range(len(prior))):
            out[..., :base] = near_ref(("prior", i))[...]
        owns2, leads = facts[OWNS2] == 1, facts[LEADS] == 1
        if loading:
            arrived("norms", "deltas", "k", "v")
            lane = lax.broadcasted_iota(I32, norms.shape, 1)
            limit = jnp.where(
                lane < PAGE, facts[N0], jnp.where(lane < 2 * PAGE, facts[N1], facts[N2])
            )
            norms[...] = jnp.where(lane % PAGE < limit, norms[...] * (1.0 / SCALE), BLOCKED)
        lower = lambda rows: lax.broadcasted_iota(I32, (rows, PAGE), 1) <= (
            lax.broadcasted_iota(I32, (rows, PAGE), 0) % PAGE
        )

        def set_pages(n, kv):
            lane = slice(kv * HD, (kv + 1) * HD)
            first, second = (near_ref(("page", i)) for i in range(2))
            if own:
                zero = jnp.zeros((), BF16)
                for slot, (at, c) in enumerate(((3, N0), (0, N1), (2, N2))):
                    ok = row_ok(facts[c], PAGE, HD)
                    rows = cols(slot, slot + 1)
                    set_keys(k_deep, k_up, at, jnp.where(ok, k[rows, lane], zero))
                    set_keys(v_deep, None, at, jnp.where(ok, v[rows, lane], zero))
                level2 = [jnp.where(owns2, first[i, :, lane], second[i, :, lane]) for i in (0, 1)]
                set_keys(k_deep, k_up, 1, level2[0])
                set_keys(v_deep, None, 1, level2[1])
            else:
                for j in range(2):
                    mine, theirs = first[j, :, lane], second[j, :, lane]
                    set_keys(k_deep, k_up, j, jnp.where(leads, mine, theirs))
                    set_keys(v_deep, None, j, jnp.where(leads, theirs, mine))
            acc[...] = jnp.zeros_like(acc)

        def turned_rows(head, kv, part, is_fresh, qs, gs, order):
            if is_fresh:
                for name, rows in (("qt", qs), ("gt", gs)):
                    for i, slot in enumerate(order):
                        held((name, kv))[:, head.turned_at(part, slot, 1)] = rows[
                            i * tall : (i + 1) * tall
                        ].T
            return lambda name, slot, slots: held((name, kv))[
                :, head.turned_at(part, slot, slots)
            ]

        def own_part(head, kv, part, n, stage_ref):
            order = (1, 2, 0)
            qs = head.stacked(held(("q", kv)), part, order)
            gs = head.stacked(held(("g", kv)), part, order)
            qd, gd = head.deep(qs, en, part, order), head.deep(gs, ed, part, order)
            turn = turned_rows(head, kv, part, fresh[n], qs, gs, order)
            low = lower(tall)

            def keep_first(p):
                masked = jnp.where(low, p[:tall, :PAGE], 0.0)
                return jnp.concatenate(
                    [jnp.concatenate([masked, p[:tall, PAGE:]], axis=1), p[tall:]], axis=0
                )

            pa, da = weigh(
                dot_n(qd[: 2 * tall], k_deep[:, : 2 * PAGE]),
                dot_n(gd[: 2 * tall], v_deep[:, : 2 * PAGE]),
                keep_first,
            )
            both = lambda x: jnp.concatenate([x[:tall, :PAGE], x[tall:, PAGE:]], axis=0)
            low2 = lower(2 * tall)
            pb, db = weigh(
                both(dot_n(qd[tall:], k_deep[:, 2 * PAGE :])),
                both(dot_n(gd[tall:], v_deep[:, 2 * PAGE :])),
                lambda p: jnp.where(low2, p, 0.0),
            )
            for i, (name, a, b) in enumerate((("qt", da, db), ("gt", pa, pb))):
                acc[i, :, : 2 * PAGE] += dot_n(turn(name, 1, 2), a)
                acc[i, :, cols(2, 3)] += dot_n(turn(name, 2, 1), b[:tall])
                acc[i, :, cols(3, 4)] += dot_n(turn(name, 0, 1), b[tall:])
            first = dot_n(da, k_up[: 2 * PAGE])
            put = lambda slot, rows: head.put_queries(
                part, slot, rows, held(("dq", kv)), not fresh[n], stage_ref
            )
            put(1, first[:tall])
            put(2, first[tall:] + dot_n(db[:tall], k_up[cols(2, 3)]))
            put(0, dot_n(db[tall:], k_up[cols(3, 4)]))

        def shared_part(head, kv, part, n, stage_ref):
            order = (0, 1, 2)
            qs = head.stacked(held(("q", kv)), part, order)
            gs = head.stacked(held(("g", kv)), part, order)
            qd, gd = head.deep(qs, en, part, order), head.deep(gs, ed, part, order)
            turn = turned_rows(head, kv, part, fresh[n], qs, gs, order)
            column = lax.broadcasted_iota(I32, (tall, 2 * PAGE), 1)
            seen = column < facts[LIMIT]

            def keep(p):
                return jnp.concatenate([jnp.where(seen, p[:tall], 0.0), p[tall:]], axis=0)

            p, ds = weigh(dot_n(qd, k_deep[...]), dot_n(gd, v_deep[...]), keep)
            acc[0] += dot_n(turn("qt", 0, SLOTS), ds)
            acc[1] += dot_n(turn("gt", 0, SLOTS), p)
            dq = dot_n(ds, k_up[...])
            for slot in range(SLOTS):
                head.put_queries(
                    part, slot, dq[slot * tall : (slot + 1) * tall], held(("dq", kv)), not fresh[n],
                    stage_ref,
                )

        def put_own(n):
            dk12, dv12, own0, send2 = results
            here = slice(base + n * HD, base + (n + 1) * HD)
            grad = [acc[0].T * SCALE, acc[1].T]
            for at, c, to in ((0, N1, 0), (2, N2, 1)):
                ok = row_ok(facts[c], PAGE, HD)
                for kind, out in ((0, dk12), (1, dv12)):
                    out[cols(to, to + 1), here] = jnp.where(
                        ok, grad[kind][cols(at, at + 1)], 0.0
                    ).astype(BF16)
            for kind in range(2):
                level2 = grad[kind][cols(1, 2)]
                own0[kind, :, here] = grad[kind][cols(3, 4)] + jnp.where(owns2, level2, 0.0)
                send2[kind, :, here] = level2.astype(BF16)

        def put_shared(n):
            kept, sent = results
            here = slice(n * HD, (n + 1) * HD)
            grad_k, grad_v = acc[0].T * SCALE, acc[1].T
            for j in range(2):
                a, b = grad_k[cols(j, j + 1)], grad_v[cols(j, j + 1)]
                kept[j, :, here] = jnp.where(leads, a, b)
                sent[j, :, here] = jnp.where(leads, b, a).astype(BF16)

        sends = []
        for n, kv in enumerate(kvs):
            arrived(("q", kv), ("g", kv))
            head = Head(kv, group, norms, deltas, en, ed)
            set_pages(n, kv)

            for part in range(parts):
                slot = n * parts + part
                (own_part if own else shared_part)(
                    head, kv, part, n, None if fresh[n] else stage.at[slot]
                )
                if not fresh[n]:
                    at = (kv * parts + part) * wide
                    sends.append(
                        pltpu.make_async_copy(
                            stage.at[slot], held("gq").at[:, at : at + wide], sem.at[slot]
                        )
                    )
                    sends[-1].start()

            (put_own if own else put_shared)(n)
        for c in sends:
            c.wait()
        arrived(*list(copies))
        if w is not None:
            w_copy.wait()

    made = kernel_call(
        body, facts, near, far, outs, scratch, aliases, after,
        pl.CostEstimate(
            flops=240 * PAGE * PAGE * HD * group * count, bytes_accessed=1000, transcendentals=0
        ),
        LARGE,
    )
    for name, at in at_out.items():
        state[name] = made[at]
    return list(made[at_results:at_loaded]) + list(made[at_end:])


def width_tiles(w):
    tile = next(t for t in (512, 640, 320, 128, w.shape[0]) if w.shape[0] % t == 0)
    return [slice(i, i + tile) for i in range(0, w.shape[0], tile)]


def input_grad(facts, side, w, rows, own, far, grads, carry=None):
    out_cols, depth = w.shape
    tiles = width_tiles(w)
    top = 0 if rows == PAGE else PAGE
    steps = len(tiles)
    width = sum(a.shape[1] for a in grads[0])
    arrays = [*own, *far, *grads[0], *grads[1]]
    count = len(grads[0])
    carry = list(carry or [])

    def body(facts, flag, *refs):
        own_r, refs = refs[: len(own)], refs[len(own) :]
        far_r, refs = refs[: len(far)], refs[len(far) :]
        grad_r, w_ref = refs[: 2 * count], refs[2 * count]
        out, dk, dv, made, w_near, stage, w_sem, sem = refs[-8:]
        loads = [
            pltpu.make_async_copy(w_ref.at[at], w_near.at[at], w_sem.at[i])
            for i, at in enumerate(tiles)
        ]
        for c in loads:
            c.start()
        made[...] = jnp.zeros_like(made)
        columns = lambda rs: jnp.concatenate([r[...] for r in rs], axis=1)
        full = columns(own_r)
        if far:
            other, leads = columns(far_r), flag[0] == 0
            full = jnp.concatenate(
                [jnp.where(leads, full, other), jnp.where(leads, other, full)], axis=1
            )
        copies = put_rows(grad_r, dk, dv, top, rows, sem, steps)
        for i, at in enumerate(tiles):
            loads[i].wait()
            stage[i] = dot_t(w_near[at], full).astype(BF16).T
            copies.append(
                pltpu.make_async_copy(stage.at[i], out.at[top : top + rows, at], sem.at[i])
            )
            copies[-1].start()
        for c in copies:
            c.wait()

    smem = pl.BlockSpec(memory_space=pltpu.SMEM)
    vmem = pl.BlockSpec(memory_space=pltpu.VMEM)
    hbm = pl.BlockSpec(memory_space=pl.ANY)
    arrays = [pltpu.with_memory_space_constraint(a, pltpu.VMEM) for a in arrays]
    kept = jax.ShapeDtypeStruct((ROWS, width), BF16)
    return pl.pallas_call(
        body,
        out_shape=(
            jax.ShapeDtypeStruct((ROWS, out_cols), BF16), kept, kept, pltpu.VMEM((8, HD), F32)
        ),
        in_specs=[smem] * 2 + [vmem] * len(arrays) + [hbm] * (1 + len(carry)),
        out_specs=(hbm, hbm, hbm, vmem),
        scratch_shapes=[
            pltpu.VMEM(w.shape, BF16),
            pltpu.VMEM((steps, rows, out_cols // steps), BF16),
            pltpu.SemaphoreType.DMA((steps,)),
            pltpu.SemaphoreType.DMA((steps + 2 * count,)),
        ],
        input_output_aliases={3 + len(arrays) + i: i for i in range(len(carry))},
        compiler_params=pltpu.CompilerParams(vmem_limit_bytes=LARGE),
        cost_estimate=SLIGHT,
    )(pltpu.with_memory_space_constraint(facts, pltpu.SMEM), side, *arrays, w, *carry)


def put_rows(pieces, dk, dv, top, rows, sem, first):
    copies = []
    count = len(pieces) // 2
    for dst, mine in ((dk, pieces[:count]), (dv, pieces[count:])):
        at = 0
        for src in mine:
            here = dst.at[top : top + rows, at : at + src.shape[1]]
            copies.append(pltpu.make_async_copy(src, here, sem.at[first + len(copies)]))
            copies[-1].start()
            at += src.shape[1]
    return copies


def begin_input_grad(facts, side, w, own, after=()):
    out_cols, depth = w.shape
    half = depth // 2
    rows = own[0].shape[0]
    count = len(own)

    def body(facts, flag, w_ref, *refs):
        mine, out = jnp.concatenate([r[...] for r in refs[:count]], axis=1), refs[-1]
        where = pl.ds(pl.multiple_of(flag[0] * half, half), half)
        for at in width_tiles(w):
            out[at] = dot_t(w_ref[at, where], mine)

    smem = pl.BlockSpec(memory_space=pltpu.SMEM)
    vmem = pl.BlockSpec(memory_space=pltpu.VMEM)
    near = [pltpu.with_memory_space_constraint(a, pltpu.VMEM) for a in (w, *own)]

    def kernel(*refs):
        body(*refs[: 3 + count], refs[-1])

    return pl.pallas_call(
        kernel,
        out_shape=pltpu.VMEM((out_cols, rows), F32),
        in_specs=[smem, smem] + [vmem] * len(near) + [pl.BlockSpec(memory_space=pl.ANY)] * len(after),
        out_specs=vmem,
        compiler_params=pltpu.CompilerParams(vmem_limit_bytes=LARGE),
        cost_estimate=SLIGHT,
    )(pltpu.with_memory_space_constraint(facts, pltpu.SMEM), side, *near, *after)


def end_input_grad(facts, side, w, far, begun, grads, carry=None, after=()):
    tiles = width_tiles(w)
    out_cols, depth = w.shape
    half = depth // 2
    steps = len(tiles)
    rows = far[0].shape[0]
    top = 0 if rows == PAGE else PAGE
    width = sum(a.shape[1] for a in grads[0])
    near = [w, begun, *far, *grads[0], *grads[1]]
    carry = list(carry or [])

    def body(facts, flag, w_r, begun_r, *refs):
        far_r, grad_r = refs[: len(far)], refs[len(far) : len(near) - 2]
        out, dk, dv, made, stage, sem = refs[-6:]
        made[...] = jnp.zeros_like(made)
        copies = put_rows(grad_r, dk, dv, top, rows, sem, steps)
        other = jnp.concatenate([r[...] for r in far_r], axis=1)
        where = pl.ds(pl.multiple_of((1 - flag[0]) * half, half), half)
        for i, at in enumerate(tiles):
            stage[i] = (dot_t(w_r[at, where], other) + begun_r[at]).astype(BF16).T
            copies.append(
                pltpu.make_async_copy(stage.at[i], out.at[top : top + rows, at], sem.at[i])
            )
            copies[-1].start()
        for c in copies:
            c.wait()

    smem = pl.BlockSpec(memory_space=pltpu.SMEM)
    vmem = pl.BlockSpec(memory_space=pltpu.VMEM)
    hbm = pl.BlockSpec(memory_space=pl.ANY)
    near = [pltpu.with_memory_space_constraint(a, pltpu.VMEM) for a in near]
    kept = jax.ShapeDtypeStruct((ROWS, width), BF16)

    def kernel(*refs):
        body(*refs[: 2 + len(near)], *refs[2 + len(near) + len(carry) + len(after) :])

    return pl.pallas_call(
        kernel,
        out_shape=(
            jax.ShapeDtypeStruct((ROWS, out_cols), BF16), kept, kept, pltpu.VMEM((8, HD), F32)
        ),
        in_specs=[smem, smem] + [vmem] * len(near) + [hbm] * (len(carry) + len(after)),
        out_specs=(hbm, hbm, hbm, vmem),
        scratch_shapes=[
            pltpu.VMEM((steps, rows, out_cols // steps), BF16),
            pltpu.SemaphoreType.DMA((steps + 2 * len(grads[0]),)),
        ],
        input_output_aliases={2 + len(near) + i: i for i in range(len(carry))},
        compiler_params=pltpu.CompilerParams(vmem_limit_bytes=LARGE),
        cost_estimate=SLIGHT,
    )(pltpu.with_memory_space_constraint(facts, pltpu.SMEM), side, *near, *carry, *after)


def flipped(block, axis, bit):
    count = lax.axis_size(axis)
    return lax.ppermute(block, axis, [(i, i ^ bit) for i in range(count) if i ^ bit < count])


def spanning(leaves, bit_index):
    return len([j for j in range(INNER) if 2 << bit_index <= leaves >> j])


def gather_small_tree(facts, own, beside_pair, beside_half):
    two = (own.shape, BF16, True)
    page = (own.shape[1:], BF16, True)
    from_core = flipped(own, "sub", 1)

    def choose_chip(facts, own_ref, far_ref, out):
        for kind in range(2):
            for mine in range(2):

                @pl.when((facts[LEADS] != kind) & (facts[OWNS2] != mine))
                def _copy(kind=kind, mine=mine):
                    out[...] = (own_ref if mine else far_ref)[kind]

    (chip,) = kernel_call(choose_chip, facts, [own, from_core], [], [page])
    from_pair = flipped(chip, "leaf", 1)

    def choose_pair(facts, near_ref, far_ref, out):
        out[...] = jnp.where(facts[ROOT_IN_CHIP] == 1, near_ref[...], far_ref[...])

    after = beside_pair(from_core, chip)
    (pair,) = kernel_call(choose_pair, facts, [chip, from_pair], [], [page], after=after)
    from_half = flipped(pair, "leaf", 2)

    def choose_all(facts, chip_ref, pair_far, pair_ref, half_far, out):
        out[0] = jnp.where(facts[ROOT_IN_PAIR] == 1, pair_ref[...], half_far[...])
        out[1] = jnp.where(facts[NEXT_IN_CHIP] == 1, chip_ref[...], pair_far[...])

    after = beside_half(pair)
    (mine,) = kernel_call(
        choose_all, facts, [chip, from_pair, pair, from_half], [], [two], after=after
    )
    return mine, flipped(mine, "sub", 1)


def over_cores(facts, kept, sent):
    width = kept.shape[-1]

    def body(_, near, away, total, root, next_one):
        for j, low in enumerate((root, next_one)):
            value = near[j] + away[j].astype(F32)
            total[j] = value
            low[...] = value.astype(BF16)

    page = ((PAGE, width), BF16, True)
    total, root, next_one = kernel_call(
        body, facts, [kept, flipped(sent, "sub", 1)], [],
        [((2, PAGE, width), F32, True), page, page],
    )
    return total, root, flipped(root, "leaf", 2), flipped(next_one, "leaf", 1)


def over_halves(facts, total, root_far, next_far, after):
    width = total.shape[-1]

    def body(_, near, root_r, next_r, out, low):
        root = near[0] + root_r[...].astype(F32)
        out[0] = root
        low[...] = root.astype(BF16)
        out[1] = near[1] + next_r[...].astype(F32)

    total, low = kernel_call(
        body, facts, [total, root_far, next_far], [],
        [((2, PAGE, width), F32, True), ((PAGE, width), BF16, True)], after=after,
    )
    return total, low, flipped(low, "leaf", 1)


def over_chips(facts, total, far, passenger, after):
    width = total.shape[-1]
    more = passenger.shape[-1]

    def body(facts, near, away, extra, out):
        root = near[0] + away[...].astype(F32)
        out[:, :width] = jnp.where(facts[ROOT_IN_CHIP] == 1, root, near[1]).astype(BF16)
        for kind in range(2):
            out[:, width + kind * more : width + (kind + 1) * more] = extra[kind]

    outs = [((PAGE, width + 2 * more), BF16, True)]
    (mine,) = kernel_call(
        body, facts, [total, far, passenger], [], outs, after=after
    )
    return mine, flipped(mine, "sub", 1)


def finish_small_tree(facts, own0, mine, far, level2_far):
    width = sum(a.shape[-1] for a in own0)

    def body(facts, own_r, own_last, mine_r, far_r, low_r, dk, dv):
        owns2, leads = facts[OWNS2] == 1, facts[LEADS] == 1
        ok = row_ok(facts[N0], PAGE, HD)
        for at in range(0, width, HD):
            c = slice(at, at + HD)
            last = at + HD == width
            near, away = mine_r[:, c], far_r[:, c]
            gained = [jnp.where(leads, near, away), jnp.where(leads, away, near)]
            for kind, out in enumerate((dk, dv)):
                if last:
                    level2 = far_r[:, width + kind * HD : width + (kind + 1) * HD]
                else:
                    level2 = low_r[kind, :, c]
                more = jnp.where(owns2, level2, gained[kind]).astype(F32)
                base = own_last[kind] if last else own_r[kind, :, c]
                out[:, c] = jnp.where(ok, base + more, 0.0).astype(BF16)

    page = ((PAGE, width), BF16, True)
    return kernel_call(
        body, facts, [*own0, mine, far, level2_far], [], [page, page]
    )


def gather_tree(ids, own):
    leaves = lax.axis_size(("leaf", "sub"))
    owned = ids[:INNER] == ids[INNER] - 1
    pages = jnp.where(owned[:, None, None, None], own[None], jnp.zeros((), BF16))
    for bit in range(leaves.bit_length() - 1):
        active = spanning(leaves, bit)
        far = flipped(pages[:active], ("leaf", "sub"), 1 << bit)
        pages = jnp.concatenate([pages[:active] + far, pages[active:]])
    return pages


def reduce_tree(ids, parts):
    leaves = lax.axis_size(("leaf", "sub"))
    for bit in range(leaves.bit_length() - 1):
        active = spanning(leaves, bit)
        far = flipped(parts[:active], ("leaf", "sub"), 1 << bit)
        parts = jnp.concatenate([parts[:active] + far, parts[active:]])
    owned = ids[:INNER] == ids[INNER] - 1
    return jnp.sum(jnp.where(owned[:, None, None, None], parts, 0.0), axis=0)


def on_device(queries, grad_out, keys, values, log_norms, row_deltas, ancestors, counts, w_value):
    kv = keys.shape[1] // HD
    group = queries.shape[1] // keys.shape[1]
    leaves = lax.axis_size(("leaf", "sub"))
    hbm = lambda a: pltpu.with_memory_space_constraint(a, pltpu.HBM)
    side = lax.axis_index("tensor").astype(I32).reshape(1)
    two_sides = lax.axis_size("tensor") == 2
    inputs = [hbm(a) for a in (queries, grad_out, keys, values, log_norms, row_deltas)]
    facts, own = start(hbm(ancestors), hbm(counts), *inputs[2:4])
    state = {}

    def own_pages(kvs, pages, prior=(), after=(), w=None):
        return attend(True, kvs, group, facts, inputs, pages, state, prior, after, w)

    def shared_pages(kvs, pages):
        return attend(False, kvs, group, facts, inputs, pages, state)

    def spread(part):
        if two_sides:
            return flipped(part, "tensor", 1)
        return lax.all_gather(part, "tensor", axis=1, tiled=True)

    kvs = tuple(range(kv))
    w = hbm(w_value)
    if leaves == 8 and lax.axis_size("sub") == 2 and kv >= 3 and two_sides:
        level2, results = [], []

        def beside_pair(from_core, chip):
            level2.extend((own, from_core))
            results.append(own_pages(kvs[:1], level2, after=(chip,)))
            return (results[-1][3],)

        def beside_half(pair):
            results.append(own_pages(kvs[1:-1], level2, results[-1], (pair,)))
            return (results[-1][3],)

        shared = gather_small_tree(facts, own, beside_pair, beside_half)
        most = results[-1]
        far_v = [spread(most[1])]
        level2_far = flipped(most[3], "sub", 1)
        kept, sent = shared_pages(kvs, shared)
        total, root, root_far, next_far = over_cores(facts, kept, sent)
        *last, w_near = own_pages(kvs[-1:], level2, after=(root,), w=w)
        both = list(zip(most, last))
        begun = begin_input_grad(facts, side, w_near, both[1], (far_v[0], level2_far))
        far_v.append(spread(last[1]))
        total, low, far = over_halves(facts, total, root_far, next_far, (begun,))
        *grads, made = end_input_grad(facts, side, w_near, far_v, begun, both[:2], after=(low,))
        mine, far = over_chips(facts, total, far, last[3], (made,))
        dk0, dv0 = finish_small_tree(facts, both[2], mine, far, level2_far)
        far_v = spread(dv0)
        begun = begin_input_grad(facts, side, w_near, [dv0])
        grads = end_input_grad(facts, side, w_near, [far_v], begun, ([dk0], [dv0]), grads)
        return (state["gq"], grads[1], grads[2], grads[0])

    first = lax.axis_index("sub") == 0
    path_ids = ancestors[0]
    pages = gather_tree(path_ids, own)
    dk12, dv12, own0, send2 = own_pages(kvs, (pages[2], pages[2]))
    kept, sent = shared_pages(
        kvs,
        (
            jnp.where(first, pages[:2, 0], pages[:2, 1]),
            jnp.where(first, pages[:2, 1], pages[:2, 0]),
        ),
    )
    sent = sent.astype(F32)
    upper = jnp.stack([jnp.where(first, kept, sent), jnp.where(first, sent, kept)], axis=1)
    low = send2.astype(F32)
    total = reduce_tree(path_ids, jnp.concatenate([upper, low[None]]))
    total += own0 - jnp.where(path_ids[2] == path_ids[INNER] - 1, low, 0.0)
    has = jnp.any(path_ids[:INNER] == path_ids[INNER] - 1)
    ok = (jnp.arange(PAGE) < jnp.where(has, counts[0, 0], 0))[:, None]
    dk0, dv0 = jnp.where(ok, total, 0.0).astype(BF16)
    if two_sides:
        pair = lambda part: ([part], [spread(part)])
    else:
        pair = lambda part: ([spread(part)], [])
    *grads, _ = input_grad(facts, side, w, 2 * PAGE, *pair(dv12), ([dk12], [dv12]))
    grads = input_grad(facts, side, w, PAGE, *pair(dv0), ([dk0], [dv0]), grads)
    return (state["gq"], grads[1], grads[2], grads[0])


def solution(mesh):
    placed = (
        P(("groups", "leaf", "sub"), "tensor"),
        P(("groups", "leaf", "sub"), "tensor"),
        P(("groups", "leaf", "sub"), "tensor"),
        P(("groups", "leaf", "sub"), "tensor"),
        P("tensor", ("groups", "leaf", "sub")),
        P("tensor", ("groups", "leaf", "sub")),
        P(("groups", "leaf", "sub"), None),
        P(("groups", "leaf", "sub"), None),
        P("tensor", None),
    )
    return jax.shard_map(
        on_device,
        mesh=mesh,
        in_specs=placed,
        out_specs=(
            P(("groups", "leaf", "sub"), "tensor"),
            P(("groups", "leaf", "sub"), "tensor"),
            P(("groups", "leaf", "sub"), "tensor"),
            P(("groups", "leaf", "sub"), "tensor"),
        ),
        check_vma=False,
    )
```

```python
import math

import jax
import jax.numpy as jnp
from jax import lax
from jax.experimental import pallas as pl
from jax.experimental.pallas import tpu as pltpu
from jax.sharding import PartitionSpec as P

HD = 128
PAGE = 128
SLOTS = 3
INNER = 3
ROWS = SLOTS * PAGE
LOG2E = math.log2(math.e)
SCALE = 1.0 / math.sqrt(HD)
BF16 = jnp.bfloat16
F32 = jnp.float32
I32 = jnp.int32
LARGE = 10 << 20
SMALL = 4 << 20
SLIGHT = pl.CostEstimate(flops=1000, bytes_accessed=1000, transcendentals=0)
BLOCKED = 1e30


def dot_t(left, right):
    return lax.dot_general(left, right, (((1,), (1,)), ((), ())), preferred_element_type=F32)


def dot_n(left, right):
    return lax.dot_general(left, right, (((1,), (0,)), ((), ())), preferred_element_type=F32)


FACTS = 16
N0, N1, N2, OWNS2, LIMIT, LEADS, ROOT_IN_CHIP, ROOT_IN_PAIR, NEXT_IN_CHIP = range(9)


def write_facts(facts, ids, counts):
    page = [ids[0, j] for j in range(INNER + 1)]
    own = page[INNER] - 1
    leaf = own // SLOTS
    owns = [page[j] == own for j in range(INNER)]
    same = lambda level, shift: ((page[level] // SLOTS) >> shift) == (leaf >> shift)
    number = lambda flag: jnp.where(flag, 1, 0)
    facts[N0] = jnp.where(owns[0] | owns[1] | owns[2], counts[0, 0], 0)
    facts[N1] = counts[0, 1]
    facts[N2] = counts[0, 2]
    facts[OWNS2] = number(owns[2])
    facts[LIMIT] = jnp.where(owns[2], 2 * PAGE, jnp.where(owns[1], PAGE, 0))
    facts[LEADS] = number(lax.rem(leaf, 2) == 0)
    facts[ROOT_IN_CHIP] = number(same(0, 1))
    facts[ROOT_IN_PAIR] = number(same(0, 2))
    facts[NEXT_IN_CHIP] = number(same(1, 1))
    for i in range(NEXT_IN_CHIP + 1, FACTS):
        facts[i] = 0


def row_ok(count, rows, width):
    return lax.broadcasted_iota(I32, (rows, width), 0) < count


def kernel_call(body, facts, near, far, outs, scratch=(), aliases=None, after=(), cost=None,
                limit=SMALL):
    smem = pl.BlockSpec(memory_space=pltpu.SMEM)
    vmem = pl.BlockSpec(memory_space=pltpu.VMEM)
    hbm = pl.BlockSpec(memory_space=pl.ANY)
    near = [pltpu.with_memory_space_constraint(a, pltpu.VMEM) for a in near]
    place = {("near", i): 1 + i for i in range(len(near))}
    place |= {("far", i): 1 + len(near) + i for i in range(len(far))}
    used = 1 + len(near) + len(far)

    def kernel(*refs):
        body(*refs[:used], *refs[used + len(after) :])

    return pl.pallas_call(
        kernel,
        out_shape=tuple(
            pltpu.VMEM(s, d) if inside else jax.ShapeDtypeStruct(s, d) for s, d, inside in outs
        ),
        in_specs=[smem] + [vmem] * len(near) + [hbm] * (len(far) + len(after)),
        out_specs=tuple(vmem if inside else hbm for _, _, inside in outs),
        scratch_shapes=list(scratch),
        input_output_aliases={place[k]: v for k, v in (aliases or {}).items()},
        compiler_params=pltpu.CompilerParams(vmem_limit_bytes=limit),
        cost_estimate=cost or SLIGHT,
    )(pltpu.with_memory_space_constraint(facts, pltpu.SMEM), *near, *far, *after)


def start(ids, counts, keys, values):
    width = keys.shape[1]

    def body(ids_ref, counts_ref, k_ref, v_ref, facts, out, held, ids_s, counts_s, sem):
        copies = [
            pltpu.make_async_copy(src, dst, sem.at[i])
            for i, (src, dst) in enumerate(
                (
                    (ids_ref, ids_s),
                    (counts_ref, counts_s),
                    (k_ref.at[:PAGE], held.at[0]),
                    (v_ref.at[:PAGE], held.at[1]),
                )
            )
        ]
        for c in copies:
            c.start()
        copies[0].wait()
        copies[1].wait()
        write_facts(facts, ids_s, counts_s)
        ok = row_ok(counts_s[0, 0], PAGE, width)
        for i in range(2):
            copies[2 + i].wait()
            out[i] = jnp.where(ok, held[i], jnp.zeros((), BF16))

    smem = pl.BlockSpec(memory_space=pltpu.SMEM)
    hbm = pl.BlockSpec(memory_space=pl.ANY)
    return pl.pallas_call(
        body,
        out_shape=(pltpu.SMEM((FACTS,), I32), pltpu.VMEM((2, PAGE, width), BF16)),
        in_specs=[hbm] * 4,
        out_specs=(smem, pl.BlockSpec(memory_space=pltpu.VMEM)),
        scratch_shapes=[
            pltpu.VMEM((2, PAGE, width), BF16),
            pltpu.SMEM(ids.shape, I32),
            pltpu.SMEM(counts.shape, I32),
            pltpu.SemaphoreType.DMA((4,)),
        ],
        compiler_params=pltpu.CompilerParams(vmem_limit_bytes=SMALL),
    )(ids, counts, keys, values)


def row_terms(rows):
    high = rows.astype(BF16).astype(F32)
    rest = rows - high
    middle = rest.astype(BF16).astype(F32)
    parts = [high, middle, rest - middle]
    spare = HD - 3 * rows.shape[0]
    parts.append(jnp.zeros((spare, rows.shape[1]), F32))
    return jnp.concatenate(parts, axis=0).T.astype(BF16)


class Head:
    def __init__(self, kv, group, q, g, norms, deltas, en, ed):
        self.kv, self.group, self.q, self.g, self.en, self.ed = kv, group, q, g, en, ed
        self.heads = min(4, group)
        self.parts = group // self.heads
        self.tall = self.heads * PAGE
        heads = slice(kv * group, (kv + 1) * group)
        en[...] = row_terms(norms[heads, :])
        ed[...] = row_terms(deltas[heads, :])

    def lanes(self, part, j):
        at = self.kv * self.group * HD + part * (self.heads * HD) + j * HD
        return pl.ds(pl.multiple_of(at, HD), HD)

    def stacked(self, ref, part, slots):
        return jnp.concatenate(
            [
                ref[slot * PAGE : (slot + 1) * PAGE, self.lanes(part, j)]
                for slot in slots
                for j in range(self.heads)
            ],
            axis=0,
        )

    def deep(self, stacked, terms, part, slots):
        column = lax.broadcasted_iota(I32, (1, HD), 1) % self.group
        picks = [
            (column == part * self.heads + j).astype(F32).astype(BF16)
            for j in range(self.heads)
        ]
        extra = [
            terms[slot * PAGE : (slot + 1) * PAGE] * pick for slot in slots for pick in picks
        ]
        return jnp.concatenate([stacked, jnp.concatenate(extra, axis=0)], axis=1)

    def turned_at(self, part, slot, count):
        at = ((self.kv * self.parts + part) * SLOTS + slot) * self.tall
        return pl.ds(pl.multiple_of(at, self.tall), self.tall * count)

    def put_queries(self, part, slot, rows_by_head, dq, add, stage):
        rows = slice(slot * PAGE, (slot + 1) * PAGE)
        for j in range(self.heads):
            value = rows_by_head[j * PAGE : (j + 1) * PAGE]
            if stage is None:
                dq[rows, self.lanes(part, j)] = value
            else:
                if add:
                    value = value + dq[rows, self.lanes(part, j)]
                stage[rows, j * HD : (j + 1) * HD] = (value * SCALE).astype(BF16)


def set_keys(deep, upright, at, page):
    where = slice(at * PAGE, (at + 1) * PAGE)
    deep[:HD, where] = page.T
    if upright is not None:
        upright[where] = page


def weigh(scores, grads, keep):
    p = keep(jnp.exp2(scores * (SCALE * LOG2E)))
    return p.astype(BF16), (p * grads).astype(BF16)


def attend(own, kvs, group, facts, inputs, pages, state, prior=(), after=()):
    loading = "loaded" not in state
    q, g, k, v, norms, deltas = inputs if loading else state["loaded"]
    count = len(kvs)
    parts = group // min(4, group)
    tall = min(4, group) * PAGE
    wide = min(4, group) * HD
    width = count * HD
    base = prior[0].shape[1] if prior else 0
    kv_total = k.shape[1] // HD
    fresh = [kv not in state["done"] for kv in kvs]
    names = ["dq", "qt", "gt"] + ([] if all(fresh) else ["gq"])
    turned = ((HD, kv_total * group * ROWS), BF16, True)
    full = {"dq": (q.shape, F32, True), "qt": turned, "gt": turned, "gq": (q.shape, BF16, False)}

    near, far, aliases, outs = [], [], {}, []
    at_near, at_far = {}, {}

    def add_near(name, array):
        at_near[name] = len(near)
        near.append(array)

    def add_far(name, array):
        at_far[name] = len(far)
        far.append(array)

    for name in names:
        outs.append(full[name])
        if name in state:
            if full[name][2]:
                add_near(name, state[name])
                aliases["near", at_near[name]] = len(outs) - 1
            else:
                add_far(name, state[name])
                aliases["far", at_far[name]] = len(outs) - 1
    at_results = len(outs)
    if own:
        outs += [
            ((2 * PAGE, base + width), BF16, True),
            ((2 * PAGE, base + width), BF16, True),
            ((2, PAGE, base + width), F32, True),
            ((2, PAGE, base + width), BF16, True),
        ]
    else:
        outs += [
            ((2, PAGE, width), F32, True),
            ((2, PAGE, width), BF16, True),
        ]
    at_loaded = len(outs)
    in_names = ["q", "g", "k", "v", "norms", "deltas"]
    in_arrays = [q, g, k, v, norms, deltas]
    for name, array in zip(in_names, in_arrays):
        if loading:
            add_far(name, array)
            outs.append((array.shape, array.dtype, True))
        else:
            add_near(name, array)
    at_end = len(outs)
    for i, page in enumerate(pages):
        add_near(("page", i), page)
    for i, array in enumerate(prior):
        add_near(("prior", i), array)
    key_pages = 4 if own else 2
    scratch = [
        pltpu.VMEM((2 * HD, key_pages * PAGE), BF16),
        pltpu.VMEM((2 * HD, key_pages * PAGE), BF16),
        pltpu.VMEM((key_pages * PAGE, HD), BF16),
        pltpu.VMEM((2, HD, key_pages * PAGE), F32),
        pltpu.VMEM((ROWS, HD), BF16),
        pltpu.VMEM((ROWS, HD), BF16),
        pltpu.VMEM((count * parts, ROWS, wide), BF16),
        pltpu.SemaphoreType.DMA((count * parts,)),
        pltpu.SemaphoreType.DMA((2 * kv_total + 4,)),
    ]
    cols = lambda a, b: slice(a * PAGE, b * PAGE)

    def body(facts, *refs):
        ins, out_refs = refs[: len(near) + len(far)], refs[len(near) + len(far) : -len(scratch)]
        k_deep, v_deep, k_up, acc, en, ed, stage, sem, load_sem = refs[-len(scratch) :]
        near_ref = lambda name: ins[at_near[name]]
        far_ref = lambda name: ins[len(near) + at_far[name]]
        held = dict(zip(names, out_refs))
        results = out_refs[at_results:at_loaded]
        copies = {}
        if loading:
            into = dict(zip(in_names, out_refs[at_loaded:at_end]))

            def load(key, name, columns=None):
                src, dst = far_ref(name), into[name]
                if columns is not None:
                    src, dst = src.at[:, columns], dst.at[:, columns]
                copies[key] = pltpu.make_async_copy(src, dst, load_sem.at[len(copies)])
                copies[key].start()

            for name in in_names[2:]:
                load(name, name)
            for kv in range(kv_total):
                at = slice(kv * group * HD, (kv + 1) * group * HD)
                load(("q", kv), "q", at)
                load(("g", kv), "g", at)
        else:
            into = {name: near_ref(name) for name in in_names}
        q, g, k, v, norms, deltas = (into[name] for name in in_names)

        def arrived(*keys):
            for key in keys:
                if key in copies:
                    copies.pop(key).wait()

        k_deep[HD:] = jnp.full((HD, key_pages * PAGE), -1.0, BF16)
        v_deep[HD:] = jnp.full((HD, key_pages * PAGE), -1.0, BF16)
        for out, i in zip(results, range(len(prior))):
            out[..., :base] = near_ref(("prior", i))[...]
        owns2, leads = facts[OWNS2] == 1, facts[LEADS] == 1
        if loading:
            arrived("norms", "deltas", "k", "v")
            lane = lax.broadcasted_iota(I32, norms.shape, 1)
            limit = jnp.where(
                lane < PAGE, facts[N0], jnp.where(lane < 2 * PAGE, facts[N1], facts[N2])
            )
            norms[...] = jnp.where(lane % PAGE < limit, norms[...] * (1.0 / SCALE), BLOCKED)
        lower = lambda rows: lax.broadcasted_iota(I32, (rows, PAGE), 1) <= (
            lax.broadcasted_iota(I32, (rows, PAGE), 0) % PAGE
        )

        def set_pages(n, kv):
            lane = slice(kv * HD, (kv + 1) * HD)
            first, second = (near_ref(("page", i)) for i in range(2))
            if own:
                zero = jnp.zeros((), BF16)
                for slot, (at, c) in enumerate(((3, N0), (0, N1), (2, N2))):
                    ok = row_ok(facts[c], PAGE, HD)
                    rows = cols(slot, slot + 1)
                    set_keys(k_deep, k_up, at, jnp.where(ok, k[rows, lane], zero))
                    set_keys(v_deep, None, at, jnp.where(ok, v[rows, lane], zero))
                level2 = [jnp.where(owns2, first[i, :, lane], second[i, :, lane]) for i in (0, 1)]
                set_keys(k_deep, k_up, 1, level2[0])
                set_keys(v_deep, None, 1, level2[1])
            else:
                for j in range(2):
                    mine, theirs = first[j, :, lane], second[j, :, lane]
                    set_keys(k_deep, k_up, j, jnp.where(leads, mine, theirs))
                    set_keys(v_deep, None, j, jnp.where(leads, theirs, mine))
            acc[...] = jnp.zeros_like(acc)

        def turned_rows(head, part, is_fresh, qs, gs, order):
            if is_fresh:
                for name, rows in (("qt", qs), ("gt", gs)):
                    for i, slot in enumerate(order):
                        held[name][:, head.turned_at(part, slot, 1)] = rows[
                            i * tall : (i + 1) * tall
                        ].T
            return lambda name, slot, slots: held[name][:, head.turned_at(part, slot, slots)]

        def own_part(head, part, n, stage_ref):
            order = (1, 2, 0)
            qs, gs = head.stacked(q, part, order), head.stacked(g, part, order)
            qd, gd = head.deep(qs, en, part, order), head.deep(gs, ed, part, order)
            turn = turned_rows(head, part, fresh[n], qs, gs, order)
            low = lower(tall)

            def keep_first(p):
                masked = jnp.where(low, p[:tall, :PAGE], 0.0)
                return jnp.concatenate(
                    [jnp.concatenate([masked, p[:tall, PAGE:]], axis=1), p[tall:]], axis=0
                )

            pa, da = weigh(
                dot_n(qd[: 2 * tall], k_deep[:, : 2 * PAGE]),
                dot_n(gd[: 2 * tall], v_deep[:, : 2 * PAGE]),
                keep_first,
            )
            both = lambda x: jnp.concatenate([x[:tall, :PAGE], x[tall:, PAGE:]], axis=0)
            low2 = lower(2 * tall)
            pb, db = weigh(
                both(dot_n(qd[tall:], k_deep[:, 2 * PAGE :])),
                both(dot_n(gd[tall:], v_deep[:, 2 * PAGE :])),
                lambda p: jnp.where(low2, p, 0.0),
            )
            for i, (name, a, b) in enumerate((("qt", da, db), ("gt", pa, pb))):
                acc[i, :, : 2 * PAGE] += dot_n(turn(name, 1, 2), a)
                acc[i, :, cols(2, 3)] += dot_n(turn(name, 2, 1), b[:tall])
                acc[i, :, cols(3, 4)] += dot_n(turn(name, 0, 1), b[tall:])
            first = dot_n(da, k_up[: 2 * PAGE])
            put = lambda slot, rows: head.put_queries(
                part, slot, rows, held["dq"], not fresh[n], stage_ref
            )
            put(1, first[:tall])
            put(2, first[tall:] + dot_n(db[:tall], k_up[cols(2, 3)]))
            put(0, dot_n(db[tall:], k_up[cols(3, 4)]))

        def shared_part(head, part, n, stage_ref):
            order = (0, 1, 2)
            qs, gs = head.stacked(q, part, order), head.stacked(g, part, order)
            qd, gd = head.deep(qs, en, part, order), head.deep(gs, ed, part, order)
            turn = turned_rows(head, part, fresh[n], qs, gs, order)
            column = lax.broadcasted_iota(I32, (tall, 2 * PAGE), 1)
            seen = column < facts[LIMIT]

            def keep(p):
                return jnp.concatenate([jnp.where(seen, p[:tall], 0.0), p[tall:]], axis=0)

            p, ds = weigh(dot_n(qd, k_deep[...]), dot_n(gd, v_deep[...]), keep)
            acc[0] += dot_n(turn("qt", 0, SLOTS), ds)
            acc[1] += dot_n(turn("gt", 0, SLOTS), p)
            dq = dot_n(ds, k_up[...])
            for slot in range(SLOTS):
                head.put_queries(
                    part, slot, dq[slot * tall : (slot + 1) * tall], held["dq"], not fresh[n],
                    stage_ref,
                )

        def put_own(n):
            dk12, dv12, own0, send2 = results
            here = slice(base + n * HD, base + (n + 1) * HD)
            grad = [acc[0].T * SCALE, acc[1].T]
            for at, c, to in ((0, N1, 0), (2, N2, 1)):
                ok = row_ok(facts[c], PAGE, HD)
                for kind, out in ((0, dk12), (1, dv12)):
                    out[cols(to, to + 1), here] = jnp.where(
                        ok, grad[kind][cols(at, at + 1)], 0.0
                    ).astype(BF16)
            for kind in range(2):
                level2 = grad[kind][cols(1, 2)]
                own0[kind, :, here] = grad[kind][cols(3, 4)] + jnp.where(owns2, level2, 0.0)
                send2[kind, :, here] = level2.astype(BF16)

        def put_shared(n):
            kept, sent = results
            here = slice(n * HD, (n + 1) * HD)
            grad_k, grad_v = acc[0].T * SCALE, acc[1].T
            for j in range(2):
                a, b = grad_k[cols(j, j + 1)], grad_v[cols(j, j + 1)]
                kept[j, :, here] = jnp.where(leads, a, b)
                sent[j, :, here] = jnp.where(leads, b, a).astype(BF16)

        sends = []
        for n, kv in enumerate(kvs):
            arrived(("q", kv), ("g", kv))
            head = Head(kv, group, q, g, norms, deltas, en, ed)
            set_pages(n, kv)

            def step(part, _, n=n, kv=kv, head=head):
                slot = n * parts + part
                (own_part if own else shared_part)(
                    head, part, n, None if fresh[n] else stage.at[slot]
                )
                if not fresh[n]:
                    at = pl.multiple_of((kv * parts + part) * wide, wide)
                    pltpu.make_async_copy(
                        stage.at[slot], held["gq"].at[:, pl.ds(at, wide)], sem.at[slot]
                    ).start()
                return 0

            for part in range(parts):
                step(part, 0)
            (put_own if own else put_shared)(n)
            if not fresh[n]:
                sends += [(n * parts + p, (kv * parts + p) * wide) for p in range(parts)]
        for slot, at in sends:
            pltpu.make_async_copy(
                stage.at[slot], held["gq"].at[:, at : at + wide], sem.at[slot]
            ).wait()
        arrived(*list(copies))

    made = kernel_call(
        body, facts, near, far, outs, scratch, aliases, after,
        pl.CostEstimate(
            flops=240 * PAGE * PAGE * HD * group * count, bytes_accessed=1000, transcendentals=0
        ),
        LARGE,
    )
    for name, array in zip(names, made):
        state[name] = array
    state["done"] = state["done"] | set(kvs)
    if loading:
        state["loaded"] = made[at_loaded:at_end]
    return list(made[at_results:at_loaded])


def width_tiles(w):
    tile = next(t for t in (512, 640, 320, 128, w.shape[0]) if w.shape[0] % t == 0)
    return [slice(i, i + tile) for i in range(0, w.shape[0], tile)]


def input_grad(facts, side, w, rows, own, far, grads, carry=None):
    out_cols, depth = w.shape
    tiles = width_tiles(w)
    top = 0 if rows == PAGE else PAGE
    steps = len(tiles)
    width = sum(a.shape[1] for a in grads[0])
    arrays = [*own, *far, *grads[0], *grads[1]]
    count = len(grads[0])
    carry = list(carry or [])

    def body(facts, flag, *refs):
        own_r, refs = refs[: len(own)], refs[len(own) :]
        far_r, refs = refs[: len(far)], refs[len(far) :]
        grad_r, w_ref = refs[: 2 * count], refs[2 * count]
        out, dk, dv, made, w_near, stage, w_sem, sem = refs[-8:]
        loads = [
            pltpu.make_async_copy(w_ref.at[at], w_near.at[at], w_sem.at[i])
            for i, at in enumerate(tiles)
        ]
        for c in loads:
            c.start()
        made[...] = jnp.zeros_like(made)
        columns = lambda rs: jnp.concatenate([r[...] for r in rs], axis=1)
        full = columns(own_r)
        if far:
            other, leads = columns(far_r), flag[0] == 0
            full = jnp.concatenate(
                [jnp.where(leads, full, other), jnp.where(leads, other, full)], axis=1
            )
        copies = put_rows(grad_r, dk, dv, top, rows, sem, steps)
        for i, at in enumerate(tiles):
            loads[i].wait()
            stage[i] = dot_t(w_near[at], full).astype(BF16).T
            copies.append(
                pltpu.make_async_copy(stage.at[i], out.at[top : top + rows, at], sem.at[i])
            )
            copies[-1].start()
        for c in copies:
            c.wait()

    smem = pl.BlockSpec(memory_space=pltpu.SMEM)
    vmem = pl.BlockSpec(memory_space=pltpu.VMEM)
    hbm = pl.BlockSpec(memory_space=pl.ANY)
    arrays = [pltpu.with_memory_space_constraint(a, pltpu.VMEM) for a in arrays]
    kept = jax.ShapeDtypeStruct((ROWS, width), BF16)
    return pl.pallas_call(
        body,
        out_shape=(
            jax.ShapeDtypeStruct((ROWS, out_cols), BF16), kept, kept, pltpu.VMEM((8, HD), F32)
        ),
        in_specs=[smem] * 2 + [vmem] * len(arrays) + [hbm] * (1 + len(carry)),
        out_specs=(hbm, hbm, hbm, vmem),
        scratch_shapes=[
            pltpu.VMEM(w.shape, BF16),
            pltpu.VMEM((steps, rows, out_cols // steps), BF16),
            pltpu.SemaphoreType.DMA((steps,)),
            pltpu.SemaphoreType.DMA((steps + 2 * count,)),
        ],
        input_output_aliases={3 + len(arrays) + i: i for i in range(len(carry))},
        compiler_params=pltpu.CompilerParams(vmem_limit_bytes=LARGE),
        cost_estimate=SLIGHT,
    )(pltpu.with_memory_space_constraint(facts, pltpu.SMEM), side, *arrays, w, *carry)


def put_rows(pieces, dk, dv, top, rows, sem, first):
    copies = []
    count = len(pieces) // 2
    for dst, mine in ((dk, pieces[:count]), (dv, pieces[count:])):
        at = 0
        for src in mine:
            here = dst.at[top : top + rows, at : at + src.shape[1]]
            copies.append(pltpu.make_async_copy(src, here, sem.at[first + len(copies)]))
            copies[-1].start()
            at += src.shape[1]
    return copies


def side_call(body, facts, side, near, far, outs, scratch, aliases=None, after=()):
    smem = pl.BlockSpec(memory_space=pltpu.SMEM)
    vmem = pl.BlockSpec(memory_space=pltpu.VMEM)
    hbm = pl.BlockSpec(memory_space=pl.ANY)
    near = [pltpu.with_memory_space_constraint(a, pltpu.VMEM) for a in near]
    used = 2 + len(near) + len(far)

    def kernel(*refs):
        body(*refs[:used], *refs[used + len(after) :])

    return pl.pallas_call(
        kernel,
        out_shape=tuple(
            pltpu.VMEM(s, d) if inside else jax.ShapeDtypeStruct(s, d) for s, d, inside in outs
        ),
        in_specs=[smem] * 2 + [vmem] * len(near) + [hbm] * (len(far) + len(after)),
        out_specs=tuple(vmem if inside else hbm for _, _, inside in outs),
        scratch_shapes=list(scratch),
        input_output_aliases={2 + len(near) + i: o for i, o in (aliases or {}).items()},
        compiler_params=pltpu.CompilerParams(vmem_limit_bytes=LARGE),
        cost_estimate=SLIGHT,
    )(pltpu.with_memory_space_constraint(facts, pltpu.SMEM), side, *near, *far, *after)


def half_columns(w, which):
    half = w.shape[1] // 2
    return pl.ds(pl.multiple_of(which * half, half), half)


class Pieces:
    def __init__(self, w_ref, which, into, sem, tiles):
        self.copies = [
            pltpu.make_async_copy(
                w_ref.at[at, half_columns(w_ref, which)], into.at[at], sem.at[i]
            )
            for i, at in enumerate(tiles)
        ]
        for c in self.copies[:2]:
            c.start()

    def wait(self, i):
        self.copies[i].wait()
        if i + 2 < len(self.copies):
            self.copies[i + 2].start()


def begin_input_grad(facts, side, w, own, rest, after=()):
    out_cols, depth = w.shape
    tiles = width_tiles(w)
    count = len(own)
    half = ((out_cols, depth // 2), BF16, True)

    def body(facts, flag, *refs):
        out, w_near, sem = refs[count + 1], refs[-2], refs[-1]
        pieces = Pieces(refs[count], flag[0], w_near, sem, tiles)
        mine = jnp.concatenate([r[...] for r in refs[:count]], axis=1)
        for i, at in enumerate(tiles):
            pieces.wait(i)
            if rest and i + 3 == len(tiles):
                other = pltpu.make_async_copy(
                    refs[count].at[:, half_columns(refs[count], 1 - flag[0])], refs[count + 2],
                    sem.at[len(tiles)],
                )
                other.start()
            out[at] = dot_t(w_near[at], mine)
        if rest:
            other.wait()

    return side_call(
        body, facts, side, own, [w],
        [((out_cols, own[0].shape[0]), F32, True)] + [half] * rest,
        [pltpu.VMEM(half[0], BF16), pltpu.SemaphoreType.DMA((len(tiles) + 1,))], after=after,
    )


def end_input_grad(facts, side, w, far, begun, grads, carry=(), after=()):
    tiles = width_tiles(w)
    out_cols = w.shape[0]
    steps = len(tiles)
    rows = far[0].shape[0]
    top = 0 if carry else PAGE
    width = sum(a.shape[1] for a in grads[0])
    near = [begun, *far, *grads[0], *grads[1]] + ([w] if carry else [])
    count = len(far)
    half = (out_cols, width)

    def body(facts, flag, begun_r, *refs):
        far_r, grad_r = refs[:count], refs[count : count + 2 * len(grads[0])]
        w_ref = refs[count + 2 * len(grads[0])]
        out, dk, dv, made, stage, w_far, w_sem, sem = refs[-8:]
        pieces = None if carry else Pieces(w_ref, 1 - flag[0], w_far, w_sem, tiles)
        made[...] = jnp.zeros_like(made)
        copies = put_rows(grad_r, dk, dv, top, rows, sem, steps)
        other = jnp.concatenate([r[...] for r in far_r], axis=1)
        for i, at in enumerate(tiles):
            if pieces:
                pieces.wait(i)
            product = dot_t((w_far if pieces else w_ref)[at], other)
            stage[i] = (product + begun_r[at]).astype(BF16).T
            copies.append(
                pltpu.make_async_copy(stage.at[i], out.at[top : top + rows, at], sem.at[i])
            )
            copies[-1].start()
        for c in copies:
            c.wait()

    full = ((ROWS, width), BF16, False)
    return side_call(
        body, facts, side, near, list(carry) if carry else [w],
        [((ROWS, out_cols), BF16, False), full, full, ((8, HD), F32, True)],
        [
            pltpu.VMEM((steps, rows, out_cols // steps), BF16),
            pltpu.VMEM((8, HD) if carry else half, BF16),
            pltpu.SemaphoreType.DMA((steps,)),
            pltpu.SemaphoreType.DMA((steps + 2 * len(grads[0]),)),
        ],
        {i: i for i in range(len(carry))}, after,
    )


def flipped(block, axis, bit):
    count = lax.axis_size(axis)
    return lax.ppermute(block, axis, [(i, i ^ bit) for i in range(count) if i ^ bit < count])


def spanning(leaves, bit_index):
    return len([j for j in range(INNER) if 2 << bit_index <= leaves >> j])


def gather_small_tree(facts, own, beside_pair, beside_half):
    two = (own.shape, BF16, True)
    page = (own.shape[1:], BF16, True)
    from_core = flipped(own, "sub", 1)

    def choose_chip(facts, own_ref, far_ref, out):
        for kind in range(2):
            for mine in range(2):

                @pl.when((facts[LEADS] != kind) & (facts[OWNS2] != mine))
                def _copy(kind=kind, mine=mine):
                    out[...] = (own_ref if mine else far_ref)[kind]

    (chip,) = kernel_call(choose_chip, facts, [own, from_core], [], [page])
    from_pair = flipped(chip, "leaf", 1)

    def choose_pair(facts, near_ref, far_ref, out):
        out[...] = jnp.where(facts[ROOT_IN_CHIP] == 1, near_ref[...], far_ref[...])

    after = beside_pair(from_core, chip)
    (pair,) = kernel_call(choose_pair, facts, [chip, from_pair], [], [page], after=after)
    from_half = flipped(pair, "leaf", 2)

    def choose_all(facts, chip_ref, pair_far, pair_ref, half_far, out):
        out[0] = jnp.where(facts[ROOT_IN_PAIR] == 1, pair_ref[...], half_far[...])
        out[1] = jnp.where(facts[NEXT_IN_CHIP] == 1, chip_ref[...], pair_far[...])

    after = beside_half(pair)
    (mine,) = kernel_call(
        choose_all, facts, [chip, from_pair, pair, from_half], [], [two], after=after
    )
    return mine, flipped(mine, "sub", 1)


def over_cores(facts, kept, sent):
    width = kept.shape[-1]

    def body(_, near, away, total, root, next_one):
        for j, low in enumerate((root, next_one)):
            value = near[j] + away[j].astype(F32)
            total[j] = value
            low[...] = value.astype(BF16)

    page = ((PAGE, width), BF16, True)
    total, root, next_one = kernel_call(
        body, facts, [kept, flipped(sent, "sub", 1)], [],
        [((2, PAGE, width), F32, True), page, page],
    )
    return total, root, flipped(root, "leaf", 2), flipped(next_one, "leaf", 1)


def over_halves(facts, total, root_far, next_far, after):
    width = total.shape[-1]

    def body(_, near, root_r, next_r, out, low):
        root = near[0] + root_r[...].astype(F32)
        out[0] = root
        low[...] = root.astype(BF16)
        out[1] = near[1] + next_r[...].astype(F32)

    total, low = kernel_call(
        body, facts, [total, root_far, next_far], [],
        [((2, PAGE, width), F32, True), ((PAGE, width), BF16, True)], after=after,
    )
    return total, low, flipped(low, "leaf", 1)


def over_chips(facts, total, far, passenger, after=()):
    width = total.shape[-1]
    more = passenger.shape[-1]

    def body(facts, near, away, extra, out):
        root = near[0] + away[...].astype(F32)
        out[:, :width] = jnp.where(facts[ROOT_IN_CHIP] == 1, root, near[1]).astype(BF16)
        for kind in range(2):
            out[:, width + kind * more : width + (kind + 1) * more] = extra[kind]

    outs = [((PAGE, width + 2 * more), BF16, True)]
    (mine,) = kernel_call(body, facts, [total, far, passenger], [], outs, after=after)
    return mine, flipped(mine, "sub", 1)


def finish_small_tree(facts, own0, mine, far, level2_far):
    width = sum(a.shape[-1] for a in own0)

    def body(facts, own_r, own_last, mine_r, far_r, low_r, dk, dv):
        owns2, leads = facts[OWNS2] == 1, facts[LEADS] == 1
        ok = row_ok(facts[N0], PAGE, HD)
        for at in range(0, width, HD):
            c = slice(at, at + HD)
            last = at + HD == width
            near, away = mine_r[:, c], far_r[:, c]
            gained = [jnp.where(leads, near, away), jnp.where(leads, away, near)]
            for kind, out in enumerate((dk, dv)):
                if last:
                    level2 = far_r[:, width + kind * HD : width + (kind + 1) * HD]
                else:
                    level2 = low_r[kind, :, c]
                more = jnp.where(owns2, level2, gained[kind]).astype(F32)
                base = own_last[kind] if last else own_r[kind, :, c]
                out[:, c] = jnp.where(ok, base + more, 0.0).astype(BF16)

    page = ((PAGE, width), BF16, True)
    return kernel_call(body, facts, [*own0, mine, far, level2_far], [], [page, page])


def gather_tree(ids, own):
    leaves = lax.axis_size(("leaf", "sub"))
    owned = ids[:INNER] == ids[INNER] - 1
    pages = jnp.where(owned[:, None, None, None], own[None], jnp.zeros((), BF16))
    for bit in range(leaves.bit_length() - 1):
        active = spanning(leaves, bit)
        far = flipped(pages[:active], ("leaf", "sub"), 1 << bit)
        pages = jnp.concatenate([pages[:active] + far, pages[active:]])
    return pages


def reduce_tree(ids, parts):
    leaves = lax.axis_size(("leaf", "sub"))
    for bit in range(leaves.bit_length() - 1):
        active = spanning(leaves, bit)
        far = flipped(parts[:active], ("leaf", "sub"), 1 << bit)
        parts = jnp.concatenate([parts[:active] + far, parts[active:]])
    owned = ids[:INNER] == ids[INNER] - 1
    return jnp.sum(jnp.where(owned[:, None, None, None], parts, 0.0), axis=0)


def on_device(queries, grad_out, keys, values, log_norms, row_deltas, ancestors, counts, w_value):
    kv = keys.shape[1] // HD
    group = queries.shape[1] // keys.shape[1]
    leaves = lax.axis_size(("leaf", "sub"))
    hbm = lambda a: pltpu.with_memory_space_constraint(a, pltpu.HBM)
    side = lax.axis_index("tensor").astype(I32).reshape(1)
    two_sides = lax.axis_size("tensor") == 2
    inputs = [hbm(a) for a in (queries, grad_out, keys, values, log_norms, row_deltas)]
    facts, own = start(hbm(ancestors), hbm(counts), *inputs[2:4])
    state = {"done": frozenset()}

    def own_pages(kvs, pages, prior=(), after=()):
        return attend(True, kvs, group, facts, inputs, pages, state, prior, after)

    def shared_pages(kvs, pages, after=()):
        return attend(False, kvs, group, facts, inputs, pages, state, after=after)

    def spread(part):
        if two_sides:
            return flipped(part, "tensor", 1)
        return lax.all_gather(part, "tensor", axis=1, tiled=True)

    kvs = tuple(range(kv))
    w = hbm(w_value)
    if leaves == 8 and lax.axis_size("sub") == 2 and kv >= 3 and two_sides:
        level2, results = [], []

        def beside_pair(from_core, chip):
            level2.extend((own, from_core))
            results.append(own_pages(kvs[:1], level2, after=(chip,)))
            return (results[-1][3],)

        def beside_half(pair):
            results.append(own_pages(kvs[1:-1], level2, results[-1], (pair,)))
            return (results[-1][3],)

        shared = gather_small_tree(facts, own, beside_pair, beside_half)
        most = results[-1]
        far_v = [spread(most[1])]
        level2_far = flipped(most[3], "sub", 1)
        kept, sent = shared_pages(kvs, shared)
        total, root, root_far, next_far = over_cores(facts, kept, sent)
        last = own_pages(kvs[-1:], level2, after=(root,))
        both = list(zip(most, last))
        begun, = begin_input_grad(facts, side, w, both[1], False, (far_v[0], level2_far))
        far_v.append(spread(last[1]))
        total, low, far = over_halves(facts, total, root_far, next_far, (begun,))
        *grads, made = end_input_grad(facts, side, w, far_v, begun, both[:2], after=(low,))
        mine, far = over_chips(facts, total, far, last[3], (made,))
        dk0, dv0 = finish_small_tree(facts, both[2], mine, far, level2_far)
        far_v = spread(dv0)
        begun, w_far = begin_input_grad(facts, side, w, [dv0], True)
        grads = end_input_grad(facts, side, w_far, [far_v], begun, ([dk0], [dv0]), grads)
        return (state["gq"], grads[1], grads[2], grads[0])

    first = lax.axis_index("sub") == 0
    path_ids = ancestors[0]
    pages = gather_tree(path_ids, own)
    dk12, dv12, own0, send2 = own_pages(kvs, (pages[2], pages[2]))
    kept, sent = shared_pages(
        kvs,
        (
            jnp.where(first, pages[:2, 0], pages[:2, 1]),
            jnp.where(first, pages[:2, 1], pages[:2, 0]),
        ),
    )
    sent = sent.astype(F32)
    upper = jnp.stack([jnp.where(first, kept, sent), jnp.where(first, sent, kept)], axis=1)
    low = send2.astype(F32)
    total = reduce_tree(path_ids, jnp.concatenate([upper, low[None]]))
    total += own0 - jnp.where(path_ids[2] == path_ids[INNER] - 1, low, 0.0)
    has = jnp.any(path_ids[:INNER] == path_ids[INNER] - 1)
    ok = (jnp.arange(PAGE) < jnp.where(has, counts[0, 0], 0))[:, None]
    dk0, dv0 = jnp.where(ok, total, 0.0).astype(BF16)
    if two_sides:
        pair = lambda part: ([part], [spread(part)])
    else:
        pair = lambda part: ([spread(part)], [])
    *grads, _ = input_grad(facts, side, w, 2 * PAGE, *pair(dv12), ([dk12], [dv12]))
    grads = input_grad(facts, side, w, PAGE, *pair(dv0), ([dk0], [dv0]), grads)
    return (state["gq"], grads[1], grads[2], grads[0])


def solution(mesh):
    placed = (
        P(("groups", "leaf", "sub"), "tensor"),
        P(("groups", "leaf", "sub"), "tensor"),
        P(("groups", "leaf", "sub"), "tensor"),
        P(("groups", "leaf", "sub"), "tensor"),
        P("tensor", ("groups", "leaf", "sub")),
        P("tensor", ("groups", "leaf", "sub")),
        P(("groups", "leaf", "sub"), None),
        P(("groups", "leaf", "sub"), None),
        P("tensor", None),
    )
    return jax.shard_map(
        on_device,
        mesh=mesh,
        in_specs=placed,
        out_specs=(
            P(("groups", "leaf", "sub"), "tensor"),
            P(("groups", "leaf", "sub"), "tensor"),
            P(("groups", "leaf", "sub"), "tensor"),
            P(("groups", "leaf", "sub"), "tensor"),
        ),
        check_vma=False,
    )
```

```python
import math

import jax
import jax.numpy as jnp
from jax import lax
from jax.experimental import pallas as pl
from jax.experimental.pallas import tpu as pltpu
from jax.sharding import PartitionSpec as P

HD = 128
PAGE = 128
SLOTS = 3
INNER = 3
ROWS = SLOTS * PAGE
LOG2E = math.log2(math.e)
SCALE = 1.0 / math.sqrt(HD)
BF16 = jnp.bfloat16
F32 = jnp.float32
I32 = jnp.int32
LARGE = 10 << 20
SMALL = 4 << 20
SLIGHT = pl.CostEstimate(flops=1000, bytes_accessed=1000, transcendentals=0)
BLOCKED = 1e30


def dot_t(left, right):
    return lax.dot_general(left, right, (((1,), (1,)), ((), ())), preferred_element_type=F32)


def dot_n(left, right):
    return lax.dot_general(left, right, (((1,), (0,)), ((), ())), preferred_element_type=F32)


FACTS = 16
N0, N1, N2, OWNS2, LIMIT, LEADS, ROOT_IN_CHIP, ROOT_IN_PAIR, NEXT_IN_CHIP, SIDE = range(10)


def write_facts(facts, ids, counts, side):
    page = [ids[0, j] for j in range(INNER + 1)]
    own = page[INNER] - 1
    leaf = own // SLOTS
    owns = [page[j] == own for j in range(INNER)]
    same = lambda level, shift: ((page[level] // SLOTS) >> shift) == (leaf >> shift)
    number = lambda flag: jnp.where(flag, 1, 0)
    facts[N0] = jnp.where(owns[0] | owns[1] | owns[2], counts[0, 0], 0)
    facts[N1] = counts[0, 1]
    facts[N2] = counts[0, 2]
    facts[OWNS2] = number(owns[2])
    facts[LIMIT] = jnp.where(owns[2], 2 * PAGE, jnp.where(owns[1], PAGE, 0))
    facts[LEADS] = number(lax.rem(leaf, 2) == 0)
    facts[ROOT_IN_CHIP] = number(same(0, 1))
    facts[ROOT_IN_PAIR] = number(same(0, 2))
    facts[NEXT_IN_CHIP] = number(same(1, 1))
    facts[SIDE] = side
    for i in range(SIDE + 1, FACTS):
        facts[i] = 0


def row_ok(count, rows, width):
    return lax.broadcasted_iota(I32, (rows, width), 0) < count


def kernel_call(body, facts, near, far, outs, scratch=(), aliases=None, after=(), cost=None,
                limit=SMALL):
    smem = pl.BlockSpec(memory_space=pltpu.SMEM)
    vmem = pl.BlockSpec(memory_space=pltpu.VMEM)
    hbm = pl.BlockSpec(memory_space=pl.ANY)
    near = [pltpu.with_memory_space_constraint(a, pltpu.VMEM) for a in near]
    place = {("near", i): 1 + i for i in range(len(near))}
    place |= {("far", i): 1 + len(near) + i for i in range(len(far))}
    used = 1 + len(near) + len(far)

    def kernel(*refs):
        body(*refs[:used], *refs[used + len(after) :])

    return pl.pallas_call(
        kernel,
        out_shape=tuple(
            pltpu.VMEM(s, d) if inside else jax.ShapeDtypeStruct(s, d) for s, d, inside in outs
        ),
        in_specs=[smem] + [vmem] * len(near) + [hbm] * (len(far) + len(after)),
        out_specs=tuple(vmem if inside else hbm for _, _, inside in outs),
        scratch_shapes=list(scratch),
        input_output_aliases={place[k]: v for k, v in (aliases or {}).items()},
        compiler_params=pltpu.CompilerParams(vmem_limit_bytes=limit),
        cost_estimate=cost or SLIGHT,
    )(pltpu.with_memory_space_constraint(facts, pltpu.SMEM), *near, *far, *after)


def start(side, ids, counts, keys, values):
    width = keys.shape[1]

    def body(side_ref, ids_ref, counts_ref, k_ref, v_ref, facts, out, held, ids_s, counts_s, sem):
        copies = [
            pltpu.make_async_copy(src, dst, sem.at[i])
            for i, (src, dst) in enumerate(
                (
                    (ids_ref, ids_s),
                    (counts_ref, counts_s),
                    (k_ref.at[:PAGE], held.at[0]),
                    (v_ref.at[:PAGE], held.at[1]),
                )
            )
        ]
        for c in copies:
            c.start()
        copies[0].wait()
        copies[1].wait()
        write_facts(facts, ids_s, counts_s, side_ref[0])
        ok = row_ok(counts_s[0, 0], PAGE, width)
        for i in range(2):
            copies[2 + i].wait()
            out[i] = jnp.where(ok, held[i], jnp.zeros((), BF16))

    smem = pl.BlockSpec(memory_space=pltpu.SMEM)
    hbm = pl.BlockSpec(memory_space=pl.ANY)
    return pl.pallas_call(
        body,
        out_shape=(pltpu.SMEM((FACTS,), I32), pltpu.VMEM((2, PAGE, width), BF16)),
        in_specs=[smem] + [hbm] * 4,
        out_specs=(smem, pl.BlockSpec(memory_space=pltpu.VMEM)),
        scratch_shapes=[
            pltpu.VMEM((2, PAGE, width), BF16),
            pltpu.SMEM(ids.shape, I32),
            pltpu.SMEM(counts.shape, I32),
            pltpu.SemaphoreType.DMA((4,)),
        ],
        compiler_params=pltpu.CompilerParams(vmem_limit_bytes=SMALL),
    )(side, ids, counts, keys, values)


def row_terms(rows):
    high = rows.astype(BF16).astype(F32)
    rest = rows - high
    middle = rest.astype(BF16).astype(F32)
    parts = [high, middle, rest - middle]
    spare = HD - 3 * rows.shape[0]
    parts.append(jnp.zeros((spare, rows.shape[1]), F32))
    return jnp.concatenate(parts, axis=0).T.astype(BF16)


class Head:
    def __init__(self, kv, group, norms, deltas, en, ed):
        self.group = group
        self.heads = min(4, group)
        self.parts = group // self.heads
        self.tall = self.heads * PAGE
        heads = slice(kv * group, (kv + 1) * group)
        en[...] = row_terms(norms[heads, :])
        ed[...] = row_terms(deltas[heads, :])

    def lanes(self, part, j):
        at = (part * self.heads + j) * HD
        return slice(at, at + HD)

    def stacked(self, ref, part, slots):
        return jnp.concatenate(
            [
                ref[slot * PAGE : (slot + 1) * PAGE, self.lanes(part, j)]
                for slot in slots
                for j in range(self.heads)
            ],
            axis=0,
        )

    def deep(self, stacked, terms, part, slots):
        column = lax.broadcasted_iota(I32, (1, HD), 1) % self.group
        picks = [
            (column == part * self.heads + j).astype(F32).astype(BF16)
            for j in range(self.heads)
        ]
        extra = [
            terms[slot * PAGE : (slot + 1) * PAGE] * pick for slot in slots for pick in picks
        ]
        return jnp.concatenate([stacked, jnp.concatenate(extra, axis=0)], axis=1)

    def turned_at(self, part, slot, count):
        at = (part * SLOTS + slot) * self.tall
        return slice(at, at + self.tall * count)

    def put_queries(self, part, slot, rows_by_head, dq, add, stage):
        rows = slice(slot * PAGE, (slot + 1) * PAGE)
        for j in range(self.heads):
            value = rows_by_head[j * PAGE : (j + 1) * PAGE]
            if stage is None:
                dq[rows, self.lanes(part, j)] = value
            else:
                if add:
                    value = value + dq[rows, self.lanes(part, j)]
                stage[rows, j * HD : (j + 1) * HD] = (value * SCALE).astype(BF16)


def set_keys(deep, upright, at, page):
    where = slice(at * PAGE, (at + 1) * PAGE)
    deep[:HD, where] = page.T
    if upright is not None:
        upright[where] = page


def weigh(scores, grads, keep):
    p = keep(jnp.exp2(scores * (SCALE * LOG2E)))
    return p.astype(BF16), (p * grads).astype(BF16)


def attend(own, kvs, group, facts, inputs, pages, state, prior=(), after=(), w=None):
    loading = "k" not in state
    q_all, k_all = inputs[0], inputs[2]
    count = len(kvs)
    parts = group // min(4, group)
    tall = min(4, group) * PAGE
    wide = min(4, group) * HD
    width = count * HD
    base = prior[0].shape[1] if prior else 0
    kv_total = k_all.shape[1] // HD
    fresh = [("dq", kv) not in state for kv in kvs]
    one_head = (ROWS, group * HD)
    turned = ((HD, group * ROWS), BF16, True)
    shapes = {"dq": (one_head, F32, True), "qt": turned, "gt": turned}

    near, far, aliases, outs = [], [], {}, []
    at_near, at_far, at_out = {}, {}, {}

    def add_near(name, array):
        at_near[name] = len(near)
        near.append(array)

    def add_far(name, array):
        at_far[name] = len(far)
        far.append(array)

    def add_out(name, out):
        at_out[name] = len(outs)
        outs.append(out)

    for kv, is_fresh in zip(kvs, fresh):
        for name, shape in shapes.items():
            if is_fresh:
                add_out((name, kv), shape)
            else:
                add_near((name, kv), state[name, kv])
    if not all(fresh):
        add_out("gq", (q_all.shape, BF16, False))
        if "gq" in state:
            add_far("gq", state["gq"])
            aliases["far", at_far["gq"]] = at_out["gq"]
    at_results = len(outs)
    if own:
        outs += [
            ((2 * PAGE, base + width), BF16, True),
            ((2 * PAGE, base + width), BF16, True),
            ((2, PAGE, base + width), F32, True),
            ((2, PAGE, base + width), BF16, True),
        ]
    else:
        outs += [
            ((2, PAGE, width), F32, True),
            ((2, PAGE, width), BF16, True),
        ]
    at_loaded = len(outs)
    if loading:
        for name, array in zip(("q", "g", "k", "v", "norms", "deltas"), inputs):
            add_far(name, array)
            if name in ("q", "g"):
                for kv in range(kv_total):
                    add_out((name, kv), (one_head, BF16, True))
            else:
                add_out(name, (array.shape, array.dtype, True))
    else:
        for name in ("k", "v", "norms", "deltas"):
            add_near(name, state[name])
        for kv in kvs:
            for name in ("q", "g"):
                add_near((name, kv), state[name, kv])
    at_end = len(outs)
    if w is not None:
        add_far("w", w)
        outs.append((w.shape, w.dtype, True))
    for i, page in enumerate(pages):
        add_near(("page", i), page)
    for i, array in enumerate(prior):
        add_near(("prior", i), array)
    key_pages = 4 if own else 2
    scratch = [
        pltpu.VMEM((2 * HD, key_pages * PAGE), BF16),
        pltpu.VMEM((2 * HD, key_pages * PAGE), BF16),
        pltpu.VMEM((key_pages * PAGE, HD), BF16),
        pltpu.VMEM((2, HD, key_pages * PAGE), F32),
        pltpu.VMEM((ROWS, HD), BF16),
        pltpu.VMEM((ROWS, HD), BF16),
        pltpu.VMEM((count * parts, ROWS, wide), BF16),
        pltpu.SemaphoreType.DMA((count * parts,)),
        pltpu.SemaphoreType.DMA((2 * kv_total + 5,)),
    ]
    cols = lambda a, b: slice(a * PAGE, b * PAGE)

    def body(facts, *refs):
        ins, out_refs = refs[: len(near) + len(far)], refs[len(near) + len(far) : -len(scratch)]
        k_deep, v_deep, k_up, acc, en, ed, stage, sem, load_sem = refs[-len(scratch) :]
        near_ref = lambda name: ins[at_near[name]]
        far_ref = lambda name: ins[len(near) + at_far[name]]
        held = lambda name: out_refs[at_out[name]] if name in at_out else near_ref(name)
        results = out_refs[at_results:at_loaded]
        copies = {}
        if loading:

            def load(key, src):
                copies[key] = pltpu.make_async_copy(src, held(key), load_sem.at[len(copies)])
                copies[key].start()

            for name in ("k", "v", "norms", "deltas"):
                load(name, far_ref(name))
            for kv in range(kv_total):
                at = slice(kv * group * HD, (kv + 1) * group * HD)
                for name in ("q", "g"):
                    load((name, kv), far_ref(name).at[:, at])
        if w is not None:
            w_copy = pltpu.make_async_copy(
                far_ref("w"), out_refs[at_end], load_sem.at[2 * kv_total + 4]
            )
            w_copy.start()
        k, v, norms, deltas = (held(name) for name in ("k", "v", "norms", "deltas"))

        def arrived(*keys):
            for key in keys:
                if key in copies:
                    copies.pop(key).wait()

        k_deep[HD:] = jnp.full((HD, key_pages * PAGE), -1.0, BF16)
        v_deep[HD:] = jnp.full((HD, key_pages * PAGE), -1.0, BF16)
        for out, i in zip(results, range(len(prior))):
            out[..., :base] = near_ref(("prior", i))[...]
        owns2, leads = facts[OWNS2] == 1, facts[LEADS] == 1
        if loading:
            arrived("norms", "deltas", "k", "v")
            lane = lax.broadcasted_iota(I32, norms.shape, 1)
            limit = jnp.where(
                lane < PAGE, facts[N0], jnp.where(lane < 2 * PAGE, facts[N1], facts[N2])
            )
            norms[...] = jnp.where(lane % PAGE < limit, norms[...] * (1.0 / SCALE), BLOCKED)
        lower = lambda rows: lax.broadcasted_iota(I32, (rows, PAGE), 1) <= (
            lax.broadcasted_iota(I32, (rows, PAGE), 0) % PAGE
        )

        def set_pages(n, kv):
            lane = slice(kv * HD, (kv + 1) * HD)
            first, second = (near_ref(("page", i)) for i in range(2))
            if own:
                zero = jnp.zeros((), BF16)
                for slot, (at, c) in enumerate(((3, N0), (0, N1), (2, N2))):
                    ok = row_ok(facts[c], PAGE, HD)
                    rows = cols(slot, slot + 1)
                    set_keys(k_deep, k_up, at, jnp.where(ok, k[rows, lane], zero))
                    set_keys(v_deep, None, at, jnp.where(ok, v[rows, lane], zero))
                level2 = [jnp.where(owns2, first[i, :, lane], second[i, :, lane]) for i in (0, 1)]
                set_keys(k_deep, k_up, 1, level2[0])
                set_keys(v_deep, None, 1, level2[1])
            else:
                for j in range(2):
                    mine, theirs = first[j, :, lane], second[j, :, lane]
                    set_keys(k_deep, k_up, j, jnp.where(leads, mine, theirs))
                    set_keys(v_deep, None, j, jnp.where(leads, theirs, mine))
            acc[...] = jnp.zeros_like(acc)

        def turned_rows(head, kv, part, is_fresh, qs, gs, order):
            if is_fresh:
                for name, rows in (("qt", qs), ("gt", gs)):
                    for i, slot in enumerate(order):
                        held((name, kv))[:, head.turned_at(part, slot, 1)] = rows[
                            i * tall : (i + 1) * tall
                        ].T
            return lambda name, slot, slots: held((name, kv))[
                :, head.turned_at(part, slot, slots)
            ]

        def own_part(head, kv, part, n, stage_ref):
            order = (1, 2, 0)
            qs = head.stacked(held(("q", kv)), part, order)
            gs = head.stacked(held(("g", kv)), part, order)
            qd, gd = head.deep(qs, en, part, order), head.deep(gs, ed, part, order)
            turn = turned_rows(head, kv, part, fresh[n], qs, gs, order)
            low = lower(tall)

            def keep_first(p):
                masked = jnp.where(low, p[:tall, :PAGE], 0.0)
                return jnp.concatenate(
                    [jnp.concatenate([masked, p[:tall, PAGE:]], axis=1), p[tall:]], axis=0
                )

            pa, da = weigh(
                dot_n(qd[: 2 * tall], k_deep[:, : 2 * PAGE]),
                dot_n(gd[: 2 * tall], v_deep[:, : 2 * PAGE]),
                keep_first,
            )
            both = lambda x: jnp.concatenate([x[:tall, :PAGE], x[tall:, PAGE:]], axis=0)
            low2 = lower(2 * tall)
            pb, db = weigh(
                both(dot_n(qd[tall:], k_deep[:, 2 * PAGE :])),
                both(dot_n(gd[tall:], v_deep[:, 2 * PAGE :])),
                lambda p: jnp.where(low2, p, 0.0),
            )
            for i, (name, a, b) in enumerate((("qt", da, db), ("gt", pa, pb))):
                acc[i, :, : 2 * PAGE] += dot_n(turn(name, 1, 2), a)
                acc[i, :, cols(2, 3)] += dot_n(turn(name, 2, 1), b[:tall])
                acc[i, :, cols(3, 4)] += dot_n(turn(name, 0, 1), b[tall:])
            first = dot_n(da, k_up[: 2 * PAGE])
            put = lambda slot, rows: head.put_queries(
                part, slot, rows, held(("dq", kv)), not fresh[n], stage_ref
            )
            put(1, first[:tall])
            put(2, first[tall:] + dot_n(db[:tall], k_up[cols(2, 3)]))
            put(0, dot_n(db[tall:], k_up[cols(3, 4)]))

        def shared_part(head, kv, part, n, stage_ref):
            order = (0, 1, 2)
            qs = head.stacked(held(("q", kv)), part, order)
            gs = head.stacked(held(("g", kv)), part, order)
            qd, gd = head.deep(qs, en, part, order), head.deep(gs, ed, part, order)
            turn = turned_rows(head, kv, part, fresh[n], qs, gs, order)
            column = lax.broadcasted_iota(I32, (tall, 2 * PAGE), 1)
            seen = column < facts[LIMIT]

            def keep(p):
                return jnp.concatenate([jnp.where(seen, p[:tall], 0.0), p[tall:]], axis=0)

            p, ds = weigh(dot_n(qd, k_deep[...]), dot_n(gd, v_deep[...]), keep)
            acc[0] += dot_n(turn("qt", 0, SLOTS), ds)
            acc[1] += dot_n(turn("gt", 0, SLOTS), p)
            dq = dot_n(ds, k_up[...])
            for slot in range(SLOTS):
                head.put_queries(
                    part, slot, dq[slot * tall : (slot + 1) * tall], held(("dq", kv)), not fresh[n],
                    stage_ref,
                )

        def put_own(n):
            dk12, dv12, own0, send2 = results
            here = slice(base + n * HD, base + (n + 1) * HD)
            grad = [acc[0].T * SCALE, acc[1].T]
            for at, c, to in ((0, N1, 0), (2, N2, 1)):
                ok = row_ok(facts[c], PAGE, HD)
                for kind, out in ((0, dk12), (1, dv12)):
                    out[cols(to, to + 1), here] = jnp.where(
                        ok, grad[kind][cols(at, at + 1)], 0.0
                    ).astype(BF16)
            for kind in range(2):
                level2 = grad[kind][cols(1, 2)]
                own0[kind, :, here] = grad[kind][cols(3, 4)] + jnp.where(owns2, level2, 0.0)
                send2[kind, :, here] = level2.astype(BF16)

        def put_shared(n):
            kept, sent = results
            here = slice(n * HD, (n + 1) * HD)
            grad_k, grad_v = acc[0].T * SCALE, acc[1].T
            for j in range(2):
                a, b = grad_k[cols(j, j + 1)], grad_v[cols(j, j + 1)]
                kept[j, :, here] = jnp.where(leads, a, b)
                sent[j, :, here] = jnp.where(leads, b, a).astype(BF16)

        sends = []
        for n, kv in enumerate(kvs):
            arrived(("q", kv), ("g", kv))
            head = Head(kv, group, norms, deltas, en, ed)
            set_pages(n, kv)

            for part in range(parts):
                slot = n * parts + part
                (own_part if own else shared_part)(
                    head, kv, part, n, None if fresh[n] else stage.at[slot]
                )
                if not fresh[n]:
                    at = (kv * parts + part) * wide
                    sends.append(
                        pltpu.make_async_copy(
                            stage.at[slot], held("gq").at[:, at : at + wide], sem.at[slot]
                        )
                    )
                    sends[-1].start()

            (put_own if own else put_shared)(n)
        for c in sends:
            c.wait()
        arrived(*list(copies))
        if w is not None:
            w_copy.wait()

    made = kernel_call(
        body, facts, near, far, outs, scratch, aliases, after,
        pl.CostEstimate(
            flops=240 * PAGE * PAGE * HD * group * count, bytes_accessed=1000, transcendentals=0
        ),
        LARGE,
    )
    for name, at in at_out.items():
        state[name] = made[at]
    return list(made[at_results:at_loaded]) + list(made[at_end:])


def width_tiles(w):
    tile = next(t for t in (512, 640, 320, 128, w.shape[0]) if w.shape[0] % t == 0)
    return [slice(i, i + tile) for i in range(0, w.shape[0], tile)]


def input_grad(facts, w, rows, own, far, grads, carry=None):
    out_cols, depth = w.shape
    tiles = width_tiles(w)
    top = 0 if rows == PAGE else PAGE
    steps = len(tiles)
    width = sum(a.shape[1] for a in grads[0])
    arrays = [*own, *far, *grads[0], *grads[1]]
    count = len(grads[0])
    carry = list(carry or [])

    def body(facts, *refs):
        own_r, refs = refs[: len(own)], refs[len(own) :]
        far_r, refs = refs[: len(far)], refs[len(far) :]
        grad_r, w_ref = refs[: 2 * count], refs[2 * count]
        out, dk, dv, made, w_near, stage, w_sem, sem = refs[-8:]
        loads = [
            pltpu.make_async_copy(w_ref.at[at], w_near.at[at], w_sem.at[i])
            for i, at in enumerate(tiles)
        ]
        for c in loads:
            c.start()
        made[...] = jnp.zeros_like(made)
        columns = lambda rs: jnp.concatenate([r[...] for r in rs], axis=1)
        full = columns(own_r)
        if far:
            other, leads = columns(far_r), facts[SIDE] == 0
            full = jnp.concatenate(
                [jnp.where(leads, full, other), jnp.where(leads, other, full)], axis=1
            )
        copies = put_rows(grad_r, dk, dv, top, rows, sem, steps)
        for i, at in enumerate(tiles):
            loads[i].wait()
            stage[i] = dot_t(w_near[at], full).astype(BF16).T
            copies.append(
                pltpu.make_async_copy(stage.at[i], out.at[top : top + rows, at], sem.at[i])
            )
            copies[-1].start()
        for c in copies:
            c.wait()

    smem = pl.BlockSpec(memory_space=pltpu.SMEM)
    vmem = pl.BlockSpec(memory_space=pltpu.VMEM)
    hbm = pl.BlockSpec(memory_space=pl.ANY)
    arrays = [pltpu.with_memory_space_constraint(a, pltpu.VMEM) for a in arrays]
    kept = jax.ShapeDtypeStruct((ROWS, width), BF16)
    return pl.pallas_call(
        body,
        out_shape=(
            jax.ShapeDtypeStruct((ROWS, out_cols), BF16), kept, kept, pltpu.VMEM((8, HD), F32)
        ),
        in_specs=[smem] + [vmem] * len(arrays) + [hbm] * (1 + len(carry)),
        out_specs=(hbm, hbm, hbm, vmem),
        scratch_shapes=[
            pltpu.VMEM(w.shape, BF16),
            pltpu.VMEM((steps, rows, out_cols // steps), BF16),
            pltpu.SemaphoreType.DMA((steps,)),
            pltpu.SemaphoreType.DMA((steps + 2 * count,)),
        ],
        input_output_aliases={2 + len(arrays) + i: i for i in range(len(carry))},
        compiler_params=pltpu.CompilerParams(vmem_limit_bytes=LARGE),
        cost_estimate=SLIGHT,
    )(pltpu.with_memory_space_constraint(facts, pltpu.SMEM), *arrays, w, *carry)


def put_rows(pieces, dk, dv, top, rows, sem, first):
    copies = []
    count = len(pieces) // 2
    for dst, mine in ((dk, pieces[:count]), (dv, pieces[count:])):
        at = 0
        for src in mine:
            here = dst.at[top : top + rows, at : at + src.shape[1]]
            copies.append(pltpu.make_async_copy(src, here, sem.at[first + len(copies)]))
            copies[-1].start()
            at += src.shape[1]
    return copies


def begin_input_grad(facts, w, own, after=()):
    out_cols, depth = w.shape
    half = depth // 2
    rows = own[0].shape[0]
    count = len(own)

    def body(facts, w_ref, *refs):
        mine, out = jnp.concatenate([r[...] for r in refs[:count]], axis=1), refs[-1]
        where = pl.ds(pl.multiple_of(facts[SIDE] * half, half), half)
        for at in width_tiles(w):
            out[at] = dot_t(w_ref[at, where], mine)

    smem = pl.BlockSpec(memory_space=pltpu.SMEM)
    vmem = pl.BlockSpec(memory_space=pltpu.VMEM)
    near = [pltpu.with_memory_space_constraint(a, pltpu.VMEM) for a in (w, *own)]

    def kernel(*refs):
        body(*refs[: 2 + count], refs[-1])

    return pl.pallas_call(
        kernel,
        out_shape=pltpu.VMEM((out_cols, rows), F32),
        in_specs=[smem] + [vmem] * len(near) + [pl.BlockSpec(memory_space=pl.ANY)] * len(after),
        out_specs=vmem,
        compiler_params=pltpu.CompilerParams(vmem_limit_bytes=LARGE),
        cost_estimate=SLIGHT,
    )(pltpu.with_memory_space_constraint(facts, pltpu.SMEM), *near, *after)


def end_input_grad(facts, w, far, begun, grads, carry=None, after=()):
    tiles = width_tiles(w)
    out_cols, depth = w.shape
    half = depth // 2
    steps = len(tiles)
    rows = far[0].shape[0]
    top = 0 if rows == PAGE else PAGE
    width = sum(a.shape[1] for a in grads[0])
    near = [w, begun, *far, *grads[0], *grads[1]]
    carry = list(carry or [])

    def body(facts, w_r, begun_r, *refs):
        far_r, grad_r = refs[: len(far)], refs[len(far) : len(near) - 2]
        out, dk, dv, made, stage, sem = refs[-6:]
        made[...] = jnp.zeros_like(made)
        copies = put_rows(grad_r, dk, dv, top, rows, sem, steps)
        other = jnp.concatenate([r[...] for r in far_r], axis=1)
        where = pl.ds(pl.multiple_of((1 - facts[SIDE]) * half, half), half)
        for i, at in enumerate(tiles):
            stage[i] = (dot_t(w_r[at, where], other) + begun_r[at]).astype(BF16).T
            copies.append(
                pltpu.make_async_copy(stage.at[i], out.at[top : top + rows, at], sem.at[i])
            )
            copies[-1].start()
        for c in copies:
            c.wait()

    smem = pl.BlockSpec(memory_space=pltpu.SMEM)
    vmem = pl.BlockSpec(memory_space=pltpu.VMEM)
    hbm = pl.BlockSpec(memory_space=pl.ANY)
    near = [pltpu.with_memory_space_constraint(a, pltpu.VMEM) for a in near]
    kept = jax.ShapeDtypeStruct((ROWS, width), BF16)

    def kernel(*refs):
        body(*refs[: 1 + len(near)], *refs[1 + len(near) + len(carry) + len(after) :])

    return pl.pallas_call(
        kernel,
        out_shape=(
            jax.ShapeDtypeStruct((ROWS, out_cols), BF16), kept, kept, pltpu.VMEM((8, HD), F32)
        ),
        in_specs=[smem] + [vmem] * len(near) + [hbm] * (len(carry) + len(after)),
        out_specs=(hbm, hbm, hbm, vmem),
        scratch_shapes=[
            pltpu.VMEM((steps, rows, out_cols // steps), BF16),
            pltpu.SemaphoreType.DMA((steps + 2 * len(grads[0]),)),
        ],
        input_output_aliases={1 + len(near) + i: i for i in range(len(carry))},
        compiler_params=pltpu.CompilerParams(vmem_limit_bytes=LARGE),
        cost_estimate=SLIGHT,
    )(pltpu.with_memory_space_constraint(facts, pltpu.SMEM), *near, *carry, *after)


def flipped(block, axis, bit):
    count = lax.axis_size(axis)
    return lax.ppermute(block, axis, [(i, i ^ bit) for i in range(count) if i ^ bit < count])


def spanning(leaves, bit_index):
    return len([j for j in range(INNER) if 2 << bit_index <= leaves >> j])


def gather_small_tree(facts, own, beside_pair, beside_half):
    two = (own.shape, BF16, True)
    page = (own.shape[1:], BF16, True)
    from_core = flipped(own, "sub", 1)

    def choose_chip(facts, own_ref, far_ref, out):
        for kind in range(2):
            for mine in range(2):

                @pl.when((facts[LEADS] != kind) & (facts[OWNS2] != mine))
                def _copy(kind=kind, mine=mine):
                    out[...] = (own_ref if mine else far_ref)[kind]

    (chip,) = kernel_call(choose_chip, facts, [own, from_core], [], [page])
    from_pair = flipped(chip, "leaf", 1)

    def choose_pair(facts, near_ref, far_ref, out):
        out[...] = jnp.where(facts[ROOT_IN_CHIP] == 1, near_ref[...], far_ref[...])

    after = beside_pair(from_core, chip)
    (pair,) = kernel_call(choose_pair, facts, [chip, from_pair], [], [page], after=after)
    from_half = flipped(pair, "leaf", 2)

    def choose_all(facts, chip_ref, pair_far, pair_ref, half_far, out):
        out[0] = jnp.where(facts[ROOT_IN_PAIR] == 1, pair_ref[...], half_far[...])
        out[1] = jnp.where(facts[NEXT_IN_CHIP] == 1, chip_ref[...], pair_far[...])

    after = beside_half(pair)
    (mine,) = kernel_call(
        choose_all, facts, [chip, from_pair, pair, from_half], [], [two], after=after
    )
    return mine, flipped(mine, "sub", 1)


def over_cores(facts, kept, sent):
    width = kept.shape[-1]

    def body(_, near, away, total, root, next_one):
        for j, low in enumerate((root, next_one)):
            value = near[j] + away[j].astype(F32)
            total[j] = value
            low[...] = value.astype(BF16)

    page = ((PAGE, width), BF16, True)
    total, root, next_one = kernel_call(
        body, facts, [kept, flipped(sent, "sub", 1)], [],
        [((2, PAGE, width), F32, True), page, page],
    )
    return total, root, flipped(root, "leaf", 2), flipped(next_one, "leaf", 1)


def over_halves(facts, total, root_far, next_far, after):
    width = total.shape[-1]

    def body(_, near, root_r, next_r, out, low):
        root = near[0] + root_r[...].astype(F32)
        out[0] = root
        low[...] = root.astype(BF16)
        out[1] = near[1] + next_r[...].astype(F32)

    total, low = kernel_call(
        body, facts, [total, root_far, next_far], [],
        [((2, PAGE, width), F32, True), ((PAGE, width), BF16, True)], after=after,
    )
    return total, low, flipped(low, "leaf", 1)


def over_chips(facts, total, far, passenger, after):
    width = total.shape[-1]
    more = passenger.shape[-1]

    def body(facts, near, away, extra, out):
        root = near[0] + away[...].astype(F32)
        out[:, :width] = jnp.where(facts[ROOT_IN_CHIP] == 1, root, near[1]).astype(BF16)
        for kind in range(2):
            out[:, width + kind * more : width + (kind + 1) * more] = extra[kind]

    outs = [((PAGE, width + 2 * more), BF16, True)]
    (mine,) = kernel_call(
        body, facts, [total, far, passenger], [], outs, after=after
    )
    return mine, flipped(mine, "sub", 1)


def finish_small_tree(facts, own0, mine, far, level2_far):
    width = sum(a.shape[-1] for a in own0)

    def body(facts, own_r, own_last, mine_r, far_r, low_r, dk, dv):
        owns2, leads = facts[OWNS2] == 1, facts[LEADS] == 1
        ok = row_ok(facts[N0], PAGE, HD)
        for at in range(0, width, HD):
            c = slice(at, at + HD)
            last = at + HD == width
            near, away = mine_r[:, c], far_r[:, c]
            gained = [jnp.where(leads, near, away), jnp.where(leads, away, near)]
            for kind, out in enumerate((dk, dv)):
                if last:
                    level2 = far_r[:, width + kind * HD : width + (kind + 1) * HD]
                else:
                    level2 = low_r[kind, :, c]
                more = jnp.where(owns2, level2, gained[kind]).astype(F32)
                base = own_last[kind] if last else own_r[kind, :, c]
                out[:, c] = jnp.where(ok, base + more, 0.0).astype(BF16)

    page = ((PAGE, width), BF16, True)
    return kernel_call(
        body, facts, [*own0, mine, far, level2_far], [], [page, page]
    )


def gather_tree(ids, own):
    leaves = lax.axis_size(("leaf", "sub"))
    owned = ids[:INNER] == ids[INNER] - 1
    pages = jnp.where(owned[:, None, None, None], own[None], jnp.zeros((), BF16))
    for bit in range(leaves.bit_length() - 1):
        active = spanning(leaves, bit)
        far = flipped(pages[:active], ("leaf", "sub"), 1 << bit)
        pages = jnp.concatenate([pages[:active] + far, pages[active:]])
    return pages


def reduce_tree(ids, parts):
    leaves = lax.axis_size(("leaf", "sub"))
    for bit in range(leaves.bit_length() - 1):
        active = spanning(leaves, bit)
        far = flipped(parts[:active], ("leaf", "sub"), 1 << bit)
        parts = jnp.concatenate([parts[:active] + far, parts[active:]])
    owned = ids[:INNER] == ids[INNER] - 1
    return jnp.sum(jnp.where(owned[:, None, None, None], parts, 0.0), axis=0)


def on_device(queries, grad_out, keys, values, log_norms, row_deltas, ancestors, counts, w_value):
    kv = keys.shape[1] // HD
    group = queries.shape[1] // keys.shape[1]
    leaves = lax.axis_size(("leaf", "sub"))
    hbm = lambda a: pltpu.with_memory_space_constraint(a, pltpu.HBM)
    side = lax.axis_index("tensor").astype(I32).reshape(1)
    two_sides = lax.axis_size("tensor") == 2
    inputs = [hbm(a) for a in (queries, grad_out, keys, values, log_norms, row_deltas)]
    facts, own = start(side, hbm(ancestors), hbm(counts), *inputs[2:4])
    state = {}

    def own_pages(kvs, pages, prior=(), after=(), w=None):
        return attend(True, kvs, group, facts, inputs, pages, state, prior, after, w)

    def shared_pages(kvs, pages):
        return attend(False, kvs, group, facts, inputs, pages, state)

    def spread(part):
        if two_sides:
            return flipped(part, "tensor", 1)
        return lax.all_gather(part, "tensor", axis=1, tiled=True)

    kvs = tuple(range(kv))
    w = hbm(w_value)
    if leaves == 8 and lax.axis_size("sub") == 2 and kv >= 3 and two_sides:
        level2, results = [], []

        def beside_pair(from_core, chip):
            level2.extend((own, from_core))
            results.append(own_pages(kvs[:1], level2, after=(chip,)))
            return (results[-1][3],)

        def beside_half(pair):
            results.append(own_pages(kvs[1:-1], level2, results[-1], (pair,)))
            return (results[-1][3],)

        shared = gather_small_tree(facts, own, beside_pair, beside_half)
        most = results[-1]
        far_v = [spread(most[1])]
        level2_far = flipped(most[3], "sub", 1)
        kept, sent = shared_pages(kvs, shared)
        total, root, root_far, next_far = over_cores(facts, kept, sent)
        *last, w_near = own_pages(kvs[-1:], level2, after=(root,), w=w)
        both = list(zip(most, last))
        begun = begin_input_grad(facts, w_near, both[1], (far_v[0], level2_far))
        far_v.append(spread(last[1]))
        total, low, far = over_halves(facts, total, root_far, next_far, (begun,))
        *grads, made = end_input_grad(facts, w_near, far_v, begun, both[:2], after=(low,))
        mine, far = over_chips(facts, total, far, last[3], (made,))
        dk0, dv0 = finish_small_tree(facts, both[2], mine, far, level2_far)
        far_v = spread(dv0)
        begun = begin_input_grad(facts, w_near, [dv0])
        grads = end_input_grad(facts, w_near, [far_v], begun, ([dk0], [dv0]), grads)
        return (state["gq"], grads[1], grads[2], grads[0])

    first = lax.axis_index("sub") == 0
    path_ids = ancestors[0]
    pages = gather_tree(path_ids, own)
    dk12, dv12, own0, send2 = own_pages(kvs, (pages[2], pages[2]))
    kept, sent = shared_pages(
        kvs,
        (
            jnp.where(first, pages[:2, 0], pages[:2, 1]),
            jnp.where(first, pages[:2, 1], pages[:2, 0]),
        ),
    )
    sent = sent.astype(F32)
    upper = jnp.stack([jnp.where(first, kept, sent), jnp.where(first, sent, kept)], axis=1)
    low = send2.astype(F32)
    total = reduce_tree(path_ids, jnp.concatenate([upper, low[None]]))
    total += own0 - jnp.where(path_ids[2] == path_ids[INNER] - 1, low, 0.0)
    has = jnp.any(path_ids[:INNER] == path_ids[INNER] - 1)
    ok = (jnp.arange(PAGE) < jnp.where(has, counts[0, 0], 0))[:, None]
    dk0, dv0 = jnp.where(ok, total, 0.0).astype(BF16)
    if two_sides:
        pair = lambda part: ([part], [spread(part)])
    else:
        pair = lambda part: ([spread(part)], [])
    *grads, _ = input_grad(facts, w, 2 * PAGE, *pair(dv12), ([dk12], [dv12]))
    grads = input_grad(facts, w, PAGE, *pair(dv0), ([dk0], [dv0]), grads)
    return (state["gq"], grads[1], grads[2], grads[0])


def solution(mesh):
    placed = (
        P(("groups", "leaf", "sub"), "tensor"),
        P(("groups", "leaf", "sub"), "tensor"),
        P(("groups", "leaf", "sub"), "tensor"),
        P(("groups", "leaf", "sub"), "tensor"),
        P("tensor", ("groups", "leaf", "sub")),
        P("tensor", ("groups", "leaf", "sub")),
        P(("groups", "leaf", "sub"), None),
        P(("groups", "leaf", "sub"), None),
        P("tensor", None),
    )
    return jax.shard_map(
        on_device,
        mesh=mesh,
        in_specs=placed,
        out_specs=(
            P(("groups", "leaf", "sub"), "tensor"),
            P(("groups", "leaf", "sub"), "tensor"),
            P(("groups", "leaf", "sub"), "tensor"),
            P(("groups", "leaf", "sub"), "tensor"),
        ),
        check_vma=False,
    )
```

```python
import math

import jax
import jax.numpy as jnp
from jax import lax
from jax.experimental import pallas as pl
from jax.experimental.pallas import tpu as pltpu
from jax.sharding import PartitionSpec as P

HD = 128
PAGE = 128
SLOTS = 3
INNER = 3
ROWS = SLOTS * PAGE
LOG2E = math.log2(math.e)
SCALE = 1.0 / math.sqrt(HD)
BF16 = jnp.bfloat16
F32 = jnp.float32
I32 = jnp.int32
LARGE = 10 << 20
SMALL = 4 << 20
SLIGHT = pl.CostEstimate(flops=1000, bytes_accessed=1000, transcendentals=0)
BLOCKED = 1e30


def dot_t(left, right):
    return lax.dot_general(left, right, (((1,), (1,)), ((), ())), preferred_element_type=F32)


def dot_n(left, right):
    return lax.dot_general(left, right, (((1,), (0,)), ((), ())), preferred_element_type=F32)


FACTS = 16
N0, N1, N2, OWNS2, LIMIT, LEADS, ROOT_IN_CHIP, ROOT_IN_PAIR, NEXT_IN_CHIP, SIDE = range(10)


def write_facts(facts, ids, counts, side):
    page = [ids[0, j] for j in range(INNER + 1)]
    own = page[INNER] - 1
    leaf = own // SLOTS
    owns = [page[j] == own for j in range(INNER)]
    same = lambda level, shift: ((page[level] // SLOTS) >> shift) == (leaf >> shift)
    number = lambda flag: jnp.where(flag, 1, 0)
    facts[N0] = jnp.where(owns[0] | owns[1] | owns[2], counts[0, 0], 0)
    facts[N1] = counts[0, 1]
    facts[N2] = counts[0, 2]
    facts[OWNS2] = number(owns[2])
    facts[LIMIT] = jnp.where(owns[2], 2 * PAGE, jnp.where(owns[1], PAGE, 0))
    facts[LEADS] = number(lax.rem(leaf, 2) == 0)
    facts[ROOT_IN_CHIP] = number(same(0, 1))
    facts[ROOT_IN_PAIR] = number(same(0, 2))
    facts[NEXT_IN_CHIP] = number(same(1, 1))
    facts[SIDE] = side
    for i in range(SIDE + 1, FACTS):
        facts[i] = 0


def row_ok(count, rows, width):
    return lax.broadcasted_iota(I32, (rows, width), 0) < count


def kernel_call(body, facts, near, far, outs, scratch=(), aliases=None, after=(), cost=None,
                limit=SMALL):
    smem = pl.BlockSpec(memory_space=pltpu.SMEM)
    vmem = pl.BlockSpec(memory_space=pltpu.VMEM)
    hbm = pl.BlockSpec(memory_space=pl.ANY)
    near = [pltpu.with_memory_space_constraint(a, pltpu.VMEM) for a in near]
    place = {("near", i): 1 + i for i in range(len(near))}
    place |= {("far", i): 1 + len(near) + i for i in range(len(far))}
    used = 1 + len(near) + len(far)

    def kernel(*refs):
        body(*refs[:used], *refs[used + len(after) :])

    return pl.pallas_call(
        kernel,
        out_shape=tuple(
            pltpu.VMEM(s, d) if inside else jax.ShapeDtypeStruct(s, d) for s, d, inside in outs
        ),
        in_specs=[smem] + [vmem] * len(near) + [hbm] * (len(far) + len(after)),
        out_specs=tuple(vmem if inside else hbm for _, _, inside in outs),
        scratch_shapes=list(scratch),
        input_output_aliases={place[k]: v for k, v in (aliases or {}).items()},
        compiler_params=pltpu.CompilerParams(vmem_limit_bytes=limit),
        cost_estimate=cost or SLIGHT,
    )(pltpu.with_memory_space_constraint(facts, pltpu.SMEM), *near, *far, *after)


def start(side, ids, counts, keys, values):
    width = keys.shape[1]

    def body(side_ref, ids_ref, counts_ref, k_ref, v_ref, facts, out, held, ids_s, counts_s, sem):
        copies = [
            pltpu.make_async_copy(src, dst, sem.at[i])
            for i, (src, dst) in enumerate(
                (
                    (ids_ref, ids_s),
                    (counts_ref, counts_s),
                    (k_ref.at[:PAGE], held.at[0]),
                    (v_ref.at[:PAGE], held.at[1]),
                )
            )
        ]
        for c in copies:
            c.start()
        copies[0].wait()
        copies[1].wait()
        write_facts(facts, ids_s, counts_s, side_ref[0])
        ok = row_ok(counts_s[0, 0], PAGE, width)
        for i in range(2):
            copies[2 + i].wait()
            out[i] = jnp.where(ok, held[i], jnp.zeros((), BF16))

    smem = pl.BlockSpec(memory_space=pltpu.SMEM)
    hbm = pl.BlockSpec(memory_space=pl.ANY)
    return pl.pallas_call(
        body,
        out_shape=(pltpu.SMEM((FACTS,), I32), pltpu.VMEM((2, PAGE, width), BF16)),
        in_specs=[smem] + [hbm] * 4,
        out_specs=(smem, pl.BlockSpec(memory_space=pltpu.VMEM)),
        scratch_shapes=[
            pltpu.VMEM((2, PAGE, width), BF16),
            pltpu.SMEM(ids.shape, I32),
            pltpu.SMEM(counts.shape, I32),
            pltpu.SemaphoreType.DMA((4,)),
        ],
        compiler_params=pltpu.CompilerParams(vmem_limit_bytes=SMALL),
    )(side, ids, counts, keys, values)


def row_terms(rows):
    high = rows.astype(BF16).astype(F32)
    rest = rows - high
    middle = rest.astype(BF16).astype(F32)
    parts = [high, middle, rest - middle]
    spare = HD - 3 * rows.shape[0]
    parts.append(jnp.zeros((spare, rows.shape[1]), F32))
    return jnp.concatenate(parts, axis=0).T.astype(BF16)


class Head:
    def __init__(self, kv, group, norms, deltas, en, ed):
        self.group = group
        self.heads = min(4, group)
        self.parts = group // self.heads
        self.tall = self.heads * PAGE
        heads = slice(kv * group, (kv + 1) * group)
        en[...] = row_terms(norms[heads, :])
        ed[...] = row_terms(deltas[heads, :])

    def lanes(self, part, j):
        at = (part * self.heads + j) * HD
        return slice(at, at + HD)

    def stacked(self, ref, part, slots):
        return jnp.concatenate(
            [
                ref[slot * PAGE : (slot + 1) * PAGE, self.lanes(part, j)]
                for slot in slots
                for j in range(self.heads)
            ],
            axis=0,
        )

    def deep(self, stacked, terms, part, slots):
        column = lax.broadcasted_iota(I32, (1, HD), 1) % self.group
        picks = [
            (column == part * self.heads + j).astype(F32).astype(BF16)
            for j in range(self.heads)
        ]
        extra = [
            terms[slot * PAGE : (slot + 1) * PAGE] * pick for slot in slots for pick in picks
        ]
        return jnp.concatenate([stacked, jnp.concatenate(extra, axis=0)], axis=1)

    def turned_at(self, part, slot, count):
        at = (part * SLOTS + slot) * self.tall
        return slice(at, at + self.tall * count)

    def put_queries(self, part, slot, rows_by_head, dq, add, stage):
        rows = slice(slot * PAGE, (slot + 1) * PAGE)
        for j in range(self.heads):
            value = rows_by_head[j * PAGE : (j + 1) * PAGE]
            if stage is None:
                dq[rows, self.lanes(part, j)] = value
            else:
                if add:
                    value = value + dq[rows, self.lanes(part, j)]
                stage[rows, j * HD : (j + 1) * HD] = (value * SCALE).astype(BF16)


def set_keys(deep, upright, at, page):
    where = slice(at * PAGE, (at + 1) * PAGE)
    deep[:HD, where] = page.T
    if upright is not None:
        upright[where] = page


def weigh(scores, grads, keep):
    p = keep(jnp.exp2(scores * (SCALE * LOG2E)))
    return p.astype(BF16), (p * grads).astype(BF16)


def attend(own, kvs, group, facts, inputs, pages, state, prior=(), after=(), w=None):
    loading = "k" not in state
    q_all, k_all = inputs[0], inputs[2]
    count = len(kvs)
    parts = group // min(4, group)
    tall = min(4, group) * PAGE
    wide = min(4, group) * HD
    width = count * HD
    base = prior[0].shape[1] if prior else 0
    kv_total = k_all.shape[1] // HD
    fresh = [("dq", kv) not in state for kv in kvs]
    one_head = (ROWS, group * HD)
    turned = ((HD, group * ROWS), BF16, True)
    shapes = {"dq": (one_head, F32, True), "qt": turned, "gt": turned}

    near, far, aliases, outs = [], [], {}, []
    at_near, at_far, at_out = {}, {}, {}

    def add_near(name, array):
        at_near[name] = len(near)
        near.append(array)

    def add_far(name, array):
        at_far[name] = len(far)
        far.append(array)

    def add_out(name, out):
        at_out[name] = len(outs)
        outs.append(out)

    for kv, is_fresh in zip(kvs, fresh):
        for name, shape in shapes.items():
            if is_fresh:
                add_out((name, kv), shape)
            elif own or name != "dq":
                add_near((name, kv), state[name, kv])
        if not own and not is_fresh:
            add_out(("ds", kv), ((group * ROWS, 2 * PAGE), BF16, True))
    if own and not all(fresh):
        add_out("gq", (q_all.shape, BF16, False))
        if "gq" in state:
            add_far("gq", state["gq"])
            aliases["far", at_far["gq"]] = at_out["gq"]
    at_results = len(outs)
    if own:
        outs += [
            ((2 * PAGE, base + width), BF16, True),
            ((2 * PAGE, base + width), BF16, True),
            ((2, PAGE, base + width), F32, True),
            ((2, PAGE, base + width), BF16, True),
        ]
    else:
        outs += [
            ((2, PAGE, width), F32, True),
            ((2, PAGE, width), BF16, True),
        ]
    at_loaded = len(outs)
    if loading:
        for name, array in zip(("q", "g", "k", "v", "norms", "deltas"), inputs):
            add_far(name, array)
            if name in ("q", "g"):
                for kv in range(kv_total):
                    add_out((name, kv), (one_head, BF16, True))
            else:
                add_out(name, (array.shape, array.dtype, True))
    else:
        for name in ("k", "v", "norms", "deltas"):
            add_near(name, state[name])
        for kv in kvs:
            for name in ("q", "g"):
                add_near((name, kv), state[name, kv])
    at_end = len(outs)
    if w is not None:
        add_far("w", w)
        outs.append((w.shape, w.dtype, True))
    for i, page in enumerate(pages):
        add_near(("page", i), page)
    for i, array in enumerate(prior):
        add_near(("prior", i), array)
    key_pages = 4 if own else 2
    scratch = [
        pltpu.VMEM((2 * HD, key_pages * PAGE), BF16),
        pltpu.VMEM((2 * HD, key_pages * PAGE), BF16),
        pltpu.VMEM((key_pages * PAGE, HD), BF16),
        pltpu.VMEM((2, HD, key_pages * PAGE), F32),
        pltpu.VMEM((ROWS, HD), BF16),
        pltpu.VMEM((ROWS, HD), BF16),
        pltpu.VMEM((count * parts, ROWS, wide), BF16),
        pltpu.SemaphoreType.DMA((count * parts,)),
        pltpu.SemaphoreType.DMA((2 * kv_total + 5,)),
    ]
    cols = lambda a, b: slice(a * PAGE, b * PAGE)

    def body(facts, *refs):
        ins, out_refs = refs[: len(near) + len(far)], refs[len(near) + len(far) : -len(scratch)]
        k_deep, v_deep, k_up, acc, en, ed, stage, sem, load_sem = refs[-len(scratch) :]
        near_ref = lambda name: ins[at_near[name]]
        far_ref = lambda name: ins[len(near) + at_far[name]]
        held = lambda name: out_refs[at_out[name]] if name in at_out else near_ref(name)
        results = out_refs[at_results:at_loaded]
        copies = {}
        if loading:

            def load(key, src):
                copies[key] = pltpu.make_async_copy(src, held(key), load_sem.at[len(copies)])
                copies[key].start()

            for name in ("k", "v", "norms", "deltas"):
                load(name, far_ref(name))
            for kv in range(kv_total):
                at = slice(kv * group * HD, (kv + 1) * group * HD)
                for name in ("q", "g"):
                    load((name, kv), far_ref(name).at[:, at])
        if w is not None:
            w_copy = pltpu.make_async_copy(
                far_ref("w"), out_refs[at_end], load_sem.at[2 * kv_total + 4]
            )
            w_copy.start()
        k, v, norms, deltas = (held(name) for name in ("k", "v", "norms", "deltas"))

        def arrived(*keys):
            for key in keys:
                if key in copies:
                    copies.pop(key).wait()

        k_deep[HD:] = jnp.full((HD, key_pages * PAGE), -1.0, BF16)
        v_deep[HD:] = jnp.full((HD, key_pages * PAGE), -1.0, BF16)
        for out, i in zip(results, range(len(prior))):
            out[..., :base] = near_ref(("prior", i))[...]
        owns2, leads = facts[OWNS2] == 1, facts[LEADS] == 1
        if loading:
            arrived("norms", "deltas", "k", "v")
            lane = lax.broadcasted_iota(I32, norms.shape, 1)
            limit = jnp.where(
                lane < PAGE, facts[N0], jnp.where(lane < 2 * PAGE, facts[N1], facts[N2])
            )
            norms[...] = jnp.where(lane % PAGE < limit, norms[...] * (1.0 / SCALE), BLOCKED)
        lower = lambda rows: lax.broadcasted_iota(I32, (rows, PAGE), 1) <= (
            lax.broadcasted_iota(I32, (rows, PAGE), 0) % PAGE
        )

        def set_pages(n, kv):
            lane = slice(kv * HD, (kv + 1) * HD)
            first, second = (near_ref(("page", i)) for i in range(2))
            if own:
                zero = jnp.zeros((), BF16)
                for slot, (at, c) in enumerate(((3, N0), (0, N1), (2, N2))):
                    ok = row_ok(facts[c], PAGE, HD)
                    rows = cols(slot, slot + 1)
                    set_keys(k_deep, k_up, at, jnp.where(ok, k[rows, lane], zero))
                    set_keys(v_deep, None, at, jnp.where(ok, v[rows, lane], zero))
                level2 = [jnp.where(owns2, first[i, :, lane], second[i, :, lane]) for i in (0, 1)]
                set_keys(k_deep, k_up, 1, level2[0])
                set_keys(v_deep, None, 1, level2[1])
            else:
                for j in range(2):
                    mine, theirs = first[j, :, lane], second[j, :, lane]
                    set_keys(k_deep, k_up, j, jnp.where(leads, mine, theirs))
                    set_keys(v_deep, None, j, jnp.where(leads, theirs, mine))
            acc[...] = jnp.zeros_like(acc)

        def turned_rows(head, kv, part, is_fresh, qs, gs, order):
            if is_fresh:
                for name, rows in (("qt", qs), ("gt", gs)):
                    for i, slot in enumerate(order):
                        held((name, kv))[:, head.turned_at(part, slot, 1)] = rows[
                            i * tall : (i + 1) * tall
                        ].T
            return lambda name, slot, slots: held((name, kv))[
                :, head.turned_at(part, slot, slots)
            ]

        def own_part(head, kv, part, n, stage_ref):
            order = (1, 2, 0)
            qs = head.stacked(held(("q", kv)), part, order)
            gs = head.stacked(held(("g", kv)), part, order)
            qd, gd = head.deep(qs, en, part, order), head.deep(gs, ed, part, order)
            turn = turned_rows(head, kv, part, fresh[n], qs, gs, order)
            low = lower(tall)

            def keep_first(p):
                masked = jnp.where(low, p[:tall, :PAGE], 0.0)
                return jnp.concatenate(
                    [jnp.concatenate([masked, p[:tall, PAGE:]], axis=1), p[tall:]], axis=0
                )

            pa, da = weigh(
                dot_n(qd[: 2 * tall], k_deep[:, : 2 * PAGE]),
                dot_n(gd[: 2 * tall], v_deep[:, : 2 * PAGE]),
                keep_first,
            )
            both = lambda x: jnp.concatenate([x[:tall, :PAGE], x[tall:, PAGE:]], axis=0)
            low2 = lower(2 * tall)
            pb, db = weigh(
                both(dot_n(qd[tall:], k_deep[:, 2 * PAGE :])),
                both(dot_n(gd[tall:], v_deep[:, 2 * PAGE :])),
                lambda p: jnp.where(low2, p, 0.0),
            )
            for i, (name, a, b) in enumerate((("qt", da, db), ("gt", pa, pb))):
                acc[i, :, : 2 * PAGE] += dot_n(turn(name, 1, 2), a)
                acc[i, :, cols(2, 3)] += dot_n(turn(name, 2, 1), b[:tall])
                acc[i, :, cols(3, 4)] += dot_n(turn(name, 0, 1), b[tall:])
            first = dot_n(da, k_up[: 2 * PAGE])
            put = lambda slot, rows: head.put_queries(
                part, slot, rows, held(("dq", kv)), not fresh[n], stage_ref
            )
            put(1, first[:tall])
            put(2, first[tall:] + dot_n(db[:tall], k_up[cols(2, 3)]))
            put(0, dot_n(db[tall:], k_up[cols(3, 4)]))

        def shared_part(head, kv, part, n, stage_ref):
            order = (0, 1, 2)
            qs = head.stacked(held(("q", kv)), part, order)
            gs = head.stacked(held(("g", kv)), part, order)
            qd, gd = head.deep(qs, en, part, order), head.deep(gs, ed, part, order)
            turn = turned_rows(head, kv, part, fresh[n], qs, gs, order)
            column = lax.broadcasted_iota(I32, (tall, 2 * PAGE), 1)
            seen = column < facts[LIMIT]

            def keep(p):
                return jnp.concatenate([jnp.where(seen, p[:tall], 0.0), p[tall:]], axis=0)

            p, ds = weigh(dot_n(qd, k_deep[...]), dot_n(gd, v_deep[...]), keep)
            acc[0] += dot_n(turn("qt", 0, SLOTS), ds)
            acc[1] += dot_n(turn("gt", 0, SLOTS), p)
            if not fresh[n]:
                held(("ds", kv))[part * SLOTS * tall : (part + 1) * SLOTS * tall] = ds
                return
            dq = dot_n(ds, k_up[...])
            for slot in range(SLOTS):
                head.put_queries(
                    part, slot, dq[slot * tall : (slot + 1) * tall], held(("dq", kv)), not fresh[n],
                    stage_ref,
                )

        def put_own(n):
            dk12, dv12, own0, send2 = results
            here = slice(base + n * HD, base + (n + 1) * HD)
            grad = [acc[0].T * SCALE, acc[1].T]
            for at, c, to in ((0, N1, 0), (2, N2, 1)):
                ok = row_ok(facts[c], PAGE, HD)
                for kind, out in ((0, dk12), (1, dv12)):
                    out[cols(to, to + 1), here] = jnp.where(
                        ok, grad[kind][cols(at, at + 1)], 0.0
                    ).astype(BF16)
            for kind in range(2):
                level2 = grad[kind][cols(1, 2)]
                own0[kind, :, here] = grad[kind][cols(3, 4)] + jnp.where(owns2, level2, 0.0)
                send2[kind, :, here] = level2.astype(BF16)

        def put_shared(n):
            kept, sent = results
            here = slice(n * HD, (n + 1) * HD)
            grad_k, grad_v = acc[0].T * SCALE, acc[1].T
            for j in range(2):
                a, b = grad_k[cols(j, j + 1)], grad_v[cols(j, j + 1)]
                kept[j, :, here] = jnp.where(leads, a, b)
                sent[j, :, here] = jnp.where(leads, b, a).astype(BF16)

        sends = []
        for n, kv in enumerate(kvs):
            arrived(("q", kv), ("g", kv))
            head = Head(kv, group, norms, deltas, en, ed)
            set_pages(n, kv)

            for part in range(parts):
                slot = n * parts + part
                (own_part if own else shared_part)(
                    head, kv, part, n, stage.at[slot] if own and not fresh[n] else None
                )
                if own and not fresh[n]:
                    at = (kv * parts + part) * wide
                    sends.append(
                        pltpu.make_async_copy(
                            stage.at[slot], held("gq").at[:, at : at + wide], sem.at[slot]
                        )
                    )
                    sends[-1].start()

            (put_own if own else put_shared)(n)
        for c in sends:
            c.wait()
        arrived(*list(copies))
        if w is not None:
            w_copy.wait()

    made = kernel_call(
        body, facts, near, far, outs, scratch, aliases, after,
        pl.CostEstimate(
            flops=240 * PAGE * PAGE * HD * group * count, bytes_accessed=1000, transcendentals=0
        ),
        LARGE,
    )
    for name, at in at_out.items():
        state[name] = made[at]
    return list(made[at_results:at_loaded]) + list(made[at_end:])


def width_tiles(w):
    tile = next(t for t in (512, 640, 320, 128, w.shape[0]) if w.shape[0] % t == 0)
    return [slice(i, i + tile) for i in range(0, w.shape[0], tile)]


def finish_queries(kvs, group, facts, pages, state, after=()):
    parts = group // min(4, group)
    heads = group // parts
    tall = heads * PAGE
    wide = heads * HD
    near = list(pages)
    for kv in kvs:
        near += [state["ds", kv], state["dq", kv]]

    def body(facts, mine, theirs, *refs):
        gq, made, stage, sem = refs[-4:]
        made[...] = jnp.zeros_like(made)
        leads = facts[LEADS] == 1
        sends = []
        for n, kv in enumerate(kvs):
            ds, dq = refs[2 * n : 2 * n + 2]
            lane = slice(kv * HD, (kv + 1) * HD)
            keys = jnp.concatenate(
                [jnp.where(leads, mine[j, :, lane], theirs[j, :, lane]) for j in range(2)], axis=0
            )
            for part in range(parts):
                at = n * parts + part
                gained = dot_n(ds[part * SLOTS * tall : (part + 1) * SLOTS * tall], keys)
                for i in range(SLOTS * heads):
                    slot, j = divmod(i, heads)
                    rows = slice(slot * PAGE, (slot + 1) * PAGE)
                    value = gained[i * PAGE : (i + 1) * PAGE] + dq[
                        rows, part * wide + j * HD : part * wide + (j + 1) * HD
                    ]
                    stage[at, rows, j * HD : (j + 1) * HD] = (value * SCALE).astype(BF16)
                to = (kv * parts + part) * wide
                sends.append(
                    pltpu.make_async_copy(stage.at[at], gq.at[:, to : to + wide], sem.at[at])
                )
                sends[-1].start()
        for c in sends:
            c.wait()

    count = len(kvs) * parts
    far = [state["gq"]] if "gq" in state else []
    shape = (ROWS, state["k"].shape[1] * group)
    state["gq"], made = kernel_call(
        body, facts, near, far, [(shape, BF16, False), ((8, HD), F32, True)],
        [pltpu.VMEM((count, ROWS, wide), BF16), pltpu.SemaphoreType.DMA((count,))],
        {("far", 0): 0} if far else {}, after, limit=LARGE,
    )
    return made


def input_grad(facts, w, rows, own, far, grads, carry=None):
    out_cols, depth = w.shape
    tiles = width_tiles(w)
    top = 0 if rows == PAGE else PAGE
    steps = len(tiles)
    width = sum(a.shape[1] for a in grads[0])
    arrays = [*own, *far, *grads[0], *grads[1]]
    count = len(grads[0])
    carry = list(carry or [])

    def body(facts, *refs):
        own_r, refs = refs[: len(own)], refs[len(own) :]
        far_r, refs = refs[: len(far)], refs[len(far) :]
        grad_r, w_ref = refs[: 2 * count], refs[2 * count]
        out, dk, dv, made, w_near, stage, w_sem, sem = refs[-8:]
        loads = [
            pltpu.make_async_copy(w_ref.at[at], w_near.at[at], w_sem.at[i])
            for i, at in enumerate(tiles)
        ]
        for c in loads:
            c.start()
        made[...] = jnp.zeros_like(made)
        columns = lambda rs: jnp.concatenate([r[...] for r in rs], axis=1)
        full = columns(own_r)
        if far:
            other, leads = columns(far_r), facts[SIDE] == 0
            full = jnp.concatenate(
                [jnp.where(leads, full, other), jnp.where(leads, other, full)], axis=1
            )
        copies = put_rows(grad_r, dk, dv, top, rows, sem, steps)
        for i, at in enumerate(tiles):
            loads[i].wait()
            stage[i] = dot_t(w_near[at], full).astype(BF16).T
            copies.append(
                pltpu.make_async_copy(stage.at[i], out.at[top : top + rows, at], sem.at[i])
            )
            copies[-1].start()
        for c in copies:
            c.wait()

    smem = pl.BlockSpec(memory_space=pltpu.SMEM)
    vmem = pl.BlockSpec(memory_space=pltpu.VMEM)
    hbm = pl.BlockSpec(memory_space=pl.ANY)
    arrays = [pltpu.with_memory_space_constraint(a, pltpu.VMEM) for a in arrays]
    kept = jax.ShapeDtypeStruct((ROWS, width), BF16)
    return pl.pallas_call(
        body,
        out_shape=(
            jax.ShapeDtypeStruct((ROWS, out_cols), BF16), kept, kept, pltpu.VMEM((8, HD), F32)
        ),
        in_specs=[smem] + [vmem] * len(arrays) + [hbm] * (1 + len(carry)),
        out_specs=(hbm, hbm, hbm, vmem),
        scratch_shapes=[
            pltpu.VMEM(w.shape, BF16),
            pltpu.VMEM((steps, rows, out_cols // steps), BF16),
            pltpu.SemaphoreType.DMA((steps,)),
            pltpu.SemaphoreType.DMA((steps + 2 * count,)),
        ],
        input_output_aliases={2 + len(arrays) + i: i for i in range(len(carry))},
        compiler_params=pltpu.CompilerParams(vmem_limit_bytes=LARGE),
        cost_estimate=SLIGHT,
    )(pltpu.with_memory_space_constraint(facts, pltpu.SMEM), *arrays, w, *carry)


def put_rows(pieces, dk, dv, top, rows, sem, first):
    copies = []
    count = len(pieces) // 2
    for dst, mine in ((dk, pieces[:count]), (dv, pieces[count:])):
        at = 0
        for src in mine:
            here = dst.at[top : top + rows, at : at + src.shape[1]]
            copies.append(pltpu.make_async_copy(src, here, sem.at[first + len(copies)]))
            copies[-1].start()
            at += src.shape[1]
    return copies


def begin_input_grad(facts, w, own, after=()):
    out_cols, depth = w.shape
    half = depth // 2
    rows = own[0].shape[0]
    count = len(own)

    def body(facts, w_ref, *refs):
        mine, out = jnp.concatenate([r[...] for r in refs[:count]], axis=1), refs[-1]
        where = pl.ds(pl.multiple_of(facts[SIDE] * half, half), half)
        for at in width_tiles(w):
            out[at] = dot_t(w_ref[at, where], mine)

    smem = pl.BlockSpec(memory_space=pltpu.SMEM)
    vmem = pl.BlockSpec(memory_space=pltpu.VMEM)
    near = [pltpu.with_memory_space_constraint(a, pltpu.VMEM) for a in (w, *own)]

    def kernel(*refs):
        body(*refs[: 2 + count], refs[-1])

    return pl.pallas_call(
        kernel,
        out_shape=pltpu.VMEM((out_cols, rows), F32),
        in_specs=[smem] + [vmem] * len(near) + [pl.BlockSpec(memory_space=pl.ANY)] * len(after),
        out_specs=vmem,
        compiler_params=pltpu.CompilerParams(vmem_limit_bytes=LARGE),
        cost_estimate=SLIGHT,
    )(pltpu.with_memory_space_constraint(facts, pltpu.SMEM), *near, *after)


def end_input_grad(facts, w, far, begun, grads, carry=None, after=()):
    tiles = width_tiles(w)
    out_cols, depth = w.shape
    half = depth // 2
    steps = len(tiles)
    rows = far[0].shape[0]
    top = 0 if rows == PAGE else PAGE
    width = sum(a.shape[1] for a in grads[0])
    near = [w, begun, *far, *grads[0], *grads[1]]
    carry = list(carry or [])

    def body(facts, w_r, begun_r, *refs):
        far_r, grad_r = refs[: len(far)], refs[len(far) : len(near) - 2]
        out, dk, dv, made, stage, sem = refs[-6:]
        made[...] = jnp.zeros_like(made)
        copies = put_rows(grad_r, dk, dv, top, rows, sem, steps)
        other = jnp.concatenate([r[...] for r in far_r], axis=1)
        where = pl.ds(pl.multiple_of((1 - facts[SIDE]) * half, half), half)
        for i, at in enumerate(tiles):
            stage[i] = (dot_t(w_r[at, where], other) + begun_r[at]).astype(BF16).T
            copies.append(
                pltpu.make_async_copy(stage.at[i], out.at[top : top + rows, at], sem.at[i])
            )
            copies[-1].start()
        for c in copies:
            c.wait()

    smem = pl.BlockSpec(memory_space=pltpu.SMEM)
    vmem = pl.BlockSpec(memory_space=pltpu.VMEM)
    hbm = pl.BlockSpec(memory_space=pl.ANY)
    near = [pltpu.with_memory_space_constraint(a, pltpu.VMEM) for a in near]
    kept = jax.ShapeDtypeStruct((ROWS, width), BF16)

    def kernel(*refs):
        body(*refs[: 1 + len(near)], *refs[1 + len(near) + len(carry) + len(after) :])

    return pl.pallas_call(
        kernel,
        out_shape=(
            jax.ShapeDtypeStruct((ROWS, out_cols), BF16), kept, kept, pltpu.VMEM((8, HD), F32)
        ),
        in_specs=[smem] + [vmem] * len(near) + [hbm] * (len(carry) + len(after)),
        out_specs=(hbm, hbm, hbm, vmem),
        scratch_shapes=[
            pltpu.VMEM((steps, rows, out_cols // steps), BF16),
            pltpu.SemaphoreType.DMA((steps + 2 * len(grads[0]),)),
        ],
        input_output_aliases={1 + len(near) + i: i for i in range(len(carry))},
        compiler_params=pltpu.CompilerParams(vmem_limit_bytes=LARGE),
        cost_estimate=SLIGHT,
    )(pltpu.with_memory_space_constraint(facts, pltpu.SMEM), *near, *carry, *after)


def flipped(block, axis, bit):
    count = lax.axis_size(axis)
    return lax.ppermute(block, axis, [(i, i ^ bit) for i in range(count) if i ^ bit < count])


def spanning(leaves, bit_index):
    return len([j for j in range(INNER) if 2 << bit_index <= leaves >> j])


def gather_small_tree(facts, own, beside_pair, beside_half):
    two = (own.shape, BF16, True)
    page = (own.shape[1:], BF16, True)
    from_core = flipped(own, "sub", 1)

    def choose_chip(facts, own_ref, far_ref, out):
        for kind in range(2):
            for mine in range(2):

                @pl.when((facts[LEADS] != kind) & (facts[OWNS2] != mine))
                def _copy(kind=kind, mine=mine):
                    out[...] = (own_ref if mine else far_ref)[kind]

    (chip,) = kernel_call(choose_chip, facts, [own, from_core], [], [page])
    from_pair = flipped(chip, "leaf", 1)

    def choose_pair(facts, near_ref, far_ref, out):
        out[...] = jnp.where(facts[ROOT_IN_CHIP] == 1, near_ref[...], far_ref[...])

    after = beside_pair(from_core, chip)
    (pair,) = kernel_call(choose_pair, facts, [chip, from_pair], [], [page], after=after)
    from_half = flipped(pair, "leaf", 2)

    def choose_all(facts, chip_ref, pair_far, pair_ref, half_far, out):
        out[0] = jnp.where(facts[ROOT_IN_PAIR] == 1, pair_ref[...], half_far[...])
        out[1] = jnp.where(facts[NEXT_IN_CHIP] == 1, chip_ref[...], pair_far[...])

    after = beside_half(pair)
    (mine,) = kernel_call(
        choose_all, facts, [chip, from_pair, pair, from_half], [], [two], after=after
    )
    return mine, flipped(mine, "sub", 1)


def over_cores(facts, kept, sent):
    width = kept.shape[-1]

    def body(_, near, away, total, root, next_one):
        for j, low in enumerate((root, next_one)):
            value = near[j] + away[j].astype(F32)
            total[j] = value
            low[...] = value.astype(BF16)

    page = ((PAGE, width), BF16, True)
    total, root, next_one = kernel_call(
        body, facts, [kept, flipped(sent, "sub", 1)], [],
        [((2, PAGE, width), F32, True), page, page],
    )
    return total, root, flipped(root, "leaf", 2), flipped(next_one, "leaf", 1)


def over_halves(facts, total, root_far, next_far, after):
    width = total.shape[-1]

    def body(_, near, root_r, next_r, out, low):
        root = near[0] + root_r[...].astype(F32)
        out[0] = root
        low[...] = root.astype(BF16)
        out[1] = near[1] + next_r[...].astype(F32)

    total, low = kernel_call(
        body, facts, [total, root_far, next_far], [],
        [((2, PAGE, width), F32, True), ((PAGE, width), BF16, True)], after=after,
    )
    return total, low, flipped(low, "leaf", 1)


def over_chips(facts, total, far, passenger, after):
    width = total.shape[-1]
    more = passenger.shape[-1]

    def body(facts, near, away, extra, out):
        root = near[0] + away[...].astype(F32)
        out[:, :width] = jnp.where(facts[ROOT_IN_CHIP] == 1, root, near[1]).astype(BF16)
        for kind in range(2):
            out[:, width + kind * more : width + (kind + 1) * more] = extra[kind]

    outs = [((PAGE, width + 2 * more), BF16, True)]
    (mine,) = kernel_call(
        body, facts, [total, far, passenger], [], outs, after=after
    )
    return mine, flipped(mine, "sub", 1)


def finish_small_tree(facts, own0, mine, far, level2_far):
    width = sum(a.shape[-1] for a in own0)

    def body(facts, own_r, own_last, mine_r, far_r, low_r, dk, dv):
        owns2, leads = facts[OWNS2] == 1, facts[LEADS] == 1
        ok = row_ok(facts[N0], PAGE, HD)
        for at in range(0, width, HD):
            c = slice(at, at + HD)
            last = at + HD == width
            near, away = mine_r[:, c], far_r[:, c]
            gained = [jnp.where(leads, near, away), jnp.where(leads, away, near)]
            for kind, out in enumerate((dk, dv)):
                if last:
                    level2 = far_r[:, width + kind * HD : width + (kind + 1) * HD]
                else:
                    level2 = low_r[kind, :, c]
                more = jnp.where(owns2, level2, gained[kind]).astype(F32)
                base = own_last[kind] if last else own_r[kind, :, c]
                out[:, c] = jnp.where(ok, base + more, 0.0).astype(BF16)

    page = ((PAGE, width), BF16, True)
    return kernel_call(
        body, facts, [*own0, mine, far, level2_far], [], [page, page]
    )


def gather_tree(ids, own):
    leaves = lax.axis_size(("leaf", "sub"))
    owned = ids[:INNER] == ids[INNER] - 1
    pages = jnp.where(owned[:, None, None, None], own[None], jnp.zeros((), BF16))
    for bit in range(leaves.bit_length() - 1):
        active = spanning(leaves, bit)
        far = flipped(pages[:active], ("leaf", "sub"), 1 << bit)
        pages = jnp.concatenate([pages[:active] + far, pages[active:]])
    return pages


def reduce_tree(ids, parts):
    leaves = lax.axis_size(("leaf", "sub"))
    for bit in range(leaves.bit_length() - 1):
        active = spanning(leaves, bit)
        far = flipped(parts[:active], ("leaf", "sub"), 1 << bit)
        parts = jnp.concatenate([parts[:active] + far, parts[active:]])
    owned = ids[:INNER] == ids[INNER] - 1
    return jnp.sum(jnp.where(owned[:, None, None, None], parts, 0.0), axis=0)


def on_device(queries, grad_out, keys, values, log_norms, row_deltas, ancestors, counts, w_value):
    kv = keys.shape[1] // HD
    group = queries.shape[1] // keys.shape[1]
    leaves = lax.axis_size(("leaf", "sub"))
    hbm = lambda a: pltpu.with_memory_space_constraint(a, pltpu.HBM)
    side = lax.axis_index("tensor").astype(I32).reshape(1)
    two_sides = lax.axis_size("tensor") == 2
    inputs = [hbm(a) for a in (queries, grad_out, keys, values, log_norms, row_deltas)]
    facts, own = start(side, hbm(ancestors), hbm(counts), *inputs[2:4])
    state = {}

    def own_pages(kvs, pages, prior=(), after=(), w=None):
        return attend(True, kvs, group, facts, inputs, pages, state, prior, after, w)

    def shared_pages(kvs, pages):
        return attend(False, kvs, group, facts, inputs, pages, state)

    def spread(part):
        if two_sides:
            return flipped(part, "tensor", 1)
        return lax.all_gather(part, "tensor", axis=1, tiled=True)

    kvs = tuple(range(kv))
    w = hbm(w_value)
    if leaves == 8 and lax.axis_size("sub") == 2 and kv >= 3 and two_sides:
        level2, results = [], []

        def beside_pair(from_core, chip):
            level2.extend((own, from_core))
            results.append(own_pages(kvs[:1], level2, after=(chip,)))
            return (results[-1][3],)

        def beside_half(pair):
            results.append(own_pages(kvs[1:-1], level2, results[-1], (pair,)))
            return (results[-1][3],)

        shared = gather_small_tree(facts, own, beside_pair, beside_half)
        most = results[-1]
        far_v = [spread(most[1])]
        level2_far = flipped(most[3], "sub", 1)
        kept, sent = shared_pages(kvs, shared)
        total, root, root_far, next_far = over_cores(facts, kept, sent)
        *last, w_near = own_pages(kvs[-1:], level2, after=(root,), w=w)
        both = list(zip(most, last))
        begun = begin_input_grad(facts, w_near, both[1], (far_v[0], level2_far))
        far_v.append(spread(last[1]))
        total, low, far = over_halves(facts, total, root_far, next_far, (begun,))
        made = finish_queries(kvs[:-1], group, facts, shared, state, (low,))
        mine, far = over_chips(facts, total, far, last[3], (made, far_v[1]))
        dk0, dv0 = finish_small_tree(facts, both[2], mine, far, level2_far)
        far_0 = spread(dv0)
        begun_0 = begin_input_grad(facts, w_near, [dv0])
        *grads, _ = end_input_grad(facts, w_near, far_v, begun, both[:2], after=(begun_0,))
        grads = end_input_grad(facts, w_near, [far_0], begun_0, ([dk0], [dv0]), grads)
        return (state["gq"], grads[1], grads[2], grads[0])

    first = lax.axis_index("sub") == 0
    path_ids = ancestors[0]
    pages = gather_tree(path_ids, own)
    dk12, dv12, own0, send2 = own_pages(kvs, (pages[2], pages[2]))
    shared = (
        jnp.where(first, pages[:2, 0], pages[:2, 1]),
        jnp.where(first, pages[:2, 1], pages[:2, 0]),
    )
    kept, sent = shared_pages(kvs, shared)
    finish_queries(kvs, group, facts, shared, state)
    sent = sent.astype(F32)
    upper = jnp.stack([jnp.where(first, kept, sent), jnp.where(first, sent, kept)], axis=1)
    low = send2.astype(F32)
    total = reduce_tree(path_ids, jnp.concatenate([upper, low[None]]))
    total += own0 - jnp.where(path_ids[2] == path_ids[INNER] - 1, low, 0.0)
    has = jnp.any(path_ids[:INNER] == path_ids[INNER] - 1)
    ok = (jnp.arange(PAGE) < jnp.where(has, counts[0, 0], 0))[:, None]
    dk0, dv0 = jnp.where(ok, total, 0.0).astype(BF16)
    if two_sides:
        pair = lambda part: ([part], [spread(part)])
    else:
        pair = lambda part: ([spread(part)], [])
    *grads, _ = input_grad(facts, w, 2 * PAGE, *pair(dv12), ([dk12], [dv12]))
    grads = input_grad(facts, w, PAGE, *pair(dv0), ([dk0], [dv0]), grads)
    return (state["gq"], grads[1], grads[2], grads[0])


def solution(mesh):
    placed = (
        P(("groups", "leaf", "sub"), "tensor"),
        P(("groups", "leaf", "sub"), "tensor"),
        P(("groups", "leaf", "sub"), "tensor"),
        P(("groups", "leaf", "sub"), "tensor"),
        P("tensor", ("groups", "leaf", "sub")),
        P("tensor", ("groups", "leaf", "sub")),
        P(("groups", "leaf", "sub"), None),
        P(("groups", "leaf", "sub"), None),
        P("tensor", None),
    )
    return jax.shard_map(
        on_device,
        mesh=mesh,
        in_specs=placed,
        out_specs=(
            P(("groups", "leaf", "sub"), "tensor"),
            P(("groups", "leaf", "sub"), "tensor"),
            P(("groups", "leaf", "sub"), "tensor"),
            P(("groups", "leaf", "sub"), "tensor"),
        ),
        check_vma=False,
    )
```

```python
import math

import jax
import jax.numpy as jnp
from jax import lax
from jax.experimental import pallas as pl
from jax.experimental.pallas import tpu as pltpu
from jax.sharding import PartitionSpec as P

HD = 128
PAGE = 128
SLOTS = 3
INNER = 3
ROWS = SLOTS * PAGE
LOG2E = math.log2(math.e)
SCALE = 1.0 / math.sqrt(HD)
BF16 = jnp.bfloat16
F32 = jnp.float32
I32 = jnp.int32
LARGE = 10 << 20
SMALL = 4 << 20
SLIGHT = pl.CostEstimate(flops=1000, bytes_accessed=1000, transcendentals=0)
BLOCKED = 1e30


def dot_t(left, right):
    return lax.dot_general(left, right, (((1,), (1,)), ((), ())), preferred_element_type=F32)


def dot_n(left, right):
    return lax.dot_general(left, right, (((1,), (0,)), ((), ())), preferred_element_type=F32)


FACTS = 16
N0, N1, N2, OWNS2, LIMIT, LEADS, ROOT_IN_CHIP, ROOT_IN_PAIR, NEXT_IN_CHIP, SIDE, SWAP = range(11)


class Order:
    def __init__(self, crossed, heads):
        self.crossed, self.heads = crossed, heads
        self.half = heads // 2 if crossed else heads

    def at(self, facts, head, unit):
        if not self.crossed:
            return head * unit
        step = ((head ^ self.half) - head) * unit
        return pl.multiple_of(facts[SWAP] * step + head * unit, unit)

    def runs(self, first, last):
        cuts = [first, *(h for h in range(first + 1, last) if h % self.half == 0), last]
        return list(zip(cuts[:-1], cuts[1:]))

    def real(self, facts, rows):
        if not self.crossed:
            return rows
        width = self.half * HD
        turned = jnp.concatenate([rows[:, width:], rows[:, :width]], axis=1)
        return jnp.where(facts[SWAP] == 1, turned, rows)


def write_facts(facts, ids, counts, side, order):
    page = [ids[0, j] for j in range(INNER + 1)]
    own = page[INNER] - 1
    leaf = own // SLOTS
    owns = [page[j] == own for j in range(INNER)]
    same = lambda level, shift: ((page[level] // SLOTS) >> shift) == (leaf >> shift)
    number = lambda flag: jnp.where(flag, 1, 0)
    facts[N0] = jnp.where(owns[0] | owns[1] | owns[2], counts[0, 0], 0)
    facts[N1] = counts[0, 1]
    facts[N2] = counts[0, 2]
    facts[OWNS2] = number(owns[2])
    facts[LIMIT] = jnp.where(owns[2], 2 * PAGE, jnp.where(owns[1], PAGE, 0))
    facts[LEADS] = number(lax.rem(leaf, 2) == 0)
    facts[ROOT_IN_CHIP] = number(same(0, 1))
    facts[ROOT_IN_PAIR] = number(same(0, 2))
    facts[NEXT_IN_CHIP] = number(same(1, 1))
    facts[SIDE] = side
    facts[SWAP] = lax.rem(leaf, 2) if order.crossed else 0
    for i in range(SWAP + 1, FACTS):
        facts[i] = 0


def row_ok(count, rows, width):
    return lax.broadcasted_iota(I32, (rows, width), 0) < count


def kernel_call(body, facts, near, far, outs, scratch=(), aliases=None, after=(), cost=None,
                limit=SMALL):
    smem = pl.BlockSpec(memory_space=pltpu.SMEM)
    vmem = pl.BlockSpec(memory_space=pltpu.VMEM)
    hbm = pl.BlockSpec(memory_space=pl.ANY)
    near = [pltpu.with_memory_space_constraint(a, pltpu.VMEM) for a in near]
    place = {("near", i): 1 + i for i in range(len(near))}
    place |= {("far", i): 1 + len(near) + i for i in range(len(far))}
    used = 1 + len(near) + len(far)

    def kernel(*refs):
        body(*refs[:used], *refs[used + len(after) :])

    return pl.pallas_call(
        kernel,
        out_shape=tuple(
            pltpu.VMEM(s, d) if inside else jax.ShapeDtypeStruct(s, d) for s, d, inside in outs
        ),
        in_specs=[smem] + [vmem] * len(near) + [hbm] * (len(far) + len(after)),
        out_specs=tuple(vmem if inside else hbm for _, _, inside in outs),
        scratch_shapes=list(scratch),
        input_output_aliases={place[k]: v for k, v in (aliases or {}).items()},
        compiler_params=pltpu.CompilerParams(vmem_limit_bytes=limit),
        cost_estimate=cost or SLIGHT,
    )(pltpu.with_memory_space_constraint(facts, pltpu.SMEM), *near, *far, *after)


def start(order, side, ids, counts, keys, values):
    width = keys.shape[1]

    def body(side_ref, ids_ref, counts_ref, k_ref, v_ref, facts, out, held, ids_s, counts_s, sem):
        copies = [
            pltpu.make_async_copy(src, dst, sem.at[i])
            for i, (src, dst) in enumerate(
                (
                    (ids_ref, ids_s),
                    (counts_ref, counts_s),
                    (k_ref.at[:PAGE], held.at[0]),
                    (v_ref.at[:PAGE], held.at[1]),
                )
            )
        ]
        for c in copies:
            c.start()
        copies[0].wait()
        copies[1].wait()
        write_facts(facts, ids_s, counts_s, side_ref[0], order)
        ok = row_ok(counts_s[0, 0], PAGE, width)
        for i in range(2):
            copies[2 + i].wait()
            out[i] = jnp.where(ok, held[i], jnp.zeros((), BF16))

    smem = pl.BlockSpec(memory_space=pltpu.SMEM)
    hbm = pl.BlockSpec(memory_space=pl.ANY)
    return pl.pallas_call(
        body,
        out_shape=(pltpu.SMEM((FACTS,), I32), pltpu.VMEM((2, PAGE, width), BF16)),
        in_specs=[smem] + [hbm] * 4,
        out_specs=(smem, pl.BlockSpec(memory_space=pltpu.VMEM)),
        scratch_shapes=[
            pltpu.VMEM((2, PAGE, width), BF16),
            pltpu.SMEM(ids.shape, I32),
            pltpu.SMEM(counts.shape, I32),
            pltpu.SemaphoreType.DMA((4,)),
        ],
        compiler_params=pltpu.CompilerParams(vmem_limit_bytes=SMALL),
    )(side, ids, counts, keys, values)


def row_terms(rows):
    high = rows.astype(BF16).astype(F32)
    rest = rows - high
    middle = rest.astype(BF16).astype(F32)
    parts = [high, middle, rest - middle]
    spare = HD - 3 * rows.shape[0]
    parts.append(jnp.zeros((spare, rows.shape[1]), F32))
    return jnp.concatenate(parts, axis=0).T.astype(BF16)


class Head:
    def __init__(self, kv, group, norms, deltas, en, ed):
        self.group = group
        self.heads = min(4, group)
        self.parts = group // self.heads
        self.tall = self.heads * PAGE
        heads = slice(kv * group, (kv + 1) * group)
        en[...] = row_terms(norms[heads, :])
        ed[...] = row_terms(deltas[heads, :])

    def lanes(self, part, j):
        at = (part * self.heads + j) * HD
        return slice(at, at + HD)

    def stacked(self, ref, part, slots):
        return jnp.concatenate(
            [
                ref[slot * PAGE : (slot + 1) * PAGE, self.lanes(part, j)]
                for slot in slots
                for j in range(self.heads)
            ],
            axis=0,
        )

    def deep(self, stacked, terms, part, slots):
        column = lax.broadcasted_iota(I32, (1, HD), 1) % self.group
        picks = [
            (column == part * self.heads + j).astype(F32).astype(BF16)
            for j in range(self.heads)
        ]
        extra = [
            terms[slot * PAGE : (slot + 1) * PAGE] * pick for slot in slots for pick in picks
        ]
        return jnp.concatenate([stacked, jnp.concatenate(extra, axis=0)], axis=1)

    def turned_at(self, part, slot, count):
        at = (part * SLOTS + slot) * self.tall
        return slice(at, at + self.tall * count)

    def put_queries(self, part, slot, rows_by_head, dq, add, stage):
        rows = slice(slot * PAGE, (slot + 1) * PAGE)
        for j in range(self.heads):
            value = rows_by_head[j * PAGE : (j + 1) * PAGE]
            if stage is None:
                dq[rows, self.lanes(part, j)] = value
            else:
                if add:
                    value = value + dq[rows, self.lanes(part, j)]
                stage[rows, j * HD : (j + 1) * HD] = (value * SCALE).astype(BF16)


def set_keys(deep, upright, at, page):
    where = slice(at * PAGE, (at + 1) * PAGE)
    deep[:HD, where] = page.T
    if upright is not None:
        upright[where] = page


def weigh(scores, grads, keep):
    p = keep(jnp.exp2(scores * (SCALE * LOG2E)))
    return p.astype(BF16), (p * grads).astype(BF16)


def attend(own, kvs, group, order, facts, inputs, pages, state, prior=(), after=(), w=None,
           ride=None):
    loading = "k" not in state
    q_all, k_all = inputs[0], inputs[2]
    count = len(kvs)
    parts = group // min(4, group)
    tall = min(4, group) * PAGE
    wide = min(4, group) * HD
    width = count * HD
    base = prior[0].shape[1] if prior else 0
    kv_total = k_all.shape[1] // HD
    fresh = [("dq", kv) not in state for kv in kvs]
    one_head = (ROWS, group * HD)
    turned = ((HD, group * ROWS), BF16, True)
    shapes = {"dq": (one_head, F32, True), "qt": turned, "gt": turned}

    near, far, aliases, outs = [], [], {}, []
    at_near, at_far, at_out = {}, {}, {}

    def add_near(name, array):
        at_near[name] = len(near)
        near.append(array)

    def add_far(name, array):
        at_far[name] = len(far)
        far.append(array)

    def add_out(name, out):
        at_out[name] = len(outs)
        outs.append(out)

    for kv, is_fresh in zip(kvs, fresh):
        for name, shape in shapes.items():
            if is_fresh:
                add_out((name, kv), shape)
            elif own or name != "dq":
                add_near((name, kv), state[name, kv])
        if not own and not is_fresh:
            add_out(("ds", kv), ((group * ROWS, 2 * PAGE), BF16, True))
    if own and not all(fresh):
        add_out("gq", (q_all.shape, BF16, False))
        if "gq" in state:
            add_far("gq", state["gq"])
            aliases["far", at_far["gq"]] = at_out["gq"]
    at_results = len(outs)
    if own:
        outs += [
            ((2 * PAGE, base + width), BF16, True),
            ((2 * PAGE, base + width), BF16, True),
            ((2, PAGE, base + width), F32, True),
            ((2, PAGE, base + width), BF16, True),
        ]
    else:
        outs += [
            ((4, PAGE, width), F32, True) if ride is None else ((7, PAGE, width), BF16, True),
        ]
    at_loaded = len(outs)
    if loading:
        for name, array in zip(("q", "g", "k", "v", "norms", "deltas"), inputs):
            add_far(name, array)
            if name in ("q", "g"):
                for kv in range(kv_total):
                    add_out((name, kv), (one_head, BF16, True))
            else:
                add_out(name, (array.shape, array.dtype, True))
    else:
        for name in ("k", "v", "norms", "deltas"):
            add_near(name, state[name])
        for kv in kvs:
            for name in ("q", "g"):
                add_near((name, kv), state[name, kv])
    at_end = len(outs)
    if w is not None:
        add_far("w", w)
        outs.append((w.shape, w.dtype, True))
    for i, page in enumerate(pages):
        add_near(("page", i), page)
    for i, array in enumerate(prior):
        add_near(("prior", i), array)
    if ride is not None:
        add_near("ride", ride)
    key_pages = 4 if own else 2
    scratch = [
        pltpu.VMEM((2 * HD, key_pages * PAGE), BF16),
        pltpu.VMEM((2 * HD, key_pages * PAGE), BF16),
        pltpu.VMEM((key_pages * PAGE, HD), BF16),
        pltpu.VMEM((2, HD, key_pages * PAGE), F32),
        pltpu.VMEM((ROWS, HD), BF16),
        pltpu.VMEM((ROWS, HD), BF16),
        pltpu.VMEM((count * parts, ROWS, wide), BF16),
        pltpu.SemaphoreType.DMA((count * parts,)),
        pltpu.SemaphoreType.DMA((2 * kv_total + 9,)),
    ]
    cols = lambda a, b: slice(a * PAGE, b * PAGE)

    def body(facts, *refs):
        ins, out_refs = refs[: len(near) + len(far)], refs[len(near) + len(far) : -len(scratch)]
        k_deep, v_deep, k_up, acc, en, ed, stage, sem, load_sem = refs[-len(scratch) :]
        near_ref = lambda name: ins[at_near[name]]
        far_ref = lambda name: ins[len(near) + at_far[name]]
        held = lambda name: out_refs[at_out[name]] if name in at_out else near_ref(name)
        results = out_refs[at_results:at_loaded]
        copies = {}
        if loading:

            def load(key, src, dst):
                copies[key] = pltpu.make_async_copy(src, dst, load_sem.at[len(copies)])
                copies[key].start()

            for lo, hi in order.runs(0, kv_total):
                for name in ("k", "v"):
                    at = pl.ds(order.at(facts, lo, HD), (hi - lo) * HD)
                    here = slice(lo * HD, hi * HD)
                    load((name, lo), far_ref(name).at[:, at], held(name).at[:, here])
                for name in ("norms", "deltas"):
                    at = pl.ds(order.at(facts, lo, group), (hi - lo) * group)
                    here = slice(lo * group, hi * group)
                    load((name, lo), far_ref(name).at[at], held(name).at[here])
            shared_loads = list(copies)
            for kv in range(kv_total):
                at = pl.ds(order.at(facts, kv, group * HD), group * HD)
                for name in ("q", "g"):
                    load((name, kv), far_ref(name).at[:, at], held((name, kv)))
        if w is not None:
            w_copy = pltpu.make_async_copy(
                far_ref("w"), out_refs[at_end], load_sem.at[2 * kv_total + 8]
            )
            w_copy.start()
        k, v, norms, deltas = (held(name) for name in ("k", "v", "norms", "deltas"))

        def arrived(*keys):
            for key in keys:
                if key in copies:
                    copies.pop(key).wait()

        k_deep[HD:] = jnp.full((HD, key_pages * PAGE), -1.0, BF16)
        v_deep[HD:] = jnp.full((HD, key_pages * PAGE), -1.0, BF16)
        for out, i in zip(results, range(len(prior))):
            out[..., :base] = near_ref(("prior", i))[...]
        if ride is not None:
            (out,), more = results, near_ref("ride")
            for kind in range(2):
                out[4 + kind] = more[kind, :, :width]
                spare = slice(kind * HD, (kind + 1) * HD)
                out[6, :, spare] = more[kind, :, width:]
        owns2 = facts[OWNS2] == 1
        if loading:
            arrived(*shared_loads)
            lane = lax.broadcasted_iota(I32, norms.shape, 1)
            limit = jnp.where(
                lane < PAGE, facts[N0], jnp.where(lane < 2 * PAGE, facts[N1], facts[N2])
            )
            norms[...] = jnp.where(lane % PAGE < limit, norms[...] * (1.0 / SCALE), BLOCKED)
        lower = lambda rows: lax.broadcasted_iota(I32, (rows, PAGE), 1) <= (
            lax.broadcasted_iota(I32, (rows, PAGE), 0) % PAGE
        )

        def set_pages(n, kv):
            lane = slice(kv * HD, (kv + 1) * HD)
            if own:
                first, second = (near_ref(("page", i)) for i in range(2))
                zero = jnp.zeros((), BF16)
                for slot, (at, c) in enumerate(((3, N0), (0, N1), (2, N2))):
                    ok = row_ok(facts[c], PAGE, HD)
                    rows = cols(slot, slot + 1)
                    set_keys(k_deep, k_up, at, jnp.where(ok, k[rows, lane], zero))
                    set_keys(v_deep, None, at, jnp.where(ok, v[rows, lane], zero))
                level2 = [jnp.where(owns2, first[i, :, lane], second[i, :, lane]) for i in (0, 1)]
                if order.crossed:
                    at = (kv ^ order.half) * HD
                    lane = slice(at, at + HD)
                    for i in range(2):
                        other = jnp.where(owns2, first[i, :, lane], second[i, :, lane])
                        level2[i] = jnp.where(facts[SWAP] == 1, other, level2[i])
                set_keys(k_deep, k_up, 1, level2[0])
                set_keys(v_deep, None, 1, level2[1])
            else:
                page = near_ref(("page", 0))
                for j in range(2):
                    here = slice(n * HD, (n + 1) * HD)
                    set_keys(k_deep, k_up, j, page[j, 0, :, here])
                    set_keys(v_deep, None, j, page[j, 1, :, here])
            acc[...] = jnp.zeros_like(acc)

        def turned_rows(head, kv, part, is_fresh, qs, gs, order):
            if is_fresh:
                for name, rows in (("qt", qs), ("gt", gs)):
                    for i, slot in enumerate(order):
                        held((name, kv))[:, head.turned_at(part, slot, 1)] = rows[
                            i * tall : (i + 1) * tall
                        ].T
            return lambda name, slot, slots: held((name, kv))[
                :, head.turned_at(part, slot, slots)
            ]

        def own_part(head, kv, part, n, stage_ref):
            order = (1, 2, 0)
            qs = head.stacked(held(("q", kv)), part, order)
            gs = head.stacked(held(("g", kv)), part, order)
            qd, gd = head.deep(qs, en, part, order), head.deep(gs, ed, part, order)
            turn = turned_rows(head, kv, part, fresh[n], qs, gs, order)
            low = lower(tall)

            def keep_first(p):
                masked = jnp.where(low, p[:tall, :PAGE], 0.0)
                return jnp.concatenate(
                    [jnp.concatenate([masked, p[:tall, PAGE:]], axis=1), p[tall:]], axis=0
                )

            pa, da = weigh(
                dot_n(qd[: 2 * tall], k_deep[:, : 2 * PAGE]),
                dot_n(gd[: 2 * tall], v_deep[:, : 2 * PAGE]),
                keep_first,
            )
            both = lambda x: jnp.concatenate([x[:tall, :PAGE], x[tall:, PAGE:]], axis=0)
            low2 = lower(2 * tall)
            pb, db = weigh(
                both(dot_n(qd[tall:], k_deep[:, 2 * PAGE :])),
                both(dot_n(gd[tall:], v_deep[:, 2 * PAGE :])),
                lambda p: jnp.where(low2, p, 0.0),
            )
            for i, (name, a, b) in enumerate((("qt", da, db), ("gt", pa, pb))):
                acc[i, :, : 2 * PAGE] += dot_n(turn(name, 1, 2), a)
                acc[i, :, cols(2, 3)] += dot_n(turn(name, 2, 1), b[:tall])
                acc[i, :, cols(3, 4)] += dot_n(turn(name, 0, 1), b[tall:])
            first = dot_n(da, k_up[: 2 * PAGE])
            put = lambda slot, rows: head.put_queries(
                part, slot, rows, held(("dq", kv)), not fresh[n], stage_ref
            )
            put(1, first[:tall])
            put(2, first[tall:] + dot_n(db[:tall], k_up[cols(2, 3)]))
            put(0, dot_n(db[tall:], k_up[cols(3, 4)]))

        def shared_part(head, kv, part, n, stage_ref):
            order = (0, 1, 2)
            qs = head.stacked(held(("q", kv)), part, order)
            gs = head.stacked(held(("g", kv)), part, order)
            qd, gd = head.deep(qs, en, part, order), head.deep(gs, ed, part, order)
            turn = turned_rows(head, kv, part, fresh[n], qs, gs, order)
            column = lax.broadcasted_iota(I32, (tall, 2 * PAGE), 1)
            seen = column < facts[LIMIT]

            def keep(p):
                return jnp.concatenate([jnp.where(seen, p[:tall], 0.0), p[tall:]], axis=0)

            p, ds = weigh(dot_n(qd, k_deep[...]), dot_n(gd, v_deep[...]), keep)
            acc[0] += dot_n(turn("qt", 0, SLOTS), ds)
            acc[1] += dot_n(turn("gt", 0, SLOTS), p)
            if not fresh[n]:
                held(("ds", kv))[part * SLOTS * tall : (part + 1) * SLOTS * tall] = ds
                return
            dq = dot_n(ds, k_up[...])
            for slot in range(SLOTS):
                head.put_queries(
                    part, slot, dq[slot * tall : (slot + 1) * tall], held(("dq", kv)), not fresh[n],
                    stage_ref,
                )

        def put_own(n):
            dk12, dv12, own0, send2 = results
            here = slice(base + n * HD, base + (n + 1) * HD)
            grad = [acc[0].T * SCALE, acc[1].T]
            for at, c, to in ((0, N1, 0), (2, N2, 1)):
                ok = row_ok(facts[c], PAGE, HD)
                for kind, out in ((0, dk12), (1, dv12)):
                    out[cols(to, to + 1), here] = jnp.where(
                        ok, grad[kind][cols(at, at + 1)], 0.0
                    ).astype(BF16)
            for kind in range(2):
                level2 = grad[kind][cols(1, 2)]
                own0[kind, :, here] = grad[kind][cols(3, 4)] + jnp.where(owns2, level2, 0.0)
                send2[kind, :, here] = level2.astype(BF16)

        def put_shared(n):
            (out,) = results
            here = slice(n * HD, (n + 1) * HD)
            grads = acc[0].T * SCALE, acc[1].T
            for j in range(2):
                for kind in range(2):
                    out[2 * j + kind, :, here] = grads[kind][cols(j, j + 1)].astype(out.dtype)

        sends = []
        for n, kv in enumerate(kvs):
            arrived(("q", kv), ("g", kv))
            head = Head(kv, group, norms, deltas, en, ed)
            set_pages(n, kv)

            for part in range(parts):
                slot = n * parts + part
                (own_part if own else shared_part)(
                    head, kv, part, n, stage.at[slot] if own and not fresh[n] else None
                )
                if own and not fresh[n]:
                    at = order.at(facts, kv, group * HD) + part * wide
                    sends.append(
                        pltpu.make_async_copy(
                            stage.at[slot],
                            held("gq").at[:, pl.ds(pl.multiple_of(at, wide), wide)],
                            sem.at[slot],
                        )
                    )
                    sends[-1].start()

            (put_own if own else put_shared)(n)
        for c in sends:
            c.wait()
        arrived(*list(copies))
        if w is not None:
            w_copy.wait()

    made = kernel_call(
        body, facts, near, far, outs, scratch, aliases, after,
        pl.CostEstimate(
            flops=240 * PAGE * PAGE * HD * group * count, bytes_accessed=1000, transcendentals=0
        ),
        LARGE,
    )
    for name, at in at_out.items():
        state[name] = made[at]
    return list(made[at_results:at_loaded]) + list(made[at_end:])


def width_tiles(w, sizes=(512, 640, 320, 128)):
    tile = next(t for t in (*sizes, w.shape[0]) if w.shape[0] % t == 0)
    return [slice(i, i + tile) for i in range(0, w.shape[0], tile)]


def finish_queries(kvs, group, order, facts, pages, state, after=()):
    parts = group // min(4, group)
    heads = group // parts
    tall = heads * PAGE
    wide = heads * HD
    near = list(pages)
    for kv in kvs:
        near += [state["ds", kv], state["dq", kv]]

    def body(facts, *refs):
        gq, made, stage, sem = refs[-4:]
        made[...] = jnp.zeros_like(made)
        sends = []
        for n, kv in enumerate(kvs):
            ds, dq = refs[len(pages) + 2 * n : len(pages) + 2 * n + 2]
            page, at = refs[kv // order.half], kv % order.half * HD
            keys = jnp.concatenate([page[j, 0, :, at : at + HD] for j in range(2)], axis=0)
            for part in range(parts):
                at = n * parts + part
                gained = dot_n(ds[part * SLOTS * tall : (part + 1) * SLOTS * tall], keys)
                for i in range(SLOTS * heads):
                    slot, j = divmod(i, heads)
                    rows = slice(slot * PAGE, (slot + 1) * PAGE)
                    value = gained[i * PAGE : (i + 1) * PAGE] + dq[
                        rows, part * wide + j * HD : part * wide + (j + 1) * HD
                    ]
                    stage[at, rows, j * HD : (j + 1) * HD] = (value * SCALE).astype(BF16)
                to = pl.multiple_of(order.at(facts, kv, group * HD) + part * wide, wide)
                sends.append(
                    pltpu.make_async_copy(stage.at[at], gq.at[:, pl.ds(to, wide)], sem.at[at])
                )
                sends[-1].start()
        for c in sends:
            c.wait()

    count = len(kvs) * parts
    far = [state["gq"]] if "gq" in state else []
    shape = (ROWS, state["k"].shape[1] * group)
    state["gq"], made = kernel_call(
        body, facts, near, far, [(shape, BF16, False), ((8, HD), F32, True)],
        [pltpu.VMEM((count, ROWS, wide), BF16), pltpu.SemaphoreType.DMA((count,))],
        {("far", 0): 0} if far else {}, after, limit=LARGE,
    )
    return made


def input_grad(order, facts, w, rows, own, far, grads, carry=None):
    out_cols, depth = w.shape
    tiles = width_tiles(w)
    top = 0 if rows == PAGE else PAGE
    steps = len(tiles)
    width = sum(a.shape[1] for a in grads[0])
    arrays = [*own, *far, *grads[0], *grads[1]]
    count = len(grads[0])
    carry = list(carry or [])

    def body(facts, *refs):
        own_r, refs = refs[: len(own)], refs[len(own) :]
        far_r, refs = refs[: len(far)], refs[len(far) :]
        grad_r, w_ref = refs[: 2 * count], refs[2 * count]
        out, dk, dv, made, w_near, stage, w_sem, sem = refs[-8:]
        loads = [
            pltpu.make_async_copy(w_ref.at[at], w_near.at[at], w_sem.at[i])
            for i, at in enumerate(tiles)
        ]
        for c in loads:
            c.start()
        made[...] = jnp.zeros_like(made)
        columns = lambda rs: jnp.concatenate([r[...] for r in rs], axis=1)
        full = columns(own_r)
        if far:
            other, leads = columns(far_r), facts[SIDE] == 0
            full = jnp.concatenate(
                [jnp.where(leads, full, other), jnp.where(leads, other, full)], axis=1
            )
        copies = put_rows(order, facts, grad_r, dk, dv, top, rows, sem, steps)
        for i, at in enumerate(tiles):
            loads[i].wait()
            stage[i] = dot_t(w_near[at], full).astype(BF16).T
            copies.append(
                pltpu.make_async_copy(stage.at[i], out.at[top : top + rows, at], sem.at[i])
            )
            copies[-1].start()
        for c in copies:
            c.wait()

    smem = pl.BlockSpec(memory_space=pltpu.SMEM)
    vmem = pl.BlockSpec(memory_space=pltpu.VMEM)
    hbm = pl.BlockSpec(memory_space=pl.ANY)
    arrays = [pltpu.with_memory_space_constraint(a, pltpu.VMEM) for a in arrays]
    kept = jax.ShapeDtypeStruct((ROWS, width), BF16)
    return pl.pallas_call(
        body,
        out_shape=(
            jax.ShapeDtypeStruct((ROWS, out_cols), BF16), kept, kept, pltpu.VMEM((8, HD), F32)
        ),
        in_specs=[smem] + [vmem] * len(arrays) + [hbm] * (1 + len(carry)),
        out_specs=(hbm, hbm, hbm, vmem),
        scratch_shapes=[
            pltpu.VMEM(w.shape, BF16),
            pltpu.VMEM((steps, rows, out_cols // steps), BF16),
            pltpu.SemaphoreType.DMA((steps,)),
            pltpu.SemaphoreType.DMA((steps + 2 * order.heads,)),
        ],
        input_output_aliases={2 + len(arrays) + i: i for i in range(len(carry))},
        compiler_params=pltpu.CompilerParams(vmem_limit_bytes=LARGE),
        cost_estimate=SLIGHT,
    )(pltpu.with_memory_space_constraint(facts, pltpu.SMEM), *arrays, w, *carry)


def put_rows(order, facts, pieces, dk, dv, top, rows, sem, first):
    copies = []
    count = len(pieces) // 2
    for dst, mine in ((dk, pieces[:count]), (dv, pieces[count:])):
        head = 0
        for src in mine:
            more = src.shape[1] // HD
            for lo, hi in order.runs(head, head + more):
                copies.append(
                    pltpu.make_async_copy(
                        src.at[:, (lo - head) * HD : (hi - head) * HD],
                        dst.at[top : top + rows, pl.ds(order.at(facts, lo, HD), (hi - lo) * HD)],
                        sem.at[first + len(copies)],
                    )
                )
                copies[-1].start()
            head += more
    return copies


def begin_input_grad(order, facts, w, own, after=()):
    out_cols, depth = w.shape
    half = depth // 2
    rows = own[0].shape[0]
    count = len(own)

    def body(facts, w_ref, *refs):
        mine, out = jnp.concatenate([r[...] for r in refs[:count]], axis=1), refs[-1]
        mine = order.real(facts, mine)
        where = pl.ds(pl.multiple_of(facts[SIDE] * half, half), half)
        for at in width_tiles(w):
            out[at] = dot_t(w_ref[at, where], mine)

    smem = pl.BlockSpec(memory_space=pltpu.SMEM)
    vmem = pl.BlockSpec(memory_space=pltpu.VMEM)
    near = [pltpu.with_memory_space_constraint(a, pltpu.VMEM) for a in (w, *own)]

    def kernel(*refs):
        body(*refs[: 2 + count], refs[-1])

    return pl.pallas_call(
        kernel,
        out_shape=pltpu.VMEM((out_cols, rows), F32),
        in_specs=[smem] + [vmem] * len(near) + [pl.BlockSpec(memory_space=pl.ANY)] * len(after),
        out_specs=vmem,
        compiler_params=pltpu.CompilerParams(vmem_limit_bytes=LARGE),
        cost_estimate=SLIGHT,
    )(pltpu.with_memory_space_constraint(facts, pltpu.SMEM), *near, *after)


def end_input_grad(order, facts, w, far, begun, grads, carry=None, after=()):
    tiles = width_tiles(w, (1280, 640, 320, 128))
    out_cols, depth = w.shape
    half = depth // 2
    steps = len(tiles)
    rows = far[0].shape[0]
    top = 0 if rows == PAGE else PAGE
    width = sum(a.shape[1] for a in grads[0])
    near = [w, begun, *far, *grads[0], *grads[1]]
    carry = list(carry or [])

    def body(facts, w_r, begun_r, *refs):
        far_r, grad_r = refs[: len(far)], refs[len(far) : len(near) - 2]
        out, dk, dv, made, stage, sem = refs[-6:]
        made[...] = jnp.zeros_like(made)
        copies = put_rows(order, facts, grad_r, dk, dv, top, rows, sem, steps)
        other = order.real(facts, jnp.concatenate([r[...] for r in far_r], axis=1))
        where = pl.ds(pl.multiple_of((1 - facts[SIDE]) * half, half), half)
        for i, at in enumerate(tiles):
            stage[i] = (dot_t(w_r[at, where], other) + begun_r[at]).astype(BF16).T
            copies.append(
                pltpu.make_async_copy(stage.at[i], out.at[top : top + rows, at], sem.at[i])
            )
            copies[-1].start()
        for c in copies:
            c.wait()

    smem = pl.BlockSpec(memory_space=pltpu.SMEM)
    vmem = pl.BlockSpec(memory_space=pltpu.VMEM)
    hbm = pl.BlockSpec(memory_space=pl.ANY)
    near = [pltpu.with_memory_space_constraint(a, pltpu.VMEM) for a in near]
    kept = jax.ShapeDtypeStruct((ROWS, width), BF16)

    def kernel(*refs):
        body(*refs[: 1 + len(near)], *refs[1 + len(near) + len(carry) + len(after) :])

    return pl.pallas_call(
        kernel,
        out_shape=(
            jax.ShapeDtypeStruct((ROWS, out_cols), BF16), kept, kept, pltpu.VMEM((8, HD), F32)
        ),
        in_specs=[smem] + [vmem] * len(near) + [hbm] * (len(carry) + len(after)),
        out_specs=(hbm, hbm, hbm, vmem),
        scratch_shapes=[
            pltpu.VMEM((steps, rows, out_cols // steps), BF16),
            pltpu.SemaphoreType.DMA((steps + 2 * order.heads,)),
        ],
        input_output_aliases={1 + len(near) + i: i for i in range(len(carry))},
        compiler_params=pltpu.CompilerParams(vmem_limit_bytes=LARGE),
        cost_estimate=SLIGHT,
    )(pltpu.with_memory_space_constraint(facts, pltpu.SMEM), *near, *carry, *after)


def flipped(block, axis, bit):
    count = lax.axis_size(axis)
    return lax.ppermute(block, axis, [(i, i ^ bit) for i in range(count) if i ^ bit < count])


def spanning(leaves, bit_index):
    return len([j for j in range(INNER) if 2 << bit_index <= leaves >> j])


def gather_small_tree(facts, own, beside_pair, beside_half):
    width = own.shape[-1] // 2
    page = ((2, PAGE, width), BF16, True)
    from_core = flipped(own, "sub", 1)

    def choose_chip(facts, own_ref, far_ref, out):
        for swap in range(2):
            for mine in range(2):

                @pl.when((facts[SWAP] == swap) & (facts[OWNS2] != mine))
                def _copy(swap=swap, mine=mine):
                    out[...] = (own_ref if mine else far_ref)[
                        :, :, swap * width : (swap + 1) * width
                    ]

    (chip,) = kernel_call(choose_chip, facts, [own, from_core], [], [page])
    from_pair = flipped(chip, "leaf", 1)

    def choose_pair(facts, near_ref, far_ref, out):
        out[...] = jnp.where(facts[ROOT_IN_CHIP] == 1, near_ref[...], far_ref[...])

    after = beside_pair(from_core, chip)
    (pair,) = kernel_call(choose_pair, facts, [chip, from_pair], [], [page], after=after)
    from_half = flipped(pair, "leaf", 2)

    def choose_all(facts, chip_ref, pair_far, pair_ref, half_far, out):
        out[0] = jnp.where(facts[ROOT_IN_PAIR] == 1, pair_ref[...], half_far[...])
        out[1] = jnp.where(facts[NEXT_IN_CHIP] == 1, chip_ref[...], pair_far[...])

    after = beside_half(pair)
    (mine,) = kernel_call(
        choose_all, facts, [chip, from_pair, pair, from_half], [],
        [((2, *page[0]), BF16, True)], after=after,
    )
    return mine, flipped(mine, "sub", 1)


def over_cores(facts, kept, far):
    width = kept.shape[-1]

    def body(_, near, away, total, root, next_one):
        for i in range(4):
            value = near[i] + away[i].astype(F32)
            total[i] = value
            (root, next_one)[i // 2][i % 2] = value.astype(BF16)

    pages = ((2, PAGE, width), BF16, True)
    total, root, next_one = kernel_call(
        body, facts, [kept, far], [], [((4, PAGE, width), F32, True), pages, pages]
    )
    return total, root, flipped(root, "leaf", 2), flipped(next_one, "leaf", 1)


def over_halves(facts, total, root_far, next_far, after):
    width = total.shape[-1]

    def body(_, near, root_r, next_r, out, low):
        root = near[:2] + root_r[...].astype(F32)
        out[:2] = root
        low[...] = root.astype(BF16)
        out[2:] = near[2:] + next_r[...].astype(F32)

    total, low = kernel_call(
        body, facts, [total, root_far, next_far], [],
        [((4, PAGE, width), F32, True), ((2, PAGE, width), BF16, True)], after=after,
    )
    return total, low, flipped(low, "leaf", 1)


def over_chips(facts, total, far, level2, after):
    width = total.shape[-1]

    def body(facts, near, away, extra, out):
        root = near[:2] + away[...].astype(F32)
        out[:, :, :width] = jnp.where(facts[ROOT_IN_CHIP] == 1, root, near[2:]).astype(BF16)
        out[:, :, width:] = extra[:, :, extra.shape[-1] - HD :]

    outs = [((2, PAGE, width + HD), BF16, True)]
    (mine,) = kernel_call(body, facts, [total, far, level2], [], outs, after=after)
    return mine, flipped(mine, "sub", 1)


def finish_small_tree(order, facts, own0, mine, far, level2_far, after):
    width = own0.shape[-1]
    part = order.half * HD

    def body(facts, own_r, mine_r, far_r, low_r, dk, dv):
        owns2 = facts[OWNS2] == 1
        ok = row_ok(facts[N0], PAGE, HD)
        for head in range(order.heads):
            c = slice(head * HD, (head + 1) * HD)
            at = head % order.half * HD
            here = slice(at, at + HD)
            theirs = head ^ order.half
            for kind, out in enumerate((dk, dv)):
                gained = (far_r if head < order.half else mine_r)[kind, :, here]
                if theirs < order.half:
                    level2 = low_r[4 + kind, :, theirs * HD : (theirs + 1) * HD]
                elif theirs + 1 < order.heads:
                    level2 = low_r[6, :, kind * HD : (kind + 1) * HD]
                else:
                    level2 = far_r[kind, :, part : part + HD]
                more = jnp.where(owns2, level2, gained).astype(F32)
                out[:, c] = jnp.where(ok, own_r[kind, :, c] + more, 0.0).astype(BF16)

    page = ((PAGE, width), BF16, True)
    return kernel_call(
        body, facts, [own0, mine, far, level2_far], [], [page, page], after=after
    )


def gather_tree(ids, own):
    leaves = lax.axis_size(("leaf", "sub"))
    owned = ids[:INNER] == ids[INNER] - 1
    pages = jnp.where(owned[:, None, None, None], own[None], jnp.zeros((), BF16))
    for bit in range(leaves.bit_length() - 1):
        active = spanning(leaves, bit)
        far = flipped(pages[:active], ("leaf", "sub"), 1 << bit)
        pages = jnp.concatenate([pages[:active] + far, pages[active:]])
    return pages


def reduce_tree(ids, parts):
    leaves = lax.axis_size(("leaf", "sub"))
    for bit in range(leaves.bit_length() - 1):
        active = spanning(leaves, bit)
        far = flipped(parts[:active], ("leaf", "sub"), 1 << bit)
        parts = jnp.concatenate([parts[:active] + far, parts[active:]])
    owned = ids[:INNER] == ids[INNER] - 1
    return jnp.sum(jnp.where(owned[:, None, None, None], parts, 0.0), axis=0)


def on_device(queries, grad_out, keys, values, log_norms, row_deltas, ancestors, counts, w_value):
    kv = keys.shape[1] // HD
    group = queries.shape[1] // keys.shape[1]
    leaves = lax.axis_size(("leaf", "sub"))
    hbm = lambda a: pltpu.with_memory_space_constraint(a, pltpu.HBM)
    side = lax.axis_index("tensor").astype(I32).reshape(1)
    two_sides = lax.axis_size("tensor") == 2
    inputs = [hbm(a) for a in (queries, grad_out, keys, values, log_norms, row_deltas)]
    fast = leaves == 8 and lax.axis_size("sub") == 2 and kv == 4 and two_sides
    order = Order(fast, kv)
    facts, own = start(order, side, hbm(ancestors), hbm(counts), *inputs[2:4])
    state = {}

    def own_pages(kvs, pages, prior=(), after=(), w=None):
        return attend(
            True, kvs, group, order, facts, inputs, pages, state, prior, after, w
        )

    def shared_pages(kvs, page, ride=None):
        return attend(False, kvs, group, order, facts, inputs, [page], state, ride=ride)[0]

    def spread(part):
        if two_sides:
            return flipped(part, "tensor", 1)
        return lax.all_gather(part, "tensor", axis=1, tiled=True)

    kvs = tuple(range(kv))
    w = hbm(w_value)
    if fast:
        level2, results = [], []

        def beside_pair(from_core, chip):
            level2.extend((own, from_core))
            results.append(own_pages(kvs[:1], level2, after=(chip,)))
            return (results[-1][3],)

        def beside_half(pair):
            results.append(own_pages(kvs[1:3], level2, results[-1], (pair,)))
            return (results[-1][3],)

        mine, theirs = gather_small_tree(facts, own, beside_pair, beside_half)
        sent = flipped(shared_pages(kvs[:2], mine, results[-1][3]), "sub", 1)
        kept = shared_pages(kvs[2:], theirs)
        total, root, root_far, next_far = over_cores(facts, kept, sent)
        dk12, dv12, own0, send2, w_near = own_pages(
            kvs[3:], level2, results[-1], (root,), w
        )
        begun = begin_input_grad(order, facts, w_near, [dv12])
        far_v = spread(dv12)
        total, low, far = over_halves(facts, total, root_far, next_far, (begun,))
        made = finish_queries(kvs[:3], group, order, facts, (mine, theirs), state, (low,))
        near, far = over_chips(facts, total, far, send2, (made,))
        dk0, dv0 = finish_small_tree(order, facts, own0, near, far, sent, (far_v,))
        far_0 = spread(dv0)
        begun_0 = begin_input_grad(order, facts, w_near, [dv0])
        *grads, _ = end_input_grad(
            order, facts, w_near, [far_v], begun, ([dk12], [dv12]), after=(begun_0,)
        )
        grads = end_input_grad(
            order, facts, w_near, [far_0], begun_0, ([dk0], [dv0]), grads
        )
        return (state["gq"], grads[1], grads[2], grads[0])

    path_ids = ancestors[0]
    pages = gather_tree(path_ids, own)
    dk12, dv12, own0, send2 = own_pages(kvs, (pages[2], pages[2]))
    grads = shared_pages(kvs, pages[:2])
    finish_queries(kvs, group, order, facts, (pages[:2],), state)
    low = send2.astype(F32)
    total = reduce_tree(path_ids, jnp.concatenate([grads.reshape(2, 2, *grads.shape[1:]), low[None]]))
    total += own0 - jnp.where(path_ids[2] == path_ids[INNER] - 1, low, 0.0)
    has = jnp.any(path_ids[:INNER] == path_ids[INNER] - 1)
    ok = (jnp.arange(PAGE) < jnp.where(has, counts[0, 0], 0))[:, None]
    dk0, dv0 = jnp.where(ok, total, 0.0).astype(BF16)
    if two_sides:
        pair = lambda part: ([part], [spread(part)])
    else:
        pair = lambda part: ([spread(part)], [])
    *grads, _ = input_grad(order, facts, w, 2 * PAGE, *pair(dv12), ([dk12], [dv12]))
    grads = input_grad(order, facts, w, PAGE, *pair(dv0), ([dk0], [dv0]), grads)
    return (state["gq"], grads[1], grads[2], grads[0])


def solution(mesh):
    placed = (
        P(("groups", "leaf", "sub"), "tensor"),
        P(("groups", "leaf", "sub"), "tensor"),
        P(("groups", "leaf", "sub"), "tensor"),
        P(("groups", "leaf", "sub"), "tensor"),
        P("tensor", ("groups", "leaf", "sub")),
        P("tensor", ("groups", "leaf", "sub")),
        P(("groups", "leaf", "sub"), None),
        P(("groups", "leaf", "sub"), None),
        P("tensor", None),
    )
    return jax.shard_map(
        on_device,
        mesh=mesh,
        in_specs=placed,
        out_specs=(
            P(("groups", "leaf", "sub"), "tensor"),
            P(("groups", "leaf", "sub"), "tensor"),
            P(("groups", "leaf", "sub"), "tensor"),
            P(("groups", "leaf", "sub"), "tensor"),
        ),
        check_vma=False,
    )
```

```python
import math

import jax
import jax.numpy as jnp
from jax import lax
from jax.experimental import pallas as pl
from jax.experimental.pallas import tpu as pltpu
from jax.sharding import PartitionSpec as P

HD = 128
PAGE = 128
SLOTS = 3
INNER = 3
ROWS = SLOTS * PAGE
LOG2E = math.log2(math.e)
SCALE = 1.0 / math.sqrt(HD)
BF16 = jnp.bfloat16
F32 = jnp.float32
I32 = jnp.int32
LARGE = 10 << 20
SMALL = 4 << 20
SLIGHT = pl.CostEstimate(flops=1000, bytes_accessed=1000, transcendentals=0)
BLOCKED = 1e30


def dot_t(left, right):
    return lax.dot_general(left, right, (((1,), (1,)), ((), ())), preferred_element_type=F32)


def dot_n(left, right):
    return lax.dot_general(left, right, (((1,), (0,)), ((), ())), preferred_element_type=F32)


FACTS = 16
N0, N1, N2, OWNS2, LIMIT, LEADS, ROOT_IN_CHIP, ROOT_IN_PAIR, NEXT_IN_CHIP, SIDE, SWAP = range(11)


class Order:
    def __init__(self, crossed, heads):
        self.crossed, self.heads = crossed, heads
        self.half = heads // 2 if crossed else heads

    def at(self, facts, head, unit):
        if not self.crossed:
            return head * unit
        step = ((head ^ self.half) - head) * unit
        return pl.multiple_of(facts[SWAP] * step + head * unit, unit)

    def runs(self, first, last):
        cuts = [first, *(h for h in range(first + 1, last) if h % self.half == 0), last]
        return list(zip(cuts[:-1], cuts[1:]))

    def real(self, facts, rows):
        if not self.crossed:
            return rows
        width = self.half * HD
        turned = jnp.concatenate([rows[:, width:], rows[:, :width]], axis=1)
        return jnp.where(facts[SWAP] == 1, turned, rows)


def write_facts(facts, ids, counts, side, order):
    page = [ids[0, j] for j in range(INNER + 1)]
    own = page[INNER] - 1
    leaf = own // SLOTS
    owns = [page[j] == own for j in range(INNER)]
    same = lambda level, shift: ((page[level] // SLOTS) >> shift) == (leaf >> shift)
    number = lambda flag: jnp.where(flag, 1, 0)
    facts[N0] = jnp.where(owns[0] | owns[1] | owns[2], counts[0, 0], 0)
    facts[N1] = counts[0, 1]
    facts[N2] = counts[0, 2]
    facts[OWNS2] = number(owns[2])
    facts[LIMIT] = jnp.where(owns[2], 2 * PAGE, jnp.where(owns[1], PAGE, 0))
    facts[LEADS] = number(lax.rem(leaf, 2) == 0)
    facts[ROOT_IN_CHIP] = number(same(0, 1))
    facts[ROOT_IN_PAIR] = number(same(0, 2))
    facts[NEXT_IN_CHIP] = number(same(1, 1))
    facts[SIDE] = side
    facts[SWAP] = lax.rem(leaf, 2) if order.crossed else 0
    for i in range(SWAP + 1, FACTS):
        facts[i] = 0


def row_ok(count, rows, width):
    return lax.broadcasted_iota(I32, (rows, width), 0) < count


def kernel_call(body, facts, near, far, outs, scratch=(), aliases=None, after=(), cost=None,
                limit=SMALL):
    smem = pl.BlockSpec(memory_space=pltpu.SMEM)
    vmem = pl.BlockSpec(memory_space=pltpu.VMEM)
    hbm = pl.BlockSpec(memory_space=pl.ANY)
    near = [pltpu.with_memory_space_constraint(a, pltpu.VMEM) for a in near]
    place = {("near", i): 1 + i for i in range(len(near))}
    place |= {("far", i): 1 + len(near) + i for i in range(len(far))}
    used = 1 + len(near) + len(far)

    def kernel(*refs):
        body(*refs[:used], *refs[used + len(after) :])

    return pl.pallas_call(
        kernel,
        out_shape=tuple(
            pltpu.VMEM(s, d) if inside else jax.ShapeDtypeStruct(s, d) for s, d, inside in outs
        ),
        in_specs=[smem] + [vmem] * len(near) + [hbm] * (len(far) + len(after)),
        out_specs=tuple(vmem if inside else hbm for _, _, inside in outs),
        scratch_shapes=list(scratch),
        input_output_aliases={place[k]: v for k, v in (aliases or {}).items()},
        compiler_params=pltpu.CompilerParams(vmem_limit_bytes=limit),
        cost_estimate=cost or SLIGHT,
    )(pltpu.with_memory_space_constraint(facts, pltpu.SMEM), *near, *far, *after)


def start(order, side, ids, counts, keys, values):
    width = keys.shape[1]

    def body(side_ref, ids_ref, counts_ref, k_ref, v_ref, facts, out, held, ids_s, counts_s, sem):
        copies = [
            pltpu.make_async_copy(src, dst, sem.at[i])
            for i, (src, dst) in enumerate(
                (
                    (ids_ref, ids_s),
                    (counts_ref, counts_s),
                    (k_ref.at[:PAGE], held.at[0]),
                    (v_ref.at[:PAGE], held.at[1]),
                )
            )
        ]
        for c in copies:
            c.start()
        copies[0].wait()
        copies[1].wait()
        write_facts(facts, ids_s, counts_s, side_ref[0], order)
        ok = row_ok(counts_s[0, 0], PAGE, width)
        for i in range(2):
            copies[2 + i].wait()
            out[i] = jnp.where(ok, held[i], jnp.zeros((), BF16))

    smem = pl.BlockSpec(memory_space=pltpu.SMEM)
    hbm = pl.BlockSpec(memory_space=pl.ANY)
    return pl.pallas_call(
        body,
        out_shape=(pltpu.SMEM((FACTS,), I32), pltpu.VMEM((2, PAGE, width), BF16)),
        in_specs=[smem] + [hbm] * 4,
        out_specs=(smem, pl.BlockSpec(memory_space=pltpu.VMEM)),
        scratch_shapes=[
            pltpu.VMEM((2, PAGE, width), BF16),
            pltpu.SMEM(ids.shape, I32),
            pltpu.SMEM(counts.shape, I32),
            pltpu.SemaphoreType.DMA((4,)),
        ],
        compiler_params=pltpu.CompilerParams(vmem_limit_bytes=SMALL),
    )(side, ids, counts, keys, values)


def row_terms(rows):
    high = rows.astype(BF16).astype(F32)
    rest = rows - high
    middle = rest.astype(BF16).astype(F32)
    parts = [high, middle, rest - middle]
    spare = HD - 3 * rows.shape[0]
    parts.append(jnp.zeros((spare, rows.shape[1]), F32))
    return jnp.concatenate(parts, axis=0).T.astype(BF16)


class Head:
    def __init__(self, kv, group, norms, deltas, en, ed):
        self.group = group
        self.heads = min(4, group)
        self.parts = group // self.heads
        self.tall = self.heads * PAGE
        heads = slice(kv * group, (kv + 1) * group)
        en[...] = row_terms(norms[heads, :])
        ed[...] = row_terms(deltas[heads, :])

    def lanes(self, part, j):
        at = (part * self.heads + j) * HD
        return slice(at, at + HD)

    def stacked(self, ref, part, slots):
        return jnp.concatenate(
            [
                ref[slot * PAGE : (slot + 1) * PAGE, self.lanes(part, j)]
                for slot in slots
                for j in range(self.heads)
            ],
            axis=0,
        )

    def deep(self, stacked, terms, part, slots):
        column = lax.broadcasted_iota(I32, (1, HD), 1) % self.group
        picks = [
            (column == part * self.heads + j).astype(F32).astype(BF16)
            for j in range(self.heads)
        ]
        extra = [
            terms[slot * PAGE : (slot + 1) * PAGE] * pick for slot in slots for pick in picks
        ]
        return jnp.concatenate([stacked, jnp.concatenate(extra, axis=0)], axis=1)

    def turned_at(self, part, slot, count):
        at = (part * SLOTS + slot) * self.tall
        return slice(at, at + self.tall * count)

    def put_queries(self, part, slot, rows_by_head, dq, add, stage):
        rows = slice(slot * PAGE, (slot + 1) * PAGE)
        for j in range(self.heads):
            value = rows_by_head[j * PAGE : (j + 1) * PAGE]
            if stage is None:
                dq[rows, self.lanes(part, j)] = value
            else:
                if add:
                    value = value + dq[rows, self.lanes(part, j)]
                stage[rows, j * HD : (j + 1) * HD] = (value * SCALE).astype(BF16)


def set_keys(deep, upright, at, page):
    where = slice(at * PAGE, (at + 1) * PAGE)
    deep[:HD, where] = page.T
    if upright is not None:
        upright[where] = page


def weigh(scores, grads, keep):
    p = keep(jnp.exp2(scores * (SCALE * LOG2E)))
    return p.astype(BF16), (p * grads).astype(BF16)


def attend(own, kvs, group, order, facts, inputs, pages, state, prior=(), after=(), w=None,
           ride=None):
    loading = "k" not in state
    q_all, k_all = inputs[0], inputs[2]
    count = len(kvs)
    parts = group // min(4, group)
    tall = min(4, group) * PAGE
    wide = min(4, group) * HD
    width = count * HD
    base = prior[0].shape[1] if prior else 0
    kv_total = k_all.shape[1] // HD
    fresh = [("dq", kv) not in state for kv in kvs]
    one_head = (ROWS, group * HD)
    turned = ((HD, group * ROWS), BF16, True)
    shapes = {"dq": (one_head, F32, True), "qt": turned, "gt": turned}

    near, far, aliases, outs = [], [], {}, []
    at_near, at_far, at_out = {}, {}, {}

    def add_near(name, array):
        at_near[name] = len(near)
        near.append(array)

    def add_far(name, array):
        at_far[name] = len(far)
        far.append(array)

    def add_out(name, out):
        at_out[name] = len(outs)
        outs.append(out)

    for kv, is_fresh in zip(kvs, fresh):
        for name, shape in shapes.items():
            if is_fresh:
                add_out((name, kv), shape)
            elif own or name != "dq":
                add_near((name, kv), state[name, kv])
        if not own and not is_fresh:
            add_out(("ds", kv), ((group * ROWS, 2 * PAGE), BF16, True))
    if own and not all(fresh):
        add_out("gq", (q_all.shape, BF16, False))
        if "gq" in state:
            add_far("gq", state["gq"])
            aliases["far", at_far["gq"]] = at_out["gq"]
    at_results = len(outs)
    if own:
        outs += [
            ((2 * PAGE, base + width), BF16, True),
            ((2 * PAGE, base + width), BF16, True),
            ((2, PAGE, base + width), F32, True),
            ((2, PAGE, base + width), BF16, True),
        ]
    else:
        outs += [
            ((4, PAGE, width), F32, True) if ride is None else ((7, PAGE, width), BF16, True),
        ]
    at_loaded = len(outs)
    if loading:
        for name, array in zip(("q", "g", "k", "v", "norms", "deltas"), inputs):
            add_far(name, array)
            if name in ("q", "g"):
                for kv in range(kv_total):
                    add_out((name, kv), (one_head, BF16, True))
            else:
                add_out(name, (array.shape, array.dtype, True))
    else:
        for name in ("k", "v", "norms", "deltas"):
            add_near(name, state[name])
        for kv in kvs:
            for name in ("q", "g"):
                add_near((name, kv), state[name, kv])
    at_end = len(outs)
    if w is not None:
        add_far("w", w)
        outs.append((w.shape, w.dtype, True))
    for i, page in enumerate(pages):
        add_near(("page", i), page)
    for i, array in enumerate(prior):
        add_near(("prior", i), array)
    for i, array in enumerate(ride or ()):
        add_near(("ride", i), array)
    key_pages = 4 if own else 2
    scratch = [
        pltpu.VMEM((2 * HD, key_pages * PAGE), BF16),
        pltpu.VMEM((2 * HD, key_pages * PAGE), BF16),
        pltpu.VMEM((key_pages * PAGE, HD), BF16),
        pltpu.VMEM((2, HD, key_pages * PAGE), F32),
        pltpu.VMEM((ROWS, HD), BF16),
        pltpu.VMEM((ROWS, HD), BF16),
        pltpu.VMEM((count * parts, ROWS, wide), BF16),
        pltpu.SemaphoreType.DMA((count * parts,)),
        pltpu.SemaphoreType.DMA((2 * kv_total + 9,)),
    ]
    cols = lambda a, b: slice(a * PAGE, b * PAGE)

    def body(facts, *refs):
        ins, out_refs = refs[: len(near) + len(far)], refs[len(near) + len(far) : -len(scratch)]
        k_deep, v_deep, k_up, acc, en, ed, stage, sem, load_sem = refs[-len(scratch) :]
        near_ref = lambda name: ins[at_near[name]]
        far_ref = lambda name: ins[len(near) + at_far[name]]
        held = lambda name: out_refs[at_out[name]] if name in at_out else near_ref(name)
        results = out_refs[at_results:at_loaded]
        copies = {}
        if loading:

            def load(key, src, dst):
                copies[key] = pltpu.make_async_copy(src, dst, load_sem.at[len(copies)])
                copies[key].start()

            for lo, hi in order.runs(0, kv_total):
                for name in ("k", "v"):
                    at = pl.ds(order.at(facts, lo, HD), (hi - lo) * HD)
                    here = slice(lo * HD, hi * HD)
                    load((name, lo), far_ref(name).at[:, at], held(name).at[:, here])
                for name in ("norms", "deltas"):
                    at = pl.ds(order.at(facts, lo, group), (hi - lo) * group)
                    here = slice(lo * group, hi * group)
                    load((name, lo), far_ref(name).at[at], held(name).at[here])
            shared_loads = list(copies)
            for kv in range(kv_total):
                at = pl.ds(order.at(facts, kv, group * HD), group * HD)
                for name in ("q", "g"):
                    load((name, kv), far_ref(name).at[:, at], held((name, kv)))
        if w is not None:
            w_copy = pltpu.make_async_copy(
                far_ref("w"), out_refs[at_end], load_sem.at[2 * kv_total + 8]
            )
            w_copy.start()
        k, v, norms, deltas = (held(name) for name in ("k", "v", "norms", "deltas"))

        def arrived(*keys):
            for key in keys:
                if key in copies:
                    copies.pop(key).wait()

        k_deep[HD:] = jnp.full((HD, key_pages * PAGE), -1.0, BF16)
        v_deep[HD:] = jnp.full((HD, key_pages * PAGE), -1.0, BF16)
        for out, i in zip(results, range(len(prior))):
            out[..., :base] = near_ref(("prior", i))[...]
        if ride is not None:
            (out,) = results
            for kind in range(2):
                out[4 + kind] = near_ref(("ride", 0))[kind]
                out[6, :, kind * HD : (kind + 1) * HD] = near_ref(("ride", 1))[kind]
        owns2 = facts[OWNS2] == 1
        if loading:
            arrived(*shared_loads)
            lane = lax.broadcasted_iota(I32, norms.shape, 1)
            limit = jnp.where(
                lane < PAGE, facts[N0], jnp.where(lane < 2 * PAGE, facts[N1], facts[N2])
            )
            norms[...] = jnp.where(lane % PAGE < limit, norms[...] * (1.0 / SCALE), BLOCKED)
        lower = lambda rows: lax.broadcasted_iota(I32, (rows, PAGE), 1) <= (
            lax.broadcasted_iota(I32, (rows, PAGE), 0) % PAGE
        )

        def set_pages(n, kv):
            lane = slice(kv * HD, (kv + 1) * HD)
            if own:
                first, second = (near_ref(("page", i)) for i in range(2))
                zero = jnp.zeros((), BF16)
                for slot, (at, c) in enumerate(((3, N0), (0, N1), (2, N2))):
                    ok = row_ok(facts[c], PAGE, HD)
                    rows = cols(slot, slot + 1)
                    set_keys(k_deep, k_up, at, jnp.where(ok, k[rows, lane], zero))
                    set_keys(v_deep, None, at, jnp.where(ok, v[rows, lane], zero))
                level2 = [jnp.where(owns2, first[i, :, lane], second[i, :, lane]) for i in (0, 1)]
                if order.crossed:
                    at = (kv ^ order.half) * HD
                    lane = slice(at, at + HD)
                    for i in range(2):
                        other = jnp.where(owns2, first[i, :, lane], second[i, :, lane])
                        level2[i] = jnp.where(facts[SWAP] == 1, other, level2[i])
                set_keys(k_deep, k_up, 1, level2[0])
                set_keys(v_deep, None, 1, level2[1])
            else:
                page = near_ref(("page", 0))
                for j in range(2):
                    here = slice(n * HD, (n + 1) * HD)
                    set_keys(k_deep, k_up, j, page[j, 0, :, here])
                    set_keys(v_deep, None, j, page[j, 1, :, here])
            acc[...] = jnp.zeros_like(acc)

        def turned_rows(head, kv, part, is_fresh, qs, gs, order):
            if is_fresh:
                for name, rows in (("qt", qs), ("gt", gs)):
                    for i, slot in enumerate(order):
                        held((name, kv))[:, head.turned_at(part, slot, 1)] = rows[
                            i * tall : (i + 1) * tall
                        ].T
            return lambda name, slot, slots: held((name, kv))[
                :, head.turned_at(part, slot, slots)
            ]

        def own_part(head, kv, part, n, stage_ref):
            order = (1, 2, 0)
            qs = head.stacked(held(("q", kv)), part, order)
            gs = head.stacked(held(("g", kv)), part, order)
            qd, gd = head.deep(qs, en, part, order), head.deep(gs, ed, part, order)
            turn = turned_rows(head, kv, part, fresh[n], qs, gs, order)
            low = lower(tall)

            def keep_first(p):
                masked = jnp.where(low, p[:tall, :PAGE], 0.0)
                return jnp.concatenate(
                    [jnp.concatenate([masked, p[:tall, PAGE:]], axis=1), p[tall:]], axis=0
                )

            pa, da = weigh(
                dot_n(qd[: 2 * tall], k_deep[:, : 2 * PAGE]),
                dot_n(gd[: 2 * tall], v_deep[:, : 2 * PAGE]),
                keep_first,
            )
            both = lambda x: jnp.concatenate([x[:tall, :PAGE], x[tall:, PAGE:]], axis=0)
            low2 = lower(2 * tall)
            pb, db = weigh(
                both(dot_n(qd[tall:], k_deep[:, 2 * PAGE :])),
                both(dot_n(gd[tall:], v_deep[:, 2 * PAGE :])),
                lambda p: jnp.where(low2, p, 0.0),
            )
            for i, (name, a, b) in enumerate((("qt", da, db), ("gt", pa, pb))):
                acc[i, :, : 2 * PAGE] += dot_n(turn(name, 1, 2), a)
                acc[i, :, cols(2, 3)] += dot_n(turn(name, 2, 1), b[:tall])
                acc[i, :, cols(3, 4)] += dot_n(turn(name, 0, 1), b[tall:])
            first = dot_n(da, k_up[: 2 * PAGE])
            put = lambda slot, rows: head.put_queries(
                part, slot, rows, held(("dq", kv)), not fresh[n], stage_ref
            )
            put(1, first[:tall])
            put(2, first[tall:] + dot_n(db[:tall], k_up[cols(2, 3)]))
            put(0, dot_n(db[tall:], k_up[cols(3, 4)]))

        def shared_part(head, kv, part, n, stage_ref):
            order = (0, 1, 2)
            qs = head.stacked(held(("q", kv)), part, order)
            gs = head.stacked(held(("g", kv)), part, order)
            qd, gd = head.deep(qs, en, part, order), head.deep(gs, ed, part, order)
            turn = turned_rows(head, kv, part, fresh[n], qs, gs, order)
            column = lax.broadcasted_iota(I32, (tall, 2 * PAGE), 1)
            seen = column < facts[LIMIT]

            def keep(p):
                return jnp.concatenate([jnp.where(seen, p[:tall], 0.0), p[tall:]], axis=0)

            p, ds = weigh(dot_n(qd, k_deep[...]), dot_n(gd, v_deep[...]), keep)
            acc[0] += dot_n(turn("qt", 0, SLOTS), ds)
            acc[1] += dot_n(turn("gt", 0, SLOTS), p)
            if not fresh[n]:
                held(("ds", kv))[part * SLOTS * tall : (part + 1) * SLOTS * tall] = ds
                return
            dq = dot_n(ds, k_up[...])
            for slot in range(SLOTS):
                head.put_queries(
                    part, slot, dq[slot * tall : (slot + 1) * tall], held(("dq", kv)), not fresh[n],
                    stage_ref,
                )

        def put_own(n):
            dk12, dv12, own0, send2 = results
            here = slice(base + n * HD, base + (n + 1) * HD)
            grad = [acc[0].T * SCALE, acc[1].T]
            for at, c, to in ((0, N1, 0), (2, N2, 1)):
                ok = row_ok(facts[c], PAGE, HD)
                for kind, out in ((0, dk12), (1, dv12)):
                    out[cols(to, to + 1), here] = jnp.where(
                        ok, grad[kind][cols(at, at + 1)], 0.0
                    ).astype(BF16)
            for kind in range(2):
                level2 = grad[kind][cols(1, 2)]
                own0[kind, :, here] = grad[kind][cols(3, 4)] + jnp.where(owns2, level2, 0.0)
                send2[kind, :, here] = level2.astype(BF16)

        def put_shared(n):
            (out,) = results
            here = slice(n * HD, (n + 1) * HD)
            grads = acc[0].T * SCALE, acc[1].T
            for j in range(2):
                for kind in range(2):
                    out[2 * j + kind, :, here] = grads[kind][cols(j, j + 1)].astype(out.dtype)

        sends = []
        for n, kv in enumerate(kvs):
            arrived(("q", kv), ("g", kv))
            head = Head(kv, group, norms, deltas, en, ed)
            set_pages(n, kv)

            for part in range(parts):
                slot = n * parts + part
                (own_part if own else shared_part)(
                    head, kv, part, n, stage.at[slot] if own and not fresh[n] else None
                )
                if own and not fresh[n]:
                    at = order.at(facts, kv, group * HD) + part * wide
                    sends.append(
                        pltpu.make_async_copy(
                            stage.at[slot],
                            held("gq").at[:, pl.ds(pl.multiple_of(at, wide), wide)],
                            sem.at[slot],
                        )
                    )
                    sends[-1].start()

            (put_own if own else put_shared)(n)
        for c in sends:
            c.wait()
        arrived(*list(copies))
        if w is not None:
            w_copy.wait()

    made = kernel_call(
        body, facts, near, far, outs, scratch, aliases, after,
        pl.CostEstimate(
            flops=240 * PAGE * PAGE * HD * group * count, bytes_accessed=1000, transcendentals=0
        ),
        LARGE,
    )
    for name, at in at_out.items():
        state[name] = made[at]
    return list(made[at_results:at_loaded]) + list(made[at_end:])


def width_tiles(w):
    tile = next(t for t in (512, 640, 320, 128, w.shape[0]) if w.shape[0] % t == 0)
    return [slice(i, i + tile) for i in range(0, w.shape[0], tile)]


def finish_queries(kvs, group, order, facts, pages, state, after=()):
    parts = group // min(4, group)
    heads = group // parts
    tall = heads * PAGE
    wide = heads * HD
    near = list(pages)
    for kv in kvs:
        near += [state["ds", kv], state["dq", kv]]

    def body(facts, *refs):
        gq, made, stage, sem = refs[-4:]
        made[...] = jnp.zeros_like(made)
        sends = []
        for n, kv in enumerate(kvs):
            ds, dq = refs[len(pages) + 2 * n : len(pages) + 2 * n + 2]
            page, at = refs[kv // order.half], kv % order.half * HD
            keys = jnp.concatenate([page[j, 0, :, at : at + HD] for j in range(2)], axis=0)
            for part in range(parts):
                at = n * parts + part
                gained = dot_n(ds[part * SLOTS * tall : (part + 1) * SLOTS * tall], keys)
                for i in range(SLOTS * heads):
                    slot, j = divmod(i, heads)
                    rows = slice(slot * PAGE, (slot + 1) * PAGE)
                    value = gained[i * PAGE : (i + 1) * PAGE] + dq[
                        rows, part * wide + j * HD : part * wide + (j + 1) * HD
                    ]
                    stage[at, rows, j * HD : (j + 1) * HD] = (value * SCALE).astype(BF16)
                to = pl.multiple_of(order.at(facts, kv, group * HD) + part * wide, wide)
                sends.append(
                    pltpu.make_async_copy(stage.at[at], gq.at[:, pl.ds(to, wide)], sem.at[at])
                )
                sends[-1].start()
        for c in sends:
            c.wait()

    count = len(kvs) * parts
    far = [state["gq"]] if "gq" in state else []
    shape = (ROWS, state["k"].shape[1] * group)
    state["gq"], made = kernel_call(
        body, facts, near, far, [(shape, BF16, False), ((8, HD), F32, True)],
        [pltpu.VMEM((count, ROWS, wide), BF16), pltpu.SemaphoreType.DMA((count,))],
        {("far", 0): 0} if far else {}, after, limit=LARGE,
    )
    return made


def input_grad(order, facts, w, rows, own, far, grads, carry=None):
    out_cols, depth = w.shape
    tiles = width_tiles(w)
    top = 0 if rows == PAGE else PAGE
    steps = len(tiles)
    width = sum(a.shape[1] for a in grads[0])
    arrays = [*own, *far, *grads[0], *grads[1]]
    count = len(grads[0])
    carry = list(carry or [])

    def body(facts, *refs):
        own_r, refs = refs[: len(own)], refs[len(own) :]
        far_r, refs = refs[: len(far)], refs[len(far) :]
        grad_r, w_ref = refs[: 2 * count], refs[2 * count]
        out, dk, dv, made, w_near, stage, w_sem, sem = refs[-8:]
        loads = [
            pltpu.make_async_copy(w_ref.at[at], w_near.at[at], w_sem.at[i])
            for i, at in enumerate(tiles)
        ]
        for c in loads:
            c.start()
        made[...] = jnp.zeros_like(made)
        columns = lambda rs: jnp.concatenate([r[...] for r in rs], axis=1)
        full = columns(own_r)
        if far:
            other, leads = columns(far_r), facts[SIDE] == 0
            full = jnp.concatenate(
                [jnp.where(leads, full, other), jnp.where(leads, other, full)], axis=1
            )
        copies = put_rows(order, facts, grad_r, dk, dv, top, rows, sem, steps)
        for i, at in enumerate(tiles):
            loads[i].wait()
            stage[i] = dot_t(w_near[at], full).astype(BF16).T
            copies.append(
                pltpu.make_async_copy(stage.at[i], out.at[top : top + rows, at], sem.at[i])
            )
            copies[-1].start()
        for c in copies:
            c.wait()

    smem = pl.BlockSpec(memory_space=pltpu.SMEM)
    vmem = pl.BlockSpec(memory_space=pltpu.VMEM)
    hbm = pl.BlockSpec(memory_space=pl.ANY)
    arrays = [pltpu.with_memory_space_constraint(a, pltpu.VMEM) for a in arrays]
    kept = jax.ShapeDtypeStruct((ROWS, width), BF16)
    return pl.pallas_call(
        body,
        out_shape=(
            jax.ShapeDtypeStruct((ROWS, out_cols), BF16), kept, kept, pltpu.VMEM((8, HD), F32)
        ),
        in_specs=[smem] + [vmem] * len(arrays) + [hbm] * (1 + len(carry)),
        out_specs=(hbm, hbm, hbm, vmem),
        scratch_shapes=[
            pltpu.VMEM(w.shape, BF16),
            pltpu.VMEM((steps, rows, out_cols // steps), BF16),
            pltpu.SemaphoreType.DMA((steps,)),
            pltpu.SemaphoreType.DMA((steps + 2 * order.heads,)),
        ],
        input_output_aliases={2 + len(arrays) + i: i for i in range(len(carry))},
        compiler_params=pltpu.CompilerParams(vmem_limit_bytes=LARGE),
        cost_estimate=SLIGHT,
    )(pltpu.with_memory_space_constraint(facts, pltpu.SMEM), *arrays, w, *carry)


def put_rows(order, facts, pieces, dk, dv, top, rows, sem, first):
    copies = []
    count = len(pieces) // 2
    for dst, mine in ((dk, pieces[:count]), (dv, pieces[count:])):
        head = 0
        for src in mine:
            more = src.shape[1] // HD
            for lo, hi in order.runs(head, head + more):
                copies.append(
                    pltpu.make_async_copy(
                        src.at[:, (lo - head) * HD : (hi - head) * HD],
                        dst.at[top : top + rows, pl.ds(order.at(facts, lo, HD), (hi - lo) * HD)],
                        sem.at[first + len(copies)],
                    )
                )
                copies[-1].start()
            head += more
    return copies


def begin_input_grad(order, facts, w, own, after=()):
    out_cols, depth = w.shape
    half = depth // 2
    rows = own[0].shape[0]
    count = len(own)

    def body(facts, w_ref, *refs):
        mine, out = jnp.concatenate([r[...] for r in refs[:count]], axis=1), refs[-1]
        mine = order.real(facts, mine)
        where = pl.ds(pl.multiple_of(facts[SIDE] * half, half), half)
        for at in width_tiles(w):
            out[at] = dot_t(w_ref[at, where], mine)

    smem = pl.BlockSpec(memory_space=pltpu.SMEM)
    vmem = pl.BlockSpec(memory_space=pltpu.VMEM)
    near = [pltpu.with_memory_space_constraint(a, pltpu.VMEM) for a in (w, *own)]

    def kernel(*refs):
        body(*refs[: 2 + count], refs[-1])

    return pl.pallas_call(
        kernel,
        out_shape=pltpu.VMEM((out_cols, rows), F32),
        in_specs=[smem] + [vmem] * len(near) + [pl.BlockSpec(memory_space=pl.ANY)] * len(after),
        out_specs=vmem,
        compiler_params=pltpu.CompilerParams(vmem_limit_bytes=LARGE),
        cost_estimate=SLIGHT,
    )(pltpu.with_memory_space_constraint(facts, pltpu.SMEM), *near, *after)


def end_input_grad(order, facts, w, far, begun, grads, carry=None, after=()):
    tiles = width_tiles(w)
    out_cols, depth = w.shape
    half = depth // 2
    steps = len(tiles)
    rows = far[0].shape[0]
    top = 0 if rows == PAGE else PAGE
    width = sum(a.shape[1] for a in grads[0])
    near = [w, begun, *far, *grads[0], *grads[1]]
    carry = list(carry or [])

    def body(facts, w_r, begun_r, *refs):
        far_r, grad_r = refs[: len(far)], refs[len(far) : len(near) - 2]
        out, dk, dv, made, stage, sem = refs[-6:]
        made[...] = jnp.zeros_like(made)
        copies = put_rows(order, facts, grad_r, dk, dv, top, rows, sem, steps)
        other = order.real(facts, jnp.concatenate([r[...] for r in far_r], axis=1))
        where = pl.ds(pl.multiple_of((1 - facts[SIDE]) * half, half), half)
        for i, at in enumerate(tiles):
            stage[i] = (dot_t(w_r[at, where], other) + begun_r[at]).astype(BF16).T
            copies.append(
                pltpu.make_async_copy(stage.at[i], out.at[top : top + rows, at], sem.at[i])
            )
            copies[-1].start()
        for c in copies:
            c.wait()

    smem = pl.BlockSpec(memory_space=pltpu.SMEM)
    vmem = pl.BlockSpec(memory_space=pltpu.VMEM)
    hbm = pl.BlockSpec(memory_space=pl.ANY)
    near = [pltpu.with_memory_space_constraint(a, pltpu.VMEM) for a in near]
    kept = jax.ShapeDtypeStruct((ROWS, width), BF16)

    def kernel(*refs):
        body(*refs[: 1 + len(near)], *refs[1 + len(near) + len(carry) + len(after) :])

    return pl.pallas_call(
        kernel,
        out_shape=(
            jax.ShapeDtypeStruct((ROWS, out_cols), BF16), kept, kept, pltpu.VMEM((8, HD), F32)
        ),
        in_specs=[smem] + [vmem] * len(near) + [hbm] * (len(carry) + len(after)),
        out_specs=(hbm, hbm, hbm, vmem),
        scratch_shapes=[
            pltpu.VMEM((steps, rows, out_cols // steps), BF16),
            pltpu.SemaphoreType.DMA((steps + 2 * order.heads,)),
        ],
        input_output_aliases={1 + len(near) + i: i for i in range(len(carry))},
        compiler_params=pltpu.CompilerParams(vmem_limit_bytes=LARGE),
        cost_estimate=SLIGHT,
    )(pltpu.with_memory_space_constraint(facts, pltpu.SMEM), *near, *carry, *after)


def flipped(block, axis, bit):
    count = lax.axis_size(axis)
    return lax.ppermute(block, axis, [(i, i ^ bit) for i in range(count) if i ^ bit < count])


def spanning(leaves, bit_index):
    return len([j for j in range(INNER) if 2 << bit_index <= leaves >> j])


def gather_small_tree(facts, own, beside_pair, beside_half):
    width = own.shape[-1] // 2
    page = ((2, PAGE, width), BF16, True)
    from_core = flipped(own, "sub", 1)

    def choose_chip(facts, own_ref, far_ref, out):
        for swap in range(2):
            for mine in range(2):

                @pl.when((facts[SWAP] == swap) & (facts[OWNS2] != mine))
                def _copy(swap=swap, mine=mine):
                    out[...] = (own_ref if mine else far_ref)[
                        :, :, swap * width : (swap + 1) * width
                    ]

    (chip,) = kernel_call(choose_chip, facts, [own, from_core], [], [page])
    from_pair = flipped(chip, "leaf", 1)

    def choose_pair(facts, near_ref, far_ref, out):
        out[...] = jnp.where(facts[ROOT_IN_CHIP] == 1, near_ref[...], far_ref[...])

    after = beside_pair(from_core, chip)
    (pair,) = kernel_call(choose_pair, facts, [chip, from_pair], [], [page], after=after)
    from_half = flipped(pair, "leaf", 2)

    def choose_all(facts, chip_ref, pair_far, pair_ref, half_far, out):
        out[0] = jnp.where(facts[ROOT_IN_PAIR] == 1, pair_ref[...], half_far[...])
        out[1] = jnp.where(facts[NEXT_IN_CHIP] == 1, chip_ref[...], pair_far[...])

    after = beside_half(pair)
    (mine,) = kernel_call(
        choose_all, facts, [chip, from_pair, pair, from_half], [],
        [((2, *page[0]), BF16, True)], after=after,
    )
    return mine, flipped(mine, "sub", 1)


def over_cores(facts, kept, far):
    width = kept.shape[-1]

    def body(_, near, away, total, root, next_one):
        for i in range(4):
            value = near[i] + away[i].astype(F32)
            total[i] = value
            (root, next_one)[i // 2][i % 2] = value.astype(BF16)

    pages = ((2, PAGE, width), BF16, True)
    total, root, next_one = kernel_call(
        body, facts, [kept, far], [], [((4, PAGE, width), F32, True), pages, pages]
    )
    return total, root, flipped(root, "leaf", 2), flipped(next_one, "leaf", 1)


def over_halves(facts, total, root_far, next_far, after):
    width = total.shape[-1]

    def body(_, near, root_r, next_r, out, low):
        root = near[:2] + root_r[...].astype(F32)
        out[:2] = root
        low[...] = root.astype(BF16)
        out[2:] = near[2:] + next_r[...].astype(F32)

    total, low = kernel_call(
        body, facts, [total, root_far, next_far], [],
        [((4, PAGE, width), F32, True), ((2, PAGE, width), BF16, True)], after=after,
    )
    return total, low, flipped(low, "leaf", 1)


def over_chips(facts, total, far, level2, after):
    width = total.shape[-1]

    def body(facts, near, away, extra, out):
        root = near[:2] + away[...].astype(F32)
        out[:, :, :width] = jnp.where(facts[ROOT_IN_CHIP] == 1, root, near[2:]).astype(BF16)
        out[:, :, width:] = extra[:, :, extra.shape[-1] - HD :]

    outs = [((2, PAGE, width + HD), BF16, True)]
    (mine,) = kernel_call(body, facts, [total, far, level2], [], outs, after=after)
    return mine, flipped(mine, "sub", 1)


def finish_small_tree(order, facts, own0, mine, far, level2_far):
    part = order.half * HD
    width = 2 * part

    def body(facts, own_first, own_second, mine_r, far_r, low_r, dk, dv):
        owns2 = facts[OWNS2] == 1
        ok = row_ok(facts[N0], PAGE, HD)
        for head in range(order.heads):
            c = slice(head * HD, (head + 1) * HD)
            at = head % order.half * HD
            here = slice(at, at + HD)
            theirs = head ^ order.half
            for kind, out in enumerate((dk, dv)):
                first = head < order.half
                gained = (far_r if first else mine_r)[kind, :, here]
                base = (own_first if first else own_second)[kind, :, here]
                if theirs < order.half:
                    level2 = low_r[4 + kind, :, theirs * HD : (theirs + 1) * HD]
                elif theirs + 1 < order.heads:
                    level2 = low_r[6, :, kind * HD : (kind + 1) * HD]
                else:
                    level2 = far_r[kind, :, part : part + HD]
                more = jnp.where(owns2, level2, gained).astype(F32)
                out[:, c] = jnp.where(ok, base + more, 0.0).astype(BF16)

    page = ((PAGE, width), BF16, True)
    return kernel_call(body, facts, [*own0, mine, far, level2_far], [], [page, page])


def gather_tree(ids, own):
    leaves = lax.axis_size(("leaf", "sub"))
    owned = ids[:INNER] == ids[INNER] - 1
    pages = jnp.where(owned[:, None, None, None], own[None], jnp.zeros((), BF16))
    for bit in range(leaves.bit_length() - 1):
        active = spanning(leaves, bit)
        far = flipped(pages[:active], ("leaf", "sub"), 1 << bit)
        pages = jnp.concatenate([pages[:active] + far, pages[active:]])
    return pages


def reduce_tree(ids, parts):
    leaves = lax.axis_size(("leaf", "sub"))
    for bit in range(leaves.bit_length() - 1):
        active = spanning(leaves, bit)
        far = flipped(parts[:active], ("leaf", "sub"), 1 << bit)
        parts = jnp.concatenate([parts[:active] + far, parts[active:]])
    owned = ids[:INNER] == ids[INNER] - 1
    return jnp.sum(jnp.where(owned[:, None, None, None], parts, 0.0), axis=0)


def on_device(queries, grad_out, keys, values, log_norms, row_deltas, ancestors, counts, w_value):
    kv = keys.shape[1] // HD
    group = queries.shape[1] // keys.shape[1]
    leaves = lax.axis_size(("leaf", "sub"))
    hbm = lambda a: pltpu.with_memory_space_constraint(a, pltpu.HBM)
    side = lax.axis_index("tensor").astype(I32).reshape(1)
    two_sides = lax.axis_size("tensor") == 2
    inputs = [hbm(a) for a in (queries, grad_out, keys, values, log_norms, row_deltas)]
    fast = leaves == 8 and lax.axis_size("sub") == 2 and kv == 4 and two_sides
    order = Order(fast, kv)
    facts, own = start(order, side, hbm(ancestors), hbm(counts), *inputs[2:4])
    state = {}

    def own_pages(kvs, pages, prior=(), after=(), w=None):
        return attend(
            True, kvs, group, order, facts, inputs, pages, state, prior, after, w
        )

    def shared_pages(kvs, page, ride=None, after=()):
        return attend(
            False, kvs, group, order, facts, inputs, [page], state, after=after, ride=ride
        )[0]

    def spread(part):
        if two_sides:
            return flipped(part, "tensor", 1)
        return lax.all_gather(part, "tensor", axis=1, tiled=True)

    kvs = tuple(range(kv))
    w = hbm(w_value)
    if fast:
        level2, by_head, far_v = [], [], []

        def beside_pair(from_core, chip):
            level2.extend((own, from_core))
            by_head.append(own_pages(kvs[:1], level2, after=(chip,)))
            return (by_head[0][3],)

        def beside_half(pair):
            by_head.append(own_pages(kvs[1:2], level2, by_head[0], (pair,)))
            far_v.append(spread(by_head[1][1]))
            by_head.append(own_pages(kvs[2:3], level2, after=(by_head[1][3],)))
            return (by_head[2][3],)

        mine, theirs = gather_small_tree(facts, own, beside_pair, beside_half)
        first, third = by_head[1:]
        sent = shared_pages(kvs[:2], mine, (first[3], third[3]), far_v)
        sent = flipped(sent, "sub", 1)
        kept = shared_pages(kvs[2:], theirs)
        total, root, root_far, next_far = over_cores(facts, kept, sent)
        *second, w_near = own_pages(kvs[3:], level2, third, (root,), w)
        both = list(zip(first, second))
        begun = begin_input_grad(order, facts, w_near, both[1])
        far_v.append(spread(second[1]))
        total, low, far = over_halves(facts, total, root_far, next_far, (begun,))
        made = finish_queries(kvs[:3], group, order, facts, (mine, theirs), state, (low,))
        near, far = over_chips(facts, total, far, second[3], (made, far_v[1]))
        dk0, dv0 = finish_small_tree(order, facts, both[2], near, far, sent)
        far_0 = spread(dv0)
        begun_0 = begin_input_grad(order, facts, w_near, [dv0])
        *grads, _ = end_input_grad(
            order, facts, w_near, far_v, begun, both[:2], after=(begun_0,)
        )
        grads = end_input_grad(
            order, facts, w_near, [far_0], begun_0, ([dk0], [dv0]), grads
        )
        return (state["gq"], grads[1], grads[2], grads[0])

    path_ids = ancestors[0]
    pages = gather_tree(path_ids, own)
    dk12, dv12, own0, send2 = own_pages(kvs, (pages[2], pages[2]))
    grads = shared_pages(kvs, pages[:2])
    finish_queries(kvs, group, order, facts, (pages[:2],), state)
    low = send2.astype(F32)
    total = reduce_tree(path_ids, jnp.concatenate([grads.reshape(2, 2, *grads.shape[1:]), low[None]]))
    total += own0 - jnp.where(path_ids[2] == path_ids[INNER] - 1, low, 0.0)
    has = jnp.any(path_ids[:INNER] == path_ids[INNER] - 1)
    ok = (jnp.arange(PAGE) < jnp.where(has, counts[0, 0], 0))[:, None]
    dk0, dv0 = jnp.where(ok, total, 0.0).astype(BF16)
    if two_sides:
        pair = lambda part: ([part], [spread(part)])
    else:
        pair = lambda part: ([spread(part)], [])
    *grads, _ = input_grad(order, facts, w, 2 * PAGE, *pair(dv12), ([dk12], [dv12]))
    grads = input_grad(order, facts, w, PAGE, *pair(dv0), ([dk0], [dv0]), grads)
    return (state["gq"], grads[1], grads[2], grads[0])


def solution(mesh):
    placed = (
        P(("groups", "leaf", "sub"), "tensor"),
        P(("groups", "leaf", "sub"), "tensor"),
        P(("groups", "leaf", "sub"), "tensor"),
        P(("groups", "leaf", "sub"), "tensor"),
        P("tensor", ("groups", "leaf", "sub")),
        P("tensor", ("groups", "leaf", "sub")),
        P(("groups", "leaf", "sub"), None),
        P(("groups", "leaf", "sub"), None),
        P("tensor", None),
    )
    return jax.shard_map(
        on_device,
        mesh=mesh,
        in_specs=placed,
        out_specs=(
            P(("groups", "leaf", "sub"), "tensor"),
            P(("groups", "leaf", "sub"), "tensor"),
            P(("groups", "leaf", "sub"), "tensor"),
            P(("groups", "leaf", "sub"), "tensor"),
        ),
        check_vma=False,
    )
```

```python
import math

import jax
import jax.numpy as jnp
from jax import lax
from jax.experimental import pallas as pl
from jax.experimental.pallas import tpu as pltpu
from jax.sharding import PartitionSpec as P

HD = 128
PAGE = 128
SLOTS = 3
INNER = 3
ROWS = SLOTS * PAGE
LOG2E = math.log2(math.e)
SCALE = 1.0 / math.sqrt(HD)
BF16 = jnp.bfloat16
F32 = jnp.float32
I32 = jnp.int32
LARGE = 10 << 20
SMALL = 4 << 20
SLIGHT = pl.CostEstimate(flops=1000, bytes_accessed=1000, transcendentals=0)
BLOCKED = 1e30


def dot_t(left, right):
    return lax.dot_general(left, right, (((1,), (1,)), ((), ())), preferred_element_type=F32)


def dot_n(left, right):
    return lax.dot_general(left, right, (((1,), (0,)), ((), ())), preferred_element_type=F32)


FACTS = 16
N0, N1, N2, OWNS2, LIMIT, LEADS, ROOT_IN_CHIP, ROOT_IN_PAIR, NEXT_IN_CHIP, SIDE, SWAP = range(11)


class Order:
    def __init__(self, crossed, heads):
        self.crossed, self.heads = crossed, heads
        self.half = heads // 2 if crossed else heads

    def at(self, facts, head, unit):
        if not self.crossed:
            return head * unit
        step = ((head ^ self.half) - head) * unit
        return pl.multiple_of(facts[SWAP] * step + head * unit, unit)

    def runs(self, first, last):
        cuts = [first, *(h for h in range(first + 1, last) if h % self.half == 0), last]
        return list(zip(cuts[:-1], cuts[1:]))

    def real(self, facts, rows):
        if not self.crossed:
            return rows
        width = self.half * HD
        turned = jnp.concatenate([rows[:, width:], rows[:, :width]], axis=1)
        return jnp.where(facts[SWAP] == 1, turned, rows)


def write_facts(facts, ids, counts, side, order):
    page = [ids[0, j] for j in range(INNER + 1)]
    own = page[INNER] - 1
    leaf = own // SLOTS
    owns = [page[j] == own for j in range(INNER)]
    same = lambda level, shift: ((page[level] // SLOTS) >> shift) == (leaf >> shift)
    number = lambda flag: jnp.where(flag, 1, 0)
    facts[N0] = jnp.where(owns[0] | owns[1] | owns[2], counts[0, 0], 0)
    facts[N1] = counts[0, 1]
    facts[N2] = counts[0, 2]
    facts[OWNS2] = number(owns[2])
    facts[LIMIT] = jnp.where(owns[2], 2 * PAGE, jnp.where(owns[1], PAGE, 0))
    facts[LEADS] = number(lax.rem(leaf, 2) == 0)
    facts[ROOT_IN_CHIP] = number(same(0, 1))
    facts[ROOT_IN_PAIR] = number(same(0, 2))
    facts[NEXT_IN_CHIP] = number(same(1, 1))
    facts[SIDE] = side
    facts[SWAP] = lax.rem(leaf, 2) if order.crossed else 0
    for i in range(SWAP + 1, FACTS):
        facts[i] = 0


def row_ok(count, rows, width):
    return lax.broadcasted_iota(I32, (rows, width), 0) < count


def kernel_call(body, facts, near, far, outs, scratch=(), aliases=None, after=(), cost=None,
                limit=SMALL):
    smem = pl.BlockSpec(memory_space=pltpu.SMEM)
    vmem = pl.BlockSpec(memory_space=pltpu.VMEM)
    hbm = pl.BlockSpec(memory_space=pl.ANY)
    near = [pltpu.with_memory_space_constraint(a, pltpu.VMEM) for a in near]
    place = {("near", i): 1 + i for i in range(len(near))}
    place |= {("far", i): 1 + len(near) + i for i in range(len(far))}
    used = 1 + len(near) + len(far)

    def kernel(*refs):
        body(*refs[:used], *refs[used + len(after) :])

    return pl.pallas_call(
        kernel,
        out_shape=tuple(
            pltpu.VMEM(s, d) if inside else jax.ShapeDtypeStruct(s, d) for s, d, inside in outs
        ),
        in_specs=[smem] + [vmem] * len(near) + [hbm] * (len(far) + len(after)),
        out_specs=tuple(vmem if inside else hbm for _, _, inside in outs),
        scratch_shapes=list(scratch),
        input_output_aliases={place[k]: v for k, v in (aliases or {}).items()},
        compiler_params=pltpu.CompilerParams(vmem_limit_bytes=limit),
        cost_estimate=cost or SLIGHT,
    )(pltpu.with_memory_space_constraint(facts, pltpu.SMEM), *near, *far, *after)


def start(order, side, ids, counts, keys, values):
    width = keys.shape[1]

    def body(side_ref, ids_ref, counts_ref, k_ref, v_ref, facts, out, held, ids_s, counts_s, sem):
        copies = [
            pltpu.make_async_copy(src, dst, sem.at[i])
            for i, (src, dst) in enumerate(
                (
                    (ids_ref, ids_s),
                    (counts_ref, counts_s),
                    (k_ref.at[:PAGE], held.at[0]),
                    (v_ref.at[:PAGE], held.at[1]),
                )
            )
        ]
        for c in copies:
            c.start()
        copies[0].wait()
        copies[1].wait()
        write_facts(facts, ids_s, counts_s, side_ref[0], order)
        ok = row_ok(counts_s[0, 0], PAGE, width)
        for i in range(2):
            copies[2 + i].wait()
            out[i] = jnp.where(ok, held[i], jnp.zeros((), BF16))

    smem = pl.BlockSpec(memory_space=pltpu.SMEM)
    hbm = pl.BlockSpec(memory_space=pl.ANY)
    return pl.pallas_call(
        body,
        out_shape=(pltpu.SMEM((FACTS,), I32), pltpu.VMEM((2, PAGE, width), BF16)),
        in_specs=[smem] + [hbm] * 4,
        out_specs=(smem, pl.BlockSpec(memory_space=pltpu.VMEM)),
        scratch_shapes=[
            pltpu.VMEM((2, PAGE, width), BF16),
            pltpu.SMEM(ids.shape, I32),
            pltpu.SMEM(counts.shape, I32),
            pltpu.SemaphoreType.DMA((4,)),
        ],
        compiler_params=pltpu.CompilerParams(vmem_limit_bytes=SMALL),
    )(side, ids, counts, keys, values)


def row_terms(rows):
    high = rows.astype(BF16).astype(F32)
    rest = rows - high
    middle = rest.astype(BF16).astype(F32)
    parts = [high, middle, rest - middle]
    spare = HD - 3 * rows.shape[0]
    parts.append(jnp.zeros((spare, rows.shape[1]), F32))
    return jnp.concatenate(parts, axis=0).T.astype(BF16)


class Head:
    def __init__(self, kv, group, norms, deltas, en, ed):
        self.group = group
        self.heads = min(4, group)
        self.parts = group // self.heads
        self.tall = self.heads * PAGE
        heads = slice(kv * group, (kv + 1) * group)
        en[...] = row_terms(norms[heads, :])
        ed[...] = row_terms(deltas[heads, :])

    def lanes(self, part, j):
        at = (part * self.heads + j) * HD
        return slice(at, at + HD)

    def stacked(self, ref, part, slots):
        return jnp.concatenate(
            [
                ref[slot * PAGE : (slot + 1) * PAGE, self.lanes(part, j)]
                for slot in slots
                for j in range(self.heads)
            ],
            axis=0,
        )

    def deep(self, stacked, terms, part, slots):
        column = lax.broadcasted_iota(I32, (1, HD), 1) % self.group
        picks = [
            (column == part * self.heads + j).astype(F32).astype(BF16)
            for j in range(self.heads)
        ]
        extra = [
            terms[slot * PAGE : (slot + 1) * PAGE] * pick for slot in slots for pick in picks
        ]
        return jnp.concatenate([stacked, jnp.concatenate(extra, axis=0)], axis=1)

    def turned_at(self, part, slot, count):
        at = (part * SLOTS + slot) * self.tall
        return slice(at, at + self.tall * count)

    def put_queries(self, part, slot, rows_by_head, dq, add, stage):
        rows = slice(slot * PAGE, (slot + 1) * PAGE)
        for j in range(self.heads):
            value = rows_by_head[j * PAGE : (j + 1) * PAGE]
            if stage is None:
                dq[rows, self.lanes(part, j)] = value
            else:
                if add:
                    value = value + dq[rows, self.lanes(part, j)]
                stage[rows, j * HD : (j + 1) * HD] = (value * SCALE).astype(BF16)


def set_keys(deep, upright, at, page):
    where = slice(at * PAGE, (at + 1) * PAGE)
    deep[:HD, where] = page.T
    if upright is not None:
        upright[where] = page


def weigh(scores, grads, keep):
    p = keep(jnp.exp2(scores * (SCALE * LOG2E)))
    return p.astype(BF16), (p * grads).astype(BF16)


def attend(own, kvs, group, order, facts, inputs, pages, state, prior=(), after=(), w=None,
           ride=None):
    loading = "k" not in state
    q_all, k_all = inputs[0], inputs[2]
    count = len(kvs)
    parts = group // min(4, group)
    tall = min(4, group) * PAGE
    wide = min(4, group) * HD
    width = count * HD
    base = prior[0].shape[1] if prior else 0
    kv_total = k_all.shape[1] // HD
    fresh = [("dq", kv) not in state for kv in kvs]
    one_head = (ROWS, group * HD)
    turned = ((HD, group * ROWS), BF16, True)
    shapes = {"dq": (one_head, F32, True), "qt": turned, "gt": turned}

    near, far, aliases, outs = [], [], {}, []
    at_near, at_far, at_out = {}, {}, {}

    def add_near(name, array):
        at_near[name] = len(near)
        near.append(array)

    def add_far(name, array):
        at_far[name] = len(far)
        far.append(array)

    def add_out(name, out):
        at_out[name] = len(outs)
        outs.append(out)

    for kv, is_fresh in zip(kvs, fresh):
        for name, shape in shapes.items():
            if is_fresh:
                add_out((name, kv), shape)
            elif own or name != "dq":
                add_near((name, kv), state[name, kv])
        if not own and not is_fresh:
            add_out(("ds", kv), ((group * ROWS, 2 * PAGE), BF16, True))
    if own and not all(fresh):
        add_out("gq", (q_all.shape, BF16, False))
        if "gq" in state:
            add_far("gq", state["gq"])
            aliases["far", at_far["gq"]] = at_out["gq"]
    at_results = len(outs)
    if own:
        outs += [
            ((2 * PAGE, base + width), BF16, True),
            ((2 * PAGE, base + width), BF16, True),
            ((2, PAGE, base + width), F32, True),
            ((2, PAGE, base + width), BF16, True),
        ]
    else:
        outs += [
            ((4, PAGE, width), F32, True) if ride is None else ((7, PAGE, width), BF16, True),
        ]
    at_loaded = len(outs)
    if loading:
        for name, array in zip(("q", "g", "k", "v", "norms", "deltas"), inputs):
            add_far(name, array)
            if name in ("q", "g"):
                for kv in range(kv_total):
                    add_out((name, kv), (one_head, BF16, True))
            else:
                add_out(name, (array.shape, array.dtype, True))
    else:
        for name in ("k", "v", "norms", "deltas"):
            add_near(name, state[name])
        for kv in kvs:
            for name in ("q", "g"):
                add_near((name, kv), state[name, kv])
    at_end = len(outs)
    if w is not None:
        add_far("w", w)
        outs.append((w.shape, w.dtype, True))
    for i, page in enumerate(pages):
        add_near(("page", i), page)
    for i, array in enumerate(prior):
        add_near(("prior", i), array)
    for i, array in enumerate(ride or ()):
        add_near(("ride", i), array)
    key_pages = 4 if own else 2
    scratch = [
        pltpu.VMEM((2 * HD, key_pages * PAGE), BF16),
        pltpu.VMEM((2 * HD, key_pages * PAGE), BF16),
        pltpu.VMEM((key_pages * PAGE, HD), BF16),
        pltpu.VMEM((2, HD, key_pages * PAGE), F32),
        pltpu.VMEM((ROWS, HD), BF16),
        pltpu.VMEM((ROWS, HD), BF16),
        pltpu.VMEM((count * parts, ROWS, wide), BF16),
        pltpu.SemaphoreType.DMA((count * parts,)),
        pltpu.SemaphoreType.DMA((2 * kv_total + 9,)),
    ]
    cols = lambda a, b: slice(a * PAGE, b * PAGE)

    def body(facts, *refs):
        ins, out_refs = refs[: len(near) + len(far)], refs[len(near) + len(far) : -len(scratch)]
        k_deep, v_deep, k_up, acc, en, ed, stage, sem, load_sem = refs[-len(scratch) :]
        near_ref = lambda name: ins[at_near[name]]
        far_ref = lambda name: ins[len(near) + at_far[name]]
        held = lambda name: out_refs[at_out[name]] if name in at_out else near_ref(name)
        results = out_refs[at_results:at_loaded]
        copies = {}
        if loading:

            def load(key, src, dst):
                copies[key] = pltpu.make_async_copy(src, dst, load_sem.at[len(copies)])
                copies[key].start()

            for lo, hi in order.runs(0, kv_total):
                for name in ("k", "v"):
                    at = pl.ds(order.at(facts, lo, HD), (hi - lo) * HD)
                    here = slice(lo * HD, hi * HD)
                    load((name, lo), far_ref(name).at[:, at], held(name).at[:, here])
                for name in ("norms", "deltas"):
                    at = pl.ds(order.at(facts, lo, group), (hi - lo) * group)
                    here = slice(lo * group, hi * group)
                    load((name, lo), far_ref(name).at[at], held(name).at[here])
            shared_loads = list(copies)
            for kv in range(kv_total):
                at = pl.ds(order.at(facts, kv, group * HD), group * HD)
                for name in ("q", "g"):
                    load((name, kv), far_ref(name).at[:, at], held((name, kv)))
        if w is not None:
            w_copy = pltpu.make_async_copy(
                far_ref("w"), out_refs[at_end], load_sem.at[2 * kv_total + 8]
            )
            w_copy.start()
        k, v, norms, deltas = (held(name) for name in ("k", "v", "norms", "deltas"))

        def arrived(*keys):
            for key in keys:
                if key in copies:
                    copies.pop(key).wait()

        k_deep[HD:] = jnp.full((HD, key_pages * PAGE), -1.0, BF16)
        v_deep[HD:] = jnp.full((HD, key_pages * PAGE), -1.0, BF16)
        for out, i in zip(results, range(len(prior))):
            out[..., :base] = near_ref(("prior", i))[...]
        if ride is not None:
            (out,) = results
            for kind in range(2):
                more = jnp.concatenate(
                    [near_ref(("ride", i))[kind] for i in range(len(ride))], axis=1
                )
                out[4 + kind] = more[:, :width]
                out[6, :, kind * HD : (kind + 1) * HD] = more[:, width:]
        owns2 = facts[OWNS2] == 1
        if loading:
            arrived(*shared_loads)
            lane = lax.broadcasted_iota(I32, norms.shape, 1)
            limit = jnp.where(
                lane < PAGE, facts[N0], jnp.where(lane < 2 * PAGE, facts[N1], facts[N2])
            )
            norms[...] = jnp.where(lane % PAGE < limit, norms[...] * (1.0 / SCALE), BLOCKED)
        lower = lambda rows: lax.broadcasted_iota(I32, (rows, PAGE), 1) <= (
            lax.broadcasted_iota(I32, (rows, PAGE), 0) % PAGE
        )

        def set_pages(n, kv):
            lane = slice(kv * HD, (kv + 1) * HD)
            if own:
                first, second = (near_ref(("page", i)) for i in range(2))
                zero = jnp.zeros((), BF16)
                for slot, (at, c) in enumerate(((3, N0), (0, N1), (2, N2))):
                    ok = row_ok(facts[c], PAGE, HD)
                    rows = cols(slot, slot + 1)
                    set_keys(k_deep, k_up, at, jnp.where(ok, k[rows, lane], zero))
                    set_keys(v_deep, None, at, jnp.where(ok, v[rows, lane], zero))
                level2 = [jnp.where(owns2, first[i, :, lane], second[i, :, lane]) for i in (0, 1)]
                if order.crossed:
                    at = (kv ^ order.half) * HD
                    lane = slice(at, at + HD)
                    for i in range(2):
                        other = jnp.where(owns2, first[i, :, lane], second[i, :, lane])
                        level2[i] = jnp.where(facts[SWAP] == 1, other, level2[i])
                set_keys(k_deep, k_up, 1, level2[0])
                set_keys(v_deep, None, 1, level2[1])
            else:
                page = near_ref(("page", 0))
                for j in range(2):
                    here = slice(n * HD, (n + 1) * HD)
                    set_keys(k_deep, k_up, j, page[j, 0, :, here])
                    set_keys(v_deep, None, j, page[j, 1, :, here])
            acc[...] = jnp.zeros_like(acc)

        def turned_rows(head, kv, part, is_fresh, qs, gs, order):
            if is_fresh:
                for name, rows in (("qt", qs), ("gt", gs)):
                    for i, slot in enumerate(order):
                        held((name, kv))[:, head.turned_at(part, slot, 1)] = rows[
                            i * tall : (i + 1) * tall
                        ].T
            return lambda name, slot, slots: held((name, kv))[
                :, head.turned_at(part, slot, slots)
            ]

        def own_part(head, kv, part, n, stage_ref):
            order = (1, 2, 0)
            qs = head.stacked(held(("q", kv)), part, order)
            gs = head.stacked(held(("g", kv)), part, order)
            qd, gd = head.deep(qs, en, part, order), head.deep(gs, ed, part, order)
            turn = turned_rows(head, kv, part, fresh[n], qs, gs, order)
            low = lower(tall)

            def keep_first(p):
                masked = jnp.where(low, p[:tall, :PAGE], 0.0)
                return jnp.concatenate(
                    [jnp.concatenate([masked, p[:tall, PAGE:]], axis=1), p[tall:]], axis=0
                )

            pa, da = weigh(
                dot_n(qd[: 2 * tall], k_deep[:, : 2 * PAGE]),
                dot_n(gd[: 2 * tall], v_deep[:, : 2 * PAGE]),
                keep_first,
            )
            both = lambda x: jnp.concatenate([x[:tall, :PAGE], x[tall:, PAGE:]], axis=0)
            low2 = lower(2 * tall)
            pb, db = weigh(
                both(dot_n(qd[tall:], k_deep[:, 2 * PAGE :])),
                both(dot_n(gd[tall:], v_deep[:, 2 * PAGE :])),
                lambda p: jnp.where(low2, p, 0.0),
            )
            for i, (name, a, b) in enumerate((("qt", da, db), ("gt", pa, pb))):
                acc[i, :, : 2 * PAGE] += dot_n(turn(name, 1, 2), a)
                acc[i, :, cols(2, 3)] += dot_n(turn(name, 2, 1), b[:tall])
                acc[i, :, cols(3, 4)] += dot_n(turn(name, 0, 1), b[tall:])
            first = dot_n(da, k_up[: 2 * PAGE])
            put = lambda slot, rows: head.put_queries(
                part, slot, rows, held(("dq", kv)), not fresh[n], stage_ref
            )
            put(1, first[:tall])
            put(2, first[tall:] + dot_n(db[:tall], k_up[cols(2, 3)]))
            put(0, dot_n(db[tall:], k_up[cols(3, 4)]))

        def shared_part(head, kv, part, n, stage_ref):
            order = (0, 1, 2)
            qs = head.stacked(held(("q", kv)), part, order)
            gs = head.stacked(held(("g", kv)), part, order)
            qd, gd = head.deep(qs, en, part, order), head.deep(gs, ed, part, order)
            turn = turned_rows(head, kv, part, fresh[n], qs, gs, order)
            column = lax.broadcasted_iota(I32, (tall, 2 * PAGE), 1)
            seen = column < facts[LIMIT]

            def keep(p):
                return jnp.concatenate([jnp.where(seen, p[:tall], 0.0), p[tall:]], axis=0)

            p, ds = weigh(dot_n(qd, k_deep[...]), dot_n(gd, v_deep[...]), keep)
            acc[0] += dot_n(turn("qt", 0, SLOTS), ds)
            acc[1] += dot_n(turn("gt", 0, SLOTS), p)
            if not fresh[n]:
                held(("ds", kv))[part * SLOTS * tall : (part + 1) * SLOTS * tall] = ds
                return
            dq = dot_n(ds, k_up[...])
            for slot in range(SLOTS):
                head.put_queries(
                    part, slot, dq[slot * tall : (slot + 1) * tall], held(("dq", kv)), not fresh[n],
                    stage_ref,
                )

        def put_own(n):
            dk12, dv12, own0, send2 = results
            here = slice(base + n * HD, base + (n + 1) * HD)
            grad = [acc[0].T * SCALE, acc[1].T]
            for at, c, to in ((0, N1, 0), (2, N2, 1)):
                ok = row_ok(facts[c], PAGE, HD)
                for kind, out in ((0, dk12), (1, dv12)):
                    out[cols(to, to + 1), here] = jnp.where(
                        ok, grad[kind][cols(at, at + 1)], 0.0
                    ).astype(BF16)
            for kind in range(2):
                level2 = grad[kind][cols(1, 2)]
                own0[kind, :, here] = grad[kind][cols(3, 4)] + jnp.where(owns2, level2, 0.0)
                send2[kind, :, here] = level2.astype(BF16)

        def put_shared(n):
            (out,) = results
            here = slice(n * HD, (n + 1) * HD)
            grads = acc[0].T * SCALE, acc[1].T
            for j in range(2):
                for kind in range(2):
                    out[2 * j + kind, :, here] = grads[kind][cols(j, j + 1)].astype(out.dtype)

        sends = []
        for n, kv in enumerate(kvs):
            arrived(("q", kv), ("g", kv))
            head = Head(kv, group, norms, deltas, en, ed)
            set_pages(n, kv)

            for part in range(parts):
                slot = n * parts + part
                (own_part if own else shared_part)(
                    head, kv, part, n, stage.at[slot] if own and not fresh[n] else None
                )
                if own and not fresh[n]:
                    at = order.at(facts, kv, group * HD) + part * wide
                    sends.append(
                        pltpu.make_async_copy(
                            stage.at[slot],
                            held("gq").at[:, pl.ds(pl.multiple_of(at, wide), wide)],
                            sem.at[slot],
                        )
                    )
                    sends[-1].start()

            (put_own if own else put_shared)(n)
        for c in sends:
            c.wait()
        arrived(*list(copies))
        if w is not None:
            w_copy.wait()

    made = kernel_call(
        body, facts, near, far, outs, scratch, aliases, after,
        pl.CostEstimate(
            flops=240 * PAGE * PAGE * HD * group * count, bytes_accessed=1000, transcendentals=0
        ),
        LARGE,
    )
    for name, at in at_out.items():
        state[name] = made[at]
    return list(made[at_results:at_loaded]) + list(made[at_end:])


def width_tiles(w):
    tile = next(t for t in (512, 640, 320, 128, w.shape[0]) if w.shape[0] % t == 0)
    return [slice(i, i + tile) for i in range(0, w.shape[0], tile)]


def finish_queries(kvs, group, order, facts, pages, state, after=()):
    parts = group // min(4, group)
    heads = group // parts
    tall = heads * PAGE
    wide = heads * HD
    near = list(pages)
    for kv in kvs:
        near += [state["ds", kv], state["dq", kv]]

    def body(facts, *refs):
        gq, made, stage, sem = refs[-4:]
        made[...] = jnp.zeros_like(made)
        sends = []
        for n, kv in enumerate(kvs):
            ds, dq = refs[len(pages) + 2 * n : len(pages) + 2 * n + 2]
            page, at = refs[kv // order.half], kv % order.half * HD
            keys = jnp.concatenate([page[j, 0, :, at : at + HD] for j in range(2)], axis=0)
            for part in range(parts):
                at = n * parts + part
                gained = dot_n(ds[part * SLOTS * tall : (part + 1) * SLOTS * tall], keys)
                for i in range(SLOTS * heads):
                    slot, j = divmod(i, heads)
                    rows = slice(slot * PAGE, (slot + 1) * PAGE)
                    value = gained[i * PAGE : (i + 1) * PAGE] + dq[
                        rows, part * wide + j * HD : part * wide + (j + 1) * HD
                    ]
                    stage[at, rows, j * HD : (j + 1) * HD] = (value * SCALE).astype(BF16)
                to = pl.multiple_of(order.at(facts, kv, group * HD) + part * wide, wide)
                sends.append(
                    pltpu.make_async_copy(stage.at[at], gq.at[:, pl.ds(to, wide)], sem.at[at])
                )
                sends[-1].start()
        for c in sends:
            c.wait()

    count = len(kvs) * parts
    far = [state["gq"]] if "gq" in state else []
    shape = (ROWS, state["k"].shape[1] * group)
    state["gq"], made = kernel_call(
        body, facts, near, far, [(shape, BF16, False), ((8, HD), F32, True)],
        [pltpu.VMEM((count, ROWS, wide), BF16), pltpu.SemaphoreType.DMA((count,))],
        {("far", 0): 0} if far else {}, after, limit=LARGE,
    )
    return made


def input_grad(order, facts, w, rows, own, far, grads, carry=None):
    out_cols, depth = w.shape
    tiles = width_tiles(w)
    top = 0 if rows == PAGE else PAGE
    steps = len(tiles)
    width = sum(a.shape[1] for a in grads[0])
    arrays = [*own, *far, *grads[0], *grads[1]]
    count = len(grads[0])
    carry = list(carry or [])

    def body(facts, *refs):
        own_r, refs = refs[: len(own)], refs[len(own) :]
        far_r, refs = refs[: len(far)], refs[len(far) :]
        grad_r, w_ref = refs[: 2 * count], refs[2 * count]
        out, dk, dv, made, w_near, stage, w_sem, sem = refs[-8:]
        loads = [
            pltpu.make_async_copy(w_ref.at[at], w_near.at[at], w_sem.at[i])
            for i, at in enumerate(tiles)
        ]
        for c in loads:
            c.start()
        made[...] = jnp.zeros_like(made)
        columns = lambda rs: jnp.concatenate([r[...] for r in rs], axis=1)
        full = columns(own_r)
        if far:
            other, leads = columns(far_r), facts[SIDE] == 0
            full = jnp.concatenate(
                [jnp.where(leads, full, other), jnp.where(leads, other, full)], axis=1
            )
        copies = put_rows(order, facts, grad_r, dk, dv, top, rows, sem, steps)
        for i, at in enumerate(tiles):
            loads[i].wait()
            stage[i] = dot_t(w_near[at], full).astype(BF16).T
            copies.append(
                pltpu.make_async_copy(stage.at[i], out.at[top : top + rows, at], sem.at[i])
            )
            copies[-1].start()
        for c in copies:
            c.wait()

    smem = pl.BlockSpec(memory_space=pltpu.SMEM)
    vmem = pl.BlockSpec(memory_space=pltpu.VMEM)
    hbm = pl.BlockSpec(memory_space=pl.ANY)
    arrays = [pltpu.with_memory_space_constraint(a, pltpu.VMEM) for a in arrays]
    kept = jax.ShapeDtypeStruct((ROWS, width), BF16)
    return pl.pallas_call(
        body,
        out_shape=(
            jax.ShapeDtypeStruct((ROWS, out_cols), BF16), kept, kept, pltpu.VMEM((8, HD), F32)
        ),
        in_specs=[smem] + [vmem] * len(arrays) + [hbm] * (1 + len(carry)),
        out_specs=(hbm, hbm, hbm, vmem),
        scratch_shapes=[
            pltpu.VMEM(w.shape, BF16),
            pltpu.VMEM((steps, rows, out_cols // steps), BF16),
            pltpu.SemaphoreType.DMA((steps,)),
            pltpu.SemaphoreType.DMA((steps + 2 * order.heads,)),
        ],
        input_output_aliases={2 + len(arrays) + i: i for i in range(len(carry))},
        compiler_params=pltpu.CompilerParams(vmem_limit_bytes=LARGE),
        cost_estimate=SLIGHT,
    )(pltpu.with_memory_space_constraint(facts, pltpu.SMEM), *arrays, w, *carry)


def put_rows(order, facts, pieces, dk, dv, top, rows, sem, first):
    copies = []
    count = len(pieces) // 2
    for dst, mine in ((dk, pieces[:count]), (dv, pieces[count:])):
        head = 0
        for src in mine:
            more = src.shape[1] // HD
            for lo, hi in order.runs(head, head + more):
                copies.append(
                    pltpu.make_async_copy(
                        src.at[:, (lo - head) * HD : (hi - head) * HD],
                        dst.at[top : top + rows, pl.ds(order.at(facts, lo, HD), (hi - lo) * HD)],
                        sem.at[first + len(copies)],
                    )
                )
                copies[-1].start()
            head += more
    return copies


def begin_input_grad(order, facts, w, own, after=()):
    out_cols, depth = w.shape
    half = depth // 2
    rows = own[0].shape[0]
    count = len(own)

    def body(facts, w_ref, *refs):
        mine, out = jnp.concatenate([r[...] for r in refs[:count]], axis=1), refs[-1]
        mine = order.real(facts, mine)
        where = pl.ds(pl.multiple_of(facts[SIDE] * half, half), half)
        for at in width_tiles(w):
            out[at] = dot_t(w_ref[at, where], mine)

    smem = pl.BlockSpec(memory_space=pltpu.SMEM)
    vmem = pl.BlockSpec(memory_space=pltpu.VMEM)
    near = [pltpu.with_memory_space_constraint(a, pltpu.VMEM) for a in (w, *own)]

    def kernel(*refs):
        body(*refs[: 2 + count], refs[-1])

    return pl.pallas_call(
        kernel,
        out_shape=pltpu.VMEM((out_cols, rows), F32),
        in_specs=[smem] + [vmem] * len(near) + [pl.BlockSpec(memory_space=pl.ANY)] * len(after),
        out_specs=vmem,
        compiler_params=pltpu.CompilerParams(vmem_limit_bytes=LARGE),
        cost_estimate=SLIGHT,
    )(pltpu.with_memory_space_constraint(facts, pltpu.SMEM), *near, *after)


def end_input_grad(order, facts, w, far, begun, grads, carry=None, after=()):
    tiles = width_tiles(w)
    out_cols, depth = w.shape
    half = depth // 2
    steps = len(tiles)
    rows = far[0].shape[0]
    top = 0 if rows == PAGE else PAGE
    width = sum(a.shape[1] for a in grads[0])
    near = [w, begun, *far, *grads[0], *grads[1]]
    carry = list(carry or [])

    def body(facts, w_r, begun_r, *refs):
        far_r, grad_r = refs[: len(far)], refs[len(far) : len(near) - 2]
        out, dk, dv, made, stage, sem = refs[-6:]
        made[...] = jnp.zeros_like(made)
        copies = put_rows(order, facts, grad_r, dk, dv, top, rows, sem, steps)
        other = order.real(facts, jnp.concatenate([r[...] for r in far_r], axis=1))
        where = pl.ds(pl.multiple_of((1 - facts[SIDE]) * half, half), half)
        for i, at in enumerate(tiles):
            stage[i] = (dot_t(w_r[at, where], other) + begun_r[at]).astype(BF16).T
            copies.append(
                pltpu.make_async_copy(stage.at[i], out.at[top : top + rows, at], sem.at[i])
            )
            copies[-1].start()
        for c in copies:
            c.wait()

    smem = pl.BlockSpec(memory_space=pltpu.SMEM)
    vmem = pl.BlockSpec(memory_space=pltpu.VMEM)
    hbm = pl.BlockSpec(memory_space=pl.ANY)
    near = [pltpu.with_memory_space_constraint(a, pltpu.VMEM) for a in near]
    kept = jax.ShapeDtypeStruct((ROWS, width), BF16)

    def kernel(*refs):
        body(*refs[: 1 + len(near)], *refs[1 + len(near) + len(carry) + len(after) :])

    return pl.pallas_call(
        kernel,
        out_shape=(
            jax.ShapeDtypeStruct((ROWS, out_cols), BF16), kept, kept, pltpu.VMEM((8, HD), F32)
        ),
        in_specs=[smem] + [vmem] * len(near) + [hbm] * (len(carry) + len(after)),
        out_specs=(hbm, hbm, hbm, vmem),
        scratch_shapes=[
            pltpu.VMEM((steps, rows, out_cols // steps), BF16),
            pltpu.SemaphoreType.DMA((steps + 2 * order.heads,)),
        ],
        input_output_aliases={1 + len(near) + i: i for i in range(len(carry))},
        compiler_params=pltpu.CompilerParams(vmem_limit_bytes=LARGE),
        cost_estimate=SLIGHT,
    )(pltpu.with_memory_space_constraint(facts, pltpu.SMEM), *near, *carry, *after)


def flipped(block, axis, bit):
    count = lax.axis_size(axis)
    return lax.ppermute(block, axis, [(i, i ^ bit) for i in range(count) if i ^ bit < count])


def spanning(leaves, bit_index):
    return len([j for j in range(INNER) if 2 << bit_index <= leaves >> j])


def gather_small_tree(facts, own, beside_pair, beside_half):
    width = own.shape[-1] // 2
    page = ((2, PAGE, width), BF16, True)
    from_core = flipped(own, "sub", 1)

    def choose_chip(facts, own_ref, far_ref, out):
        for swap in range(2):
            for mine in range(2):

                @pl.when((facts[SWAP] == swap) & (facts[OWNS2] != mine))
                def _copy(swap=swap, mine=mine):
                    out[...] = (own_ref if mine else far_ref)[
                        :, :, swap * width : (swap + 1) * width
                    ]

    (chip,) = kernel_call(choose_chip, facts, [own, from_core], [], [page])
    from_pair = flipped(chip, "leaf", 1)

    def choose_pair(facts, near_ref, far_ref, out):
        out[...] = jnp.where(facts[ROOT_IN_CHIP] == 1, near_ref[...], far_ref[...])

    after = beside_pair(from_core, chip)
    (pair,) = kernel_call(choose_pair, facts, [chip, from_pair], [], [page], after=after)
    from_half = flipped(pair, "leaf", 2)

    def choose_all(facts, chip_ref, pair_far, pair_ref, half_far, out):
        out[0] = jnp.where(facts[ROOT_IN_PAIR] == 1, pair_ref[...], half_far[...])
        out[1] = jnp.where(facts[NEXT_IN_CHIP] == 1, chip_ref[...], pair_far[...])

    after = beside_half(pair)
    (mine,) = kernel_call(
        choose_all, facts, [chip, from_pair, pair, from_half], [],
        [((2, *page[0]), BF16, True)], after=after,
    )
    return mine, flipped(mine, "sub", 1)


def over_cores(facts, kept, far):
    width = kept.shape[-1]

    def body(_, near, away, total, root, next_one):
        for i in range(4):
            value = near[i] + away[i].astype(F32)
            total[i] = value
            (root, next_one)[i // 2][i % 2] = value.astype(BF16)

    pages = ((2, PAGE, width), BF16, True)
    total, root, next_one = kernel_call(
        body, facts, [kept, far], [], [((4, PAGE, width), F32, True), pages, pages]
    )
    return total, root, flipped(root, "leaf", 2), flipped(next_one, "leaf", 1)


def over_halves(facts, total, root_far, next_far, after):
    width = total.shape[-1]

    def body(_, near, root_r, next_r, out, low):
        root = near[:2] + root_r[...].astype(F32)
        out[:2] = root
        low[...] = root.astype(BF16)
        out[2:] = near[2:] + next_r[...].astype(F32)

    total, low = kernel_call(
        body, facts, [total, root_far, next_far], [],
        [((4, PAGE, width), F32, True), ((2, PAGE, width), BF16, True)], after=after,
    )
    return total, low, flipped(low, "leaf", 1)


def over_chips(facts, total, far, level2, after):
    width = total.shape[-1]

    def body(facts, near, away, extra, out):
        root = near[:2] + away[...].astype(F32)
        out[:, :, :width] = jnp.where(facts[ROOT_IN_CHIP] == 1, root, near[2:]).astype(BF16)
        out[:, :, width:] = extra[:, :, extra.shape[-1] - HD :]

    outs = [((2, PAGE, width + HD), BF16, True)]
    (mine,) = kernel_call(body, facts, [total, far, level2], [], outs, after=after)
    return mine, flipped(mine, "sub", 1)


def finish_small_tree(order, facts, own0, mine, far, level2_far):
    part = order.half * HD
    width = 2 * part

    def body(facts, *refs):
        mine_r, far_r, low_r, dk, dv = refs[len(own0) :]
        owns2 = facts[OWNS2] == 1
        own_r = [(r, at) for r in refs[: len(own0)] for at in range(0, r.shape[-1], HD)]
        ok = row_ok(facts[N0], PAGE, HD)
        for head in range(order.heads):
            c = slice(head * HD, (head + 1) * HD)
            at = head % order.half * HD
            here = slice(at, at + HD)
            theirs = head ^ order.half
            for kind, out in enumerate((dk, dv)):
                gained = (far_r if head < order.half else mine_r)[kind, :, here]
                ref, start_at = own_r[head]
                base = ref[kind, :, start_at : start_at + HD]
                if theirs < order.half:
                    level2 = low_r[4 + kind, :, theirs * HD : (theirs + 1) * HD]
                elif theirs + 1 < order.heads:
                    level2 = low_r[6, :, kind * HD : (kind + 1) * HD]
                else:
                    level2 = far_r[kind, :, part : part + HD]
                more = jnp.where(owns2, level2, gained).astype(F32)
                out[:, c] = jnp.where(ok, base + more, 0.0).astype(BF16)

    page = ((PAGE, width), BF16, True)
    return kernel_call(body, facts, [*own0, mine, far, level2_far], [], [page, page])


def gather_tree(ids, own):
    leaves = lax.axis_size(("leaf", "sub"))
    owned = ids[:INNER] == ids[INNER] - 1
    pages = jnp.where(owned[:, None, None, None], own[None], jnp.zeros((), BF16))
    for bit in range(leaves.bit_length() - 1):
        active = spanning(leaves, bit)
        far = flipped(pages[:active], ("leaf", "sub"), 1 << bit)
        pages = jnp.concatenate([pages[:active] + far, pages[active:]])
    return pages


def reduce_tree(ids, parts):
    leaves = lax.axis_size(("leaf", "sub"))
    for bit in range(leaves.bit_length() - 1):
        active = spanning(leaves, bit)
        far = flipped(parts[:active], ("leaf", "sub"), 1 << bit)
        parts = jnp.concatenate([parts[:active] + far, parts[active:]])
    owned = ids[:INNER] == ids[INNER] - 1
    return jnp.sum(jnp.where(owned[:, None, None, None], parts, 0.0), axis=0)


def on_device(queries, grad_out, keys, values, log_norms, row_deltas, ancestors, counts, w_value):
    kv = keys.shape[1] // HD
    group = queries.shape[1] // keys.shape[1]
    leaves = lax.axis_size(("leaf", "sub"))
    hbm = lambda a: pltpu.with_memory_space_constraint(a, pltpu.HBM)
    side = lax.axis_index("tensor").astype(I32).reshape(1)
    two_sides = lax.axis_size("tensor") == 2
    inputs = [hbm(a) for a in (queries, grad_out, keys, values, log_norms, row_deltas)]
    fast = leaves == 8 and lax.axis_size("sub") == 2 and kv == 4 and two_sides
    order = Order(fast, kv)
    facts, own = start(order, side, hbm(ancestors), hbm(counts), *inputs[2:4])
    state = {}

    def own_pages(kvs, pages, prior=(), after=(), w=None):
        return attend(
            True, kvs, group, order, facts, inputs, pages, state, prior, after, w
        )

    def shared_pages(kvs, page, ride=None, after=()):
        return attend(
            False, kvs, group, order, facts, inputs, [page], state, after=after, ride=ride
        )[0]

    def spread(part):
        if two_sides:
            return flipped(part, "tensor", 1)
        return lax.all_gather(part, "tensor", axis=1, tiled=True)

    kvs = tuple(range(kv))
    w = hbm(w_value)
    if fast:
        level2, by_head, far_v = [], [], []

        def beside_pair(from_core, chip):
            level2.extend((own, from_core))
            by_head.append(own_pages(kvs[:1], level2, after=(chip,)))
            return (by_head[0][3],)

        def beside_half(pair):
            by_head.append(own_pages(kvs[1:3], level2, by_head[0], (pair,)))
            return (by_head[1][3],)

        mine, theirs = gather_small_tree(facts, own, beside_pair, beside_half)
        most = by_head[1]
        sent = shared_pages(kvs[:2], mine, (most[3],))
        sent = flipped(sent, "sub", 1)
        kept = shared_pages(kvs[2:], theirs)
        total, root, root_far, next_far = over_cores(facts, kept, sent)
        *last, w_near = own_pages(kvs[3:], level2, most, (root,), w)
        both = [[piece] for piece in last]
        begun = begin_input_grad(order, facts, w_near, both[1])
        far_v.append(spread(last[1]))
        total, low, far = over_halves(facts, total, root_far, next_far, (begun,))
        made = finish_queries(kvs[:3], group, order, facts, (mine, theirs), state, (low,))
        near, far = over_chips(facts, total, far, last[3], (made, *far_v))
        dk0, dv0 = finish_small_tree(order, facts, both[2], near, far, sent)
        far_0 = spread(dv0)
        begun_0 = begin_input_grad(order, facts, w_near, [dv0])
        *grads, _ = end_input_grad(
            order, facts, w_near, far_v, begun, both[:2], after=(begun_0,)
        )
        grads = end_input_grad(
            order, facts, w_near, [far_0], begun_0, ([dk0], [dv0]), grads
        )
        return (state["gq"], grads[1], grads[2], grads[0])

    path_ids = ancestors[0]
    pages = gather_tree(path_ids, own)
    dk12, dv12, own0, send2 = own_pages(kvs, (pages[2], pages[2]))
    grads = shared_pages(kvs, pages[:2])
    finish_queries(kvs, group, order, facts, (pages[:2],), state)
    low = send2.astype(F32)
    total = reduce_tree(path_ids, jnp.concatenate([grads.reshape(2, 2, *grads.shape[1:]), low[None]]))
    total += own0 - jnp.where(path_ids[2] == path_ids[INNER] - 1, low, 0.0)
    has = jnp.any(path_ids[:INNER] == path_ids[INNER] - 1)
    ok = (jnp.arange(PAGE) < jnp.where(has, counts[0, 0], 0))[:, None]
    dk0, dv0 = jnp.where(ok, total, 0.0).astype(BF16)
    if two_sides:
        pair = lambda part: ([part], [spread(part)])
    else:
        pair = lambda part: ([spread(part)], [])
    *grads, _ = input_grad(order, facts, w, 2 * PAGE, *pair(dv12), ([dk12], [dv12]))
    grads = input_grad(order, facts, w, PAGE, *pair(dv0), ([dk0], [dv0]), grads)
    return (state["gq"], grads[1], grads[2], grads[0])


def solution(mesh):
    placed = (
        P(("groups", "leaf", "sub"), "tensor"),
        P(("groups", "leaf", "sub"), "tensor"),
        P(("groups", "leaf", "sub"), "tensor"),
        P(("groups", "leaf", "sub"), "tensor"),
        P("tensor", ("groups", "leaf", "sub")),
        P("tensor", ("groups", "leaf", "sub")),
        P(("groups", "leaf", "sub"), None),
        P(("groups", "leaf", "sub"), None),
        P("tensor", None),
    )
    return jax.shard_map(
        on_device,
        mesh=mesh,
        in_specs=placed,
        out_specs=(
            P(("groups", "leaf", "sub"), "tensor"),
            P(("groups", "leaf", "sub"), "tensor"),
            P(("groups", "leaf", "sub"), "tensor"),
            P(("groups", "leaf", "sub"), "tensor"),
        ),
        check_vma=False,
    )
```

```python
import math

import jax
import jax.numpy as jnp
from jax import lax
from jax.experimental import pallas as pl
from jax.experimental.pallas import tpu as pltpu
from jax.sharding import PartitionSpec as P

HD = 128
PAGE = 128
SLOTS = 3
INNER = 3
ROWS = SLOTS * PAGE
LOG2E = math.log2(math.e)
SCALE = 1.0 / math.sqrt(HD)
BF16 = jnp.bfloat16
F32 = jnp.float32
I32 = jnp.int32
LARGE = 10 << 20
SMALL = 4 << 20
SLIGHT = pl.CostEstimate(flops=1000, bytes_accessed=1000, transcendentals=0)
BLOCKED = 1e30


def dot_t(left, right):
    return lax.dot_general(left, right, (((1,), (1,)), ((), ())), preferred_element_type=F32)


def dot_n(left, right):
    return lax.dot_general(left, right, (((1,), (0,)), ((), ())), preferred_element_type=F32)


FACTS = 16
N0, N1, N2, OWNS2, LIMIT, LEADS, ROOT_IN_CHIP, ROOT_IN_PAIR, NEXT_IN_CHIP, SIDE, SWAP = range(11)


class Order:
    def __init__(self, crossed, heads):
        self.crossed, self.heads = crossed, heads
        self.half = heads // 2 if crossed else heads

    def at(self, facts, head, unit):
        if not self.crossed:
            return head * unit
        step = ((head ^ self.half) - head) * unit
        return pl.multiple_of(facts[SWAP] * step + head * unit, unit)

    def runs(self, first, last):
        cuts = [first, *(h for h in range(first + 1, last) if h % self.half == 0), last]
        return list(zip(cuts[:-1], cuts[1:]))

    def real(self, facts, rows):
        if not self.crossed:
            return rows
        width = self.half * HD
        turned = jnp.concatenate([rows[:, width:], rows[:, :width]], axis=1)
        return jnp.where(facts[SWAP] == 1, turned, rows)


def write_facts(facts, ids, counts, side, order):
    page = [ids[0, j] for j in range(INNER + 1)]
    own = page[INNER] - 1
    leaf = own // SLOTS
    owns = [page[j] == own for j in range(INNER)]
    same = lambda level, shift: ((page[level] // SLOTS) >> shift) == (leaf >> shift)
    number = lambda flag: jnp.where(flag, 1, 0)
    facts[N0] = jnp.where(owns[0] | owns[1] | owns[2], counts[0, 0], 0)
    facts[N1] = counts[0, 1]
    facts[N2] = counts[0, 2]
    facts[OWNS2] = number(owns[2])
    facts[LIMIT] = jnp.where(owns[2], 2 * PAGE, jnp.where(owns[1], PAGE, 0))
    facts[LEADS] = number(lax.rem(leaf, 2) == 0)
    facts[ROOT_IN_CHIP] = number(same(0, 1))
    facts[ROOT_IN_PAIR] = number(same(0, 2))
    facts[NEXT_IN_CHIP] = number(same(1, 1))
    facts[SIDE] = side
    facts[SWAP] = lax.rem(leaf, 2) if order.crossed else 0
    for i in range(SWAP + 1, FACTS):
        facts[i] = 0


def row_ok(count, rows, width):
    return lax.broadcasted_iota(I32, (rows, width), 0) < count


def kernel_call(body, facts, near, far, outs, scratch=(), aliases=None, after=(), cost=None,
                limit=SMALL):
    smem = pl.BlockSpec(memory_space=pltpu.SMEM)
    vmem = pl.BlockSpec(memory_space=pltpu.VMEM)
    hbm = pl.BlockSpec(memory_space=pl.ANY)
    near = [pltpu.with_memory_space_constraint(a, pltpu.VMEM) for a in near]
    place = {("near", i): 1 + i for i in range(len(near))}
    place |= {("far", i): 1 + len(near) + i for i in range(len(far))}
    used = 1 + len(near) + len(far)

    def kernel(*refs):
        body(*refs[:used], *refs[used + len(after) :])

    return pl.pallas_call(
        kernel,
        out_shape=tuple(
            pltpu.VMEM(s, d) if inside else jax.ShapeDtypeStruct(s, d) for s, d, inside in outs
        ),
        in_specs=[smem] + [vmem] * len(near) + [hbm] * (len(far) + len(after)),
        out_specs=tuple(vmem if inside else hbm for _, _, inside in outs),
        scratch_shapes=list(scratch),
        input_output_aliases={place[k]: v for k, v in (aliases or {}).items()},
        compiler_params=pltpu.CompilerParams(vmem_limit_bytes=limit),
        cost_estimate=cost or SLIGHT,
    )(pltpu.with_memory_space_constraint(facts, pltpu.SMEM), *near, *far, *after)


def start(order, side, ids, counts, keys, values):
    width = keys.shape[1]

    def body(side_ref, ids_ref, counts_ref, k_ref, v_ref, facts, out, held, ids_s, counts_s, sem):
        copies = [
            pltpu.make_async_copy(src, dst, sem.at[i])
            for i, (src, dst) in enumerate(
                (
                    (ids_ref, ids_s),
                    (counts_ref, counts_s),
                    (k_ref.at[:PAGE], held.at[0]),
                    (v_ref.at[:PAGE], held.at[1]),
                )
            )
        ]
        for c in copies:
            c.start()
        copies[0].wait()
        copies[1].wait()
        write_facts(facts, ids_s, counts_s, side_ref[0], order)
        ok = row_ok(counts_s[0, 0], PAGE, width)
        for i in range(2):
            copies[2 + i].wait()
            out[i] = jnp.where(ok, held[i], jnp.zeros((), BF16))

    smem = pl.BlockSpec(memory_space=pltpu.SMEM)
    hbm = pl.BlockSpec(memory_space=pl.ANY)
    return pl.pallas_call(
        body,
        out_shape=(pltpu.SMEM((FACTS,), I32), pltpu.VMEM((2, PAGE, width), BF16)),
        in_specs=[smem] + [hbm] * 4,
        out_specs=(smem, pl.BlockSpec(memory_space=pltpu.VMEM)),
        scratch_shapes=[
            pltpu.VMEM((2, PAGE, width), BF16),
            pltpu.SMEM(ids.shape, I32),
            pltpu.SMEM(counts.shape, I32),
            pltpu.SemaphoreType.DMA((4,)),
        ],
        compiler_params=pltpu.CompilerParams(vmem_limit_bytes=SMALL),
    )(side, ids, counts, keys, values)


def row_terms(rows):
    high = rows.astype(BF16).astype(F32)
    rest = rows - high
    middle = rest.astype(BF16).astype(F32)
    parts = [high, middle, rest - middle]
    spare = HD - 3 * rows.shape[0]
    parts.append(jnp.zeros((spare, rows.shape[1]), F32))
    return jnp.concatenate(parts, axis=0).T.astype(BF16)


class Head:
    def __init__(self, kv, group, norms, deltas, en, ed):
        self.group = group
        self.heads = min(4, group)
        self.parts = group // self.heads
        self.tall = self.heads * PAGE
        heads = slice(kv * group, (kv + 1) * group)
        en[...] = row_terms(norms[heads, :])
        ed[...] = row_terms(deltas[heads, :])

    def lanes(self, part, j):
        at = (part * self.heads + j) * HD
        return slice(at, at + HD)

    def stacked(self, ref, part, slots):
        return jnp.concatenate(
            [
                ref[slot * PAGE : (slot + 1) * PAGE, self.lanes(part, j)]
                for slot in slots
                for j in range(self.heads)
            ],
            axis=0,
        )

    def deep(self, stacked, terms, part, slots):
        column = lax.broadcasted_iota(I32, (1, HD), 1) % self.group
        picks = [
            (column == part * self.heads + j).astype(F32).astype(BF16)
            for j in range(self.heads)
        ]
        extra = [
            terms[slot * PAGE : (slot + 1) * PAGE] * pick for slot in slots for pick in picks
        ]
        return jnp.concatenate([stacked, jnp.concatenate(extra, axis=0)], axis=1)

    def turned_at(self, part, slot, count):
        at = (part * SLOTS + slot) * self.tall
        return slice(at, at + self.tall * count)

    def put_queries(self, part, slot, rows_by_head, dq, add, stage):
        rows = slice(slot * PAGE, (slot + 1) * PAGE)
        for j in range(self.heads):
            value = rows_by_head[j * PAGE : (j + 1) * PAGE]
            if stage is None:
                dq[rows, self.lanes(part, j)] = value
            else:
                if add:
                    value = value + dq[rows, self.lanes(part, j)]
                stage[rows, j * HD : (j + 1) * HD] = (value * SCALE).astype(BF16)


def set_keys(deep, upright, at, page):
    where = slice(at * PAGE, (at + 1) * PAGE)
    deep[:HD, where] = page.T
    if upright is not None:
        upright[where] = page


def weigh(scores, grads, keep):
    p = keep(jnp.exp2(scores * (SCALE * LOG2E)))
    return p.astype(BF16), (p * grads).astype(BF16)


def attend(own, kvs, group, order, facts, inputs, pages, state, prior=(), after=(),
           ride=None):
    loading = "k" not in state
    q_all, k_all = inputs[0], inputs[2]
    count = len(kvs)
    parts = group // min(4, group)
    tall = min(4, group) * PAGE
    wide = min(4, group) * HD
    width = count * HD
    base = prior[0].shape[1] if prior else 0
    kv_total = k_all.shape[1] // HD
    fresh = [("dq", kv) not in state for kv in kvs]
    one_head = (ROWS, group * HD)
    turned = ((HD, group * ROWS), BF16, True)
    shapes = {"dq": (one_head, F32, True), "qt": turned, "gt": turned}

    near, far, aliases, outs = [], [], {}, []
    at_near, at_far, at_out = {}, {}, {}

    def add_near(name, array):
        at_near[name] = len(near)
        near.append(array)

    def add_far(name, array):
        at_far[name] = len(far)
        far.append(array)

    def add_out(name, out):
        at_out[name] = len(outs)
        outs.append(out)

    for kv, is_fresh in zip(kvs, fresh):
        for name, shape in shapes.items():
            if is_fresh:
                add_out((name, kv), shape)
            elif own or name != "dq":
                add_near((name, kv), state[name, kv])
        if not own and not is_fresh:
            add_out(("ds", kv), ((group * ROWS, 2 * PAGE), BF16, True))
    if own and not all(fresh):
        add_out("gq", (q_all.shape, BF16, False))
        if "gq" in state:
            add_far("gq", state["gq"])
            aliases["far", at_far["gq"]] = at_out["gq"]
    at_results = len(outs)
    if own:
        outs += [
            ((2 * PAGE, base + width), BF16, True),
            ((2 * PAGE, base + width), BF16, True),
            ((2, PAGE, base + width), F32, True),
            ((2, PAGE, base + width), BF16, True),
        ]
    else:
        outs += [
            ((4, PAGE, width), F32, True) if ride is None else ((7, PAGE, width), BF16, True),
        ]
    at_loaded = len(outs)
    if loading:
        for name, array in zip(("q", "g", "k", "v", "norms", "deltas"), inputs):
            add_far(name, array)
            if name in ("q", "g"):
                for kv in range(kv_total):
                    add_out((name, kv), (one_head, BF16, True))
            else:
                add_out(name, (array.shape, array.dtype, True))
    else:
        for name in ("k", "v", "norms", "deltas"):
            add_near(name, state[name])
        for kv in kvs:
            for name in ("q", "g"):
                add_near((name, kv), state[name, kv])
    for i, page in enumerate(pages):
        add_near(("page", i), page)
    for i, array in enumerate(prior):
        add_near(("prior", i), array)
    for i, array in enumerate(ride or ()):
        add_near(("ride", i), array)
    key_pages = 4 if own else 2
    scratch = [
        pltpu.VMEM((2 * HD, key_pages * PAGE), BF16),
        pltpu.VMEM((2 * HD, key_pages * PAGE), BF16),
        pltpu.VMEM((key_pages * PAGE, HD), BF16),
        pltpu.VMEM((2, HD, key_pages * PAGE), F32),
        pltpu.VMEM((ROWS, HD), BF16),
        pltpu.VMEM((ROWS, HD), BF16),
        pltpu.VMEM((count * parts, ROWS, wide), BF16),
        pltpu.SemaphoreType.DMA((count * parts,)),
        pltpu.SemaphoreType.DMA((2 * kv_total + 8,)),
    ]
    cols = lambda a, b: slice(a * PAGE, b * PAGE)

    def body(facts, *refs):
        ins, out_refs = refs[: len(near) + len(far)], refs[len(near) + len(far) : -len(scratch)]
        k_deep, v_deep, k_up, acc, en, ed, stage, sem, load_sem = refs[-len(scratch) :]
        near_ref = lambda name: ins[at_near[name]]
        far_ref = lambda name: ins[len(near) + at_far[name]]
        held = lambda name: out_refs[at_out[name]] if name in at_out else near_ref(name)
        results = out_refs[at_results:at_loaded]
        copies = {}
        if loading:

            def load(key, src, dst):
                copies[key] = pltpu.make_async_copy(src, dst, load_sem.at[len(copies)])
                copies[key].start()

            for lo, hi in order.runs(0, kv_total):
                for name in ("k", "v"):
                    at = pl.ds(order.at(facts, lo, HD), (hi - lo) * HD)
                    here = slice(lo * HD, hi * HD)
                    load((name, lo), far_ref(name).at[:, at], held(name).at[:, here])
                for name in ("norms", "deltas"):
                    at = pl.ds(order.at(facts, lo, group), (hi - lo) * group)
                    here = slice(lo * group, hi * group)
                    load((name, lo), far_ref(name).at[at], held(name).at[here])
            shared_loads = list(copies)
            for kv in range(kv_total):
                at = pl.ds(order.at(facts, kv, group * HD), group * HD)
                for name in ("q", "g"):
                    load((name, kv), far_ref(name).at[:, at], held((name, kv)))
        k, v, norms, deltas = (held(name) for name in ("k", "v", "norms", "deltas"))

        def arrived(*keys):
            for key in keys:
                if key in copies:
                    copies.pop(key).wait()

        k_deep[HD:] = jnp.full((HD, key_pages * PAGE), -1.0, BF16)
        v_deep[HD:] = jnp.full((HD, key_pages * PAGE), -1.0, BF16)
        for out, i in zip(results, range(len(prior))):
            out[..., :base] = near_ref(("prior", i))[...]
        if ride is not None:
            (out,) = results
            for kind in range(2):
                more = jnp.concatenate(
                    [near_ref(("ride", i))[kind] for i in range(len(ride))], axis=1
                )
                out[4 + kind] = more[:, :width]
                out[6, :, kind * HD : (kind + 1) * HD] = more[:, width:]
        owns2 = facts[OWNS2] == 1
        if loading:
            arrived(*shared_loads)
            lane = lax.broadcasted_iota(I32, norms.shape, 1)
            limit = jnp.where(
                lane < PAGE, facts[N0], jnp.where(lane < 2 * PAGE, facts[N1], facts[N2])
            )
            norms[...] = jnp.where(lane % PAGE < limit, norms[...] * (1.0 / SCALE), BLOCKED)
        lower = lambda rows: lax.broadcasted_iota(I32, (rows, PAGE), 1) <= (
            lax.broadcasted_iota(I32, (rows, PAGE), 0) % PAGE
        )

        def set_pages(n, kv):
            lane = slice(kv * HD, (kv + 1) * HD)
            if own:
                first, second = (near_ref(("page", i)) for i in range(2))
                zero = jnp.zeros((), BF16)
                for slot, (at, c) in enumerate(((3, N0), (0, N1), (2, N2))):
                    ok = row_ok(facts[c], PAGE, HD)
                    rows = cols(slot, slot + 1)
                    set_keys(k_deep, k_up, at, jnp.where(ok, k[rows, lane], zero))
                    set_keys(v_deep, None, at, jnp.where(ok, v[rows, lane], zero))
                level2 = [jnp.where(owns2, first[i, :, lane], second[i, :, lane]) for i in (0, 1)]
                if order.crossed:
                    at = (kv ^ order.half) * HD
                    lane = slice(at, at + HD)
                    for i in range(2):
                        other = jnp.where(owns2, first[i, :, lane], second[i, :, lane])
                        level2[i] = jnp.where(facts[SWAP] == 1, other, level2[i])
                set_keys(k_deep, k_up, 1, level2[0])
                set_keys(v_deep, None, 1, level2[1])
            else:
                page = near_ref(("page", 0))
                for j in range(2):
                    here = slice(n * HD, (n + 1) * HD)
                    set_keys(k_deep, k_up, j, page[j, 0, :, here])
                    set_keys(v_deep, None, j, page[j, 1, :, here])
            acc[...] = jnp.zeros_like(acc)

        def turned_rows(head, kv, part, is_fresh, qs, gs, order):
            if is_fresh:
                for name, rows in (("qt", qs), ("gt", gs)):
                    for i, slot in enumerate(order):
                        held((name, kv))[:, head.turned_at(part, slot, 1)] = rows[
                            i * tall : (i + 1) * tall
                        ].T
            return lambda name, slot, slots: held((name, kv))[
                :, head.turned_at(part, slot, slots)
            ]

        def own_part(head, kv, part, n, stage_ref):
            order = (1, 2, 0)
            qs = head.stacked(held(("q", kv)), part, order)
            gs = head.stacked(held(("g", kv)), part, order)
            qd, gd = head.deep(qs, en, part, order), head.deep(gs, ed, part, order)
            turn = turned_rows(head, kv, part, fresh[n], qs, gs, order)
            low = lower(tall)

            def keep_first(p):
                masked = jnp.where(low, p[:tall, :PAGE], 0.0)
                return jnp.concatenate(
                    [jnp.concatenate([masked, p[:tall, PAGE:]], axis=1), p[tall:]], axis=0
                )

            pa, da = weigh(
                dot_n(qd[: 2 * tall], k_deep[:, : 2 * PAGE]),
                dot_n(gd[: 2 * tall], v_deep[:, : 2 * PAGE]),
                keep_first,
            )
            both = lambda x: jnp.concatenate([x[:tall, :PAGE], x[tall:, PAGE:]], axis=0)
            low2 = lower(2 * tall)
            pb, db = weigh(
                both(dot_n(qd[tall:], k_deep[:, 2 * PAGE :])),
                both(dot_n(gd[tall:], v_deep[:, 2 * PAGE :])),
                lambda p: jnp.where(low2, p, 0.0),
            )
            for i, (name, a, b) in enumerate((("qt", da, db), ("gt", pa, pb))):
                acc[i, :, : 2 * PAGE] += dot_n(turn(name, 1, 2), a)
                acc[i, :, cols(2, 3)] += dot_n(turn(name, 2, 1), b[:tall])
                acc[i, :, cols(3, 4)] += dot_n(turn(name, 0, 1), b[tall:])
            first = dot_n(da, k_up[: 2 * PAGE])
            put = lambda slot, rows: head.put_queries(
                part, slot, rows, held(("dq", kv)), not fresh[n], stage_ref
            )
            put(1, first[:tall])
            put(2, first[tall:] + dot_n(db[:tall], k_up[cols(2, 3)]))
            put(0, dot_n(db[tall:], k_up[cols(3, 4)]))

        def shared_part(head, kv, part, n, stage_ref):
            order = (0, 1, 2)
            qs = head.stacked(held(("q", kv)), part, order)
            gs = head.stacked(held(("g", kv)), part, order)
            qd, gd = head.deep(qs, en, part, order), head.deep(gs, ed, part, order)
            turn = turned_rows(head, kv, part, fresh[n], qs, gs, order)
            column = lax.broadcasted_iota(I32, (tall, 2 * PAGE), 1)
            seen = column < facts[LIMIT]

            def keep(p):
                return jnp.concatenate([jnp.where(seen, p[:tall], 0.0), p[tall:]], axis=0)

            p, ds = weigh(dot_n(qd, k_deep[...]), dot_n(gd, v_deep[...]), keep)
            acc[0] += dot_n(turn("qt", 0, SLOTS), ds)
            acc[1] += dot_n(turn("gt", 0, SLOTS), p)
            if not fresh[n]:
                held(("ds", kv))[part * SLOTS * tall : (part + 1) * SLOTS * tall] = ds
                return
            dq = dot_n(ds, k_up[...])
            for slot in range(SLOTS):
                head.put_queries(
                    part, slot, dq[slot * tall : (slot + 1) * tall], held(("dq", kv)), not fresh[n],
                    stage_ref,
                )

        def put_own(n):
            dk12, dv12, own0, send2 = results
            here = slice(base + n * HD, base + (n + 1) * HD)
            grad = [acc[0].T * SCALE, acc[1].T]
            for at, c, to in ((0, N1, 0), (2, N2, 1)):
                ok = row_ok(facts[c], PAGE, HD)
                for kind, out in ((0, dk12), (1, dv12)):
                    out[cols(to, to + 1), here] = jnp.where(
                        ok, grad[kind][cols(at, at + 1)], 0.0
                    ).astype(BF16)
            for kind in range(2):
                level2 = grad[kind][cols(1, 2)]
                own0[kind, :, here] = grad[kind][cols(3, 4)] + jnp.where(owns2, level2, 0.0)
                send2[kind, :, here] = level2.astype(BF16)

        def put_shared(n):
            (out,) = results
            here = slice(n * HD, (n + 1) * HD)
            grads = acc[0].T * SCALE, acc[1].T
            for j in range(2):
                for kind in range(2):
                    out[2 * j + kind, :, here] = grads[kind][cols(j, j + 1)].astype(out.dtype)

        sends = []
        for n, kv in enumerate(kvs):
            arrived(("q", kv), ("g", kv))
            head = Head(kv, group, norms, deltas, en, ed)
            set_pages(n, kv)

            for part in range(parts):
                slot = n * parts + part
                (own_part if own else shared_part)(
                    head, kv, part, n, stage.at[slot] if own and not fresh[n] else None
                )
                if own and not fresh[n]:
                    at = order.at(facts, kv, group * HD) + part * wide
                    sends.append(
                        pltpu.make_async_copy(
                            stage.at[slot],
                            held("gq").at[:, pl.ds(pl.multiple_of(at, wide), wide)],
                            sem.at[slot],
                        )
                    )
                    sends[-1].start()

            (put_own if own else put_shared)(n)
        for c in sends:
            c.wait()
        arrived(*list(copies))

    made = kernel_call(
        body, facts, near, far, outs, scratch, aliases, after,
        pl.CostEstimate(
            flops=240 * PAGE * PAGE * HD * group * count, bytes_accessed=1000, transcendentals=0
        ),
        LARGE,
    )
    for name, at in at_out.items():
        state[name] = made[at]
    return list(made[at_results:at_loaded])


def width_tiles(w):
    tile = next(t for t in (512, 640, 320, 128, w.shape[0]) if w.shape[0] % t == 0)
    return [slice(i, i + tile) for i in range(0, w.shape[0], tile)]


def finish_queries(kvs, group, order, facts, pages, state, after=(), w=None):
    parts = group // min(4, group)
    heads = group // parts
    tall = heads * PAGE
    wide = heads * HD
    near = list(pages)
    for kv in kvs:
        near += [state["ds", kv], state["dq", kv]]

    def body(facts, *refs):
        stage, sem = refs[-2:]
        if w is not None:
            gq, made, w_near = refs[-5:-2]
            w_copy = pltpu.make_async_copy(refs[-6], w_near, sem.at[len(kvs) * parts])
            w_copy.start()
        else:
            gq, made = refs[-4:-2]
        made[...] = jnp.zeros_like(made)
        sends = []
        for n, kv in enumerate(kvs):
            ds, dq = refs[len(pages) + 2 * n : len(pages) + 2 * n + 2]
            page, at = refs[kv // order.half], kv % order.half * HD
            keys = jnp.concatenate([page[j, 0, :, at : at + HD] for j in range(2)], axis=0)
            for part in range(parts):
                at = n * parts + part
                gained = dot_n(ds[part * SLOTS * tall : (part + 1) * SLOTS * tall], keys)
                for i in range(SLOTS * heads):
                    slot, j = divmod(i, heads)
                    rows = slice(slot * PAGE, (slot + 1) * PAGE)
                    value = gained[i * PAGE : (i + 1) * PAGE] + dq[
                        rows, part * wide + j * HD : part * wide + (j + 1) * HD
                    ]
                    stage[at, rows, j * HD : (j + 1) * HD] = (value * SCALE).astype(BF16)
                to = pl.multiple_of(order.at(facts, kv, group * HD) + part * wide, wide)
                sends.append(
                    pltpu.make_async_copy(stage.at[at], gq.at[:, pl.ds(to, wide)], sem.at[at])
                )
                sends[-1].start()
        for c in sends:
            c.wait()
        if w is not None:
            w_copy.wait()

    count = len(kvs) * parts
    far = [state["gq"]] if "gq" in state else []
    aliases = {("far", 0): 0} if far else {}
    shape = (ROWS, state["k"].shape[1] * group)
    outs = [(shape, BF16, False), ((8, HD), F32, True)]
    if w is not None:
        far = far + [w]
        outs.append((w.shape, w.dtype, True))
    state["gq"], *made = kernel_call(
        body, facts, near, far, outs,
        [pltpu.VMEM((count, ROWS, wide), BF16), pltpu.SemaphoreType.DMA((count + 1,))],
        aliases, after, limit=LARGE,
    )
    return made


def input_grad(order, facts, w, rows, own, far, grads, carry=None, near_w=False, after=()):
    out_cols, depth = w.shape
    tiles = width_tiles(w)
    top = 0 if rows == PAGE else PAGE
    steps = len(tiles)
    width = sum(a.shape[1] for a in grads[0])
    arrays = [*own, *far, *grads[0], *grads[1]] + [w] * near_w
    count = len(grads[0])
    carry = list(carry or [])
    lead = [] if near_w else [w]
    rest = [*lead, *carry, *after]

    def body(facts, *refs):
        own_r, refs = refs[: len(own)], refs[len(own) :]
        far_r, refs = refs[: len(far)], refs[len(far) :]
        grad_r, w_ref = refs[: 2 * count], refs[2 * count]
        out, dk, dv, made, w_near, stage, w_sem, sem = refs[-8:]
        loads = []
        if not near_w:
            loads = [
                pltpu.make_async_copy(w_ref.at[at], w_near.at[at], w_sem.at[i])
                for i, at in enumerate(tiles)
            ]
        for c in loads:
            c.start()
        made[...] = jnp.zeros_like(made)
        columns = lambda rs: jnp.concatenate([r[...] for r in rs], axis=1)
        full = order.real(facts, columns(own_r))
        if far:
            other, first = order.real(facts, columns(far_r)), facts[SIDE] == 0
            full = jnp.concatenate(
                [jnp.where(first, full, other), jnp.where(first, other, full)], axis=1
            )
        copies = put_rows(order, facts, grad_r, dk, dv, top, rows, sem, steps)
        for i, at in enumerate(tiles):
            if loads:
                loads[i].wait()
            stage[i] = dot_t((w_ref if near_w else w_near)[at], full).astype(BF16).T
            copies.append(
                pltpu.make_async_copy(stage.at[i], out.at[top : top + rows, at], sem.at[i])
            )
            copies[-1].start()
        for c in copies:
            c.wait()

    smem = pl.BlockSpec(memory_space=pltpu.SMEM)
    vmem = pl.BlockSpec(memory_space=pltpu.VMEM)
    hbm = pl.BlockSpec(memory_space=pl.ANY)
    arrays = [pltpu.with_memory_space_constraint(a, pltpu.VMEM) for a in arrays]
    kept = jax.ShapeDtypeStruct((ROWS, width), BF16)
    return pl.pallas_call(
        body,
        out_shape=(
            jax.ShapeDtypeStruct((ROWS, out_cols), BF16), kept, kept, pltpu.VMEM((8, HD), F32)
        ),
        in_specs=[smem] + [vmem] * len(arrays) + [hbm] * len(rest),
        out_specs=(hbm, hbm, hbm, vmem),
        scratch_shapes=[
            pltpu.VMEM((8, HD) if near_w else w.shape, BF16),
            pltpu.VMEM((steps, rows, out_cols // steps), BF16),
            pltpu.SemaphoreType.DMA((steps,)),
            pltpu.SemaphoreType.DMA((steps + 2 * order.heads,)),
        ],
        input_output_aliases={
            1 + len(arrays) + len(lead) + i: i for i in range(len(carry))
        },
        compiler_params=pltpu.CompilerParams(vmem_limit_bytes=LARGE),
        cost_estimate=SLIGHT,
    )(pltpu.with_memory_space_constraint(facts, pltpu.SMEM), *arrays, *rest)


def put_rows(order, facts, pieces, dk, dv, top, rows, sem, first):
    copies = []
    count = len(pieces) // 2
    for dst, mine in ((dk, pieces[:count]), (dv, pieces[count:])):
        head = 0
        for src in mine:
            more = src.shape[1] // HD
            for lo, hi in order.runs(head, head + more):
                copies.append(
                    pltpu.make_async_copy(
                        src.at[:, (lo - head) * HD : (hi - head) * HD],
                        dst.at[top : top + rows, pl.ds(order.at(facts, lo, HD), (hi - lo) * HD)],
                        sem.at[first + len(copies)],
                    )
                )
                copies[-1].start()
            head += more
    return copies


def begin_input_grad(order, facts, w, own, after=()):
    out_cols, depth = w.shape
    half = depth // 2
    rows = own[0].shape[0]
    count = len(own)

    def body(facts, w_ref, *refs):
        mine, out = jnp.concatenate([r[...] for r in refs[:count]], axis=1), refs[-1]
        mine = order.real(facts, mine)
        where = pl.ds(pl.multiple_of(facts[SIDE] * half, half), half)
        for at in width_tiles(w):
            out[at] = dot_t(w_ref[at, where], mine)

    smem = pl.BlockSpec(memory_space=pltpu.SMEM)
    vmem = pl.BlockSpec(memory_space=pltpu.VMEM)
    near = [pltpu.with_memory_space_constraint(a, pltpu.VMEM) for a in (w, *own)]

    def kernel(*refs):
        body(*refs[: 2 + count], refs[-1])

    return pl.pallas_call(
        kernel,
        out_shape=pltpu.VMEM((out_cols, rows), F32),
        in_specs=[smem] + [vmem] * len(near) + [pl.BlockSpec(memory_space=pl.ANY)] * len(after),
        out_specs=vmem,
        compiler_params=pltpu.CompilerParams(vmem_limit_bytes=LARGE),
        cost_estimate=SLIGHT,
    )(pltpu.with_memory_space_constraint(facts, pltpu.SMEM), *near, *after)


def end_input_grad(order, facts, w, far, begun, grads, carry=None, after=()):
    tiles = width_tiles(w)
    out_cols, depth = w.shape
    half = depth // 2
    steps = len(tiles)
    rows = far[0].shape[0]
    top = 0 if rows == PAGE else PAGE
    width = sum(a.shape[1] for a in grads[0])
    near = [w, begun, *far, *grads[0], *grads[1]]
    carry = list(carry or [])

    def body(facts, w_r, begun_r, *refs):
        far_r, grad_r = refs[: len(far)], refs[len(far) : len(near) - 2]
        out, dk, dv, made, stage, sem = refs[-6:]
        made[...] = jnp.zeros_like(made)
        copies = put_rows(order, facts, grad_r, dk, dv, top, rows, sem, steps)
        other = order.real(facts, jnp.concatenate([r[...] for r in far_r], axis=1))
        where = pl.ds(pl.multiple_of((1 - facts[SIDE]) * half, half), half)
        for i, at in enumerate(tiles):
            stage[i] = (dot_t(w_r[at, where], other) + begun_r[at]).astype(BF16).T
            copies.append(
                pltpu.make_async_copy(stage.at[i], out.at[top : top + rows, at], sem.at[i])
            )
            copies[-1].start()
        for c in copies:
            c.wait()

    smem = pl.BlockSpec(memory_space=pltpu.SMEM)
    vmem = pl.BlockSpec(memory_space=pltpu.VMEM)
    hbm = pl.BlockSpec(memory_space=pl.ANY)
    near = [pltpu.with_memory_space_constraint(a, pltpu.VMEM) for a in near]
    kept = jax.ShapeDtypeStruct((ROWS, width), BF16)

    def kernel(*refs):
        body(*refs[: 1 + len(near)], *refs[1 + len(near) + len(carry) + len(after) :])

    return pl.pallas_call(
        kernel,
        out_shape=(
            jax.ShapeDtypeStruct((ROWS, out_cols), BF16), kept, kept, pltpu.VMEM((8, HD), F32)
        ),
        in_specs=[smem] + [vmem] * len(near) + [hbm] * (len(carry) + len(after)),
        out_specs=(hbm, hbm, hbm, vmem),
        scratch_shapes=[
            pltpu.VMEM((steps, rows, out_cols // steps), BF16),
            pltpu.SemaphoreType.DMA((steps + 2 * order.heads,)),
        ],
        input_output_aliases={1 + len(near) + i: i for i in range(len(carry))},
        compiler_params=pltpu.CompilerParams(vmem_limit_bytes=LARGE),
        cost_estimate=SLIGHT,
    )(pltpu.with_memory_space_constraint(facts, pltpu.SMEM), *near, *carry, *after)


def flipped(block, axis, bit):
    count = lax.axis_size(axis)
    return lax.ppermute(block, axis, [(i, i ^ bit) for i in range(count) if i ^ bit < count])


def spanning(leaves, bit_index):
    return len([j for j in range(INNER) if 2 << bit_index <= leaves >> j])


def gather_small_tree(facts, own, beside_pair, beside_half):
    width = own.shape[-1] // 2
    page = ((2, PAGE, width), BF16, True)
    from_core = flipped(own, "sub", 1)

    def choose_chip(facts, own_ref, far_ref, out):
        for swap in range(2):
            for mine in range(2):

                @pl.when((facts[SWAP] == swap) & (facts[OWNS2] != mine))
                def _copy(swap=swap, mine=mine):
                    out[...] = (own_ref if mine else far_ref)[
                        :, :, swap * width : (swap + 1) * width
                    ]

    (chip,) = kernel_call(choose_chip, facts, [own, from_core], [], [page])
    from_pair = flipped(chip, "leaf", 1)

    def choose_pair(facts, near_ref, far_ref, out):
        out[...] = jnp.where(facts[ROOT_IN_CHIP] == 1, near_ref[...], far_ref[...])

    after = beside_pair(from_core, chip)
    (pair,) = kernel_call(choose_pair, facts, [chip, from_pair], [], [page], after=after)
    from_half = flipped(pair, "leaf", 2)

    def choose_all(facts, chip_ref, pair_far, pair_ref, half_far, out):
        out[0] = jnp.where(facts[ROOT_IN_PAIR] == 1, pair_ref[...], half_far[...])
        out[1] = jnp.where(facts[NEXT_IN_CHIP] == 1, chip_ref[...], pair_far[...])

    after = beside_half(pair)
    (mine,) = kernel_call(
        choose_all, facts, [chip, from_pair, pair, from_half], [],
        [((2, *page[0]), BF16, True)], after=after,
    )
    return mine, flipped(mine, "sub", 1)


def over_cores(facts, kept, far):
    width = kept.shape[-1]

    def body(_, near, away, total, root, next_one):
        for i in range(4):
            value = near[i] + away[i].astype(F32)
            total[i] = value
            (root, next_one)[i // 2][i % 2] = value.astype(BF16)

    pages = ((2, PAGE, width), BF16, True)
    total, root, next_one = kernel_call(
        body, facts, [kept, far], [], [((4, PAGE, width), F32, True), pages, pages]
    )
    return total, root, flipped(root, "leaf", 2), flipped(next_one, "leaf", 1)


def over_halves(facts, total, root_far, next_far, after):
    width = total.shape[-1]

    def body(_, near, root_r, next_r, out, low):
        root = near[:2] + root_r[...].astype(F32)
        out[:2] = root
        low[...] = root.astype(BF16)
        out[2:] = near[2:] + next_r[...].astype(F32)

    total, low = kernel_call(
        body, facts, [total, root_far, next_far], [],
        [((4, PAGE, width), F32, True), ((2, PAGE, width), BF16, True)], after=after,
    )
    return total, low, flipped(low, "leaf", 1)


def over_chips(facts, total, far, level2, after):
    width = total.shape[-1]

    def body(facts, near, away, extra, out):
        root = near[:2] + away[...].astype(F32)
        out[:, :, :width] = jnp.where(facts[ROOT_IN_CHIP] == 1, root, near[2:]).astype(BF16)
        out[:, :, width:] = extra[:, :, extra.shape[-1] - HD :]

    outs = [((2, PAGE, width + HD), BF16, True)]
    (mine,) = kernel_call(body, facts, [total, far, level2], [], outs, after=after)
    return mine, flipped(mine, "sub", 1)


def finish_small_tree(order, facts, own0, mine, far, level2_far):
    part = order.half * HD
    width = 2 * part

    def body(facts, *refs):
        mine_r, far_r, low_r, dk, dv = refs[len(own0) :]
        owns2 = facts[OWNS2] == 1
        own_r = [(r, at) for r in refs[: len(own0)] for at in range(0, r.shape[-1], HD)]
        ok = row_ok(facts[N0], PAGE, HD)
        for head in range(order.heads):
            c = slice(head * HD, (head + 1) * HD)
            at = head % order.half * HD
            here = slice(at, at + HD)
            theirs = head ^ order.half
            for kind, out in enumerate((dk, dv)):
                gained = (far_r if head < order.half else mine_r)[kind, :, here]
                ref, start_at = own_r[head]
                base = ref[kind, :, start_at : start_at + HD]
                if theirs < order.half:
                    level2 = low_r[4 + kind, :, theirs * HD : (theirs + 1) * HD]
                elif theirs + 1 < order.heads:
                    level2 = low_r[6, :, kind * HD : (kind + 1) * HD]
                else:
                    level2 = far_r[kind, :, part : part + HD]
                more = jnp.where(owns2, level2, gained).astype(F32)
                out[:, c] = jnp.where(ok, base + more, 0.0).astype(BF16)

    page = ((PAGE, width), BF16, True)
    return kernel_call(body, facts, [*own0, mine, far, level2_far], [], [page, page])


def gather_tree(ids, own):
    leaves = lax.axis_size(("leaf", "sub"))
    owned = ids[:INNER] == ids[INNER] - 1
    pages = jnp.where(owned[:, None, None, None], own[None], jnp.zeros((), BF16))
    for bit in range(leaves.bit_length() - 1):
        active = spanning(leaves, bit)
        far = flipped(pages[:active], ("leaf", "sub"), 1 << bit)
        pages = jnp.concatenate([pages[:active] + far, pages[active:]])
    return pages


def reduce_tree(ids, parts):
    leaves = lax.axis_size(("leaf", "sub"))
    for bit in range(leaves.bit_length() - 1):
        active = spanning(leaves, bit)
        far = flipped(parts[:active], ("leaf", "sub"), 1 << bit)
        parts = jnp.concatenate([parts[:active] + far, parts[active:]])
    owned = ids[:INNER] == ids[INNER] - 1
    return jnp.sum(jnp.where(owned[:, None, None, None], parts, 0.0), axis=0)


def on_device(queries, grad_out, keys, values, log_norms, row_deltas, ancestors, counts, w_value):
    kv = keys.shape[1] // HD
    group = queries.shape[1] // keys.shape[1]
    leaves = lax.axis_size(("leaf", "sub"))
    hbm = lambda a: pltpu.with_memory_space_constraint(a, pltpu.HBM)
    side = lax.axis_index("tensor").astype(I32).reshape(1)
    two_sides = lax.axis_size("tensor") == 2
    inputs = [hbm(a) for a in (queries, grad_out, keys, values, log_norms, row_deltas)]
    fast = leaves == 8 and lax.axis_size("sub") == 2 and kv == 4 and two_sides
    order = Order(fast, kv)
    facts, own = start(order, side, hbm(ancestors), hbm(counts), *inputs[2:4])
    state = {}

    def own_pages(kvs, pages, prior=(), after=()):
        return attend(True, kvs, group, order, facts, inputs, pages, state, prior, after)

    def shared_pages(kvs, page, ride=None, after=()):
        return attend(
            False, kvs, group, order, facts, inputs, [page], state, after=after, ride=ride
        )[0]

    def spread(part):
        if two_sides:
            return flipped(part, "tensor", 1)
        return lax.all_gather(part, "tensor", axis=1, tiled=True)

    kvs = tuple(range(kv))
    w = hbm(w_value)
    if fast:
        level2, by_head = [], []

        def beside_pair(from_core, chip):
            level2.extend((own, from_core))
            by_head.append(own_pages(kvs[:1], level2, after=(chip,)))
            return (by_head[0][3],)

        def beside_half(pair):
            by_head.append(own_pages(kvs[1:3], level2, by_head[0], (pair,)))
            return (by_head[1][3],)

        mine, theirs = gather_small_tree(facts, own, beside_pair, beside_half)
        most = by_head[1]
        sent = shared_pages(kvs[:2], mine, (most[3],))
        sent = flipped(sent, "sub", 1)
        kept = shared_pages(kvs[2:], theirs)
        total, root, root_far, next_far = over_cores(facts, kept, sent)
        dk12, dv12, own0, send2 = own_pages(kvs[3:], level2, most, (root,))
        far_v = spread(dv12)
        total, low, far = over_halves(facts, total, root_far, next_far, (send2,))
        made, w_near = finish_queries(
            kvs[:3], group, order, facts, (mine, theirs), state, (low,), w
        )
        near, far = over_chips(facts, total, far, send2, (made, far_v))
        dk0, dv0 = finish_small_tree(order, facts, [own0], near, far, sent)
        far_0 = spread(dv0)
        begun = begin_input_grad(order, facts, w_near, [dv0])
        *grads, _ = input_grad(
            order, facts, w_near, 2 * PAGE, [dv12], [far_v], ([dk12], [dv12]), near_w=True,
            after=(begun,),
        )
        grads = end_input_grad(order, facts, w_near, [far_0], begun, ([dk0], [dv0]), grads)
        return (state["gq"], grads[1], grads[2], grads[0])

    path_ids = ancestors[0]
    pages = gather_tree(path_ids, own)
    dk12, dv12, own0, send2 = own_pages(kvs, (pages[2], pages[2]))
    grads = shared_pages(kvs, pages[:2])
    finish_queries(kvs, group, order, facts, (pages[:2],), state)
    low = send2.astype(F32)
    total = reduce_tree(path_ids, jnp.concatenate([grads.reshape(2, 2, *grads.shape[1:]), low[None]]))
    total += own0 - jnp.where(path_ids[2] == path_ids[INNER] - 1, low, 0.0)
    has = jnp.any(path_ids[:INNER] == path_ids[INNER] - 1)
    ok = (jnp.arange(PAGE) < jnp.where(has, counts[0, 0], 0))[:, None]
    dk0, dv0 = jnp.where(ok, total, 0.0).astype(BF16)
    if two_sides:
        pair = lambda part: ([part], [spread(part)])
    else:
        pair = lambda part: ([spread(part)], [])
    *grads, _ = input_grad(order, facts, w, 2 * PAGE, *pair(dv12), ([dk12], [dv12]))
    grads = input_grad(order, facts, w, PAGE, *pair(dv0), ([dk0], [dv0]), grads)
    return (state["gq"], grads[1], grads[2], grads[0])


def solution(mesh):
    placed = (
        P(("groups", "leaf", "sub"), "tensor"),
        P(("groups", "leaf", "sub"), "tensor"),
        P(("groups", "leaf", "sub"), "tensor"),
        P(("groups", "leaf", "sub"), "tensor"),
        P("tensor", ("groups", "leaf", "sub")),
        P("tensor", ("groups", "leaf", "sub")),
        P(("groups", "leaf", "sub"), None),
        P(("groups", "leaf", "sub"), None),
        P("tensor", None),
    )
    return jax.shard_map(
        on_device,
        mesh=mesh,
        in_specs=placed,
        out_specs=(
            P(("groups", "leaf", "sub"), "tensor"),
            P(("groups", "leaf", "sub"), "tensor"),
            P(("groups", "leaf", "sub"), "tensor"),
            P(("groups", "leaf", "sub"), "tensor"),
        ),
        check_vma=False,
    )
```

```python
import math

import jax
import jax.numpy as jnp
from jax import lax
from jax.experimental import pallas as pl
from jax.experimental.pallas import tpu as pltpu
from jax.sharding import PartitionSpec as P

HD = 128
PAGE = 128
SLOTS = 3
INNER = 3
ROWS = SLOTS * PAGE
LOG2E = math.log2(math.e)
SCALE = 1.0 / math.sqrt(HD)
BF16 = jnp.bfloat16
F32 = jnp.float32
I32 = jnp.int32
LARGE = 10 << 20
SMALL = 4 << 20
SLIGHT = pl.CostEstimate(flops=1000, bytes_accessed=1000, transcendentals=0)
BLOCKED = 1e30


def dot_t(left, right):
    return lax.dot_general(left, right, (((1,), (1,)), ((), ())), preferred_element_type=F32)


def dot_n(left, right):
    return lax.dot_general(left, right, (((1,), (0,)), ((), ())), preferred_element_type=F32)


FACTS = 16
N0, N1, N2, OWNS2, LIMIT, LEADS, ROOT_IN_CHIP, ROOT_IN_PAIR, NEXT_IN_CHIP, SIDE, SWAP = range(11)


class Order:
    def __init__(self, crossed, heads):
        self.crossed, self.heads = crossed, heads
        self.half = heads // 2 if crossed else heads

    def at(self, facts, head, unit):
        if not self.crossed:
            return head * unit
        step = ((head ^ self.half) - head) * unit
        return pl.multiple_of(facts[SWAP] * step + head * unit, unit)

    def runs(self, first, last):
        cuts = [first, *(h for h in range(first + 1, last) if h % self.half == 0), last]
        return list(zip(cuts[:-1], cuts[1:]))

    def real(self, facts, rows):
        if not self.crossed:
            return rows
        width = self.half * HD
        turned = jnp.concatenate([rows[:, width:], rows[:, :width]], axis=1)
        return jnp.where(facts[SWAP] == 1, turned, rows)


def write_facts(facts, ids, counts, side, order):
    page = [ids[0, j] for j in range(INNER + 1)]
    own = page[INNER] - 1
    leaf = own // SLOTS
    owns = [page[j] == own for j in range(INNER)]
    same = lambda level, shift: ((page[level] // SLOTS) >> shift) == (leaf >> shift)
    number = lambda flag: jnp.where(flag, 1, 0)
    facts[N0] = jnp.where(owns[0] | owns[1] | owns[2], counts[0, 0], 0)
    facts[N1] = counts[0, 1]
    facts[N2] = counts[0, 2]
    facts[OWNS2] = number(owns[2])
    facts[LIMIT] = jnp.where(owns[2], 2 * PAGE, jnp.where(owns[1], PAGE, 0))
    facts[LEADS] = number(lax.rem(leaf, 2) == 0)
    facts[ROOT_IN_CHIP] = number(same(0, 1))
    facts[ROOT_IN_PAIR] = number(same(0, 2))
    facts[NEXT_IN_CHIP] = number(same(1, 1))
    facts[SIDE] = side
    facts[SWAP] = lax.rem(leaf, 2) if order.crossed else 0
    for i in range(SWAP + 1, FACTS):
        facts[i] = 0


def row_ok(count, rows, width):
    return lax.broadcasted_iota(I32, (rows, width), 0) < count


def kernel_call(body, facts, near, far, outs, scratch=(), aliases=None, after=(), cost=None,
                limit=SMALL):
    smem = pl.BlockSpec(memory_space=pltpu.SMEM)
    vmem = pl.BlockSpec(memory_space=pltpu.VMEM)
    hbm = pl.BlockSpec(memory_space=pl.ANY)
    near = [pltpu.with_memory_space_constraint(a, pltpu.VMEM) for a in near]
    place = {("near", i): 1 + i for i in range(len(near))}
    place |= {("far", i): 1 + len(near) + i for i in range(len(far))}
    used = 1 + len(near) + len(far)

    def kernel(*refs):
        body(*refs[:used], *refs[used + len(after) :])

    return pl.pallas_call(
        kernel,
        out_shape=tuple(
            pltpu.VMEM(s, d) if inside else jax.ShapeDtypeStruct(s, d) for s, d, inside in outs
        ),
        in_specs=[smem] + [vmem] * len(near) + [hbm] * (len(far) + len(after)),
        out_specs=tuple(vmem if inside else hbm for _, _, inside in outs),
        scratch_shapes=list(scratch),
        input_output_aliases={place[k]: v for k, v in (aliases or {}).items()},
        compiler_params=pltpu.CompilerParams(vmem_limit_bytes=limit),
        cost_estimate=cost or SLIGHT,
    )(pltpu.with_memory_space_constraint(facts, pltpu.SMEM), *near, *far, *after)


def start(order, side, ids, counts, keys, values):
    width = keys.shape[1]

    def body(side_ref, ids_ref, counts_ref, k_ref, v_ref, facts, out, held, ids_s, counts_s, sem):
        copies = [
            pltpu.make_async_copy(src, dst, sem.at[i])
            for i, (src, dst) in enumerate(
                (
                    (ids_ref, ids_s),
                    (counts_ref, counts_s),
                    (k_ref.at[:PAGE], held.at[0]),
                    (v_ref.at[:PAGE], held.at[1]),
                )
            )
        ]
        for c in copies:
            c.start()
        copies[0].wait()
        copies[1].wait()
        write_facts(facts, ids_s, counts_s, side_ref[0], order)
        ok = row_ok(counts_s[0, 0], PAGE, width)
        for i in range(2):
            copies[2 + i].wait()
            out[i] = jnp.where(ok, held[i], jnp.zeros((), BF16))

    smem = pl.BlockSpec(memory_space=pltpu.SMEM)
    hbm = pl.BlockSpec(memory_space=pl.ANY)
    return pl.pallas_call(
        body,
        out_shape=(pltpu.SMEM((FACTS,), I32), pltpu.VMEM((2, PAGE, width), BF16)),
        in_specs=[smem] + [hbm] * 4,
        out_specs=(smem, pl.BlockSpec(memory_space=pltpu.VMEM)),
        scratch_shapes=[
            pltpu.VMEM((2, PAGE, width), BF16),
            pltpu.SMEM(ids.shape, I32),
            pltpu.SMEM(counts.shape, I32),
            pltpu.SemaphoreType.DMA((4,)),
        ],
        compiler_params=pltpu.CompilerParams(vmem_limit_bytes=SMALL),
    )(side, ids, counts, keys, values)


def row_terms(rows):
    high = rows.astype(BF16).astype(F32)
    rest = rows - high
    middle = rest.astype(BF16).astype(F32)
    parts = [high, middle, rest - middle]
    spare = HD - 3 * rows.shape[0]
    parts.append(jnp.zeros((spare, rows.shape[1]), F32))
    return jnp.concatenate(parts, axis=0).T.astype(BF16)


class Head:
    def __init__(self, kv, group, norms, deltas, en, ed):
        self.group = group
        self.heads = min(4, group)
        self.parts = group // self.heads
        self.tall = self.heads * PAGE
        heads = slice(kv * group, (kv + 1) * group)
        en[...] = row_terms(norms[heads, :])
        ed[...] = row_terms(deltas[heads, :])

    def lanes(self, part, j):
        at = (part * self.heads + j) * HD
        return slice(at, at + HD)

    def stacked(self, ref, part, slots):
        return jnp.concatenate(
            [
                ref[slot * PAGE : (slot + 1) * PAGE, self.lanes(part, j)]
                for slot in slots
                for j in range(self.heads)
            ],
            axis=0,
        )

    def deep(self, stacked, terms, part, slots):
        column = lax.broadcasted_iota(I32, (1, HD), 1) % self.group
        picks = [
            (column == part * self.heads + j).astype(F32).astype(BF16)
            for j in range(self.heads)
        ]
        extra = [
            terms[slot * PAGE : (slot + 1) * PAGE] * pick for slot in slots for pick in picks
        ]
        return jnp.concatenate([stacked, jnp.concatenate(extra, axis=0)], axis=1)

    def turned_at(self, part, slot, count):
        at = (part * SLOTS + slot) * self.tall
        return slice(at, at + self.tall * count)

    def put_queries(self, part, slot, rows_by_head, dq, add, stage):
        rows = slice(slot * PAGE, (slot + 1) * PAGE)
        for j in range(self.heads):
            value = rows_by_head[j * PAGE : (j + 1) * PAGE]
            if stage is None:
                dq[rows, self.lanes(part, j)] = value
            else:
                if add:
                    value = value + dq[rows, self.lanes(part, j)]
                stage[rows, j * HD : (j + 1) * HD] = (value * SCALE).astype(BF16)


def set_keys(deep, upright, at, page):
    where = slice(at * PAGE, (at + 1) * PAGE)
    deep[:HD, where] = page.T
    if upright is not None:
        upright[where] = page


def weigh(scores, grads, keep):
    p = keep(jnp.exp2(scores * (SCALE * LOG2E)))
    return p.astype(BF16), (p * grads).astype(BF16)


def attend(own, kvs, group, order, facts, inputs, pages, state, prior=(), after=(),
           ride=None):
    loading = "k" not in state
    q_all, k_all = inputs[0], inputs[2]
    count = len(kvs)
    parts = group // min(4, group)
    tall = min(4, group) * PAGE
    wide = min(4, group) * HD
    width = count * HD
    base = prior[0].shape[1] if prior else 0
    kv_total = k_all.shape[1] // HD
    fresh = [("dq", kv) not in state for kv in kvs]
    one_head = (ROWS, group * HD)
    turned = ((HD, group * ROWS), BF16, True)
    shapes = {"dq": (one_head, F32, True), "qt": turned, "gt": turned}

    near, far, aliases, outs = [], [], {}, []
    at_near, at_far, at_out = {}, {}, {}

    def add_near(name, array):
        at_near[name] = len(near)
        near.append(array)

    def add_far(name, array):
        at_far[name] = len(far)
        far.append(array)

    def add_out(name, out):
        at_out[name] = len(outs)
        outs.append(out)

    for kv, is_fresh in zip(kvs, fresh):
        for name, shape in shapes.items():
            if is_fresh:
                add_out((name, kv), shape)
            elif own or name != "dq":
                add_near((name, kv), state[name, kv])
        if not own and not is_fresh:
            add_out(("ds", kv), ((group * ROWS, 2 * PAGE), BF16, True))
    if own and not all(fresh):
        add_out("gq", (q_all.shape, BF16, False))
        if "gq" in state:
            add_far("gq", state["gq"])
            aliases["far", at_far["gq"]] = at_out["gq"]
    at_results = len(outs)
    if own:
        outs += [
            ((2 * PAGE, base + width), BF16, True),
            ((2 * PAGE, base + width), BF16, True),
            ((2, PAGE, base + width), F32, True),
            ((2, PAGE, base + width), BF16, True),
        ]
    else:
        outs += [
            ((4, PAGE, width), F32, True) if ride is None else ((8, PAGE, width), BF16, True),
        ]
    at_loaded = len(outs)
    if loading:
        for name, array in zip(("q", "g", "k", "v", "norms", "deltas"), inputs):
            add_far(name, array)
            if name in ("q", "g"):
                for kv in range(kv_total):
                    add_out((name, kv), (one_head, BF16, True))
            else:
                add_out(name, (array.shape, array.dtype, True))
    else:
        for name in ("k", "v", "norms", "deltas"):
            add_near(name, state[name])
        for kv in kvs:
            for name in ("q", "g"):
                add_near((name, kv), state[name, kv])
    for i, page in enumerate(pages):
        add_near(("page", i), page)
    for i, array in enumerate(prior):
        add_near(("prior", i), array)
    if ride is not None:
        add_near("ride", ride)
    key_pages = 4 if own else 2
    scratch = [
        pltpu.VMEM((2 * HD, key_pages * PAGE), BF16),
        pltpu.VMEM((2 * HD, key_pages * PAGE), BF16),
        pltpu.VMEM((key_pages * PAGE, HD), BF16),
        pltpu.VMEM((2, HD, key_pages * PAGE), F32),
        pltpu.VMEM((ROWS, HD), BF16),
        pltpu.VMEM((ROWS, HD), BF16),
        pltpu.VMEM((count * parts, ROWS, wide), BF16),
        pltpu.SemaphoreType.DMA((count * parts,)),
        pltpu.SemaphoreType.DMA((2 * kv_total + 8,)),
    ]
    cols = lambda a, b: slice(a * PAGE, b * PAGE)

    def body(facts, *refs):
        ins, out_refs = refs[: len(near) + len(far)], refs[len(near) + len(far) : -len(scratch)]
        k_deep, v_deep, k_up, acc, en, ed, stage, sem, load_sem = refs[-len(scratch) :]
        near_ref = lambda name: ins[at_near[name]]
        far_ref = lambda name: ins[len(near) + at_far[name]]
        held = lambda name: out_refs[at_out[name]] if name in at_out else near_ref(name)
        results = out_refs[at_results:at_loaded]
        copies = {}
        if loading:

            def load(key, src, dst):
                copies[key] = pltpu.make_async_copy(src, dst, load_sem.at[len(copies)])
                copies[key].start()

            for lo, hi in order.runs(0, kv_total):
                for name in ("k", "v"):
                    at = pl.ds(order.at(facts, lo, HD), (hi - lo) * HD)
                    here = slice(lo * HD, hi * HD)
                    load((name, lo), far_ref(name).at[:, at], held(name).at[:, here])
                for name in ("norms", "deltas"):
                    at = pl.ds(order.at(facts, lo, group), (hi - lo) * group)
                    here = slice(lo * group, hi * group)
                    load((name, lo), far_ref(name).at[at], held(name).at[here])
            shared_loads = list(copies)
            for kv in range(kv_total):
                at = pl.ds(order.at(facts, kv, group * HD), group * HD)
                for name in ("q", "g"):
                    load((name, kv), far_ref(name).at[:, at], held((name, kv)))
        k, v, norms, deltas = (held(name) for name in ("k", "v", "norms", "deltas"))

        def arrived(*keys):
            for key in keys:
                if key in copies:
                    copies.pop(key).wait()

        k_deep[HD:] = jnp.full((HD, key_pages * PAGE), -1.0, BF16)
        v_deep[HD:] = jnp.full((HD, key_pages * PAGE), -1.0, BF16)
        for out, i in zip(results, range(len(prior))):
            out[..., :base] = near_ref(("prior", i))[...]
        if ride is not None:
            (out,), more = results, near_ref("ride")
            for kind in range(2):
                out[4 + kind] = more[kind, :, :width]
                out[6 + kind] = more[kind, :, width:]
        owns2 = facts[OWNS2] == 1
        if loading:
            arrived(*shared_loads)
            lane = lax.broadcasted_iota(I32, norms.shape, 1)
            limit = jnp.where(
                lane < PAGE, facts[N0], jnp.where(lane < 2 * PAGE, facts[N1], facts[N2])
            )
            norms[...] = jnp.where(lane % PAGE < limit, norms[...] * (1.0 / SCALE), BLOCKED)
        lower = lambda rows: lax.broadcasted_iota(I32, (rows, PAGE), 1) <= (
            lax.broadcasted_iota(I32, (rows, PAGE), 0) % PAGE
        )

        def set_pages(n, kv):
            lane = slice(kv * HD, (kv + 1) * HD)
            if own:
                first, second = (near_ref(("page", i)) for i in range(2))
                zero = jnp.zeros((), BF16)
                for slot, (at, c) in enumerate(((3, N0), (0, N1), (2, N2))):
                    ok = row_ok(facts[c], PAGE, HD)
                    rows = cols(slot, slot + 1)
                    set_keys(k_deep, k_up, at, jnp.where(ok, k[rows, lane], zero))
                    set_keys(v_deep, None, at, jnp.where(ok, v[rows, lane], zero))
                level2 = [jnp.where(owns2, first[i, :, lane], second[i, :, lane]) for i in (0, 1)]
                if order.crossed:
                    at = (kv ^ order.half) * HD
                    lane = slice(at, at + HD)
                    for i in range(2):
                        other = jnp.where(owns2, first[i, :, lane], second[i, :, lane])
                        level2[i] = jnp.where(facts[SWAP] == 1, other, level2[i])
                set_keys(k_deep, k_up, 1, level2[0])
                set_keys(v_deep, None, 1, level2[1])
            else:
                page = near_ref(("page", 0))
                for j in range(2):
                    here = slice(n * HD, (n + 1) * HD)
                    set_keys(k_deep, k_up, j, page[j, 0, :, here])
                    set_keys(v_deep, None, j, page[j, 1, :, here])
            acc[...] = jnp.zeros_like(acc)

        def turned_rows(head, kv, part, is_fresh, qs, gs, order):
            if is_fresh:
                for name, rows in (("qt", qs), ("gt", gs)):
                    for i, slot in enumerate(order):
                        held((name, kv))[:, head.turned_at(part, slot, 1)] = rows[
                            i * tall : (i + 1) * tall
                        ].T
            return lambda name, slot, slots: held((name, kv))[
                :, head.turned_at(part, slot, slots)
            ]

        def own_part(head, kv, part, n, stage_ref):
            order = (1, 2, 0)
            qs = head.stacked(held(("q", kv)), part, order)
            gs = head.stacked(held(("g", kv)), part, order)
            qd, gd = head.deep(qs, en, part, order), head.deep(gs, ed, part, order)
            turn = turned_rows(head, kv, part, fresh[n], qs, gs, order)
            low = lower(tall)

            def keep_first(p):
                masked = jnp.where(low, p[:tall, :PAGE], 0.0)
                return jnp.concatenate(
                    [jnp.concatenate([masked, p[:tall, PAGE:]], axis=1), p[tall:]], axis=0
                )

            pa, da = weigh(
                dot_n(qd[: 2 * tall], k_deep[:, : 2 * PAGE]),
                dot_n(gd[: 2 * tall], v_deep[:, : 2 * PAGE]),
                keep_first,
            )
            both = lambda x: jnp.concatenate([x[:tall, :PAGE], x[tall:, PAGE:]], axis=0)
            low2 = lower(2 * tall)
            pb, db = weigh(
                both(dot_n(qd[tall:], k_deep[:, 2 * PAGE :])),
                both(dot_n(gd[tall:], v_deep[:, 2 * PAGE :])),
                lambda p: jnp.where(low2, p, 0.0),
            )
            for i, (name, a, b) in enumerate((("qt", da, db), ("gt", pa, pb))):
                acc[i, :, : 2 * PAGE] += dot_n(turn(name, 1, 2), a)
                acc[i, :, cols(2, 3)] += dot_n(turn(name, 2, 1), b[:tall])
                acc[i, :, cols(3, 4)] += dot_n(turn(name, 0, 1), b[tall:])
            first = dot_n(da, k_up[: 2 * PAGE])
            put = lambda slot, rows: head.put_queries(
                part, slot, rows, held(("dq", kv)), not fresh[n], stage_ref
            )
            put(1, first[:tall])
            put(2, first[tall:] + dot_n(db[:tall], k_up[cols(2, 3)]))
            put(0, dot_n(db[tall:], k_up[cols(3, 4)]))

        def shared_part(head, kv, part, n, stage_ref):
            order = (0, 1, 2)
            qs = head.stacked(held(("q", kv)), part, order)
            gs = head.stacked(held(("g", kv)), part, order)
            qd, gd = head.deep(qs, en, part, order), head.deep(gs, ed, part, order)
            turn = turned_rows(head, kv, part, fresh[n], qs, gs, order)
            column = lax.broadcasted_iota(I32, (tall, 2 * PAGE), 1)
            seen = column < facts[LIMIT]

            def keep(p):
                return jnp.concatenate([jnp.where(seen, p[:tall], 0.0), p[tall:]], axis=0)

            p, ds = weigh(dot_n(qd, k_deep[...]), dot_n(gd, v_deep[...]), keep)
            acc[0] += dot_n(turn("qt", 0, SLOTS), ds)
            acc[1] += dot_n(turn("gt", 0, SLOTS), p)
            if not fresh[n]:
                held(("ds", kv))[part * SLOTS * tall : (part + 1) * SLOTS * tall] = ds
                return
            dq = dot_n(ds, k_up[...])
            for slot in range(SLOTS):
                head.put_queries(
                    part, slot, dq[slot * tall : (slot + 1) * tall], held(("dq", kv)), not fresh[n],
                    stage_ref,
                )

        def put_own(n):
            dk12, dv12, own0, send2 = results
            here = slice(base + n * HD, base + (n + 1) * HD)
            grad = [acc[0].T * SCALE, acc[1].T]
            for at, c, to in ((0, N1, 0), (2, N2, 1)):
                ok = row_ok(facts[c], PAGE, HD)
                for kind, out in ((0, dk12), (1, dv12)):
                    out[cols(to, to + 1), here] = jnp.where(
                        ok, grad[kind][cols(at, at + 1)], 0.0
                    ).astype(BF16)
            for kind in range(2):
                level2 = grad[kind][cols(1, 2)]
                own0[kind, :, here] = grad[kind][cols(3, 4)] + jnp.where(owns2, level2, 0.0)
                send2[kind, :, here] = level2.astype(BF16)

        def put_shared(n):
            (out,) = results
            here = slice(n * HD, (n + 1) * HD)
            grads = acc[0].T * SCALE, acc[1].T
            for j in range(2):
                for kind in range(2):
                    out[2 * j + kind, :, here] = grads[kind][cols(j, j + 1)].astype(out.dtype)

        sends = []
        for n, kv in enumerate(kvs):
            arrived(("q", kv), ("g", kv))
            head = Head(kv, group, norms, deltas, en, ed)
            set_pages(n, kv)

            for part in range(parts):
                slot = n * parts + part
                (own_part if own else shared_part)(
                    head, kv, part, n, stage.at[slot] if own and not fresh[n] else None
                )
                if own and not fresh[n]:
                    at = order.at(facts, kv, group * HD) + part * wide
                    sends.append(
                        pltpu.make_async_copy(
                            stage.at[slot],
                            held("gq").at[:, pl.ds(pl.multiple_of(at, wide), wide)],
                            sem.at[slot],
                        )
                    )
                    sends[-1].start()

            (put_own if own else put_shared)(n)
        for c in sends:
            c.wait()
        arrived(*list(copies))

    made = kernel_call(
        body, facts, near, far, outs, scratch, aliases, after,
        pl.CostEstimate(
            flops=240 * PAGE * PAGE * HD * group * count, bytes_accessed=1000, transcendentals=0
        ),
        LARGE,
    )
    for name, at in at_out.items():
        state[name] = made[at]
    return list(made[at_results:at_loaded])


def width_tiles(w):
    tile = next(t for t in (512, 640, 320, 128, w.shape[0]) if w.shape[0] % t == 0)
    return [slice(i, i + tile) for i in range(0, w.shape[0], tile)]


def finish_queries(kvs, group, order, facts, pages, state, after=(), w=None):
    parts = group // min(4, group)
    heads = group // parts
    tall = heads * PAGE
    wide = heads * HD
    near = list(pages)
    for kv in kvs:
        near += [state["ds", kv], state["dq", kv]]

    def body(facts, *refs):
        stage, sem = refs[-2:]
        if w is not None:
            gq, made, w_near = refs[-5:-2]
            w_copy = pltpu.make_async_copy(refs[-6], w_near, sem.at[len(kvs) * parts])
            w_copy.start()
        else:
            gq, made = refs[-4:-2]
        made[...] = jnp.zeros_like(made)
        sends = []
        for n, kv in enumerate(kvs):
            ds, dq = refs[len(pages) + 2 * n : len(pages) + 2 * n + 2]
            page, at = refs[kv // order.half], kv % order.half * HD
            keys = jnp.concatenate([page[j, 0, :, at : at + HD] for j in range(2)], axis=0)
            for part in range(parts):
                at = n * parts + part
                gained = dot_n(ds[part * SLOTS * tall : (part + 1) * SLOTS * tall], keys)
                for i in range(SLOTS * heads):
                    slot, j = divmod(i, heads)
                    rows = slice(slot * PAGE, (slot + 1) * PAGE)
                    value = gained[i * PAGE : (i + 1) * PAGE] + dq[
                        rows, part * wide + j * HD : part * wide + (j + 1) * HD
                    ]
                    stage[at, rows, j * HD : (j + 1) * HD] = (value * SCALE).astype(BF16)
                to = pl.multiple_of(order.at(facts, kv, group * HD) + part * wide, wide)
                sends.append(
                    pltpu.make_async_copy(stage.at[at], gq.at[:, pl.ds(to, wide)], sem.at[at])
                )
                sends[-1].start()
        for c in sends:
            c.wait()
        if w is not None:
            w_copy.wait()

    count = len(kvs) * parts
    far = [state["gq"]] if "gq" in state else []
    aliases = {("far", 0): 0} if far else {}
    shape = (ROWS, state["k"].shape[1] * group)
    outs = [(shape, BF16, False), ((8, HD), F32, True)]
    if w is not None:
        far = far + [w]
        outs.append((w.shape, w.dtype, True))
    state["gq"], *made = kernel_call(
        body, facts, near, far, outs,
        [pltpu.VMEM((count, ROWS, wide), BF16), pltpu.SemaphoreType.DMA((count + 1,))],
        aliases, after, limit=LARGE,
    )
    return made


def input_grad(order, facts, w, rows, own, far, grads, carry=None, near_w=False, after=()):
    out_cols, depth = w.shape
    tiles = width_tiles(w)
    top = 0 if rows == PAGE else PAGE
    steps = len(tiles)
    width = sum(a.shape[1] for a in grads[0])
    arrays = [*own, *far, *grads[0], *grads[1]] + [w] * near_w
    count = len(grads[0])
    carry = list(carry or [])
    lead = [] if near_w else [w]
    rest = [*lead, *carry, *after]

    def body(facts, *refs):
        own_r, refs = refs[: len(own)], refs[len(own) :]
        far_r, refs = refs[: len(far)], refs[len(far) :]
        grad_r, w_ref = refs[: 2 * count], refs[2 * count]
        out, dk, dv, made, w_near, stage, w_sem, sem = refs[-8:]
        loads = []
        if not near_w:
            loads = [
                pltpu.make_async_copy(w_ref.at[at], w_near.at[at], w_sem.at[i])
                for i, at in enumerate(tiles)
            ]
        for c in loads:
            c.start()
        made[...] = jnp.zeros_like(made)
        columns = lambda rs: jnp.concatenate([r[...] for r in rs], axis=1)
        full = order.real(facts, columns(own_r))
        if far:
            other, first = order.real(facts, columns(far_r)), facts[SIDE] == 0
            full = jnp.concatenate(
                [jnp.where(first, full, other), jnp.where(first, other, full)], axis=1
            )
        copies = put_rows(order, facts, grad_r, dk, dv, top, rows, sem, steps)
        for i, at in enumerate(tiles):
            if loads:
                loads[i].wait()
            stage[i] = dot_t((w_ref if near_w else w_near)[at], full).astype(BF16).T
            copies.append(
                pltpu.make_async_copy(stage.at[i], out.at[top : top + rows, at], sem.at[i])
            )
            copies[-1].start()
        for c in copies:
            c.wait()

    smem = pl.BlockSpec(memory_space=pltpu.SMEM)
    vmem = pl.BlockSpec(memory_space=pltpu.VMEM)
    hbm = pl.BlockSpec(memory_space=pl.ANY)
    arrays = [pltpu.with_memory_space_constraint(a, pltpu.VMEM) for a in arrays]
    kept = jax.ShapeDtypeStruct((ROWS, width), BF16)
    return pl.pallas_call(
        body,
        out_shape=(
            jax.ShapeDtypeStruct((ROWS, out_cols), BF16), kept, kept, pltpu.VMEM((8, HD), F32)
        ),
        in_specs=[smem] + [vmem] * len(arrays) + [hbm] * len(rest),
        out_specs=(hbm, hbm, hbm, vmem),
        scratch_shapes=[
            pltpu.VMEM((8, HD) if near_w else w.shape, BF16),
            pltpu.VMEM((steps, rows, out_cols // steps), BF16),
            pltpu.SemaphoreType.DMA((steps,)),
            pltpu.SemaphoreType.DMA((steps + 2 * order.heads,)),
        ],
        input_output_aliases={
            1 + len(arrays) + len(lead) + i: i for i in range(len(carry))
        },
        compiler_params=pltpu.CompilerParams(vmem_limit_bytes=LARGE),
        cost_estimate=SLIGHT,
    )(pltpu.with_memory_space_constraint(facts, pltpu.SMEM), *arrays, *rest)


def put_rows(order, facts, pieces, dk, dv, top, rows, sem, first):
    copies = []
    count = len(pieces) // 2
    for dst, mine in ((dk, pieces[:count]), (dv, pieces[count:])):
        head = 0
        for src in mine:
            more = src.shape[1] // HD
            for lo, hi in order.runs(head, head + more):
                copies.append(
                    pltpu.make_async_copy(
                        src.at[:, (lo - head) * HD : (hi - head) * HD],
                        dst.at[top : top + rows, pl.ds(order.at(facts, lo, HD), (hi - lo) * HD)],
                        sem.at[first + len(copies)],
                    )
                )
                copies[-1].start()
            head += more
    return copies


def begin_input_grad(order, facts, w, own, after=()):
    out_cols, depth = w.shape
    half = depth // 2
    rows = own[0].shape[0]
    count = len(own)

    def body(facts, w_ref, *refs):
        mine, out = jnp.concatenate([r[...] for r in refs[:count]], axis=1), refs[-1]
        mine = order.real(facts, mine)
        where = pl.ds(pl.multiple_of(facts[SIDE] * half, half), half)
        for at in width_tiles(w):
            out[at] = dot_t(w_ref[at, where], mine)

    smem = pl.BlockSpec(memory_space=pltpu.SMEM)
    vmem = pl.BlockSpec(memory_space=pltpu.VMEM)
    near = [pltpu.with_memory_space_constraint(a, pltpu.VMEM) for a in (w, *own)]

    def kernel(*refs):
        body(*refs[: 2 + count], refs[-1])

    return pl.pallas_call(
        kernel,
        out_shape=pltpu.VMEM((out_cols, rows), F32),
        in_specs=[smem] + [vmem] * len(near) + [pl.BlockSpec(memory_space=pl.ANY)] * len(after),
        out_specs=vmem,
        compiler_params=pltpu.CompilerParams(vmem_limit_bytes=LARGE),
        cost_estimate=SLIGHT,
    )(pltpu.with_memory_space_constraint(facts, pltpu.SMEM), *near, *after)


def end_input_grad(order, facts, w, base, across, corner, begun, grads, carry):
    tiles = width_tiles(w)
    out_cols, depth = w.shape
    half = depth // 2
    steps = len(tiles)
    rows = base.shape[0]

    def body(facts, w_r, begun_r, base_r, across_r, corner_r, *refs):
        out, dk, dv, stage, sem = refs[-5:]
        copies = put_rows(order, facts, refs[:2], dk, dv, 0, rows, sem, steps)
        gained = jnp.concatenate([corner_r[...], across_r[...]], axis=1).astype(F32)
        known = base_r[...]
        more = jnp.where(row_ok(facts[N0], rows, half), known.astype(F32) + gained, 0.0)
        other = order.real(facts, jnp.where(facts[OWNS2] == 1, known, more.astype(BF16)))
        where = pl.ds(pl.multiple_of((1 - facts[SIDE]) * half, half), half)
        for i, at in enumerate(tiles):
            stage[i] = (dot_t(w_r[at, where], other) + begun_r[at]).astype(BF16).T
            copies.append(pltpu.make_async_copy(stage.at[i], out.at[:rows, at], sem.at[i]))
            copies[-1].start()
        for c in copies:
            c.wait()

    return kernel_call(
        body, facts, [w, begun, base, across, corner, *grads], list(carry),
        [(a.shape, a.dtype, False) for a in carry],
        [
            pltpu.VMEM((steps, rows, out_cols // steps), BF16),
            pltpu.SemaphoreType.DMA((steps + 2 * order.heads,)),
        ],
        {("far", i): i for i in range(len(carry))},
    )


def flipped(block, axis, bit):
    count = lax.axis_size(axis)
    return lax.ppermute(block, axis, [(i, i ^ bit) for i in range(count) if i ^ bit < count])


def spanning(leaves, bit_index):
    return len([j for j in range(INNER) if 2 << bit_index <= leaves >> j])


def gather_small_tree(facts, own, beside_pair, beside_half):
    width = own.shape[-1] // 2
    page = ((2, PAGE, width), BF16, True)
    from_core = flipped(own, "sub", 1)

    def choose_chip(facts, own_ref, far_ref, out):
        for swap in range(2):
            for mine in range(2):

                @pl.when((facts[SWAP] == swap) & (facts[OWNS2] != mine))
                def _copy(swap=swap, mine=mine):
                    out[...] = (own_ref if mine else far_ref)[
                        :, :, swap * width : (swap + 1) * width
                    ]

    (chip,) = kernel_call(choose_chip, facts, [own, from_core], [], [page])
    from_pair = flipped(chip, "leaf", 1)

    def choose_pair(facts, near_ref, far_ref, out):
        out[...] = jnp.where(facts[ROOT_IN_CHIP] == 1, near_ref[...], far_ref[...])

    after = beside_pair(from_core, chip)
    (pair,) = kernel_call(choose_pair, facts, [chip, from_pair], [], [page], after=after)
    from_half = flipped(pair, "leaf", 2)

    def choose_all(facts, chip_ref, pair_far, pair_ref, half_far, out):
        out[0] = jnp.where(facts[ROOT_IN_PAIR] == 1, pair_ref[...], half_far[...])
        out[1] = jnp.where(facts[NEXT_IN_CHIP] == 1, chip_ref[...], pair_far[...])

    after = beside_half(pair)
    (mine,) = kernel_call(
        choose_all, facts, [chip, from_pair, pair, from_half], [],
        [((2, *page[0]), BF16, True)], after=after,
    )
    return mine, flipped(mine, "sub", 1)


def over_cores(facts, kept, far):
    width = kept.shape[-1]

    def body(_, near, away, total, root, next_one):
        for i in range(4):
            value = near[i] + away[i].astype(F32)
            total[i] = value
            (root, next_one)[i // 2][i % 2] = value.astype(BF16)

    pages = ((2, PAGE, width), BF16, True)
    total, root, next_one = kernel_call(
        body, facts, [kept, far], [], [((4, PAGE, width), F32, True), pages, pages]
    )
    return total, root, flipped(root, "leaf", 2), flipped(next_one, "leaf", 1)


def over_halves(facts, total, root_far, next_far, after):
    width = total.shape[-1]

    def body(_, near, root_r, next_r, out, low):
        root = near[:2] + root_r[...].astype(F32)
        out[:2] = root
        low[...] = root.astype(BF16)
        out[2:] = near[2:] + next_r[...].astype(F32)

    total, low = kernel_call(
        body, facts, [total, root_far, next_far], [],
        [((4, PAGE, width), F32, True), ((2, PAGE, width), BF16, True)], after=after,
    )
    return total, low, flipped(low, "leaf", 1)


def over_chips(facts, total, far, after):
    width = total.shape[-1]

    def body(facts, near, away, out, values):
        root = near[:2] + away[...].astype(F32)
        picked = jnp.where(facts[ROOT_IN_CHIP] == 1, root, near[2:]).astype(BF16)
        out[...] = picked
        values[...] = picked[1]

    outs = [((2, PAGE, width), BF16, True), ((PAGE, width), BF16, True)]
    mine, values = kernel_call(body, facts, [total, far], [], outs, after=after)
    across = flipped(values, "tensor", 1)
    corner = lax.ppermute(values, ("tensor", "sub"), [(i, 3 - i) for i in range(4)])
    return mine, flipped(mine, "sub", 1), across, corner


def other_level2(order, head, kind, ref):
    theirs = head ^ order.half
    at = theirs % order.half * HD
    return ref[4 + 2 * (theirs // order.half) + kind, :, at : at + HD]


def begin_values(order, facts, own0, level2_far):
    def body(facts, own_r, low_r, out):
        ok = row_ok(facts[N0], PAGE, HD)
        for head in range(order.heads):
            c = slice(head * HD, (head + 1) * HD)
            low = other_level2(order, head, 1, low_r).astype(F32)
            value = own_r[1, :, c] + jnp.where(facts[OWNS2] == 1, low, 0.0)
            out[:, c] = jnp.where(ok, value, 0.0).astype(BF16)

    outs = [((PAGE, own0.shape[-1]), BF16, True)]
    return kernel_call(body, facts, [own0, level2_far], [], outs)[0]


def finish_small_tree(order, facts, own0, mine, far, level2_far):
    width = own0.shape[-1]

    def body(facts, own_r, mine_r, far_r, low_r, dk, dv):
        owns2 = facts[OWNS2] == 1
        ok = row_ok(facts[N0], PAGE, HD)
        for head in range(order.heads):
            c = slice(head * HD, (head + 1) * HD)
            at = head % order.half * HD
            for kind, out in enumerate((dk, dv)):
                gained = (far_r if head < order.half else mine_r)[kind, :, at : at + HD]
                level2 = other_level2(order, head, kind, low_r)
                more = jnp.where(owns2, level2, gained).astype(F32)
                out[:, c] = jnp.where(ok, own_r[kind, :, c] + more, 0.0).astype(BF16)

    page = ((PAGE, width), BF16, True)
    return kernel_call(body, facts, [own0, mine, far, level2_far], [], [page, page])


def gather_tree(ids, own):
    leaves = lax.axis_size(("leaf", "sub"))
    owned = ids[:INNER] == ids[INNER] - 1
    pages = jnp.where(owned[:, None, None, None], own[None], jnp.zeros((), BF16))
    for bit in range(leaves.bit_length() - 1):
        active = spanning(leaves, bit)
        far = flipped(pages[:active], ("leaf", "sub"), 1 << bit)
        pages = jnp.concatenate([pages[:active] + far, pages[active:]])
    return pages


def reduce_tree(ids, parts):
    leaves = lax.axis_size(("leaf", "sub"))
    for bit in range(leaves.bit_length() - 1):
        active = spanning(leaves, bit)
        far = flipped(parts[:active], ("leaf", "sub"), 1 << bit)
        parts = jnp.concatenate([parts[:active] + far, parts[active:]])
    owned = ids[:INNER] == ids[INNER] - 1
    return jnp.sum(jnp.where(owned[:, None, None, None], parts, 0.0), axis=0)


def on_device(queries, grad_out, keys, values, log_norms, row_deltas, ancestors, counts, w_value):
    kv = keys.shape[1] // HD
    group = queries.shape[1] // keys.shape[1]
    leaves = lax.axis_size(("leaf", "sub"))
    hbm = lambda a: pltpu.with_memory_space_constraint(a, pltpu.HBM)
    side = lax.axis_index("tensor").astype(I32).reshape(1)
    two_sides = lax.axis_size("tensor") == 2
    inputs = [hbm(a) for a in (queries, grad_out, keys, values, log_norms, row_deltas)]
    fast = leaves == 8 and lax.axis_size("sub") == 2 and kv == 4 and two_sides
    order = Order(fast, kv)
    facts, own = start(order, side, hbm(ancestors), hbm(counts), *inputs[2:4])
    state = {}

    def own_pages(kvs, pages, prior=(), after=()):
        return attend(True, kvs, group, order, facts, inputs, pages, state, prior, after)

    def shared_pages(kvs, page, ride=None, after=()):
        return attend(
            False, kvs, group, order, facts, inputs, [page], state, after=after, ride=ride
        )[0]

    def spread(part):
        if two_sides:
            return flipped(part, "tensor", 1)
        return lax.all_gather(part, "tensor", axis=1, tiled=True)

    kvs = tuple(range(kv))
    w = hbm(w_value)
    if fast:
        level2, halves = [], []

        def beside_pair(from_core, chip):
            level2.extend((own, from_core))
            halves.append(own_pages(kvs[:2], level2, after=(chip,)))
            return (halves[0][3],)

        def beside_half(pair):
            halves.append(own_pages(kvs[2:], level2, halves[0], (pair,)))
            return (halves[1][3],)

        mine, theirs = gather_small_tree(facts, own, beside_pair, beside_half)
        dk12, dv12, own0, send2 = halves[1]
        sent = flipped(shared_pages(kvs[:2], mine, send2), "sub", 1)
        kept = shared_pages(kvs[2:], theirs)
        total, root, root_far, next_far = over_cores(facts, kept, sent)
        far_v = spread(dv12)
        base = begin_values(order, facts, own0, sent)
        made, w_near = finish_queries(
            kvs, group, order, facts, (mine, theirs), state, (root, base), w
        )
        total, low, far = over_halves(facts, total, root_far, next_far, (made,))
        base_far = spread(base)
        *grads, made = input_grad(
            order, facts, w_near, 2 * PAGE, [dv12], [far_v], ([dk12], [dv12]), near_w=True,
            after=(low,),
        )
        near, far, across, corner = over_chips(facts, total, far, (made, base_far))
        dk0, dv0 = finish_small_tree(order, facts, own0, near, far, sent)
        begun = begin_input_grad(order, facts, w_near, [dv0])
        grads = end_input_grad(
            order, facts, w_near, base_far, across, corner, begun, [dk0, dv0], grads
        )
        return (state["gq"], grads[1], grads[2], grads[0])

    path_ids = ancestors[0]
    pages = gather_tree(path_ids, own)
    dk12, dv12, own0, send2 = own_pages(kvs, (pages[2], pages[2]))
    grads = shared_pages(kvs, pages[:2])
    finish_queries(kvs, group, order, facts, (pages[:2],), state)
    low = send2.astype(F32)
    total = reduce_tree(path_ids, jnp.concatenate([grads.reshape(2, 2, *grads.shape[1:]), low[None]]))
    total += own0 - jnp.where(path_ids[2] == path_ids[INNER] - 1, low, 0.0)
    has = jnp.any(path_ids[:INNER] == path_ids[INNER] - 1)
    ok = (jnp.arange(PAGE) < jnp.where(has, counts[0, 0], 0))[:, None]
    dk0, dv0 = jnp.where(ok, total, 0.0).astype(BF16)
    if two_sides:
        pair = lambda part: ([part], [spread(part)])
    else:
        pair = lambda part: ([spread(part)], [])
    *grads, _ = input_grad(order, facts, w, 2 * PAGE, *pair(dv12), ([dk12], [dv12]))
    grads = input_grad(order, facts, w, PAGE, *pair(dv0), ([dk0], [dv0]), grads)
    return (state["gq"], grads[1], grads[2], grads[0])


def solution(mesh):
    placed = (
        P(("groups", "leaf", "sub"), "tensor"),
        P(("groups", "leaf", "sub"), "tensor"),
        P(("groups", "leaf", "sub"), "tensor"),
        P(("groups", "leaf", "sub"), "tensor"),
        P("tensor", ("groups", "leaf", "sub")),
        P("tensor", ("groups", "leaf", "sub")),
        P(("groups", "leaf", "sub"), None),
        P(("groups", "leaf", "sub"), None),
        P("tensor", None),
    )
    return jax.shard_map(
        on_device,
        mesh=mesh,
        in_specs=placed,
        out_specs=(
            P(("groups", "leaf", "sub"), "tensor"),
            P(("groups", "leaf", "sub"), "tensor"),
            P(("groups", "leaf", "sub"), "tensor"),
            P(("groups", "leaf", "sub"), "tensor"),
        ),
        check_vma=False,
    )
```

```python
import math

import jax
import jax.numpy as jnp
from jax import lax
from jax.experimental import pallas as pl
from jax.experimental.pallas import tpu as pltpu
from jax.sharding import PartitionSpec as P

HD = 128
PAGE = 128
SLOTS = 3
INNER = 3
ROWS = SLOTS * PAGE
LOG2E = math.log2(math.e)
SCALE = 1.0 / math.sqrt(HD)
BF16 = jnp.bfloat16
F32 = jnp.float32
I32 = jnp.int32
LARGE = 10 << 20
SMALL = 4 << 20
SLIGHT = pl.CostEstimate(flops=1000, bytes_accessed=1000, transcendentals=0)
BLOCKED = 1e30


def dot_t(left, right):
    return lax.dot_general(left, right, (((1,), (1,)), ((), ())), preferred_element_type=F32)


def dot_n(left, right):
    return lax.dot_general(left, right, (((1,), (0,)), ((), ())), preferred_element_type=F32)


FACTS = 16
N0, N1, N2, OWNS2, LIMIT, LEADS, ROOT_IN_CHIP, ROOT_IN_PAIR, NEXT_IN_CHIP, SIDE, SWAP = range(11)


class Order:
    def __init__(self, crossed, heads):
        self.crossed, self.heads = crossed, heads
        self.half = heads // 2 if crossed else heads

    def at(self, facts, head, unit):
        if not self.crossed:
            return head * unit
        step = ((head ^ self.half) - head) * unit
        return pl.multiple_of(facts[SWAP] * step + head * unit, unit)

    def runs(self, first, last):
        cuts = [first, *(h for h in range(first + 1, last) if h % self.half == 0), last]
        return list(zip(cuts[:-1], cuts[1:]))

    def real(self, facts, rows):
        if not self.crossed:
            return rows
        width = self.half * HD
        turned = jnp.concatenate([rows[:, width:], rows[:, :width]], axis=1)
        return jnp.where(facts[SWAP] == 1, turned, rows)


def write_facts(facts, ids, counts, side, order):
    page = [ids[0, j] for j in range(INNER + 1)]
    own = page[INNER] - 1
    leaf = own // SLOTS
    owns = [page[j] == own for j in range(INNER)]
    same = lambda level, shift: ((page[level] // SLOTS) >> shift) == (leaf >> shift)
    number = lambda flag: jnp.where(flag, 1, 0)
    facts[N0] = jnp.where(owns[0] | owns[1] | owns[2], counts[0, 0], 0)
    facts[N1] = counts[0, 1]
    facts[N2] = counts[0, 2]
    facts[OWNS2] = number(owns[2])
    facts[LIMIT] = jnp.where(owns[2], 2 * PAGE, jnp.where(owns[1], PAGE, 0))
    facts[LEADS] = number(lax.rem(leaf, 2) == 0)
    facts[ROOT_IN_CHIP] = number(same(0, 1))
    facts[ROOT_IN_PAIR] = number(same(0, 2))
    facts[NEXT_IN_CHIP] = number(same(1, 1))
    facts[SIDE] = side
    facts[SWAP] = lax.rem(leaf, 2) if order.crossed else 0
    for i in range(SWAP + 1, FACTS):
        facts[i] = 0


def row_ok(count, rows, width):
    return lax.broadcasted_iota(I32, (rows, width), 0) < count


def kernel_call(body, facts, near, far, outs, scratch=(), aliases=None, after=(), cost=None,
                limit=SMALL):
    smem = pl.BlockSpec(memory_space=pltpu.SMEM)
    vmem = pl.BlockSpec(memory_space=pltpu.VMEM)
    hbm = pl.BlockSpec(memory_space=pl.ANY)
    near = [pltpu.with_memory_space_constraint(a, pltpu.VMEM) for a in near]
    place = {("near", i): 1 + i for i in range(len(near))}
    place |= {("far", i): 1 + len(near) + i for i in range(len(far))}
    used = 1 + len(near) + len(far)

    def kernel(*refs):
        body(*refs[:used], *refs[used + len(after) :])

    return pl.pallas_call(
        kernel,
        out_shape=tuple(
            pltpu.VMEM(s, d) if inside else jax.ShapeDtypeStruct(s, d) for s, d, inside in outs
        ),
        in_specs=[smem] + [vmem] * len(near) + [hbm] * (len(far) + len(after)),
        out_specs=tuple(vmem if inside else hbm for _, _, inside in outs),
        scratch_shapes=list(scratch),
        input_output_aliases={place[k]: v for k, v in (aliases or {}).items()},
        compiler_params=pltpu.CompilerParams(vmem_limit_bytes=limit),
        cost_estimate=cost or SLIGHT,
    )(pltpu.with_memory_space_constraint(facts, pltpu.SMEM), *near, *far, *after)


def start(order, side, ids, counts, keys, values):
    width = keys.shape[1]

    def body(side_ref, ids_ref, counts_ref, k_ref, v_ref, facts, out, held, ids_s, counts_s, sem):
        copies = [
            pltpu.make_async_copy(src, dst, sem.at[i])
            for i, (src, dst) in enumerate(
                (
                    (ids_ref, ids_s),
                    (counts_ref, counts_s),
                    (k_ref.at[:PAGE], held.at[0]),
                    (v_ref.at[:PAGE], held.at[1]),
                )
            )
        ]
        for c in copies:
            c.start()
        copies[0].wait()
        copies[1].wait()
        write_facts(facts, ids_s, counts_s, side_ref[0], order)
        ok = row_ok(counts_s[0, 0], PAGE, width)
        for i in range(2):
            copies[2 + i].wait()
            out[i] = jnp.where(ok, held[i], jnp.zeros((), BF16))

    smem = pl.BlockSpec(memory_space=pltpu.SMEM)
    hbm = pl.BlockSpec(memory_space=pl.ANY)
    return pl.pallas_call(
        body,
        out_shape=(pltpu.SMEM((FACTS,), I32), pltpu.VMEM((2, PAGE, width), BF16)),
        in_specs=[smem] + [hbm] * 4,
        out_specs=(smem, pl.BlockSpec(memory_space=pltpu.VMEM)),
        scratch_shapes=[
            pltpu.VMEM((2, PAGE, width), BF16),
            pltpu.SMEM(ids.shape, I32),
            pltpu.SMEM(counts.shape, I32),
            pltpu.SemaphoreType.DMA((4,)),
        ],
        compiler_params=pltpu.CompilerParams(vmem_limit_bytes=SMALL),
    )(side, ids, counts, keys, values)


def row_terms(rows):
    high = rows.astype(BF16).astype(F32)
    rest = rows - high
    middle = rest.astype(BF16).astype(F32)
    parts = [high, middle, rest - middle]
    spare = HD - 3 * rows.shape[0]
    parts.append(jnp.zeros((spare, rows.shape[1]), F32))
    return jnp.concatenate(parts, axis=0).T.astype(BF16)


class Head:
    def __init__(self, kv, group, norms, deltas, en, ed):
        self.group = group
        self.heads = min(4, group)
        self.parts = group // self.heads
        self.tall = self.heads * PAGE
        heads = slice(kv * group, (kv + 1) * group)
        en[...] = row_terms(norms[heads, :])
        ed[...] = row_terms(deltas[heads, :])

    def lanes(self, part, j):
        at = (part * self.heads + j) * HD
        return slice(at, at + HD)

    def stacked(self, ref, part, slots):
        return jnp.concatenate(
            [
                ref[slot * PAGE : (slot + 1) * PAGE, self.lanes(part, j)]
                for slot in slots
                for j in range(self.heads)
            ],
            axis=0,
        )

    def deep(self, stacked, terms, part, slots):
        column = lax.broadcasted_iota(I32, (1, HD), 1) % self.group
        picks = [
            (column == part * self.heads + j).astype(F32).astype(BF16)
            for j in range(self.heads)
        ]
        extra = [
            terms[slot * PAGE : (slot + 1) * PAGE] * pick for slot in slots for pick in picks
        ]
        return jnp.concatenate([stacked, jnp.concatenate(extra, axis=0)], axis=1)

    def turned_at(self, part, slot, count):
        at = (part * SLOTS + slot) * self.tall
        return slice(at, at + self.tall * count)

    def put_queries(self, part, slot, rows_by_head, dq, add, stage):
        rows = slice(slot * PAGE, (slot + 1) * PAGE)
        for j in range(self.heads):
            value = rows_by_head[j * PAGE : (j + 1) * PAGE]
            if stage is None:
                dq[rows, self.lanes(part, j)] = value
            else:
                if add:
                    value = value + dq[rows, self.lanes(part, j)]
                stage[rows, j * HD : (j + 1) * HD] = (value * SCALE).astype(BF16)


def set_keys(deep, upright, at, page):
    where = slice(at * PAGE, (at + 1) * PAGE)
    deep[:HD, where] = page.T
    if upright is not None:
        upright[where] = page


def weigh(scores, grads, keep):
    p = keep(jnp.exp2(scores * (SCALE * LOG2E)))
    return p.astype(BF16), (p * grads).astype(BF16)


def attend(own, kvs, group, order, facts, inputs, pages, state, prior=(), after=(),
           ride=None):
    loading = "k" not in state
    q_all, k_all = inputs[0], inputs[2]
    count = len(kvs)
    parts = group // min(4, group)
    tall = min(4, group) * PAGE
    wide = min(4, group) * HD
    width = count * HD
    base = prior[0].shape[1] if prior else 0
    kv_total = k_all.shape[1] // HD
    fresh = [("dq", kv) not in state for kv in kvs]
    one_head = (ROWS, group * HD)
    turned = ((HD, group * ROWS), BF16, True)
    shapes = {"dq": (one_head, F32, True), "qt": turned, "gt": turned}

    near, far, aliases, outs = [], [], {}, []
    at_near, at_far, at_out = {}, {}, {}

    def add_near(name, array):
        at_near[name] = len(near)
        near.append(array)

    def add_far(name, array):
        at_far[name] = len(far)
        far.append(array)

    def add_out(name, out):
        at_out[name] = len(outs)
        outs.append(out)

    for kv, is_fresh in zip(kvs, fresh):
        for name, shape in shapes.items():
            if is_fresh:
                add_out((name, kv), shape)
            elif own or name != "dq":
                add_near((name, kv), state[name, kv])
        if not own and not is_fresh:
            add_out(("ds", kv), ((group * ROWS, 2 * PAGE), BF16, True))
    if own and not all(fresh):
        add_out("gq", (q_all.shape, BF16, False))
        if "gq" in state:
            add_far("gq", state["gq"])
            aliases["far", at_far["gq"]] = at_out["gq"]
    at_results = len(outs)
    if own:
        outs += [
            ((2 * PAGE, base + width), BF16, True),
            ((2 * PAGE, base + width), BF16, True),
            ((2, PAGE, base + width), F32, True),
            ((2, PAGE, base + width), BF16, True),
        ]
    else:
        outs += [
            ((4, PAGE, width), F32, True) if ride is None else ((8, PAGE, width), BF16, True),
        ]
    at_loaded = len(outs)
    if loading:
        for name, array in zip(("q", "g", "k", "v", "norms", "deltas"), inputs):
            add_far(name, array)
            if name in ("q", "g"):
                for kv in range(kv_total):
                    add_out((name, kv), (one_head, BF16, True))
            else:
                add_out(name, (array.shape, array.dtype, True))
    else:
        for name in ("k", "v", "norms", "deltas"):
            add_near(name, state[name])
        for kv in kvs:
            for name in ("q", "g"):
                add_near((name, kv), state[name, kv])
    for i, page in enumerate(pages):
        add_near(("page", i), page)
    for i, array in enumerate(prior):
        add_near(("prior", i), array)
    if ride is not None:
        add_near("ride", ride)
    key_pages = 4 if own else 2
    scratch = [
        pltpu.VMEM((2 * HD, key_pages * PAGE), BF16),
        pltpu.VMEM((2 * HD, key_pages * PAGE), BF16),
        pltpu.VMEM((key_pages * PAGE, HD), BF16),
        pltpu.VMEM((2, HD, key_pages * PAGE), F32),
        pltpu.VMEM((ROWS, HD), BF16),
        pltpu.VMEM((ROWS, HD), BF16),
        pltpu.VMEM((count * parts, ROWS, wide), BF16),
        pltpu.SemaphoreType.DMA((count * parts,)),
        pltpu.SemaphoreType.DMA((2 * kv_total + 8,)),
    ]
    cols = lambda a, b: slice(a * PAGE, b * PAGE)

    def body(facts, *refs):
        ins, out_refs = refs[: len(near) + len(far)], refs[len(near) + len(far) : -len(scratch)]
        k_deep, v_deep, k_up, acc, en, ed, stage, sem, load_sem = refs[-len(scratch) :]
        near_ref = lambda name: ins[at_near[name]]
        far_ref = lambda name: ins[len(near) + at_far[name]]
        held = lambda name: out_refs[at_out[name]] if name in at_out else near_ref(name)
        results = out_refs[at_results:at_loaded]
        copies = {}
        if loading:

            def load(key, src, dst):
                copies[key] = pltpu.make_async_copy(src, dst, load_sem.at[len(copies)])

            for lo, hi in order.runs(0, kv_total):
                for name in ("k", "v"):
                    at = pl.ds(order.at(facts, lo, HD), (hi - lo) * HD)
                    here = slice(lo * HD, hi * HD)
                    load((name, lo), far_ref(name).at[:, at], held(name).at[:, here])
                for name in ("norms", "deltas"):
                    at = pl.ds(order.at(facts, lo, group), (hi - lo) * group)
                    here = slice(lo * group, hi * group)
                    load((name, lo), far_ref(name).at[at], held(name).at[here])
            for kv in range(kv_total):
                at = pl.ds(order.at(facts, kv, group * HD), group * HD)
                for name in ("q", "g"):
                    load((name, kv), far_ref(name).at[:, at], held((name, kv)))
            rows_of = [(name, 0) for name in ("k", "v", "norms", "deltas")]
            first = [*rows_of, ("q", kvs[0]), ("g", kvs[0])]
            rest = [key for key in copies if key not in first]
            for key in first:
                copies[key].start()
        k, v, norms, deltas = (held(name) for name in ("k", "v", "norms", "deltas"))

        def arrived(*keys):
            for key in keys:
                if key in copies:
                    copies.pop(key).wait()

        k_deep[HD:] = jnp.full((HD, key_pages * PAGE), -1.0, BF16)
        v_deep[HD:] = jnp.full((HD, key_pages * PAGE), -1.0, BF16)
        for out, i in zip(results, range(len(prior))):
            out[..., :base] = near_ref(("prior", i))[...]
        if ride is not None:
            (out,), more = results, near_ref("ride")
            for kind in range(2):
                out[4 + kind] = more[kind, :, :width]
                out[6 + kind] = more[kind, :, width:]
        owns2 = facts[OWNS2] == 1

        def set_norms(lo, hi):
            rows = slice(lo * group, hi * group)
            lane = lax.broadcasted_iota(I32, ((hi - lo) * group, ROWS), 1)
            limit = jnp.where(
                lane < PAGE, facts[N0], jnp.where(lane < 2 * PAGE, facts[N1], facts[N2])
            )
            norms[rows] = jnp.where(lane % PAGE < limit, norms[rows] * (1.0 / SCALE), BLOCKED)

        if loading:
            arrived(*first)
            for key in rest:
                copies[key].start()
            ready, *later = order.runs(0, kv_total)
            set_norms(*ready)
        lower = lambda rows: lax.broadcasted_iota(I32, (rows, PAGE), 1) <= (
            lax.broadcasted_iota(I32, (rows, PAGE), 0) % PAGE
        )

        def set_pages(n, kv):
            lane = slice(kv * HD, (kv + 1) * HD)
            if own:
                first, second = (near_ref(("page", i)) for i in range(2))
                zero = jnp.zeros((), BF16)
                for slot, (at, c) in enumerate(((3, N0), (0, N1), (2, N2))):
                    ok = row_ok(facts[c], PAGE, HD)
                    rows = cols(slot, slot + 1)
                    set_keys(k_deep, k_up, at, jnp.where(ok, k[rows, lane], zero))
                    set_keys(v_deep, None, at, jnp.where(ok, v[rows, lane], zero))
                level2 = [jnp.where(owns2, first[i, :, lane], second[i, :, lane]) for i in (0, 1)]
                if order.crossed:
                    at = (kv ^ order.half) * HD
                    lane = slice(at, at + HD)
                    for i in range(2):
                        other = jnp.where(owns2, first[i, :, lane], second[i, :, lane])
                        level2[i] = jnp.where(facts[SWAP] == 1, other, level2[i])
                set_keys(k_deep, k_up, 1, level2[0])
                set_keys(v_deep, None, 1, level2[1])
            else:
                page = near_ref(("page", 0))
                for j in range(2):
                    here = slice(n * HD, (n + 1) * HD)
                    set_keys(k_deep, k_up, j, page[j, 0, :, here])
                    set_keys(v_deep, None, j, page[j, 1, :, here])
            acc[...] = jnp.zeros_like(acc)

        def turned_rows(head, kv, part, is_fresh, qs, gs, order):
            if is_fresh:
                for name, rows in (("qt", qs), ("gt", gs)):
                    for i, slot in enumerate(order):
                        held((name, kv))[:, head.turned_at(part, slot, 1)] = rows[
                            i * tall : (i + 1) * tall
                        ].T
            return lambda name, slot, slots: held((name, kv))[
                :, head.turned_at(part, slot, slots)
            ]

        def own_part(head, kv, part, n, stage_ref):
            order = (1, 2, 0)
            qs = head.stacked(held(("q", kv)), part, order)
            gs = head.stacked(held(("g", kv)), part, order)
            qd, gd = head.deep(qs, en, part, order), head.deep(gs, ed, part, order)
            turn = turned_rows(head, kv, part, fresh[n], qs, gs, order)
            low = lower(tall)

            def keep_first(p):
                masked = jnp.where(low, p[:tall, :PAGE], 0.0)
                return jnp.concatenate(
                    [jnp.concatenate([masked, p[:tall, PAGE:]], axis=1), p[tall:]], axis=0
                )

            pa, da = weigh(
                dot_n(qd[: 2 * tall], k_deep[:, : 2 * PAGE]),
                dot_n(gd[: 2 * tall], v_deep[:, : 2 * PAGE]),
                keep_first,
            )
            both = lambda x: jnp.concatenate([x[:tall, :PAGE], x[tall:, PAGE:]], axis=0)
            low2 = lower(2 * tall)
            pb, db = weigh(
                both(dot_n(qd[tall:], k_deep[:, 2 * PAGE :])),
                both(dot_n(gd[tall:], v_deep[:, 2 * PAGE :])),
                lambda p: jnp.where(low2, p, 0.0),
            )
            for i, (name, a, b) in enumerate((("qt", da, db), ("gt", pa, pb))):
                acc[i, :, : 2 * PAGE] += dot_n(turn(name, 1, 2), a)
                acc[i, :, cols(2, 3)] += dot_n(turn(name, 2, 1), b[:tall])
                acc[i, :, cols(3, 4)] += dot_n(turn(name, 0, 1), b[tall:])
            first = dot_n(da, k_up[: 2 * PAGE])
            put = lambda slot, rows: head.put_queries(
                part, slot, rows, held(("dq", kv)), not fresh[n], stage_ref
            )
            put(1, first[:tall])
            put(2, first[tall:] + dot_n(db[:tall], k_up[cols(2, 3)]))
            put(0, dot_n(db[tall:], k_up[cols(3, 4)]))

        def shared_part(head, kv, part, n, stage_ref):
            order = (0, 1, 2)
            qs = head.stacked(held(("q", kv)), part, order)
            gs = head.stacked(held(("g", kv)), part, order)
            qd, gd = head.deep(qs, en, part, order), head.deep(gs, ed, part, order)
            turn = turned_rows(head, kv, part, fresh[n], qs, gs, order)
            column = lax.broadcasted_iota(I32, (tall, 2 * PAGE), 1)
            seen = column < facts[LIMIT]

            def keep(p):
                return jnp.concatenate([jnp.where(seen, p[:tall], 0.0), p[tall:]], axis=0)

            p, ds = weigh(dot_n(qd, k_deep[...]), dot_n(gd, v_deep[...]), keep)
            acc[0] += dot_n(turn("qt", 0, SLOTS), ds)
            acc[1] += dot_n(turn("gt", 0, SLOTS), p)
            if not fresh[n]:
                held(("ds", kv))[part * SLOTS * tall : (part + 1) * SLOTS * tall] = ds
                return
            dq = dot_n(ds, k_up[...])
            for slot in range(SLOTS):
                head.put_queries(
                    part, slot, dq[slot * tall : (slot + 1) * tall], held(("dq", kv)), not fresh[n],
                    stage_ref,
                )

        def put_own(n):
            dk12, dv12, own0, send2 = results
            here = slice(base + n * HD, base + (n + 1) * HD)
            grad = [acc[0].T * SCALE, acc[1].T]
            for at, c, to in ((0, N1, 0), (2, N2, 1)):
                ok = row_ok(facts[c], PAGE, HD)
                for kind, out in ((0, dk12), (1, dv12)):
                    out[cols(to, to + 1), here] = jnp.where(
                        ok, grad[kind][cols(at, at + 1)], 0.0
                    ).astype(BF16)
            for kind in range(2):
                level2 = grad[kind][cols(1, 2)]
                own0[kind, :, here] = grad[kind][cols(3, 4)] + jnp.where(owns2, level2, 0.0)
                send2[kind, :, here] = level2.astype(BF16)

        def put_shared(n):
            (out,) = results
            here = slice(n * HD, (n + 1) * HD)
            grads = acc[0].T * SCALE, acc[1].T
            for j in range(2):
                for kind in range(2):
                    out[2 * j + kind, :, here] = grads[kind][cols(j, j + 1)].astype(out.dtype)

        sends = []
        for n, kv in enumerate(kvs):
            arrived(("q", kv), ("g", kv))
            head = Head(kv, group, norms, deltas, en, ed)
            set_pages(n, kv)

            for part in range(parts):
                slot = n * parts + part
                (own_part if own else shared_part)(
                    head, kv, part, n, stage.at[slot] if own and not fresh[n] else None
                )
                if own and not fresh[n]:
                    at = order.at(facts, kv, group * HD) + part * wide
                    sends.append(
                        pltpu.make_async_copy(
                            stage.at[slot],
                            held("gq").at[:, pl.ds(pl.multiple_of(at, wide), wide)],
                            sem.at[slot],
                        )
                    )
                    sends[-1].start()

            (put_own if own else put_shared)(n)
        for c in sends:
            c.wait()
        if loading:
            arrived(*list(copies))
            for heads in later:
                set_norms(*heads)

    made = kernel_call(
        body, facts, near, far, outs, scratch, aliases, after,
        pl.CostEstimate(
            flops=240 * PAGE * PAGE * HD * group * count, bytes_accessed=1000, transcendentals=0
        ),
        LARGE,
    )
    for name, at in at_out.items():
        state[name] = made[at]
    return list(made[at_results:at_loaded])


def width_tiles(w):
    tile = next(t for t in (512, 640, 320, 128, w.shape[0]) if w.shape[0] % t == 0)
    return [slice(i, i + tile) for i in range(0, w.shape[0], tile)]


def finish_queries(kvs, group, order, facts, pages, state, after=(), w=None):
    parts = group // min(4, group)
    heads = group // parts
    tall = heads * PAGE
    wide = heads * HD
    near = list(pages)
    for kv in kvs:
        near += [state["ds", kv], state["dq", kv]]

    def body(facts, *refs):
        stage, sem = refs[-2:]
        if w is not None:
            gq, made, w_near = refs[-5:-2]
            w_copy = pltpu.make_async_copy(refs[-6], w_near, sem.at[len(kvs) * parts])
            w_copy.start()
        else:
            gq, made = refs[-4:-2]
        made[...] = jnp.zeros_like(made)
        sends = []
        for n, kv in enumerate(kvs):
            ds, dq = refs[len(pages) + 2 * n : len(pages) + 2 * n + 2]
            page, at = refs[kv // order.half], kv % order.half * HD
            keys = jnp.concatenate([page[j, 0, :, at : at + HD] for j in range(2)], axis=0)
            for part in range(parts):
                at = n * parts + part
                gained = dot_n(ds[part * SLOTS * tall : (part + 1) * SLOTS * tall], keys)
                for i in range(SLOTS * heads):
                    slot, j = divmod(i, heads)
                    rows = slice(slot * PAGE, (slot + 1) * PAGE)
                    value = gained[i * PAGE : (i + 1) * PAGE] + dq[
                        rows, part * wide + j * HD : part * wide + (j + 1) * HD
                    ]
                    stage[at, rows, j * HD : (j + 1) * HD] = (value * SCALE).astype(BF16)
                to = pl.multiple_of(order.at(facts, kv, group * HD) + part * wide, wide)
                sends.append(
                    pltpu.make_async_copy(stage.at[at], gq.at[:, pl.ds(to, wide)], sem.at[at])
                )
                sends[-1].start()
        for c in sends:
            c.wait()
        if w is not None:
            w_copy.wait()

    count = len(kvs) * parts
    far = [state["gq"]] if "gq" in state else []
    aliases = {("far", 0): 0} if far else {}
    shape = (ROWS, state["k"].shape[1] * group)
    outs = [(shape, BF16, False), ((8, HD), F32, True)]
    if w is not None:
        far = far + [w]
        outs.append((w.shape, w.dtype, True))
    state["gq"], *made = kernel_call(
        body, facts, near, far, outs,
        [pltpu.VMEM((count, ROWS, wide), BF16), pltpu.SemaphoreType.DMA((count + 1,))],
        aliases, after, limit=LARGE,
    )
    return made


def input_grad(order, facts, w, rows, own, far, grads, carry=None, near_w=False, after=()):
    out_cols, depth = w.shape
    tiles = width_tiles(w)
    top = 0 if rows == PAGE else PAGE
    steps = len(tiles)
    width = sum(a.shape[1] for a in grads[0])
    arrays = [*own, *far, *grads[0], *grads[1]] + [w] * near_w
    count = len(grads[0])
    carry = list(carry or [])
    lead = [] if near_w else [w]
    rest = [*lead, *carry, *after]

    def body(facts, *refs):
        own_r, refs = refs[: len(own)], refs[len(own) :]
        far_r, refs = refs[: len(far)], refs[len(far) :]
        grad_r, w_ref = refs[: 2 * count], refs[2 * count]
        out, dk, dv, made, w_near, stage, w_sem, sem = refs[-8:]
        loads = []
        if not near_w:
            loads = [
                pltpu.make_async_copy(w_ref.at[at], w_near.at[at], w_sem.at[i])
                for i, at in enumerate(tiles)
            ]
        for c in loads:
            c.start()
        made[...] = jnp.zeros_like(made)
        columns = lambda rs: jnp.concatenate([r[...] for r in rs], axis=1)
        full = order.real(facts, columns(own_r))
        if far:
            other, first = order.real(facts, columns(far_r)), facts[SIDE] == 0
            full = jnp.concatenate(
                [jnp.where(first, full, other), jnp.where(first, other, full)], axis=1
            )
        copies = put_rows(order, facts, grad_r, dk, dv, top, rows, sem, steps)
        for i, at in enumerate(tiles):
            if loads:
                loads[i].wait()
            stage[i] = dot_t((w_ref if near_w else w_near)[at], full).astype(BF16).T
            copies.append(
                pltpu.make_async_copy(stage.at[i], out.at[top : top + rows, at], sem.at[i])
            )
            copies[-1].start()
        for c in copies:
            c.wait()

    smem = pl.BlockSpec(memory_space=pltpu.SMEM)
    vmem = pl.BlockSpec(memory_space=pltpu.VMEM)
    hbm = pl.BlockSpec(memory_space=pl.ANY)
    arrays = [pltpu.with_memory_space_constraint(a, pltpu.VMEM) for a in arrays]
    kept = jax.ShapeDtypeStruct((ROWS, width), BF16)
    return pl.pallas_call(
        body,
        out_shape=(
            jax.ShapeDtypeStruct((ROWS, out_cols), BF16), kept, kept, pltpu.VMEM((8, HD), F32)
        ),
        in_specs=[smem] + [vmem] * len(arrays) + [hbm] * len(rest),
        out_specs=(hbm, hbm, hbm, vmem),
        scratch_shapes=[
            pltpu.VMEM((8, HD) if near_w else w.shape, BF16),
            pltpu.VMEM((steps, rows, out_cols // steps), BF16),
            pltpu.SemaphoreType.DMA((steps,)),
            pltpu.SemaphoreType.DMA((steps + 2 * order.heads,)),
        ],
        input_output_aliases={
            1 + len(arrays) + len(lead) + i: i for i in range(len(carry))
        },
        compiler_params=pltpu.CompilerParams(vmem_limit_bytes=LARGE),
        cost_estimate=SLIGHT,
    )(pltpu.with_memory_space_constraint(facts, pltpu.SMEM), *arrays, *rest)


def put_rows(order, facts, pieces, dk, dv, top, rows, sem, first):
    copies = []
    count = len(pieces) // 2
    for dst, mine in ((dk, pieces[:count]), (dv, pieces[count:])):
        head = 0
        for src in mine:
            more = src.shape[1] // HD
            for lo, hi in order.runs(head, head + more):
                copies.append(
                    pltpu.make_async_copy(
                        src.at[:, (lo - head) * HD : (hi - head) * HD],
                        dst.at[top : top + rows, pl.ds(order.at(facts, lo, HD), (hi - lo) * HD)],
                        sem.at[first + len(copies)],
                    )
                )
                copies[-1].start()
            head += more
    return copies


def begin_input_grad(order, facts, w, own, after=()):
    out_cols, depth = w.shape
    half = depth // 2
    rows = own[0].shape[0]
    count = len(own)

    def body(facts, w_ref, *refs):
        mine, out = jnp.concatenate([r[...] for r in refs[:count]], axis=1), refs[-1]
        mine = order.real(facts, mine)
        where = pl.ds(pl.multiple_of(facts[SIDE] * half, half), half)
        for at in width_tiles(w):
            out[at] = dot_t(w_ref[at, where], mine)

    smem = pl.BlockSpec(memory_space=pltpu.SMEM)
    vmem = pl.BlockSpec(memory_space=pltpu.VMEM)
    near = [pltpu.with_memory_space_constraint(a, pltpu.VMEM) for a in (w, *own)]

    def kernel(*refs):
        body(*refs[: 2 + count], refs[-1])

    return pl.pallas_call(
        kernel,
        out_shape=pltpu.VMEM((out_cols, rows), F32),
        in_specs=[smem] + [vmem] * len(near) + [pl.BlockSpec(memory_space=pl.ANY)] * len(after),
        out_specs=vmem,
        compiler_params=pltpu.CompilerParams(vmem_limit_bytes=LARGE),
        cost_estimate=SLIGHT,
    )(pltpu.with_memory_space_constraint(facts, pltpu.SMEM), *near, *after)


def end_input_grad(order, facts, w, base, across, corner, begun, grads, carry):
    tiles = width_tiles(w)
    out_cols, depth = w.shape
    half = depth // 2
    steps = len(tiles)
    rows = base.shape[0]

    def body(facts, w_r, begun_r, base_r, across_r, corner_r, *refs):
        out, dk, dv, stage, sem = refs[-5:]
        copies = put_rows(order, facts, refs[:2], dk, dv, 0, rows, sem, steps)
        gained = jnp.concatenate([corner_r[...], across_r[...]], axis=1).astype(F32)
        known = base_r[...]
        more = jnp.where(row_ok(facts[N0], rows, half), known.astype(F32) + gained, 0.0)
        other = order.real(facts, jnp.where(facts[OWNS2] == 1, known, more.astype(BF16)))
        where = pl.ds(pl.multiple_of((1 - facts[SIDE]) * half, half), half)
        for i, at in enumerate(tiles):
            stage[i] = (dot_t(w_r[at, where], other) + begun_r[at]).astype(BF16).T
            copies.append(pltpu.make_async_copy(stage.at[i], out.at[:rows, at], sem.at[i]))
            copies[-1].start()
        for c in copies:
            c.wait()

    return kernel_call(
        body, facts, [w, begun, base, across, corner, *grads], list(carry),
        [(a.shape, a.dtype, False) for a in carry],
        [
            pltpu.VMEM((steps, rows, out_cols // steps), BF16),
            pltpu.SemaphoreType.DMA((steps + 2 * order.heads,)),
        ],
        {("far", i): i for i in range(len(carry))},
    )


def flipped(block, axis, bit):
    count = lax.axis_size(axis)
    return lax.ppermute(block, axis, [(i, i ^ bit) for i in range(count) if i ^ bit < count])


def spanning(leaves, bit_index):
    return len([j for j in range(INNER) if 2 << bit_index <= leaves >> j])


def gather_small_tree(facts, own, beside_pair, beside_half):
    width = own.shape[-1] // 2
    page = ((2, PAGE, width), BF16, True)
    from_core = flipped(own, "sub", 1)

    def choose_chip(facts, own_ref, far_ref, out):
        for swap in range(2):
            for mine in range(2):

                @pl.when((facts[SWAP] == swap) & (facts[OWNS2] != mine))
                def _copy(swap=swap, mine=mine):
                    out[...] = (own_ref if mine else far_ref)[
                        :, :, swap * width : (swap + 1) * width
                    ]

    (chip,) = kernel_call(choose_chip, facts, [own, from_core], [], [page])
    from_pair = flipped(chip, "leaf", 1)

    def choose_pair(facts, near_ref, far_ref, out):
        out[...] = jnp.where(facts[ROOT_IN_CHIP] == 1, near_ref[...], far_ref[...])

    after = beside_pair(from_core, chip)
    (pair,) = kernel_call(choose_pair, facts, [chip, from_pair], [], [page], after=after)
    from_half = flipped(pair, "leaf", 2)

    def choose_all(facts, chip_ref, pair_far, pair_ref, half_far, out):
        out[0] = jnp.where(facts[ROOT_IN_PAIR] == 1, pair_ref[...], half_far[...])
        out[1] = jnp.where(facts[NEXT_IN_CHIP] == 1, chip_ref[...], pair_far[...])

    after = beside_half(pair)
    (mine,) = kernel_call(
        choose_all, facts, [chip, from_pair, pair, from_half], [],
        [((2, *page[0]), BF16, True)], after=after,
    )
    return mine, flipped(mine, "sub", 1)


def over_cores(facts, kept, far):
    width = kept.shape[-1]

    def body(_, near, away, total, root, next_one):
        for i in range(4):
            value = near[i] + away[i].astype(F32)
            total[i] = value
            (root, next_one)[i // 2][i % 2] = value.astype(BF16)

    pages = ((2, PAGE, width), BF16, True)
    total, root, next_one = kernel_call(
        body, facts, [kept, far], [], [((4, PAGE, width), F32, True), pages, pages]
    )
    return total, root, flipped(root, "leaf", 2), flipped(next_one, "leaf", 1)


def over_halves(facts, total, root_far, next_far, after):
    width = total.shape[-1]

    def body(_, near, root_r, next_r, out, low):
        root = near[:2] + root_r[...].astype(F32)
        out[:2] = root
        low[...] = root.astype(BF16)
        out[2:] = near[2:] + next_r[...].astype(F32)

    total, low = kernel_call(
        body, facts, [total, root_far, next_far], [],
        [((4, PAGE, width), F32, True), ((2, PAGE, width), BF16, True)], after=after,
    )
    return total, low, flipped(low, "leaf", 1)


def over_chips(facts, total, far, after):
    width = total.shape[-1]

    def body(facts, near, away, out, values):
        root = near[:2] + away[...].astype(F32)
        picked = jnp.where(facts[ROOT_IN_CHIP] == 1, root, near[2:]).astype(BF16)
        out[...] = picked
        values[...] = picked[1]

    outs = [((2, PAGE, width), BF16, True), ((PAGE, width), BF16, True)]
    mine, values = kernel_call(body, facts, [total, far], [], outs, after=after)
    across = flipped(values, "tensor", 1)
    corner = lax.ppermute(values, ("tensor", "sub"), [(i, 3 - i) for i in range(4)])
    return mine, flipped(mine, "sub", 1), across, corner


def other_level2(order, head, kind, ref):
    theirs = head ^ order.half
    at = theirs % order.half * HD
    return ref[4 + 2 * (theirs // order.half) + kind, :, at : at + HD]


def begin_values(order, facts, own0, level2_far):
    def body(facts, own_r, low_r, out):
        ok = row_ok(facts[N0], PAGE, HD)
        for head in range(order.heads):
            c = slice(head * HD, (head + 1) * HD)
            low = other_level2(order, head, 1, low_r).astype(F32)
            value = own_r[1, :, c] + jnp.where(facts[OWNS2] == 1, low, 0.0)
            out[:, c] = jnp.where(ok, value, 0.0).astype(BF16)

    outs = [((PAGE, own0.shape[-1]), BF16, True)]
    return kernel_call(body, facts, [own0, level2_far], [], outs)[0]


def finish_small_tree(order, facts, own0, mine, far, level2_far):
    width = own0.shape[-1]

    def body(facts, own_r, mine_r, far_r, low_r, dk, dv):
        owns2 = facts[OWNS2] == 1
        ok = row_ok(facts[N0], PAGE, HD)
        for head in range(order.heads):
            c = slice(head * HD, (head + 1) * HD)
            at = head % order.half * HD
            for kind, out in enumerate((dk, dv)):
                gained = (far_r if head < order.half else mine_r)[kind, :, at : at + HD]
                level2 = other_level2(order, head, kind, low_r)
                more = jnp.where(owns2, level2, gained).astype(F32)
                out[:, c] = jnp.where(ok, own_r[kind, :, c] + more, 0.0).astype(BF16)

    page = ((PAGE, width), BF16, True)
    return kernel_call(body, facts, [own0, mine, far, level2_far], [], [page, page])


def gather_tree(ids, own):
    leaves = lax.axis_size(("leaf", "sub"))
    owned = ids[:INNER] == ids[INNER] - 1
    pages = jnp.where(owned[:, None, None, None], own[None], jnp.zeros((), BF16))
    for bit in range(leaves.bit_length() - 1):
        active = spanning(leaves, bit)
        far = flipped(pages[:active], ("leaf", "sub"), 1 << bit)
        pages = jnp.concatenate([pages[:active] + far, pages[active:]])
    return pages


def reduce_tree(ids, parts):
    leaves = lax.axis_size(("leaf", "sub"))
    for bit in range(leaves.bit_length() - 1):
        active = spanning(leaves, bit)
        far = flipped(parts[:active], ("leaf", "sub"), 1 << bit)
        parts = jnp.concatenate([parts[:active] + far, parts[active:]])
    owned = ids[:INNER] == ids[INNER] - 1
    return jnp.sum(jnp.where(owned[:, None, None, None], parts, 0.0), axis=0)


def on_device(queries, grad_out, keys, values, log_norms, row_deltas, ancestors, counts, w_value):
    kv = keys.shape[1] // HD
    group = queries.shape[1] // keys.shape[1]
    leaves = lax.axis_size(("leaf", "sub"))
    hbm = lambda a: pltpu.with_memory_space_constraint(a, pltpu.HBM)
    side = lax.axis_index("tensor").astype(I32).reshape(1)
    two_sides = lax.axis_size("tensor") == 2
    inputs = [hbm(a) for a in (queries, grad_out, keys, values, log_norms, row_deltas)]
    fast = leaves == 8 and lax.axis_size("sub") == 2 and kv == 4 and two_sides
    order = Order(fast, kv)
    facts, own = start(order, side, hbm(ancestors), hbm(counts), *inputs[2:4])
    state = {}

    def own_pages(kvs, pages, prior=(), after=()):
        return attend(True, kvs, group, order, facts, inputs, pages, state, prior, after)

    def shared_pages(kvs, page, ride=None, after=()):
        return attend(
            False, kvs, group, order, facts, inputs, [page], state, after=after, ride=ride
        )[0]

    def spread(part):
        if two_sides:
            return flipped(part, "tensor", 1)
        return lax.all_gather(part, "tensor", axis=1, tiled=True)

    kvs = tuple(range(kv))
    w = hbm(w_value)
    if fast:
        level2, halves = [], []

        def beside_pair(from_core, chip):
            level2.extend((own, from_core))
            halves.append(own_pages(kvs[:2], level2, after=(chip,)))
            return (halves[0][3],)

        def beside_half(pair):
            halves.append(own_pages(kvs[2:], level2, halves[0], (pair,)))
            return (halves[1][3],)

        mine, theirs = gather_small_tree(facts, own, beside_pair, beside_half)
        dk12, dv12, own0, send2 = halves[1]
        sent = flipped(shared_pages(kvs[:2], mine, send2), "sub", 1)
        kept = shared_pages(kvs[2:], theirs)
        total, root, root_far, next_far = over_cores(facts, kept, sent)
        far_v = spread(dv12)
        base = begin_values(order, facts, own0, sent)
        made, w_near = finish_queries(
            kvs, group, order, facts, (mine, theirs), state, (root, base), w
        )
        total, low, far = over_halves(facts, total, root_far, next_far, (made,))
        base_far = spread(base)
        *grads, made = input_grad(
            order, facts, w_near, 2 * PAGE, [dv12], [far_v], ([dk12], [dv12]), near_w=True,
            after=(low,),
        )
        near, far, across, corner = over_chips(facts, total, far, (made, base_far))
        dk0, dv0 = finish_small_tree(order, facts, own0, near, far, sent)
        begun = begin_input_grad(order, facts, w_near, [dv0])
        grads = end_input_grad(
            order, facts, w_near, base_far, across, corner, begun, [dk0, dv0], grads
        )
        return (state["gq"], grads[1], grads[2], grads[0])

    path_ids = ancestors[0]
    pages = gather_tree(path_ids, own)
    dk12, dv12, own0, send2 = own_pages(kvs, (pages[2], pages[2]))
    grads = shared_pages(kvs, pages[:2])
    finish_queries(kvs, group, order, facts, (pages[:2],), state)
    low = send2.astype(F32)
    total = reduce_tree(path_ids, jnp.concatenate([grads.reshape(2, 2, *grads.shape[1:]), low[None]]))
    total += own0 - jnp.where(path_ids[2] == path_ids[INNER] - 1, low, 0.0)
    has = jnp.any(path_ids[:INNER] == path_ids[INNER] - 1)
    ok = (jnp.arange(PAGE) < jnp.where(has, counts[0, 0], 0))[:, None]
    dk0, dv0 = jnp.where(ok, total, 0.0).astype(BF16)
    if two_sides:
        pair = lambda part: ([part], [spread(part)])
    else:
        pair = lambda part: ([spread(part)], [])
    *grads, _ = input_grad(order, facts, w, 2 * PAGE, *pair(dv12), ([dk12], [dv12]))
    grads = input_grad(order, facts, w, PAGE, *pair(dv0), ([dk0], [dv0]), grads)
    return (state["gq"], grads[1], grads[2], grads[0])


def solution(mesh):
    placed = (
        P(("groups", "leaf", "sub"), "tensor"),
        P(("groups", "leaf", "sub"), "tensor"),
        P(("groups", "leaf", "sub"), "tensor"),
        P(("groups", "leaf", "sub"), "tensor"),
        P("tensor", ("groups", "leaf", "sub")),
        P("tensor", ("groups", "leaf", "sub")),
        P(("groups", "leaf", "sub"), None),
        P(("groups", "leaf", "sub"), None),
        P("tensor", None),
    )
    return jax.shard_map(
        on_device,
        mesh=mesh,
        in_specs=placed,
        out_specs=(
            P(("groups", "leaf", "sub"), "tensor"),
            P(("groups", "leaf", "sub"), "tensor"),
            P(("groups", "leaf", "sub"), "tensor"),
            P(("groups", "leaf", "sub"), "tensor"),
        ),
        check_vma=False,
    )
```

```python
import math

import jax
import jax.numpy as jnp
from jax import lax
from jax.experimental import pallas as pl
from jax.experimental.pallas import tpu as pltpu
from jax.sharding import PartitionSpec as P

HD = 128
PAGE = 128
SLOTS = 3
INNER = 3
ROWS = SLOTS * PAGE
LOG2E = math.log2(math.e)
SCALE = 1.0 / math.sqrt(HD)
BF16 = jnp.bfloat16
F32 = jnp.float32
I32 = jnp.int32
LARGE = 10 << 20
SMALL = 4 << 20
SLIGHT = pl.CostEstimate(flops=1000, bytes_accessed=1000, transcendentals=0)
BLOCKED = 1e30


def dot_t(left, right):
    return lax.dot_general(left, right, (((1,), (1,)), ((), ())), preferred_element_type=F32)


def dot_n(left, right):
    return lax.dot_general(left, right, (((1,), (0,)), ((), ())), preferred_element_type=F32)


FACTS = 16
N0, N1, N2, OWNS2, LIMIT, LEADS, ROOT_IN_CHIP, ROOT_IN_PAIR, NEXT_IN_CHIP, SIDE, SWAP = range(11)


class Order:
    def __init__(self, crossed, heads):
        self.crossed, self.heads = crossed, heads
        self.half = heads // 2 if crossed else heads

    def at(self, facts, head, unit):
        if not self.crossed:
            return head * unit
        step = ((head ^ self.half) - head) * unit
        return pl.multiple_of(facts[SWAP] * step + head * unit, unit)

    def runs(self, first, last):
        cuts = [first, *(h for h in range(first + 1, last) if h % self.half == 0), last]
        return list(zip(cuts[:-1], cuts[1:]))

    def real(self, facts, rows):
        if not self.crossed:
            return rows
        width = self.half * HD
        turned = jnp.concatenate([rows[:, width:], rows[:, :width]], axis=1)
        return jnp.where(facts[SWAP] == 1, turned, rows)


def write_facts(facts, ids, counts, side, order):
    page = [ids[0, j] for j in range(INNER + 1)]
    own = page[INNER] - 1
    leaf = own // SLOTS
    owns = [page[j] == own for j in range(INNER)]
    same = lambda level, shift: ((page[level] // SLOTS) >> shift) == (leaf >> shift)
    number = lambda flag: jnp.where(flag, 1, 0)
    facts[N0] = jnp.where(owns[0] | owns[1] | owns[2], counts[0, 0], 0)
    facts[N1] = counts[0, 1]
    facts[N2] = counts[0, 2]
    facts[OWNS2] = number(owns[2])
    facts[LIMIT] = jnp.where(owns[2], 2 * PAGE, jnp.where(owns[1], PAGE, 0))
    facts[LEADS] = number(lax.rem(leaf, 2) == 0)
    facts[ROOT_IN_CHIP] = number(same(0, 1))
    facts[ROOT_IN_PAIR] = number(same(0, 2))
    facts[NEXT_IN_CHIP] = number(same(1, 1))
    facts[SIDE] = side
    facts[SWAP] = lax.rem(leaf, 2) if order.crossed else 0
    for i in range(SWAP + 1, FACTS):
        facts[i] = 0


def row_ok(count, rows, width):
    return lax.broadcasted_iota(I32, (rows, width), 0) < count


def kernel_call(body, facts, near, far, outs, scratch=(), aliases=None, after=(), cost=None,
                limit=SMALL):
    smem = pl.BlockSpec(memory_space=pltpu.SMEM)
    vmem = pl.BlockSpec(memory_space=pltpu.VMEM)
    hbm = pl.BlockSpec(memory_space=pl.ANY)
    near = [pltpu.with_memory_space_constraint(a, pltpu.VMEM) for a in near]
    place = {("near", i): 1 + i for i in range(len(near))}
    place |= {("far", i): 1 + len(near) + i for i in range(len(far))}
    used = 1 + len(near) + len(far)

    def kernel(*refs):
        body(*refs[:used], *refs[used + len(after) :])

    return pl.pallas_call(
        kernel,
        out_shape=tuple(
            pltpu.VMEM(s, d) if inside else jax.ShapeDtypeStruct(s, d) for s, d, inside in outs
        ),
        in_specs=[smem] + [vmem] * len(near) + [hbm] * (len(far) + len(after)),
        out_specs=tuple(vmem if inside else hbm for _, _, inside in outs),
        scratch_shapes=list(scratch),
        input_output_aliases={place[k]: v for k, v in (aliases or {}).items()},
        compiler_params=pltpu.CompilerParams(vmem_limit_bytes=limit),
        cost_estimate=cost or SLIGHT,
    )(pltpu.with_memory_space_constraint(facts, pltpu.SMEM), *near, *far, *after)


def start(order, side, ids, counts, keys, values):
    width = keys.shape[1]

    def body(side_ref, ids_ref, counts_ref, k_ref, v_ref, facts, out, held, ids_s, counts_s, sem):
        copies = [
            pltpu.make_async_copy(src, dst, sem.at[i])
            for i, (src, dst) in enumerate(
                (
                    (ids_ref, ids_s),
                    (counts_ref, counts_s),
                    (k_ref.at[:PAGE], held.at[0]),
                    (v_ref.at[:PAGE], held.at[1]),
                )
            )
        ]
        for c in copies:
            c.start()
        copies[0].wait()
        copies[1].wait()
        write_facts(facts, ids_s, counts_s, side_ref[0], order)
        ok = row_ok(counts_s[0, 0], PAGE, width)
        for i in range(2):
            copies[2 + i].wait()
            out[i] = jnp.where(ok, held[i], jnp.zeros((), BF16))

    smem = pl.BlockSpec(memory_space=pltpu.SMEM)
    hbm = pl.BlockSpec(memory_space=pl.ANY)
    return pl.pallas_call(
        body,
        out_shape=(pltpu.SMEM((FACTS,), I32), pltpu.VMEM((2, PAGE, width), BF16)),
        in_specs=[smem] + [hbm] * 4,
        out_specs=(smem, pl.BlockSpec(memory_space=pltpu.VMEM)),
        scratch_shapes=[
            pltpu.VMEM((2, PAGE, width), BF16),
            pltpu.SMEM(ids.shape, I32),
            pltpu.SMEM(counts.shape, I32),
            pltpu.SemaphoreType.DMA((4,)),
        ],
        compiler_params=pltpu.CompilerParams(vmem_limit_bytes=SMALL),
    )(side, ids, counts, keys, values)


def row_terms(rows):
    high = rows.astype(BF16).astype(F32)
    rest = rows - high
    middle = rest.astype(BF16).astype(F32)
    parts = [high, middle, rest - middle]
    spare = HD - 3 * rows.shape[0]
    parts.append(jnp.zeros((spare, rows.shape[1]), F32))
    return jnp.concatenate(parts, axis=0).T.astype(BF16)


class Head:
    def __init__(self, kv, group, norms, deltas, en, ed):
        self.group = group
        self.heads = min(4, group)
        self.parts = group // self.heads
        self.tall = self.heads * PAGE
        heads = slice(kv * group, (kv + 1) * group)
        en[...] = row_terms(norms[heads, :])
        ed[...] = row_terms(deltas[heads, :])

    def lanes(self, part, j):
        at = (part * self.heads + j) * HD
        return slice(at, at + HD)

    def stacked(self, ref, part, slots):
        return jnp.concatenate(
            [
                ref[slot * PAGE : (slot + 1) * PAGE, self.lanes(part, j)]
                for slot in slots
                for j in range(self.heads)
            ],
            axis=0,
        )

    def deep(self, stacked, terms, part, slots):
        column = lax.broadcasted_iota(I32, (1, HD), 1) % self.group
        picks = [
            (column == part * self.heads + j).astype(F32).astype(BF16)
            for j in range(self.heads)
        ]
        extra = [
            terms[slot * PAGE : (slot + 1) * PAGE] * pick for slot in slots for pick in picks
        ]
        return jnp.concatenate([stacked, jnp.concatenate(extra, axis=0)], axis=1)

    def turned_at(self, part, slot, count):
        at = (part * SLOTS + slot) * self.tall
        return slice(at, at + self.tall * count)

    def put_queries(self, part, slot, rows_by_head, dq, add, stage):
        rows = slice(slot * PAGE, (slot + 1) * PAGE)
        for j in range(self.heads):
            value = rows_by_head[j * PAGE : (j + 1) * PAGE]
            if stage is None:
                dq[rows, self.lanes(part, j)] = value
            else:
                if add:
                    value = value + dq[rows, self.lanes(part, j)]
                stage[rows, j * HD : (j + 1) * HD] = (value * SCALE).astype(BF16)


def set_keys(deep, upright, at, page):
    where = slice(at * PAGE, (at + 1) * PAGE)
    deep[:HD, where] = page.T
    if upright is not None:
        upright[where] = page


def weigh(scores, grads, keep):
    p = keep(jnp.exp2(scores * (SCALE * LOG2E)))
    return p.astype(BF16), (p * grads).astype(BF16)


def attend(own, kvs, group, order, facts, inputs, pages, state, prior=(), after=(),
           ride=None):
    loading = "k" not in state
    q_all, k_all = inputs[0], inputs[2]
    count = len(kvs)
    parts = group // min(4, group)
    tall = min(4, group) * PAGE
    wide = min(4, group) * HD
    width = count * HD
    base = prior[0].shape[1] if prior else 0
    kv_total = k_all.shape[1] // HD
    fresh = [("dq", kv) not in state for kv in kvs]
    one_head = (ROWS, group * HD)
    turned = ((HD, group * ROWS), BF16, True)
    shapes = {"dq": (one_head, F32, True), "qt": turned, "gt": turned}

    near, far, aliases, outs = [], [], {}, []
    at_near, at_far, at_out = {}, {}, {}

    def add_near(name, array):
        at_near[name] = len(near)
        near.append(array)

    def add_far(name, array):
        at_far[name] = len(far)
        far.append(array)

    def add_out(name, out):
        at_out[name] = len(outs)
        outs.append(out)

    for kv, is_fresh in zip(kvs, fresh):
        for name, shape in shapes.items():
            if is_fresh:
                add_out((name, kv), shape)
            elif own or name != "dq":
                add_near((name, kv), state[name, kv])
        if not own and not is_fresh:
            add_out(("ds", kv), ((group * ROWS, 2 * PAGE), BF16, True))
    if own and not all(fresh):
        add_out("gq", (q_all.shape, BF16, False))
        if "gq" in state:
            add_far("gq", state["gq"])
            aliases["far", at_far["gq"]] = at_out["gq"]
    at_results = len(outs)
    if own:
        outs += [
            ((2 * PAGE, base + width), BF16, True),
            ((2 * PAGE, base + width), BF16, True),
            ((2, PAGE, base + width), F32, True),
            ((2, PAGE, base + width), BF16, True),
        ]
    else:
        outs += [
            ((4, PAGE, width), F32, True) if ride is None else ((8, PAGE, width), BF16, True),
        ]
    at_loaded = len(outs)
    if loading:
        for name, array in zip(("q", "g", "k", "v", "norms", "deltas"), inputs):
            add_far(name, array)
            if name in ("q", "g"):
                for kv in range(kv_total):
                    add_out((name, kv), (one_head, BF16, True))
            else:
                add_out(name, (array.shape, array.dtype, True))
    else:
        for name in ("k", "v", "norms", "deltas"):
            add_near(name, state[name])
        for kv in kvs:
            for name in ("q", "g"):
                add_near((name, kv), state[name, kv])
    for i, page in enumerate(pages):
        add_near(("page", i), page)
    for i, array in enumerate(prior):
        add_near(("prior", i), array)
    if ride is not None:
        add_near("ride", ride)
    key_pages = 4 if own else 2
    scratch = [
        pltpu.VMEM((2 * HD, key_pages * PAGE), BF16),
        pltpu.VMEM((2 * HD, key_pages * PAGE), BF16),
        pltpu.VMEM((key_pages * PAGE, HD), BF16),
        pltpu.VMEM((2, HD, key_pages * PAGE), F32),
        pltpu.VMEM((ROWS, HD), BF16),
        pltpu.VMEM((ROWS, HD), BF16),
        pltpu.VMEM((count * parts, ROWS, wide), BF16),
        pltpu.SemaphoreType.DMA((count * parts,)),
        pltpu.SemaphoreType.DMA((2 * kv_total + 8,)),
    ]
    cols = lambda a, b: slice(a * PAGE, b * PAGE)

    def body(facts, *refs):
        ins, out_refs = refs[: len(near) + len(far)], refs[len(near) + len(far) : -len(scratch)]
        k_deep, v_deep, k_up, acc, en, ed, stage, sem, load_sem = refs[-len(scratch) :]
        near_ref = lambda name: ins[at_near[name]]
        far_ref = lambda name: ins[len(near) + at_far[name]]
        held = lambda name: out_refs[at_out[name]] if name in at_out else near_ref(name)
        results = out_refs[at_results:at_loaded]
        copies = {}
        if loading:

            def load(key, src, dst):
                copies[key] = pltpu.make_async_copy(src, dst, load_sem.at[len(copies)])
                copies[key].start()

            for lo, hi in order.runs(0, kv_total):
                for name in ("k", "v"):
                    at = pl.ds(order.at(facts, lo, HD), (hi - lo) * HD)
                    here = slice(lo * HD, hi * HD)
                    load((name, lo), far_ref(name).at[:, at], held(name).at[:, here])
                for name in ("norms", "deltas"):
                    at = pl.ds(order.at(facts, lo, group), (hi - lo) * group)
                    here = slice(lo * group, hi * group)
                    load((name, lo), far_ref(name).at[at], held(name).at[here])
            shared_loads = list(copies)
            for kv in range(kv_total):
                at = pl.ds(order.at(facts, kv, group * HD), group * HD)
                for name in ("q", "g"):
                    load((name, kv), far_ref(name).at[:, at], held((name, kv)))
        k, v, norms, deltas = (held(name) for name in ("k", "v", "norms", "deltas"))

        def arrived(*keys):
            for key in keys:
                if key in copies:
                    copies.pop(key).wait()

        k_deep[HD:] = jnp.full((HD, key_pages * PAGE), -1.0, BF16)
        v_deep[HD:] = jnp.full((HD, key_pages * PAGE), -1.0, BF16)
        for out, i in zip(results, range(len(prior))):
            out[..., :base] = near_ref(("prior", i))[...]
        if ride is not None:
            (out,), more = results, near_ref("ride")
            for kind in range(2):
                out[4 + kind] = more[kind, :, :width]
                out[6 + kind] = more[kind, :, width:]
        owns2 = facts[OWNS2] == 1
        if loading:
            arrived(*shared_loads)
            lane = lax.broadcasted_iota(I32, norms.shape, 1)
            limit = jnp.where(
                lane < PAGE, facts[N0], jnp.where(lane < 2 * PAGE, facts[N1], facts[N2])
            )
            norms[...] = jnp.where(lane % PAGE < limit, norms[...] * (1.0 / SCALE), BLOCKED)
        lower = lambda rows: lax.broadcasted_iota(I32, (rows, PAGE), 1) <= (
            lax.broadcasted_iota(I32, (rows, PAGE), 0) % PAGE
        )

        def set_pages(n, kv):
            lane = slice(kv * HD, (kv + 1) * HD)
            if own:
                first, second = (near_ref(("page", i)) for i in range(2))
                zero = jnp.zeros((), BF16)
                for slot, (at, c) in enumerate(((3, N0), (0, N1), (2, N2))):
                    ok = row_ok(facts[c], PAGE, HD)
                    rows = cols(slot, slot + 1)
                    set_keys(k_deep, k_up, at, jnp.where(ok, k[rows, lane], zero))
                    set_keys(v_deep, None, at, jnp.where(ok, v[rows, lane], zero))
                level2 = [jnp.where(owns2, first[i, :, lane], second[i, :, lane]) for i in (0, 1)]
                if order.crossed:
                    at = (kv ^ order.half) * HD
                    lane = slice(at, at + HD)
                    for i in range(2):
                        other = jnp.where(owns2, first[i, :, lane], second[i, :, lane])
                        level2[i] = jnp.where(facts[SWAP] == 1, other, level2[i])
                set_keys(k_deep, k_up, 1, level2[0])
                set_keys(v_deep, None, 1, level2[1])
            else:
                page = near_ref(("page", 0))
                for j in range(2):
                    here = slice(n * HD, (n + 1) * HD)
                    set_keys(k_deep, k_up, j, page[j, 0, :, here])
                    set_keys(v_deep, None, j, page[j, 1, :, here])
            acc[...] = jnp.zeros_like(acc)

        def turned_rows(head, kv, part, is_fresh, qs, gs, order):
            if is_fresh:
                for name, rows in (("qt", qs), ("gt", gs)):
                    for i, slot in enumerate(order):
                        held((name, kv))[:, head.turned_at(part, slot, 1)] = rows[
                            i * tall : (i + 1) * tall
                        ].T
            return lambda name, slot, slots: held((name, kv))[
                :, head.turned_at(part, slot, slots)
            ]

        def own_part(head, kv, part, n, stage_ref):
            order = (1, 2, 0)
            qs = head.stacked(held(("q", kv)), part, order)
            gs = head.stacked(held(("g", kv)), part, order)
            qd, gd = head.deep(qs, en, part, order), head.deep(gs, ed, part, order)
            turn = turned_rows(head, kv, part, fresh[n], qs, gs, order)
            low = lower(tall)

            def keep_first(p):
                masked = jnp.where(low, p[:tall, :PAGE], 0.0)
                return jnp.concatenate(
                    [jnp.concatenate([masked, p[:tall, PAGE:]], axis=1), p[tall:]], axis=0
                )

            pa, da = weigh(
                dot_n(qd[: 2 * tall], k_deep[:, : 2 * PAGE]),
                dot_n(gd[: 2 * tall], v_deep[:, : 2 * PAGE]),
                keep_first,
            )
            both = lambda x: jnp.concatenate([x[:tall, :PAGE], x[tall:, PAGE:]], axis=0)
            low2 = lower(2 * tall)
            pb, db = weigh(
                both(dot_n(qd[tall:], k_deep[:, 2 * PAGE :])),
                both(dot_n(gd[tall:], v_deep[:, 2 * PAGE :])),
                lambda p: jnp.where(low2, p, 0.0),
            )
            for i, (name, a, b) in enumerate((("qt", da, db), ("gt", pa, pb))):
                acc[i, :, : 2 * PAGE] += dot_n(turn(name, 1, 2), a)
                acc[i, :, cols(2, 3)] += dot_n(turn(name, 2, 1), b[:tall])
                acc[i, :, cols(3, 4)] += dot_n(turn(name, 0, 1), b[tall:])
            first = dot_n(da, k_up[: 2 * PAGE])
            put = lambda slot, rows: head.put_queries(
                part, slot, rows, held(("dq", kv)), not fresh[n], stage_ref
            )
            put(1, first[:tall])
            put(2, first[tall:] + dot_n(db[:tall], k_up[cols(2, 3)]))
            put(0, dot_n(db[tall:], k_up[cols(3, 4)]))

        def shared_part(head, kv, part, n, stage_ref):
            order = (0, 1, 2)
            qs = head.stacked(held(("q", kv)), part, order)
            gs = head.stacked(held(("g", kv)), part, order)
            qd, gd = head.deep(qs, en, part, order), head.deep(gs, ed, part, order)
            turn = turned_rows(head, kv, part, fresh[n], qs, gs, order)
            column = lax.broadcasted_iota(I32, (tall, 2 * PAGE), 1)
            seen = column < facts[LIMIT]

            def keep(p):
                return jnp.concatenate([jnp.where(seen, p[:tall], 0.0), p[tall:]], axis=0)

            p, ds = weigh(dot_n(qd, k_deep[...]), dot_n(gd, v_deep[...]), keep)
            acc[0] += dot_n(turn("qt", 0, SLOTS), ds)
            acc[1] += dot_n(turn("gt", 0, SLOTS), p)
            if not fresh[n]:
                held(("ds", kv))[part * SLOTS * tall : (part + 1) * SLOTS * tall] = ds
                return
            dq = dot_n(ds, k_up[...])
            for slot in range(SLOTS):
                head.put_queries(
                    part, slot, dq[slot * tall : (slot + 1) * tall], held(("dq", kv)), not fresh[n],
                    stage_ref,
                )

        def put_own(n):
            dk12, dv12, own0, send2 = results
            here = slice(base + n * HD, base + (n + 1) * HD)
            grad = [acc[0].T * SCALE, acc[1].T]
            for at, c, to in ((0, N1, 0), (2, N2, 1)):
                ok = row_ok(facts[c], PAGE, HD)
                for kind, out in ((0, dk12), (1, dv12)):
                    out[cols(to, to + 1), here] = jnp.where(
                        ok, grad[kind][cols(at, at + 1)], 0.0
                    ).astype(BF16)
            for kind in range(2):
                level2 = grad[kind][cols(1, 2)]
                own0[kind, :, here] = grad[kind][cols(3, 4)] + jnp.where(owns2, level2, 0.0)
                send2[kind, :, here] = level2.astype(BF16)

        def put_shared(n):
            (out,) = results
            here = slice(n * HD, (n + 1) * HD)
            grads = acc[0].T * SCALE, acc[1].T
            for j in range(2):
                for kind in range(2):
                    out[2 * j + kind, :, here] = grads[kind][cols(j, j + 1)].astype(out.dtype)

        sends = []
        for n, kv in enumerate(kvs):
            arrived(("q", kv), ("g", kv))
            head = Head(kv, group, norms, deltas, en, ed)
            set_pages(n, kv)

            for part in range(parts):
                slot = n * parts + part
                (own_part if own else shared_part)(
                    head, kv, part, n, stage.at[slot] if own and not fresh[n] else None
                )
                if own and not fresh[n]:
                    at = order.at(facts, kv, group * HD) + part * wide
                    sends.append(
                        pltpu.make_async_copy(
                            stage.at[slot],
                            held("gq").at[:, pl.ds(pl.multiple_of(at, wide), wide)],
                            sem.at[slot],
                        )
                    )
                    sends[-1].start()

            (put_own if own else put_shared)(n)
        for c in sends:
            c.wait()
        arrived(*list(copies))

    made = kernel_call(
        body, facts, near, far, outs, scratch, aliases, after,
        pl.CostEstimate(
            flops=240 * PAGE * PAGE * HD * group * count, bytes_accessed=1000, transcendentals=0
        ),
        LARGE,
    )
    for name, at in at_out.items():
        state[name] = made[at]
    return list(made[at_results:at_loaded])


def width_tiles(w):
    tile = next(t for t in (512, 640, 320, 128, w.shape[0]) if w.shape[0] % t == 0)
    return [slice(i, i + tile) for i in range(0, w.shape[0], tile)]


def finish_queries(kvs, group, order, facts, pages, state, after=(), w=None):
    parts = group // min(4, group)
    heads = group // parts
    tall = heads * PAGE
    wide = heads * HD
    near = list(pages)
    for kv in kvs:
        near += [state["ds", kv], state["dq", kv]]

    def body(facts, *refs):
        stage, sem = refs[-2:]
        if w is not None:
            gq, made, w_near = refs[-5:-2]
            w_copy = pltpu.make_async_copy(refs[-6], w_near, sem.at[len(kvs) * parts])
            w_copy.start()
        else:
            gq, made = refs[-4:-2]
        made[...] = jnp.zeros_like(made)
        sends = []
        for n, kv in enumerate(kvs):
            ds, dq = refs[len(pages) + 2 * n : len(pages) + 2 * n + 2]
            page, at = refs[kv // order.half], kv % order.half * HD
            keys = jnp.concatenate([page[j, 0, :, at : at + HD] for j in range(2)], axis=0)
            for part in range(parts):
                at = n * parts + part
                gained = dot_n(ds[part * SLOTS * tall : (part + 1) * SLOTS * tall], keys)
                for i in range(SLOTS * heads):
                    slot, j = divmod(i, heads)
                    rows = slice(slot * PAGE, (slot + 1) * PAGE)
                    value = gained[i * PAGE : (i + 1) * PAGE] + dq[
                        rows, part * wide + j * HD : part * wide + (j + 1) * HD
                    ]
                    stage[at, rows, j * HD : (j + 1) * HD] = (value * SCALE).astype(BF16)
                to = pl.multiple_of(order.at(facts, kv, group * HD) + part * wide, wide)
                sends.append(
                    pltpu.make_async_copy(stage.at[at], gq.at[:, pl.ds(to, wide)], sem.at[at])
                )
                sends[-1].start()
        for c in sends:
            c.wait()
        if w is not None:
            w_copy.wait()

    count = len(kvs) * parts
    far = [state["gq"]] if "gq" in state else []
    aliases = {("far", 0): 0} if far else {}
    shape = (ROWS, state["k"].shape[1] * group)
    outs = [(shape, BF16, False), ((8, HD), F32, True)]
    if w is not None:
        far = far + [w]
        outs.append((w.shape, w.dtype, True))
    state["gq"], *made = kernel_call(
        body, facts, near, far, outs,
        [pltpu.VMEM((count, ROWS, wide), BF16), pltpu.SemaphoreType.DMA((count + 1,))],
        aliases, after, limit=LARGE,
    )
    return made


def input_grad(order, facts, w, rows, own, far, grads, carry=None, near_w=False, after=()):
    out_cols, depth = w.shape
    tiles = width_tiles(w)
    top = 0 if rows == PAGE else PAGE
    steps = len(tiles)
    width = sum(a.shape[1] for a in grads[0])
    arrays = [*own, *far, *grads[0], *grads[1]] + [w] * near_w
    count = len(grads[0])
    carry = list(carry or [])
    lead = [] if near_w else [w]
    rest = [*lead, *carry, *after]

    def body(facts, *refs):
        own_r, refs = refs[: len(own)], refs[len(own) :]
        far_r, refs = refs[: len(far)], refs[len(far) :]
        grad_r, w_ref = refs[: 2 * count], refs[2 * count]
        out, dk, dv, made, w_near, stage, w_sem, sem = refs[-8:]
        loads = []
        if not near_w:
            loads = [
                pltpu.make_async_copy(w_ref.at[at], w_near.at[at], w_sem.at[i])
                for i, at in enumerate(tiles)
            ]
        for c in loads:
            c.start()
        made[...] = jnp.zeros_like(made)
        columns = lambda rs: jnp.concatenate([r[...] for r in rs], axis=1)
        full = order.real(facts, columns(own_r))
        if far:
            other, first = order.real(facts, columns(far_r)), facts[SIDE] == 0
            full = jnp.concatenate(
                [jnp.where(first, full, other), jnp.where(first, other, full)], axis=1
            )
        copies = put_rows(order, facts, grad_r, dk, dv, top, rows, sem, steps)
        for i, at in enumerate(tiles):
            if loads:
                loads[i].wait()
            stage[i] = dot_t((w_ref if near_w else w_near)[at], full).astype(BF16).T
            copies.append(
                pltpu.make_async_copy(stage.at[i], out.at[top : top + rows, at], sem.at[i])
            )
            copies[-1].start()
        for c in copies:
            c.wait()

    smem = pl.BlockSpec(memory_space=pltpu.SMEM)
    vmem = pl.BlockSpec(memory_space=pltpu.VMEM)
    hbm = pl.BlockSpec(memory_space=pl.ANY)
    arrays = [pltpu.with_memory_space_constraint(a, pltpu.VMEM) for a in arrays]
    kept = jax.ShapeDtypeStruct((ROWS, width), BF16)
    return pl.pallas_call(
        body,
        out_shape=(
            jax.ShapeDtypeStruct((ROWS, out_cols), BF16), kept, kept, pltpu.VMEM((8, HD), F32)
        ),
        in_specs=[smem] + [vmem] * len(arrays) + [hbm] * len(rest),
        out_specs=(hbm, hbm, hbm, vmem),
        scratch_shapes=[
            pltpu.VMEM((8, HD) if near_w else w.shape, BF16),
            pltpu.VMEM((steps, rows, out_cols // steps), BF16),
            pltpu.SemaphoreType.DMA((steps,)),
            pltpu.SemaphoreType.DMA((steps + 2 * order.heads,)),
        ],
        input_output_aliases={
            1 + len(arrays) + len(lead) + i: i for i in range(len(carry))
        },
        compiler_params=pltpu.CompilerParams(vmem_limit_bytes=LARGE),
        cost_estimate=SLIGHT,
    )(pltpu.with_memory_space_constraint(facts, pltpu.SMEM), *arrays, *rest)


def put_rows(order, facts, pieces, dk, dv, top, rows, sem, first):
    copies = []
    count = len(pieces) // 2
    for dst, mine in ((dk, pieces[:count]), (dv, pieces[count:])):
        head = 0
        for src in mine:
            more = src.shape[1] // HD
            for lo, hi in order.runs(head, head + more):
                copies.append(
                    pltpu.make_async_copy(
                        src.at[:, (lo - head) * HD : (hi - head) * HD],
                        dst.at[top : top + rows, pl.ds(order.at(facts, lo, HD), (hi - lo) * HD)],
                        sem.at[first + len(copies)],
                    )
                )
                copies[-1].start()
            head += more
    return copies


def begin_input_grad(order, facts, w, own, after=()):
    out_cols, depth = w.shape
    half = depth // 2
    rows = own[0].shape[0]
    count = len(own)

    def body(facts, w_ref, *refs):
        mine, out = jnp.concatenate([r[...] for r in refs[:count]], axis=1), refs[-1]
        mine = order.real(facts, mine)
        where = pl.ds(pl.multiple_of(facts[SIDE] * half, half), half)
        for at in width_tiles(w):
            out[at] = dot_t(w_ref[at, where], mine)

    smem = pl.BlockSpec(memory_space=pltpu.SMEM)
    vmem = pl.BlockSpec(memory_space=pltpu.VMEM)
    near = [pltpu.with_memory_space_constraint(a, pltpu.VMEM) for a in (w, *own)]

    def kernel(*refs):
        body(*refs[: 2 + count], refs[-1])

    return pl.pallas_call(
        kernel,
        out_shape=pltpu.VMEM((out_cols, rows), F32),
        in_specs=[smem] + [vmem] * len(near) + [pl.BlockSpec(memory_space=pl.ANY)] * len(after),
        out_specs=vmem,
        compiler_params=pltpu.CompilerParams(vmem_limit_bytes=LARGE),
        cost_estimate=SLIGHT,
    )(pltpu.with_memory_space_constraint(facts, pltpu.SMEM), *near, *after)


def end_input_grad(order, facts, w, base, across, corner, begun, grads, carry):
    tiles = width_tiles(w)
    out_cols, depth = w.shape
    half = depth // 2
    steps = len(tiles)
    rows = base.shape[0]

    def body(facts, w_r, begun_r, base_r, across_r, corner_r, *refs):
        out, dk, dv, stage, sem = refs[-5:]
        copies = put_rows(order, facts, refs[:2], dk, dv, 0, rows, sem, steps)
        gained = jnp.concatenate([corner_r[...], across_r[...]], axis=1).astype(F32)
        known = base_r[...]
        more = jnp.where(row_ok(facts[N0], rows, half), known.astype(F32) + gained, 0.0)
        other = order.real(facts, jnp.where(facts[OWNS2] == 1, known, more.astype(BF16)))
        where = pl.ds(pl.multiple_of((1 - facts[SIDE]) * half, half), half)
        for i, at in enumerate(tiles):
            stage[i] = (dot_t(w_r[at, where], other) + begun_r[at]).astype(BF16).T
            copies.append(pltpu.make_async_copy(stage.at[i], out.at[:rows, at], sem.at[i]))
            copies[-1].start()
        for c in copies:
            c.wait()

    return kernel_call(
        body, facts, [w, begun, base, across, corner, *grads], list(carry),
        [(a.shape, a.dtype, False) for a in carry],
        [
            pltpu.VMEM((steps, rows, out_cols // steps), BF16),
            pltpu.SemaphoreType.DMA((steps + 2 * order.heads,)),
        ],
        {("far", i): i for i in range(len(carry))},
    )


def flipped(block, axis, bit):
    count = lax.axis_size(axis)
    return lax.ppermute(block, axis, [(i, i ^ bit) for i in range(count) if i ^ bit < count])


def spanning(leaves, bit_index):
    return len([j for j in range(INNER) if 2 << bit_index <= leaves >> j])


def gather_small_tree(facts, own, beside_pair, beside_half):
    width = own.shape[-1] // 2
    page = ((2, PAGE, width), BF16, True)
    from_core = flipped(own, "sub", 1)

    def choose_chip(facts, own_ref, far_ref, out):
        for swap in range(2):
            for mine in range(2):

                @pl.when((facts[SWAP] == swap) & (facts[OWNS2] != mine))
                def _copy(swap=swap, mine=mine):
                    out[...] = (own_ref if mine else far_ref)[
                        :, :, swap * width : (swap + 1) * width
                    ]

    (chip,) = kernel_call(choose_chip, facts, [own, from_core], [], [page])
    from_pair = flipped(chip, "leaf", 1)

    def choose_pair(facts, near_ref, far_ref, out):
        out[...] = jnp.where(facts[ROOT_IN_CHIP] == 1, near_ref[...], far_ref[...])

    after = beside_pair(from_core, chip)
    (pair,) = kernel_call(choose_pair, facts, [chip, from_pair], [], [page], after=after)
    from_half = flipped(pair, "leaf", 2)

    def choose_all(facts, chip_ref, pair_far, pair_ref, half_far, out):
        out[0] = jnp.where(facts[ROOT_IN_PAIR] == 1, pair_ref[...], half_far[...])
        out[1] = jnp.where(facts[NEXT_IN_CHIP] == 1, chip_ref[...], pair_far[...])

    after = beside_half(pair)
    (mine,) = kernel_call(
        choose_all, facts, [chip, from_pair, pair, from_half], [],
        [((2, *page[0]), BF16, True)], after=after,
    )
    return mine, flipped(mine, "sub", 1)


def over_cores(facts, kept, far):
    width = kept.shape[-1]

    def body(_, near, away, total, root, next_one):
        for i in range(4):
            value = near[i] + away[i].astype(F32)
            total[i] = value
            (root, next_one)[i // 2][i % 2] = value.astype(BF16)

    pages = ((2, PAGE, width), BF16, True)
    total, root, next_one = kernel_call(
        body, facts, [kept, far], [], [((4, PAGE, width), F32, True), pages, pages]
    )
    return total, root, flipped(root, "leaf", 2), flipped(next_one, "leaf", 1)


def over_halves(facts, total, root_far, next_far, after):
    width = total.shape[-1]

    def body(_, near, root_r, next_r, out, low):
        root = near[:2] + root_r[...].astype(F32)
        out[:2] = root
        low[...] = root.astype(BF16)
        out[2:] = near[2:] + next_r[...].astype(F32)

    total, low = kernel_call(
        body, facts, [total, root_far, next_far], [],
        [((4, PAGE, width), F32, True), ((2, PAGE, width), BF16, True)], after=after,
    )
    return total, low, flipped(low, "leaf", 1)


def over_chips(facts, total, far, after):
    width = total.shape[-1]

    def body(facts, near, away, out, values):
        root = near[:2] + away[...].astype(F32)
        picked = jnp.where(facts[ROOT_IN_CHIP] == 1, root, near[2:]).astype(BF16)
        out[...] = picked
        values[...] = picked[1]

    outs = [((2, PAGE, width), BF16, True), ((PAGE, width), BF16, True)]
    mine, values = kernel_call(body, facts, [total, far], [], outs, after=after)
    across = flipped(values, "tensor", 1)
    corner = lax.ppermute(values, ("tensor", "sub"), [(i, 3 - i) for i in range(4)])
    return mine, flipped(mine, "sub", 1), across, corner


def other_level2(order, head, kind, ref):
    theirs = head ^ order.half
    at = theirs % order.half * HD
    return ref[4 + 2 * (theirs // order.half) + kind, :, at : at + HD]


def begin_values(order, facts, own0, level2_far, handed):
    def body(facts, own_r, low_r, handed_r, out, handed_out):
        handed_out[...] = handed_r[...]
        ok = row_ok(facts[N0], PAGE, HD)
        for head in range(order.heads):
            c = slice(head * HD, (head + 1) * HD)
            low = other_level2(order, head, 1, low_r).astype(F32)
            value = own_r[1, :, c] + jnp.where(facts[OWNS2] == 1, low, 0.0)
            out[:, c] = jnp.where(ok, value, 0.0).astype(BF16)

    outs = [((PAGE, own0.shape[-1]), BF16, True), (handed.shape, handed.dtype, True)]
    return kernel_call(body, facts, [own0, level2_far, handed], [], outs)


def finish_small_tree(order, facts, own0, mine, far, level2_far):
    width = own0.shape[-1]

    def body(facts, own_r, mine_r, far_r, low_r, dk, dv):
        owns2 = facts[OWNS2] == 1
        ok = row_ok(facts[N0], PAGE, HD)
        for head in range(order.heads):
            c = slice(head * HD, (head + 1) * HD)
            at = head % order.half * HD
            for kind, out in enumerate((dk, dv)):
                gained = (far_r if head < order.half else mine_r)[kind, :, at : at + HD]
                level2 = other_level2(order, head, kind, low_r)
                more = jnp.where(owns2, level2, gained).astype(F32)
                out[:, c] = jnp.where(ok, own_r[kind, :, c] + more, 0.0).astype(BF16)

    page = ((PAGE, width), BF16, True)
    return kernel_call(body, facts, [own0, mine, far, level2_far], [], [page, page])


def gather_tree(ids, own):
    leaves = lax.axis_size(("leaf", "sub"))
    owned = ids[:INNER] == ids[INNER] - 1
    pages = jnp.where(owned[:, None, None, None], own[None], jnp.zeros((), BF16))
    for bit in range(leaves.bit_length() - 1):
        active = spanning(leaves, bit)
        far = flipped(pages[:active], ("leaf", "sub"), 1 << bit)
        pages = jnp.concatenate([pages[:active] + far, pages[active:]])
    return pages


def reduce_tree(ids, parts):
    leaves = lax.axis_size(("leaf", "sub"))
    for bit in range(leaves.bit_length() - 1):
        active = spanning(leaves, bit)
        far = flipped(parts[:active], ("leaf", "sub"), 1 << bit)
        parts = jnp.concatenate([parts[:active] + far, parts[active:]])
    owned = ids[:INNER] == ids[INNER] - 1
    return jnp.sum(jnp.where(owned[:, None, None, None], parts, 0.0), axis=0)


def on_device(queries, grad_out, keys, values, log_norms, row_deltas, ancestors, counts, w_value):
    kv = keys.shape[1] // HD
    group = queries.shape[1] // keys.shape[1]
    leaves = lax.axis_size(("leaf", "sub"))
    hbm = lambda a: pltpu.with_memory_space_constraint(a, pltpu.HBM)
    side = lax.axis_index("tensor").astype(I32).reshape(1)
    two_sides = lax.axis_size("tensor") == 2
    inputs = [hbm(a) for a in (queries, grad_out, keys, values, log_norms, row_deltas)]
    fast = leaves == 8 and lax.axis_size("sub") == 2 and kv == 4 and two_sides
    order = Order(fast, kv)
    facts, own = start(order, side, hbm(ancestors), hbm(counts), *inputs[2:4])
    state = {}

    def own_pages(kvs, pages, prior=(), after=()):
        return attend(True, kvs, group, order, facts, inputs, pages, state, prior, after)

    def shared_pages(kvs, page, ride=None, after=()):
        return attend(
            False, kvs, group, order, facts, inputs, [page], state, after=after, ride=ride
        )[0]

    def spread(part):
        if two_sides:
            return flipped(part, "tensor", 1)
        return lax.all_gather(part, "tensor", axis=1, tiled=True)

    kvs = tuple(range(kv))
    w = hbm(w_value)
    if fast:
        level2, calls = [], []

        def beside_pair(from_core, chip):
            level2.extend((own, from_core))
            calls.append(own_pages(kvs[:1], level2, after=(chip,)))
            return (calls[0][3],)

        def beside_half(pair):
            calls.append(own_pages(kvs[1:], level2, calls[0], (pair,)))
            return (calls[1][3],)

        mine, theirs = gather_small_tree(facts, own, beside_pair, beside_half)
        dk12, dv12, own0, send2 = calls[1]
        sent = flipped(shared_pages(kvs[:2], mine, send2), "sub", 1)
        kept = shared_pages(kvs[2:], theirs)
        total, root, root_far, next_far = over_cores(facts, kept, sent)
        base, dv12 = begin_values(order, facts, own0, sent, dv12)
        far_v = spread(dv12)
        made, w_near = finish_queries(
            kvs, group, order, facts, (mine, theirs), state, (root, base), w
        )
        total, low, far = over_halves(facts, total, root_far, next_far, (made,))
        base_far = spread(base)
        *grads, made = input_grad(
            order, facts, w_near, 2 * PAGE, [dv12], [far_v], ([dk12], [dv12]), near_w=True,
            after=(low,),
        )
        near, far, across, corner = over_chips(facts, total, far, (made, base_far))
        dk0, dv0 = finish_small_tree(order, facts, own0, near, far, sent)
        begun = begin_input_grad(order, facts, w_near, [dv0])
        grads = end_input_grad(
            order, facts, w_near, base_far, across, corner, begun, [dk0, dv0], grads
        )
        return (state["gq"], grads[1], grads[2], grads[0])

    path_ids = ancestors[0]
    pages = gather_tree(path_ids, own)
    dk12, dv12, own0, send2 = own_pages(kvs, (pages[2], pages[2]))
    grads = shared_pages(kvs, pages[:2])
    finish_queries(kvs, group, order, facts, (pages[:2],), state)
    low = send2.astype(F32)
    total = reduce_tree(path_ids, jnp.concatenate([grads.reshape(2, 2, *grads.shape[1:]), low[None]]))
    total += own0 - jnp.where(path_ids[2] == path_ids[INNER] - 1, low, 0.0)
    has = jnp.any(path_ids[:INNER] == path_ids[INNER] - 1)
    ok = (jnp.arange(PAGE) < jnp.where(has, counts[0, 0], 0))[:, None]
    dk0, dv0 = jnp.where(ok, total, 0.0).astype(BF16)
    if two_sides:
        pair = lambda part: ([part], [spread(part)])
    else:
        pair = lambda part: ([spread(part)], [])
    *grads, _ = input_grad(order, facts, w, 2 * PAGE, *pair(dv12), ([dk12], [dv12]))
    grads = input_grad(order, facts, w, PAGE, *pair(dv0), ([dk0], [dv0]), grads)
    return (state["gq"], grads[1], grads[2], grads[0])


def solution(mesh):
    placed = (
        P(("groups", "leaf", "sub"), "tensor"),
        P(("groups", "leaf", "sub"), "tensor"),
        P(("groups", "leaf", "sub"), "tensor"),
        P(("groups", "leaf", "sub"), "tensor"),
        P("tensor", ("groups", "leaf", "sub")),
        P("tensor", ("groups", "leaf", "sub")),
        P(("groups", "leaf", "sub"), None),
        P(("groups", "leaf", "sub"), None),
        P("tensor", None),
    )
    return jax.shard_map(
        on_device,
        mesh=mesh,
        in_specs=placed,
        out_specs=(
            P(("groups", "leaf", "sub"), "tensor"),
            P(("groups", "leaf", "sub"), "tensor"),
            P(("groups", "leaf", "sub"), "tensor"),
            P(("groups", "leaf", "sub"), "tensor"),
        ),
        check_vma=False,
    )
```

```python
import math

import jax
import jax.numpy as jnp
from jax import lax
from jax.experimental import pallas as pl
from jax.experimental.pallas import tpu as pltpu
from jax.sharding import PartitionSpec as P

HD = 128
PAGE = 128
SLOTS = 3
INNER = 3
ROWS = SLOTS * PAGE
LOG2E = math.log2(math.e)
SCALE = 1.0 / math.sqrt(HD)
BF16 = jnp.bfloat16
F32 = jnp.float32
I32 = jnp.int32
LARGE = 10 << 20
SMALL = 4 << 20
SLIGHT = pl.CostEstimate(flops=1000, bytes_accessed=1000, transcendentals=0)
BLOCKED = 1e30


def dot_t(left, right):
    return lax.dot_general(left, right, (((1,), (1,)), ((), ())), preferred_element_type=F32)


def dot_n(left, right):
    return lax.dot_general(left, right, (((1,), (0,)), ((), ())), preferred_element_type=F32)


FACTS = 16
N0, N1, N2, OWNS2, LIMIT, LEADS, ROOT_IN_CHIP, ROOT_IN_PAIR, NEXT_IN_CHIP, SIDE, SWAP = range(11)


class Order:
    def __init__(self, crossed, heads):
        self.crossed, self.heads = crossed, heads
        self.half = heads // 2 if crossed else heads

    def at(self, facts, head, unit):
        if not self.crossed:
            return head * unit
        step = ((head ^ self.half) - head) * unit
        return pl.multiple_of(facts[SWAP] * step + head * unit, unit)

    def runs(self, first, last):
        cuts = [first, *(h for h in range(first + 1, last) if h % self.half == 0), last]
        return list(zip(cuts[:-1], cuts[1:]))

    def real(self, facts, rows):
        if not self.crossed:
            return rows
        width = self.half * HD
        turned = jnp.concatenate([rows[:, width:], rows[:, :width]], axis=1)
        return jnp.where(facts[SWAP] == 1, turned, rows)


def write_facts(facts, ids, counts, side, order):
    page = [ids[0, j] for j in range(INNER + 1)]
    own = page[INNER] - 1
    leaf = own // SLOTS
    owns = [page[j] == own for j in range(INNER)]
    same = lambda level, shift: ((page[level] // SLOTS) >> shift) == (leaf >> shift)
    number = lambda flag: jnp.where(flag, 1, 0)
    facts[N0] = jnp.where(owns[0] | owns[1] | owns[2], counts[0, 0], 0)
    facts[N1] = counts[0, 1]
    facts[N2] = counts[0, 2]
    facts[OWNS2] = number(owns[2])
    facts[LIMIT] = jnp.where(owns[2], 2 * PAGE, jnp.where(owns[1], PAGE, 0))
    facts[LEADS] = number(lax.rem(leaf, 2) == 0)
    facts[ROOT_IN_CHIP] = number(same(0, 1))
    facts[ROOT_IN_PAIR] = number(same(0, 2))
    facts[NEXT_IN_CHIP] = number(same(1, 1))
    facts[SIDE] = side
    facts[SWAP] = lax.rem(leaf, 2) if order.crossed else 0
    for i in range(SWAP + 1, FACTS):
        facts[i] = 0


def row_ok(count, rows, width):
    return lax.broadcasted_iota(I32, (rows, width), 0) < count


def kernel_call(body, facts, near, far, outs, scratch=(), aliases=None, after=(), cost=None,
                limit=SMALL):
    smem = pl.BlockSpec(memory_space=pltpu.SMEM)
    vmem = pl.BlockSpec(memory_space=pltpu.VMEM)
    hbm = pl.BlockSpec(memory_space=pl.ANY)
    near = [pltpu.with_memory_space_constraint(a, pltpu.VMEM) for a in near]
    place = {("near", i): 1 + i for i in range(len(near))}
    place |= {("far", i): 1 + len(near) + i for i in range(len(far))}
    used = 1 + len(near) + len(far)

    def kernel(*refs):
        body(*refs[:used], *refs[used + len(after) :])

    return pl.pallas_call(
        kernel,
        out_shape=tuple(
            pltpu.VMEM(s, d) if inside else jax.ShapeDtypeStruct(s, d) for s, d, inside in outs
        ),
        in_specs=[smem] + [vmem] * len(near) + [hbm] * (len(far) + len(after)),
        out_specs=tuple(vmem if inside else hbm for _, _, inside in outs),
        scratch_shapes=list(scratch),
        input_output_aliases={place[k]: v for k, v in (aliases or {}).items()},
        compiler_params=pltpu.CompilerParams(vmem_limit_bytes=limit),
        cost_estimate=cost or SLIGHT,
    )(pltpu.with_memory_space_constraint(facts, pltpu.SMEM), *near, *far, *after)


def start(order, side, ids, counts, keys, values):
    width = keys.shape[1]

    def body(side_ref, ids_ref, counts_ref, k_ref, v_ref, facts, out, held, ids_s, counts_s, sem):
        copies = [
            pltpu.make_async_copy(src, dst, sem.at[i])
            for i, (src, dst) in enumerate(
                (
                    (ids_ref, ids_s),
                    (counts_ref, counts_s),
                    (k_ref.at[:PAGE], held.at[0]),
                    (v_ref.at[:PAGE], held.at[1]),
                )
            )
        ]
        for c in copies:
            c.start()
        copies[0].wait()
        copies[1].wait()
        write_facts(facts, ids_s, counts_s, side_ref[0], order)
        ok = row_ok(counts_s[0, 0], PAGE, width)
        for i in range(2):
            copies[2 + i].wait()
            out[i] = jnp.where(ok, held[i], jnp.zeros((), BF16))

    smem = pl.BlockSpec(memory_space=pltpu.SMEM)
    hbm = pl.BlockSpec(memory_space=pl.ANY)
    return pl.pallas_call(
        body,
        out_shape=(pltpu.SMEM((FACTS,), I32), pltpu.VMEM((2, PAGE, width), BF16)),
        in_specs=[smem] + [hbm] * 4,
        out_specs=(smem, pl.BlockSpec(memory_space=pltpu.VMEM)),
        scratch_shapes=[
            pltpu.VMEM((2, PAGE, width), BF16),
            pltpu.SMEM(ids.shape, I32),
            pltpu.SMEM(counts.shape, I32),
            pltpu.SemaphoreType.DMA((4,)),
        ],
        compiler_params=pltpu.CompilerParams(vmem_limit_bytes=SMALL),
    )(side, ids, counts, keys, values)


def row_terms(rows):
    high = rows.astype(BF16).astype(F32)
    rest = rows - high
    middle = rest.astype(BF16).astype(F32)
    parts = [high, middle, rest - middle]
    spare = HD - 3 * rows.shape[0]
    parts.append(jnp.zeros((spare, rows.shape[1]), F32))
    return jnp.concatenate(parts, axis=0).T.astype(BF16)


class Head:
    def __init__(self, kv, group, norms, deltas, en, ed):
        self.group = group
        self.heads = min(4, group)
        self.parts = group // self.heads
        self.tall = self.heads * PAGE
        heads = slice(kv * group, (kv + 1) * group)
        en[...] = row_terms(norms[heads, :])
        ed[...] = row_terms(deltas[heads, :])

    def lanes(self, part, j):
        at = (part * self.heads + j) * HD
        return slice(at, at + HD)

    def stacked(self, ref, part, slots):
        return jnp.concatenate(
            [
                ref[slot * PAGE : (slot + 1) * PAGE, self.lanes(part, j)]
                for slot in slots
                for j in range(self.heads)
            ],
            axis=0,
        )

    def deep(self, stacked, terms, part, slots):
        column = lax.broadcasted_iota(I32, (1, HD), 1) % self.group
        picks = [
            (column == part * self.heads + j).astype(F32).astype(BF16)
            for j in range(self.heads)
        ]
        extra = [
            terms[slot * PAGE : (slot + 1) * PAGE] * pick for slot in slots for pick in picks
        ]
        return jnp.concatenate([stacked, jnp.concatenate(extra, axis=0)], axis=1)

    def turned_at(self, part, slot, count):
        at = (part * SLOTS + slot) * self.tall
        return slice(at, at + self.tall * count)


def set_keys(deep, upright, at, page):
    where = slice(at * PAGE, (at + 1) * PAGE)
    deep[:HD, where] = page.T
    if upright is not None:
        upright[where] = page


def weigh(scores, grads, keep):
    p = keep(jnp.exp2(scores * (SCALE * LOG2E)))
    return p.astype(BF16), (p * grads).astype(BF16)


def attend(own, kvs, group, order, facts, inputs, pages, state, prior=(), after=(),
           ride=None):
    loading = "k" not in state
    q_all, k_all = inputs[0], inputs[2]
    count = len(kvs)
    parts = group // min(4, group)
    tall = min(4, group) * PAGE
    width = count * HD
    base = prior[0].shape[1] if prior else 0
    kv_total = k_all.shape[1] // HD
    fresh = [("qt", kv) not in state for kv in kvs]
    one_head = (ROWS, group * HD)
    turned = ((HD, group * ROWS), BF16, True)
    low = lambda rows, columns: ((rows, columns), BF16, True)
    shapes = {
        "da": low(2 * group * PAGE, 2 * PAGE),
        "db": low(2 * group * PAGE, PAGE),
        "ku": low(4 * PAGE, HD),
        "qt": turned,
        "gt": turned,
    }

    near, far, aliases, outs = [], [], {}, []
    at_near, at_far, at_out = {}, {}, {}

    def add_near(name, array):
        at_near[name] = len(near)
        near.append(array)

    def add_far(name, array):
        at_far[name] = len(far)
        far.append(array)

    def add_out(name, out):
        at_out[name] = len(outs)
        outs.append(out)

    for kv, is_fresh in zip(kvs, fresh):
        for name, shape in shapes.items():
            if is_fresh:
                add_out((name, kv), shape)
            elif name in ("qt", "gt"):
                add_near((name, kv), state[name, kv])
        if not own and not is_fresh:
            add_out(("ds", kv), ((group * ROWS, 2 * PAGE), BF16, True))
    at_results = len(outs)
    if own:
        outs += [
            ((2 * PAGE, base + width), BF16, True),
            ((2 * PAGE, base + width), BF16, True),
            ((2, PAGE, base + width), F32, True),
            ((2, PAGE, base + width), BF16, True),
        ]
    else:
        outs += [
            ((4, PAGE, width), F32, True) if ride is None else ((8, PAGE, width), BF16, True),
        ]
    at_loaded = len(outs)
    if loading:
        for name, array in zip(("q", "g", "k", "v", "norms", "deltas"), inputs):
            add_far(name, array)
            if name in ("q", "g"):
                for kv in range(kv_total):
                    add_out((name, kv), (one_head, BF16, True))
            else:
                add_out(name, (array.shape, array.dtype, True))
    else:
        for name in ("k", "v", "norms", "deltas"):
            add_near(name, state[name])
        for kv in kvs:
            for name in ("q", "g"):
                add_near((name, kv), state[name, kv])
    for i, page in enumerate(pages):
        add_near(("page", i), page)
    for i, array in enumerate(prior):
        add_near(("prior", i), array)
    if ride is not None:
        add_near("ride", ride)
    key_pages = 4 if own else 2
    scratch = [
        pltpu.VMEM((2 * HD, key_pages * PAGE), BF16),
        pltpu.VMEM((2 * HD, key_pages * PAGE), BF16),
        pltpu.VMEM((key_pages * PAGE, HD), BF16),
        pltpu.VMEM((2, HD, key_pages * PAGE), F32),
        pltpu.VMEM((ROWS, HD), BF16),
        pltpu.VMEM((ROWS, HD), BF16),
        pltpu.SemaphoreType.DMA((2 * kv_total + 8,)),
    ]
    cols = lambda a, b: slice(a * PAGE, b * PAGE)

    def body(facts, *refs):
        ins, out_refs = refs[: len(near) + len(far)], refs[len(near) + len(far) : -len(scratch)]
        k_deep, v_deep, k_up, acc, en, ed, load_sem = refs[-len(scratch) :]
        near_ref = lambda name: ins[at_near[name]]
        far_ref = lambda name: ins[len(near) + at_far[name]]
        held = lambda name: out_refs[at_out[name]] if name in at_out else near_ref(name)
        results = out_refs[at_results:at_loaded]
        copies = {}
        if loading:

            def load(key, src, dst):
                copies[key] = pltpu.make_async_copy(src, dst, load_sem.at[len(copies)])
                copies[key].start()

            for lo, hi in order.runs(0, kv_total):
                for name in ("k", "v"):
                    at = pl.ds(order.at(facts, lo, HD), (hi - lo) * HD)
                    here = slice(lo * HD, hi * HD)
                    load((name, lo), far_ref(name).at[:, at], held(name).at[:, here])
                for name in ("norms", "deltas"):
                    at = pl.ds(order.at(facts, lo, group), (hi - lo) * group)
                    here = slice(lo * group, hi * group)
                    load((name, lo), far_ref(name).at[at], held(name).at[here])
            shared_loads = list(copies)
            for kv in range(kv_total):
                at = pl.ds(order.at(facts, kv, group * HD), group * HD)
                for name in ("q", "g"):
                    load((name, kv), far_ref(name).at[:, at], held((name, kv)))
        k, v, norms, deltas = (held(name) for name in ("k", "v", "norms", "deltas"))

        def arrived(*keys):
            for key in keys:
                if key in copies:
                    copies.pop(key).wait()

        k_deep[HD:] = jnp.full((HD, key_pages * PAGE), -1.0, BF16)
        v_deep[HD:] = jnp.full((HD, key_pages * PAGE), -1.0, BF16)
        for out, i in zip(results, range(len(prior))):
            out[..., :base] = near_ref(("prior", i))[...]
        if ride is not None:
            (out,), more = results, near_ref("ride")
            for kind in range(2):
                out[4 + kind] = more[kind, :, :width]
                out[6 + kind] = more[kind, :, width:]
        owns2 = facts[OWNS2] == 1
        if loading:
            arrived(*shared_loads)
            lane = lax.broadcasted_iota(I32, norms.shape, 1)
            limit = jnp.where(
                lane < PAGE, facts[N0], jnp.where(lane < 2 * PAGE, facts[N1], facts[N2])
            )
            norms[...] = jnp.where(lane % PAGE < limit, norms[...] * (1.0 / SCALE), BLOCKED)
        lower = lambda rows: lax.broadcasted_iota(I32, (rows, PAGE), 1) <= (
            lax.broadcasted_iota(I32, (rows, PAGE), 0) % PAGE
        )

        def set_pages(n, kv):
            lane = slice(kv * HD, (kv + 1) * HD)
            if own:
                first, second = (near_ref(("page", i)) for i in range(2))
                zero = jnp.zeros((), BF16)
                for slot, (at, c) in enumerate(((3, N0), (0, N1), (2, N2))):
                    ok = row_ok(facts[c], PAGE, HD)
                    rows = cols(slot, slot + 1)
                    set_keys(k_deep, k_up, at, jnp.where(ok, k[rows, lane], zero))
                    set_keys(v_deep, None, at, jnp.where(ok, v[rows, lane], zero))
                level2 = [jnp.where(owns2, first[i, :, lane], second[i, :, lane]) for i in (0, 1)]
                if order.crossed:
                    at = (kv ^ order.half) * HD
                    lane = slice(at, at + HD)
                    for i in range(2):
                        other = jnp.where(owns2, first[i, :, lane], second[i, :, lane])
                        level2[i] = jnp.where(facts[SWAP] == 1, other, level2[i])
                set_keys(k_deep, k_up, 1, level2[0])
                set_keys(v_deep, None, 1, level2[1])
            else:
                page = near_ref(("page", 0))
                for j in range(2):
                    here = slice(n * HD, (n + 1) * HD)
                    set_keys(k_deep, k_up, j, page[j, 0, :, here])
                    set_keys(v_deep, None, j, page[j, 1, :, here])
            acc[...] = jnp.zeros_like(acc)

        def turned_rows(head, kv, part, is_fresh, qs, gs, order):
            if is_fresh:
                for name, rows in (("qt", qs), ("gt", gs)):
                    for i, slot in enumerate(order):
                        held((name, kv))[:, head.turned_at(part, slot, 1)] = rows[
                            i * tall : (i + 1) * tall
                        ].T
            return lambda name, slot, slots: held((name, kv))[
                :, head.turned_at(part, slot, slots)
            ]

        def own_part(head, kv, part, n):
            order = (1, 2, 0)
            qs = head.stacked(held(("q", kv)), part, order)
            gs = head.stacked(held(("g", kv)), part, order)
            qd, gd = head.deep(qs, en, part, order), head.deep(gs, ed, part, order)
            turn = turned_rows(head, kv, part, fresh[n], qs, gs, order)
            low = lower(tall)

            def keep_first(p):
                masked = jnp.where(low, p[:tall, :PAGE], 0.0)
                return jnp.concatenate(
                    [jnp.concatenate([masked, p[:tall, PAGE:]], axis=1), p[tall:]], axis=0
                )

            pa, da = weigh(
                dot_n(qd[: 2 * tall], k_deep[:, : 2 * PAGE]),
                dot_n(gd[: 2 * tall], v_deep[:, : 2 * PAGE]),
                keep_first,
            )
            both = lambda x: jnp.concatenate([x[:tall, :PAGE], x[tall:, PAGE:]], axis=0)
            low2 = lower(2 * tall)
            pb, db = weigh(
                both(dot_n(qd[tall:], k_deep[:, 2 * PAGE :])),
                both(dot_n(gd[tall:], v_deep[:, 2 * PAGE :])),
                lambda p: jnp.where(low2, p, 0.0),
            )
            for i, (name, a, b) in enumerate((("qt", da, db), ("gt", pa, pb))):
                acc[i, :, : 2 * PAGE] += dot_n(turn(name, 1, 2), a)
                acc[i, :, cols(2, 3)] += dot_n(turn(name, 2, 1), b[:tall])
                acc[i, :, cols(3, 4)] += dot_n(turn(name, 0, 1), b[tall:])
            here = slice(part * 2 * tall, (part + 1) * 2 * tall)
            held(("da", kv))[here] = da
            held(("db", kv))[here] = db

        def shared_part(head, kv, part, n):
            order = (0, 1, 2)
            qs = head.stacked(held(("q", kv)), part, order)
            gs = head.stacked(held(("g", kv)), part, order)
            qd, gd = head.deep(qs, en, part, order), head.deep(gs, ed, part, order)
            turn = turned_rows(head, kv, part, fresh[n], qs, gs, order)
            column = lax.broadcasted_iota(I32, (tall, 2 * PAGE), 1)
            seen = column < facts[LIMIT]

            def keep(p):
                return jnp.concatenate([jnp.where(seen, p[:tall], 0.0), p[tall:]], axis=0)

            p, ds = weigh(dot_n(qd, k_deep[...]), dot_n(gd, v_deep[...]), keep)
            acc[0] += dot_n(turn("qt", 0, SLOTS), ds)
            acc[1] += dot_n(turn("gt", 0, SLOTS), p)
            held(("ds", kv))[part * SLOTS * tall : (part + 1) * SLOTS * tall] = ds

        def put_own(n):
            dk12, dv12, own0, send2 = results
            here = slice(base + n * HD, base + (n + 1) * HD)
            grad = [acc[0].T * SCALE, acc[1].T]
            for at, c, to in ((0, N1, 0), (2, N2, 1)):
                ok = row_ok(facts[c], PAGE, HD)
                for kind, out in ((0, dk12), (1, dv12)):
                    out[cols(to, to + 1), here] = jnp.where(
                        ok, grad[kind][cols(at, at + 1)], 0.0
                    ).astype(BF16)
            for kind in range(2):
                level2 = grad[kind][cols(1, 2)]
                own0[kind, :, here] = grad[kind][cols(3, 4)] + jnp.where(owns2, level2, 0.0)
                send2[kind, :, here] = level2.astype(BF16)

        def put_shared(n):
            (out,) = results
            here = slice(n * HD, (n + 1) * HD)
            grads = acc[0].T * SCALE, acc[1].T
            for j in range(2):
                for kind in range(2):
                    out[2 * j + kind, :, here] = grads[kind][cols(j, j + 1)].astype(out.dtype)

        for n, kv in enumerate(kvs):
            arrived(("q", kv), ("g", kv))
            head = Head(kv, group, norms, deltas, en, ed)
            set_pages(n, kv)

            for part in range(parts):
                (own_part if own else shared_part)(head, kv, part, n)
            if own:
                held(("ku", kv))[...] = k_up[...]
            (put_own if own else put_shared)(n)
        arrived(*list(copies))

    made = kernel_call(
        body, facts, near, far, outs, scratch, aliases, after,
        pl.CostEstimate(
            flops=240 * PAGE * PAGE * HD * group * count, bytes_accessed=1000, transcendentals=0
        ),
        LARGE,
    )
    for name, at in at_out.items():
        state[name] = made[at]
    return list(made[at_results:at_loaded])


def width_tiles(w):
    tile = next(t for t in (512, 640, 320, 128, w.shape[0]) if w.shape[0] % t == 0)
    return [slice(i, i + tile) for i in range(0, w.shape[0], tile)]


def finish_queries(kvs, group, order, facts, pages, state, after=(), w=None):
    parts = group // min(4, group)
    heads = group // parts
    tall = heads * PAGE
    wide = heads * HD
    near = list(pages)
    names = ("ds", "da", "db", "ku")
    for kv in kvs:
        near += [state[name, kv] for name in names]

    def body(facts, *refs):
        stage, sem = refs[-2:]
        if w is not None:
            gq, made, w_near = refs[-5:-2]
            w_copy = pltpu.make_async_copy(refs[-6], w_near, sem.at[len(kvs) * parts])
            w_copy.start()
        else:
            gq, made = refs[-4:-2]
        made[...] = jnp.zeros_like(made)
        sends = []
        for n, kv in enumerate(kvs):
            first = len(pages) + len(names) * n
            ds, da, db, ku = refs[first : first + len(names)]
            page, at = refs[kv // order.half], kv % order.half * HD
            keys = jnp.concatenate([page[j, 0, :, at : at + HD] for j in range(2)], axis=0)
            for part in range(parts):
                at = n * parts + part
                gained = dot_n(ds[part * SLOTS * tall : (part + 1) * SLOTS * tall], keys)
                here = part * 2 * tall
                wide_part = dot_n(da[here : here + 2 * tall], ku[: 2 * PAGE])
                own2 = dot_n(db[here : here + tall], ku[2 * PAGE : 3 * PAGE])
                own0 = dot_n(db[here + tall : here + 2 * tall], ku[3 * PAGE :])
                by_slot = (
                    gained[:tall] + own0,
                    gained[tall : 2 * tall] + wide_part[:tall],
                    gained[2 * tall :] + (wide_part[tall:] + own2),
                )
                for i in range(SLOTS * heads):
                    slot, j = divmod(i, heads)
                    rows = slice(slot * PAGE, (slot + 1) * PAGE)
                    value = by_slot[slot][j * PAGE : (j + 1) * PAGE]
                    stage[at, rows, j * HD : (j + 1) * HD] = (value * SCALE).astype(BF16)
                to = pl.multiple_of(order.at(facts, kv, group * HD) + part * wide, wide)
                sends.append(
                    pltpu.make_async_copy(stage.at[at], gq.at[:, pl.ds(to, wide)], sem.at[at])
                )
                sends[-1].start()
        for c in sends:
            c.wait()
        if w is not None:
            w_copy.wait()

    count = len(kvs) * parts
    far = [state["gq"]] if "gq" in state else []
    aliases = {("far", 0): 0} if far else {}
    shape = (ROWS, state["k"].shape[1] * group)
    outs = [(shape, BF16, False), ((8, HD), F32, True)]
    if w is not None:
        far = far + [w]
        outs.append((w.shape, w.dtype, True))
    state["gq"], *made = kernel_call(
        body, facts, near, far, outs,
        [pltpu.VMEM((count, ROWS, wide), BF16), pltpu.SemaphoreType.DMA((count + 1,))],
        aliases, after, limit=LARGE,
    )
    return made


def input_grad(order, facts, w, rows, own, far, grads, carry=None, near_w=False, after=()):
    out_cols, depth = w.shape
    tiles = width_tiles(w)
    top = 0 if rows == PAGE else PAGE
    steps = len(tiles)
    width = sum(a.shape[1] for a in grads[0])
    arrays = [*own, *far, *grads[0], *grads[1]] + [w] * near_w
    count = len(grads[0])
    carry = list(carry or [])
    lead = [] if near_w else [w]
    rest = [*lead, *carry, *after]

    def body(facts, *refs):
        own_r, refs = refs[: len(own)], refs[len(own) :]
        far_r, refs = refs[: len(far)], refs[len(far) :]
        grad_r, w_ref = refs[: 2 * count], refs[2 * count]
        out, dk, dv, made, w_near, stage, w_sem, sem = refs[-8:]
        loads = []
        if not near_w:
            loads = [
                pltpu.make_async_copy(w_ref.at[at], w_near.at[at], w_sem.at[i])
                for i, at in enumerate(tiles)
            ]
        for c in loads:
            c.start()
        made[...] = jnp.zeros_like(made)
        columns = lambda rs: jnp.concatenate([r[...] for r in rs], axis=1)
        full = order.real(facts, columns(own_r))
        if far:
            other, first = order.real(facts, columns(far_r)), facts[SIDE] == 0
            full = jnp.concatenate(
                [jnp.where(first, full, other), jnp.where(first, other, full)], axis=1
            )
        copies = put_rows(order, facts, grad_r, dk, dv, top, rows, sem, steps)
        for i, at in enumerate(tiles):
            if loads:
                loads[i].wait()
            stage[i] = dot_t((w_ref if near_w else w_near)[at], full).astype(BF16).T
            copies.append(
                pltpu.make_async_copy(stage.at[i], out.at[top : top + rows, at], sem.at[i])
            )
            copies[-1].start()
        for c in copies:
            c.wait()

    smem = pl.BlockSpec(memory_space=pltpu.SMEM)
    vmem = pl.BlockSpec(memory_space=pltpu.VMEM)
    hbm = pl.BlockSpec(memory_space=pl.ANY)
    arrays = [pltpu.with_memory_space_constraint(a, pltpu.VMEM) for a in arrays]
    kept = jax.ShapeDtypeStruct((ROWS, width), BF16)
    return pl.pallas_call(
        body,
        out_shape=(
            jax.ShapeDtypeStruct((ROWS, out_cols), BF16), kept, kept, pltpu.VMEM((8, HD), F32)
        ),
        in_specs=[smem] + [vmem] * len(arrays) + [hbm] * len(rest),
        out_specs=(hbm, hbm, hbm, vmem),
        scratch_shapes=[
            pltpu.VMEM((8, HD) if near_w else w.shape, BF16),
            pltpu.VMEM((steps, rows, out_cols // steps), BF16),
            pltpu.SemaphoreType.DMA((steps,)),
            pltpu.SemaphoreType.DMA((steps + 2 * order.heads,)),
        ],
        input_output_aliases={
            1 + len(arrays) + len(lead) + i: i for i in range(len(carry))
        },
        compiler_params=pltpu.CompilerParams(vmem_limit_bytes=LARGE),
        cost_estimate=SLIGHT,
    )(pltpu.with_memory_space_constraint(facts, pltpu.SMEM), *arrays, *rest)


def put_rows(order, facts, pieces, dk, dv, top, rows, sem, first):
    copies = []
    count = len(pieces) // 2
    for dst, mine in ((dk, pieces[:count]), (dv, pieces[count:])):
        head = 0
        for src in mine:
            more = src.shape[1] // HD
            for lo, hi in order.runs(head, head + more):
                copies.append(
                    pltpu.make_async_copy(
                        src.at[:, (lo - head) * HD : (hi - head) * HD],
                        dst.at[top : top + rows, pl.ds(order.at(facts, lo, HD), (hi - lo) * HD)],
                        sem.at[first + len(copies)],
                    )
                )
                copies[-1].start()
            head += more
    return copies


def begin_input_grad(order, facts, w, own, after=()):
    out_cols, depth = w.shape
    half = depth // 2
    rows = own[0].shape[0]
    count = len(own)

    def body(facts, w_ref, *refs):
        mine, out = jnp.concatenate([r[...] for r in refs[:count]], axis=1), refs[-1]
        mine = order.real(facts, mine)
        where = pl.ds(pl.multiple_of(facts[SIDE] * half, half), half)
        for at in width_tiles(w):
            out[at] = dot_t(w_ref[at, where], mine)

    smem = pl.BlockSpec(memory_space=pltpu.SMEM)
    vmem = pl.BlockSpec(memory_space=pltpu.VMEM)
    near = [pltpu.with_memory_space_constraint(a, pltpu.VMEM) for a in (w, *own)]

    def kernel(*refs):
        body(*refs[: 2 + count], refs[-1])

    return pl.pallas_call(
        kernel,
        out_shape=pltpu.VMEM((out_cols, rows), F32),
        in_specs=[smem] + [vmem] * len(near) + [pl.BlockSpec(memory_space=pl.ANY)] * len(after),
        out_specs=vmem,
        compiler_params=pltpu.CompilerParams(vmem_limit_bytes=LARGE),
        cost_estimate=SLIGHT,
    )(pltpu.with_memory_space_constraint(facts, pltpu.SMEM), *near, *after)


def end_input_grad(order, facts, w, base, across, corner, begun, grads, carry):
    tiles = width_tiles(w)
    out_cols, depth = w.shape
    half = depth // 2
    steps = len(tiles)
    rows = base.shape[0]

    def body(facts, w_r, begun_r, base_r, across_r, corner_r, *refs):
        out, dk, dv, stage, sem = refs[-5:]
        copies = put_rows(order, facts, refs[:2], dk, dv, 0, rows, sem, steps)
        gained = jnp.concatenate([corner_r[...], across_r[...]], axis=1).astype(F32)
        known = base_r[...]
        more = jnp.where(row_ok(facts[N0], rows, half), known.astype(F32) + gained, 0.0)
        other = order.real(facts, jnp.where(facts[OWNS2] == 1, known, more.astype(BF16)))
        where = pl.ds(pl.multiple_of((1 - facts[SIDE]) * half, half), half)
        for i, at in enumerate(tiles):
            stage[i] = (dot_t(w_r[at, where], other) + begun_r[at]).astype(BF16).T
            copies.append(pltpu.make_async_copy(stage.at[i], out.at[:rows, at], sem.at[i]))
            copies[-1].start()
        for c in copies:
            c.wait()

    return kernel_call(
        body, facts, [w, begun, base, across, corner, *grads], list(carry),
        [(a.shape, a.dtype, False) for a in carry],
        [
            pltpu.VMEM((steps, rows, out_cols // steps), BF16),
            pltpu.SemaphoreType.DMA((steps + 2 * order.heads,)),
        ],
        {("far", i): i for i in range(len(carry))},
    )


def flipped(block, axis, bit):
    count = lax.axis_size(axis)
    return lax.ppermute(block, axis, [(i, i ^ bit) for i in range(count) if i ^ bit < count])


def spanning(leaves, bit_index):
    return len([j for j in range(INNER) if 2 << bit_index <= leaves >> j])


def gather_small_tree(facts, own, beside_pair, beside_half):
    width = own.shape[-1] // 2
    page = ((2, PAGE, width), BF16, True)
    from_core = flipped(own, "sub", 1)

    def choose_chip(facts, own_ref, far_ref, out):
        for swap in range(2):
            for mine in range(2):

                @pl.when((facts[SWAP] == swap) & (facts[OWNS2] != mine))
                def _copy(swap=swap, mine=mine):
                    out[...] = (own_ref if mine else far_ref)[
                        :, :, swap * width : (swap + 1) * width
                    ]

    (chip,) = kernel_call(choose_chip, facts, [own, from_core], [], [page])
    from_pair = flipped(chip, "leaf", 1)

    def choose_pair(facts, near_ref, far_ref, out):
        out[...] = jnp.where(facts[ROOT_IN_CHIP] == 1, near_ref[...], far_ref[...])

    after = beside_pair(from_core, chip)
    (pair,) = kernel_call(choose_pair, facts, [chip, from_pair], [], [page], after=after)
    from_half = flipped(pair, "leaf", 2)

    def choose_all(facts, chip_ref, pair_far, pair_ref, half_far, out):
        out[0] = jnp.where(facts[ROOT_IN_PAIR] == 1, pair_ref[...], half_far[...])
        out[1] = jnp.where(facts[NEXT_IN_CHIP] == 1, chip_ref[...], pair_far[...])

    after = beside_half(pair)
    (mine,) = kernel_call(
        choose_all, facts, [chip, from_pair, pair, from_half], [],
        [((2, *page[0]), BF16, True)], after=after,
    )
    return mine, flipped(mine, "sub", 1)


def over_cores(facts, kept, far):
    width = kept.shape[-1]

    def body(_, near, away, total, root, next_one):
        for i in range(4):
            value = near[i] + away[i].astype(F32)
            total[i] = value
            (root, next_one)[i // 2][i % 2] = value.astype(BF16)

    pages = ((2, PAGE, width), BF16, True)
    total, root, next_one = kernel_call(
        body, facts, [kept, far], [], [((4, PAGE, width), F32, True), pages, pages]
    )
    return total, root, flipped(root, "leaf", 2), flipped(next_one, "leaf", 1)


def over_halves(facts, total, root_far, next_far, after):
    width = total.shape[-1]

    def body(_, near, root_r, next_r, out, low):
        root = near[:2] + root_r[...].astype(F32)
        out[:2] = root
        low[...] = root.astype(BF16)
        out[2:] = near[2:] + next_r[...].astype(F32)

    total, low = kernel_call(
        body, facts, [total, root_far, next_far], [],
        [((4, PAGE, width), F32, True), ((2, PAGE, width), BF16, True)], after=after,
    )
    return total, low, flipped(low, "leaf", 1)


def over_chips(facts, total, far, after):
    width = total.shape[-1]

    def body(facts, near, away, out, values):
        root = near[:2] + away[...].astype(F32)
        picked = jnp.where(facts[ROOT_IN_CHIP] == 1, root, near[2:]).astype(BF16)
        out[...] = picked
        values[...] = picked[1]

    outs = [((2, PAGE, width), BF16, True), ((PAGE, width), BF16, True)]
    mine, values = kernel_call(body, facts, [total, far], [], outs, after=after)
    across = flipped(values, "tensor", 1)
    corner = lax.ppermute(values, ("tensor", "sub"), [(i, 3 - i) for i in range(4)])
    return mine, flipped(mine, "sub", 1), across, corner


def other_level2(order, head, kind, ref):
    theirs = head ^ order.half
    at = theirs % order.half * HD
    return ref[4 + 2 * (theirs // order.half) + kind, :, at : at + HD]


def begin_values(order, facts, own0, level2_far, handed):
    def body(facts, own_r, low_r, handed_r, out, handed_out):
        handed_out[...] = handed_r[...]
        ok = row_ok(facts[N0], PAGE, HD)
        for head in range(order.heads):
            c = slice(head * HD, (head + 1) * HD)
            low = other_level2(order, head, 1, low_r).astype(F32)
            value = own_r[1, :, c] + jnp.where(facts[OWNS2] == 1, low, 0.0)
            out[:, c] = jnp.where(ok, value, 0.0).astype(BF16)

    outs = [((PAGE, own0.shape[-1]), BF16, True), (handed.shape, handed.dtype, True)]
    return kernel_call(body, facts, [own0, level2_far, handed], [], outs)


def finish_small_tree(order, facts, own0, mine, far, level2_far):
    width = own0.shape[-1]

    def body(facts, own_r, mine_r, far_r, low_r, dk, dv):
        owns2 = facts[OWNS2] == 1
        ok = row_ok(facts[N0], PAGE, HD)
        for head in range(order.heads):
            c = slice(head * HD, (head + 1) * HD)
            at = head % order.half * HD
            for kind, out in enumerate((dk, dv)):
                gained = (far_r if head < order.half else mine_r)[kind, :, at : at + HD]
                level2 = other_level2(order, head, kind, low_r)
                more = jnp.where(owns2, level2, gained).astype(F32)
                out[:, c] = jnp.where(ok, own_r[kind, :, c] + more, 0.0).astype(BF16)

    page = ((PAGE, width), BF16, True)
    return kernel_call(body, facts, [own0, mine, far, level2_far], [], [page, page])


def gather_tree(ids, own):
    leaves = lax.axis_size(("leaf", "sub"))
    owned = ids[:INNER] == ids[INNER] - 1
    pages = jnp.where(owned[:, None, None, None], own[None], jnp.zeros((), BF16))
    for bit in range(leaves.bit_length() - 1):
        active = spanning(leaves, bit)
        far = flipped(pages[:active], ("leaf", "sub"), 1 << bit)
        pages = jnp.concatenate([pages[:active] + far, pages[active:]])
    return pages


def reduce_tree(ids, parts):
    leaves = lax.axis_size(("leaf", "sub"))
    for bit in range(leaves.bit_length() - 1):
        active = spanning(leaves, bit)
        far = flipped(parts[:active], ("leaf", "sub"), 1 << bit)
        parts = jnp.concatenate([parts[:active] + far, parts[active:]])
    owned = ids[:INNER] == ids[INNER] - 1
    return jnp.sum(jnp.where(owned[:, None, None, None], parts, 0.0), axis=0)


def on_device(queries, grad_out, keys, values, log_norms, row_deltas, ancestors, counts, w_value):
    kv = keys.shape[1] // HD
    group = queries.shape[1] // keys.shape[1]
    leaves = lax.axis_size(("leaf", "sub"))
    hbm = lambda a: pltpu.with_memory_space_constraint(a, pltpu.HBM)
    side = lax.axis_index("tensor").astype(I32).reshape(1)
    two_sides = lax.axis_size("tensor") == 2
    inputs = [hbm(a) for a in (queries, grad_out, keys, values, log_norms, row_deltas)]
    fast = leaves == 8 and lax.axis_size("sub") == 2 and kv == 4 and two_sides
    order = Order(fast, kv)
    facts, own = start(order, side, hbm(ancestors), hbm(counts), *inputs[2:4])
    state = {}

    def own_pages(kvs, pages, prior=(), after=()):
        return attend(True, kvs, group, order, facts, inputs, pages, state, prior, after)

    def shared_pages(kvs, page, ride=None, after=()):
        return attend(
            False, kvs, group, order, facts, inputs, [page], state, after=after, ride=ride
        )[0]

    def spread(part):
        if two_sides:
            return flipped(part, "tensor", 1)
        return lax.all_gather(part, "tensor", axis=1, tiled=True)

    kvs = tuple(range(kv))
    w = hbm(w_value)
    if fast:
        level2, calls = [], []

        def beside_pair(from_core, chip):
            level2.extend((own, from_core))
            calls.append(own_pages(kvs[:1], level2, after=(chip,)))
            return (calls[0][3],)

        def beside_half(pair):
            calls.append(own_pages(kvs[1:], level2, calls[0], (pair,)))
            return (calls[1][3],)

        mine, theirs = gather_small_tree(facts, own, beside_pair, beside_half)
        dk12, dv12, own0, send2 = calls[1]
        sent = flipped(shared_pages(kvs[:2], mine, send2), "sub", 1)
        kept = shared_pages(kvs[2:], theirs)
        total, root, root_far, next_far = over_cores(facts, kept, sent)
        base, dv12 = begin_values(order, facts, own0, sent, dv12)
        far_v = spread(dv12)
        made, w_near = finish_queries(
            kvs, group, order, facts, (mine, theirs), state, (root, base), w
        )
        total, low, far = over_halves(facts, total, root_far, next_far, (made,))
        base_far = spread(base)
        *grads, made = input_grad(
            order, facts, w_near, 2 * PAGE, [dv12], [far_v], ([dk12], [dv12]), near_w=True,
            after=(low,),
        )
        near, far, across, corner = over_chips(facts, total, far, (made, base_far))
        dk0, dv0 = finish_small_tree(order, facts, own0, near, far, sent)
        begun = begin_input_grad(order, facts, w_near, [dv0])
        grads = end_input_grad(
            order, facts, w_near, base_far, across, corner, begun, [dk0, dv0], grads
        )
        return (state["gq"], grads[1], grads[2], grads[0])

    path_ids = ancestors[0]
    pages = gather_tree(path_ids, own)
    dk12, dv12, own0, send2 = own_pages(kvs, (pages[2], pages[2]))
    grads = shared_pages(kvs, pages[:2])
    finish_queries(kvs, group, order, facts, (pages[:2],), state)
    low = send2.astype(F32)
    total = reduce_tree(path_ids, jnp.concatenate([grads.reshape(2, 2, *grads.shape[1:]), low[None]]))
    total += own0 - jnp.where(path_ids[2] == path_ids[INNER] - 1, low, 0.0)
    has = jnp.any(path_ids[:INNER] == path_ids[INNER] - 1)
    ok = (jnp.arange(PAGE) < jnp.where(has, counts[0, 0], 0))[:, None]
    dk0, dv0 = jnp.where(ok, total, 0.0).astype(BF16)
    if two_sides:
        pair = lambda part: ([part], [spread(part)])
    else:
        pair = lambda part: ([spread(part)], [])
    *grads, _ = input_grad(order, facts, w, 2 * PAGE, *pair(dv12), ([dk12], [dv12]))
    grads = input_grad(order, facts, w, PAGE, *pair(dv0), ([dk0], [dv0]), grads)
    return (state["gq"], grads[1], grads[2], grads[0])


def solution(mesh):
    placed = (
        P(("groups", "leaf", "sub"), "tensor"),
        P(("groups", "leaf", "sub"), "tensor"),
        P(("groups", "leaf", "sub"), "tensor"),
        P(("groups", "leaf", "sub"), "tensor"),
        P("tensor", ("groups", "leaf", "sub")),
        P("tensor", ("groups", "leaf", "sub")),
        P(("groups", "leaf", "sub"), None),
        P(("groups", "leaf", "sub"), None),
        P("tensor", None),
    )
    return jax.shard_map(
        on_device,
        mesh=mesh,
        in_specs=placed,
        out_specs=(
            P(("groups", "leaf", "sub"), "tensor"),
            P(("groups", "leaf", "sub"), "tensor"),
            P(("groups", "leaf", "sub"), "tensor"),
            P(("groups", "leaf", "sub"), "tensor"),
        ),
        check_vma=False,
    )
```

```python
import math

import jax
import jax.numpy as jnp
from jax import lax
from jax.experimental import pallas as pl
from jax.experimental.pallas import tpu as pltpu
from jax.sharding import PartitionSpec as P

HD = 128
PAGE = 128
SLOTS = 3
INNER = 3
ROWS = SLOTS * PAGE
LOG2E = math.log2(math.e)
SCALE = 1.0 / math.sqrt(HD)
BF16 = jnp.bfloat16
F32 = jnp.float32
I32 = jnp.int32
LARGE = 10 << 20
SMALL = 4 << 20
SLIGHT = pl.CostEstimate(flops=1000, bytes_accessed=1000, transcendentals=0)
BLOCKED = 1e30


def dot_t(left, right):
    return lax.dot_general(left, right, (((1,), (1,)), ((), ())), preferred_element_type=F32)


def dot_n(left, right):
    return lax.dot_general(left, right, (((1,), (0,)), ((), ())), preferred_element_type=F32)


FACTS = 16
N0, N1, N2, OWNS2, LIMIT, LEADS, ROOT_IN_CHIP, ROOT_IN_PAIR, NEXT_IN_CHIP, SIDE, SWAP = range(11)


class Order:
    def __init__(self, crossed, heads):
        self.crossed, self.heads = crossed, heads
        self.half = heads // 2 if crossed else heads

    def at(self, facts, head, unit):
        if not self.crossed:
            return head * unit
        step = ((head ^ self.half) - head) * unit
        return pl.multiple_of(facts[SWAP] * step + head * unit, unit)

    def runs(self, first, last):
        cuts = [first, *(h for h in range(first + 1, last) if h % self.half == 0), last]
        return list(zip(cuts[:-1], cuts[1:]))

    def real(self, facts, rows):
        if not self.crossed:
            return rows
        width = self.half * HD
        turned = jnp.concatenate([rows[:, width:], rows[:, :width]], axis=1)
        return jnp.where(facts[SWAP] == 1, turned, rows)


def write_facts(facts, ids, counts, side, order):
    page = [ids[0, j] for j in range(INNER + 1)]
    own = page[INNER] - 1
    leaf = own // SLOTS
    owns = [page[j] == own for j in range(INNER)]
    same = lambda level, shift: ((page[level] // SLOTS) >> shift) == (leaf >> shift)
    number = lambda flag: jnp.where(flag, 1, 0)
    facts[N0] = jnp.where(owns[0] | owns[1] | owns[2], counts[0, 0], 0)
    facts[N1] = counts[0, 1]
    facts[N2] = counts[0, 2]
    facts[OWNS2] = number(owns[2])
    facts[LIMIT] = jnp.where(owns[2], 2 * PAGE, jnp.where(owns[1], PAGE, 0))
    facts[LEADS] = number(lax.rem(leaf, 2) == 0)
    facts[ROOT_IN_CHIP] = number(same(0, 1))
    facts[ROOT_IN_PAIR] = number(same(0, 2))
    facts[NEXT_IN_CHIP] = number(same(1, 1))
    facts[SIDE] = side
    facts[SWAP] = lax.rem(leaf, 2) if order.crossed else 0
    for i in range(SWAP + 1, FACTS):
        facts[i] = 0


def row_ok(count, rows, width):
    return lax.broadcasted_iota(I32, (rows, width), 0) < count


def kernel_call(body, facts, near, far, outs, scratch=(), aliases=None, after=(), cost=None,
                limit=SMALL):
    smem = pl.BlockSpec(memory_space=pltpu.SMEM)
    vmem = pl.BlockSpec(memory_space=pltpu.VMEM)
    hbm = pl.BlockSpec(memory_space=pl.ANY)
    near = [pltpu.with_memory_space_constraint(a, pltpu.VMEM) for a in near]
    place = {("near", i): 1 + i for i in range(len(near))}
    place |= {("far", i): 1 + len(near) + i for i in range(len(far))}
    used = 1 + len(near) + len(far)

    def kernel(*refs):
        body(*refs[:used], *refs[used + len(after) :])

    return pl.pallas_call(
        kernel,
        out_shape=tuple(
            pltpu.VMEM(s, d) if inside else jax.ShapeDtypeStruct(s, d) for s, d, inside in outs
        ),
        in_specs=[smem] + [vmem] * len(near) + [hbm] * (len(far) + len(after)),
        out_specs=tuple(vmem if inside else hbm for _, _, inside in outs),
        scratch_shapes=list(scratch),
        input_output_aliases={place[k]: v for k, v in (aliases or {}).items()},
        compiler_params=pltpu.CompilerParams(vmem_limit_bytes=limit),
        cost_estimate=cost or SLIGHT,
    )(pltpu.with_memory_space_constraint(facts, pltpu.SMEM), *near, *far, *after)


def start(order, side, ids, counts, keys, values):
    width = keys.shape[1]

    def body(side_ref, ids_ref, counts_ref, k_ref, v_ref, facts, out, held, ids_s, counts_s, sem):
        copies = [
            pltpu.make_async_copy(src, dst, sem.at[i])
            for i, (src, dst) in enumerate(
                (
                    (ids_ref, ids_s),
                    (counts_ref, counts_s),
                    (k_ref.at[:PAGE], held.at[0]),
                    (v_ref.at[:PAGE], held.at[1]),
                )
            )
        ]
        for c in copies:
            c.start()
        copies[0].wait()
        copies[1].wait()
        write_facts(facts, ids_s, counts_s, side_ref[0], order)
        ok = row_ok(counts_s[0, 0], PAGE, width)
        for i in range(2):
            copies[2 + i].wait()
            out[i] = jnp.where(ok, held[i], jnp.zeros((), BF16))

    smem = pl.BlockSpec(memory_space=pltpu.SMEM)
    hbm = pl.BlockSpec(memory_space=pl.ANY)
    return pl.pallas_call(
        body,
        out_shape=(pltpu.SMEM((FACTS,), I32), pltpu.VMEM((2, PAGE, width), BF16)),
        in_specs=[smem] + [hbm] * 4,
        out_specs=(smem, pl.BlockSpec(memory_space=pltpu.VMEM)),
        scratch_shapes=[
            pltpu.VMEM((2, PAGE, width), BF16),
            pltpu.SMEM(ids.shape, I32),
            pltpu.SMEM(counts.shape, I32),
            pltpu.SemaphoreType.DMA((4,)),
        ],
        compiler_params=pltpu.CompilerParams(vmem_limit_bytes=SMALL),
    )(side, ids, counts, keys, values)


def row_terms(rows):
    high = rows.astype(BF16).astype(F32)
    rest = rows - high
    middle = rest.astype(BF16).astype(F32)
    parts = [high, middle, rest - middle]
    spare = HD - 3 * rows.shape[0]
    parts.append(jnp.zeros((spare, rows.shape[1]), F32))
    return jnp.concatenate(parts, axis=0).T.astype(BF16)


class Head:
    def __init__(self, kv, group, norms, deltas, en, ed):
        self.group = group
        self.heads = min(4, group)
        self.parts = group // self.heads
        self.tall = self.heads * PAGE
        heads = slice(kv * group, (kv + 1) * group)
        en[...] = row_terms(norms[heads, :])
        ed[...] = row_terms(deltas[heads, :])

    def lanes(self, part, j):
        at = (part * self.heads + j) * HD
        return slice(at, at + HD)

    def stacked(self, ref, part, slots):
        return jnp.concatenate(
            [
                ref[slot * PAGE : (slot + 1) * PAGE, self.lanes(part, j)]
                for slot in slots
                for j in range(self.heads)
            ],
            axis=0,
        )

    def deep(self, stacked, terms, part, slots):
        column = lax.broadcasted_iota(I32, (1, HD), 1) % self.group
        picks = [
            (column == part * self.heads + j).astype(F32).astype(BF16)
            for j in range(self.heads)
        ]
        extra = [
            terms[slot * PAGE : (slot + 1) * PAGE] * pick for slot in slots for pick in picks
        ]
        return jnp.concatenate([stacked, jnp.concatenate(extra, axis=0)], axis=1)

    def turned_at(self, part, slot, count):
        at = (part * SLOTS + slot) * self.tall
        return slice(at, at + self.tall * count)


def set_keys(deep, upright, at, page):
    where = slice(at * PAGE, (at + 1) * PAGE)
    deep[:HD, where] = page.T
    if upright is not None:
        upright[where] = page


def weigh(scores, grads, keep):
    p = keep(jnp.exp2(scores * (SCALE * LOG2E)))
    return p.astype(BF16), (p * grads).astype(BF16)


def attend(own, kvs, group, order, facts, inputs, pages, state, prior=(), after=(),
           ride=None):
    loading = "k" not in state
    q_all, k_all = inputs[0], inputs[2]
    count = len(kvs)
    parts = group // min(4, group)
    tall = min(4, group) * PAGE
    width = count * HD
    base = prior[0].shape[1] if prior else 0
    kv_total = k_all.shape[1] // HD
    fresh = [("qt", kv) not in state for kv in kvs]
    one_head = (ROWS, group * HD)
    turned = ((HD, group * ROWS), BF16, True)
    low = lambda rows, columns: ((rows, columns), BF16, True)
    shapes = {
        "da": low(2 * group * PAGE, 2 * PAGE),
        "db": low(2 * group * PAGE, PAGE),
        "ku": low(4 * PAGE, HD),
        "qt": turned,
        "gt": turned,
    }

    near, far, aliases, outs = [], [], {}, []
    at_near, at_far, at_out = {}, {}, {}

    def add_near(name, array):
        at_near[name] = len(near)
        near.append(array)

    def add_far(name, array):
        at_far[name] = len(far)
        far.append(array)

    def add_out(name, out):
        at_out[name] = len(outs)
        outs.append(out)

    for kv, is_fresh in zip(kvs, fresh):
        for name, shape in shapes.items():
            if is_fresh:
                add_out((name, kv), shape)
            elif name in ("qt", "gt"):
                add_near((name, kv), state[name, kv])
        if not own and not is_fresh:
            add_out(("ds", kv), ((group * ROWS, 2 * PAGE), BF16, True))
    at_results = len(outs)
    if own:
        outs += [
            ((2 * PAGE, base + width), BF16, True),
            ((2 * PAGE, base + width), BF16, True),
            ((2, PAGE, base + width), F32, True),
            ((2, PAGE, base + width), BF16, True),
        ]
    else:
        outs += [
            ((4, PAGE, width), F32, True) if ride is None else ((8, PAGE, width), BF16, True),
        ]
    at_loaded = len(outs)
    if loading:
        for name, array in zip(("q", "g", "k", "v", "norms", "deltas"), inputs):
            add_far(name, array)
            if name in ("q", "g"):
                for kv in range(kv_total):
                    add_out((name, kv), (one_head, BF16, True))
            else:
                add_out(name, (array.shape, array.dtype, True))
    else:
        for name in ("k", "v", "norms", "deltas"):
            add_near(name, state[name])
        for kv in kvs:
            for name in ("q", "g"):
                add_near((name, kv), state[name, kv])
    for i, page in enumerate(pages):
        add_near(("page", i), page)
    for i, array in enumerate(prior):
        add_near(("prior", i), array)
    if ride is not None:
        add_near("ride", ride)
    key_pages = 4 if own else 2
    scratch = [
        pltpu.VMEM((2 * HD, key_pages * PAGE), BF16),
        pltpu.VMEM((2 * HD, key_pages * PAGE), BF16),
        pltpu.VMEM((key_pages * PAGE, HD), BF16),
        pltpu.VMEM((2, HD, key_pages * PAGE), F32),
        pltpu.VMEM((ROWS, HD), BF16),
        pltpu.VMEM((ROWS, HD), BF16),
        pltpu.SemaphoreType.DMA((2 * kv_total + 8,)),
    ]
    cols = lambda a, b: slice(a * PAGE, b * PAGE)

    def body(facts, *refs):
        ins, out_refs = refs[: len(near) + len(far)], refs[len(near) + len(far) : -len(scratch)]
        k_deep, v_deep, k_up, acc, en, ed, load_sem = refs[-len(scratch) :]
        near_ref = lambda name: ins[at_near[name]]
        far_ref = lambda name: ins[len(near) + at_far[name]]
        held = lambda name: out_refs[at_out[name]] if name in at_out else near_ref(name)
        results = out_refs[at_results:at_loaded]
        copies = {}
        if loading:

            def load(key, src, dst):
                copies[key] = pltpu.make_async_copy(src, dst, load_sem.at[len(copies)])
                copies[key].start()

            for lo, hi in order.runs(0, kv_total):
                for name in ("k", "v"):
                    at = pl.ds(order.at(facts, lo, HD), (hi - lo) * HD)
                    here = slice(lo * HD, hi * HD)
                    load((name, lo), far_ref(name).at[:, at], held(name).at[:, here])
                for name in ("norms", "deltas"):
                    at = pl.ds(order.at(facts, lo, group), (hi - lo) * group)
                    here = slice(lo * group, hi * group)
                    load((name, lo), far_ref(name).at[at], held(name).at[here])
            shared_loads = list(copies)
            for kv in range(kv_total):
                at = pl.ds(order.at(facts, kv, group * HD), group * HD)
                for name in ("q", "g"):
                    load((name, kv), far_ref(name).at[:, at], held((name, kv)))
        k, v, norms, deltas = (held(name) for name in ("k", "v", "norms", "deltas"))

        def arrived(*keys):
            for key in keys:
                if key in copies:
                    copies.pop(key).wait()

        k_deep[HD:] = jnp.full((HD, key_pages * PAGE), -1.0, BF16)
        v_deep[HD:] = jnp.full((HD, key_pages * PAGE), -1.0, BF16)
        for out, i in zip(results, range(len(prior))):
            out[..., :base] = near_ref(("prior", i))[...]
        if ride is not None:
            (out,), more = results, near_ref("ride")
            for kind in range(2):
                out[4 + kind] = more[kind, :, :width]
                out[6 + kind] = more[kind, :, width:]
        owns2 = facts[OWNS2] == 1
        if loading:
            arrived(*shared_loads)
            lane = lax.broadcasted_iota(I32, norms.shape, 1)
            limit = jnp.where(
                lane < PAGE, facts[N0], jnp.where(lane < 2 * PAGE, facts[N1], facts[N2])
            )
            norms[...] = jnp.where(lane % PAGE < limit, norms[...] * (1.0 / SCALE), BLOCKED)
        lower = lambda rows: lax.broadcasted_iota(I32, (rows, PAGE), 1) <= (
            lax.broadcasted_iota(I32, (rows, PAGE), 0) % PAGE
        )

        def set_pages(n, kv):
            lane = slice(kv * HD, (kv + 1) * HD)
            if own:
                first, second = (near_ref(("page", i)) for i in range(2))
                zero = jnp.zeros((), BF16)
                for slot, (at, c) in enumerate(((3, N0), (0, N1), (2, N2))):
                    ok = row_ok(facts[c], PAGE, HD)
                    rows = cols(slot, slot + 1)
                    set_keys(k_deep, k_up, at, jnp.where(ok, k[rows, lane], zero))
                    set_keys(v_deep, None, at, jnp.where(ok, v[rows, lane], zero))
                level2 = [jnp.where(owns2, first[i, :, lane], second[i, :, lane]) for i in (0, 1)]
                if order.crossed:
                    at = (kv ^ order.half) * HD
                    lane = slice(at, at + HD)
                    for i in range(2):
                        other = jnp.where(owns2, first[i, :, lane], second[i, :, lane])
                        level2[i] = jnp.where(facts[SWAP] == 1, other, level2[i])
                set_keys(k_deep, k_up, 1, level2[0])
                set_keys(v_deep, None, 1, level2[1])
            else:
                page = near_ref(("page", 0))
                for j in range(2):
                    here = slice(n * HD, (n + 1) * HD)
                    set_keys(k_deep, k_up, j, page[j, 0, :, here])
                    set_keys(v_deep, None, j, page[j, 1, :, here])
            acc[...] = jnp.zeros_like(acc)

        def turned_rows(head, kv, part, is_fresh, qs, gs, order):
            if is_fresh:
                for name, rows in (("qt", qs), ("gt", gs)):
                    for i, slot in enumerate(order):
                        held((name, kv))[:, head.turned_at(part, slot, 1)] = rows[
                            i * tall : (i + 1) * tall
                        ].T
            return lambda name, slot, slots: held((name, kv))[
                :, head.turned_at(part, slot, slots)
            ]

        def own_part(head, kv, part, n):
            order = (1, 2, 0)
            qs = head.stacked(held(("q", kv)), part, order)
            gs = head.stacked(held(("g", kv)), part, order)
            qd, gd = head.deep(qs, en, part, order), head.deep(gs, ed, part, order)
            turn = turned_rows(head, kv, part, fresh[n], qs, gs, order)
            low = lower(tall)

            def keep_first(p):
                masked = jnp.where(low, p[:tall, :PAGE], 0.0)
                return jnp.concatenate(
                    [jnp.concatenate([masked, p[:tall, PAGE:]], axis=1), p[tall:]], axis=0
                )

            pa, da = weigh(
                dot_n(qd[: 2 * tall], k_deep[:, : 2 * PAGE]),
                dot_n(gd[: 2 * tall], v_deep[:, : 2 * PAGE]),
                keep_first,
            )
            both = lambda x: jnp.concatenate([x[:tall, :PAGE], x[tall:, PAGE:]], axis=0)
            low2 = lower(2 * tall)
            pb, db = weigh(
                both(dot_n(qd[tall:], k_deep[:, 2 * PAGE :])),
                both(dot_n(gd[tall:], v_deep[:, 2 * PAGE :])),
                lambda p: jnp.where(low2, p, 0.0),
            )
            for i, (name, a, b) in enumerate((("qt", da, db), ("gt", pa, pb))):
                acc[i, :, : 2 * PAGE] += dot_n(turn(name, 1, 2), a)
                acc[i, :, cols(2, 3)] += dot_n(turn(name, 2, 1), b[:tall])
                acc[i, :, cols(3, 4)] += dot_n(turn(name, 0, 1), b[tall:])
            here = slice(part * 2 * tall, (part + 1) * 2 * tall)
            held(("da", kv))[here] = da
            held(("db", kv))[here] = db

        def shared_part(head, kv, part, n):
            order = (0, 1, 2)
            qs = head.stacked(held(("q", kv)), part, order)
            gs = head.stacked(held(("g", kv)), part, order)
            qd, gd = head.deep(qs, en, part, order), head.deep(gs, ed, part, order)
            turn = turned_rows(head, kv, part, fresh[n], qs, gs, order)
            column = lax.broadcasted_iota(I32, (tall, 2 * PAGE), 1)
            seen = column < facts[LIMIT]

            def keep(p):
                return jnp.concatenate([jnp.where(seen, p[:tall], 0.0), p[tall:]], axis=0)

            p, ds = weigh(dot_n(qd, k_deep[...]), dot_n(gd, v_deep[...]), keep)
            acc[0] += dot_n(turn("qt", 0, SLOTS), ds)
            acc[1] += dot_n(turn("gt", 0, SLOTS), p)
            held(("ds", kv))[part * SLOTS * tall : (part + 1) * SLOTS * tall] = ds

        def put_own(n):
            dk12, dv12, own0, send2 = results
            here = slice(base + n * HD, base + (n + 1) * HD)
            grad = [acc[0].T * SCALE, acc[1].T]
            for at, c, to in ((0, N1, 0), (2, N2, 1)):
                ok = row_ok(facts[c], PAGE, HD)
                for kind, out in ((0, dk12), (1, dv12)):
                    out[cols(to, to + 1), here] = jnp.where(
                        ok, grad[kind][cols(at, at + 1)], 0.0
                    ).astype(BF16)
            for kind in range(2):
                level2 = grad[kind][cols(1, 2)]
                own0[kind, :, here] = grad[kind][cols(3, 4)] + jnp.where(owns2, level2, 0.0)
                send2[kind, :, here] = level2.astype(BF16)

        def put_shared(n):
            (out,) = results
            here = slice(n * HD, (n + 1) * HD)
            grads = acc[0].T * SCALE, acc[1].T
            for j in range(2):
                for kind in range(2):
                    out[2 * j + kind, :, here] = grads[kind][cols(j, j + 1)].astype(out.dtype)

        for n, kv in enumerate(kvs):
            arrived(("q", kv), ("g", kv))
            head = Head(kv, group, norms, deltas, en, ed)
            set_pages(n, kv)

            for part in range(parts):
                (own_part if own else shared_part)(head, kv, part, n)
            if own:
                held(("ku", kv))[...] = k_up[...]
            (put_own if own else put_shared)(n)
        arrived(*list(copies))

    made = kernel_call(
        body, facts, near, far, outs, scratch, aliases, after,
        pl.CostEstimate(
            flops=240 * PAGE * PAGE * HD * group * count, bytes_accessed=1000, transcendentals=0
        ),
        LARGE,
    )
    for name, at in at_out.items():
        state[name] = made[at]
    return list(made[at_results:at_loaded])


def width_tiles(w):
    tile = next(t for t in (512, 640, 320, 128, w.shape[0]) if w.shape[0] % t == 0)
    return [slice(i, i + tile) for i in range(0, w.shape[0], tile)]


def finish_queries(kvs, group, order, facts, pages, state, after=(), w=None):
    parts = group // min(4, group)
    heads = group // parts
    tall = heads * PAGE
    wide = heads * HD
    near = list(pages)
    names = ("ds", "da", "db", "ku")
    for kv in kvs:
        near += [state[name, kv] for name in names]

    def body(facts, *refs):
        stage, sem = refs[-2:]
        if w is not None:
            gq, made, w_near = refs[-5:-2]
            w_copy = pltpu.make_async_copy(refs[-6], w_near, sem.at[len(kvs) * parts])
            w_copy.start()
        else:
            gq, made = refs[-4:-2]
        made[...] = jnp.zeros_like(made)
        sends = []
        for n, kv in enumerate(kvs):
            first = len(pages) + len(names) * n
            ds, da, db, ku = refs[first : first + len(names)]
            page, at = refs[kv // order.half], kv % order.half * HD
            keys = jnp.concatenate([page[j, 0, :, at : at + HD] for j in range(2)], axis=0)
            for part in range(parts):
                at = n * parts + part
                gained = dot_n(ds[part * SLOTS * tall : (part + 1) * SLOTS * tall], keys)
                here = part * 2 * tall
                wide_part = dot_n(da[here : here + 2 * tall], ku[: 2 * PAGE])
                own2 = dot_n(db[here : here + tall], ku[2 * PAGE : 3 * PAGE])
                own0 = dot_n(db[here + tall : here + 2 * tall], ku[3 * PAGE :])
                by_slot = (
                    gained[:tall] + own0,
                    gained[tall : 2 * tall] + wide_part[:tall],
                    gained[2 * tall :] + (wide_part[tall:] + own2),
                )
                for i in range(SLOTS * heads):
                    slot, j = divmod(i, heads)
                    rows = slice(slot * PAGE, (slot + 1) * PAGE)
                    value = by_slot[slot][j * PAGE : (j + 1) * PAGE]
                    stage[at, rows, j * HD : (j + 1) * HD] = (value * SCALE).astype(BF16)
                to = pl.multiple_of(order.at(facts, kv, group * HD) + part * wide, wide)
                sends.append(
                    pltpu.make_async_copy(stage.at[at], gq.at[:, pl.ds(to, wide)], sem.at[at])
                )
                sends[-1].start()
        for c in sends:
            c.wait()
        if w is not None:
            w_copy.wait()

    count = len(kvs) * parts
    far = [state["gq"]] if "gq" in state else []
    aliases = {("far", 0): 0} if far else {}
    shape = (ROWS, state["k"].shape[1] * group)
    outs = [(shape, BF16, False), ((8, HD), F32, True)]
    if w is not None:
        far = far + [w]
        outs.append((w.shape, w.dtype, True))
    state["gq"], *made = kernel_call(
        body, facts, near, far, outs,
        [pltpu.VMEM((count, ROWS, wide), BF16), pltpu.SemaphoreType.DMA((count + 1,))],
        aliases, after, limit=LARGE,
    )
    return made


def input_grad(order, facts, w, rows, own, far, grads, carry=None, near_w=False, after=()):
    out_cols, depth = w.shape
    tiles = width_tiles(w)
    top = 0 if rows == PAGE else PAGE
    steps = len(tiles)
    width = sum(a.shape[1] for a in grads[0])
    arrays = [*own, *far, *grads[0], *grads[1]] + [w] * near_w
    count = len(grads[0])
    carry = list(carry or [])
    lead = [] if near_w else [w]
    rest = [*lead, *carry, *after]

    def body(facts, *refs):
        own_r, refs = refs[: len(own)], refs[len(own) :]
        far_r, refs = refs[: len(far)], refs[len(far) :]
        grad_r, w_ref = refs[: 2 * count], refs[2 * count]
        out, dk, dv, made, w_near, stage, w_sem, sem = refs[-8:]
        loads = []
        if not near_w:
            loads = [
                pltpu.make_async_copy(w_ref.at[at], w_near.at[at], w_sem.at[i])
                for i, at in enumerate(tiles)
            ]
        for c in loads:
            c.start()
        made[...] = jnp.zeros_like(made)
        columns = lambda rs: jnp.concatenate([r[...] for r in rs], axis=1)
        full = order.real(facts, columns(own_r))
        if far:
            other, first = order.real(facts, columns(far_r)), facts[SIDE] == 0
            full = jnp.concatenate(
                [jnp.where(first, full, other), jnp.where(first, other, full)], axis=1
            )
        copies = put_rows(order, facts, grad_r, dk, dv, top, rows, sem, steps)
        for i, at in enumerate(tiles):
            if loads:
                loads[i].wait()
            stage[i] = dot_t((w_ref if near_w else w_near)[at], full).astype(BF16).T
            copies.append(
                pltpu.make_async_copy(stage.at[i], out.at[top : top + rows, at], sem.at[i])
            )
            copies[-1].start()
        for c in copies:
            c.wait()

    smem = pl.BlockSpec(memory_space=pltpu.SMEM)
    vmem = pl.BlockSpec(memory_space=pltpu.VMEM)
    hbm = pl.BlockSpec(memory_space=pl.ANY)
    arrays = [pltpu.with_memory_space_constraint(a, pltpu.VMEM) for a in arrays]
    kept = jax.ShapeDtypeStruct((ROWS, width), BF16)
    return pl.pallas_call(
        body,
        out_shape=(
            jax.ShapeDtypeStruct((ROWS, out_cols), BF16), kept, kept, pltpu.VMEM((8, HD), F32)
        ),
        in_specs=[smem] + [vmem] * len(arrays) + [hbm] * len(rest),
        out_specs=(hbm, hbm, hbm, vmem),
        scratch_shapes=[
            pltpu.VMEM((8, HD) if near_w else w.shape, BF16),
            pltpu.VMEM((steps, rows, out_cols // steps), BF16),
            pltpu.SemaphoreType.DMA((steps,)),
            pltpu.SemaphoreType.DMA((steps + 2 * order.heads,)),
        ],
        input_output_aliases={
            1 + len(arrays) + len(lead) + i: i for i in range(len(carry))
        },
        compiler_params=pltpu.CompilerParams(vmem_limit_bytes=LARGE),
        cost_estimate=SLIGHT,
    )(pltpu.with_memory_space_constraint(facts, pltpu.SMEM), *arrays, *rest)


def put_rows(order, facts, pieces, dk, dv, top, rows, sem, first):
    copies = []
    count = len(pieces) // 2
    for dst, mine in ((dk, pieces[:count]), (dv, pieces[count:])):
        head = 0
        for src in mine:
            more = src.shape[1] // HD
            for lo, hi in order.runs(head, head + more):
                copies.append(
                    pltpu.make_async_copy(
                        src.at[:, (lo - head) * HD : (hi - head) * HD],
                        dst.at[top : top + rows, pl.ds(order.at(facts, lo, HD), (hi - lo) * HD)],
                        sem.at[first + len(copies)],
                    )
                )
                copies[-1].start()
            head += more
    return copies


def begin_input_grad(order, facts, w, own, after=()):
    out_cols, depth = w.shape
    half = depth // 2
    rows = own[0].shape[0]
    count = len(own)

    def body(facts, w_ref, *refs):
        mine, out = jnp.concatenate([r[...] for r in refs[:count]], axis=1), refs[-1]
        mine = order.real(facts, mine)
        where = pl.ds(pl.multiple_of(facts[SIDE] * half, half), half)
        for at in width_tiles(w):
            out[at] = dot_t(w_ref[at, where], mine)

    smem = pl.BlockSpec(memory_space=pltpu.SMEM)
    vmem = pl.BlockSpec(memory_space=pltpu.VMEM)
    near = [pltpu.with_memory_space_constraint(a, pltpu.VMEM) for a in (w, *own)]

    def kernel(*refs):
        body(*refs[: 2 + count], refs[-1])

    return pl.pallas_call(
        kernel,
        out_shape=pltpu.VMEM((out_cols, rows), F32),
        in_specs=[smem] + [vmem] * len(near) + [pl.BlockSpec(memory_space=pl.ANY)] * len(after),
        out_specs=vmem,
        compiler_params=pltpu.CompilerParams(vmem_limit_bytes=LARGE),
        cost_estimate=SLIGHT,
    )(pltpu.with_memory_space_constraint(facts, pltpu.SMEM), *near, *after)


def end_input_grad(order, facts, w, base, across, corner, begun, grads, carry, after):
    tiles = width_tiles(w)
    out_cols, depth = w.shape
    half = depth // 2
    steps = len(tiles)
    rows = base.shape[0]

    def body(facts, w_r, begun_r, base_r, across_r, corner_r, *refs):
        out, dk, dv, stage, sem = refs[-5:]
        copies = put_rows(order, facts, refs[:2], dk, dv, 0, rows, sem, steps)
        gained = jnp.concatenate([corner_r[...], across_r[...]], axis=1).astype(F32)
        known = base_r[...]
        more = jnp.where(row_ok(facts[N0], rows, half), known.astype(F32) + gained, 0.0)
        other = order.real(facts, jnp.where(facts[OWNS2] == 1, known, more.astype(BF16)))
        where = pl.ds(pl.multiple_of((1 - facts[SIDE]) * half, half), half)
        for i, at in enumerate(tiles):
            stage[i] = (dot_t(w_r[at, where], other) + begun_r[at]).astype(BF16).T
            copies.append(pltpu.make_async_copy(stage.at[i], out.at[:rows, at], sem.at[i]))
            copies[-1].start()
        for c in copies:
            c.wait()

    return kernel_call(
        body, facts, [w, begun, base, across, corner, *grads], list(carry),
        [(a.shape, a.dtype, False) for a in carry],
        [
            pltpu.VMEM((steps, rows, out_cols // steps), BF16),
            pltpu.SemaphoreType.DMA((steps + 2 * order.heads,)),
        ],
        {("far", i): i for i in range(len(carry))}, after,
    )


def flipped(block, axis, bit):
    count = lax.axis_size(axis)
    return lax.ppermute(block, axis, [(i, i ^ bit) for i in range(count) if i ^ bit < count])


def spanning(leaves, bit_index):
    return len([j for j in range(INNER) if 2 << bit_index <= leaves >> j])


def gather_small_tree(facts, own, beside_pair, beside_half):
    width = own.shape[-1] // 2
    page = ((2, PAGE, width), BF16, True)
    from_core = flipped(own, "sub", 1)

    def choose_chip(facts, own_ref, far_ref, out):
        for swap in range(2):
            for mine in range(2):

                @pl.when((facts[SWAP] == swap) & (facts[OWNS2] != mine))
                def _copy(swap=swap, mine=mine):
                    out[...] = (own_ref if mine else far_ref)[
                        :, :, swap * width : (swap + 1) * width
                    ]

    (chip,) = kernel_call(choose_chip, facts, [own, from_core], [], [page])
    from_pair = flipped(chip, "leaf", 1)

    def choose_pair(facts, near_ref, far_ref, out):
        out[...] = jnp.where(facts[ROOT_IN_CHIP] == 1, near_ref[...], far_ref[...])

    after = beside_pair(from_core, chip)
    (pair,) = kernel_call(choose_pair, facts, [chip, from_pair], [], [page], after=after)
    from_half = flipped(pair, "leaf", 2)

    def choose_all(facts, chip_ref, pair_far, pair_ref, half_far, out):
        out[0] = jnp.where(facts[ROOT_IN_PAIR] == 1, pair_ref[...], half_far[...])
        out[1] = jnp.where(facts[NEXT_IN_CHIP] == 1, chip_ref[...], pair_far[...])

    after = beside_half(pair)
    (mine,) = kernel_call(
        choose_all, facts, [chip, from_pair, pair, from_half], [],
        [((2, *page[0]), BF16, True)], after=after,
    )
    return mine, flipped(mine, "sub", 1)


def over_cores(facts, kept, far):
    width = kept.shape[-1]

    def body(_, near, away, total, root, next_one):
        for i in range(4):
            value = near[i] + away[i].astype(F32)
            total[i] = value
            (root, next_one)[i // 2][i % 2] = value.astype(BF16)

    pages = ((2, PAGE, width), BF16, True)
    total, root, next_one = kernel_call(
        body, facts, [kept, far], [], [((4, PAGE, width), F32, True), pages, pages]
    )
    return total, root, flipped(root, "leaf", 2), flipped(next_one, "leaf", 1)


def over_halves(facts, total, root_far, next_far, after):
    width = total.shape[-1]

    def body(_, near, root_r, next_r, out, low):
        root = near[:2] + root_r[...].astype(F32)
        out[:2] = root
        low[...] = root.astype(BF16)
        out[2:] = near[2:] + next_r[...].astype(F32)

    total, low = kernel_call(
        body, facts, [total, root_far, next_far], [],
        [((4, PAGE, width), F32, True), ((2, PAGE, width), BF16, True)], after=after,
    )
    return total, low, flipped(low, "leaf", 1)


def over_chips(facts, total, far, after):
    width = total.shape[-1]

    def body(facts, near, away, out, values):
        root = near[:2] + away[...].astype(F32)
        picked = jnp.where(facts[ROOT_IN_CHIP] == 1, root, near[2:]).astype(BF16)
        out[...] = picked
        values[...] = picked[1]

    outs = [((2, PAGE, width), BF16, True), ((PAGE, width), BF16, True)]
    mine, values = kernel_call(body, facts, [total, far], [], outs, after=after)
    across = flipped(values, "tensor", 1)
    corner = lax.ppermute(values, ("tensor", "sub"), [(i, 3 - i) for i in range(4)])
    return mine, flipped(mine, "sub", 1), across, corner


def other_level2(order, head, kind, ref):
    theirs = head ^ order.half
    at = theirs % order.half * HD
    return ref[4 + 2 * (theirs // order.half) + kind, :, at : at + HD]


def begin_values(order, facts, own0, level2_far, handed):
    def body(facts, own_r, low_r, handed_r, out, handed_out):
        handed_out[...] = handed_r[...]
        ok = row_ok(facts[N0], PAGE, HD)
        for head in range(order.heads):
            c = slice(head * HD, (head + 1) * HD)
            low = other_level2(order, head, 1, low_r).astype(F32)
            value = own_r[1, :, c] + jnp.where(facts[OWNS2] == 1, low, 0.0)
            out[:, c] = jnp.where(ok, value, 0.0).astype(BF16)

    outs = [((PAGE, own0.shape[-1]), BF16, True), (handed.shape, handed.dtype, True)]
    return kernel_call(body, facts, [own0, level2_far, handed], [], outs)


def finish_small_tree(order, facts, own0, mine, far, level2_far):
    width = own0.shape[-1]

    def body(facts, own_r, mine_r, far_r, low_r, dk, dv):
        owns2 = facts[OWNS2] == 1
        ok = row_ok(facts[N0], PAGE, HD)
        for head in range(order.heads):
            c = slice(head * HD, (head + 1) * HD)
            at = head % order.half * HD
            for kind, out in enumerate((dk, dv)):
                gained = (far_r if head < order.half else mine_r)[kind, :, at : at + HD]
                level2 = other_level2(order, head, kind, low_r)
                more = jnp.where(owns2, level2, gained).astype(F32)
                out[:, c] = jnp.where(ok, own_r[kind, :, c] + more, 0.0).astype(BF16)

    page = ((PAGE, width), BF16, True)
    return kernel_call(body, facts, [own0, mine, far, level2_far], [], [page, page])


def gather_tree(ids, own):
    leaves = lax.axis_size(("leaf", "sub"))
    owned = ids[:INNER] == ids[INNER] - 1
    pages = jnp.where(owned[:, None, None, None], own[None], jnp.zeros((), BF16))
    for bit in range(leaves.bit_length() - 1):
        active = spanning(leaves, bit)
        far = flipped(pages[:active], ("leaf", "sub"), 1 << bit)
        pages = jnp.concatenate([pages[:active] + far, pages[active:]])
    return pages


def reduce_tree(ids, parts):
    leaves = lax.axis_size(("leaf", "sub"))
    for bit in range(leaves.bit_length() - 1):
        active = spanning(leaves, bit)
        far = flipped(parts[:active], ("leaf", "sub"), 1 << bit)
        parts = jnp.concatenate([parts[:active] + far, parts[active:]])
    owned = ids[:INNER] == ids[INNER] - 1
    return jnp.sum(jnp.where(owned[:, None, None, None], parts, 0.0), axis=0)


def on_device(queries, grad_out, keys, values, log_norms, row_deltas, ancestors, counts, w_value):
    kv = keys.shape[1] // HD
    group = queries.shape[1] // keys.shape[1]
    leaves = lax.axis_size(("leaf", "sub"))
    hbm = lambda a: pltpu.with_memory_space_constraint(a, pltpu.HBM)
    side = lax.axis_index("tensor").astype(I32).reshape(1)
    two_sides = lax.axis_size("tensor") == 2
    inputs = [hbm(a) for a in (queries, grad_out, keys, values, log_norms, row_deltas)]
    fast = leaves == 8 and lax.axis_size("sub") == 2 and kv == 4 and two_sides
    order = Order(fast, kv)
    facts, own = start(order, side, hbm(ancestors), hbm(counts), *inputs[2:4])
    state = {}

    def own_pages(kvs, pages, prior=(), after=()):
        return attend(True, kvs, group, order, facts, inputs, pages, state, prior, after)

    def shared_pages(kvs, page, ride=None, after=()):
        return attend(
            False, kvs, group, order, facts, inputs, [page], state, after=after, ride=ride
        )[0]

    def spread(part):
        if two_sides:
            return flipped(part, "tensor", 1)
        return lax.all_gather(part, "tensor", axis=1, tiled=True)

    kvs = tuple(range(kv))
    w = hbm(w_value)
    if fast:
        level2, calls = [], []

        def beside_pair(from_core, chip):
            level2.extend((own, from_core))
            calls.append(own_pages(kvs[:1], level2, after=(chip,)))
            return (calls[0][3],)

        def beside_half(pair):
            calls.append(own_pages(kvs[1:], level2, calls[0], (pair,)))
            return (calls[1][3],)

        mine, theirs = gather_small_tree(facts, own, beside_pair, beside_half)
        dk12, dv12, own0, send2 = calls[1]
        sent = flipped(shared_pages(kvs[:2], mine, send2), "sub", 1)
        kept = shared_pages(kvs[2:], theirs)
        total, root, root_far, next_far = over_cores(facts, kept, sent)
        base, dv12 = begin_values(order, facts, own0, sent, dv12)
        far_v = spread(dv12)
        made, w_near = finish_queries(
            kvs[:3], group, order, facts, (mine, theirs), state, (root, base), w
        )
        total, low, far = over_halves(facts, total, root_far, next_far, (made,))
        base_far = spread(base)
        *grads, made = input_grad(
            order, facts, w_near, 2 * PAGE, [dv12], [far_v], ([dk12], [dv12]), near_w=True,
            after=(low,),
        )
        near, far, across, corner = over_chips(facts, total, far, (made, base_far))
        dk0, dv0 = finish_small_tree(order, facts, own0, near, far, sent)
        begun = begin_input_grad(order, facts, w_near, [dv0])
        made = finish_queries(
            kvs[3:], group, order, facts, (mine, theirs), state, (begun,)
        )
        grads = end_input_grad(
            order, facts, w_near, base_far, across, corner, begun, [dk0, dv0], grads, made
        )
        return (state["gq"], grads[1], grads[2], grads[0])

    path_ids = ancestors[0]
    pages = gather_tree(path_ids, own)
    dk12, dv12, own0, send2 = own_pages(kvs, (pages[2], pages[2]))
    grads = shared_pages(kvs, pages[:2])
    finish_queries(kvs, group, order, facts, (pages[:2],), state)
    low = send2.astype(F32)
    total = reduce_tree(path_ids, jnp.concatenate([grads.reshape(2, 2, *grads.shape[1:]), low[None]]))
    total += own0 - jnp.where(path_ids[2] == path_ids[INNER] - 1, low, 0.0)
    has = jnp.any(path_ids[:INNER] == path_ids[INNER] - 1)
    ok = (jnp.arange(PAGE) < jnp.where(has, counts[0, 0], 0))[:, None]
    dk0, dv0 = jnp.where(ok, total, 0.0).astype(BF16)
    if two_sides:
        pair = lambda part: ([part], [spread(part)])
    else:
        pair = lambda part: ([spread(part)], [])
    *grads, _ = input_grad(order, facts, w, 2 * PAGE, *pair(dv12), ([dk12], [dv12]))
    grads = input_grad(order, facts, w, PAGE, *pair(dv0), ([dk0], [dv0]), grads)
    return (state["gq"], grads[1], grads[2], grads[0])


def solution(mesh):
    placed = (
        P(("groups", "leaf", "sub"), "tensor"),
        P(("groups", "leaf", "sub"), "tensor"),
        P(("groups", "leaf", "sub"), "tensor"),
        P(("groups", "leaf", "sub"), "tensor"),
        P("tensor", ("groups", "leaf", "sub")),
        P("tensor", ("groups", "leaf", "sub")),
        P(("groups", "leaf", "sub"), None),
        P(("groups", "leaf", "sub"), None),
        P("tensor", None),
    )
    return jax.shard_map(
        on_device,
        mesh=mesh,
        in_specs=placed,
        out_specs=(
            P(("groups", "leaf", "sub"), "tensor"),
            P(("groups", "leaf", "sub"), "tensor"),
            P(("groups", "leaf", "sub"), "tensor"),
            P(("groups", "leaf", "sub"), "tensor"),
        ),
        check_vma=False,
    )
```

```python
import math

import jax
import jax.numpy as jnp
from jax import lax
from jax.experimental import pallas as pl
from jax.experimental.pallas import tpu as pltpu
from jax.sharding import PartitionSpec as P

HD = 128
PAGE = 128
SLOTS = 3
INNER = 3
ROWS = SLOTS * PAGE
LOG2E = math.log2(math.e)
SCALE = 1.0 / math.sqrt(HD)
BF16 = jnp.bfloat16
F32 = jnp.float32
I32 = jnp.int32
LARGE = 10 << 20
SMALL = 4 << 20
SLIGHT = pl.CostEstimate(flops=1000, bytes_accessed=1000, transcendentals=0)
BLOCKED = 1e30


def dot_t(left, right):
    return lax.dot_general(left, right, (((1,), (1,)), ((), ())), preferred_element_type=F32)


def dot_n(left, right):
    return lax.dot_general(left, right, (((1,), (0,)), ((), ())), preferred_element_type=F32)


FACTS = 16
N0, N1, N2, OWNS2, LIMIT, LEADS, ROOT_IN_CHIP, ROOT_IN_PAIR, NEXT_IN_CHIP, SIDE, SWAP = range(11)


class Order:
    def __init__(self, crossed, heads):
        self.crossed, self.heads = crossed, heads
        self.half = heads // 2 if crossed else heads

    def at(self, facts, head, unit):
        if not self.crossed:
            return head * unit
        step = ((head ^ self.half) - head) * unit
        return pl.multiple_of(facts[SWAP] * step + head * unit, unit)

    def runs(self, first, last):
        cuts = [first, *(h for h in range(first + 1, last) if h % self.half == 0), last]
        return list(zip(cuts[:-1], cuts[1:]))

    def real(self, facts, rows):
        if not self.crossed:
            return rows
        width = self.half * HD
        turned = jnp.concatenate([rows[:, width:], rows[:, :width]], axis=1)
        return jnp.where(facts[SWAP] == 1, turned, rows)


def write_facts(facts, ids, counts, side, order):
    page = [ids[0, j] for j in range(INNER + 1)]
    own = page[INNER] - 1
    leaf = own // SLOTS
    owns = [page[j] == own for j in range(INNER)]
    same = lambda level, shift: ((page[level] // SLOTS) >> shift) == (leaf >> shift)
    number = lambda flag: jnp.where(flag, 1, 0)
    facts[N0] = jnp.where(owns[0] | owns[1] | owns[2], counts[0, 0], 0)
    facts[N1] = counts[0, 1]
    facts[N2] = counts[0, 2]
    facts[OWNS2] = number(owns[2])
    facts[LIMIT] = jnp.where(owns[2], 2 * PAGE, jnp.where(owns[1], PAGE, 0))
    facts[LEADS] = number(lax.rem(leaf, 2) == 0)
    facts[ROOT_IN_CHIP] = number(same(0, 1))
    facts[ROOT_IN_PAIR] = number(same(0, 2))
    facts[NEXT_IN_CHIP] = number(same(1, 1))
    facts[SIDE] = side
    facts[SWAP] = lax.rem(leaf, 2) if order.crossed else 0
    for i in range(SWAP + 1, FACTS):
        facts[i] = 0


def row_ok(count, rows, width):
    return lax.broadcasted_iota(I32, (rows, width), 0) < count


def kernel_call(body, facts, near, far, outs, scratch=(), aliases=None, after=(), cost=None,
                limit=SMALL):
    smem = pl.BlockSpec(memory_space=pltpu.SMEM)
    vmem = pl.BlockSpec(memory_space=pltpu.VMEM)
    hbm = pl.BlockSpec(memory_space=pl.ANY)
    near = [pltpu.with_memory_space_constraint(a, pltpu.VMEM) for a in near]
    place = {("near", i): 1 + i for i in range(len(near))}
    place |= {("far", i): 1 + len(near) + i for i in range(len(far))}
    used = 1 + len(near) + len(far)

    def kernel(*refs):
        body(*refs[:used], *refs[used + len(after) :])

    return pl.pallas_call(
        kernel,
        out_shape=tuple(
            pltpu.VMEM(s, d) if inside else jax.ShapeDtypeStruct(s, d) for s, d, inside in outs
        ),
        in_specs=[smem] + [vmem] * len(near) + [hbm] * (len(far) + len(after)),
        out_specs=tuple(vmem if inside else hbm for _, _, inside in outs),
        scratch_shapes=list(scratch),
        input_output_aliases={place[k]: v for k, v in (aliases or {}).items()},
        compiler_params=pltpu.CompilerParams(vmem_limit_bytes=limit),
        cost_estimate=cost or SLIGHT,
    )(pltpu.with_memory_space_constraint(facts, pltpu.SMEM), *near, *far, *after)


def start(order, side, ids, counts, keys, values):
    width = keys.shape[1]

    def body(side_ref, ids_ref, counts_ref, k_ref, v_ref, facts, out, held, ids_s, counts_s, sem):
        copies = [
            pltpu.make_async_copy(src, dst, sem.at[i])
            for i, (src, dst) in enumerate(
                (
                    (ids_ref, ids_s),
                    (counts_ref, counts_s),
                    (k_ref.at[:PAGE], held.at[0]),
                    (v_ref.at[:PAGE], held.at[1]),
                )
            )
        ]
        for c in copies:
            c.start()
        copies[0].wait()
        copies[1].wait()
        write_facts(facts, ids_s, counts_s, side_ref[0], order)
        ok = row_ok(counts_s[0, 0], PAGE, width)
        for i in range(2):
            copies[2 + i].wait()
            out[i] = jnp.where(ok, held[i], jnp.zeros((), BF16))

    smem = pl.BlockSpec(memory_space=pltpu.SMEM)
    hbm = pl.BlockSpec(memory_space=pl.ANY)
    return pl.pallas_call(
        body,
        out_shape=(pltpu.SMEM((FACTS,), I32), pltpu.VMEM((2, PAGE, width), BF16)),
        in_specs=[smem] + [hbm] * 4,
        out_specs=(smem, pl.BlockSpec(memory_space=pltpu.VMEM)),
        scratch_shapes=[
            pltpu.VMEM((2, PAGE, width), BF16),
            pltpu.SMEM(ids.shape, I32),
            pltpu.SMEM(counts.shape, I32),
            pltpu.SemaphoreType.DMA((4,)),
        ],
        compiler_params=pltpu.CompilerParams(vmem_limit_bytes=SMALL),
    )(side, ids, counts, keys, values)


def row_terms(rows):
    high = rows.astype(BF16).astype(F32)
    rest = rows - high
    middle = rest.astype(BF16).astype(F32)
    parts = [high, middle, rest - middle]
    spare = HD - 3 * rows.shape[0]
    parts.append(jnp.zeros((spare, rows.shape[1]), F32))
    return jnp.concatenate(parts, axis=0).T.astype(BF16)


class Head:
    def __init__(self, kv, group, norms, deltas, en, ed):
        self.group = group
        self.heads = min(4, group)
        self.parts = group // self.heads
        self.tall = self.heads * PAGE
        heads = slice(kv * group, (kv + 1) * group)
        en[...] = row_terms(norms[heads, :])
        ed[...] = row_terms(deltas[heads, :])

    def lanes(self, part, j):
        at = (part * self.heads + j) * HD
        return slice(at, at + HD)

    def stacked(self, ref, part, slots):
        return jnp.concatenate(
            [
                ref[slot * PAGE : (slot + 1) * PAGE, self.lanes(part, j)]
                for slot in slots
                for j in range(self.heads)
            ],
            axis=0,
        )

    def deep(self, stacked, terms, part, slots):
        column = lax.broadcasted_iota(I32, (1, HD), 1) % self.group
        picks = [
            (column == part * self.heads + j).astype(F32).astype(BF16)
            for j in range(self.heads)
        ]
        extra = [
            terms[slot * PAGE : (slot + 1) * PAGE] * pick for slot in slots for pick in picks
        ]
        return jnp.concatenate([stacked, jnp.concatenate(extra, axis=0)], axis=1)

    def turned_at(self, part, slot, count):
        at = (part * SLOTS + slot) * self.tall
        return slice(at, at + self.tall * count)


def set_keys(deep, upright, at, page):
    where = slice(at * PAGE, (at + 1) * PAGE)
    deep[:HD, where] = page.T
    if upright is not None:
        upright[where] = page


def weigh(scores, grads, keep):
    p = keep(jnp.exp2(scores * (SCALE * LOG2E)))
    return p.astype(BF16), (p * grads).astype(BF16)


def attend(own, kvs, group, order, facts, inputs, pages, state, prior=(), after=(),
           ride=None):
    loading = "k" not in state
    q_all, k_all = inputs[0], inputs[2]
    count = len(kvs)
    parts = group // min(4, group)
    tall = min(4, group) * PAGE
    width = count * HD
    base = prior[0].shape[1] if prior else 0
    kv_total = k_all.shape[1] // HD
    fresh = [("qt", kv) not in state for kv in kvs]
    one_head = (ROWS, group * HD)
    turned = ((HD, group * ROWS), BF16, True)
    low = lambda rows, columns: ((rows, columns), BF16, True)
    shapes = {
        "da": low(2 * group * PAGE, 2 * PAGE),
        "db": low(2 * group * PAGE, PAGE),
        "ku": low(4 * PAGE, HD),
        "qt": turned,
        "gt": turned,
    }

    near, far, aliases, outs = [], [], {}, []
    at_near, at_far, at_out = {}, {}, {}

    def add_near(name, array):
        at_near[name] = len(near)
        near.append(array)

    def add_far(name, array):
        at_far[name] = len(far)
        far.append(array)

    def add_out(name, out):
        at_out[name] = len(outs)
        outs.append(out)

    for kv, is_fresh in zip(kvs, fresh):
        for name, shape in shapes.items():
            if is_fresh:
                add_out((name, kv), shape)
            elif name in ("qt", "gt"):
                add_near((name, kv), state[name, kv])
        if not own and not is_fresh:
            add_out(("ds", kv), ((group * ROWS, 2 * PAGE), BF16, True))
    at_results = len(outs)
    if own:
        outs += [
            ((2 * PAGE, base + width), BF16, True),
            ((2 * PAGE, base + width), BF16, True),
            ((2, PAGE, base + width), F32, True),
            ((2, PAGE, base + width), BF16, True),
        ]
    else:
        outs += [
            ((4, PAGE, width), F32, True) if ride is None else ((8, PAGE, width), BF16, True),
        ]
    at_loaded = len(outs)
    if loading:
        for name, array in zip(("q", "g", "k", "v", "norms", "deltas"), inputs):
            add_far(name, array)
            if name in ("q", "g"):
                for kv in range(kv_total):
                    add_out((name, kv), (one_head, BF16, True))
            else:
                add_out(name, (array.shape, array.dtype, True))
    else:
        for name in ("k", "v", "norms", "deltas"):
            add_near(name, state[name])
        for kv in kvs:
            for name in ("q", "g"):
                add_near((name, kv), state[name, kv])
    for i, page in enumerate(pages):
        add_near(("page", i), page)
    for i, array in enumerate(prior):
        add_near(("prior", i), array)
    if ride is not None:
        add_near("ride", ride)
    key_pages = 4 if own else 2
    scratch = [
        pltpu.VMEM((2 * HD, key_pages * PAGE), BF16),
        pltpu.VMEM((2 * HD, key_pages * PAGE), BF16),
        pltpu.VMEM((key_pages * PAGE, HD), BF16),
        pltpu.VMEM((2, HD, key_pages * PAGE), F32),
        pltpu.VMEM((ROWS, HD), BF16),
        pltpu.VMEM((ROWS, HD), BF16),
        pltpu.SemaphoreType.DMA((2 * kv_total + 8,)),
    ]
    cols = lambda a, b: slice(a * PAGE, b * PAGE)

    def body(facts, *refs):
        ins, out_refs = refs[: len(near) + len(far)], refs[len(near) + len(far) : -len(scratch)]
        k_deep, v_deep, k_up, acc, en, ed, load_sem = refs[-len(scratch) :]
        near_ref = lambda name: ins[at_near[name]]
        far_ref = lambda name: ins[len(near) + at_far[name]]
        held = lambda name: out_refs[at_out[name]] if name in at_out else near_ref(name)
        results = out_refs[at_results:at_loaded]
        copies = {}
        if loading:

            def load(key, src, dst):
                copies[key] = pltpu.make_async_copy(src, dst, load_sem.at[len(copies)])
                copies[key].start()

            for lo, hi in order.runs(0, kv_total):
                for name in ("k", "v"):
                    at = pl.ds(order.at(facts, lo, HD), (hi - lo) * HD)
                    here = slice(lo * HD, hi * HD)
                    load((name, lo), far_ref(name).at[:, at], held(name).at[:, here])
                for name in ("norms", "deltas"):
                    at = pl.ds(order.at(facts, lo, group), (hi - lo) * group)
                    here = slice(lo * group, hi * group)
                    load((name, lo), far_ref(name).at[at], held(name).at[here])
            shared_loads = list(copies)
            for kv in range(kv_total):
                at = pl.ds(order.at(facts, kv, group * HD), group * HD)
                for name in ("q", "g"):
                    load((name, kv), far_ref(name).at[:, at], held((name, kv)))
        k, v, norms, deltas = (held(name) for name in ("k", "v", "norms", "deltas"))

        def arrived(*keys):
            for key in keys:
                if key in copies:
                    copies.pop(key).wait()

        k_deep[HD:] = jnp.full((HD, key_pages * PAGE), -1.0, BF16)
        v_deep[HD:] = jnp.full((HD, key_pages * PAGE), -1.0, BF16)
        for out, i in zip(results, range(len(prior))):
            out[..., :base] = near_ref(("prior", i))[...]
        if ride is not None:
            (out,), more = results, near_ref("ride")
            for kind in range(2):
                out[4 + kind] = more[kind, :, :width]
                out[6 + kind] = more[kind, :, width:]
        owns2 = facts[OWNS2] == 1
        if loading:
            arrived(*shared_loads)
            lane = lax.broadcasted_iota(I32, norms.shape, 1)
            limit = jnp.where(
                lane < PAGE, facts[N0], jnp.where(lane < 2 * PAGE, facts[N1], facts[N2])
            )
            norms[...] = jnp.where(lane % PAGE < limit, norms[...] * (1.0 / SCALE), BLOCKED)
        lower = lambda rows: lax.broadcasted_iota(I32, (rows, PAGE), 1) <= (
            lax.broadcasted_iota(I32, (rows, PAGE), 0) % PAGE
        )

        def set_pages(n, kv):
            lane = slice(kv * HD, (kv + 1) * HD)
            if own:
                first, second = (near_ref(("page", i)) for i in range(2))
                zero = jnp.zeros((), BF16)
                for slot, (at, c) in enumerate(((3, N0), (0, N1), (2, N2))):
                    ok = row_ok(facts[c], PAGE, HD)
                    rows = cols(slot, slot + 1)
                    set_keys(k_deep, k_up, at, jnp.where(ok, k[rows, lane], zero))
                    set_keys(v_deep, None, at, jnp.where(ok, v[rows, lane], zero))
                level2 = [jnp.where(owns2, first[i, :, lane], second[i, :, lane]) for i in (0, 1)]
                if order.crossed:
                    at = (kv ^ order.half) * HD
                    lane = slice(at, at + HD)
                    for i in range(2):
                        other = jnp.where(owns2, first[i, :, lane], second[i, :, lane])
                        level2[i] = jnp.where(facts[SWAP] == 1, other, level2[i])
                set_keys(k_deep, k_up, 1, level2[0])
                set_keys(v_deep, None, 1, level2[1])
            else:
                page = near_ref(("page", 0))
                for j in range(2):
                    here = slice(n * HD, (n + 1) * HD)
                    set_keys(k_deep, k_up, j, page[j, 0, :, here])
                    set_keys(v_deep, None, j, page[j, 1, :, here])
            acc[...] = jnp.zeros_like(acc)

        def turned_rows(head, kv, part, is_fresh, qs, gs, order):
            if is_fresh:
                for name, rows in (("qt", qs), ("gt", gs)):
                    for i, slot in enumerate(order):
                        held((name, kv))[:, head.turned_at(part, slot, 1)] = rows[
                            i * tall : (i + 1) * tall
                        ].T
            return lambda name, slot, slots: held((name, kv))[
                :, head.turned_at(part, slot, slots)
            ]

        def own_part(head, kv, part, n):
            order = (1, 2, 0)
            qs = head.stacked(held(("q", kv)), part, order)
            gs = head.stacked(held(("g", kv)), part, order)
            qd, gd = head.deep(qs, en, part, order), head.deep(gs, ed, part, order)
            turn = turned_rows(head, kv, part, fresh[n], qs, gs, order)
            low = lower(tall)

            def keep_first(p):
                masked = jnp.where(low, p[:tall, :PAGE], 0.0)
                return jnp.concatenate(
                    [jnp.concatenate([masked, p[:tall, PAGE:]], axis=1), p[tall:]], axis=0
                )

            pa, da = weigh(
                dot_n(qd[: 2 * tall], k_deep[:, : 2 * PAGE]),
                dot_n(gd[: 2 * tall], v_deep[:, : 2 * PAGE]),
                keep_first,
            )
            both = lambda x: jnp.concatenate([x[:tall, :PAGE], x[tall:, PAGE:]], axis=0)
            low2 = lower(2 * tall)
            pb, db = weigh(
                both(dot_n(qd[tall:], k_deep[:, 2 * PAGE :])),
                both(dot_n(gd[tall:], v_deep[:, 2 * PAGE :])),
                lambda p: jnp.where(low2, p, 0.0),
            )
            for i, (name, a, b) in enumerate((("qt", da, db), ("gt", pa, pb))):
                acc[i, :, : 2 * PAGE] += dot_n(turn(name, 1, 2), a)
                acc[i, :, cols(2, 3)] += dot_n(turn(name, 2, 1), b[:tall])
                acc[i, :, cols(3, 4)] += dot_n(turn(name, 0, 1), b[tall:])
            here = slice(part * 2 * tall, (part + 1) * 2 * tall)
            held(("da", kv))[here] = da
            held(("db", kv))[here] = db

        def shared_part(head, kv, part, n):
            order = (0, 1, 2)
            qs = head.stacked(held(("q", kv)), part, order)
            gs = head.stacked(held(("g", kv)), part, order)
            qd, gd = head.deep(qs, en, part, order), head.deep(gs, ed, part, order)
            turn = turned_rows(head, kv, part, fresh[n], qs, gs, order)
            column = lax.broadcasted_iota(I32, (tall, 2 * PAGE), 1)
            seen = column < facts[LIMIT]

            def keep(p):
                return jnp.concatenate([jnp.where(seen, p[:tall], 0.0), p[tall:]], axis=0)

            p, ds = weigh(dot_n(qd, k_deep[...]), dot_n(gd, v_deep[...]), keep)
            acc[0] += dot_n(turn("qt", 0, SLOTS), ds)
            acc[1] += dot_n(turn("gt", 0, SLOTS), p)
            held(("ds", kv))[part * SLOTS * tall : (part + 1) * SLOTS * tall] = ds

        def put_own(n):
            dk12, dv12, own0, send2 = results
            here = slice(base + n * HD, base + (n + 1) * HD)
            grad = [acc[0].T * SCALE, acc[1].T]
            for at, c, to in ((0, N1, 0), (2, N2, 1)):
                ok = row_ok(facts[c], PAGE, HD)
                for kind, out in ((0, dk12), (1, dv12)):
                    out[cols(to, to + 1), here] = jnp.where(
                        ok, grad[kind][cols(at, at + 1)], 0.0
                    ).astype(BF16)
            for kind in range(2):
                level2 = grad[kind][cols(1, 2)]
                own0[kind, :, here] = grad[kind][cols(3, 4)] + jnp.where(owns2, level2, 0.0)
                send2[kind, :, here] = level2.astype(BF16)

        def put_shared(n):
            (out,) = results
            here = slice(n * HD, (n + 1) * HD)
            grads = acc[0].T * SCALE, acc[1].T
            for j in range(2):
                for kind in range(2):
                    out[2 * j + kind, :, here] = grads[kind][cols(j, j + 1)].astype(out.dtype)

        for n, kv in enumerate(kvs):
            arrived(("q", kv), ("g", kv))
            head = Head(kv, group, norms, deltas, en, ed)
            set_pages(n, kv)

            for part in range(parts):
                (own_part if own else shared_part)(head, kv, part, n)
            if own:
                held(("ku", kv))[...] = k_up[...]
            (put_own if own else put_shared)(n)
        arrived(*list(copies))

    made = kernel_call(
        body, facts, near, far, outs, scratch, aliases, after,
        pl.CostEstimate(
            flops=240 * PAGE * PAGE * HD * group * count, bytes_accessed=1000, transcendentals=0
        ),
        LARGE,
    )
    for name, at in at_out.items():
        state[name] = made[at]
    return list(made[at_results:at_loaded])


def width_tiles(w):
    tile = next(t for t in (512, 640, 320, 128, w.shape[0]) if w.shape[0] % t == 0)
    return [slice(i, i + tile) for i in range(0, w.shape[0], tile)]


def finish_queries(kvs, group, order, facts, pages, state, after=(), w=None):
    parts = group // min(4, group)
    heads = group // parts
    tall = heads * PAGE
    wide = heads * HD
    near = list(pages)
    names = ("ds", "da", "db", "ku")
    for kv in kvs:
        near += [state[name, kv] for name in names]

    def body(facts, *refs):
        stage, sem = refs[-2:]
        if w is not None:
            gq, made, w_near = refs[-5:-2]
            w_copy = pltpu.make_async_copy(refs[-6], w_near, sem.at[len(kvs) * parts])
            w_copy.start()
        else:
            gq, made = refs[-4:-2]
        made[...] = jnp.zeros_like(made)
        sends = []
        for n, kv in enumerate(kvs):
            first = len(pages) + len(names) * n
            ds, da, db, ku = refs[first : first + len(names)]
            page, at = refs[kv // order.half], kv % order.half * HD
            keys = jnp.concatenate([page[j, 0, :, at : at + HD] for j in range(2)], axis=0)
            for part in range(parts):
                at = n * parts + part
                gained = dot_n(ds[part * SLOTS * tall : (part + 1) * SLOTS * tall], keys)
                here = part * 2 * tall
                wide_part = dot_n(da[here : here + 2 * tall], ku[: 2 * PAGE])
                own2 = dot_n(db[here : here + tall], ku[2 * PAGE : 3 * PAGE])
                own0 = dot_n(db[here + tall : here + 2 * tall], ku[3 * PAGE :])
                by_slot = (
                    gained[:tall] + own0,
                    gained[tall : 2 * tall] + wide_part[:tall],
                    gained[2 * tall :] + (wide_part[tall:] + own2),
                )
                for i in range(SLOTS * heads):
                    slot, j = divmod(i, heads)
                    rows = slice(slot * PAGE, (slot + 1) * PAGE)
                    value = by_slot[slot][j * PAGE : (j + 1) * PAGE]
                    stage[at, rows, j * HD : (j + 1) * HD] = (value * SCALE).astype(BF16)
                to = pl.multiple_of(order.at(facts, kv, group * HD) + part * wide, wide)
                sends.append(
                    pltpu.make_async_copy(stage.at[at], gq.at[:, pl.ds(to, wide)], sem.at[at])
                )
                sends[-1].start()
        for c in sends:
            c.wait()
        if w is not None:
            w_copy.wait()

    count = len(kvs) * parts
    far = [state["gq"]] if "gq" in state else []
    aliases = {("far", 0): 0} if far else {}
    shape = (ROWS, state["k"].shape[1] * group)
    outs = [(shape, BF16, False), ((8, HD), F32, True)]
    if w is not None:
        far = far + [w]
        outs.append((w.shape, w.dtype, True))
    state["gq"], *made = kernel_call(
        body, facts, near, far, outs,
        [pltpu.VMEM((count, ROWS, wide), BF16), pltpu.SemaphoreType.DMA((count + 1,))],
        aliases, after, limit=LARGE,
    )
    return made


def input_grad(order, facts, w, rows, own, far, grads, carry=None, near_w=False, after=()):
    out_cols, depth = w.shape
    tiles = width_tiles(w)
    top = 0 if rows == PAGE else PAGE
    steps = len(tiles)
    width = sum(a.shape[1] for a in grads[0])
    arrays = [*own, *far, *grads[0], *grads[1]] + [w] * near_w
    count = len(grads[0])
    carry = list(carry or [])
    lead = [] if near_w else [w]
    rest = [*lead, *carry, *after]

    def body(facts, *refs):
        own_r, refs = refs[: len(own)], refs[len(own) :]
        far_r, refs = refs[: len(far)], refs[len(far) :]
        grad_r, w_ref = refs[: 2 * count], refs[2 * count]
        out, dk, dv, made, w_near, stage, w_sem, sem = refs[-8:]
        loads = []
        if not near_w:
            loads = [
                pltpu.make_async_copy(w_ref.at[at], w_near.at[at], w_sem.at[i])
                for i, at in enumerate(tiles)
            ]
        for c in loads:
            c.start()
        made[...] = jnp.zeros_like(made)
        columns = lambda rs: jnp.concatenate([r[...] for r in rs], axis=1)
        full = order.real(facts, columns(own_r))
        if far:
            other, first = order.real(facts, columns(far_r)), facts[SIDE] == 0
            full = jnp.concatenate(
                [jnp.where(first, full, other), jnp.where(first, other, full)], axis=1
            )
        copies = put_rows(order, facts, grad_r, dk, dv, top, rows, sem, steps)
        for i, at in enumerate(tiles):
            if loads:
                loads[i].wait()
            stage[i] = dot_t((w_ref if near_w else w_near)[at], full).astype(BF16).T
            copies.append(
                pltpu.make_async_copy(stage.at[i], out.at[top : top + rows, at], sem.at[i])
            )
            copies[-1].start()
        for c in copies:
            c.wait()

    smem = pl.BlockSpec(memory_space=pltpu.SMEM)
    vmem = pl.BlockSpec(memory_space=pltpu.VMEM)
    hbm = pl.BlockSpec(memory_space=pl.ANY)
    arrays = [pltpu.with_memory_space_constraint(a, pltpu.VMEM) for a in arrays]
    kept = jax.ShapeDtypeStruct((ROWS, width), BF16)
    return pl.pallas_call(
        body,
        out_shape=(
            jax.ShapeDtypeStruct((ROWS, out_cols), BF16), kept, kept, pltpu.VMEM((8, HD), F32)
        ),
        in_specs=[smem] + [vmem] * len(arrays) + [hbm] * len(rest),
        out_specs=(hbm, hbm, hbm, vmem),
        scratch_shapes=[
            pltpu.VMEM((8, HD) if near_w else w.shape, BF16),
            pltpu.VMEM((steps, rows, out_cols // steps), BF16),
            pltpu.SemaphoreType.DMA((steps,)),
            pltpu.SemaphoreType.DMA((steps + 2 * order.heads,)),
        ],
        input_output_aliases={
            1 + len(arrays) + len(lead) + i: i for i in range(len(carry))
        },
        compiler_params=pltpu.CompilerParams(vmem_limit_bytes=LARGE),
        cost_estimate=SLIGHT,
    )(pltpu.with_memory_space_constraint(facts, pltpu.SMEM), *arrays, *rest)


def put_rows(order, facts, pieces, dk, dv, top, rows, sem, first):
    copies = []
    count = len(pieces) // 2
    for dst, mine in ((dk, pieces[:count]), (dv, pieces[count:])):
        head = 0
        for src in mine:
            more = src.shape[1] // HD
            for lo, hi in order.runs(head, head + more):
                copies.append(
                    pltpu.make_async_copy(
                        src.at[:, (lo - head) * HD : (hi - head) * HD],
                        dst.at[top : top + rows, pl.ds(order.at(facts, lo, HD), (hi - lo) * HD)],
                        sem.at[first + len(copies)],
                    )
                )
                copies[-1].start()
            head += more
    return copies


def begin_input_grad(order, facts, w, own, after=()):
    out_cols, depth = w.shape
    half = depth // 2
    rows = own[0].shape[0]
    count = len(own)

    def body(facts, w_ref, *refs):
        mine, out = jnp.concatenate([r[...] for r in refs[:count]], axis=1), refs[-1]
        mine = order.real(facts, mine)
        where = pl.ds(pl.multiple_of(facts[SIDE] * half, half), half)
        for at in width_tiles(w):
            out[at] = dot_t(w_ref[at, where], mine)

    smem = pl.BlockSpec(memory_space=pltpu.SMEM)
    vmem = pl.BlockSpec(memory_space=pltpu.VMEM)
    near = [pltpu.with_memory_space_constraint(a, pltpu.VMEM) for a in (w, *own)]

    def kernel(*refs):
        body(*refs[: 2 + count], refs[-1])

    return pl.pallas_call(
        kernel,
        out_shape=pltpu.VMEM((out_cols, rows), F32),
        in_specs=[smem] + [vmem] * len(near) + [pl.BlockSpec(memory_space=pl.ANY)] * len(after),
        out_specs=vmem,
        compiler_params=pltpu.CompilerParams(vmem_limit_bytes=LARGE),
        cost_estimate=SLIGHT,
    )(pltpu.with_memory_space_constraint(facts, pltpu.SMEM), *near, *after)


def end_input_grad(order, facts, w, base, across, corner, begun, grads, carry):
    tiles = width_tiles(w)
    out_cols, depth = w.shape
    half = depth // 2
    steps = len(tiles)
    rows = base.shape[0]

    def body(facts, w_r, begun_r, base_r, across_r, corner_r, *refs):
        out, dk, dv, stage, sem = refs[-5:]
        copies = put_rows(order, facts, refs[:2], dk, dv, 0, rows, sem, steps)
        gained = jnp.concatenate([corner_r[...], across_r[...]], axis=1).astype(F32)
        known = base_r[...]
        more = jnp.where(row_ok(facts[N0], rows, half), known.astype(F32) + gained, 0.0)
        other = order.real(facts, jnp.where(facts[OWNS2] == 1, known, more.astype(BF16)))
        where = pl.ds(pl.multiple_of((1 - facts[SIDE]) * half, half), half)
        for i, at in enumerate(tiles):
            stage[i] = (dot_t(w_r[at, where], other) + begun_r[at]).astype(BF16).T
            copies.append(pltpu.make_async_copy(stage.at[i], out.at[:rows, at], sem.at[i]))
            copies[-1].start()
        for c in copies:
            c.wait()

    return kernel_call(
        body, facts, [w, begun, base, across, corner, *grads], list(carry),
        [(a.shape, a.dtype, False) for a in carry],
        [
            pltpu.VMEM((steps, rows, out_cols // steps), BF16),
            pltpu.SemaphoreType.DMA((steps + 2 * order.heads,)),
        ],
        {("far", i): i for i in range(len(carry))},
    )


def flipped(block, axis, bit):
    count = lax.axis_size(axis)
    return lax.ppermute(block, axis, [(i, i ^ bit) for i in range(count) if i ^ bit < count])


def spanning(leaves, bit_index):
    return len([j for j in range(INNER) if 2 << bit_index <= leaves >> j])


def gather_small_tree(facts, own, beside_pair, beside_half):
    width = own.shape[-1] // 2
    page = ((2, PAGE, width), BF16, True)
    from_core = flipped(own, "sub", 1)

    def choose_chip(facts, own_ref, far_ref, out):
        for swap in range(2):
            for mine in range(2):

                @pl.when((facts[SWAP] == swap) & (facts[OWNS2] != mine))
                def _copy(swap=swap, mine=mine):
                    out[...] = (own_ref if mine else far_ref)[
                        :, :, swap * width : (swap + 1) * width
                    ]

    (chip,) = kernel_call(choose_chip, facts, [own, from_core], [], [page])
    from_pair = flipped(chip, "leaf", 1)

    def choose_pair(facts, near_ref, far_ref, out):
        out[...] = jnp.where(facts[ROOT_IN_CHIP] == 1, near_ref[...], far_ref[...])

    after = beside_pair(from_core, chip)
    (pair,) = kernel_call(choose_pair, facts, [chip, from_pair], [], [page], after=after)
    from_half = flipped(pair, "leaf", 2)

    def choose_all(facts, chip_ref, pair_far, pair_ref, half_far, out):
        out[0] = jnp.where(facts[ROOT_IN_PAIR] == 1, pair_ref[...], half_far[...])
        out[1] = jnp.where(facts[NEXT_IN_CHIP] == 1, chip_ref[...], pair_far[...])

    after = beside_half(pair)
    (mine,) = kernel_call(
        choose_all, facts, [chip, from_pair, pair, from_half], [],
        [((2, *page[0]), BF16, True)], after=after,
    )
    return mine, flipped(mine, "sub", 1)


def over_cores(facts, kept, far):
    width = kept.shape[-1]

    def body(_, near, away, total, root, next_one):
        for i in range(4):
            value = near[i] + away[i].astype(F32)
            total[i] = value
            (root, next_one)[i // 2][i % 2] = value.astype(BF16)

    pages = ((2, PAGE, width), BF16, True)
    total, root, next_one = kernel_call(
        body, facts, [kept, far], [], [((4, PAGE, width), F32, True), pages, pages]
    )
    return total, root, flipped(root, "leaf", 2), flipped(next_one, "leaf", 1)


def over_halves(facts, total, root_far, next_far, after):
    width = total.shape[-1]

    def body(_, near, root_r, next_r, out, low):
        root = near[:2] + root_r[...].astype(F32)
        out[:2] = root
        low[...] = root.astype(BF16)
        out[2:] = near[2:] + next_r[...].astype(F32)

    total, low = kernel_call(
        body, facts, [total, root_far, next_far], [],
        [((4, PAGE, width), F32, True), ((2, PAGE, width), BF16, True)], after=after,
    )
    return total, low, flipped(low, "leaf", 1)


def over_chips(facts, total, far, after):
    width = total.shape[-1]

    def body(facts, near, away, out, values):
        root = near[:2] + away[...].astype(F32)
        picked = jnp.where(facts[ROOT_IN_CHIP] == 1, root, near[2:]).astype(BF16)
        out[...] = picked
        values[...] = picked[1]

    outs = [((2, PAGE, width), BF16, True), ((PAGE, width), BF16, True)]
    mine, values = kernel_call(body, facts, [total, far], [], outs, after=after)
    across = flipped(values, "tensor", 1)
    corner = lax.ppermute(values, ("tensor", "sub"), [(i, 3 - i) for i in range(4)])
    return mine, flipped(mine, "sub", 1), across, corner


def other_level2(order, head, kind, ref):
    theirs = head ^ order.half
    at = theirs % order.half * HD
    return ref[4 + 2 * (theirs // order.half) + kind, :, at : at + HD]


def begin_values(order, facts, own0, level2_far, handed):
    def body(facts, own_r, low_r, handed_r, out, handed_out):
        handed_out[...] = handed_r[...]
        ok = row_ok(facts[N0], PAGE, HD)
        for head in range(order.heads):
            c = slice(head * HD, (head + 1) * HD)
            low = other_level2(order, head, 1, low_r).astype(F32)
            value = own_r[1, :, c] + jnp.where(facts[OWNS2] == 1, low, 0.0)
            out[:, c] = jnp.where(ok, value, 0.0).astype(BF16)

    outs = [((PAGE, own0.shape[-1]), BF16, True), (handed.shape, handed.dtype, True)]
    return kernel_call(body, facts, [own0, level2_far, handed], [], outs)


def finish_small_tree(order, facts, own0, mine, far, level2_far):
    width = own0.shape[-1]

    def body(facts, own_r, mine_r, far_r, low_r, dk, dv):
        owns2 = facts[OWNS2] == 1
        ok = row_ok(facts[N0], PAGE, HD)
        for head in range(order.heads):
            c = slice(head * HD, (head + 1) * HD)
            at = head % order.half * HD
            for kind, out in enumerate((dk, dv)):
                gained = (far_r if head < order.half else mine_r)[kind, :, at : at + HD]
                level2 = other_level2(order, head, kind, low_r)
                more = jnp.where(owns2, level2, gained).astype(F32)
                out[:, c] = jnp.where(ok, own_r[kind, :, c] + more, 0.0).astype(BF16)

    page = ((PAGE, width), BF16, True)
    return kernel_call(body, facts, [own0, mine, far, level2_far], [], [page, page])


def gather_tree(ids, own):
    leaves = lax.axis_size(("leaf", "sub"))
    owned = ids[:INNER] == ids[INNER] - 1
    pages = jnp.where(owned[:, None, None, None], own[None], jnp.zeros((), BF16))
    for bit in range(leaves.bit_length() - 1):
        active = spanning(leaves, bit)
        far = flipped(pages[:active], ("leaf", "sub"), 1 << bit)
        pages = jnp.concatenate([pages[:active] + far, pages[active:]])
    return pages


def reduce_tree(ids, parts):
    leaves = lax.axis_size(("leaf", "sub"))
    for bit in range(leaves.bit_length() - 1):
        active = spanning(leaves, bit)
        far = flipped(parts[:active], ("leaf", "sub"), 1 << bit)
        parts = jnp.concatenate([parts[:active] + far, parts[active:]])
    owned = ids[:INNER] == ids[INNER] - 1
    return jnp.sum(jnp.where(owned[:, None, None, None], parts, 0.0), axis=0)


def on_device(queries, grad_out, keys, values, log_norms, row_deltas, ancestors, counts, w_value):
    kv = keys.shape[1] // HD
    group = queries.shape[1] // keys.shape[1]
    leaves = lax.axis_size(("leaf", "sub"))
    hbm = lambda a: pltpu.with_memory_space_constraint(a, pltpu.HBM)
    side = lax.axis_index("tensor").astype(I32).reshape(1)
    two_sides = lax.axis_size("tensor") == 2
    inputs = [hbm(a) for a in (queries, grad_out, keys, values, log_norms, row_deltas)]
    fast = leaves == 8 and lax.axis_size("sub") == 2 and kv == 4 and two_sides
    order = Order(fast, kv)
    facts, own = start(order, side, hbm(ancestors), hbm(counts), *inputs[2:4])
    state = {}

    def own_pages(kvs, pages, prior=(), after=()):
        return attend(True, kvs, group, order, facts, inputs, pages, state, prior, after)

    def shared_pages(kvs, page, ride=None, after=()):
        return attend(
            False, kvs, group, order, facts, inputs, [page], state, after=after, ride=ride
        )[0]

    def spread(part):
        if two_sides:
            return flipped(part, "tensor", 1)
        return lax.all_gather(part, "tensor", axis=1, tiled=True)

    kvs = tuple(range(kv))
    w = hbm(w_value)
    if fast:
        level2, calls = [], []

        def beside_pair(from_core, chip):
            level2.extend((own, from_core))
            calls.append(own_pages(kvs[:1], level2, after=(chip,)))
            return (calls[0][3],)

        def beside_half(pair):
            calls.append(own_pages(kvs[1:], level2, calls[0], (pair,)))
            return (calls[1][3],)

        mine, theirs = gather_small_tree(facts, own, beside_pair, beside_half)
        dk12, dv12, own0, send2 = calls[1]
        sent = flipped(shared_pages(kvs[:2], mine, send2), "sub", 1)
        kept = shared_pages(kvs[2:], theirs)
        total, root, root_far, next_far = over_cores(facts, kept, sent)
        base, dv12 = begin_values(order, facts, own0, sent, dv12)
        far_v = spread(dv12)
        made, w_near = finish_queries(
            kvs, group, order, facts, (mine, theirs), state, (root, base), w
        )
        total, low, far = over_halves(facts, total, root_far, next_far, (made,))
        base_far = spread(base)
        near, far, across, corner = over_chips(facts, total, far, (low, base_far, far_v))
        dk0, dv0 = finish_small_tree(order, facts, own0, near, far, sent)
        begun = begin_input_grad(order, facts, w_near, [dv0])
        *grads, _ = input_grad(
            order, facts, w_near, 2 * PAGE, [dv12], [far_v], ([dk12], [dv12]), near_w=True,
            after=(begun,),
        )
        grads = end_input_grad(
            order, facts, w_near, base_far, across, corner, begun, [dk0, dv0], grads
        )
        return (state["gq"], grads[1], grads[2], grads[0])

    path_ids = ancestors[0]
    pages = gather_tree(path_ids, own)
    dk12, dv12, own0, send2 = own_pages(kvs, (pages[2], pages[2]))
    grads = shared_pages(kvs, pages[:2])
    finish_queries(kvs, group, order, facts, (pages[:2],), state)
    low = send2.astype(F32)
    total = reduce_tree(path_ids, jnp.concatenate([grads.reshape(2, 2, *grads.shape[1:]), low[None]]))
    total += own0 - jnp.where(path_ids[2] == path_ids[INNER] - 1, low, 0.0)
    has = jnp.any(path_ids[:INNER] == path_ids[INNER] - 1)
    ok = (jnp.arange(PAGE) < jnp.where(has, counts[0, 0], 0))[:, None]
    dk0, dv0 = jnp.where(ok, total, 0.0).astype(BF16)
    if two_sides:
        pair = lambda part: ([part], [spread(part)])
    else:
        pair = lambda part: ([spread(part)], [])
    *grads, _ = input_grad(order, facts, w, 2 * PAGE, *pair(dv12), ([dk12], [dv12]))
    grads = input_grad(order, facts, w, PAGE, *pair(dv0), ([dk0], [dv0]), grads)
    return (state["gq"], grads[1], grads[2], grads[0])


def solution(mesh):
    placed = (
        P(("groups", "leaf", "sub"), "tensor"),
        P(("groups", "leaf", "sub"), "tensor"),
        P(("groups", "leaf", "sub"), "tensor"),
        P(("groups", "leaf", "sub"), "tensor"),
        P("tensor", ("groups", "leaf", "sub")),
        P("tensor", ("groups", "leaf", "sub")),
        P(("groups", "leaf", "sub"), None),
        P(("groups", "leaf", "sub"), None),
        P("tensor", None),
    )
    return jax.shard_map(
        on_device,
        mesh=mesh,
        in_specs=placed,
        out_specs=(
            P(("groups", "leaf", "sub"), "tensor"),
            P(("groups", "leaf", "sub"), "tensor"),
            P(("groups", "leaf", "sub"), "tensor"),
            P(("groups", "leaf", "sub"), "tensor"),
        ),
        check_vma=False,
    )
```
